32 devices in a mesh: seq: 8 (over z, y), ch: 4 (over x, core).
Axes of the slice: x: 2, y: 2, z: 4, core: 2. Of those that a mesh axis runs over, the one named last changes fastest.
Arguments:
- qkv: bfloat16 [3, 1024, 2048], P(None, 'seq', 'ch'), may hold values from -6 to 6
- filt: float32 [1024, 2048], P('seq', 'ch'), may hold values from -0.75 to 0.75
- skip_gain: float32 [2048], P('ch'), may hold values from -4 to 4
- short_weight: float32 [3, 3, 2048], P(None, None, 'ch'), may hold values from -3.5 to 3.5
- w_out: bfloat16 [2048, 2048], P(None, 'ch'), may hold values from -0.125 to 0.125
- g_out: bfloat16 [1024, 2048], P('seq', 'ch'), may hold values from -6 to 6
Outputs:
- output: bfloat16 [1024, 2048], P('seq', 'ch')
- grad_qkv: bfloat16 [3, 1024, 2048], P(None, 'seq', 'ch')
- grad_filter: float32 [1024, 2048], P('seq', 'ch')
The draws below stay inside these ranges and needn't reach their ends.
All inputs are finite; a program needn't handle non-finite values.
Results may differ from the reference program's by a relative error of at most 0.0049.
Values may be sent and summed in bfloat16 or wider, within the bound.
No kernel may reach another device: no remote copies, remote signals or barrier semaphores. Data moves between devices by JAX's collectives and lax.ppermute only.
A program may use at most 64 MiB of HBM per device.

```python
import math
import jax
import jax.numpy as jnp
from jax import lax

C = 2048
TOKENS = 1024


def block_levels(own_key, extent, split, low, high):
    loudness = 1.0
    for dim, shards_of in split:
        heights = jax.random.uniform(jax.random.fold_in(jax.random.fold_in(own_key, 6), dim), (shards_of,), jnp.float32, low / len(split), high / len(split))
        loudness = loudness * jnp.repeat(jnp.exp(heights), extent[dim] // shards_of).reshape((-1,) + (1,) * (len(extent) - 1 - dim))
    return loudness


def bell_draw(rng, shape, width, reach, cuts=(), held_as=jnp.bfloat16):
    result = width * jax.random.normal(rng, shape, jnp.float32)
    if cuts:
        result = result * block_levels(rng, shape, cuts, -0.22, 0.18)
    return jnp.clip(result, -reach, reach).astype(held_as)


def setup_inputs(seed: int = 0) -> dict:
    key_list = jax.random.split(jax.random.key(seed), 7)
    return {
        "qkv": bell_draw(key_list[0], (3, TOKENS, C), 1.0, 6.0, ((1, 8), (2, 4))),
        "filt": bell_draw(key_list[1], (TOKENS, C), (TOKENS // 16) ** -0.5, 0.75, ((0, 8), (1, 4)), jnp.float32),
        "skip_gain": bell_draw(key_list[2], (C,), 1.0, 4.0, ((0, 4),), jnp.float32),
        "short_weight": bell_draw(key_list[3], (3, 3, C), 3 ** -0.5, 3.5, ((2, 4),), jnp.float32),
        "w_out": bell_draw(key_list[4], (C, C), C ** -0.5, 0.125, ((1, 4),)),
        "g_out": bell_draw(key_list[5], (TOKENS, C), 1.0, 6.0, ((0, 8), (1, 4))),
    }


def reference(qkv, filt, skip_gain, short_weight, w_out, g_out):
    token_count = qkv.shape[1]
    padded = jnp.pad(qkv, ((0, 0), (2, 0), (0, 0)))
    short = short_weight[:, 0, None, :] * padded[:, 2:, :] + short_weight[:, 1, None, :] * padded[:, 1:-1, :] + short_weight[:, 2, None, :] * padded[:, :-2, :]
    query_gate = short[0]
    key_short = short[1]
    value_short = short[2]
    mixed = key_short * value_short
    length = 2 * token_count
    mixed_spec = jnp.fft.rfft(mixed, n=length, axis=0)
    kernel_spec = jnp.fft.rfft(filt, n=length, axis=0)
    conv_out = jnp.fft.irfft(mixed_spec * kernel_spec, n=length, axis=0)[:token_count]
    long_out = conv_out + skip_gain * mixed
    gated = (query_gate * long_out).astype(jnp.bfloat16)
    output = jnp.dot(gated, w_out, preferred_element_type=jnp.float32).astype(jnp.bfloat16)
    grad_gated = lax.dot_general(g_out, w_out, (((1,), (1,)), ((), ())), preferred_element_type=jnp.float32)
    grad_long = grad_gated * query_gate
    grad_query = grad_gated * long_out
    grad_spec = jnp.fft.rfft(grad_long, n=length, axis=0)
    correlated = jnp.fft.irfft(jnp.conj(kernel_spec) * grad_spec, n=length, axis=0)[:token_count]
    grad_mixed = correlated + skip_gain * grad_long
    grad_filter = jnp.fft.irfft(jnp.conj(mixed_spec) * grad_spec, n=length, axis=0)[:token_count] * (1.0 / math.sqrt(token_count))
    grad_short = jnp.stack([grad_query, grad_mixed * value_short, grad_mixed * key_short])
    padded_grad = jnp.pad(grad_short, ((0, 0), (0, 2), (0, 0)))
    grad_qkv = (short_weight[:, 0, None, :] * padded_grad[:, :-2, :] + short_weight[:, 1, None, :] * padded_grad[:, 1:-1, :] + short_weight[:, 2, None, :] * padded_grad[:, 2:, :]).astype(jnp.bfloat16)
    return (output, grad_qkv, grad_filter)
```

```python
import math

import jax
import jax.numpy as jnp
import numpy as np
from jax import lax
from jax.experimental import pallas as pl
from jax.experimental.pallas import tpu as pltpu
from jax.sharding import PartitionSpec as P

HIGHEST = lax.Precision.HIGHEST
TWO_PI = 2.0 * math.pi
LANES = 128
HALF = 64
PHASES = 4
BF16 = jnp.bfloat16
F32 = jnp.float32
VMEM_LIMIT = 24 * 1024 * 1024


def passed_along(block, axis, distance):
    devices = range(lax.axis_size(axis))
    route = [(i - distance, i) for i in devices if i - distance in devices]
    return lax.ppermute(block, axis, route)


def phase_pair(left_count, right_count, period, left_start, right_start):
    left_idx = lax.broadcasted_iota(jnp.int32, (left_count, right_count), 0) + left_start
    right_idx = lax.broadcasted_iota(jnp.int32, (left_count, right_count), 1) + right_start
    angle_all = (left_idx * right_idx % period).astype(jnp.float32) * (TWO_PI / period)
    return (jnp.cos(angle_all), jnp.sin(angle_all))


def contract(pattern, matrix, values):
    return jnp.einsum(
        pattern, matrix, values, precision=HIGHEST, preferred_element_type=jnp.float32
    )


def forward_spectrum(signal):
    seq_parts = lax.axis_size("seq")
    row_count = signal.shape[0]
    row_share = row_count // seq_parts
    period = 2 * seq_parts * row_count
    spread_in = lax.all_to_all(signal[None], "seq", split_axis=1, concat_axis=0, tiled=True)
    outer_cos, outer_sin = phase_pair(2 * seq_parts, seq_parts, 2 * seq_parts, 0, 0)
    section_re = contract("cp,prw->crw", outer_cos, spread_in)
    section_im = -contract("cp,prw->crw", outer_sin, spread_in)
    twist_cos, twist_sin = phase_pair(
        2 * seq_parts, row_share, period, 0, lax.axis_index("seq") * row_share
    )
    twist_cos = twist_cos[:, :, None]
    twist_sin = twist_sin[:, :, None]
    turned_re = section_re * twist_cos + section_im * twist_sin
    turned_im = section_im * twist_cos - section_re * twist_sin
    inner_cos, inner_sin = phase_pair(row_count, row_count, row_count, 0, 0)
    piece_re = lax.all_to_all(turned_re, "seq", split_axis=0, concat_axis=1, tiled=True)
    piece_im = lax.all_to_all(turned_im, "seq", split_axis=0, concat_axis=1, tiled=True)
    spec_re = contract("dm,cmk->cdk", inner_cos, piece_re) + contract(
        "dm,cmk->cdk", inner_sin, piece_im
    )
    spec_im = contract("dm,cmk->cdk", inner_cos, piece_im) - contract(
        "dm,cmk->cdk", inner_sin, piece_re
    )
    return (spec_re, spec_im)


def time_signal(spec_re, spec_im):
    seq_parts = lax.axis_size("seq")
    row_count = spec_re.shape[1]
    period = 2 * seq_parts * row_count
    inner_cos, inner_sin = phase_pair(row_count, row_count, row_count, 0, 0)
    back_re = contract("md,cdk->cmk", inner_cos, spec_re) - contract(
        "md,cdk->cmk", inner_sin, spec_im
    )
    back_im = contract("md,cdk->cmk", inner_cos, spec_im) + contract(
        "md,cdk->cmk", inner_sin, spec_re
    )
    twist_cos, twist_sin = phase_pair(2, row_count, period, 2 * lax.axis_index("seq"), 0)
    twist_cos = twist_cos[:, :, None]
    twist_sin = twist_sin[:, :, None]
    turned_re = back_re * twist_cos - back_im * twist_sin
    turned_im = back_im * twist_cos + back_re * twist_sin
    outer_cos, outer_sin = phase_pair(seq_parts, 2 * seq_parts, 2 * seq_parts, 0, 0)
    piece_re = lax.all_to_all(turned_re, "seq", split_axis=1, concat_axis=0, tiled=True)
    piece_im = lax.all_to_all(turned_im, "seq", split_axis=1, concat_axis=0, tiled=True)
    summed = contract("pc,crk->prk", outer_cos, piece_re) - contract(
        "pc,crk->prk", outer_sin, piece_im
    )
    returned = summed * (1.0 / period)
    return lax.all_to_all(returned, "seq", split_axis=0, concat_axis=1, tiled=True)[0]


def spread_layer(qkv, filt, skip_gain, short_weight, w_out, g_out):
    row_count = qkv.shape[1]
    slab_width = qkv.shape[2]
    tail_rows = passed_along(qkv[:, row_count - 2 :, :], "seq", 1)
    extended = jnp.concatenate([tail_rows, qkv], axis=1)
    short = (
        short_weight[:, 0, None, :] * extended[:, 2:, :]
        + short_weight[:, 1, None, :] * extended[:, 1:-1, :]
        + short_weight[:, 2, None, :] * extended[:, :-2, :]
    )
    query_gate = short[0]
    key_short = short[1]
    value_short = short[2]
    mixed = key_short * value_short
    both_re, both_im = forward_spectrum(jnp.concatenate([mixed, filt], axis=1))
    signal_re = both_re[:, :, :slab_width]
    signal_im = both_im[:, :, :slab_width]
    kernel_re = both_re[:, :, slab_width:]
    kernel_im = both_im[:, :, slab_width:]
    conv_out = time_signal(
        signal_re * kernel_re - signal_im * kernel_im, signal_re * kernel_im + signal_im * kernel_re
    )
    long_out = conv_out + skip_gain * mixed
    gated_out = (query_gate * long_out).astype(jnp.bfloat16)
    projected = jnp.dot(
        lax.all_gather(gated_out, "ch", axis=1, tiled=True),
        w_out,
        preferred_element_type=jnp.float32,
    )
    output = projected.astype(jnp.bfloat16)
    grad_all = lax.all_gather(g_out, "ch", axis=1, tiled=True)
    rows_all = lax.all_to_all(w_out, "ch", split_axis=0, concat_axis=1, tiled=True)
    grad_gated = lax.dot_general(
        grad_all, rows_all, (((1,), (1,)), ((), ())), preferred_element_type=jnp.float32
    )
    grad_long = grad_gated * query_gate
    grad_query = grad_gated * long_out
    grad_re, grad_im = forward_spectrum(grad_long)
    pair_re = jnp.concatenate(
        [kernel_re * grad_re + kernel_im * grad_im, signal_re * grad_re + signal_im * grad_im],
        axis=2,
    )
    pair_im = jnp.concatenate(
        [kernel_re * grad_im - kernel_im * grad_re, signal_re * grad_im - signal_im * grad_re],
        axis=2,
    )
    pair_time = time_signal(pair_re, pair_im)
    grad_mixed = pair_time[:, :slab_width] + skip_gain * grad_long
    token_total = lax.axis_size("seq") * row_count
    grad_filter = pair_time[:, slab_width:] * (1.0 / math.sqrt(token_total))
    grad_short = jnp.stack([grad_query, grad_mixed * value_short, grad_mixed * key_short])
    head_rows = passed_along(grad_short[:, :2, :], "seq", -1)
    extended_grad = jnp.concatenate([grad_short, head_rows], axis=1)
    grad_qkv = (
        short_weight[:, 0, None, :] * extended_grad[:, :-2, :]
        + short_weight[:, 1, None, :] * extended_grad[:, 1:-1, :]
        + short_weight[:, 2, None, :] * extended_grad[:, 2:, :]
    ).astype(jnp.bfloat16)
    return (output, grad_qkv, grad_filter)


def split_bf16(values):
    high = values.astype(np.float32).astype(jnp.bfloat16)
    low = (values - high.astype(np.float64)).astype(np.float32).astype(jnp.bfloat16)
    return high, low


def phase_tables(tokens):
    quarter = tokens // PHASES
    freq = np.arange(quarter)[:, None]
    forward = []
    for phase in range(PHASES):
        time = PHASES * np.arange(quarter)[None, :] + phase
        turns = ((2 * freq + 1) * time) % (4 * tokens)
        angle = turns * (math.pi / (2 * tokens))
        forward.append(np.concatenate([np.cos(angle), -np.sin(angle)], axis=0))
    forward = np.stack(forward)
    backward = np.transpose(forward, (0, 2, 1)) * (1.0 / tokens)
    return split_bf16(forward), split_bf16(backward)


def row_order(rows):
    order = np.zeros((rows, rows), np.float32)
    share = rows // PHASES
    for phase in range(PHASES):
        for j in range(share):
            order[phase * share + j, PHASES * j + phase] = 1.0
    return order.astype(jnp.bfloat16)


def mm(a, b):
    return lax.dot_general(a, b, (((1,), (0,)), ((), ())), preferred_element_type=F32)


def low_lanes(shape):
    return lax.broadcasted_iota(jnp.int32, shape, 1) < HALF


def swap(x):
    return pltpu.roll(x, HALF, 1)


def call(kernel, out_shape, *args, flops=0):
    vmem = pl.BlockSpec(memory_space=pltpu.VMEM)
    outs = out_shape if isinstance(out_shape, (list, tuple)) else [out_shape]
    moved = sum(math.prod(a.shape) * a.dtype.itemsize for a in list(args) + list(outs))
    return pl.pallas_call(
        kernel,
        out_shape=out_shape,
        in_specs=[vmem] * len(args),
        out_specs=[vmem] * len(outs) if isinstance(out_shape, (list, tuple)) else vmem,
        compiler_params=pltpu.CompilerParams(vmem_limit_bytes=VMEM_LIMIT),
        cost_estimate=pl.CostEstimate(flops=flops, bytes_accessed=moved, transcendentals=0),
    )(*args)


def project_kernel(g_ref, w_ref, out_ref):
    for part in range(out_ref.shape[0]):
        width = out_ref.shape[2]
        out_ref[part] = lax.dot_general(
            g_ref[...],
            w_ref[part * width : (part + 1) * width, :],
            (((1,), (1,)), ((), ())),
            preferred_element_type=F32,
        ).astype(BF16)


def shifted(x, before):
    rows = lax.broadcasted_iota(jnp.int32, x.shape, 0)
    last, first = before[1:2, :], before[0:1, :]
    one = jnp.where(rows == 0, last, pltpu.roll(x, 1, 0))
    two = jnp.where(rows == 0, first, jnp.where(rows == 1, last, pltpu.roll(x, 2, 0)))
    return one, two


def advanced(x, after):
    count = x.shape[0]
    rows = lax.broadcasted_iota(jnp.int32, x.shape, 0)
    first, last = after[0:1, :], after[1:2, :]
    one = jnp.where(rows == count - 1, first, pltpu.roll(x, count - 1, 0))
    two = jnp.where(
        rows == count - 1, last, jnp.where(rows == count - 2, first, pltpu.roll(x, count - 2, 0))
    )
    return one, two


def short_kernel(qkv_ref, tail_ref, filt_ref, weight_ref, order_ref, short_ref, send_ref):
    for i in range(3):
        x = qkv_ref[i].astype(F32)
        one, two = shifted(x, tail_ref[i].astype(F32))
        short_ref[i] = (
            weight_ref[i, 0:1, :] * x + weight_ref[i, 1:2, :] * one + weight_ref[i, 2:3, :] * two
        )
    mixed = (short_ref[1] * short_ref[2]).astype(BF16)
    mixed = mm(order_ref[...], mixed)
    taps = mm(order_ref[...], filt_ref[...].astype(BF16))
    for tile in range(mixed.shape[1] // LANES):
        m = mixed[:, tile * LANES : (tile + 1) * LANES]
        f = taps[:, tile * LANES : (tile + 1) * LANES]
        low = low_lanes(m.shape)
        send_ref[2 * tile] = jnp.where(low, m, swap(f)).astype(BF16)
        send_ref[2 * tile + 1] = jnp.where(low, swap(m), f).astype(BF16)


def grad_kernel(parts_ref, short_ref, order_ref, gated_ref, send_ref):
    total = parts_ref[0].astype(F32)
    for part in range(1, parts_ref.shape[0]):
        total = total + parts_ref[part].astype(F32)
    gated_ref[...] = total
    grad_long = mm(order_ref[...], (total * short_ref[0]).astype(BF16))
    half = grad_long.shape[0] // 2
    for tile in range(grad_long.shape[1] // LANES):
        g = grad_long[:, tile * LANES : (tile + 1) * LANES]
        top, bottom = g[:half], g[half:]
        low = low_lanes(top.shape)
        send_ref[2 * tile] = jnp.where(low, top, swap(bottom)).astype(BF16)
        send_ref[2 * tile + 1] = jnp.where(low, swap(top), bottom).astype(BF16)


def spread_phases(parts):
    (a_re, a_im), (b_re, b_im), (c_re, c_im), (d_re, d_im) = parts
    s_re, s_im, t_re, t_im = a_re + c_re, a_im + c_im, a_re - c_re, a_im - c_im
    u_re, u_im, v_re, v_im = b_re + d_re, b_im + d_im, b_re - d_re, b_im - d_im
    return [
        (s_re + u_re, s_im + u_im),
        (t_re + v_im, t_im - v_re),
        (s_re - u_re, s_im - u_im),
        (t_re - v_im, t_im + v_re),
    ]


def gather_phases(parts):
    (a_re, a_im), (b_re, b_im), (c_re, c_im), (d_re, d_im) = parts
    s_re, s_im, t_re, t_im = a_re + c_re, a_im + c_im, a_re - c_re, a_im - c_im
    u_re, u_im, v_re, v_im = b_re + d_re, b_im + d_im, b_re - d_re, b_im - d_im
    return [
        (s_re + u_re, s_im + u_im),
        (t_re - v_im, t_im + v_re),
        (s_re - u_re, s_im - u_im),
        (t_re + v_im, t_im - v_re),
    ]


def rows_of(ref, start, count):
    block = ref[:, start : start + count, :]
    return block.reshape(ref.shape[0] * count, ref.shape[2])


def conv_kernel(recv_ref, fh_ref, fl_ref, bh_ref, bl_ref, spec_ref, send_ref):
    parts = []
    share = recv_ref.shape[1] // PHASES
    quarter = fh_ref.shape[2]
    for phase in range(PHASES):
        x = rows_of(recv_ref, phase * share, share)
        s = mm(fh_ref[phase], x) + mm(fl_ref[phase], x)
        parts.append((s[:quarter], s[quarter:]))
    products = []
    for r, (re, im) in enumerate(spread_phases(parts)):
        spec_ref[r, :quarter, :] = re
        spec_ref[r, quarter:, :] = im
        other_re, other_im = swap(re), swap(im)
        products.append((re * other_re - im * other_im, re * other_im + im * other_re))
    times = []
    low = low_lanes((2 * quarter, LANES))
    for phase, (re, im) in enumerate(gather_phases(products)):
        y = jnp.concatenate([re, im], axis=0)
        high = y.astype(BF16)
        rest = y - high.astype(F32)
        packed = jnp.where(low, high.astype(F32), rest).astype(BF16)
        t = mm(bh_ref[phase], packed)
        times.append(t + swap(t) + mm(bl_ref[phase], high))
    low = low_lanes((quarter, LANES))
    for phase in range(PHASES // 2):
        t = jnp.where(low, times[phase], times[phase + 2]).astype(BF16)
        send_ref[:, phase * share : (phase + 1) * share, :] = t.reshape(
            send_ref.shape[0], share, LANES
        )


def corr_kernel(recv_ref, spec_ref, fh_ref, fl_ref, bh_ref, bl_ref, send_ref):
    blocks = recv_ref.shape[0]
    share = recv_ref.shape[1] * 2 // PHASES
    quarter = fh_ref.shape[2]
    parts = []
    low = low_lanes((2 * quarter, LANES))
    for phase in range(PHASES):
        x = rows_of(recv_ref, phase % 2 * share, share)
        s = mm(fh_ref[phase], x) + mm(fl_ref[phase], x)
        turned = swap(s)
        s = jnp.where(low, s, turned) if phase < 2 else jnp.where(low, turned, s)
        parts.append((s[:quarter], s[quarter:]))
    products = []
    for r, (re, im) in enumerate(spread_phases(parts)):
        k_re, k_im = spec_ref[r, :quarter, :], spec_ref[r, quarter:, :]
        products.append((k_re * re + k_im * im, k_re * im - k_im * re))
    low = low_lanes((quarter, LANES))
    scale = jnp.where(low, 1.0 / math.sqrt(PHASES * quarter), 1.0)
    rows = PHASES * share
    send_ref[:, rows:, :] = jnp.zeros((blocks, send_ref.shape[1] - rows, LANES), BF16)
    heads = []
    for phase, (re, im) in enumerate(gather_phases(products)):
        y = jnp.concatenate([re, im], axis=0)
        high = y.astype(BF16)
        rest = (y - high.astype(F32)).astype(BF16)
        t = mm(bh_ref[phase], high) + mm(bh_ref[phase], rest) + mm(bl_ref[phase], high)
        t = t * scale
        send_ref[:, phase * share : (phase + 1) * share, :] = t.astype(BF16).reshape(
            blocks, share, LANES
        )
        if phase < 2:
            heads.append(t)
    extra = send_ref.shape[1] - rows
    row = lax.broadcasted_iota(jnp.int32, (extra, LANES), 0)
    for block in range(blocks - 1):
        at = (block + 1) * share
        first, second = heads[0][at : at + 1, :], heads[1][at : at + 1, :]
        send_ref[block, rows:, :] = jnp.where(
            row == 0, first, jnp.where(row == 1, second, 0.0)
        ).astype(BF16)


def gate_kernel(recv_ref, short_ref, grad_gated_ref, gain_ref, order_ref, gated_ref, query_ref, head_ref):
    low = low_lanes((recv_ref.shape[1], LANES))
    tiles = []
    for tile in range(recv_ref.shape[0] // 2):
        a = recv_ref[2 * tile].astype(F32)
        b = recv_ref[2 * tile + 1].astype(F32)
        top = jnp.where(low, a, swap(b))
        bottom = jnp.where(low, swap(a), b)
        tiles.append(jnp.concatenate([top, bottom], axis=0))
    conv = mm(order_ref[...], jnp.concatenate(tiles, axis=1).astype(BF16))
    query, key, value = short_ref[0], short_ref[1], short_ref[2]
    long_out = conv + gain_ref[...] * (key * value)
    gated_ref[...] = (query * long_out).astype(BF16)
    grad_gated = grad_gated_ref[...]
    grad_query = grad_gated * long_out
    query_ref[...] = grad_query
    head_ref[0:2, :] = grad_query[0:2, :]
    head_ref[2:4, :] = gain_ref[...] * (grad_gated[0:2, :] * query[0:2, :])
    head_ref[4:6, :] = key[0:2, :]
    head_ref[6:8, :] = value[0:2, :]


def close_kernel(
    recv_ref, short_ref, grad_gated_ref, query_ref, next_ref, gain_ref, weight_ref, order_ref,
    grad_ref, filter_ref,
):
    rows = grad_ref.shape[1]
    low = low_lanes((recv_ref.shape[1], LANES))
    filters, mixes = [], []
    for tile in range(recv_ref.shape[0] // 2):
        a = recv_ref[2 * tile].astype(F32)
        b = recv_ref[2 * tile + 1].astype(F32)
        filters.append(jnp.where(low, a, swap(b))[:rows])
        mixes.append(jnp.where(low, swap(a), b))
    filter_ref[...] = mm(order_ref[...], jnp.concatenate(filters, axis=1).astype(BF16))
    mixes = jnp.concatenate(mixes, axis=1)
    gain = gain_ref[...]
    grad_long = grad_gated_ref[...] * short_ref[0]
    grad_mixed = mm(order_ref[...], mixes[:rows].astype(BF16)) + gain * grad_long
    heads = next_ref[...]
    next_mixed = mixes[rows : rows + 2] + heads[2:4]
    key, value = short_ref[1], short_ref[2]
    grads = [query_ref[...], grad_mixed * value, grad_mixed * key]
    afters = [heads[0:2], next_mixed * heads[6:8], next_mixed * heads[4:6]]
    for i in range(3):
        one, two = advanced(grads[i], afters[i])
        grad_ref[i] = (
            weight_ref[i, 0:1, :] * grads[i]
            + weight_ref[i, 1:2, :] * one
            + weight_ref[i, 2:3, :] * two
        ).astype(BF16)


def exchanged(x, axis):
    return lax.all_to_all(x, axis, split_axis=0, concat_axis=0, tiled=True)


def owner_layer(qkv, filt, skip_gain, short_weight, w_out, g_out):
    shape = jax.ShapeDtypeStruct
    seq_parts, ch_parts = lax.axis_size("seq"), lax.axis_size("ch")
    rows, width = qkv.shape[1], qkv.shape[2]
    tokens = seq_parts * rows
    (fh, fl), (bh, bl) = phase_tables(tokens)
    order = row_order(rows)
    back_order = order.T
    gain = skip_gain[None, :]
    tables = (fh, fl, bh, bl)
    table_flops = 2 * 2 * tokens * tokens // PHASES * 2 * LANES

    tail_rows = passed_along(qkv[:, rows - 2 :, :], "seq", 1)
    partial = call(
        project_kernel,
        shape((ch_parts, rows, width), BF16),
        g_out,
        w_out,
        flops=2 * rows * width * width * ch_parts,
    )
    partial = exchanged(partial, "ch")
    short, send = call(
        short_kernel,
        [shape((3, rows, width), F32), shape((seq_parts, rows, LANES), BF16)],
        qkv,
        tail_rows,
        filt,
        short_weight,
        order,
    )
    recv = exchanged(send, "seq")
    grad_gated, send = call(
        grad_kernel,
        [shape((rows, width), F32), shape((seq_parts, rows // 2, LANES), BF16)],
        partial,
        short,
        order,
    )
    grad_recv = exchanged(send, "seq")
    spec, send = call(
        conv_kernel,
        [shape((PHASES, tokens // 2, LANES), F32), shape((seq_parts, rows // 2, LANES), BF16)],
        recv,
        *tables,
        flops=table_flops,
    )
    conv_recv = exchanged(send, "seq")
    send = call(
        corr_kernel,
        shape((seq_parts, rows + 16, LANES), BF16),
        grad_recv,
        spec,
        *tables,
        flops=table_flops,
    )
    corr_recv = exchanged(send, "seq")
    gated, grad_query, heads = call(
        gate_kernel,
        [shape((rows, width), BF16), shape((rows, width), F32), shape((8, width), F32)],
        conv_recv,
        short,
        grad_gated,
        gain,
        back_order,
    )
    next_heads = passed_along(heads, "seq", -1)
    projected = jnp.dot(
        lax.all_gather(gated, "ch", axis=1, tiled=True), w_out, preferred_element_type=F32
    )
    output = projected.astype(BF16)
    grad_qkv, grad_filter = call(
        close_kernel,
        [shape((3, rows, width), BF16), shape((rows, width), F32)],
        corr_recv,
        short,
        grad_gated,
        grad_query,
        next_heads,
        gain,
        short_weight,
        back_order,
    )
    return (output, grad_qkv, grad_filter)


def local(qkv, filt, skip_gain, short_weight, w_out, g_out):
    seq_parts = lax.axis_size("seq")
    rows, width = qkv.shape[1], qkv.shape[2]
    if width == HALF * seq_parts and rows % HALF == 0 and rows * seq_parts <= 2048:
        return owner_layer(qkv, filt, skip_gain, short_weight, w_out, g_out)
    return spread_layer(qkv, filt, skip_gain, short_weight, w_out, g_out)


def solution(mesh):
    in_specs = (
        P(None, "seq", "ch"),
        P("seq", "ch"),
        P("ch"),
        P(None, None, "ch"),
        P(None, "ch"),
        P("seq", "ch"),
    )
    out_specs = (P("seq", "ch"), P(None, "seq", "ch"), P("seq", "ch"))
    return jax.shard_map(local, mesh=mesh, in_specs=in_specs, out_specs=out_specs, check_vma=False)
```

```python
import functools
import math

import jax
import jax.numpy as jnp
import numpy as np
from jax import lax
from jax.experimental import pallas as pl
from jax.experimental.pallas import tpu as pltpu
from jax.sharding import PartitionSpec as P

HIGHEST = lax.Precision.HIGHEST
TWO_PI = 2.0 * math.pi
LANES = 128
HALF = 64
PHASES = 4
BF16 = jnp.bfloat16
F32 = jnp.float32
VMEM_LIMIT = 24 * 1024 * 1024


def passed_along(block, axis, distance):
    devices = range(lax.axis_size(axis))
    route = [(i - distance, i) for i in devices if i - distance in devices]
    return lax.ppermute(block, axis, route)


def phase_pair(left_count, right_count, period, left_start, right_start):
    left_idx = lax.broadcasted_iota(jnp.int32, (left_count, right_count), 0) + left_start
    right_idx = lax.broadcasted_iota(jnp.int32, (left_count, right_count), 1) + right_start
    angle_all = (left_idx * right_idx % period).astype(jnp.float32) * (TWO_PI / period)
    return (jnp.cos(angle_all), jnp.sin(angle_all))


def contract(pattern, matrix, values):
    return jnp.einsum(
        pattern, matrix, values, precision=HIGHEST, preferred_element_type=jnp.float32
    )


def forward_spectrum(signal):
    seq_parts = lax.axis_size("seq")
    row_count = signal.shape[0]
    row_share = row_count // seq_parts
    period = 2 * seq_parts * row_count
    spread_in = lax.all_to_all(signal[None], "seq", split_axis=1, concat_axis=0, tiled=True)
    outer_cos, outer_sin = phase_pair(2 * seq_parts, seq_parts, 2 * seq_parts, 0, 0)
    section_re = contract("cp,prw->crw", outer_cos, spread_in)
    section_im = -contract("cp,prw->crw", outer_sin, spread_in)
    twist_cos, twist_sin = phase_pair(
        2 * seq_parts, row_share, period, 0, lax.axis_index("seq") * row_share
    )
    twist_cos = twist_cos[:, :, None]
    twist_sin = twist_sin[:, :, None]
    turned_re = section_re * twist_cos + section_im * twist_sin
    turned_im = section_im * twist_cos - section_re * twist_sin
    inner_cos, inner_sin = phase_pair(row_count, row_count, row_count, 0, 0)
    piece_re = lax.all_to_all(turned_re, "seq", split_axis=0, concat_axis=1, tiled=True)
    piece_im = lax.all_to_all(turned_im, "seq", split_axis=0, concat_axis=1, tiled=True)
    spec_re = contract("dm,cmk->cdk", inner_cos, piece_re) + contract(
        "dm,cmk->cdk", inner_sin, piece_im
    )
    spec_im = contract("dm,cmk->cdk", inner_cos, piece_im) - contract(
        "dm,cmk->cdk", inner_sin, piece_re
    )
    return (spec_re, spec_im)


def time_signal(spec_re, spec_im):
    seq_parts = lax.axis_size("seq")
    row_count = spec_re.shape[1]
    period = 2 * seq_parts * row_count
    inner_cos, inner_sin = phase_pair(row_count, row_count, row_count, 0, 0)
    back_re = contract("md,cdk->cmk", inner_cos, spec_re) - contract(
        "md,cdk->cmk", inner_sin, spec_im
    )
    back_im = contract("md,cdk->cmk", inner_cos, spec_im) + contract(
        "md,cdk->cmk", inner_sin, spec_re
    )
    twist_cos, twist_sin = phase_pair(2, row_count, period, 2 * lax.axis_index("seq"), 0)
    twist_cos = twist_cos[:, :, None]
    twist_sin = twist_sin[:, :, None]
    turned_re = back_re * twist_cos - back_im * twist_sin
    turned_im = back_im * twist_cos + back_re * twist_sin
    outer_cos, outer_sin = phase_pair(seq_parts, 2 * seq_parts, 2 * seq_parts, 0, 0)
    piece_re = lax.all_to_all(turned_re, "seq", split_axis=1, concat_axis=0, tiled=True)
    piece_im = lax.all_to_all(turned_im, "seq", split_axis=1, concat_axis=0, tiled=True)
    summed = contract("pc,crk->prk", outer_cos, piece_re) - contract(
        "pc,crk->prk", outer_sin, piece_im
    )
    returned = summed * (1.0 / period)
    return lax.all_to_all(returned, "seq", split_axis=0, concat_axis=1, tiled=True)[0]


def spread_layer(qkv, filt, skip_gain, short_weight, w_out, g_out):
    row_count = qkv.shape[1]
    slab_width = qkv.shape[2]
    tail_rows = passed_along(qkv[:, row_count - 2 :, :], "seq", 1)
    extended = jnp.concatenate([tail_rows, qkv], axis=1)
    short = (
        short_weight[:, 0, None, :] * extended[:, 2:, :]
        + short_weight[:, 1, None, :] * extended[:, 1:-1, :]
        + short_weight[:, 2, None, :] * extended[:, :-2, :]
    )
    query_gate = short[0]
    key_short = short[1]
    value_short = short[2]
    mixed = key_short * value_short
    both_re, both_im = forward_spectrum(jnp.concatenate([mixed, filt], axis=1))
    signal_re = both_re[:, :, :slab_width]
    signal_im = both_im[:, :, :slab_width]
    kernel_re = both_re[:, :, slab_width:]
    kernel_im = both_im[:, :, slab_width:]
    conv_out = time_signal(
        signal_re * kernel_re - signal_im * kernel_im, signal_re * kernel_im + signal_im * kernel_re
    )
    long_out = conv_out + skip_gain * mixed
    gated_out = (query_gate * long_out).astype(jnp.bfloat16)
    projected = jnp.dot(
        lax.all_gather(gated_out, "ch", axis=1, tiled=True),
        w_out,
        preferred_element_type=jnp.float32,
    )
    output = projected.astype(jnp.bfloat16)
    grad_all = lax.all_gather(g_out, "ch", axis=1, tiled=True)
    rows_all = lax.all_to_all(w_out, "ch", split_axis=0, concat_axis=1, tiled=True)
    grad_gated = lax.dot_general(
        grad_all, rows_all, (((1,), (1,)), ((), ())), preferred_element_type=jnp.float32
    )
    grad_long = grad_gated * query_gate
    grad_query = grad_gated * long_out
    grad_re, grad_im = forward_spectrum(grad_long)
    pair_re = jnp.concatenate(
        [kernel_re * grad_re + kernel_im * grad_im, signal_re * grad_re + signal_im * grad_im],
        axis=2,
    )
    pair_im = jnp.concatenate(
        [kernel_re * grad_im - kernel_im * grad_re, signal_re * grad_im - signal_im * grad_re],
        axis=2,
    )
    pair_time = time_signal(pair_re, pair_im)
    grad_mixed = pair_time[:, :slab_width] + skip_gain * grad_long
    token_total = lax.axis_size("seq") * row_count
    grad_filter = pair_time[:, slab_width:] * (1.0 / math.sqrt(token_total))
    grad_short = jnp.stack([grad_query, grad_mixed * value_short, grad_mixed * key_short])
    head_rows = passed_along(grad_short[:, :2, :], "seq", -1)
    extended_grad = jnp.concatenate([grad_short, head_rows], axis=1)
    grad_qkv = (
        short_weight[:, 0, None, :] * extended_grad[:, :-2, :]
        + short_weight[:, 1, None, :] * extended_grad[:, 1:-1, :]
        + short_weight[:, 2, None, :] * extended_grad[:, 2:, :]
    ).astype(jnp.bfloat16)
    return (output, grad_qkv, grad_filter)


def split_bf16(values):
    high = values.astype(np.float32).astype(jnp.bfloat16)
    low = (values - high.astype(np.float64)).astype(np.float32).astype(jnp.bfloat16)
    return high, low


def phase_tables(tokens):
    quarter = tokens // PHASES
    freq = 2 * np.arange(quarter)[:, None] + 1
    turn = math.pi / (2 * tokens)
    angle = (freq * PHASES * np.arange(quarter)[None, :] % (4 * tokens)) * turn
    forward = np.concatenate([np.cos(angle), -np.sin(angle)], axis=0)
    backward = np.transpose(forward) * (1.0 / tokens)
    angle = freq * np.arange(PHASES)[None, :] * turn
    twist = np.concatenate([np.cos(angle), np.sin(angle)], axis=1).astype(np.float32)
    twist = np.pad(twist, ((0, 0), (0, LANES - 2 * PHASES)))
    return (*split_bf16(forward), *split_bf16(backward), twist)


def row_order(rows):
    order = np.zeros((rows, rows), np.float32)
    share = rows // PHASES
    for phase in range(PHASES):
        for j in range(share):
            order[phase * share + j, PHASES * j + phase] = 1.0
    return order.astype(jnp.bfloat16)


def mm(a, b):
    return lax.dot_general(a, b, (((1,), (0,)), ((), ())), preferred_element_type=F32)


def low_lanes(shape):
    return lax.broadcasted_iota(jnp.int32, shape, 1) < HALF


def swap(x):
    return pltpu.roll(x, HALF, 1)


def call(kernel, out_shape, *args, flops=0, in_place=(), scratch=()):
    vmem = pl.BlockSpec(memory_space=pltpu.VMEM)
    anywhere = pl.BlockSpec(memory_space=pl.ANY)
    outs = out_shape if isinstance(out_shape, (list, tuple)) else [out_shape]
    moved = sum(math.prod(a.shape) * a.dtype.itemsize for a in list(args) + list(outs))
    return pl.pallas_call(
        kernel,
        out_shape=out_shape,
        in_specs=[anywhere if i in in_place else vmem for i in range(len(args))],
        out_specs=[vmem] * len(outs) if isinstance(out_shape, (list, tuple)) else vmem,
        scratch_shapes=list(scratch),
        compiler_params=pltpu.CompilerParams(vmem_limit_bytes=VMEM_LIMIT),
        cost_estimate=pl.CostEstimate(flops=flops, bytes_accessed=moved, transcendentals=0),
    )(*args)


def project_kernel(count, *refs):
    g_in, w_in, loads = refs[0], refs[1], refs[2 : 2 + count]
    out_ref, w_ref, kept = refs[2 + count], refs[3 + count], refs[4 + count : 4 + 2 * count]
    g_ref, sems = refs[4 + 2 * count :]
    parts, _, width = out_ref.shape
    first = pltpu.make_async_copy(g_in, g_ref, sems.at[0])
    first.start()
    chunks = []
    for part in range(parts):
        rows = pl.ds(part * width, width)
        chunks.append(pltpu.make_async_copy(w_in.at[rows], w_ref.at[rows], sems.at[1 + part]))
        chunks[-1].start()
    others = []
    for i in range(count):
        others.append(pltpu.make_async_copy(loads[i], kept[i], sems.at[1 + parts + i]))
        others[-1].start()
    first.wait()
    for part in range(parts):
        chunks[part].wait()
        out_ref[part] = lax.dot_general(
            g_ref[...],
            w_ref[part * width : (part + 1) * width, :],
            (((1,), (1,)), ((), ())),
            preferred_element_type=F32,
        ).astype(BF16)
    for copy in others:
        copy.wait()


def shifted(x, before):
    rows = lax.broadcasted_iota(jnp.int32, x.shape, 0)
    last, first = before[1:2, :], before[0:1, :]
    one = jnp.where(rows == 0, last, pltpu.roll(x, 1, 0))
    two = jnp.where(rows == 0, first, jnp.where(rows == 1, last, pltpu.roll(x, 2, 0)))
    return one, two


def advanced(x, after):
    count = x.shape[0]
    rows = lax.broadcasted_iota(jnp.int32, x.shape, 0)
    first, last = after[0:1, :], after[1:2, :]
    one = jnp.where(rows == count - 1, first, pltpu.roll(x, count - 1, 0))
    two = jnp.where(
        rows == count - 1, last, jnp.where(rows == count - 2, first, pltpu.roll(x, count - 2, 0))
    )
    return one, two


def short_kernel(qkv_ref, tail_ref, filt_ref, weight_ref, order_ref, short_ref, send_ref):
    for i in range(3):
        x = qkv_ref[i].astype(F32)
        one, two = shifted(x, tail_ref[i].astype(F32))
        short_ref[i] = (
            weight_ref[i, 0:1, :] * x + weight_ref[i, 1:2, :] * one + weight_ref[i, 2:3, :] * two
        )
    mixed = (short_ref[1] * short_ref[2]).astype(BF16)
    mixed = mm(order_ref[...], mixed)
    taps = mm(order_ref[...], filt_ref[...].astype(BF16))
    for tile in range(mixed.shape[1] // LANES):
        m = mixed[:, tile * LANES : (tile + 1) * LANES]
        f = taps[:, tile * LANES : (tile + 1) * LANES]
        low = low_lanes(m.shape)
        send_ref[2 * tile] = jnp.where(low, m, swap(f)).astype(BF16)
        send_ref[2 * tile + 1] = jnp.where(low, swap(m), f).astype(BF16)


def grad_kernel(parts_ref, short_ref, order_ref, gated_ref, send_ref):
    total = parts_ref[0].astype(F32)
    for part in range(1, parts_ref.shape[0]):
        total = total + parts_ref[part].astype(F32)
    gated_ref[...] = total
    grad_long = mm(order_ref[...], (total * short_ref[0]).astype(BF16))
    half = grad_long.shape[0] // 2
    for tile in range(grad_long.shape[1] // LANES):
        g = grad_long[:, tile * LANES : (tile + 1) * LANES]
        top, bottom = g[:half], g[half:]
        low = low_lanes(top.shape)
        send_ref[2 * tile] = jnp.where(low, top, swap(bottom)).astype(BF16)
        send_ref[2 * tile + 1] = jnp.where(low, swap(top), bottom).astype(BF16)


def spread_phases(parts):
    (a_re, a_im), (b_re, b_im), (c_re, c_im), (d_re, d_im) = parts
    s_re, s_im, t_re, t_im = a_re + c_re, a_im + c_im, a_re - c_re, a_im - c_im
    u_re, u_im, v_re, v_im = b_re + d_re, b_im + d_im, b_re - d_re, b_im - d_im
    return [
        (s_re + u_re, s_im + u_im),
        (t_re + v_im, t_im - v_re),
        (s_re - u_re, s_im - u_im),
        (t_re - v_im, t_im + v_re),
    ]


def gather_phases(parts):
    (a_re, a_im), (b_re, b_im), (c_re, c_im), (d_re, d_im) = parts
    s_re, s_im, t_re, t_im = a_re + c_re, a_im + c_im, a_re - c_re, a_im - c_im
    u_re, u_im, v_re, v_im = b_re + d_re, b_im + d_im, b_re - d_re, b_im - d_im
    return [
        (s_re + u_re, s_im + u_im),
        (t_re - v_im, t_im + v_re),
        (s_re - u_re, s_im - u_im),
        (t_re + v_im, t_im - v_re),
    ]


def rows_of(ref, start, count):
    block = ref[:, start : start + count, :]
    return block.reshape(ref.shape[0] * count, ref.shape[2])


def turned_back(re, im, twist, phase):
    if phase == 0:
        return re, im
    c, s = twist[:, phase : phase + 1], twist[:, PHASES + phase : PHASES + phase + 1]
    return re * c + im * s, im * c - re * s


def turned_on(re, im, twist, phase):
    if phase == 0:
        return re, im
    c, s = twist[:, phase : phase + 1], twist[:, PHASES + phase : PHASES + phase + 1]
    return re * c - im * s, re * s + im * c


def lane_tile(x, index):
    return x[:, index * LANES : (index + 1) * LANES]


def conv_kernel(recv_ref, fh_ref, fl_ref, bh_ref, bl_ref, twist_ref, spec_ref, send_ref):
    share = recv_ref.shape[1] // PHASES
    quarter = fh_ref.shape[1]
    twist = twist_ref[...]
    x = jnp.concatenate([rows_of(recv_ref, p * share, share) for p in range(PHASES)], axis=1)
    s = mm(fh_ref[...], x) + mm(fl_ref[...], x)
    parts = []
    for phase in range(PHASES):
        t = lane_tile(s, phase)
        parts.append(turned_back(t[:quarter], t[quarter:], twist, phase))
    products = []
    for r, (re, im) in enumerate(spread_phases(parts)):
        spec_ref[r, :quarter, :] = re
        spec_ref[r, quarter:, :] = im
        other_re, other_im = swap(re), swap(im)
        products.append((re * other_re - im * other_im, re * other_im + im * other_re))
    highs, packs = [], []
    low = low_lanes((2 * quarter, LANES))
    for phase, (re, im) in enumerate(gather_phases(products)):
        y = jnp.concatenate(turned_on(re, im, twist, phase), axis=0)
        high = y.astype(BF16)
        highs.append(high)
        high = high.astype(F32)
        packs.append(jnp.where(low, high, y - high).astype(BF16))
    main = mm(bh_ref[...], jnp.concatenate(packs, axis=1))
    rest = mm(bl_ref[...], jnp.concatenate(highs, axis=1))
    times = []
    for phase in range(PHASES):
        t = lane_tile(main, phase)
        times.append(t + swap(t) + lane_tile(rest, phase))
    low = low_lanes((quarter, LANES))
    for phase in range(PHASES // 2):
        t = jnp.where(low, times[phase], times[phase + 2]).astype(BF16)
        send_ref[:, phase * share : (phase + 1) * share, :] = t.reshape(
            send_ref.shape[0], share, LANES
        )


def corr_kernel(recv_ref, spec_ref, fh_ref, fl_ref, bh_ref, bl_ref, twist_ref, send_ref):
    blocks = recv_ref.shape[0]
    share = recv_ref.shape[1] * 2 // PHASES
    quarter = fh_ref.shape[1]
    twist = twist_ref[...]
    x = jnp.concatenate([rows_of(recv_ref, p * share, share) for p in range(2)], axis=1)
    s = mm(fh_ref[...], x) + mm(fl_ref[...], x)
    parts = []
    low = low_lanes((2 * quarter, LANES))
    for phase in range(PHASES):
        t = lane_tile(s, phase % 2)
        t = jnp.where(low, t, swap(t)) if phase < 2 else jnp.where(low, swap(t), t)
        parts.append(turned_back(t[:quarter], t[quarter:], twist, phase))
    products = []
    for r, (re, im) in enumerate(spread_phases(parts)):
        k_re, k_im = spec_ref[r, :quarter, :], spec_ref[r, quarter:, :]
        products.append((k_re * re + k_im * im, k_re * im - k_im * re))
    highs, rests = [], []
    for phase, (re, im) in enumerate(gather_phases(products)):
        y = jnp.concatenate(turned_on(re, im, twist, phase), axis=0)
        highs.append(y.astype(BF16))
        rests.append((y - highs[-1].astype(F32)).astype(BF16))
    highs, rests = jnp.concatenate(highs, axis=1), jnp.concatenate(rests, axis=1)
    times = mm(bh_ref[...], highs) + mm(bh_ref[...], rests) + mm(bl_ref[...], highs)
    low = low_lanes((quarter, LANES))
    scale = jnp.where(low, 1.0 / math.sqrt(PHASES * quarter), 1.0)
    rows = PHASES * share
    heads = []
    for phase in range(PHASES):
        t = lane_tile(times, phase) * scale
        send_ref[:, phase * share : (phase + 1) * share, :] = t.astype(BF16).reshape(
            blocks, share, LANES
        )
        heads.append(t)
    extra = send_ref.shape[1] - rows
    row = lax.broadcasted_iota(jnp.int32, (extra, LANES), 0)
    for block in range(blocks):
        at = (block + 1) % blocks * share
        first, second = heads[0][at : at + 1, :], heads[1][at : at + 1, :]
        after = jnp.where(row == 0, first, jnp.where(row == 1, second, 0.0))
        if block == blocks - 1:
            after = jnp.zeros_like(after)
        send_ref[block, rows:, :] = after.astype(BF16)


def gate_kernel(recv_ref, short_ref, grad_gated_ref, gain_ref, order_ref, gated_ref, query_ref, head_ref):
    low = low_lanes((recv_ref.shape[1], LANES))
    tiles = []
    for tile in range(recv_ref.shape[0] // 2):
        a = recv_ref[2 * tile].astype(F32)
        b = recv_ref[2 * tile + 1].astype(F32)
        top = jnp.where(low, a, swap(b))
        bottom = jnp.where(low, swap(a), b)
        tiles.append(jnp.concatenate([top, bottom], axis=0))
    conv = mm(order_ref[...], jnp.concatenate(tiles, axis=1).astype(BF16))
    query, key, value = short_ref[0], short_ref[1], short_ref[2]
    long_out = conv + gain_ref[...] * (key * value)
    gated_ref[...] = (query * long_out).astype(BF16)
    grad_gated = grad_gated_ref[...]
    grad_query = grad_gated * long_out
    query_ref[...] = grad_query
    head_ref[0:2, :] = grad_query[0:2, :]
    head_ref[2:4, :] = gain_ref[...] * (grad_gated[0:2, :] * query[0:2, :])
    head_ref[4:6, :] = key[0:2, :]
    head_ref[6:8, :] = value[0:2, :]


def close_kernel(
    recv_ref, short_ref, grad_gated_ref, query_ref, next_ref, gain_ref, weight_ref, order_ref,
    grad_ref, filter_ref,
):
    rows = grad_ref.shape[1]
    low = low_lanes((recv_ref.shape[1], LANES))
    filters, mixes = [], []
    for tile in range(recv_ref.shape[0] // 2):
        a = recv_ref[2 * tile].astype(F32)
        b = recv_ref[2 * tile + 1].astype(F32)
        filters.append(jnp.where(low, a, swap(b))[:rows])
        mixes.append(jnp.where(low, swap(a), b))
    filter_ref[...] = mm(order_ref[...], jnp.concatenate(filters, axis=1).astype(BF16))
    mixes = jnp.concatenate(mixes, axis=1)
    gain = gain_ref[...]
    grad_long = grad_gated_ref[...] * short_ref[0]
    grad_mixed = mm(order_ref[...], mixes[:rows].astype(BF16)) + gain * grad_long
    heads = next_ref[...]
    next_mixed = mixes[rows : rows + 2] + heads[2:4]
    key, value = short_ref[1], short_ref[2]
    grads = [query_ref[...], grad_mixed * value, grad_mixed * key]
    afters = [heads[0:2], next_mixed * heads[6:8], next_mixed * heads[4:6]]
    for i in range(3):
        one, two = advanced(grads[i], afters[i])
        grad_ref[i] = (
            weight_ref[i, 0:1, :] * grads[i]
            + weight_ref[i, 1:2, :] * one
            + weight_ref[i, 2:3, :] * two
        ).astype(BF16)


def output_kernel(own_ref, near_ref, across_ref, far_ref, w_ref, out_ref):
    width = own_ref.shape[1]
    me = lax.axis_index("ch")
    total = None
    for i, ref in enumerate((own_ref, near_ref, across_ref, far_ref)):
        rows = pl.ds(pl.multiple_of((me ^ i) * width, width), width)
        term = mm(ref[...], w_ref[rows, :])
        total = term if total is None else total + term
    out_ref[...] = total.astype(BF16)


def exchanged(x, axis):
    return lax.all_to_all(x, axis, split_axis=0, concat_axis=0, tiled=True)


def partner(x, axis, mask):
    return lax.ppermute(x, axis, [(i, i ^ mask) for i in range(lax.axis_size(axis))])


def owner_layer(qkv, filt, skip_gain, short_weight, w_out, g_out):
    shape = jax.ShapeDtypeStruct
    seq_parts, ch_parts = lax.axis_size("seq"), lax.axis_size("ch")
    rows, width = qkv.shape[1], qkv.shape[2]
    tokens = seq_parts * rows
    order = row_order(rows)
    tables = phase_tables(tokens)
    table_flops = 2 * 2 * 2 * tokens * tokens // PHASES * LANES
    tail_rows = passed_along(qkv[:, rows - 2 :, :], "seq", 1)
    loads = [qkv, filt, short_weight, skip_gain[None, :], order, order.T, *tables]
    partial, w_kept, *kept = call(
        functools.partial(project_kernel, len(loads)),
        [shape((ch_parts, rows, width), BF16), shape(w_out.shape, BF16)]
        + [shape(x.shape, x.dtype) for x in loads],
        g_out,
        w_out,
        *loads,
        flops=2 * rows * width * width * ch_parts,
        in_place=range(2 + len(loads)),
        scratch=[
            pltpu.VMEM(g_out.shape, BF16),
            pltpu.SemaphoreType.DMA((1 + ch_parts + len(loads),)),
        ],
    )
    qkv, filt, short_weight, gain, order, back_order, *tables = kept
    partial = exchanged(partial, "ch")
    short, send = call(
        short_kernel,
        [shape((3, rows, width), F32), shape((seq_parts, rows, LANES), BF16)],
        qkv,
        tail_rows,
        filt,
        short_weight,
        order,
    )
    recv = exchanged(send, "seq")
    grad_gated, send = call(
        grad_kernel,
        [shape((rows, width), F32), shape((seq_parts, rows // 2, LANES), BF16)],
        partial,
        short,
        order,
    )
    grad_recv = exchanged(send, "seq")
    spec, send = call(
        conv_kernel,
        [shape((PHASES, tokens // 2, LANES), F32), shape((seq_parts, rows // 2, LANES), BF16)],
        recv,
        *tables,
        flops=table_flops,
    )
    conv_recv = exchanged(send, "seq")
    send = call(
        corr_kernel,
        shape((seq_parts, rows + 16, LANES), BF16),
        grad_recv,
        spec,
        *tables,
        flops=table_flops,
    )
    corr_recv = exchanged(send, "seq")
    gated, grad_query, heads = call(
        gate_kernel,
        [shape((rows, width), BF16), shape((rows, width), F32), shape((8, width), F32)],
        conv_recv,
        short,
        grad_gated,
        gain,
        back_order,
    )
    next_heads = passed_along(heads, "seq", -1)
    others = [partner(gated, "ch", mask) for mask in (1, 2, 3)]
    grad_qkv, grad_filter = call(
        close_kernel,
        [shape((3, rows, width), BF16), shape((rows, width), F32)],
        corr_recv,
        short,
        grad_gated,
        grad_query,
        next_heads,
        gain,
        short_weight,
        back_order,
    )
    output = call(
        output_kernel,
        shape((rows, width), BF16),
        gated,
        *others,
        w_kept,
        flops=2 * rows * width * width * ch_parts,
    )
    return (output, grad_qkv, grad_filter)


def local(qkv, filt, skip_gain, short_weight, w_out, g_out):
    seq_parts = lax.axis_size("seq")
    rows, width = qkv.shape[1], qkv.shape[2]
    fits = width == HALF * seq_parts and rows % HALF == 0 and rows * seq_parts <= 2048
    if fits and lax.axis_size("ch") == 4:
        return owner_layer(qkv, filt, skip_gain, short_weight, w_out, g_out)
    return spread_layer(qkv, filt, skip_gain, short_weight, w_out, g_out)


def solution(mesh):
    in_specs = (
        P(None, "seq", "ch"),
        P("seq", "ch"),
        P("ch"),
        P(None, None, "ch"),
        P(None, "ch"),
        P("seq", "ch"),
    )
    out_specs = (P("seq", "ch"), P(None, "seq", "ch"), P("seq", "ch"))
    return jax.shard_map(local, mesh=mesh, in_specs=in_specs, out_specs=out_specs, check_vma=False)
```

```python
import functools
import math

import jax
import jax.numpy as jnp
import numpy as np
from jax import lax
from jax.experimental import pallas as pl
from jax.experimental.pallas import tpu as pltpu
from jax.sharding import PartitionSpec as P

HIGHEST = lax.Precision.HIGHEST
TWO_PI = 2.0 * math.pi
LANES = 128
HALF = 64
PHASES = 4
BF16 = jnp.bfloat16
F32 = jnp.float32
VMEM_LIMIT = 24 * 1024 * 1024


def passed_along(block, axis, distance):
    devices = range(lax.axis_size(axis))
    route = [(i - distance, i) for i in devices if i - distance in devices]
    return lax.ppermute(block, axis, route)


def phase_pair(left_count, right_count, period, left_start, right_start):
    left_idx = lax.broadcasted_iota(jnp.int32, (left_count, right_count), 0) + left_start
    right_idx = lax.broadcasted_iota(jnp.int32, (left_count, right_count), 1) + right_start
    angle_all = (left_idx * right_idx % period).astype(jnp.float32) * (TWO_PI / period)
    return (jnp.cos(angle_all), jnp.sin(angle_all))


def contract(pattern, matrix, values):
    return jnp.einsum(
        pattern, matrix, values, precision=HIGHEST, preferred_element_type=jnp.float32
    )


def forward_spectrum(signal):
    seq_parts = lax.axis_size("seq")
    row_count = signal.shape[0]
    row_share = row_count // seq_parts
    period = 2 * seq_parts * row_count
    spread_in = lax.all_to_all(signal[None], "seq", split_axis=1, concat_axis=0, tiled=True)
    outer_cos, outer_sin = phase_pair(2 * seq_parts, seq_parts, 2 * seq_parts, 0, 0)
    section_re = contract("cp,prw->crw", outer_cos, spread_in)
    section_im = -contract("cp,prw->crw", outer_sin, spread_in)
    twist_cos, twist_sin = phase_pair(
        2 * seq_parts, row_share, period, 0, lax.axis_index("seq") * row_share
    )
    twist_cos = twist_cos[:, :, None]
    twist_sin = twist_sin[:, :, None]
    turned_re = section_re * twist_cos + section_im * twist_sin
    turned_im = section_im * twist_cos - section_re * twist_sin
    inner_cos, inner_sin = phase_pair(row_count, row_count, row_count, 0, 0)
    piece_re = lax.all_to_all(turned_re, "seq", split_axis=0, concat_axis=1, tiled=True)
    piece_im = lax.all_to_all(turned_im, "seq", split_axis=0, concat_axis=1, tiled=True)
    spec_re = contract("dm,cmk->cdk", inner_cos, piece_re) + contract(
        "dm,cmk->cdk", inner_sin, piece_im
    )
    spec_im = contract("dm,cmk->cdk", inner_cos, piece_im) - contract(
        "dm,cmk->cdk", inner_sin, piece_re
    )
    return (spec_re, spec_im)


def time_signal(spec_re, spec_im):
    seq_parts = lax.axis_size("seq")
    row_count = spec_re.shape[1]
    period = 2 * seq_parts * row_count
    inner_cos, inner_sin = phase_pair(row_count, row_count, row_count, 0, 0)
    back_re = contract("md,cdk->cmk", inner_cos, spec_re) - contract(
        "md,cdk->cmk", inner_sin, spec_im
    )
    back_im = contract("md,cdk->cmk", inner_cos, spec_im) + contract(
        "md,cdk->cmk", inner_sin, spec_re
    )
    twist_cos, twist_sin = phase_pair(2, row_count, period, 2 * lax.axis_index("seq"), 0)
    twist_cos = twist_cos[:, :, None]
    twist_sin = twist_sin[:, :, None]
    turned_re = back_re * twist_cos - back_im * twist_sin
    turned_im = back_im * twist_cos + back_re * twist_sin
    outer_cos, outer_sin = phase_pair(seq_parts, 2 * seq_parts, 2 * seq_parts, 0, 0)
    piece_re = lax.all_to_all(turned_re, "seq", split_axis=1, concat_axis=0, tiled=True)
    piece_im = lax.all_to_all(turned_im, "seq", split_axis=1, concat_axis=0, tiled=True)
    summed = contract("pc,crk->prk", outer_cos, piece_re) - contract(
        "pc,crk->prk", outer_sin, piece_im
    )
    returned = summed * (1.0 / period)
    return lax.all_to_all(returned, "seq", split_axis=0, concat_axis=1, tiled=True)[0]


def spread_layer(qkv, filt, skip_gain, short_weight, w_out, g_out):
    row_count = qkv.shape[1]
    slab_width = qkv.shape[2]
    tail_rows = passed_along(qkv[:, row_count - 2 :, :], "seq", 1)
    extended = jnp.concatenate([tail_rows, qkv], axis=1)
    short = (
        short_weight[:, 0, None, :] * extended[:, 2:, :]
        + short_weight[:, 1, None, :] * extended[:, 1:-1, :]
        + short_weight[:, 2, None, :] * extended[:, :-2, :]
    )
    query_gate = short[0]
    key_short = short[1]
    value_short = short[2]
    mixed = key_short * value_short
    both_re, both_im = forward_spectrum(jnp.concatenate([mixed, filt], axis=1))
    signal_re = both_re[:, :, :slab_width]
    signal_im = both_im[:, :, :slab_width]
    kernel_re = both_re[:, :, slab_width:]
    kernel_im = both_im[:, :, slab_width:]
    conv_out = time_signal(
        signal_re * kernel_re - signal_im * kernel_im, signal_re * kernel_im + signal_im * kernel_re
    )
    long_out = conv_out + skip_gain * mixed
    gated_out = (query_gate * long_out).astype(jnp.bfloat16)
    projected = jnp.dot(
        lax.all_gather(gated_out, "ch", axis=1, tiled=True),
        w_out,
        preferred_element_type=jnp.float32,
    )
    output = projected.astype(jnp.bfloat16)
    grad_all = lax.all_gather(g_out, "ch", axis=1, tiled=True)
    rows_all = lax.all_to_all(w_out, "ch", split_axis=0, concat_axis=1, tiled=True)
    grad_gated = lax.dot_general(
        grad_all, rows_all, (((1,), (1,)), ((), ())), preferred_element_type=jnp.float32
    )
    grad_long = grad_gated * query_gate
    grad_query = grad_gated * long_out
    grad_re, grad_im = forward_spectrum(grad_long)
    pair_re = jnp.concatenate(
        [kernel_re * grad_re + kernel_im * grad_im, signal_re * grad_re + signal_im * grad_im],
        axis=2,
    )
    pair_im = jnp.concatenate(
        [kernel_re * grad_im - kernel_im * grad_re, signal_re * grad_im - signal_im * grad_re],
        axis=2,
    )
    pair_time = time_signal(pair_re, pair_im)
    grad_mixed = pair_time[:, :slab_width] + skip_gain * grad_long
    token_total = lax.axis_size("seq") * row_count
    grad_filter = pair_time[:, slab_width:] * (1.0 / math.sqrt(token_total))
    grad_short = jnp.stack([grad_query, grad_mixed * value_short, grad_mixed * key_short])
    head_rows = passed_along(grad_short[:, :2, :], "seq", -1)
    extended_grad = jnp.concatenate([grad_short, head_rows], axis=1)
    grad_qkv = (
        short_weight[:, 0, None, :] * extended_grad[:, :-2, :]
        + short_weight[:, 1, None, :] * extended_grad[:, 1:-1, :]
        + short_weight[:, 2, None, :] * extended_grad[:, 2:, :]
    ).astype(jnp.bfloat16)
    return (output, grad_qkv, grad_filter)


def split_bf16(values):
    high = values.astype(np.float32).astype(jnp.bfloat16)
    low = (values - high.astype(np.float64)).astype(np.float32).astype(jnp.bfloat16)
    return high, low


def phase_tables(tokens):
    quarter = tokens // PHASES
    freq = 2 * np.arange(quarter)[:, None] + 1
    turn = math.pi / (2 * tokens)
    angle = (freq * PHASES * np.arange(quarter)[None, :] % (4 * tokens)) * turn
    forward = np.concatenate([np.cos(angle), -np.sin(angle)], axis=0)
    backward = np.transpose(forward) * (1.0 / tokens)
    angle = freq * np.arange(PHASES)[None, :] * turn
    twist = np.concatenate([np.cos(angle), np.sin(angle)], axis=1).astype(np.float32)
    twist = np.pad(twist, ((0, 0), (0, LANES - 2 * PHASES)))
    return (*split_bf16(forward), *split_bf16(backward), twist)


def row_order(rows):
    order = np.zeros((rows, rows), np.float32)
    share = rows // PHASES
    for phase in range(PHASES):
        for j in range(share):
            order[phase * share + j, PHASES * j + phase] = 1.0
    return order.astype(jnp.bfloat16)


def mm(a, b):
    return lax.dot_general(a, b, (((1,), (0,)), ((), ())), preferred_element_type=F32)


def low_lanes(shape):
    return lax.broadcasted_iota(jnp.int32, shape, 1) < HALF


def swap(x):
    return pltpu.roll(x, HALF, 1)


class Stage:
    def __init__(self, count_in, count_out, pieces, refs):
        count = count_in + count_out
        sems = refs[2 * count]
        self.held = refs[count : 2 * count]
        self.count_in = count_in
        self.copies = []
        self.waiting = []
        self.given = []
        used = 0
        for i in range(count):
            here, there = refs[i], self.held[i]
            if i >= count_in:
                here, there = there, here
            cuts = pieces if i == 0 else 1
            step = here.shape[0] // cuts
            group = []
            for cut in range(cuts):
                rows = pl.ds(cut * step, step)
                ends = (here.at[rows], there.at[rows]) if cuts > 1 else (here, there)
                group.append(pltpu.make_async_copy(*ends, sems.at[used]))
                used += 1
            self.copies.append(group)
            self.waiting.append(set(range(cuts)))

    def take(self, index, piece=None):
        for cut in sorted(self.waiting[index]):
            if piece is None or piece == cut:
                self.copies[index][cut].wait()
                self.waiting[index].discard(cut)
        return self.held[index]

    def out(self, index):
        return self.held[self.count_in + index]

    def give(self, index):
        if index not in self.given:
            self.copies[self.count_in + index][0].start()
            self.given.append(index)


def staged(kernel, count_in, count_out, pieces, *refs):
    stage = Stage(count_in, count_out, pieces, refs)
    for i in range(1, count_in):
        stage.copies[i][0].start()
        if i == 1:
            for copy in stage.copies[0]:
                copy.start()
    kernel(stage)
    for i in range(count_in):
        stage.take(i)
    for i in range(count_out):
        stage.give(i)
    for i in range(count_out):
        stage.copies[count_in + i][0].wait()


def call(kernel, out_shape, *args, flops=0, pieces=1):
    far = pl.BlockSpec(memory_space=pltpu.HBM)
    arrays = list(args) + list(out_shape)
    moved = sum(math.prod(a.shape) * a.dtype.itemsize for a in arrays)
    return pl.pallas_call(
        functools.partial(staged, kernel, len(args), len(out_shape), pieces),
        out_shape=out_shape,
        in_specs=[far] * len(args),
        out_specs=[far] * len(out_shape),
        scratch_shapes=[pltpu.VMEM(x.shape, x.dtype) for x in arrays]
        + [pltpu.SemaphoreType.DMA((len(arrays) + pieces - 1,))],
        compiler_params=pltpu.CompilerParams(vmem_limit_bytes=VMEM_LIMIT),
        cost_estimate=pl.CostEstimate(flops=flops, bytes_accessed=moved, transcendentals=0),
    )(*args)


def project_kernel(parts, stage):
    out_ref = stage.out(0)
    g = stage.take(1)[...]
    width = g.shape[1]
    for part in range(parts):
        w = stage.take(0, part)[part * width : (part + 1) * width, :]
        out_ref[part] = lax.dot_general(
            g, w, (((1,), (1,)), ((), ())), preferred_element_type=F32
        ).astype(BF16)


def shifted(x, before):
    rows = lax.broadcasted_iota(jnp.int32, x.shape, 0)
    last, first = before[1:2, :], before[0:1, :]
    one = jnp.where(rows == 0, last, pltpu.roll(x, 1, 0))
    two = jnp.where(rows == 0, first, jnp.where(rows == 1, last, pltpu.roll(x, 2, 0)))
    return one, two


def advanced(x, after):
    count = x.shape[0]
    rows = lax.broadcasted_iota(jnp.int32, x.shape, 0)
    first, last = after[0:1, :], after[1:2, :]
    one = jnp.where(rows == count - 1, first, pltpu.roll(x, count - 1, 0))
    two = jnp.where(
        rows == count - 1, last, jnp.where(rows == count - 2, first, pltpu.roll(x, count - 2, 0))
    )
    return one, two


def short_kernel(stage):
    qkv_ref, tail_ref, weight_ref = stage.take(0), stage.take(1), stage.take(2)
    short_ref, send_ref = stage.out(0), stage.out(1)
    for i in range(3):
        x = qkv_ref[i].astype(F32)
        one, two = shifted(x, tail_ref[i].astype(F32))
        short_ref[i] = (
            weight_ref[i, 0:1, :] * x + weight_ref[i, 1:2, :] * one + weight_ref[i, 2:3, :] * two
        )
    stage.give(0)
    order_ref, filt_ref = stage.take(3), stage.take(4)
    mixed = (short_ref[1] * short_ref[2]).astype(BF16)
    mixed = mm(order_ref[...], mixed)
    taps = mm(order_ref[...], filt_ref[...].astype(BF16))
    for tile in range(mixed.shape[1] // LANES):
        m = mixed[:, tile * LANES : (tile + 1) * LANES]
        f = taps[:, tile * LANES : (tile + 1) * LANES]
        low = low_lanes(m.shape)
        send_ref[2 * tile] = jnp.where(low, m, swap(f)).astype(BF16)
        send_ref[2 * tile + 1] = jnp.where(low, swap(m), f).astype(BF16)


def grad_kernel(stage):
    parts_ref, query_ref, order_ref = stage.take(0), stage.take(1), stage.take(2)
    gated_ref, send_ref = stage.out(0), stage.out(1)
    total = parts_ref[0].astype(F32)
    for part in range(1, parts_ref.shape[0]):
        total = total + parts_ref[part].astype(F32)
    gated_ref[...] = total
    stage.give(0)
    grad_long = mm(order_ref[...], (total * query_ref[0]).astype(BF16))
    half = grad_long.shape[0] // 2
    for tile in range(grad_long.shape[1] // LANES):
        g = grad_long[:, tile * LANES : (tile + 1) * LANES]
        top, bottom = g[:half], g[half:]
        low = low_lanes(top.shape)
        send_ref[2 * tile] = jnp.where(low, top, swap(bottom)).astype(BF16)
        send_ref[2 * tile + 1] = jnp.where(low, swap(top), bottom).astype(BF16)


def spread_phases(parts):
    (a_re, a_im), (b_re, b_im), (c_re, c_im), (d_re, d_im) = parts
    s_re, s_im, t_re, t_im = a_re + c_re, a_im + c_im, a_re - c_re, a_im - c_im
    u_re, u_im, v_re, v_im = b_re + d_re, b_im + d_im, b_re - d_re, b_im - d_im
    return [
        (s_re + u_re, s_im + u_im),
        (t_re + v_im, t_im - v_re),
        (s_re - u_re, s_im - u_im),
        (t_re - v_im, t_im + v_re),
    ]


def gather_phases(parts):
    (a_re, a_im), (b_re, b_im), (c_re, c_im), (d_re, d_im) = parts
    s_re, s_im, t_re, t_im = a_re + c_re, a_im + c_im, a_re - c_re, a_im - c_im
    u_re, u_im, v_re, v_im = b_re + d_re, b_im + d_im, b_re - d_re, b_im - d_im
    return [
        (s_re + u_re, s_im + u_im),
        (t_re - v_im, t_im + v_re),
        (s_re - u_re, s_im - u_im),
        (t_re + v_im, t_im - v_re),
    ]


def rows_of(ref, start, count):
    block = ref[:, start : start + count, :]
    return block.reshape(ref.shape[0] * count, ref.shape[2])


def turned_back(re, im, twist, phase):
    if phase == 0:
        return re, im
    c, s = twist[:, phase : phase + 1], twist[:, PHASES + phase : PHASES + phase + 1]
    return re * c + im * s, im * c - re * s


def turned_on(re, im, twist, phase):
    if phase == 0:
        return re, im
    c, s = twist[:, phase : phase + 1], twist[:, PHASES + phase : PHASES + phase + 1]
    return re * c - im * s, re * s + im * c


def lane_tile(x, index):
    return x[:, index * LANES : (index + 1) * LANES]


def conv_kernel(stage):
    recv_ref, fh_ref, fl_ref, twist_ref = [stage.take(i) for i in range(4)]
    spec_ref, send_ref = stage.out(0), stage.out(1)
    share = recv_ref.shape[1] // PHASES
    quarter = fh_ref.shape[1]
    twist = twist_ref[...]
    x = jnp.concatenate([rows_of(recv_ref, p * share, share) for p in range(PHASES)], axis=1)
    s = mm(fh_ref[...], x) + mm(fl_ref[...], x)
    parts = []
    for phase in range(PHASES):
        t = lane_tile(s, phase)
        parts.append(turned_back(t[:quarter], t[quarter:], twist, phase))
    products = []
    for r, (re, im) in enumerate(spread_phases(parts)):
        spec_ref[r, :quarter, :] = re
        spec_ref[r, quarter:, :] = im
        other_re, other_im = swap(re), swap(im)
        products.append((re * other_re - im * other_im, re * other_im + im * other_re))
    stage.give(0)
    bh_ref, bl_ref = stage.take(4), stage.take(5)
    highs, packs = [], []
    low = low_lanes((2 * quarter, LANES))
    for phase, (re, im) in enumerate(gather_phases(products)):
        y = jnp.concatenate(turned_on(re, im, twist, phase), axis=0)
        high = y.astype(BF16)
        highs.append(high)
        high = high.astype(F32)
        packs.append(jnp.where(low, high, y - high).astype(BF16))
    main = mm(bh_ref[...], jnp.concatenate(packs, axis=1))
    rest = mm(bl_ref[...], jnp.concatenate(highs, axis=1))
    times = []
    for phase in range(PHASES):
        t = lane_tile(main, phase)
        times.append(t + swap(t) + lane_tile(rest, phase))
    low = low_lanes((quarter, LANES))
    for phase in range(PHASES // 2):
        t = jnp.where(low, times[phase], times[phase + 2]).astype(BF16)
        send_ref[:, phase * share : (phase + 1) * share, :] = t.reshape(
            send_ref.shape[0], share, LANES
        )


def corr_kernel(stage):
    recv_ref, fh_ref, fl_ref, twist_ref = [stage.take(i) for i in range(4)]
    send_ref = stage.out(0)
    blocks = recv_ref.shape[0]
    share = recv_ref.shape[1] * 2 // PHASES
    quarter = fh_ref.shape[1]
    twist = twist_ref[...]
    x = jnp.concatenate([rows_of(recv_ref, p * share, share) for p in range(2)], axis=1)
    s = mm(fh_ref[...], x) + mm(fl_ref[...], x)
    parts = []
    low = low_lanes((2 * quarter, LANES))
    for phase in range(PHASES):
        t = lane_tile(s, phase % 2)
        t = jnp.where(low, t, swap(t)) if phase < 2 else jnp.where(low, swap(t), t)
        parts.append(turned_back(t[:quarter], t[quarter:], twist, phase))
    products = []
    spec_ref, bh_ref, bl_ref = stage.take(4), stage.take(5), stage.take(6)
    for r, (re, im) in enumerate(spread_phases(parts)):
        k_re, k_im = spec_ref[r, :quarter, :], spec_ref[r, quarter:, :]
        products.append((k_re * re + k_im * im, k_re * im - k_im * re))
    highs, rests = [], []
    for phase, (re, im) in enumerate(gather_phases(products)):
        y = jnp.concatenate(turned_on(re, im, twist, phase), axis=0)
        highs.append(y.astype(BF16))
        rests.append((y - highs[-1].astype(F32)).astype(BF16))
    highs, rests = jnp.concatenate(highs, axis=1), jnp.concatenate(rests, axis=1)
    times = mm(bh_ref[...], highs) + mm(bh_ref[...], rests) + mm(bl_ref[...], highs)
    low = low_lanes((quarter, LANES))
    scale = jnp.where(low, 1.0 / math.sqrt(PHASES * quarter), 1.0)
    rows = PHASES * share
    heads = []
    for phase in range(PHASES):
        t = lane_tile(times, phase) * scale
        send_ref[:, phase * share : (phase + 1) * share, :] = t.astype(BF16).reshape(
            blocks, share, LANES
        )
        heads.append(t)
    extra = send_ref.shape[1] - rows
    row = lax.broadcasted_iota(jnp.int32, (extra, LANES), 0)
    for block in range(blocks):
        at = (block + 1) % blocks * share
        first, second = heads[0][at : at + 1, :], heads[1][at : at + 1, :]
        after = jnp.where(row == 0, first, jnp.where(row == 1, second, 0.0))
        if block == blocks - 1:
            after = jnp.zeros_like(after)
        send_ref[block, rows:, :] = after.astype(BF16)


def gate_kernel(stage):
    recv_ref, order_ref, short_ref, gain_ref, grad_gated_ref = [stage.take(i) for i in range(5)]
    gated_ref, query_ref, head_ref = [stage.out(i) for i in range(3)]
    low = low_lanes((recv_ref.shape[1], LANES))
    tiles = []
    for tile in range(recv_ref.shape[0] // 2):
        a = recv_ref[2 * tile].astype(F32)
        b = recv_ref[2 * tile + 1].astype(F32)
        top = jnp.where(low, a, swap(b))
        bottom = jnp.where(low, swap(a), b)
        tiles.append(jnp.concatenate([top, bottom], axis=0))
    conv = mm(order_ref[...], jnp.concatenate(tiles, axis=1).astype(BF16))
    query, key, value = short_ref[0], short_ref[1], short_ref[2]
    long_out = conv + gain_ref[...] * (key * value)
    gated_ref[...] = (query * long_out).astype(BF16)
    stage.give(0)
    grad_gated = grad_gated_ref[...]
    grad_query = grad_gated * long_out
    query_ref[...] = grad_query
    head_ref[0:2, :] = grad_query[0:2, :]
    head_ref[2:4, :] = gain_ref[...] * (grad_gated[0:2, :] * query[0:2, :])
    head_ref[4:6, :] = key[0:2, :]
    head_ref[6:8, :] = value[0:2, :]


def close_kernel(stage):
    recv_ref, order_ref = stage.take(0), stage.take(1)
    grad_ref, filter_ref = stage.out(0), stage.out(1)
    rows = grad_ref.shape[1]
    low = low_lanes((recv_ref.shape[1], LANES))
    filters, mixes = [], []
    for tile in range(recv_ref.shape[0] // 2):
        a = recv_ref[2 * tile].astype(F32)
        b = recv_ref[2 * tile + 1].astype(F32)
        filters.append(jnp.where(low, a, swap(b))[:rows])
        mixes.append(jnp.where(low, swap(a), b))
    filter_ref[...] = mm(order_ref[...], jnp.concatenate(filters, axis=1).astype(BF16))
    stage.give(1)
    short_ref, grad_gated_ref, query_ref, next_ref, gain_ref, weight_ref = [
        stage.take(i) for i in range(2, 8)
    ]
    mixes = jnp.concatenate(mixes, axis=1)
    gain = gain_ref[...]
    grad_long = grad_gated_ref[...] * short_ref[0]
    grad_mixed = mm(order_ref[...], mixes[:rows].astype(BF16)) + gain * grad_long
    heads = next_ref[...]
    next_mixed = mixes[rows : rows + 2] + heads[2:4]
    key, value = short_ref[1], short_ref[2]
    grads = [query_ref[...], grad_mixed * value, grad_mixed * key]
    afters = [heads[0:2], next_mixed * heads[6:8], next_mixed * heads[4:6]]
    for i in range(3):
        one, two = advanced(grads[i], afters[i])
        grad_ref[i] = (
            weight_ref[i, 0:1, :] * grads[i]
            + weight_ref[i, 1:2, :] * one
            + weight_ref[i, 2:3, :] * two
        ).astype(BF16)


def output_kernel(parts, stage):
    w_ref = stage.take(parts)
    width = w_ref.shape[0] // parts
    me = lax.axis_index("ch")
    total = None
    for i in range(parts):
        rows = pl.ds(pl.multiple_of((me ^ i) * width, width), width)
        term = mm(stage.take(i)[...], w_ref[rows, :])
        total = term if total is None else total + term
    stage.out(0)[...] = total.astype(BF16)


def exchanged(x, axis):
    return lax.all_to_all(x, axis, split_axis=0, concat_axis=0, tiled=True)


def partner(x, axis, mask):
    return lax.ppermute(x, axis, [(i, i ^ mask) for i in range(lax.axis_size(axis))])


def owner_layer(qkv, filt, skip_gain, short_weight, w_out, g_out):
    shape = jax.ShapeDtypeStruct
    seq_parts, ch_parts = lax.axis_size("seq"), lax.axis_size("ch")
    rows, width = qkv.shape[1], qkv.shape[2]
    tokens = seq_parts * rows
    order = row_order(rows)
    back_order = order.T
    gain = skip_gain[None, :]
    fh, fl, bh, bl, twist = phase_tables(tokens)
    table_flops = 2 * 2 * 2 * tokens * tokens // PHASES * LANES
    product_flops = 2 * rows * width * width * ch_parts

    tail_rows = passed_along(qkv[:, rows - 2 :, :], "seq", 1)
    (partial,) = call(
        functools.partial(project_kernel, ch_parts),
        [shape((ch_parts, rows, width), BF16)],
        w_out,
        g_out,
        flops=product_flops,
        pieces=ch_parts,
    )
    partial = exchanged(partial, "ch")
    short, send = call(
        short_kernel,
        [shape((3, rows, width), F32), shape((seq_parts, rows, LANES), BF16)],
        qkv,
        tail_rows,
        short_weight,
        order,
        filt,
    )
    recv = exchanged(send, "seq")
    grad_gated, send = call(
        grad_kernel,
        [shape((rows, width), F32), shape((seq_parts, rows // 2, LANES), BF16)],
        partial,
        short,
        order,
    )
    grad_recv = exchanged(send, "seq")
    spec, send = call(
        conv_kernel,
        [shape((PHASES, tokens // 2, LANES), F32), shape((seq_parts, rows // 2, LANES), BF16)],
        recv,
        fh,
        fl,
        twist,
        bh,
        bl,
        flops=table_flops,
    )
    conv_recv = exchanged(send, "seq")
    (send,) = call(
        corr_kernel,
        [shape((seq_parts, rows + 16, LANES), BF16)],
        grad_recv,
        fh,
        fl,
        twist,
        spec,
        bh,
        bl,
        flops=table_flops,
    )
    corr_recv = exchanged(send, "seq")
    gated, grad_query, heads = call(
        gate_kernel,
        [shape((rows, width), BF16), shape((rows, width), F32), shape((8, width), F32)],
        conv_recv,
        back_order,
        short,
        gain,
        grad_gated,
    )
    next_heads = passed_along(heads, "seq", -1)
    others = [partner(gated, "ch", mask) for mask in range(1, ch_parts)]
    grad_qkv, grad_filter = call(
        close_kernel,
        [shape((3, rows, width), BF16), shape((rows, width), F32)],
        corr_recv,
        back_order,
        short,
        grad_gated,
        grad_query,
        next_heads,
        gain,
        short_weight,
    )
    (output,) = call(
        functools.partial(output_kernel, ch_parts),
        [shape((rows, width), BF16)],
        gated,
        *others,
        w_out,
        flops=product_flops,
    )
    return (output, grad_qkv, grad_filter)


def local(qkv, filt, skip_gain, short_weight, w_out, g_out):
    seq_parts = lax.axis_size("seq")
    rows, width = qkv.shape[1], qkv.shape[2]
    fits = width == HALF * seq_parts and rows % HALF == 0 and rows * seq_parts <= 2048
    if fits and lax.axis_size("ch") == 4:
        return owner_layer(qkv, filt, skip_gain, short_weight, w_out, g_out)
    return spread_layer(qkv, filt, skip_gain, short_weight, w_out, g_out)


def solution(mesh):
    in_specs = (
        P(None, "seq", "ch"),
        P("seq", "ch"),
        P("ch"),
        P(None, None, "ch"),
        P(None, "ch"),
        P("seq", "ch"),
    )
    out_specs = (P("seq", "ch"), P(None, "seq", "ch"), P("seq", "ch"))
    return jax.shard_map(local, mesh=mesh, in_specs=in_specs, out_specs=out_specs, check_vma=False)
```

```python
import functools
import math

import jax
import jax.numpy as jnp
import numpy as np
from jax import lax
from jax.experimental import pallas as pl
from jax.experimental.pallas import tpu as pltpu
from jax.sharding import PartitionSpec as P

HIGHEST = lax.Precision.HIGHEST
TWO_PI = 2.0 * math.pi
LANES = 128
HALF = 64
PHASES = 4
BF16 = jnp.bfloat16
F32 = jnp.float32
VMEM_LIMIT = 64 * 1024 * 1024


def passed_along(block, axis, distance):
    devices = range(lax.axis_size(axis))
    route = [(i - distance, i) for i in devices if i - distance in devices]
    return lax.ppermute(block, axis, route)


def phase_pair(left_count, right_count, period, left_start, right_start):
    left_idx = lax.broadcasted_iota(jnp.int32, (left_count, right_count), 0) + left_start
    right_idx = lax.broadcasted_iota(jnp.int32, (left_count, right_count), 1) + right_start
    angle_all = (left_idx * right_idx % period).astype(jnp.float32) * (TWO_PI / period)
    return (jnp.cos(angle_all), jnp.sin(angle_all))


def contract(pattern, matrix, values):
    return jnp.einsum(
        pattern, matrix, values, precision=HIGHEST, preferred_element_type=jnp.float32
    )


def forward_spectrum(signal):
    seq_parts = lax.axis_size("seq")
    row_count = signal.shape[0]
    row_share = row_count // seq_parts
    period = 2 * seq_parts * row_count
    spread_in = lax.all_to_all(signal[None], "seq", split_axis=1, concat_axis=0, tiled=True)
    outer_cos, outer_sin = phase_pair(2 * seq_parts, seq_parts, 2 * seq_parts, 0, 0)
    section_re = contract("cp,prw->crw", outer_cos, spread_in)
    section_im = -contract("cp,prw->crw", outer_sin, spread_in)
    twist_cos, twist_sin = phase_pair(
        2 * seq_parts, row_share, period, 0, lax.axis_index("seq") * row_share
    )
    twist_cos = twist_cos[:, :, None]
    twist_sin = twist_sin[:, :, None]
    turned_re = section_re * twist_cos + section_im * twist_sin
    turned_im = section_im * twist_cos - section_re * twist_sin
    inner_cos, inner_sin = phase_pair(row_count, row_count, row_count, 0, 0)
    piece_re = lax.all_to_all(turned_re, "seq", split_axis=0, concat_axis=1, tiled=True)
    piece_im = lax.all_to_all(turned_im, "seq", split_axis=0, concat_axis=1, tiled=True)
    spec_re = contract("dm,cmk->cdk", inner_cos, piece_re) + contract(
        "dm,cmk->cdk", inner_sin, piece_im
    )
    spec_im = contract("dm,cmk->cdk", inner_cos, piece_im) - contract(
        "dm,cmk->cdk", inner_sin, piece_re
    )
    return (spec_re, spec_im)


def time_signal(spec_re, spec_im):
    seq_parts = lax.axis_size("seq")
    row_count = spec_re.shape[1]
    period = 2 * seq_parts * row_count
    inner_cos, inner_sin = phase_pair(row_count, row_count, row_count, 0, 0)
    back_re = contract("md,cdk->cmk", inner_cos, spec_re) - contract(
        "md,cdk->cmk", inner_sin, spec_im
    )
    back_im = contract("md,cdk->cmk", inner_cos, spec_im) + contract(
        "md,cdk->cmk", inner_sin, spec_re
    )
    twist_cos, twist_sin = phase_pair(2, row_count, period, 2 * lax.axis_index("seq"), 0)
    twist_cos = twist_cos[:, :, None]
    twist_sin = twist_sin[:, :, None]
    turned_re = back_re * twist_cos - back_im * twist_sin
    turned_im = back_im * twist_cos + back_re * twist_sin
    outer_cos, outer_sin = phase_pair(seq_parts, 2 * seq_parts, 2 * seq_parts, 0, 0)
    piece_re = lax.all_to_all(turned_re, "seq", split_axis=1, concat_axis=0, tiled=True)
    piece_im = lax.all_to_all(turned_im, "seq", split_axis=1, concat_axis=0, tiled=True)
    summed = contract("pc,crk->prk", outer_cos, piece_re) - contract(
        "pc,crk->prk", outer_sin, piece_im
    )
    returned = summed * (1.0 / period)
    return lax.all_to_all(returned, "seq", split_axis=0, concat_axis=1, tiled=True)[0]


def spread_layer(qkv, filt, skip_gain, short_weight, w_out, g_out):
    row_count = qkv.shape[1]
    slab_width = qkv.shape[2]
    tail_rows = passed_along(qkv[:, row_count - 2 :, :], "seq", 1)
    extended = jnp.concatenate([tail_rows, qkv], axis=1)
    short = (
        short_weight[:, 0, None, :] * extended[:, 2:, :]
        + short_weight[:, 1, None, :] * extended[:, 1:-1, :]
        + short_weight[:, 2, None, :] * extended[:, :-2, :]
    )
    query_gate = short[0]
    key_short = short[1]
    value_short = short[2]
    mixed = key_short * value_short
    both_re, both_im = forward_spectrum(jnp.concatenate([mixed, filt], axis=1))
    signal_re = both_re[:, :, :slab_width]
    signal_im = both_im[:, :, :slab_width]
    kernel_re = both_re[:, :, slab_width:]
    kernel_im = both_im[:, :, slab_width:]
    conv_out = time_signal(
        signal_re * kernel_re - signal_im * kernel_im, signal_re * kernel_im + signal_im * kernel_re
    )
    long_out = conv_out + skip_gain * mixed
    gated_out = (query_gate * long_out).astype(jnp.bfloat16)
    projected = jnp.dot(
        lax.all_gather(gated_out, "ch", axis=1, tiled=True),
        w_out,
        preferred_element_type=jnp.float32,
    )
    output = projected.astype(jnp.bfloat16)
    grad_all = lax.all_gather(g_out, "ch", axis=1, tiled=True)
    rows_all = lax.all_to_all(w_out, "ch", split_axis=0, concat_axis=1, tiled=True)
    grad_gated = lax.dot_general(
        grad_all, rows_all, (((1,), (1,)), ((), ())), preferred_element_type=jnp.float32
    )
    grad_long = grad_gated * query_gate
    grad_query = grad_gated * long_out
    grad_re, grad_im = forward_spectrum(grad_long)
    pair_re = jnp.concatenate(
        [kernel_re * grad_re + kernel_im * grad_im, signal_re * grad_re + signal_im * grad_im],
        axis=2,
    )
    pair_im = jnp.concatenate(
        [kernel_re * grad_im - kernel_im * grad_re, signal_re * grad_im - signal_im * grad_re],
        axis=2,
    )
    pair_time = time_signal(pair_re, pair_im)
    grad_mixed = pair_time[:, :slab_width] + skip_gain * grad_long
    token_total = lax.axis_size("seq") * row_count
    grad_filter = pair_time[:, slab_width:] * (1.0 / math.sqrt(token_total))
    grad_short = jnp.stack([grad_query, grad_mixed * value_short, grad_mixed * key_short])
    head_rows = passed_along(grad_short[:, :2, :], "seq", -1)
    extended_grad = jnp.concatenate([grad_short, head_rows], axis=1)
    grad_qkv = (
        short_weight[:, 0, None, :] * extended_grad[:, :-2, :]
        + short_weight[:, 1, None, :] * extended_grad[:, 1:-1, :]
        + short_weight[:, 2, None, :] * extended_grad[:, 2:, :]
    ).astype(jnp.bfloat16)
    return (output, grad_qkv, grad_filter)


def split_bf16(values):
    high = values.astype(np.float32).astype(jnp.bfloat16)
    low = (values - high.astype(np.float64)).astype(np.float32).astype(jnp.bfloat16)
    return high, low


def phase_tables(tokens):
    quarter = tokens // PHASES
    freq = 2 * np.arange(quarter)[:, None] + 1
    turn = math.pi / (2 * tokens)
    angle = (freq * PHASES * np.arange(quarter)[None, :] % (4 * tokens)) * turn
    forward = np.concatenate([np.cos(angle), -np.sin(angle)], axis=0)
    backward = np.transpose(forward) * (1.0 / tokens)
    angle = freq * np.arange(PHASES)[None, :] * turn
    twist = np.concatenate([np.cos(angle), np.sin(angle)], axis=1).astype(np.float32)
    twist = np.pad(twist, ((0, 0), (0, LANES - 2 * PHASES)))
    return (*split_bf16(forward), *split_bf16(backward), twist)


def row_order(rows):
    order = np.zeros((rows, rows), np.float32)
    share = rows // PHASES
    for phase in range(PHASES):
        for j in range(share):
            order[phase * share + j, PHASES * j + phase] = 1.0
    return order.astype(jnp.bfloat16)


def mm(a, b):
    return lax.dot_general(a, b, (((1,), (0,)), ((), ())), preferred_element_type=F32)


def low_lanes(shape):
    return lax.broadcasted_iota(jnp.int32, shape, 1) < HALF


def swap(x):
    return pltpu.roll(x, HALF, 1)


class Stage:
    def __init__(self, count_in, count_out, pieces, refs):
        count = count_in + count_out
        sems = refs[2 * count]
        self.held = refs[count : 2 * count]
        self.count_in = count_in
        self.copies = []
        self.waiting = []
        self.given = []
        used = 0
        for i in range(count):
            here, there = refs[i], self.held[i]
            if i >= count_in:
                here, there = there, here
            cuts = pieces if i == 0 else 1
            step = here.shape[0] // cuts
            group = []
            for cut in range(cuts):
                rows = pl.ds(cut * step, step)
                ends = (here.at[rows], there.at[rows]) if cuts > 1 else (here, there)
                group.append(pltpu.make_async_copy(*ends, sems.at[used]))
                used += 1
            self.copies.append(group)
            self.waiting.append(set(range(cuts)))

    def take(self, index, piece=None):
        for cut in sorted(self.waiting[index]):
            if piece is None or piece == cut:
                self.copies[index][cut].wait()
                self.waiting[index].discard(cut)
        return self.held[index]

    def out(self, index):
        return self.held[self.count_in + index]

    def give(self, index):
        if index not in self.given:
            self.copies[self.count_in + index][0].start()
            self.given.append(index)


def staged(kernel, count_in, count_out, pieces, *refs):
    stage = Stage(count_in, count_out, pieces, refs)
    for i in range(1, count_in):
        stage.copies[i][0].start()
        if i == 1:
            for copy in stage.copies[0]:
                copy.start()
    kernel(stage)
    for i in range(count_in):
        stage.take(i)
    for i in range(count_out):
        stage.give(i)
    for i in range(count_out):
        stage.copies[count_in + i][0].wait()


def call(kernel, out_shape, *args, flops=0, pieces=1):
    far = pl.BlockSpec(memory_space=pltpu.HBM)
    arrays = list(args) + list(out_shape)
    moved = sum(math.prod(a.shape) * a.dtype.itemsize for a in arrays)
    return pl.pallas_call(
        functools.partial(staged, kernel, len(args), len(out_shape), pieces),
        out_shape=out_shape,
        in_specs=[far] * len(args),
        out_specs=[far] * len(out_shape),
        scratch_shapes=[pltpu.VMEM(x.shape, x.dtype) for x in arrays]
        + [pltpu.SemaphoreType.DMA((len(arrays) + pieces - 1,))],
        compiler_params=pltpu.CompilerParams(vmem_limit_bytes=VMEM_LIMIT),
        cost_estimate=pl.CostEstimate(flops=flops, bytes_accessed=moved, transcendentals=0),
    )(*args)


def project_kernel(parts, stage):
    out_ref = stage.out(0)
    g = stage.take(1)[...]
    width = g.shape[1]
    for part in range(parts):
        w = stage.take(0, part)[part * width : (part + 1) * width, :]
        out_ref[part] = lax.dot_general(
            g, w, (((1,), (1,)), ((), ())), preferred_element_type=F32
        ).astype(BF16)


def shifted(x, before):
    rows = lax.broadcasted_iota(jnp.int32, x.shape, 0)
    last, first = before[1:2, :], before[0:1, :]
    one = jnp.where(rows == 0, last, pltpu.roll(x, 1, 0))
    two = jnp.where(rows == 0, first, jnp.where(rows == 1, last, pltpu.roll(x, 2, 0)))
    return one, two


def advanced(x, after):
    count = x.shape[0]
    rows = lax.broadcasted_iota(jnp.int32, x.shape, 0)
    first, last = after[0:1, :], after[1:2, :]
    one = jnp.where(rows == count - 1, first, pltpu.roll(x, count - 1, 0))
    two = jnp.where(
        rows == count - 1, last, jnp.where(rows == count - 2, first, pltpu.roll(x, count - 2, 0))
    )
    return one, two


def short_kernel(stage):
    qkv_ref, tail_ref, weight_ref = stage.take(0), stage.take(1), stage.take(2)
    short_ref, send_ref = stage.out(0), stage.out(1)
    for i in range(3):
        x = qkv_ref[i].astype(F32)
        one, two = shifted(x, tail_ref[i].astype(F32))
        short_ref[i] = (
            weight_ref[i, 0:1, :] * x + weight_ref[i, 1:2, :] * one + weight_ref[i, 2:3, :] * two
        )
    stage.give(0)
    order_ref, filt_ref = stage.take(3), stage.take(4)
    mixed = (short_ref[1] * short_ref[2]).astype(BF16)
    mixed = mm(order_ref[...], mixed)
    taps = mm(order_ref[...], filt_ref[...].astype(BF16))
    for tile in range(mixed.shape[1] // LANES):
        m = mixed[:, tile * LANES : (tile + 1) * LANES]
        f = taps[:, tile * LANES : (tile + 1) * LANES]
        low = low_lanes(m.shape)
        send_ref[2 * tile] = jnp.where(low, m, swap(f)).astype(BF16)
        send_ref[2 * tile + 1] = jnp.where(low, swap(m), f).astype(BF16)


def grad_kernel(stage):
    parts_ref, query_ref, order_ref = stage.take(0), stage.take(1), stage.take(2)
    gated_ref, send_ref = stage.out(0), stage.out(1)
    total = parts_ref[0].astype(F32)
    for part in range(1, parts_ref.shape[0]):
        total = total + parts_ref[part].astype(F32)
    gated_ref[...] = total
    stage.give(0)
    grad_long = mm(order_ref[...], (total * query_ref[0]).astype(BF16))
    half = grad_long.shape[0] // 2
    for tile in range(grad_long.shape[1] // LANES):
        g = grad_long[:, tile * LANES : (tile + 1) * LANES]
        top, bottom = g[:half], g[half:]
        low = low_lanes(top.shape)
        send_ref[2 * tile] = jnp.where(low, top, swap(bottom)).astype(BF16)
        send_ref[2 * tile + 1] = jnp.where(low, swap(top), bottom).astype(BF16)


def spread_phases(parts):
    (a_re, a_im), (b_re, b_im), (c_re, c_im), (d_re, d_im) = parts
    s_re, s_im, t_re, t_im = a_re + c_re, a_im + c_im, a_re - c_re, a_im - c_im
    u_re, u_im, v_re, v_im = b_re + d_re, b_im + d_im, b_re - d_re, b_im - d_im
    return [
        (s_re + u_re, s_im + u_im),
        (t_re + v_im, t_im - v_re),
        (s_re - u_re, s_im - u_im),
        (t_re - v_im, t_im + v_re),
    ]


def gather_phases(parts):
    (a_re, a_im), (b_re, b_im), (c_re, c_im), (d_re, d_im) = parts
    s_re, s_im, t_re, t_im = a_re + c_re, a_im + c_im, a_re - c_re, a_im - c_im
    u_re, u_im, v_re, v_im = b_re + d_re, b_im + d_im, b_re - d_re, b_im - d_im
    return [
        (s_re + u_re, s_im + u_im),
        (t_re - v_im, t_im + v_re),
        (s_re - u_re, s_im - u_im),
        (t_re + v_im, t_im - v_re),
    ]


def rows_of(ref, start, count):
    block = ref[:, start : start + count, :]
    return block.reshape(ref.shape[0] * count, ref.shape[2])


def turned_back(re, im, twist, phase):
    if phase == 0:
        return re, im
    c, s = twist[:, phase : phase + 1], twist[:, PHASES + phase : PHASES + phase + 1]
    return re * c + im * s, im * c - re * s


def turned_on(re, im, twist, phase):
    if phase == 0:
        return re, im
    c, s = twist[:, phase : phase + 1], twist[:, PHASES + phase : PHASES + phase + 1]
    return re * c - im * s, re * s + im * c


def lane_tile(x, index):
    return x[:, index * LANES : (index + 1) * LANES]


def conv_kernel(stage):
    recv_ref, fh_ref, fl_ref, twist_ref = [stage.take(i) for i in range(4)]
    spec_ref, send_ref = stage.out(0), stage.out(1)
    share = recv_ref.shape[1] // PHASES
    quarter = fh_ref.shape[1]
    twist = twist_ref[...]
    x = jnp.concatenate([rows_of(recv_ref, p * share, share) for p in range(PHASES)], axis=1)
    s = mm(fh_ref[...], x) + mm(fl_ref[...], x)
    parts = []
    for phase in range(PHASES):
        t = lane_tile(s, phase)
        parts.append(turned_back(t[:quarter], t[quarter:], twist, phase))
    products = []
    for r, (re, im) in enumerate(spread_phases(parts)):
        spec_ref[r, :quarter, :] = re
        spec_ref[r, quarter:, :] = im
        other_re, other_im = swap(re), swap(im)
        products.append((re * other_re - im * other_im, re * other_im + im * other_re))
    stage.give(0)
    bh_ref, bl_ref = stage.take(4), stage.take(5)
    highs, packs = [], []
    low = low_lanes((2 * quarter, LANES))
    for phase, (re, im) in enumerate(gather_phases(products)):
        y = jnp.concatenate(turned_on(re, im, twist, phase), axis=0)
        high = y.astype(BF16)
        highs.append(high)
        high = high.astype(F32)
        packs.append(jnp.where(low, high, y - high).astype(BF16))
    main = mm(bh_ref[...], jnp.concatenate(packs, axis=1))
    rest = mm(bl_ref[...], jnp.concatenate(highs, axis=1))
    times = []
    for phase in range(PHASES):
        t = lane_tile(main, phase)
        times.append(t + swap(t) + lane_tile(rest, phase))
    low = low_lanes((quarter, LANES))
    for phase in range(PHASES // 2):
        t = jnp.where(low, times[phase], times[phase + 2]).astype(BF16)
        send_ref[:, phase * share : (phase + 1) * share, :] = t.reshape(
            send_ref.shape[0], share, LANES
        )


def corr_kernel(stage):
    recv_ref, fh_ref, fl_ref, twist_ref = [stage.take(i) for i in range(4)]
    send_ref = stage.out(0)
    blocks = recv_ref.shape[0]
    share = recv_ref.shape[1] * 2 // PHASES
    quarter = fh_ref.shape[1]
    twist = twist_ref[...]
    x = jnp.concatenate([rows_of(recv_ref, p * share, share) for p in range(2)], axis=1)
    s = mm(fh_ref[...], x) + mm(fl_ref[...], x)
    parts = []
    low = low_lanes((2 * quarter, LANES))
    for phase in range(PHASES):
        t = lane_tile(s, phase % 2)
        t = jnp.where(low, t, swap(t)) if phase < 2 else jnp.where(low, swap(t), t)
        parts.append(turned_back(t[:quarter], t[quarter:], twist, phase))
    products = []
    spec_ref, bh_ref, bl_ref = stage.take(4), stage.take(5), stage.take(6)
    for r, (re, im) in enumerate(spread_phases(parts)):
        k_re, k_im = spec_ref[r, :quarter, :], spec_ref[r, quarter:, :]
        products.append((k_re * re + k_im * im, k_re * im - k_im * re))
    highs, rests = [], []
    for phase, (re, im) in enumerate(gather_phases(products)):
        y = jnp.concatenate(turned_on(re, im, twist, phase), axis=0)
        highs.append(y.astype(BF16))
        rests.append((y - highs[-1].astype(F32)).astype(BF16))
    highs, rests = jnp.concatenate(highs, axis=1), jnp.concatenate(rests, axis=1)
    times = mm(bh_ref[...], highs) + mm(bh_ref[...], rests) + mm(bl_ref[...], highs)
    low = low_lanes((quarter, LANES))
    scale = jnp.where(low, 1.0 / math.sqrt(PHASES * quarter), 1.0)
    rows = PHASES * share
    heads = []
    for phase in range(PHASES):
        t = lane_tile(times, phase) * scale
        send_ref[:, phase * share : (phase + 1) * share, :] = t.astype(BF16).reshape(
            blocks, share, LANES
        )
        heads.append(t)
    extra = send_ref.shape[1] - rows
    row = lax.broadcasted_iota(jnp.int32, (extra, LANES), 0)
    for block in range(blocks):
        at = (block + 1) % blocks * share
        first, second = heads[0][at : at + 1, :], heads[1][at : at + 1, :]
        after = jnp.where(row == 0, first, jnp.where(row == 1, second, 0.0))
        if block == blocks - 1:
            after = jnp.zeros_like(after)
        send_ref[block, rows:, :] = after.astype(BF16)


def gate_kernel(stage):
    recv_ref, order_ref, short_ref, gain_ref, grad_gated_ref = [stage.take(i) for i in range(5)]
    gated_ref, query_ref, head_ref = [stage.out(i) for i in range(3)]
    low = low_lanes((recv_ref.shape[1], LANES))
    tiles = []
    for tile in range(recv_ref.shape[0] // 2):
        a = recv_ref[2 * tile].astype(F32)
        b = recv_ref[2 * tile + 1].astype(F32)
        top = jnp.where(low, a, swap(b))
        bottom = jnp.where(low, swap(a), b)
        tiles.append(jnp.concatenate([top, bottom], axis=0))
    conv = mm(order_ref[...], jnp.concatenate(tiles, axis=1).astype(BF16))
    query, key, value = short_ref[0], short_ref[1], short_ref[2]
    long_out = conv + gain_ref[...] * (key * value)
    gated_ref[...] = (query * long_out).astype(BF16)
    stage.give(0)
    grad_gated = grad_gated_ref[...]
    grad_query = grad_gated * long_out
    query_ref[...] = grad_query
    head_ref[0:2, :] = grad_query[0:2, :]
    head_ref[2:4, :] = gain_ref[...] * (grad_gated[0:2, :] * query[0:2, :])
    head_ref[4:6, :] = key[0:2, :]
    head_ref[6:8, :] = value[0:2, :]


def close_kernel(stage):
    recv_ref, order_ref = stage.take(0), stage.take(1)
    grad_ref, filter_ref = stage.out(0), stage.out(1)
    rows = grad_ref.shape[1]
    low = low_lanes((recv_ref.shape[1], LANES))
    filters, mixes = [], []
    for tile in range(recv_ref.shape[0] // 2):
        a = recv_ref[2 * tile].astype(F32)
        b = recv_ref[2 * tile + 1].astype(F32)
        filters.append(jnp.where(low, a, swap(b))[:rows])
        mixes.append(jnp.where(low, swap(a), b))
    filter_ref[...] = mm(order_ref[...], jnp.concatenate(filters, axis=1).astype(BF16))
    stage.give(1)
    short_ref, grad_gated_ref, query_ref, next_ref, gain_ref, weight_ref = [
        stage.take(i) for i in range(2, 8)
    ]
    mixes = jnp.concatenate(mixes, axis=1)
    gain = gain_ref[...]
    grad_long = grad_gated_ref[...] * short_ref[0]
    grad_mixed = mm(order_ref[...], mixes[:rows].astype(BF16)) + gain * grad_long
    heads = next_ref[...]
    next_mixed = mixes[rows : rows + 2] + heads[2:4]
    key, value = short_ref[1], short_ref[2]
    grads = [query_ref[...], grad_mixed * value, grad_mixed * key]
    afters = [heads[0:2], next_mixed * heads[6:8], next_mixed * heads[4:6]]
    for i in range(3):
        one, two = advanced(grads[i], afters[i])
        grad_ref[i] = (
            weight_ref[i, 0:1, :] * grads[i]
            + weight_ref[i, 1:2, :] * one
            + weight_ref[i, 2:3, :] * two
        ).astype(BF16)


def output_kernel(parts, stage):
    w_ref = stage.take(parts)
    width = w_ref.shape[0] // parts
    me = lax.axis_index("ch")
    total = None
    for i in range(parts):
        rows = pl.ds(pl.multiple_of((me ^ i) * width, width), width)
        term = mm(stage.take(i)[...], w_ref[rows, :])
        total = term if total is None else total + term
    stage.out(0)[...] = total.astype(BF16)


def exchanged(x, axis):
    return lax.all_to_all(x, axis, split_axis=0, concat_axis=0, tiled=True)


def partner(x, axis, mask):
    return lax.ppermute(x, axis, [(i, i ^ mask) for i in range(lax.axis_size(axis))])


def owner_layer(qkv, filt, skip_gain, short_weight, w_out, g_out):
    shape = jax.ShapeDtypeStruct
    seq_parts, ch_parts = lax.axis_size("seq"), lax.axis_size("ch")
    rows, width = qkv.shape[1], qkv.shape[2]
    tokens = seq_parts * rows
    order = row_order(rows)
    back_order = order.T
    gain = skip_gain[None, :]
    fh, fl, bh, bl, twist = phase_tables(tokens)
    table_flops = 2 * 2 * 2 * tokens * tokens // PHASES * LANES
    product_flops = 2 * rows * width * width * ch_parts

    tail_rows = passed_along(qkv[:, rows - 2 :, :], "seq", 1)
    (partial,) = call(
        functools.partial(project_kernel, ch_parts),
        [shape((ch_parts, rows, width), BF16)],
        w_out,
        g_out,
        flops=product_flops,
        pieces=ch_parts,
    )
    partial = exchanged(partial, "ch")
    short, send = call(
        short_kernel,
        [shape((3, rows, width), F32), shape((seq_parts, rows, LANES), BF16)],
        qkv,
        tail_rows,
        short_weight,
        order,
        filt,
    )
    recv = exchanged(send, "seq")
    grad_gated, send = call(
        grad_kernel,
        [shape((rows, width), F32), shape((seq_parts, rows // 2, LANES), BF16)],
        partial,
        short,
        order,
    )
    grad_recv = exchanged(send, "seq")
    spec, send = call(
        conv_kernel,
        [shape((PHASES, tokens // 2, LANES), F32), shape((seq_parts, rows // 2, LANES), BF16)],
        recv,
        fh,
        fl,
        twist,
        bh,
        bl,
        flops=table_flops,
    )
    conv_recv = exchanged(send, "seq")
    (send,) = call(
        corr_kernel,
        [shape((seq_parts, rows + 16, LANES), BF16)],
        grad_recv,
        fh,
        fl,
        twist,
        spec,
        bh,
        bl,
        flops=table_flops,
    )
    corr_recv = exchanged(send, "seq")
    gated, grad_query, heads = call(
        gate_kernel,
        [shape((rows, width), BF16), shape((rows, width), F32), shape((8, width), F32)],
        conv_recv,
        back_order,
        short,
        gain,
        grad_gated,
    )
    next_heads = passed_along(heads, "seq", -1)
    others = [partner(gated, "ch", mask) for mask in range(1, ch_parts)]
    grad_qkv, grad_filter = call(
        close_kernel,
        [shape((3, rows, width), BF16), shape((rows, width), F32)],
        corr_recv,
        back_order,
        short,
        grad_gated,
        grad_query,
        next_heads,
        gain,
        short_weight,
    )
    (output,) = call(
        functools.partial(output_kernel, ch_parts),
        [shape((rows, width), BF16)],
        gated,
        *others,
        w_out,
        flops=product_flops,
    )
    return (output, grad_qkv, grad_filter)


def local(qkv, filt, skip_gain, short_weight, w_out, g_out):
    seq_parts = lax.axis_size("seq")
    rows, width = qkv.shape[1], qkv.shape[2]
    fits = width == HALF * seq_parts and rows % HALF == 0 and rows * seq_parts <= 2048
    if fits and lax.axis_size("ch") == 4:
        return owner_layer(qkv, filt, skip_gain, short_weight, w_out, g_out)
    return spread_layer(qkv, filt, skip_gain, short_weight, w_out, g_out)


def solution(mesh):
    in_specs = (
        P(None, "seq", "ch"),
        P("seq", "ch"),
        P("ch"),
        P(None, None, "ch"),
        P(None, "ch"),
        P("seq", "ch"),
    )
    out_specs = (P("seq", "ch"), P(None, "seq", "ch"), P("seq", "ch"))
    return jax.shard_map(local, mesh=mesh, in_specs=in_specs, out_specs=out_specs, check_vma=False)
```

```python
import functools
import math

import jax
import jax.numpy as jnp
import numpy as np
from jax import lax
from jax.experimental import pallas as pl
from jax.experimental.pallas import tpu as pltpu
from jax.sharding import PartitionSpec as P

HIGHEST = lax.Precision.HIGHEST
TWO_PI = 2.0 * math.pi
LANES = 128
HALF = 64
PHASES = 4
BF16 = jnp.bfloat16
F32 = jnp.float32
VMEM_LIMIT = 64 * 1024 * 1024


def passed_along(block, axis, distance):
    devices = range(lax.axis_size(axis))
    route = [(i - distance, i) for i in devices if i - distance in devices]
    return lax.ppermute(block, axis, route)


def phase_pair(left_count, right_count, period, left_start, right_start):
    left_idx = lax.broadcasted_iota(jnp.int32, (left_count, right_count), 0) + left_start
    right_idx = lax.broadcasted_iota(jnp.int32, (left_count, right_count), 1) + right_start
    angle_all = (left_idx * right_idx % period).astype(jnp.float32) * (TWO_PI / period)
    return (jnp.cos(angle_all), jnp.sin(angle_all))


def contract(pattern, matrix, values):
    return jnp.einsum(
        pattern, matrix, values, precision=HIGHEST, preferred_element_type=jnp.float32
    )


def forward_spectrum(signal):
    seq_parts = lax.axis_size("seq")
    row_count = signal.shape[0]
    row_share = row_count // seq_parts
    period = 2 * seq_parts * row_count
    spread_in = lax.all_to_all(signal[None], "seq", split_axis=1, concat_axis=0, tiled=True)
    outer_cos, outer_sin = phase_pair(2 * seq_parts, seq_parts, 2 * seq_parts, 0, 0)
    section_re = contract("cp,prw->crw", outer_cos, spread_in)
    section_im = -contract("cp,prw->crw", outer_sin, spread_in)
    twist_cos, twist_sin = phase_pair(
        2 * seq_parts, row_share, period, 0, lax.axis_index("seq") * row_share
    )
    twist_cos = twist_cos[:, :, None]
    twist_sin = twist_sin[:, :, None]
    turned_re = section_re * twist_cos + section_im * twist_sin
    turned_im = section_im * twist_cos - section_re * twist_sin
    inner_cos, inner_sin = phase_pair(row_count, row_count, row_count, 0, 0)
    piece_re = lax.all_to_all(turned_re, "seq", split_axis=0, concat_axis=1, tiled=True)
    piece_im = lax.all_to_all(turned_im, "seq", split_axis=0, concat_axis=1, tiled=True)
    spec_re = contract("dm,cmk->cdk", inner_cos, piece_re) + contract(
        "dm,cmk->cdk", inner_sin, piece_im
    )
    spec_im = contract("dm,cmk->cdk", inner_cos, piece_im) - contract(
        "dm,cmk->cdk", inner_sin, piece_re
    )
    return (spec_re, spec_im)


def time_signal(spec_re, spec_im):
    seq_parts = lax.axis_size("seq")
    row_count = spec_re.shape[1]
    period = 2 * seq_parts * row_count
    inner_cos, inner_sin = phase_pair(row_count, row_count, row_count, 0, 0)
    back_re = contract("md,cdk->cmk", inner_cos, spec_re) - contract(
        "md,cdk->cmk", inner_sin, spec_im
    )
    back_im = contract("md,cdk->cmk", inner_cos, spec_im) + contract(
        "md,cdk->cmk", inner_sin, spec_re
    )
    twist_cos, twist_sin = phase_pair(2, row_count, period, 2 * lax.axis_index("seq"), 0)
    twist_cos = twist_cos[:, :, None]
    twist_sin = twist_sin[:, :, None]
    turned_re = back_re * twist_cos - back_im * twist_sin
    turned_im = back_im * twist_cos + back_re * twist_sin
    outer_cos, outer_sin = phase_pair(seq_parts, 2 * seq_parts, 2 * seq_parts, 0, 0)
    piece_re = lax.all_to_all(turned_re, "seq", split_axis=1, concat_axis=0, tiled=True)
    piece_im = lax.all_to_all(turned_im, "seq", split_axis=1, concat_axis=0, tiled=True)
    summed = contract("pc,crk->prk", outer_cos, piece_re) - contract(
        "pc,crk->prk", outer_sin, piece_im
    )
    returned = summed * (1.0 / period)
    return lax.all_to_all(returned, "seq", split_axis=0, concat_axis=1, tiled=True)[0]


def spread_layer(qkv, filt, skip_gain, short_weight, w_out, g_out):
    row_count = qkv.shape[1]
    slab_width = qkv.shape[2]
    tail_rows = passed_along(qkv[:, row_count - 2 :, :], "seq", 1)
    extended = jnp.concatenate([tail_rows, qkv], axis=1)
    short = (
        short_weight[:, 0, None, :] * extended[:, 2:, :]
        + short_weight[:, 1, None, :] * extended[:, 1:-1, :]
        + short_weight[:, 2, None, :] * extended[:, :-2, :]
    )
    query_gate = short[0]
    key_short = short[1]
    value_short = short[2]
    mixed = key_short * value_short
    both_re, both_im = forward_spectrum(jnp.concatenate([mixed, filt], axis=1))
    signal_re = both_re[:, :, :slab_width]
    signal_im = both_im[:, :, :slab_width]
    kernel_re = both_re[:, :, slab_width:]
    kernel_im = both_im[:, :, slab_width:]
    conv_out = time_signal(
        signal_re * kernel_re - signal_im * kernel_im, signal_re * kernel_im + signal_im * kernel_re
    )
    long_out = conv_out + skip_gain * mixed
    gated_out = (query_gate * long_out).astype(jnp.bfloat16)
    projected = jnp.dot(
        lax.all_gather(gated_out, "ch", axis=1, tiled=True),
        w_out,
        preferred_element_type=jnp.float32,
    )
    output = projected.astype(jnp.bfloat16)
    grad_all = lax.all_gather(g_out, "ch", axis=1, tiled=True)
    rows_all = lax.all_to_all(w_out, "ch", split_axis=0, concat_axis=1, tiled=True)
    grad_gated = lax.dot_general(
        grad_all, rows_all, (((1,), (1,)), ((), ())), preferred_element_type=jnp.float32
    )
    grad_long = grad_gated * query_gate
    grad_query = grad_gated * long_out
    grad_re, grad_im = forward_spectrum(grad_long)
    pair_re = jnp.concatenate(
        [kernel_re * grad_re + kernel_im * grad_im, signal_re * grad_re + signal_im * grad_im],
        axis=2,
    )
    pair_im = jnp.concatenate(
        [kernel_re * grad_im - kernel_im * grad_re, signal_re * grad_im - signal_im * grad_re],
        axis=2,
    )
    pair_time = time_signal(pair_re, pair_im)
    grad_mixed = pair_time[:, :slab_width] + skip_gain * grad_long
    token_total = lax.axis_size("seq") * row_count
    grad_filter = pair_time[:, slab_width:] * (1.0 / math.sqrt(token_total))
    grad_short = jnp.stack([grad_query, grad_mixed * value_short, grad_mixed * key_short])
    head_rows = passed_along(grad_short[:, :2, :], "seq", -1)
    extended_grad = jnp.concatenate([grad_short, head_rows], axis=1)
    grad_qkv = (
        short_weight[:, 0, None, :] * extended_grad[:, :-2, :]
        + short_weight[:, 1, None, :] * extended_grad[:, 1:-1, :]
        + short_weight[:, 2, None, :] * extended_grad[:, 2:, :]
    ).astype(jnp.bfloat16)
    return (output, grad_qkv, grad_filter)


def split_bf16(values):
    high = values.astype(np.float32).astype(jnp.bfloat16)
    low = (values - high.astype(np.float64)).astype(np.float32).astype(jnp.bfloat16)
    return high, low


def phase_tables(tokens):
    quarter = tokens // PHASES
    freq = 2 * np.arange(quarter)[:, None] + 1
    turn = math.pi / (2 * tokens)
    angle = (freq * PHASES * np.arange(quarter)[None, :] % (4 * tokens)) * turn
    forward = np.concatenate([np.cos(angle), -np.sin(angle)], axis=0)
    backward = np.transpose(forward) * (1.0 / tokens)
    angle = freq * np.arange(PHASES)[None, :] * turn
    twist = np.concatenate([np.cos(angle), np.sin(angle)], axis=1).astype(np.float32)
    twist = np.pad(twist, ((0, 0), (0, LANES - 2 * PHASES)))
    return (*split_bf16(forward), *split_bf16(backward), twist)


def row_order(rows):
    order = np.zeros((rows, rows), np.float32)
    share = rows // PHASES
    for phase in range(PHASES):
        for j in range(share):
            order[phase * share + j, PHASES * j + phase] = 1.0
    return order.astype(jnp.bfloat16)


def mm(a, b):
    return lax.dot_general(a, b, (((1,), (0,)), ((), ())), preferred_element_type=F32)


def low_lanes(shape):
    return lax.broadcasted_iota(jnp.int32, shape, 1) < HALF


def swap(x):
    return pltpu.roll(x, HALF, 1)


class Stage:
    def __init__(self, count_in, count_out, pieces, refs):
        count = count_in + count_out
        sems = refs[2 * count]
        self.held = refs[count : 2 * count]
        self.count_in = count_in
        self.copies = []
        self.waiting = []
        self.given = []
        used = 0
        for i in range(count):
            here, there = refs[i], self.held[i]
            if i >= count_in:
                here, there = there, here
            cuts = pieces if i == 0 else 1
            step = here.shape[0] // cuts
            group = []
            for cut in range(cuts):
                rows = pl.ds(cut * step, step)
                ends = (here.at[rows], there.at[rows]) if cuts > 1 else (here, there)
                group.append(pltpu.make_async_copy(*ends, sems.at[used]))
                used += 1
            self.copies.append(group)
            self.waiting.append(set(range(cuts)))

    def take(self, index, piece=None):
        for cut in sorted(self.waiting[index]):
            if piece is None or piece == cut:
                self.copies[index][cut].wait()
                self.waiting[index].discard(cut)
        return self.held[index]

    def out(self, index):
        return self.held[self.count_in + index]

    def give(self, index):
        if index not in self.given:
            self.copies[self.count_in + index][0].start()
            self.given.append(index)


def staged(kernel, count_in, count_out, pieces, *refs):
    stage = Stage(count_in, count_out, pieces, refs)
    for i in range(1, count_in):
        stage.copies[i][0].start()
        if i == 1:
            for copy in stage.copies[0]:
                copy.start()
    kernel(stage)
    for i in range(count_in):
        stage.take(i)
    for i in range(count_out):
        stage.give(i)
    for i in range(count_out):
        stage.copies[count_in + i][0].wait()


def call(kernel, out_shape, *args, flops=0, pieces=1):
    far = pl.BlockSpec(memory_space=pltpu.HBM)
    arrays = list(args) + list(out_shape)
    moved = sum(math.prod(a.shape) * a.dtype.itemsize for a in arrays)
    return pl.pallas_call(
        functools.partial(staged, kernel, len(args), len(out_shape), pieces),
        out_shape=out_shape,
        in_specs=[far] * len(args),
        out_specs=[far] * len(out_shape),
        scratch_shapes=[pltpu.VMEM(x.shape, x.dtype) for x in arrays]
        + [pltpu.SemaphoreType.DMA((len(arrays) + pieces - 1,))],
        compiler_params=pltpu.CompilerParams(vmem_limit_bytes=VMEM_LIMIT),
        cost_estimate=pl.CostEstimate(flops=flops, bytes_accessed=moved, transcendentals=0),
    )(*args)


def lane_tile(x, index):
    return x[:, index * LANES : (index + 1) * LANES]


def pair(first, second):
    low = low_lanes(first.shape)
    return jnp.where(low, first, swap(second)), jnp.where(low, swap(first), second)


def both(x):
    turned, low = swap(x), low_lanes(x.shape)
    return jnp.where(low, x, turned), jnp.where(low, turned, x)


def start_kernel(parts, stage):
    partial_ref, send_ref = stage.out(0), stage.out(1)
    g = stage.take(1)[...]
    width = g.shape[1]
    for part in range(parts):
        w = stage.take(0, part)[part * width : (part + 1) * width, :]
        partial_ref[part] = lax.dot_general(
            g, w, (((1,), (1,)), ((), ())), preferred_element_type=F32
        ).astype(BF16)
    stage.give(0)
    order = stage.take(2)[...]
    qkv_ref = stage.take(3)
    query, key, value = [mm(order, qkv_ref[i]) for i in range(3)]
    taps = mm(order, stage.take(4)[...].astype(BF16))
    rows = query.shape[0]
    for tile in range(width // LANES):
        for row, (x, y) in enumerate(((key, value), (query, taps))):
            here = slice(row * rows, (row + 1) * rows)
            x, y = pair(lane_tile(x, tile), lane_tile(y, tile))
            send_ref[2 * tile, here] = x.astype(BF16)
            send_ref[2 * tile + 1, here] = y.astype(BF16)


def sum_kernel(stage):
    parts_ref, order_ref, send_ref = stage.take(0), stage.take(1), stage.out(0)
    total = parts_ref[0].astype(F32)
    for part in range(1, parts_ref.shape[0]):
        total = total + parts_ref[part].astype(F32)
    total = mm(order_ref[...], total.astype(BF16))
    half = total.shape[0] // 2
    for tile in range(total.shape[1] // LANES):
        t = lane_tile(total, tile)
        x, y = pair(t[:half], t[half:])
        send_ref[2 * tile] = x.astype(BF16)
        send_ref[2 * tile + 1] = y.astype(BF16)


def spread_phases(parts):
    (a_re, a_im), (b_re, b_im), (c_re, c_im), (d_re, d_im) = parts
    s_re, s_im, t_re, t_im = a_re + c_re, a_im + c_im, a_re - c_re, a_im - c_im
    u_re, u_im, v_re, v_im = b_re + d_re, b_im + d_im, b_re - d_re, b_im - d_im
    return [
        (s_re + u_re, s_im + u_im),
        (t_re + v_im, t_im - v_re),
        (s_re - u_re, s_im - u_im),
        (t_re - v_im, t_im + v_re),
    ]


def gather_phases(parts):
    (a_re, a_im), (b_re, b_im), (c_re, c_im), (d_re, d_im) = parts
    s_re, s_im, t_re, t_im = a_re + c_re, a_im + c_im, a_re - c_re, a_im - c_im
    u_re, u_im, v_re, v_im = b_re + d_re, b_im + d_im, b_re - d_re, b_im - d_im
    return [
        (s_re + u_re, s_im + u_im),
        (t_re - v_im, t_im + v_re),
        (s_re - u_re, s_im - u_im),
        (t_re + v_im, t_im - v_re),
    ]


def rows_of(ref, start, count):
    block = ref[:, start : start + count, :]
    return block.reshape(ref.shape[0] * count, ref.shape[2])


def turned_back(re, im, twist, phase):
    if phase == 0:
        return re, im
    c, s = twist[:, phase : phase + 1], twist[:, PHASES + phase : PHASES + phase + 1]
    return re * c + im * s, im * c - re * s


def turned_on(re, im, twist, phase):
    if phase == 0:
        return re, im
    c, s = twist[:, phase : phase + 1], twist[:, PHASES + phase : PHASES + phase + 1]
    return re * c - im * s, re * s + im * c


def lane_tile(x, index):
    return x[:, index * LANES : (index + 1) * LANES]


def causal(parts, weight):
    rows = lax.broadcasted_iota(jnp.int32, parts[0].shape, 0)
    two, three = [jnp.where(rows == 0, 0.0, pltpu.roll(parts[p], 1, 0)) for p in (2, 3)]
    once, twice = [three, *parts[:3]], [two, three, *parts[:2]]
    return [
        weight[0:1] * x + weight[1:2] * y + weight[2:3] * z for x, y, z in zip(parts, once, twice)
    ]


def anticausal(parts, weight):
    count = parts[0].shape[0]
    rows = lax.broadcasted_iota(jnp.int32, parts[0].shape, 0)
    zero, one = [
        jnp.where(rows == count - 1, 0.0, pltpu.roll(parts[p], count - 1, 0)) for p in (0, 1)
    ]
    once, twice = [*parts[1:], zero], [*parts[2:], zero, one]
    return [
        weight[0:1] * x + weight[1:2] * y + weight[2:3] * z for x, y, z in zip(parts, once, twice)
    ]


def halves(x):
    high = x.astype(BF16)
    return high, (x - high.astype(F32)).astype(BF16)


def transformed(parts, fh, fl, twist):
    quarter = parts[0].shape[0]
    high, rest = halves(jnp.concatenate(parts, axis=1))
    s = mm(fh, high) + mm(fl, high) + mm(fh, rest)
    turned = []
    for phase in range(PHASES):
        t = lane_tile(s, phase)
        turned.append(turned_back(t[:quarter], t[quarter:], twist, phase))
    return spread_phases(turned)


def in_time(spectrum, bh, bl, twist):
    parts = []
    for phase, (re, im) in enumerate(gather_phases(spectrum)):
        parts.append(jnp.concatenate(turned_on(re, im, twist, phase), axis=0))
    high, rest = halves(jnp.concatenate(parts, axis=1))
    t = mm(bh, high) + mm(bl, high) + mm(bh, rest)
    return [lane_tile(t, phase) for phase in range(PHASES)]


def owner_kernel(stage):
    recv_ref, weight_ref, gain_ref, twist_ref, fh_ref, fl_ref, bh_ref, bl_ref, grad_ref = [
        stage.take(i) for i in range(9)
    ]
    gated_ref, send_ref = stage.out(0), stage.out(1)
    blocks = recv_ref.shape[0]
    rows = recv_ref.shape[1] // 2
    share = rows // PHASES
    quarter = blocks * share
    place = lax.axis_index("seq")
    lanes = pl.ds(pl.multiple_of(place // 2 * LANES, LANES), LANES)
    odd = place % 2 == 1

    def mine(x):
        return jnp.where(odd, swap(x), x)

    weights = [mine(weight_ref[i, :, lanes]) for i in range(3)]
    gain = both(mine(gain_ref[:, lanes]))[0]
    low_w = low_lanes(weights[0].shape)
    only = (lax.broadcasted_iota(jnp.int32, weights[0].shape, 0) == 0).astype(F32)
    weight_pair = jnp.where(low_w, weights[1], swap(weights[2]))
    weight_query = jnp.where(low_w, weights[0], only)
    twist = twist_ref[...]
    low = low_lanes((quarter, LANES))
    tables = (fh_ref[...], fl_ref[...], twist)
    back_tables = (bh_ref[...], bl_ref[...], twist)

    starts = [phase * share for phase in range(PHASES)]
    pairs = causal([rows_of(recv_ref, at, share).astype(F32) for at in starts], weight_pair)
    gates = causal([rows_of(recv_ref, rows + at, share).astype(F32) for at in starts], weight_query)
    mixed = [x * swap(x) for x in pairs]
    query = [both(x)[0] for x in gates]
    spectrum = transformed(
        [jnp.where(low, x, y) for x, y in zip(mixed, gates)], *tables
    )
    product = []
    for re, im in spectrum:
        other_re, other_im = swap(re), swap(im)
        product.append((re * other_re - im * other_im, re * other_im + im * other_re))
    conv = in_time(product, *back_tables)
    long_out = [x + gain * y for x, y in zip(conv, mixed)]
    gated = [x * y for x, y in zip(query, long_out)]
    for phase in range(PHASES // 2):
        t = jnp.where(low, gated[phase], gated[phase + 2]).astype(BF16)
        gated_ref[:, starts[phase] : starts[phase] + share, :] = t.reshape(blocks, share, LANES)
    stage.give(0)

    packed = [rows_of(grad_ref, at, share).astype(F32) for at in starts[:2]]
    grad_gated = [both(x)[i] for i in range(2) for x in packed]
    grad_long = [x * y for x, y in zip(grad_gated, query)]
    grad_query = [x * y for x, y in zip(grad_gated, long_out)]
    product = []
    for (k_re, k_im), (re, im) in zip(spectrum, transformed(grad_long, *tables)):
        product.append((k_re * re + k_im * im, k_re * im - k_im * re))
    times = in_time(product, *back_tables)
    grad_mixed = [both(x + gain * y)[1] for x, y in zip(times, grad_long)]
    grad_pairs = anticausal([x * swap(y) for x, y in zip(grad_mixed, pairs)], weight_pair)
    grad_query = anticausal(grad_query, weight_query)
    scale = 1.0 / math.sqrt(PHASES * quarter)
    for phase, at in enumerate(starts):
        x = grad_pairs[phase].astype(BF16)
        y = jnp.where(low, grad_query[phase], swap(times[phase]) * scale).astype(BF16)
        send_ref[:, at : at + share, :] = x.reshape(blocks, share, LANES)
        send_ref[:, rows + at : rows + at + share, :] = y.reshape(blocks, share, LANES)


def unpacked(blocks, order):
    half = blocks[0].shape[0]
    tiles = []
    for tile in range(len(blocks) // 2):
        top, bottom = pair(blocks[2 * tile].astype(F32), blocks[2 * tile + 1].astype(F32))
        tiles.append(jnp.concatenate([top, bottom], axis=0))
    return mm(order, jnp.concatenate(tiles, axis=1).astype(BF16))


def end_kernel(stage):
    recv_ref, order_ref = stage.take(0), stage.take(1)
    output_ref, grad_ref, filter_ref = [stage.out(i) for i in range(3)]
    order = order_ref[...]
    blocks = recv_ref.shape[0]
    rows = recv_ref.shape[1] // 2
    sides = []
    for at in (0, rows):
        firsts, seconds = [], []
        for tile in range(blocks // 2):
            x, y = [recv_ref[2 * tile + i, at : at + rows].astype(F32) for i in range(2)]
            first, second = pair(x, y)
            firsts.append(first)
            seconds.append(second)
        for side in (firsts, seconds):
            sides.append(mm(order, jnp.concatenate(side, axis=1).astype(BF16)))
    key, value, query, taps = sides
    filter_ref[...] = taps
    stage.give(2)
    grad_ref[0] = query.astype(BF16)
    grad_ref[1] = key.astype(BF16)
    grad_ref[2] = value.astype(BF16)
    stage.give(1)
    gated_ref, w_ref = stage.take(2), stage.take(3)
    parts = gated_ref.shape[0]
    width = w_ref.shape[0] // parts
    total = None
    for part in range(parts):
        block = unpacked([gated_ref[part, i] for i in range(blocks)], order).astype(BF16)
        term = mm(block, w_ref[part * width : (part + 1) * width, :])
        total = term if total is None else total + term
    output_ref[...] = total.astype(BF16)


def exchanged(x, axis):
    return lax.all_to_all(x, axis, split_axis=0, concat_axis=0, tiled=True)


def owner_layer(qkv, filt, skip_gain, short_weight, w_out, g_out):
    shape = jax.ShapeDtypeStruct
    seq_parts, ch_parts = lax.axis_size("seq"), lax.axis_size("ch")
    rows, width = qkv.shape[1], qkv.shape[2]
    tokens = seq_parts * rows
    order = row_order(rows)
    fh, fl, bh, bl, twist = phase_tables(tokens)
    table_flops = 2 * 2 * 2 * 3 * tokens * tokens // PHASES * LANES
    product_flops = 2 * rows * width * width * ch_parts
    packed = shape((seq_parts, rows // 2, LANES), BF16)
    double = shape((seq_parts, 2 * rows, LANES), BF16)

    partial, send = call(
        functools.partial(start_kernel, ch_parts),
        [shape((ch_parts, rows, width), BF16), double],
        w_out,
        g_out,
        order,
        qkv,
        filt,
        flops=product_flops,
        pieces=ch_parts,
    )
    partial = exchanged(partial, "ch")
    recv = exchanged(send, "seq")
    (send,) = call(sum_kernel, [packed], partial, order)
    grad_recv = exchanged(send, "seq")
    gated, send = call(
        owner_kernel,
        [packed, double],
        recv,
        short_weight,
        skip_gain[None, :],
        twist,
        fh,
        fl,
        bh,
        bl,
        grad_recv,
        flops=table_flops,
    )
    gated = exchanged(gated, "seq")
    grad_recv = exchanged(send, "seq")
    gated = lax.all_gather(gated, "ch", axis=0, tiled=False)
    output, grad_qkv, grad_filter = call(
        end_kernel,
        [shape((rows, width), BF16), shape((3, rows, width), BF16), shape((rows, width), F32)],
        grad_recv,
        order.T,
        gated,
        w_out,
        flops=product_flops,
    )
    return (output, grad_qkv, grad_filter)


def local(qkv, filt, skip_gain, short_weight, w_out, g_out):
    seq_parts = lax.axis_size("seq")
    rows, width = qkv.shape[1], qkv.shape[2]
    fits = width == HALF * seq_parts and rows % HALF == 0 and rows * seq_parts <= 2048
    if fits and lax.axis_size("ch") == 4:
        return owner_layer(qkv, filt, skip_gain, short_weight, w_out, g_out)
    return spread_layer(qkv, filt, skip_gain, short_weight, w_out, g_out)


def solution(mesh):
    in_specs = (
        P(None, "seq", "ch"),
        P("seq", "ch"),
        P("ch"),
        P(None, None, "ch"),
        P(None, "ch"),
        P("seq", "ch"),
    )
    out_specs = (P("seq", "ch"), P(None, "seq", "ch"), P("seq", "ch"))
    return jax.shard_map(local, mesh=mesh, in_specs=in_specs, out_specs=out_specs, check_vma=False)
```

```python
import functools
import math

import jax
import jax.numpy as jnp
import numpy as np
from jax import lax
from jax.experimental import pallas as pl
from jax.experimental.pallas import tpu as pltpu
from jax.sharding import PartitionSpec as P

HIGHEST = lax.Precision.HIGHEST
TWO_PI = 2.0 * math.pi
LANES = 128
HALF = 64
PHASES = 4
BF16 = jnp.bfloat16
F32 = jnp.float32
VMEM_LIMIT = 64 * 1024 * 1024


def passed_along(block, axis, distance):
    devices = range(lax.axis_size(axis))
    route = [(i - distance, i) for i in devices if i - distance in devices]
    return lax.ppermute(block, axis, route)


def phase_pair(left_count, right_count, period, left_start, right_start):
    left_idx = lax.broadcasted_iota(jnp.int32, (left_count, right_count), 0) + left_start
    right_idx = lax.broadcasted_iota(jnp.int32, (left_count, right_count), 1) + right_start
    angle_all = (left_idx * right_idx % period).astype(jnp.float32) * (TWO_PI / period)
    return (jnp.cos(angle_all), jnp.sin(angle_all))


def contract(pattern, matrix, values):
    return jnp.einsum(
        pattern, matrix, values, precision=HIGHEST, preferred_element_type=jnp.float32
    )


def forward_spectrum(signal):
    seq_parts = lax.axis_size("seq")
    row_count = signal.shape[0]
    row_share = row_count // seq_parts
    period = 2 * seq_parts * row_count
    spread_in = lax.all_to_all(signal[None], "seq", split_axis=1, concat_axis=0, tiled=True)
    outer_cos, outer_sin = phase_pair(2 * seq_parts, seq_parts, 2 * seq_parts, 0, 0)
    section_re = contract("cp,prw->crw", outer_cos, spread_in)
    section_im = -contract("cp,prw->crw", outer_sin, spread_in)
    twist_cos, twist_sin = phase_pair(
        2 * seq_parts, row_share, period, 0, lax.axis_index("seq") * row_share
    )
    twist_cos = twist_cos[:, :, None]
    twist_sin = twist_sin[:, :, None]
    turned_re = section_re * twist_cos + section_im * twist_sin
    turned_im = section_im * twist_cos - section_re * twist_sin
    inner_cos, inner_sin = phase_pair(row_count, row_count, row_count, 0, 0)
    piece_re = lax.all_to_all(turned_re, "seq", split_axis=0, concat_axis=1, tiled=True)
    piece_im = lax.all_to_all(turned_im, "seq", split_axis=0, concat_axis=1, tiled=True)
    spec_re = contract("dm,cmk->cdk", inner_cos, piece_re) + contract(
        "dm,cmk->cdk", inner_sin, piece_im
    )
    spec_im = contract("dm,cmk->cdk", inner_cos, piece_im) - contract(
        "dm,cmk->cdk", inner_sin, piece_re
    )
    return (spec_re, spec_im)


def time_signal(spec_re, spec_im):
    seq_parts = lax.axis_size("seq")
    row_count = spec_re.shape[1]
    period = 2 * seq_parts * row_count
    inner_cos, inner_sin = phase_pair(row_count, row_count, row_count, 0, 0)
    back_re = contract("md,cdk->cmk", inner_cos, spec_re) - contract(
        "md,cdk->cmk", inner_sin, spec_im
    )
    back_im = contract("md,cdk->cmk", inner_cos, spec_im) + contract(
        "md,cdk->cmk", inner_sin, spec_re
    )
    twist_cos, twist_sin = phase_pair(2, row_count, period, 2 * lax.axis_index("seq"), 0)
    twist_cos = twist_cos[:, :, None]
    twist_sin = twist_sin[:, :, None]
    turned_re = back_re * twist_cos - back_im * twist_sin
    turned_im = back_im * twist_cos + back_re * twist_sin
    outer_cos, outer_sin = phase_pair(seq_parts, 2 * seq_parts, 2 * seq_parts, 0, 0)
    piece_re = lax.all_to_all(turned_re, "seq", split_axis=1, concat_axis=0, tiled=True)
    piece_im = lax.all_to_all(turned_im, "seq", split_axis=1, concat_axis=0, tiled=True)
    summed = contract("pc,crk->prk", outer_cos, piece_re) - contract(
        "pc,crk->prk", outer_sin, piece_im
    )
    returned = summed * (1.0 / period)
    return lax.all_to_all(returned, "seq", split_axis=0, concat_axis=1, tiled=True)[0]


def spread_layer(qkv, filt, skip_gain, short_weight, w_out, g_out):
    row_count = qkv.shape[1]
    slab_width = qkv.shape[2]
    tail_rows = passed_along(qkv[:, row_count - 2 :, :], "seq", 1)
    extended = jnp.concatenate([tail_rows, qkv], axis=1)
    short = (
        short_weight[:, 0, None, :] * extended[:, 2:, :]
        + short_weight[:, 1, None, :] * extended[:, 1:-1, :]
        + short_weight[:, 2, None, :] * extended[:, :-2, :]
    )
    query_gate = short[0]
    key_short = short[1]
    value_short = short[2]
    mixed = key_short * value_short
    both_re, both_im = forward_spectrum(jnp.concatenate([mixed, filt], axis=1))
    signal_re = both_re[:, :, :slab_width]
    signal_im = both_im[:, :, :slab_width]
    kernel_re = both_re[:, :, slab_width:]
    kernel_im = both_im[:, :, slab_width:]
    conv_out = time_signal(
        signal_re * kernel_re - signal_im * kernel_im, signal_re * kernel_im + signal_im * kernel_re
    )
    long_out = conv_out + skip_gain * mixed
    gated_out = (query_gate * long_out).astype(jnp.bfloat16)
    projected = jnp.dot(
        lax.all_gather(gated_out, "ch", axis=1, tiled=True),
        w_out,
        preferred_element_type=jnp.float32,
    )
    output = projected.astype(jnp.bfloat16)
    grad_all = lax.all_gather(g_out, "ch", axis=1, tiled=True)
    rows_all = lax.all_to_all(w_out, "ch", split_axis=0, concat_axis=1, tiled=True)
    grad_gated = lax.dot_general(
        grad_all, rows_all, (((1,), (1,)), ((), ())), preferred_element_type=jnp.float32
    )
    grad_long = grad_gated * query_gate
    grad_query = grad_gated * long_out
    grad_re, grad_im = forward_spectrum(grad_long)
    pair_re = jnp.concatenate(
        [kernel_re * grad_re + kernel_im * grad_im, signal_re * grad_re + signal_im * grad_im],
        axis=2,
    )
    pair_im = jnp.concatenate(
        [kernel_re * grad_im - kernel_im * grad_re, signal_re * grad_im - signal_im * grad_re],
        axis=2,
    )
    pair_time = time_signal(pair_re, pair_im)
    grad_mixed = pair_time[:, :slab_width] + skip_gain * grad_long
    token_total = lax.axis_size("seq") * row_count
    grad_filter = pair_time[:, slab_width:] * (1.0 / math.sqrt(token_total))
    grad_short = jnp.stack([grad_query, grad_mixed * value_short, grad_mixed * key_short])
    head_rows = passed_along(grad_short[:, :2, :], "seq", -1)
    extended_grad = jnp.concatenate([grad_short, head_rows], axis=1)
    grad_qkv = (
        short_weight[:, 0, None, :] * extended_grad[:, :-2, :]
        + short_weight[:, 1, None, :] * extended_grad[:, 1:-1, :]
        + short_weight[:, 2, None, :] * extended_grad[:, 2:, :]
    ).astype(jnp.bfloat16)
    return (output, grad_qkv, grad_filter)


def split_bf16(values):
    high = values.astype(np.float32).astype(jnp.bfloat16)
    low = (values - high.astype(np.float64)).astype(np.float32).astype(jnp.bfloat16)
    return high, low


def phase_tables(tokens):
    quarter = tokens // PHASES
    freq = 2 * np.arange(quarter)[:, None] + 1
    turn = math.pi / (2 * tokens)
    angle = (freq * PHASES * np.arange(quarter)[None, :] % (4 * tokens)) * turn
    forward = np.concatenate([np.cos(angle), -np.sin(angle)], axis=0)
    backward = np.transpose(forward) * (1.0 / tokens)
    angle = freq * np.arange(PHASES)[None, :] * turn
    twist = np.concatenate([np.cos(angle), np.sin(angle)], axis=1).astype(np.float32)
    twist = np.pad(twist, ((0, 0), (0, LANES - 2 * PHASES)))
    return (*split_bf16(forward), *split_bf16(backward), twist)


def row_order(rows):
    order = np.zeros((rows, rows), np.float32)
    share = rows // PHASES
    for phase in range(PHASES):
        for j in range(share):
            order[phase * share + j, PHASES * j + phase] = 1.0
    return order.astype(jnp.bfloat16)


def mm(a, b):
    return lax.dot_general(a, b, (((1,), (0,)), ((), ())), preferred_element_type=F32)


def low_lanes(shape):
    return lax.broadcasted_iota(jnp.int32, shape, 1) < HALF


def swap(x):
    return pltpu.roll(x, HALF, 1)


class Stage:
    def __init__(self, count_in, count_out, pieces, refs):
        me = lax.axis_index("ch") if pieces > 1 else 0
        count = count_in + count_out
        sems = refs[2 * count]
        self.held = refs[count : 2 * count]
        self.count_in = count_in
        self.copies = []
        self.waiting = []
        self.given = []
        used = 0
        for i in range(count):
            here, there = refs[i], self.held[i]
            if i >= count_in:
                here, there = there, here
            cuts = pieces if i == 0 else 1
            step = here.shape[0] // cuts
            group = []
            for cut in range(cuts):
                ends = (here, there)
                if cuts > 1:
                    rows = pl.ds(pl.multiple_of((me ^ cut) * step, step), step)
                    ends = (here.at[rows], there.at[pl.ds(cut * step, step)])
                group.append(pltpu.make_async_copy(*ends, sems.at[used]))
                used += 1
            self.copies.append(group)
            self.waiting.append(set(range(cuts)))

    def take(self, index, piece=None):
        for cut in sorted(self.waiting[index]):
            if piece is None or piece == cut:
                self.copies[index][cut].wait()
                self.waiting[index].discard(cut)
        return self.held[index]

    def out(self, index):
        return self.held[self.count_in + index]

    def give(self, index):
        if index not in self.given:
            self.copies[self.count_in + index][0].start()
            self.given.append(index)


def staged(kernel, count_in, count_out, pieces, *refs):
    stage = Stage(count_in, count_out, pieces, refs)
    for i in range(1, count_in):
        stage.copies[i][0].start()
        if i == 1:
            for copy in stage.copies[0]:
                copy.start()
    kernel(stage)
    for i in range(count_in):
        stage.take(i)
    for i in range(count_out):
        stage.give(i)
    for i in range(count_out):
        stage.copies[count_in + i][0].wait()


def call(kernel, out_shape, *args, flops=0, pieces=1):
    far = pl.BlockSpec(memory_space=pltpu.HBM)
    arrays = list(args) + list(out_shape)
    moved = sum(math.prod(a.shape) * a.dtype.itemsize for a in arrays)
    return pl.pallas_call(
        functools.partial(staged, kernel, len(args), len(out_shape), pieces),
        out_shape=out_shape,
        in_specs=[far] * len(args),
        out_specs=[far] * len(out_shape),
        scratch_shapes=[pltpu.VMEM(x.shape, x.dtype) for x in arrays]
        + [pltpu.SemaphoreType.DMA((len(arrays) + pieces - 1,))],
        compiler_params=pltpu.CompilerParams(vmem_limit_bytes=VMEM_LIMIT),
        cost_estimate=pl.CostEstimate(flops=flops, bytes_accessed=moved, transcendentals=0),
    )(*args)


def lane_tile(x, index):
    return x[:, index * LANES : (index + 1) * LANES]


def pair(first, second):
    low = low_lanes(first.shape)
    return jnp.where(low, first, swap(second)), jnp.where(low, swap(first), second)


def both(x):
    turned, low = swap(x), low_lanes(x.shape)
    return jnp.where(low, x, turned), jnp.where(low, turned, x)


def start_kernel(parts, stage):
    g = stage.take(1)[...]
    width = g.shape[1]
    for part in range(parts):
        w = stage.take(0, part)[part * width : (part + 1) * width, :]
        stage.out(part)[...] = lax.dot_general(
            g, w, (((1,), (1,)), ((), ())), preferred_element_type=F32
        ).astype(BF16)
        stage.give(part)
    send_ref = stage.out(parts)
    order = stage.take(2)[...]
    qkv_ref = stage.take(3)
    query, key, value = [mm(order, qkv_ref[i]) for i in range(3)]
    taps = mm(order, stage.take(4)[...].astype(BF16))
    rows = query.shape[0]
    for tile in range(width // LANES):
        for row, (x, y) in enumerate(((key, value), (query, taps))):
            here = slice(row * rows, (row + 1) * rows)
            x, y = pair(lane_tile(x, tile), lane_tile(y, tile))
            send_ref[2 * tile, here] = x.astype(BF16)
            send_ref[2 * tile + 1, here] = y.astype(BF16)


def sum_kernel(parts, stage):
    send_ref, order_ref = stage.out(0), stage.take(0)
    total = stage.take(1)[...].astype(F32)
    for part in range(1, parts):
        total = total + stage.take(1 + part)[...].astype(F32)
    total = mm(order_ref[...], total.astype(BF16))
    half = total.shape[0] // 2
    for tile in range(total.shape[1] // LANES):
        t = lane_tile(total, tile)
        x, y = pair(t[:half], t[half:])
        send_ref[2 * tile] = x.astype(BF16)
        send_ref[2 * tile + 1] = y.astype(BF16)


def spread_phases(parts):
    (a_re, a_im), (b_re, b_im), (c_re, c_im), (d_re, d_im) = parts
    s_re, s_im, t_re, t_im = a_re + c_re, a_im + c_im, a_re - c_re, a_im - c_im
    u_re, u_im, v_re, v_im = b_re + d_re, b_im + d_im, b_re - d_re, b_im - d_im
    return [
        (s_re + u_re, s_im + u_im),
        (t_re + v_im, t_im - v_re),
        (s_re - u_re, s_im - u_im),
        (t_re - v_im, t_im + v_re),
    ]


def gather_phases(parts):
    (a_re, a_im), (b_re, b_im), (c_re, c_im), (d_re, d_im) = parts
    s_re, s_im, t_re, t_im = a_re + c_re, a_im + c_im, a_re - c_re, a_im - c_im
    u_re, u_im, v_re, v_im = b_re + d_re, b_im + d_im, b_re - d_re, b_im - d_im
    return [
        (s_re + u_re, s_im + u_im),
        (t_re - v_im, t_im + v_re),
        (s_re - u_re, s_im - u_im),
        (t_re + v_im, t_im - v_re),
    ]


def rows_of(ref, start, count):
    block = ref[:, start : start + count, :]
    return block.reshape(ref.shape[0] * count, ref.shape[2])


def turned_back(re, im, twist, phase):
    if phase == 0:
        return re, im
    c, s = twist[:, phase : phase + 1], twist[:, PHASES + phase : PHASES + phase + 1]
    return re * c + im * s, im * c - re * s


def turned_on(re, im, twist, phase):
    if phase == 0:
        return re, im
    c, s = twist[:, phase : phase + 1], twist[:, PHASES + phase : PHASES + phase + 1]
    return re * c - im * s, re * s + im * c


def lane_tile(x, index):
    return x[:, index * LANES : (index + 1) * LANES]


def causal(parts, weight):
    rows = lax.broadcasted_iota(jnp.int32, parts[0].shape, 0)
    two, three = [jnp.where(rows == 0, 0.0, pltpu.roll(parts[p], 1, 0)) for p in (2, 3)]
    once, twice = [three, *parts[:3]], [two, three, *parts[:2]]
    return [
        weight[0:1] * x + weight[1:2] * y + weight[2:3] * z for x, y, z in zip(parts, once, twice)
    ]


def anticausal(parts, weight):
    count = parts[0].shape[0]
    rows = lax.broadcasted_iota(jnp.int32, parts[0].shape, 0)
    zero, one = [
        jnp.where(rows == count - 1, 0.0, pltpu.roll(parts[p], count - 1, 0)) for p in (0, 1)
    ]
    once, twice = [*parts[1:], zero], [*parts[2:], zero, one]
    return [
        weight[0:1] * x + weight[1:2] * y + weight[2:3] * z for x, y, z in zip(parts, once, twice)
    ]


def halves(x):
    high = x.astype(BF16)
    return high, (x - high.astype(F32)).astype(BF16)


def transformed(parts, fh, fl, twist):
    quarter = parts[0].shape[0]
    high, rest = halves(jnp.concatenate(parts, axis=1))
    s = mm(fh, high) + mm(fl, high) + mm(fh, rest)
    turned = []
    for phase in range(PHASES):
        t = lane_tile(s, phase)
        turned.append(turned_back(t[:quarter], t[quarter:], twist, phase))
    return spread_phases(turned)


def in_time(spectrum, bh, bl, twist):
    parts = []
    for phase, (re, im) in enumerate(gather_phases(spectrum)):
        parts.append(jnp.concatenate(turned_on(re, im, twist, phase), axis=0))
    high, rest = halves(jnp.concatenate(parts, axis=1))
    t = mm(bh, high) + mm(bl, high) + mm(bh, rest)
    return [lane_tile(t, phase) for phase in range(PHASES)]


def own_weights(weight_ref, gain_ref):
    place = lax.axis_index("seq")
    lanes = pl.ds(pl.multiple_of(place // 2 * LANES, LANES), LANES)
    odd = place % 2 == 1

    def mine(x):
        return jnp.where(odd, swap(x), x)

    weights = [mine(weight_ref[i, :, lanes]) for i in range(3)]
    gain = both(mine(gain_ref[:, lanes]))[0]
    low = low_lanes(weights[0].shape)
    only = (lax.broadcasted_iota(jnp.int32, weights[0].shape, 0) == 0).astype(F32)
    pair_weight = jnp.where(low, weights[1], swap(weights[2]))
    query_weight = jnp.where(low, weights[0], only)
    return pair_weight, query_weight, gain


def forward_kernel(stage):
    recv_ref, weight_ref, gain_ref = [stage.take(i) for i in range(3)]
    gated_ref, spec_ref, pairs_ref, gates_ref = [stage.out(i) for i in range(4)]
    blocks = recv_ref.shape[0]
    rows = recv_ref.shape[1] // 2
    share = rows // PHASES
    quarter = blocks * share
    low = low_lanes((quarter, LANES))
    pair_weight, query_weight, gain = own_weights(weight_ref, gain_ref)

    starts = [phase * share for phase in range(PHASES)]
    pairs = causal([rows_of(recv_ref, at, share).astype(F32) for at in starts], pair_weight)
    gates = causal([rows_of(recv_ref, rows + at, share).astype(F32) for at in starts], query_weight)
    for phase in range(PHASES):
        pairs_ref[phase] = pairs[phase]
    stage.give(2)
    mixed = [x * swap(x) for x in pairs]
    query = [both(x)[0] for x in gates]
    fh, fl, twist = [stage.take(i)[...] for i in (3, 4, 5)]
    spectrum = transformed([jnp.where(low, x, y) for x, y in zip(mixed, gates)], fh, fl, twist)
    product = []
    for r, (re, im) in enumerate(spectrum):
        spec_ref[r, :quarter, :] = re
        spec_ref[r, quarter:, :] = im
        other_re, other_im = swap(re), swap(im)
        product.append((re * other_re - im * other_im, re * other_im + im * other_re))
    stage.give(1)
    conv = in_time(product, stage.take(6)[...], stage.take(7)[...], twist)
    long_out = [x + gain * y for x, y in zip(conv, mixed)]
    gated = [x * y for x, y in zip(query, long_out)]
    for phase in range(PHASES // 2):
        t = jnp.where(low, gated[phase], gated[phase + 2]).astype(BF16)
        gated_ref[:, starts[phase] : starts[phase] + share, :] = t.reshape(blocks, share, LANES)
    stage.give(0)
    for phase in range(PHASES):
        gates_ref[phase] = jnp.where(low, query[phase], long_out[phase])


def backward_kernel(stage):
    grad_ref, weight_ref, gain_ref, gates_ref = [stage.take(i) for i in range(4)]
    send_ref = stage.out(0)
    blocks = grad_ref.shape[0]
    share = grad_ref.shape[1] // 2
    rows = PHASES * share
    quarter = blocks * share
    low = low_lanes((quarter, LANES))
    pair_weight, query_weight, gain = own_weights(weight_ref, gain_ref)

    starts = [phase * share for phase in range(PHASES)]
    packed = [rows_of(grad_ref, at, share).astype(F32) for at in starts[:2]]
    grad_gated = [both(x)[i] for i in range(2) for x in packed]
    gates = [both(gates_ref[phase]) for phase in range(PHASES)]
    grad_long = [x * y for x, (y, _) in zip(grad_gated, gates)]
    grad_query = anticausal([x * y for x, (_, y) in zip(grad_gated, gates)], query_weight)
    fh, fl, twist = [stage.take(i)[...] for i in (4, 5, 6)]
    grad_spectrum = transformed(grad_long, fh, fl, twist)
    spec_ref = stage.take(7)
    product = []
    for r, (re, im) in enumerate(grad_spectrum):
        k_re, k_im = spec_ref[r, :quarter, :], spec_ref[r, quarter:, :]
        product.append((k_re * re + k_im * im, k_re * im - k_im * re))
    times = in_time(product, stage.take(8)[...], stage.take(9)[...], twist)
    pairs_ref = stage.take(10)
    grad_mixed = [both(x + gain * y)[1] for x, y in zip(times, grad_long)]
    grad_pairs = anticausal(
        [x * swap(pairs_ref[phase]) for phase, x in enumerate(grad_mixed)], pair_weight
    )
    scale = 1.0 / math.sqrt(PHASES * quarter)
    for phase, at in enumerate(starts):
        x = grad_pairs[phase].astype(BF16)
        y = jnp.where(low, grad_query[phase], swap(times[phase]) * scale).astype(BF16)
        send_ref[:, at : at + share, :] = x.reshape(blocks, share, LANES)
        send_ref[:, rows + at : rows + at + share, :] = y.reshape(blocks, share, LANES)


def unpacked(blocks, order):
    half = blocks[0].shape[0]
    tiles = []
    for tile in range(len(blocks) // 2):
        top, bottom = pair(blocks[2 * tile].astype(F32), blocks[2 * tile + 1].astype(F32))
        tiles.append(jnp.concatenate([top, bottom], axis=0))
    return mm(order, jnp.concatenate(tiles, axis=1).astype(BF16))


def end_kernel(stage):
    recv_ref, order_ref = stage.take(0), stage.take(1)
    output_ref, grad_ref, filter_ref = [stage.out(i) for i in range(3)]
    order = order_ref[...]
    blocks = recv_ref.shape[0]
    rows = recv_ref.shape[1] // 2
    sides = []
    for at in (0, rows):
        firsts, seconds = [], []
        for tile in range(blocks // 2):
            x, y = [recv_ref[2 * tile + i, at : at + rows].astype(F32) for i in range(2)]
            first, second = pair(x, y)
            firsts.append(first)
            seconds.append(second)
        for side in (firsts, seconds):
            sides.append(mm(order, jnp.concatenate(side, axis=1).astype(BF16)))
    key, value, query, taps = sides
    filter_ref[...] = taps
    stage.give(2)
    grad_ref[0] = query.astype(BF16)
    grad_ref[1] = key.astype(BF16)
    grad_ref[2] = value.astype(BF16)
    stage.give(1)
    gated_ref, w_ref = stage.take(2), stage.take(3)
    parts = gated_ref.shape[0]
    width = w_ref.shape[0] // parts
    total = None
    for part in range(parts):
        block = unpacked([gated_ref[part, i] for i in range(blocks)], order).astype(BF16)
        term = mm(block, w_ref[part * width : (part + 1) * width, :])
        total = term if total is None else total + term
    output_ref[...] = total.astype(BF16)


def partner(x, axis, mask):
    return lax.ppermute(x, axis, [(i, i ^ mask) for i in range(lax.axis_size(axis))])


def exchanged(x, axis):
    return lax.all_to_all(x, axis, split_axis=0, concat_axis=0, tiled=True)


def owner_layer(qkv, filt, skip_gain, short_weight, w_out, g_out):
    shape = jax.ShapeDtypeStruct
    seq_parts, ch_parts = lax.axis_size("seq"), lax.axis_size("ch")
    rows, width = qkv.shape[1], qkv.shape[2]
    tokens = seq_parts * rows
    order = row_order(rows)
    fh, fl, bh, bl, twist = phase_tables(tokens)
    table_flops = 2 * 2 * 2 * 3 * tokens * tokens // PHASES * LANES
    product_flops = 2 * rows * width * width * ch_parts
    packed = shape((seq_parts, rows // 2, LANES), BF16)
    double = shape((seq_parts, 2 * rows, LANES), BF16)

    *partial, send = call(
        functools.partial(start_kernel, ch_parts),
        [shape((rows, width), BF16)] * ch_parts + [double],
        w_out,
        g_out,
        order,
        qkv,
        filt,
        flops=product_flops,
        pieces=ch_parts,
    )
    recv = exchanged(send, "seq")
    partial = [partner(x, "ch", mask) if mask else x for mask, x in enumerate(partial)]
    (send,) = call(functools.partial(sum_kernel, ch_parts), [packed], order, *partial)
    grad_recv = exchanged(send, "seq")
    gain = skip_gain[None, :]
    quarter = tokens // PHASES
    gated, spec, pairs, gates = call(
        forward_kernel,
        [
            packed,
            shape((PHASES, 2 * quarter, LANES), F32),
            shape((PHASES, quarter, LANES), F32),
            shape((PHASES, quarter, LANES), F32),
        ],
        recv,
        short_weight,
        gain,
        fh,
        fl,
        twist,
        bh,
        bl,
        flops=table_flops,
    )
    gated = exchanged(gated, "seq")
    (send,) = call(
        backward_kernel,
        [double],
        grad_recv,
        short_weight,
        gain,
        gates,
        fh,
        fl,
        twist,
        spec,
        bh,
        bl,
        pairs,
        flops=table_flops,
    )
    grad_recv = exchanged(send, "seq")
    gated = lax.all_gather(gated, "ch", axis=0, tiled=False)
    output, grad_qkv, grad_filter = call(
        end_kernel,
        [shape((rows, width), BF16), shape((3, rows, width), BF16), shape((rows, width), F32)],
        grad_recv,
        order.T,
        gated,
        w_out,
        flops=product_flops,
    )
    return (output, grad_qkv, grad_filter)


def local(qkv, filt, skip_gain, short_weight, w_out, g_out):
    seq_parts = lax.axis_size("seq")
    rows, width = qkv.shape[1], qkv.shape[2]
    fits = width == HALF * seq_parts and rows % HALF == 0 and rows * seq_parts <= 2048
    if fits and lax.axis_size("ch") == 4:
        return owner_layer(qkv, filt, skip_gain, short_weight, w_out, g_out)
    return spread_layer(qkv, filt, skip_gain, short_weight, w_out, g_out)


def solution(mesh):
    in_specs = (
        P(None, "seq", "ch"),
        P("seq", "ch"),
        P("ch"),
        P(None, None, "ch"),
        P(None, "ch"),
        P("seq", "ch"),
    )
    out_specs = (P("seq", "ch"), P(None, "seq", "ch"), P("seq", "ch"))
    return jax.shard_map(local, mesh=mesh, in_specs=in_specs, out_specs=out_specs, check_vma=False)
```

```python
import functools
import math

import jax
import jax.numpy as jnp
import numpy as np
from jax import lax
from jax.experimental import pallas as pl
from jax.experimental.pallas import tpu as pltpu
from jax.sharding import PartitionSpec as P

HIGHEST = lax.Precision.HIGHEST
TWO_PI = 2.0 * math.pi
LANES = 128
HALF = 64
PHASES = 4
BF16 = jnp.bfloat16
F32 = jnp.float32
VMEM_LIMIT = 64 * 1024 * 1024


def passed_along(block, axis, distance):
    devices = range(lax.axis_size(axis))
    route = [(i - distance, i) for i in devices if i - distance in devices]
    return lax.ppermute(block, axis, route)


def phase_pair(left_count, right_count, period, left_start, right_start):
    left_idx = lax.broadcasted_iota(jnp.int32, (left_count, right_count), 0) + left_start
    right_idx = lax.broadcasted_iota(jnp.int32, (left_count, right_count), 1) + right_start
    angle_all = (left_idx * right_idx % period).astype(jnp.float32) * (TWO_PI / period)
    return (jnp.cos(angle_all), jnp.sin(angle_all))


def contract(pattern, matrix, values):
    return jnp.einsum(
        pattern, matrix, values, precision=HIGHEST, preferred_element_type=jnp.float32
    )


def forward_spectrum(signal):
    seq_parts = lax.axis_size("seq")
    row_count = signal.shape[0]
    row_share = row_count // seq_parts
    period = 2 * seq_parts * row_count
    spread_in = lax.all_to_all(signal[None], "seq", split_axis=1, concat_axis=0, tiled=True)
    outer_cos, outer_sin = phase_pair(2 * seq_parts, seq_parts, 2 * seq_parts, 0, 0)
    section_re = contract("cp,prw->crw", outer_cos, spread_in)
    section_im = -contract("cp,prw->crw", outer_sin, spread_in)
    twist_cos, twist_sin = phase_pair(
        2 * seq_parts, row_share, period, 0, lax.axis_index("seq") * row_share
    )
    twist_cos = twist_cos[:, :, None]
    twist_sin = twist_sin[:, :, None]
    turned_re = section_re * twist_cos + section_im * twist_sin
    turned_im = section_im * twist_cos - section_re * twist_sin
    inner_cos, inner_sin = phase_pair(row_count, row_count, row_count, 0, 0)
    piece_re = lax.all_to_all(turned_re, "seq", split_axis=0, concat_axis=1, tiled=True)
    piece_im = lax.all_to_all(turned_im, "seq", split_axis=0, concat_axis=1, tiled=True)
    spec_re = contract("dm,cmk->cdk", inner_cos, piece_re) + contract(
        "dm,cmk->cdk", inner_sin, piece_im
    )
    spec_im = contract("dm,cmk->cdk", inner_cos, piece_im) - contract(
        "dm,cmk->cdk", inner_sin, piece_re
    )
    return (spec_re, spec_im)


def time_signal(spec_re, spec_im):
    seq_parts = lax.axis_size("seq")
    row_count = spec_re.shape[1]
    period = 2 * seq_parts * row_count
    inner_cos, inner_sin = phase_pair(row_count, row_count, row_count, 0, 0)
    back_re = contract("md,cdk->cmk", inner_cos, spec_re) - contract(
        "md,cdk->cmk", inner_sin, spec_im
    )
    back_im = contract("md,cdk->cmk", inner_cos, spec_im) + contract(
        "md,cdk->cmk", inner_sin, spec_re
    )
    twist_cos, twist_sin = phase_pair(2, row_count, period, 2 * lax.axis_index("seq"), 0)
    twist_cos = twist_cos[:, :, None]
    twist_sin = twist_sin[:, :, None]
    turned_re = back_re * twist_cos - back_im * twist_sin
    turned_im = back_im * twist_cos + back_re * twist_sin
    outer_cos, outer_sin = phase_pair(seq_parts, 2 * seq_parts, 2 * seq_parts, 0, 0)
    piece_re = lax.all_to_all(turned_re, "seq", split_axis=1, concat_axis=0, tiled=True)
    piece_im = lax.all_to_all(turned_im, "seq", split_axis=1, concat_axis=0, tiled=True)
    summed = contract("pc,crk->prk", outer_cos, piece_re) - contract(
        "pc,crk->prk", outer_sin, piece_im
    )
    returned = summed * (1.0 / period)
    return lax.all_to_all(returned, "seq", split_axis=0, concat_axis=1, tiled=True)[0]


def spread_layer(qkv, filt, skip_gain, short_weight, w_out, g_out):
    row_count = qkv.shape[1]
    slab_width = qkv.shape[2]
    tail_rows = passed_along(qkv[:, row_count - 2 :, :], "seq", 1)
    extended = jnp.concatenate([tail_rows, qkv], axis=1)
    short = (
        short_weight[:, 0, None, :] * extended[:, 2:, :]
        + short_weight[:, 1, None, :] * extended[:, 1:-1, :]
        + short_weight[:, 2, None, :] * extended[:, :-2, :]
    )
    query_gate = short[0]
    key_short = short[1]
    value_short = short[2]
    mixed = key_short * value_short
    both_re, both_im = forward_spectrum(jnp.concatenate([mixed, filt], axis=1))
    signal_re = both_re[:, :, :slab_width]
    signal_im = both_im[:, :, :slab_width]
    kernel_re = both_re[:, :, slab_width:]
    kernel_im = both_im[:, :, slab_width:]
    conv_out = time_signal(
        signal_re * kernel_re - signal_im * kernel_im, signal_re * kernel_im + signal_im * kernel_re
    )
    long_out = conv_out + skip_gain * mixed
    gated_out = (query_gate * long_out).astype(jnp.bfloat16)
    projected = jnp.dot(
        lax.all_gather(gated_out, "ch", axis=1, tiled=True),
        w_out,
        preferred_element_type=jnp.float32,
    )
    output = projected.astype(jnp.bfloat16)
    grad_all = lax.all_gather(g_out, "ch", axis=1, tiled=True)
    rows_all = lax.all_to_all(w_out, "ch", split_axis=0, concat_axis=1, tiled=True)
    grad_gated = lax.dot_general(
        grad_all, rows_all, (((1,), (1,)), ((), ())), preferred_element_type=jnp.float32
    )
    grad_long = grad_gated * query_gate
    grad_query = grad_gated * long_out
    grad_re, grad_im = forward_spectrum(grad_long)
    pair_re = jnp.concatenate(
        [kernel_re * grad_re + kernel_im * grad_im, signal_re * grad_re + signal_im * grad_im],
        axis=2,
    )
    pair_im = jnp.concatenate(
        [kernel_re * grad_im - kernel_im * grad_re, signal_re * grad_im - signal_im * grad_re],
        axis=2,
    )
    pair_time = time_signal(pair_re, pair_im)
    grad_mixed = pair_time[:, :slab_width] + skip_gain * grad_long
    token_total = lax.axis_size("seq") * row_count
    grad_filter = pair_time[:, slab_width:] * (1.0 / math.sqrt(token_total))
    grad_short = jnp.stack([grad_query, grad_mixed * value_short, grad_mixed * key_short])
    head_rows = passed_along(grad_short[:, :2, :], "seq", -1)
    extended_grad = jnp.concatenate([grad_short, head_rows], axis=1)
    grad_qkv = (
        short_weight[:, 0, None, :] * extended_grad[:, :-2, :]
        + short_weight[:, 1, None, :] * extended_grad[:, 1:-1, :]
        + short_weight[:, 2, None, :] * extended_grad[:, 2:, :]
    ).astype(jnp.bfloat16)
    return (output, grad_qkv, grad_filter)


def split_bf16(values):
    high = values.astype(np.float32).astype(jnp.bfloat16)
    low = (values - high.astype(np.float64)).astype(np.float32).astype(jnp.bfloat16)
    return high, low


def phase_tables(tokens):
    quarter = tokens // PHASES
    freq = 2 * np.arange(quarter)[:, None] + 1
    turn = math.pi / (2 * tokens)
    angle = (freq * PHASES * np.arange(quarter)[None, :] % (4 * tokens)) * turn
    forward = np.concatenate([np.cos(angle), -np.sin(angle)], axis=0)
    backward = np.transpose(forward) * (1.0 / tokens)
    angle = freq * np.arange(PHASES)[None, :] * turn
    twist = np.concatenate([np.cos(angle), np.sin(angle)], axis=1).astype(np.float32)
    twist = np.pad(twist, ((0, 0), (0, LANES - 2 * PHASES)))
    return (*split_bf16(forward), *split_bf16(backward), twist)


def row_order(rows):
    order = np.zeros((rows, rows), np.float32)
    share = rows // PHASES
    for phase in range(PHASES):
        for j in range(share):
            order[phase * share + j, PHASES * j + phase] = 1.0
    return order.astype(jnp.bfloat16)


def mm(a, b):
    return lax.dot_general(a, b, (((1,), (0,)), ((), ())), preferred_element_type=F32)


def low_lanes(shape):
    return lax.broadcasted_iota(jnp.int32, shape, 1) < HALF


def swap(x):
    return pltpu.roll(x, HALF, 1)


class Stage:
    def __init__(self, count_in, count_out, pieces, refs):
        me = lax.axis_index("ch") if pieces > 1 else 0
        count = count_in + count_out
        sems = refs[2 * count]
        self.held = refs[count : 2 * count]
        self.count_in = count_in
        self.copies = []
        self.waiting = []
        self.given = []
        used = 0
        for i in range(count):
            here, there = refs[i], self.held[i]
            if i >= count_in:
                here, there = there, here
            cuts = pieces if i == 0 else 1
            step = here.shape[0] // cuts
            group = []
            for cut in range(cuts):
                ends = (here, there)
                if cuts > 1:
                    rows = pl.ds(pl.multiple_of((me ^ cut) * step, step), step)
                    ends = (here.at[rows], there.at[pl.ds(cut * step, step)])
                group.append(pltpu.make_async_copy(*ends, sems.at[used]))
                used += 1
            self.copies.append(group)
            self.waiting.append(set(range(cuts)))

    def take(self, index, piece=None):
        for cut in sorted(self.waiting[index]):
            if piece is None or piece == cut:
                self.copies[index][cut].wait()
                self.waiting[index].discard(cut)
        return self.held[index]

    def out(self, index):
        return self.held[self.count_in + index]

    def give(self, index):
        if index not in self.given:
            self.copies[self.count_in + index][0].start()
            self.given.append(index)


def staged(kernel, count_in, count_out, pieces, *refs):
    stage = Stage(count_in, count_out, pieces, refs)
    for i in range(1, count_in):
        stage.copies[i][0].start()
        if i == 1:
            for copy in stage.copies[0]:
                copy.start()
    kernel(stage)
    for i in range(count_in):
        stage.take(i)
    for i in range(count_out):
        stage.give(i)
    for i in range(count_out):
        stage.copies[count_in + i][0].wait()


def call(kernel, out_shape, *args, flops=0, pieces=1):
    far = pl.BlockSpec(memory_space=pltpu.HBM)
    arrays = list(args) + list(out_shape)
    moved = sum(math.prod(a.shape) * a.dtype.itemsize for a in arrays)
    return pl.pallas_call(
        functools.partial(staged, kernel, len(args), len(out_shape), pieces),
        out_shape=out_shape,
        in_specs=[far] * len(args),
        out_specs=[far] * len(out_shape),
        scratch_shapes=[pltpu.VMEM(x.shape, x.dtype) for x in arrays]
        + [pltpu.SemaphoreType.DMA((len(arrays) + pieces - 1,))],
        compiler_params=pltpu.CompilerParams(vmem_limit_bytes=VMEM_LIMIT),
        cost_estimate=pl.CostEstimate(flops=flops, bytes_accessed=moved, transcendentals=0),
    )(*args)


def lane_tile(x, index):
    return x[:, index * LANES : (index + 1) * LANES]


def pair(first, second):
    low = low_lanes(first.shape)
    return jnp.where(low, first, swap(second)), jnp.where(low, swap(first), second)


def both(x):
    turned, low = swap(x), low_lanes(x.shape)
    return jnp.where(low, x, turned), jnp.where(low, turned, x)


def start_kernel(parts, stage):
    g = stage.take(1)[...]
    width = g.shape[1]
    for part in range(parts):
        w = stage.take(0, part)[part * width : (part + 1) * width, :]
        turned = lax.dot_general(w, g, (((1,), (1,)), ((), ())), preferred_element_type=F32)
        stage.out(part)[...] = turned.T.astype(BF16)
        stage.give(part)
    send_ref = stage.out(parts)
    order = stage.take(2)[...]
    qkv_ref = stage.take(3)
    query, key, value = [mm(order, qkv_ref[i]) for i in range(3)]
    taps = mm(order, stage.take(4)[...].astype(BF16))
    rows = query.shape[0]
    for tile in range(width // LANES):
        for row, (x, y) in enumerate(((key, value), (query, taps))):
            here = slice(row * rows, (row + 1) * rows)
            x, y = pair(lane_tile(x, tile), lane_tile(y, tile))
            send_ref[2 * tile, here] = x.astype(BF16)
            send_ref[2 * tile + 1, here] = y.astype(BF16)


def pack_sum(stage, parts, first, order, send_ref):
    total = stage.take(first)[...].astype(F32)
    for part in range(1, parts):
        total = total + stage.take(first + part)[...].astype(F32)
    total = mm(order, total.astype(BF16))
    half = total.shape[0] // 2
    for tile in range(total.shape[1] // LANES):
        t = lane_tile(total, tile)
        x, y = pair(t[:half], t[half:])
        send_ref[2 * tile, half:] = x.astype(BF16)
        send_ref[2 * tile + 1, half:] = y.astype(BF16)


def spread_phases(parts):
    (a_re, a_im), (b_re, b_im), (c_re, c_im), (d_re, d_im) = parts
    s_re, s_im, t_re, t_im = a_re + c_re, a_im + c_im, a_re - c_re, a_im - c_im
    u_re, u_im, v_re, v_im = b_re + d_re, b_im + d_im, b_re - d_re, b_im - d_im
    return [
        (s_re + u_re, s_im + u_im),
        (t_re + v_im, t_im - v_re),
        (s_re - u_re, s_im - u_im),
        (t_re - v_im, t_im + v_re),
    ]


def gather_phases(parts):
    (a_re, a_im), (b_re, b_im), (c_re, c_im), (d_re, d_im) = parts
    s_re, s_im, t_re, t_im = a_re + c_re, a_im + c_im, a_re - c_re, a_im - c_im
    u_re, u_im, v_re, v_im = b_re + d_re, b_im + d_im, b_re - d_re, b_im - d_im
    return [
        (s_re + u_re, s_im + u_im),
        (t_re - v_im, t_im + v_re),
        (s_re - u_re, s_im - u_im),
        (t_re + v_im, t_im - v_re),
    ]


def rows_of(ref, start, count):
    block = ref[:, start : start + count, :]
    return block.reshape(ref.shape[0] * count, ref.shape[2])


def turned_back(re, im, twist, phase):
    if phase == 0:
        return re, im
    c, s = twist[:, phase : phase + 1], twist[:, PHASES + phase : PHASES + phase + 1]
    return re * c + im * s, im * c - re * s


def turned_on(re, im, twist, phase):
    if phase == 0:
        return re, im
    c, s = twist[:, phase : phase + 1], twist[:, PHASES + phase : PHASES + phase + 1]
    return re * c - im * s, re * s + im * c


def lane_tile(x, index):
    return x[:, index * LANES : (index + 1) * LANES]


def causal(parts, weight):
    rows = lax.broadcasted_iota(jnp.int32, parts[0].shape, 0)
    two, three = [jnp.where(rows == 0, 0.0, pltpu.roll(parts[p], 1, 0)) for p in (2, 3)]
    once, twice = [three, *parts[:3]], [two, three, *parts[:2]]
    return [
        weight[0:1] * x + weight[1:2] * y + weight[2:3] * z for x, y, z in zip(parts, once, twice)
    ]


def anticausal(parts, weight):
    count = parts[0].shape[0]
    rows = lax.broadcasted_iota(jnp.int32, parts[0].shape, 0)
    zero, one = [
        jnp.where(rows == count - 1, 0.0, pltpu.roll(parts[p], count - 1, 0)) for p in (0, 1)
    ]
    once, twice = [*parts[1:], zero], [*parts[2:], zero, one]
    return [
        weight[0:1] * x + weight[1:2] * y + weight[2:3] * z for x, y, z in zip(parts, once, twice)
    ]


def halves(x):
    high = x.astype(BF16)
    return high, (x - high.astype(F32)).astype(BF16)


def transformed(parts, fh, fl, twist):
    quarter = parts[0].shape[0]
    high, rest = halves(jnp.concatenate(parts, axis=1))
    s = mm(fh, high) + mm(fl, high) + mm(fh, rest)
    turned = []
    for phase in range(PHASES):
        t = lane_tile(s, phase)
        turned.append(turned_back(t[:quarter], t[quarter:], twist, phase))
    return spread_phases(turned)


def in_time(spectrum, bh, bl, twist):
    parts = []
    for phase, (re, im) in enumerate(gather_phases(spectrum)):
        parts.append(jnp.concatenate(turned_on(re, im, twist, phase), axis=0))
    high, rest = halves(jnp.concatenate(parts, axis=1))
    t = mm(bh, high) + mm(bl, high) + mm(bh, rest)
    return [lane_tile(t, phase) for phase in range(PHASES)]


def own_weights(weight_ref, gain_ref):
    place = lax.axis_index("seq")
    lanes = pl.ds(pl.multiple_of(place // 2 * LANES, LANES), LANES)
    odd = place % 2 == 1

    def mine(x):
        return jnp.where(odd, swap(x), x)

    weights = [mine(weight_ref[i, :, lanes]) for i in range(3)]
    gain = both(mine(gain_ref[:, lanes]))[0]
    low = low_lanes(weights[0].shape)
    only = (lax.broadcasted_iota(jnp.int32, weights[0].shape, 0) == 0).astype(F32)
    pair_weight = jnp.where(low, weights[1], swap(weights[2]))
    query_weight = jnp.where(low, weights[0], only)
    return pair_weight, query_weight, gain


def forward_kernel(parts, stage):
    recv_ref, weight_ref, gain_ref = [stage.take(i) for i in range(3)]
    gated_ref, spec_ref, pairs_ref, gates_ref = [stage.out(i) for i in range(4)]
    blocks = recv_ref.shape[0]
    rows = recv_ref.shape[1] // 2
    share = rows // PHASES
    quarter = blocks * share
    low = low_lanes((quarter, LANES))
    pair_weight, query_weight, gain = own_weights(weight_ref, gain_ref)

    starts = [phase * share for phase in range(PHASES)]
    pairs = causal([rows_of(recv_ref, at, share).astype(F32) for at in starts], pair_weight)
    gates = causal([rows_of(recv_ref, rows + at, share).astype(F32) for at in starts], query_weight)
    for phase in range(PHASES):
        pairs_ref[phase] = pairs[phase]
    stage.give(2)
    mixed = [x * swap(x) for x in pairs]
    query = [both(x)[0] for x in gates]
    fh, fl, twist = [stage.take(i)[...] for i in (3, 4, 5)]
    spectrum = transformed([jnp.where(low, x, y) for x, y in zip(mixed, gates)], fh, fl, twist)
    product = []
    for r, (re, im) in enumerate(spectrum):
        spec_ref[r, :quarter, :] = re
        spec_ref[r, quarter:, :] = im
        other_re, other_im = swap(re), swap(im)
        product.append((re * other_re - im * other_im, re * other_im + im * other_re))
    stage.give(1)
    pack_sum(stage, parts, 9, stage.take(8)[...], gated_ref)
    conv = in_time(product, stage.take(6)[...], stage.take(7)[...], twist)
    long_out = [x + gain * y for x, y in zip(conv, mixed)]
    gated = [x * y for x, y in zip(query, long_out)]
    for phase in range(PHASES // 2):
        t = jnp.where(low, gated[phase], gated[phase + 2]).astype(BF16)
        gated_ref[:, starts[phase] : starts[phase] + share, :] = t.reshape(blocks, share, LANES)
    stage.give(0)
    for phase in range(PHASES):
        gates_ref[phase] = jnp.where(low, query[phase], long_out[phase])


def backward_kernel(stage):
    grad_ref, weight_ref, gain_ref, gates_ref = [stage.take(i) for i in range(4)]
    send_ref = stage.out(0)
    blocks = grad_ref.shape[0]
    rows = grad_ref.shape[1]
    share = rows // PHASES
    quarter = blocks * share
    low = low_lanes((quarter, LANES))
    pair_weight, query_weight, gain = own_weights(weight_ref, gain_ref)

    starts = [phase * share for phase in range(PHASES)]
    packed = [rows_of(grad_ref, at, share).astype(F32) for at in starts[2:]]
    grad_gated = [both(x)[i] for i in range(2) for x in packed]
    gates = [both(gates_ref[phase]) for phase in range(PHASES)]
    grad_long = [x * y for x, (y, _) in zip(grad_gated, gates)]
    grad_query = anticausal([x * y for x, (_, y) in zip(grad_gated, gates)], query_weight)
    fh, fl, twist = [stage.take(i)[...] for i in (4, 5, 6)]
    grad_spectrum = transformed(grad_long, fh, fl, twist)
    spec_ref = stage.take(7)
    product = []
    for r, (re, im) in enumerate(grad_spectrum):
        k_re, k_im = spec_ref[r, :quarter, :], spec_ref[r, quarter:, :]
        product.append((k_re * re + k_im * im, k_re * im - k_im * re))
    times = in_time(product, stage.take(8)[...], stage.take(9)[...], twist)
    pairs_ref = stage.take(10)
    grad_mixed = [both(x + gain * y)[1] for x, y in zip(times, grad_long)]
    grad_pairs = anticausal(
        [x * swap(pairs_ref[phase]) for phase, x in enumerate(grad_mixed)], pair_weight
    )
    scale = 1.0 / math.sqrt(PHASES * quarter)
    for phase, at in enumerate(starts):
        x = grad_pairs[phase].astype(BF16)
        y = jnp.where(low, grad_query[phase], swap(times[phase]) * scale).astype(BF16)
        send_ref[:, at : at + share, :] = x.reshape(blocks, share, LANES)
        send_ref[:, rows + at : rows + at + share, :] = y.reshape(blocks, share, LANES)


def unpacked(blocks, order):
    half = blocks[0].shape[0]
    tiles = []
    for tile in range(len(blocks) // 2):
        top, bottom = pair(blocks[2 * tile].astype(F32), blocks[2 * tile + 1].astype(F32))
        tiles.append(jnp.concatenate([top, bottom], axis=0))
    return mm(order, jnp.concatenate(tiles, axis=1).astype(BF16))


def end_kernel(stage):
    recv_ref, order_ref = stage.take(0), stage.take(1)
    grad_ref, filter_ref = stage.out(0), stage.out(1)
    order = order_ref[...]
    blocks = recv_ref.shape[0]
    rows = recv_ref.shape[1] // 2
    sides = []
    for at in (0, rows):
        firsts, seconds = [], []
        for tile in range(blocks // 2):
            x, y = [recv_ref[2 * tile + i, at : at + rows].astype(F32) for i in range(2)]
            first, second = pair(x, y)
            firsts.append(first)
            seconds.append(second)
        for side in (firsts, seconds):
            sides.append(mm(order, jnp.concatenate(side, axis=1).astype(BF16)))
    key, value, query, taps = sides
    filter_ref[...] = taps
    stage.give(1)
    grad_ref[0] = query.astype(BF16)
    grad_ref[1] = key.astype(BF16)
    grad_ref[2] = value.astype(BF16)


def output_kernel(parts, stage):
    order = stage.take(1)[...]
    total = None
    for part in range(parts):
        gated_ref = stage.take(2 + part)
        block = unpacked([gated_ref[i] for i in range(gated_ref.shape[0])], order).astype(BF16)
        width = block.shape[1]
        term = mm(block, stage.take(0, part)[part * width : (part + 1) * width, :])
        total = term if total is None else total + term
    stage.out(0)[...] = total.astype(BF16)


def partner(x, axis, mask):
    return lax.ppermute(x, axis, [(i, i ^ mask) for i in range(lax.axis_size(axis))])


def exchanged(x, axis):
    return lax.all_to_all(x, axis, split_axis=0, concat_axis=0, tiled=True)


def owner_layer(qkv, filt, skip_gain, short_weight, w_out, g_out):
    shape = jax.ShapeDtypeStruct
    seq_parts, ch_parts = lax.axis_size("seq"), lax.axis_size("ch")
    rows, width = qkv.shape[1], qkv.shape[2]
    tokens = seq_parts * rows
    order = row_order(rows)
    fh, fl, bh, bl, twist = phase_tables(tokens)
    table_flops = 2 * 2 * 2 * 3 * tokens * tokens // PHASES * LANES
    product_flops = 2 * rows * width * width * ch_parts
    double = shape((seq_parts, 2 * rows, LANES), BF16)

    *partial, send = call(
        functools.partial(start_kernel, ch_parts),
        [shape((rows, width), BF16)] * ch_parts + [double],
        w_out,
        g_out,
        order,
        qkv,
        filt,
        flops=product_flops,
        pieces=ch_parts,
    )
    recv = exchanged(send, "seq")
    partial = [partner(x, "ch", mask) if mask else x for mask, x in enumerate(partial)]
    gain = skip_gain[None, :]
    quarter = tokens // PHASES
    send, spec, pairs, gates = call(
        functools.partial(forward_kernel, ch_parts),
        [
            shape((seq_parts, rows, LANES), BF16),
            shape((PHASES, 2 * quarter, LANES), F32),
            shape((PHASES, quarter, LANES), F32),
            shape((PHASES, quarter, LANES), F32),
        ],
        recv,
        short_weight,
        gain,
        fh,
        fl,
        twist,
        bh,
        bl,
        order,
        *partial,
        flops=table_flops,
    )
    swapped = exchanged(send, "seq")
    gated = swapped[:, : rows // 2, :]
    gated = [partner(gated, "ch", mask) if mask else gated for mask in range(ch_parts)]
    (send,) = call(
        backward_kernel,
        [double],
        swapped,
        short_weight,
        gain,
        gates,
        fh,
        fl,
        twist,
        spec,
        bh,
        bl,
        pairs,
        flops=table_flops,
    )
    grad_recv = exchanged(send, "seq")
    back_order = order.T
    (output,) = call(
        functools.partial(output_kernel, ch_parts),
        [shape((rows, width), BF16)],
        w_out,
        back_order,
        *gated,
        flops=product_flops,
        pieces=ch_parts,
    )
    grad_qkv, grad_filter = call(
        end_kernel,
        [shape((3, rows, width), BF16), shape((rows, width), F32)],
        grad_recv,
        back_order,
    )
    return (output, grad_qkv, grad_filter)


def local(qkv, filt, skip_gain, short_weight, w_out, g_out):
    seq_parts = lax.axis_size("seq")
    rows, width = qkv.shape[1], qkv.shape[2]
    fits = width == HALF * seq_parts and rows % HALF == 0 and rows * seq_parts <= 2048
    if fits and lax.axis_size("ch") == 4:
        return owner_layer(qkv, filt, skip_gain, short_weight, w_out, g_out)
    return spread_layer(qkv, filt, skip_gain, short_weight, w_out, g_out)


def solution(mesh):
    in_specs = (
        P(None, "seq", "ch"),
        P("seq", "ch"),
        P("ch"),
        P(None, None, "ch"),
        P(None, "ch"),
        P("seq", "ch"),
    )
    out_specs = (P("seq", "ch"), P(None, "seq", "ch"), P("seq", "ch"))
    return jax.shard_map(local, mesh=mesh, in_specs=in_specs, out_specs=out_specs, check_vma=False)
```

```python
import functools
import math

import jax
import jax.numpy as jnp
import numpy as np
from jax import lax
from jax.experimental import pallas as pl
from jax.experimental.pallas import tpu as pltpu
from jax.sharding import PartitionSpec as P

HIGHEST = lax.Precision.HIGHEST
TWO_PI = 2.0 * math.pi
LANES = 128
HALF = 64
PHASES = 4
BF16 = jnp.bfloat16
F32 = jnp.float32
VMEM_LIMIT = 64 * 1024 * 1024


def passed_along(block, axis, distance):
    devices = range(lax.axis_size(axis))
    route = [(i - distance, i) for i in devices if i - distance in devices]
    return lax.ppermute(block, axis, route)


def phase_pair(left_count, right_count, period, left_start, right_start):
    left_idx = lax.broadcasted_iota(jnp.int32, (left_count, right_count), 0) + left_start
    right_idx = lax.broadcasted_iota(jnp.int32, (left_count, right_count), 1) + right_start
    angle_all = (left_idx * right_idx % period).astype(jnp.float32) * (TWO_PI / period)
    return (jnp.cos(angle_all), jnp.sin(angle_all))


def contract(pattern, matrix, values):
    return jnp.einsum(
        pattern, matrix, values, precision=HIGHEST, preferred_element_type=jnp.float32
    )


def forward_spectrum(signal):
    seq_parts = lax.axis_size("seq")
    row_count = signal.shape[0]
    row_share = row_count // seq_parts
    period = 2 * seq_parts * row_count
    spread_in = lax.all_to_all(signal[None], "seq", split_axis=1, concat_axis=0, tiled=True)
    outer_cos, outer_sin = phase_pair(2 * seq_parts, seq_parts, 2 * seq_parts, 0, 0)
    section_re = contract("cp,prw->crw", outer_cos, spread_in)
    section_im = -contract("cp,prw->crw", outer_sin, spread_in)
    twist_cos, twist_sin = phase_pair(
        2 * seq_parts, row_share, period, 0, lax.axis_index("seq") * row_share
    )
    twist_cos = twist_cos[:, :, None]
    twist_sin = twist_sin[:, :, None]
    turned_re = section_re * twist_cos + section_im * twist_sin
    turned_im = section_im * twist_cos - section_re * twist_sin
    inner_cos, inner_sin = phase_pair(row_count, row_count, row_count, 0, 0)
    piece_re = lax.all_to_all(turned_re, "seq", split_axis=0, concat_axis=1, tiled=True)
    piece_im = lax.all_to_all(turned_im, "seq", split_axis=0, concat_axis=1, tiled=True)
    spec_re = contract("dm,cmk->cdk", inner_cos, piece_re) + contract(
        "dm,cmk->cdk", inner_sin, piece_im
    )
    spec_im = contract("dm,cmk->cdk", inner_cos, piece_im) - contract(
        "dm,cmk->cdk", inner_sin, piece_re
    )
    return (spec_re, spec_im)


def time_signal(spec_re, spec_im):
    seq_parts = lax.axis_size("seq")
    row_count = spec_re.shape[1]
    period = 2 * seq_parts * row_count
    inner_cos, inner_sin = phase_pair(row_count, row_count, row_count, 0, 0)
    back_re = contract("md,cdk->cmk", inner_cos, spec_re) - contract(
        "md,cdk->cmk", inner_sin, spec_im
    )
    back_im = contract("md,cdk->cmk", inner_cos, spec_im) + contract(
        "md,cdk->cmk", inner_sin, spec_re
    )
    twist_cos, twist_sin = phase_pair(2, row_count, period, 2 * lax.axis_index("seq"), 0)
    twist_cos = twist_cos[:, :, None]
    twist_sin = twist_sin[:, :, None]
    turned_re = back_re * twist_cos - back_im * twist_sin
    turned_im = back_im * twist_cos + back_re * twist_sin
    outer_cos, outer_sin = phase_pair(seq_parts, 2 * seq_parts, 2 * seq_parts, 0, 0)
    piece_re = lax.all_to_all(turned_re, "seq", split_axis=1, concat_axis=0, tiled=True)
    piece_im = lax.all_to_all(turned_im, "seq", split_axis=1, concat_axis=0, tiled=True)
    summed = contract("pc,crk->prk", outer_cos, piece_re) - contract(
        "pc,crk->prk", outer_sin, piece_im
    )
    returned = summed * (1.0 / period)
    return lax.all_to_all(returned, "seq", split_axis=0, concat_axis=1, tiled=True)[0]


def spread_layer(qkv, filt, skip_gain, short_weight, w_out, g_out):
    row_count = qkv.shape[1]
    slab_width = qkv.shape[2]
    tail_rows = passed_along(qkv[:, row_count - 2 :, :], "seq", 1)
    extended = jnp.concatenate([tail_rows, qkv], axis=1)
    short = (
        short_weight[:, 0, None, :] * extended[:, 2:, :]
        + short_weight[:, 1, None, :] * extended[:, 1:-1, :]
        + short_weight[:, 2, None, :] * extended[:, :-2, :]
    )
    query_gate = short[0]
    key_short = short[1]
    value_short = short[2]
    mixed = key_short * value_short
    both_re, both_im = forward_spectrum(jnp.concatenate([mixed, filt], axis=1))
    signal_re = both_re[:, :, :slab_width]
    signal_im = both_im[:, :, :slab_width]
    kernel_re = both_re[:, :, slab_width:]
    kernel_im = both_im[:, :, slab_width:]
    conv_out = time_signal(
        signal_re * kernel_re - signal_im * kernel_im, signal_re * kernel_im + signal_im * kernel_re
    )
    long_out = conv_out + skip_gain * mixed
    gated_out = (query_gate * long_out).astype(jnp.bfloat16)
    projected = jnp.dot(
        lax.all_gather(gated_out, "ch", axis=1, tiled=True),
        w_out,
        preferred_element_type=jnp.float32,
    )
    output = projected.astype(jnp.bfloat16)
    grad_all = lax.all_gather(g_out, "ch", axis=1, tiled=True)
    rows_all = lax.all_to_all(w_out, "ch", split_axis=0, concat_axis=1, tiled=True)
    grad_gated = lax.dot_general(
        grad_all, rows_all, (((1,), (1,)), ((), ())), preferred_element_type=jnp.float32
    )
    grad_long = grad_gated * query_gate
    grad_query = grad_gated * long_out
    grad_re, grad_im = forward_spectrum(grad_long)
    pair_re = jnp.concatenate(
        [kernel_re * grad_re + kernel_im * grad_im, signal_re * grad_re + signal_im * grad_im],
        axis=2,
    )
    pair_im = jnp.concatenate(
        [kernel_re * grad_im - kernel_im * grad_re, signal_re * grad_im - signal_im * grad_re],
        axis=2,
    )
    pair_time = time_signal(pair_re, pair_im)
    grad_mixed = pair_time[:, :slab_width] + skip_gain * grad_long
    token_total = lax.axis_size("seq") * row_count
    grad_filter = pair_time[:, slab_width:] * (1.0 / math.sqrt(token_total))
    grad_short = jnp.stack([grad_query, grad_mixed * value_short, grad_mixed * key_short])
    head_rows = passed_along(grad_short[:, :2, :], "seq", -1)
    extended_grad = jnp.concatenate([grad_short, head_rows], axis=1)
    grad_qkv = (
        short_weight[:, 0, None, :] * extended_grad[:, :-2, :]
        + short_weight[:, 1, None, :] * extended_grad[:, 1:-1, :]
        + short_weight[:, 2, None, :] * extended_grad[:, 2:, :]
    ).astype(jnp.bfloat16)
    return (output, grad_qkv, grad_filter)


def split_bf16(values):
    high = values.astype(np.float32).astype(jnp.bfloat16)
    low = (values - high.astype(np.float64)).astype(np.float32).astype(jnp.bfloat16)
    return high, low


def phase_tables(tokens):
    quarter = tokens // PHASES
    freq = 2 * np.arange(quarter)[:, None] + 1
    turn = math.pi / (2 * tokens)
    angle = (freq * PHASES * np.arange(quarter)[None, :] % (4 * tokens)) * turn
    forward = np.concatenate([np.cos(angle), -np.sin(angle)], axis=0)
    backward = np.transpose(forward) * (1.0 / tokens)
    angle = freq * np.arange(PHASES)[None, :] * turn
    twist = np.concatenate([np.cos(angle), np.sin(angle)], axis=1).astype(np.float32)
    twist = np.pad(twist, ((0, 0), (0, LANES - 2 * PHASES)))
    return (*split_bf16(forward), *split_bf16(backward), twist)


def row_order(rows):
    order = np.zeros((rows, rows), np.float32)
    share = rows // PHASES
    for phase in range(PHASES):
        for j in range(share):
            order[phase * share + j, PHASES * j + phase] = 1.0
    return order.astype(jnp.bfloat16)


def mm(a, b):
    return lax.dot_general(a, b, (((1,), (0,)), ((), ())), preferred_element_type=F32)


def low_lanes(shape):
    return lax.broadcasted_iota(jnp.int32, shape, 1) < HALF


def swap(x):
    return pltpu.roll(x, HALF, 1)


class Stage:
    def __init__(self, sizes_in, sizes_out, pieces, refs):
        place, column = lax.axis_index("seq"), lax.axis_index("ch")
        sizes = sizes_in + sizes_out
        flat = sum(max(size, 1) for size in sizes)
        arrays, sems = list(refs[:flat]), refs[-1]
        self.held = refs[flat:-1]
        self.count_in = len(sizes_in)
        self.copies = []
        used = 0
        for i, size in enumerate(sizes):
            ends = []
            if size:
                for m in range(size):
                    ends.append((arrays.pop(0), self.held[i].at[place ^ m]))
            else:
                ends.append((arrays.pop(0), self.held[i]))
            if i == 0 and pieces > 1:
                here, there = ends.pop()
                step = here.shape[0] // pieces
                for cut in range(pieces):
                    rows = pl.ds(pl.multiple_of((column ^ cut) * step, step), step)
                    ends.append((here.at[rows], there.at[pl.ds(cut * step, step)]))
            if i >= self.count_in:
                ends = [(there, here) for here, there in ends]
            group = []
            for here, there in ends:
                group.append(pltpu.make_async_copy(here, there, sems.at[used]))
                used += 1
            self.copies.append(group)
        self.waiting = [set(range(len(group))) for group in self.copies]
        self.given = []

    def bring(self, index):
        for copy in self.copies[index]:
            copy.start()

    def take(self, index, piece=None):
        for cut in sorted(self.waiting[index]):
            if piece is None or piece == cut:
                self.copies[index][cut].wait()
                self.waiting[index].discard(cut)
        return self.held[index]

    def out(self, index):
        return self.held[self.count_in + index]

    def give(self, index):
        if index not in self.given:
            self.bring(self.count_in + index)
            self.given.append(index)


def staged(kernel, sizes_in, sizes_out, pieces, *refs):
    stage = Stage(sizes_in, sizes_out, pieces, refs)
    order = list(range(len(sizes_in)))
    if pieces > 1:
        order[:2] = 1, 0
    for i in order:
        stage.bring(i)
    kernel(stage)
    for i in range(len(sizes_in)):
        stage.take(i)
    for i in range(len(sizes_out)):
        stage.give(i)
    for i in range(len(sizes_out)):
        stage.take(len(sizes_in) + i)


def call(kernel, out_shape, *args, flops=0, pieces=1):
    far = pl.BlockSpec(memory_space=pltpu.HBM)

    def sizes(items):
        return [len(x) if isinstance(x, (list, tuple)) else 0 for x in items]

    def flat(items):
        return [y for x in items for y in (x if isinstance(x, (list, tuple)) else [x])]

    def buffer(x):
        if isinstance(x, (list, tuple)):
            return pltpu.VMEM((len(x), *x[0].shape), x[0].dtype)
        return pltpu.VMEM(x.shape, x.dtype)

    ins, outs = flat(args), flat(out_shape)
    moved = sum(math.prod(a.shape) * a.dtype.itemsize for a in ins + outs)
    results = pl.pallas_call(
        functools.partial(staged, kernel, sizes(args), sizes(out_shape), pieces),
        out_shape=outs,
        in_specs=[far] * len(ins),
        out_specs=[far] * len(outs),
        scratch_shapes=[buffer(x) for x in (*args, *out_shape)]
        + [pltpu.SemaphoreType.DMA((len(ins) + len(outs) + pieces - 1,))],
        compiler_params=pltpu.CompilerParams(vmem_limit_bytes=VMEM_LIMIT),
        cost_estimate=pl.CostEstimate(flops=flops, bytes_accessed=moved, transcendentals=0),
    )(*ins)
    results = list(results)
    return [
        [results.pop(0) for _ in x] if isinstance(x, (list, tuple)) else results.pop(0)
        for x in out_shape
    ]


def lane_tile(x, index):
    return x[:, index * LANES : (index + 1) * LANES]


def pair(first, second):
    low = low_lanes(first.shape)
    return jnp.where(low, first, swap(second)), jnp.where(low, swap(first), second)


def both(x):
    turned, low = swap(x), low_lanes(x.shape)
    return jnp.where(low, x, turned), jnp.where(low, turned, x)


def start_kernel(parts, stage):
    g = stage.take(1)[...]
    width = g.shape[1]
    for part in range(parts):
        w = stage.take(0, part)[part * width : (part + 1) * width, :]
        stage.out(part)[...] = lax.dot_general(
            g, w, (((1,), (1,)), ((), ())), preferred_element_type=F32
        ).astype(BF16)
        stage.give(part)
    send_ref = stage.out(parts)
    order = stage.take(2)[...]
    qkv_ref = stage.take(3)
    query, key, value = [mm(order, qkv_ref[i]) for i in range(3)]
    taps = mm(order, stage.take(4)[...].astype(BF16))
    rows = query.shape[0]
    for tile in range(width // LANES):
        for row, (x, y) in enumerate(((key, value), (query, taps))):
            here = slice(row * rows, (row + 1) * rows)
            x, y = pair(lane_tile(x, tile), lane_tile(y, tile))
            send_ref[2 * tile, here] = x.astype(BF16)
            send_ref[2 * tile + 1, here] = y.astype(BF16)


def sum_kernel(parts, stage):
    send_ref, order_ref = stage.out(0), stage.take(0)
    total = stage.take(1)[...].astype(F32)
    for part in range(1, parts):
        total = total + stage.take(1 + part)[...].astype(F32)
    total = mm(order_ref[...], total.astype(BF16))
    half = total.shape[0] // 2
    for tile in range(total.shape[1] // LANES):
        t = lane_tile(total, tile)
        x, y = pair(t[:half], t[half:])
        send_ref[2 * tile] = x.astype(BF16)
        send_ref[2 * tile + 1] = y.astype(BF16)


def spread_phases(parts):
    (a_re, a_im), (b_re, b_im), (c_re, c_im), (d_re, d_im) = parts
    s_re, s_im, t_re, t_im = a_re + c_re, a_im + c_im, a_re - c_re, a_im - c_im
    u_re, u_im, v_re, v_im = b_re + d_re, b_im + d_im, b_re - d_re, b_im - d_im
    return [
        (s_re + u_re, s_im + u_im),
        (t_re + v_im, t_im - v_re),
        (s_re - u_re, s_im - u_im),
        (t_re - v_im, t_im + v_re),
    ]


def gather_phases(parts):
    (a_re, a_im), (b_re, b_im), (c_re, c_im), (d_re, d_im) = parts
    s_re, s_im, t_re, t_im = a_re + c_re, a_im + c_im, a_re - c_re, a_im - c_im
    u_re, u_im, v_re, v_im = b_re + d_re, b_im + d_im, b_re - d_re, b_im - d_im
    return [
        (s_re + u_re, s_im + u_im),
        (t_re - v_im, t_im + v_re),
        (s_re - u_re, s_im - u_im),
        (t_re + v_im, t_im - v_re),
    ]


def rows_of(ref, start, count):
    block = ref[:, start : start + count, :]
    return block.reshape(ref.shape[0] * count, ref.shape[2])


def turned_back(re, im, twist, phase):
    if phase == 0:
        return re, im
    c, s = twist[:, phase : phase + 1], twist[:, PHASES + phase : PHASES + phase + 1]
    return re * c + im * s, im * c - re * s


def turned_on(re, im, twist, phase):
    if phase == 0:
        return re, im
    c, s = twist[:, phase : phase + 1], twist[:, PHASES + phase : PHASES + phase + 1]
    return re * c - im * s, re * s + im * c


def lane_tile(x, index):
    return x[:, index * LANES : (index + 1) * LANES]


def causal(parts, weight):
    rows = lax.broadcasted_iota(jnp.int32, parts[0].shape, 0)
    two, three = [jnp.where(rows == 0, 0.0, pltpu.roll(parts[p], 1, 0)) for p in (2, 3)]
    once, twice = [three, *parts[:3]], [two, three, *parts[:2]]
    return [
        weight[0:1] * x + weight[1:2] * y + weight[2:3] * z for x, y, z in zip(parts, once, twice)
    ]


def anticausal(parts, weight):
    count = parts[0].shape[0]
    rows = lax.broadcasted_iota(jnp.int32, parts[0].shape, 0)
    zero, one = [
        jnp.where(rows == count - 1, 0.0, pltpu.roll(parts[p], count - 1, 0)) for p in (0, 1)
    ]
    once, twice = [*parts[1:], zero], [*parts[2:], zero, one]
    return [
        weight[0:1] * x + weight[1:2] * y + weight[2:3] * z for x, y, z in zip(parts, once, twice)
    ]


def halves(x):
    high = x.astype(BF16)
    return high, (x - high.astype(F32)).astype(BF16)


def transformed(parts, fh, fl, twist):
    quarter = parts[0].shape[0]
    high, rest = halves(jnp.concatenate(parts, axis=1))
    s = mm(fh, high) + mm(fl, high) + mm(fh, rest)
    turned = []
    for phase in range(PHASES):
        t = lane_tile(s, phase)
        turned.append(turned_back(t[:quarter], t[quarter:], twist, phase))
    return spread_phases(turned)


def in_time(spectrum, bh, bl, twist):
    parts = []
    for phase, (re, im) in enumerate(gather_phases(spectrum)):
        parts.append(jnp.concatenate(turned_on(re, im, twist, phase), axis=0))
    high, rest = halves(jnp.concatenate(parts, axis=1))
    t = mm(bh, high) + mm(bl, high) + mm(bh, rest)
    return [lane_tile(t, phase) for phase in range(PHASES)]


def own_weights(weight_ref, gain_ref):
    place = lax.axis_index("seq")
    lanes = pl.ds(pl.multiple_of(place // 2 * LANES, LANES), LANES)
    odd = place % 2 == 1

    def mine(x):
        return jnp.where(odd, swap(x), x)

    weights = [mine(weight_ref[i, :, lanes]) for i in range(3)]
    gain = both(mine(gain_ref[:, lanes]))[0]
    low = low_lanes(weights[0].shape)
    only = (lax.broadcasted_iota(jnp.int32, weights[0].shape, 0) == 0).astype(F32)
    pair_weight = jnp.where(low, weights[1], swap(weights[2]))
    query_weight = jnp.where(low, weights[0], only)
    return pair_weight, query_weight, gain


def forward_kernel(stage):
    recv_ref, weight_ref, gain_ref = [stage.take(i) for i in range(3)]
    gated_ref, spec_ref, pairs_ref, gates_ref = [stage.out(i) for i in range(4)]
    blocks = recv_ref.shape[0]
    rows = recv_ref.shape[1] // 2
    share = rows // PHASES
    quarter = blocks * share
    low = low_lanes((quarter, LANES))
    pair_weight, query_weight, gain = own_weights(weight_ref, gain_ref)

    starts = [phase * share for phase in range(PHASES)]
    pairs = causal([rows_of(recv_ref, at, share).astype(F32) for at in starts], pair_weight)
    gates = causal([rows_of(recv_ref, rows + at, share).astype(F32) for at in starts], query_weight)
    for phase in range(PHASES):
        pairs_ref[phase] = pairs[phase]
    stage.give(2)
    mixed = [x * swap(x) for x in pairs]
    query = [both(x)[0] for x in gates]
    fh, fl, twist = [stage.take(i)[...] for i in (3, 4, 5)]
    spectrum = transformed([jnp.where(low, x, y) for x, y in zip(mixed, gates)], fh, fl, twist)
    product = []
    for r, (re, im) in enumerate(spectrum):
        spec_ref[r, :quarter, :] = re
        spec_ref[r, quarter:, :] = im
        other_re, other_im = swap(re), swap(im)
        product.append((re * other_re - im * other_im, re * other_im + im * other_re))
    stage.give(1)
    conv = in_time(product, stage.take(6)[...], stage.take(7)[...], twist)
    long_out = [x + gain * y for x, y in zip(conv, mixed)]
    gated = [x * y for x, y in zip(query, long_out)]
    for phase in range(PHASES // 2):
        t = jnp.where(low, gated[phase], gated[phase + 2]).astype(BF16)
        gated_ref[:, starts[phase] : starts[phase] + share, :] = t.reshape(blocks, share, LANES)
    stage.give(0)
    for phase in range(PHASES):
        gates_ref[phase] = jnp.where(low, query[phase], long_out[phase])


def backward_kernel(stage):
    grad_ref, weight_ref, gain_ref, gates_ref = [stage.take(i) for i in range(4)]
    send_ref = stage.out(0)
    blocks = grad_ref.shape[0]
    share = grad_ref.shape[1] // 2
    rows = PHASES * share
    quarter = blocks * share
    low = low_lanes((quarter, LANES))
    pair_weight, query_weight, gain = own_weights(weight_ref, gain_ref)

    starts = [phase * share for phase in range(PHASES)]
    packed = [rows_of(grad_ref, at, share).astype(F32) for at in starts[:2]]
    grad_gated = [both(x)[i] for i in range(2) for x in packed]
    gates = [both(gates_ref[phase]) for phase in range(PHASES)]
    grad_long = [x * y for x, (y, _) in zip(grad_gated, gates)]
    grad_query = anticausal([x * y for x, (_, y) in zip(grad_gated, gates)], query_weight)
    fh, fl, twist = [stage.take(i)[...] for i in (4, 5, 6)]
    grad_spectrum = transformed(grad_long, fh, fl, twist)
    spec_ref = stage.take(7)
    product = []
    for r, (re, im) in enumerate(grad_spectrum):
        k_re, k_im = spec_ref[r, :quarter, :], spec_ref[r, quarter:, :]
        product.append((k_re * re + k_im * im, k_re * im - k_im * re))
    times = in_time(product, stage.take(8)[...], stage.take(9)[...], twist)
    pairs_ref = stage.take(10)
    grad_mixed = [both(x + gain * y)[1] for x, y in zip(times, grad_long)]
    grad_pairs = anticausal(
        [x * swap(pairs_ref[phase]) for phase, x in enumerate(grad_mixed)], pair_weight
    )
    scale = 1.0 / math.sqrt(PHASES * quarter)
    for phase, at in enumerate(starts):
        x = grad_pairs[phase].astype(BF16)
        y = jnp.where(low, grad_query[phase], swap(times[phase]) * scale).astype(BF16)
        send_ref[:, at : at + share, :] = x.reshape(blocks, share, LANES)
        send_ref[:, rows + at : rows + at + share, :] = y.reshape(blocks, share, LANES)


def unpacked(blocks, order):
    half = blocks[0].shape[0]
    tiles = []
    for tile in range(len(blocks) // 2):
        top, bottom = pair(blocks[2 * tile].astype(F32), blocks[2 * tile + 1].astype(F32))
        tiles.append(jnp.concatenate([top, bottom], axis=0))
    return mm(order, jnp.concatenate(tiles, axis=1).astype(BF16))


def end_kernel(stage):
    recv_ref, order_ref = stage.take(0), stage.take(1)
    output_ref, grad_ref, filter_ref = [stage.out(i) for i in range(3)]
    order = order_ref[...]
    blocks = recv_ref.shape[0]
    rows = recv_ref.shape[1] // 2
    sides = []
    for at in (0, rows):
        firsts, seconds = [], []
        for tile in range(blocks // 2):
            x, y = [recv_ref[2 * tile + i, at : at + rows].astype(F32) for i in range(2)]
            first, second = pair(x, y)
            firsts.append(first)
            seconds.append(second)
        for side in (firsts, seconds):
            sides.append(mm(order, jnp.concatenate(side, axis=1).astype(BF16)))
    key, value, query, taps = sides
    filter_ref[...] = taps
    stage.give(2)
    grad_ref[0] = query.astype(BF16)
    grad_ref[1] = key.astype(BF16)
    grad_ref[2] = value.astype(BF16)
    stage.give(1)
    gated_ref, w_ref = stage.take(2), stage.take(3)
    parts = gated_ref.shape[0]
    width = w_ref.shape[0] // parts
    total = None
    for part in range(parts):
        block = unpacked([gated_ref[part, i] for i in range(blocks)], order).astype(BF16)
        term = mm(block, w_ref[part * width : (part + 1) * width, :])
        total = term if total is None else total + term
    output_ref[...] = total.astype(BF16)


def partner(x, axis, mask):
    return lax.ppermute(x, axis, [(i, i ^ mask) for i in range(lax.axis_size(axis))])


def exchanged(x, axis):
    return lax.all_to_all(x, axis, split_axis=0, concat_axis=0, tiled=True)


def owner_layer(qkv, filt, skip_gain, short_weight, w_out, g_out):
    shape = jax.ShapeDtypeStruct
    seq_parts, ch_parts = lax.axis_size("seq"), lax.axis_size("ch")
    rows, width = qkv.shape[1], qkv.shape[2]
    tokens = seq_parts * rows
    order = row_order(rows)
    fh, fl, bh, bl, twist = phase_tables(tokens)
    table_flops = 2 * 2 * 2 * 3 * tokens * tokens // PHASES * LANES
    product_flops = 2 * rows * width * width * ch_parts
    packed = shape((seq_parts, rows // 2, LANES), BF16)
    double = shape((seq_parts, 2 * rows, LANES), BF16)

    *partial, send = call(
        functools.partial(start_kernel, ch_parts),
        [shape((rows, width), BF16)] * ch_parts + [[shape(double.shape[1:], BF16)] * seq_parts],
        w_out,
        g_out,
        order,
        qkv,
        filt,
        flops=product_flops,
        pieces=ch_parts,
    )
    partial = [partner(x, "ch", mask) if mask else x for mask, x in enumerate(partial)]
    recv = [partner(x, "seq", mask) if mask else x for mask, x in enumerate(send)]
    (send,) = call(functools.partial(sum_kernel, ch_parts), [packed], order, *partial)
    grad_recv = exchanged(send, "seq")
    gain = skip_gain[None, :]
    quarter = tokens // PHASES
    gated, spec, pairs, gates = call(
        forward_kernel,
        [
            packed,
            shape((PHASES, 2 * quarter, LANES), F32),
            shape((PHASES, quarter, LANES), F32),
            shape((PHASES, quarter, LANES), F32),
        ],
        recv,
        short_weight,
        gain,
        fh,
        fl,
        twist,
        bh,
        bl,
        flops=table_flops,
    )
    gated = exchanged(gated, "seq")
    (send,) = call(
        backward_kernel,
        [double],
        grad_recv,
        short_weight,
        gain,
        gates,
        fh,
        fl,
        twist,
        spec,
        bh,
        bl,
        pairs,
        flops=table_flops,
    )
    grad_recv = exchanged(send, "seq")
    gated = lax.all_gather(gated, "ch", axis=0, tiled=False)
    output, grad_qkv, grad_filter = call(
        end_kernel,
        [shape((rows, width), BF16), shape((3, rows, width), BF16), shape((rows, width), F32)],
        grad_recv,
        order.T,
        gated,
        w_out,
        flops=product_flops,
    )
    return (output, grad_qkv, grad_filter)


def local(qkv, filt, skip_gain, short_weight, w_out, g_out):
    seq_parts = lax.axis_size("seq")
    rows, width = qkv.shape[1], qkv.shape[2]
    fits = width == HALF * seq_parts and rows % HALF == 0 and rows * seq_parts <= 2048
    if fits and lax.axis_size("ch") == 4 and seq_parts == 8:
        return owner_layer(qkv, filt, skip_gain, short_weight, w_out, g_out)
    return spread_layer(qkv, filt, skip_gain, short_weight, w_out, g_out)


def solution(mesh):
    in_specs = (
        P(None, "seq", "ch"),
        P("seq", "ch"),
        P("ch"),
        P(None, None, "ch"),
        P(None, "ch"),
        P("seq", "ch"),
    )
    out_specs = (P("seq", "ch"), P(None, "seq", "ch"), P("seq", "ch"))
    return jax.shard_map(local, mesh=mesh, in_specs=in_specs, out_specs=out_specs, check_vma=False)
```

```python
import functools
import math

import jax
import jax.numpy as jnp
import numpy as np
from jax import lax
from jax.experimental import pallas as pl
from jax.experimental.pallas import tpu as pltpu
from jax.sharding import PartitionSpec as P

HIGHEST = lax.Precision.HIGHEST
TWO_PI = 2.0 * math.pi
LANES = 128
HALF = 64
PHASES = 4
BF16 = jnp.bfloat16
F32 = jnp.float32
WHOLE_VMEM = 64 * 1024 * 1024
VMEM_LIMIT = WHOLE_VMEM - 1792 * 1024


def passed_along(block, axis, distance):
    devices = range(lax.axis_size(axis))
    route = [(i - distance, i) for i in devices if i - distance in devices]
    return lax.ppermute(block, axis, route)


def phase_pair(left_count, right_count, period, left_start, right_start):
    left_idx = lax.broadcasted_iota(jnp.int32, (left_count, right_count), 0) + left_start
    right_idx = lax.broadcasted_iota(jnp.int32, (left_count, right_count), 1) + right_start
    angle_all = (left_idx * right_idx % period).astype(jnp.float32) * (TWO_PI / period)
    return (jnp.cos(angle_all), jnp.sin(angle_all))


def contract(pattern, matrix, values):
    return jnp.einsum(
        pattern, matrix, values, precision=HIGHEST, preferred_element_type=jnp.float32
    )


def forward_spectrum(signal):
    seq_parts = lax.axis_size("seq")
    row_count = signal.shape[0]
    row_share = row_count // seq_parts
    period = 2 * seq_parts * row_count
    spread_in = lax.all_to_all(signal[None], "seq", split_axis=1, concat_axis=0, tiled=True)
    outer_cos, outer_sin = phase_pair(2 * seq_parts, seq_parts, 2 * seq_parts, 0, 0)
    section_re = contract("cp,prw->crw", outer_cos, spread_in)
    section_im = -contract("cp,prw->crw", outer_sin, spread_in)
    twist_cos, twist_sin = phase_pair(
        2 * seq_parts, row_share, period, 0, lax.axis_index("seq") * row_share
    )
    twist_cos = twist_cos[:, :, None]
    twist_sin = twist_sin[:, :, None]
    turned_re = section_re * twist_cos + section_im * twist_sin
    turned_im = section_im * twist_cos - section_re * twist_sin
    inner_cos, inner_sin = phase_pair(row_count, row_count, row_count, 0, 0)
    piece_re = lax.all_to_all(turned_re, "seq", split_axis=0, concat_axis=1, tiled=True)
    piece_im = lax.all_to_all(turned_im, "seq", split_axis=0, concat_axis=1, tiled=True)
    spec_re = contract("dm,cmk->cdk", inner_cos, piece_re) + contract(
        "dm,cmk->cdk", inner_sin, piece_im
    )
    spec_im = contract("dm,cmk->cdk", inner_cos, piece_im) - contract(
        "dm,cmk->cdk", inner_sin, piece_re
    )
    return (spec_re, spec_im)


def time_signal(spec_re, spec_im):
    seq_parts = lax.axis_size("seq")
    row_count = spec_re.shape[1]
    period = 2 * seq_parts * row_count
    inner_cos, inner_sin = phase_pair(row_count, row_count, row_count, 0, 0)
    back_re = contract("md,cdk->cmk", inner_cos, spec_re) - contract(
        "md,cdk->cmk", inner_sin, spec_im
    )
    back_im = contract("md,cdk->cmk", inner_cos, spec_im) + contract(
        "md,cdk->cmk", inner_sin, spec_re
    )
    twist_cos, twist_sin = phase_pair(2, row_count, period, 2 * lax.axis_index("seq"), 0)
    twist_cos = twist_cos[:, :, None]
    twist_sin = twist_sin[:, :, None]
    turned_re = back_re * twist_cos - back_im * twist_sin
    turned_im = back_im * twist_cos + back_re * twist_sin
    outer_cos, outer_sin = phase_pair(seq_parts, 2 * seq_parts, 2 * seq_parts, 0, 0)
    piece_re = lax.all_to_all(turned_re, "seq", split_axis=1, concat_axis=0, tiled=True)
    piece_im = lax.all_to_all(turned_im, "seq", split_axis=1, concat_axis=0, tiled=True)
    summed = contract("pc,crk->prk", outer_cos, piece_re) - contract(
        "pc,crk->prk", outer_sin, piece_im
    )
    returned = summed * (1.0 / period)
    return lax.all_to_all(returned, "seq", split_axis=0, concat_axis=1, tiled=True)[0]


def spread_layer(qkv, filt, skip_gain, short_weight, w_out, g_out):
    row_count = qkv.shape[1]
    slab_width = qkv.shape[2]
    tail_rows = passed_along(qkv[:, row_count - 2 :, :], "seq", 1)
    extended = jnp.concatenate([tail_rows, qkv], axis=1)
    short = (
        short_weight[:, 0, None, :] * extended[:, 2:, :]
        + short_weight[:, 1, None, :] * extended[:, 1:-1, :]
        + short_weight[:, 2, None, :] * extended[:, :-2, :]
    )
    query_gate = short[0]
    key_short = short[1]
    value_short = short[2]
    mixed = key_short * value_short
    both_re, both_im = forward_spectrum(jnp.concatenate([mixed, filt], axis=1))
    signal_re = both_re[:, :, :slab_width]
    signal_im = both_im[:, :, :slab_width]
    kernel_re = both_re[:, :, slab_width:]
    kernel_im = both_im[:, :, slab_width:]
    conv_out = time_signal(
        signal_re * kernel_re - signal_im * kernel_im, signal_re * kernel_im + signal_im * kernel_re
    )
    long_out = conv_out + skip_gain * mixed
    gated_out = (query_gate * long_out).astype(jnp.bfloat16)
    projected = jnp.dot(
        lax.all_gather(gated_out, "ch", axis=1, tiled=True),
        w_out,
        preferred_element_type=jnp.float32,
    )
    output = projected.astype(jnp.bfloat16)
    grad_all = lax.all_gather(g_out, "ch", axis=1, tiled=True)
    rows_all = lax.all_to_all(w_out, "ch", split_axis=0, concat_axis=1, tiled=True)
    grad_gated = lax.dot_general(
        grad_all, rows_all, (((1,), (1,)), ((), ())), preferred_element_type=jnp.float32
    )
    grad_long = grad_gated * query_gate
    grad_query = grad_gated * long_out
    grad_re, grad_im = forward_spectrum(grad_long)
    pair_re = jnp.concatenate(
        [kernel_re * grad_re + kernel_im * grad_im, signal_re * grad_re + signal_im * grad_im],
        axis=2,
    )
    pair_im = jnp.concatenate(
        [kernel_re * grad_im - kernel_im * grad_re, signal_re * grad_im - signal_im * grad_re],
        axis=2,
    )
    pair_time = time_signal(pair_re, pair_im)
    grad_mixed = pair_time[:, :slab_width] + skip_gain * grad_long
    token_total = lax.axis_size("seq") * row_count
    grad_filter = pair_time[:, slab_width:] * (1.0 / math.sqrt(token_total))
    grad_short = jnp.stack([grad_query, grad_mixed * value_short, grad_mixed * key_short])
    head_rows = passed_along(grad_short[:, :2, :], "seq", -1)
    extended_grad = jnp.concatenate([grad_short, head_rows], axis=1)
    grad_qkv = (
        short_weight[:, 0, None, :] * extended_grad[:, :-2, :]
        + short_weight[:, 1, None, :] * extended_grad[:, 1:-1, :]
        + short_weight[:, 2, None, :] * extended_grad[:, 2:, :]
    ).astype(jnp.bfloat16)
    return (output, grad_qkv, grad_filter)


def split_bf16(values):
    high = values.astype(np.float32).astype(jnp.bfloat16)
    low = (values - high.astype(np.float64)).astype(np.float32).astype(jnp.bfloat16)
    return high, low


def phase_tables(tokens):
    quarter = tokens // PHASES
    freq = 2 * np.arange(quarter)[:, None] + 1
    turn = math.pi / (2 * tokens)
    angle = (freq * PHASES * np.arange(quarter)[None, :] % (4 * tokens)) * turn
    forward = np.concatenate([np.cos(angle), -np.sin(angle)], axis=1)
    backward = np.concatenate([np.cos(angle).T, -np.sin(angle).T], axis=1) / tokens
    angle = freq * np.arange(PHASES)[None, :] * turn
    twist = np.concatenate([np.cos(angle), np.sin(angle)], axis=1)
    twist = np.pad(twist, ((0, 0), (0, LANES - 2 * PHASES)))
    high, rest = split_bf16(twist)
    last = split_bf16(twist - high.astype(np.float64) - rest.astype(np.float64))[0]
    tables = np.zeros((8, quarter, 2 * quarter), jnp.bfloat16)
    tables[0], tables[1] = split_bf16(forward)
    tables[2], tables[3] = split_bf16(backward)
    for i, term in enumerate((high, rest, last)):
        tables[4, :, i * LANES : (i + 1) * LANES] = term
    return tables


def row_order(rows):
    order = np.zeros((rows, rows), np.float32)
    share = rows // PHASES
    for phase in range(PHASES):
        for j in range(share):
            order[phase * share + j, PHASES * j + phase] = 1.0
    return order.astype(jnp.bfloat16)


def mm(a, b):
    return lax.dot_general(a, b, (((1,), (0,)), ((), ())), preferred_element_type=F32)


def low_lanes(shape):
    return lax.broadcasted_iota(jnp.int32, shape, 1) < HALF


def swap(x):
    return pltpu.roll(x, HALF, 1)


class Near:
    def __init__(self, array):
        self.array = array


class Far:
    def __init__(self, array, cuts=None, turned=0):
        self.array = array
        self.turned = turned
        if turned:
            step = array.shape[0] // turned
            cuts = [(i * step, step) for i in range(turned)]
        self.cuts = cuts or [(0, array.shape[0])]
        self.rows = sum(count for _, count in self.cuts)


class Stage:
    def __init__(self, items, count_in, refs):
        arrays, scratch = list(refs[: len(items)]), list(refs[len(items) :])
        sems = scratch.pop()
        self.count_in = count_in
        self.held, self.copies, self.waiting = [], [], []
        used = 0
        for i, (item, array) in enumerate(zip(items, arrays)):
            group = []
            if isinstance(item, Near):
                self.held.append(array)
            else:
                held = scratch.pop(0)
                self.held.append(held)
                for cut, (start, count) in enumerate(item.cuts):
                    there = held.at[pl.ds(start, count)]
                    if item.turned:
                        start = pl.multiple_of((lax.axis_index("ch") ^ cut) * count, count)
                    here = array.at[pl.ds(start, count)]
                    if i >= count_in:
                        here, there = there, here
                    group.append(pltpu.make_async_copy(here, there, sems.at[used]))
                    used += 1
            self.copies.append(group)
            self.waiting.append(set(range(len(group))))
        self.given = set()

    def bring(self, index):
        for copy in self.copies[index]:
            copy.start()

    def take(self, index, cut=None):
        for i in sorted(self.waiting[index]):
            if cut is None or cut == i:
                self.copies[index][i].wait()
                self.waiting[index].discard(i)
        return self.held[index]

    def out(self, index):
        return self.held[self.count_in + index]

    def give(self, index):
        if index not in self.given:
            self.bring(self.count_in + index)
            self.given.add(index)


def staged(kernel, items, count_in, *refs):
    stage = Stage(items, count_in, refs)
    for i in range(count_in):
        stage.bring(i)
    kernel(stage)
    for i in range(count_in):
        stage.take(i)
    for i in range(len(items) - count_in):
        stage.give(i)
    for i in range(len(items) - count_in):
        stage.take(count_in + i)


def call(kernel, results, *args, flops=0, limit=VMEM_LIMIT):
    items = list(args) + list(results)
    specs, scratch, used = [], [], 0
    for item in items:
        near = isinstance(item, Near)
        specs.append(pl.BlockSpec(memory_space=pltpu.VMEM if near else pltpu.HBM))
        if not near:
            scratch.append(pltpu.VMEM((item.rows, *item.array.shape[1:]), item.array.dtype))
            used += len(item.cuts)
    moved = sum(math.prod(x.array.shape) * x.array.dtype.itemsize for x in items)
    return pl.pallas_call(
        functools.partial(staged, kernel, items, len(args)),
        out_shape=[jax.ShapeDtypeStruct(x.array.shape, x.array.dtype) for x in results],
        in_specs=specs[: len(args)],
        out_specs=specs[len(args) :],
        scratch_shapes=scratch + [pltpu.SemaphoreType.DMA((max(used, 1),))],
        compiler_params=pltpu.CompilerParams(vmem_limit_bytes=limit),
        cost_estimate=pl.CostEstimate(flops=flops, bytes_accessed=moved, transcendentals=0),
    )(*[x.array for x in args])


def lane_tile(x, index):
    return x[:, index * LANES : (index + 1) * LANES]


def pair(first, second):
    low = low_lanes(first.shape)
    return jnp.where(low, first, swap(second)), jnp.where(low, swap(first), second)


def both(x):
    turned, low = swap(x), low_lanes(x.shape)
    return jnp.where(low, x, turned), jnp.where(low, turned, x)


def start_kernel(parts, stage):
    g = stage.take(0)[...]
    width = g.shape[1]
    for part in range(parts):
        w = stage.take(1, part)[part * width : (part + 1) * width, :]
        stage.out(part)[...] = lax.dot_general(
            g, w, (((1,), (1,)), ((), ())), preferred_element_type=F32
        ).astype(BF16)
        stage.give(part)
    send_ref = stage.out(parts)
    order = stage.take(2)[...]
    qkv_ref = stage.take(3)
    query, key, value = [mm(order, qkv_ref[i]) for i in range(3)]
    taps = mm(order, stage.take(4)[...].astype(BF16))
    rows = query.shape[0]
    for tile in range(width // LANES):
        for row, (x, y) in enumerate(((key, value), (query, taps))):
            here = slice(row * rows, (row + 1) * rows)
            x, y = pair(lane_tile(x, tile), lane_tile(y, tile))
            send_ref[2 * tile, here] = x.astype(BF16)
            send_ref[2 * tile + 1, here] = y.astype(BF16)


def sum_kernel(parts, stage):
    send_ref, order_ref = stage.out(0), stage.take(0)
    total = stage.take(1)[...].astype(F32)
    for part in range(1, parts):
        total = total + stage.take(1 + part)[...].astype(F32)
    total = mm(order_ref[...], total.astype(BF16))
    half = total.shape[0] // 2
    for tile in range(total.shape[1] // LANES):
        t = lane_tile(total, tile)
        x, y = pair(t[:half], t[half:])
        send_ref[2 * tile] = x.astype(BF16)
        send_ref[2 * tile + 1] = y.astype(BF16)


def spread_phases(parts):
    (a_re, a_im), (b_re, b_im), (c_re, c_im), (d_re, d_im) = parts
    s_re, s_im, t_re, t_im = a_re + c_re, a_im + c_im, a_re - c_re, a_im - c_im
    u_re, u_im, v_re, v_im = b_re + d_re, b_im + d_im, b_re - d_re, b_im - d_im
    return [
        (s_re + u_re, s_im + u_im),
        (t_re + v_im, t_im - v_re),
        (s_re - u_re, s_im - u_im),
        (t_re - v_im, t_im + v_re),
    ]


def gather_phases(parts):
    (a_re, a_im), (b_re, b_im), (c_re, c_im), (d_re, d_im) = parts
    s_re, s_im, t_re, t_im = a_re + c_re, a_im + c_im, a_re - c_re, a_im - c_im
    u_re, u_im, v_re, v_im = b_re + d_re, b_im + d_im, b_re - d_re, b_im - d_im
    return [
        (s_re + u_re, s_im + u_im),
        (t_re - v_im, t_im + v_re),
        (s_re - u_re, s_im - u_im),
        (t_re + v_im, t_im - v_re),
    ]


def rows_of(ref, start, count):
    block = ref[:, start : start + count, :]
    return block.reshape(ref.shape[0] * count, ref.shape[2])


def turned_back(re, im, twist, phase):
    if phase == 0:
        return re, im
    c, s = twist[:, phase : phase + 1], twist[:, PHASES + phase : PHASES + phase + 1]
    return re * c + im * s, im * c - re * s


def turned_on(re, im, twist, phase):
    if phase == 0:
        return re, im
    c, s = twist[:, phase : phase + 1], twist[:, PHASES + phase : PHASES + phase + 1]
    return re * c - im * s, re * s + im * c


def lane_tile(x, index):
    return x[:, index * LANES : (index + 1) * LANES]


def causal(parts, weight):
    rows = lax.broadcasted_iota(jnp.int32, parts[0].shape, 0)
    two, three = [jnp.where(rows == 0, 0.0, pltpu.roll(parts[p], 1, 0)) for p in (2, 3)]
    once, twice = [three, *parts[:3]], [two, three, *parts[:2]]
    return [
        weight[0:1] * x + weight[1:2] * y + weight[2:3] * z for x, y, z in zip(parts, once, twice)
    ]


def anticausal(parts, weight):
    count = parts[0].shape[0]
    rows = lax.broadcasted_iota(jnp.int32, parts[0].shape, 0)
    zero, one = [
        jnp.where(rows == count - 1, 0.0, pltpu.roll(parts[p], count - 1, 0)) for p in (0, 1)
    ]
    once, twice = [*parts[1:], zero], [*parts[2:], zero, one]
    return [
        weight[0:1] * x + weight[1:2] * y + weight[2:3] * z for x, y, z in zip(parts, once, twice)
    ]


def halves(x):
    high = x.astype(BF16)
    return high, (x - high.astype(F32)).astype(BF16)


def twiddles(table_ref):
    terms = [table_ref[4, :, i * LANES : (i + 1) * LANES].astype(F32) for i in range(3)]
    return terms[0] + (terms[1] + terms[2])


def transformed(parts, table_ref, twist):
    quarter = parts[0].shape[0]
    high, rest = halves(jnp.concatenate(parts, axis=1))
    sides = []
    for side in (slice(0, quarter), slice(quarter, 2 * quarter)):
        fh, fl = table_ref[0, :, side], table_ref[1, :, side]
        sides.append(mm(fh, high) + mm(fl, high) + mm(fh, rest))
    turned = []
    for phase in range(PHASES):
        re, im = [lane_tile(side, phase) for side in sides]
        turned.append(turned_back(re, im, twist, phase))
    return spread_phases(turned)


def in_time(spectrum, table_ref, twist):
    bh, bl = table_ref[2], table_ref[3]
    parts = []
    for phase, (re, im) in enumerate(gather_phases(spectrum)):
        parts.append(jnp.concatenate(turned_on(re, im, twist, phase), axis=0))
    high, rest = halves(jnp.concatenate(parts, axis=1))
    t = mm(bh, high) + mm(bl, high) + mm(bh, rest)
    return [lane_tile(t, phase) for phase in range(PHASES)]


def own_weights(weight_ref, gain_ref):
    place = lax.axis_index("seq")
    lanes = pl.ds(pl.multiple_of(place // 2 * LANES, LANES), LANES)
    odd = place % 2 == 1

    def mine(x):
        return jnp.where(odd, swap(x), x)

    weights = [mine(weight_ref[i, :, lanes]) for i in range(3)]
    gain = both(mine(gain_ref[:, lanes]))[0]
    low = low_lanes(weights[0].shape)
    only = (lax.broadcasted_iota(jnp.int32, weights[0].shape, 0) == 0).astype(F32)
    pair_weight = jnp.where(low, weights[1], swap(weights[2]))
    query_weight = jnp.where(low, weights[0], only)
    return pair_weight, query_weight, gain


def forward_kernel(stage):
    recv_ref, weight_ref, gain_ref = [stage.take(i) for i in range(3)]
    gated_ref, saved_ref = stage.out(0), stage.out(1)
    blocks = recv_ref.shape[0]
    rows = recv_ref.shape[1] // 2
    share = rows // PHASES
    quarter = blocks * share
    low = low_lanes((quarter, LANES))
    pair_weight, query_weight, gain = own_weights(weight_ref, gain_ref)

    starts = [phase * share for phase in range(PHASES)]
    pairs = causal([rows_of(recv_ref, at, share).astype(F32) for at in starts], pair_weight)
    gates = causal([rows_of(recv_ref, rows + at, share).astype(F32) for at in starts], query_weight)
    for phase in range(PHASES):
        saved_ref[8 + phase] = pairs[phase]
    mixed = [x * swap(x) for x in pairs]
    query = [both(x)[0] for x in gates]
    stage.take(3, 1)
    table_ref = stage.take(3, 0)
    twist = twiddles(table_ref)
    spectrum = transformed([jnp.where(low, x, y) for x, y in zip(mixed, gates)], table_ref, twist)
    product = []
    for r, (re, im) in enumerate(spectrum):
        saved_ref[2 * r] = re
        saved_ref[2 * r + 1] = im
        other_re, other_im = swap(re), swap(im)
        product.append((re * other_re - im * other_im, re * other_im + im * other_re))
    stage.copies[stage.count_in + 1][0].start()
    conv = in_time(product, stage.take(3), twist)
    long_out = [x + gain * y for x, y in zip(conv, mixed)]
    gated = [x * y for x, y in zip(query, long_out)]
    for phase in range(PHASES // 2):
        t = jnp.where(low, gated[phase], gated[phase + 2]).astype(BF16)
        gated_ref[:, starts[phase] : starts[phase] + share, :] = t.reshape(blocks, share, LANES)
    for phase in range(PHASES):
        saved_ref[12 + phase] = jnp.where(low, query[phase], long_out[phase])
    stage.copies[stage.count_in + 1][1].start()
    stage.given.add(1)


def backward_kernel(stage):
    grad_ref, weight_ref, gain_ref = [stage.take(i) for i in range(3)]
    saved_ref = stage.take(4, 0)
    send_ref = stage.out(0)
    blocks = grad_ref.shape[0]
    share = grad_ref.shape[1] // 2
    rows = PHASES * share
    quarter = blocks * share
    low = low_lanes((quarter, LANES))
    pair_weight, query_weight, gain = own_weights(weight_ref, gain_ref)

    starts = [phase * share for phase in range(PHASES)]
    packed = [rows_of(grad_ref, at, share).astype(F32) for at in starts[:2]]
    grad_gated = [both(x)[i] for i in range(2) for x in packed]
    gates = [both(saved_ref[12 + phase]) for phase in range(PHASES)]
    grad_long = [x * y for x, (y, _) in zip(grad_gated, gates)]
    grad_query = anticausal([x * y for x, (_, y) in zip(grad_gated, gates)], query_weight)
    stage.take(3, 1)
    table_ref = stage.take(3, 0)
    twist = twiddles(table_ref)
    grad_spectrum = transformed(grad_long, table_ref, twist)
    stage.take(4)
    product = []
    for r, (re, im) in enumerate(grad_spectrum):
        k_re, k_im = saved_ref[2 * r], saved_ref[2 * r + 1]
        product.append((k_re * re + k_im * im, k_re * im - k_im * re))
    times = in_time(product, stage.take(3), twist)
    grad_mixed = [both(x + gain * y)[1] for x, y in zip(times, grad_long)]
    grad_pairs = anticausal(
        [x * swap(saved_ref[8 + phase]) for phase, x in enumerate(grad_mixed)], pair_weight
    )
    scale = 1.0 / math.sqrt(PHASES * quarter)
    for phase, at in enumerate(starts):
        x = grad_pairs[phase].astype(BF16)
        y = jnp.where(low, grad_query[phase], swap(times[phase]) * scale).astype(BF16)
        send_ref[:, at : at + share, :] = x.reshape(blocks, share, LANES)
        send_ref[:, rows + at : rows + at + share, :] = y.reshape(blocks, share, LANES)


def unpacked(blocks, order):
    half = blocks[0].shape[0]
    tiles = []
    for tile in range(len(blocks) // 2):
        top, bottom = pair(blocks[2 * tile].astype(F32), blocks[2 * tile + 1].astype(F32))
        tiles.append(jnp.concatenate([top, bottom], axis=0))
    return mm(order, jnp.concatenate(tiles, axis=1).astype(BF16))


def end_kernel(stage):
    recv_ref, order_ref = stage.take(0), stage.take(1)
    output_ref, grad_ref, filter_ref = [stage.out(i) for i in range(3)]
    order = order_ref[...]
    blocks = recv_ref.shape[0]
    rows = recv_ref.shape[1] // 2
    sides = []
    for at in (0, rows):
        firsts, seconds = [], []
        for tile in range(blocks // 2):
            x, y = [recv_ref[2 * tile + i, at : at + rows].astype(F32) for i in range(2)]
            first, second = pair(x, y)
            firsts.append(first)
            seconds.append(second)
        for side in (firsts, seconds):
            sides.append(mm(order, jnp.concatenate(side, axis=1).astype(BF16)))
    key, value, query, taps = sides
    filter_ref[...] = taps
    stage.give(2)
    grad_ref[0] = query.astype(BF16)
    grad_ref[1] = key.astype(BF16)
    grad_ref[2] = value.astype(BF16)
    stage.give(1)
    gated_ref, w_ref = stage.take(2), stage.take(3)
    parts = gated_ref.shape[0]
    width = w_ref.shape[0] // parts
    total = None
    for part in range(parts):
        block = unpacked([gated_ref[part, i] for i in range(blocks)], order).astype(BF16)
        term = mm(block, w_ref[part * width : (part + 1) * width, :])
        total = term if total is None else total + term
    output_ref[...] = total.astype(BF16)


def partner(x, axis, mask):
    return lax.ppermute(x, axis, [(i, i ^ mask) for i in range(lax.axis_size(axis))])


def exchanged(x, axis):
    return lax.all_to_all(x, axis, split_axis=0, concat_axis=0, tiled=True)


def owner_layer(qkv, filt, skip_gain, short_weight, w_out, g_out):
    shape = jax.ShapeDtypeStruct
    seq_parts, ch_parts = lax.axis_size("seq"), lax.axis_size("ch")
    rows, width = qkv.shape[1], qkv.shape[2]
    tokens = seq_parts * rows
    quarter = tokens // PHASES
    order = row_order(rows)
    tables = Far(jnp.asarray(phase_tables(tokens)), [(0, 2), (4, 1), (2, 2)])
    table_flops = 2 * 2 * 2 * 3 * tokens * tokens // PHASES * LANES
    product_flops = 2 * rows * width * width * ch_parts
    packed = shape((seq_parts, rows // 2, LANES), BF16)
    double = shape((seq_parts, 2 * rows, LANES), BF16)
    column = shape((rows, width), BF16)
    saved = shape((4 * PHASES, quarter, LANES), F32)
    weight, gain = Near(short_weight), Near(skip_gain[None, :])

    *partial, send = call(
        functools.partial(start_kernel, ch_parts),
        [Far(column)] * ch_parts + [Far(double)],
        Far(g_out),
        Far(w_out, turned=ch_parts),
        Far(order),
        Far(qkv),
        Far(filt),
        flops=product_flops,
        limit=WHOLE_VMEM,
    )
    recv = exchanged(send, "seq")
    partial = [partner(x, "ch", mask) if mask else x for mask, x in enumerate(partial)]
    (send,) = call(
        functools.partial(sum_kernel, ch_parts),
        [Near(packed)],
        Near(order),
        *[Near(x) for x in partial],
    )
    grad_recv = exchanged(send, "seq")
    send, kept = call(
        forward_kernel,
        [Near(packed), Far(saved, [(0, 12), (12, 4)])],
        Near(recv),
        weight,
        gain,
        tables,
        flops=table_flops,
    )
    gated = exchanged(send, "seq")
    (send,) = call(
        backward_kernel,
        [Near(double)],
        Near(grad_recv),
        weight,
        gain,
        tables,
        Far(kept, [(12, 4), (0, 12)]),
        flops=table_flops,
    )
    grad_recv = exchanged(send, "seq")
    gated = lax.all_gather(gated, "ch", axis=0, tiled=False)
    output, grad_qkv, grad_filter = call(
        end_kernel,
        [Far(column), Far(shape((3, rows, width), BF16)), Far(shape((rows, width), F32))],
        Near(grad_recv),
        Near(order.T),
        Near(gated),
        Far(w_out),
        flops=product_flops,
    )
    return (output, grad_qkv, grad_filter)


def local(qkv, filt, skip_gain, short_weight, w_out, g_out):
    seq_parts = lax.axis_size("seq")
    rows, width = qkv.shape[1], qkv.shape[2]
    fits = width == HALF * seq_parts and rows % HALF == 0 and rows * seq_parts <= 2048
    if fits and lax.axis_size("ch") == 4:
        return owner_layer(qkv, filt, skip_gain, short_weight, w_out, g_out)
    return spread_layer(qkv, filt, skip_gain, short_weight, w_out, g_out)


def solution(mesh):
    in_specs = (
        P(None, "seq", "ch"),
        P("seq", "ch"),
        P("ch"),
        P(None, None, "ch"),
        P(None, "ch"),
        P("seq", "ch"),
    )
    out_specs = (P("seq", "ch"), P(None, "seq", "ch"), P("seq", "ch"))
    return jax.shard_map(local, mesh=mesh, in_specs=in_specs, out_specs=out_specs, check_vma=False)
```

```python
import functools
import math

import jax
import jax.numpy as jnp
import numpy as np
from jax import lax
from jax.experimental import pallas as pl
from jax.experimental.pallas import tpu as pltpu
from jax.sharding import PartitionSpec as P

HIGHEST = lax.Precision.HIGHEST
TWO_PI = 2.0 * math.pi
LANES = 128
HALF = 64
PHASES = 4
BF16 = jnp.bfloat16
F32 = jnp.float32
VMEM_LIMIT = 24 * 1024 * 1024


def passed_along(block, axis, distance):
    devices = range(lax.axis_size(axis))
    route = [(i - distance, i) for i in devices if i - distance in devices]
    return lax.ppermute(block, axis, route)


def phase_pair(left_count, right_count, period, left_start, right_start):
    left_idx = lax.broadcasted_iota(jnp.int32, (left_count, right_count), 0) + left_start
    right_idx = lax.broadcasted_iota(jnp.int32, (left_count, right_count), 1) + right_start
    angle_all = (left_idx * right_idx % period).astype(jnp.float32) * (TWO_PI / period)
    return (jnp.cos(angle_all), jnp.sin(angle_all))


def contract(pattern, matrix, values):
    return jnp.einsum(
        pattern, matrix, values, precision=HIGHEST, preferred_element_type=jnp.float32
    )


def forward_spectrum(signal):
    seq_parts = lax.axis_size("seq")
    row_count = signal.shape[0]
    row_share = row_count // seq_parts
    period = 2 * seq_parts * row_count
    spread_in = lax.all_to_all(signal[None], "seq", split_axis=1, concat_axis=0, tiled=True)
    outer_cos, outer_sin = phase_pair(2 * seq_parts, seq_parts, 2 * seq_parts, 0, 0)
    section_re = contract("cp,prw->crw", outer_cos, spread_in)
    section_im = -contract("cp,prw->crw", outer_sin, spread_in)
    twist_cos, twist_sin = phase_pair(
        2 * seq_parts, row_share, period, 0, lax.axis_index("seq") * row_share
    )
    twist_cos = twist_cos[:, :, None]
    twist_sin = twist_sin[:, :, None]
    turned_re = section_re * twist_cos + section_im * twist_sin
    turned_im = section_im * twist_cos - section_re * twist_sin
    inner_cos, inner_sin = phase_pair(row_count, row_count, row_count, 0, 0)
    piece_re = lax.all_to_all(turned_re, "seq", split_axis=0, concat_axis=1, tiled=True)
    piece_im = lax.all_to_all(turned_im, "seq", split_axis=0, concat_axis=1, tiled=True)
    spec_re = contract("dm,cmk->cdk", inner_cos, piece_re) + contract(
        "dm,cmk->cdk", inner_sin, piece_im
    )
    spec_im = contract("dm,cmk->cdk", inner_cos, piece_im) - contract(
        "dm,cmk->cdk", inner_sin, piece_re
    )
    return (spec_re, spec_im)


def time_signal(spec_re, spec_im):
    seq_parts = lax.axis_size("seq")
    row_count = spec_re.shape[1]
    period = 2 * seq_parts * row_count
    inner_cos, inner_sin = phase_pair(row_count, row_count, row_count, 0, 0)
    back_re = contract("md,cdk->cmk", inner_cos, spec_re) - contract(
        "md,cdk->cmk", inner_sin, spec_im
    )
    back_im = contract("md,cdk->cmk", inner_cos, spec_im) + contract(
        "md,cdk->cmk", inner_sin, spec_re
    )
    twist_cos, twist_sin = phase_pair(2, row_count, period, 2 * lax.axis_index("seq"), 0)
    twist_cos = twist_cos[:, :, None]
    twist_sin = twist_sin[:, :, None]
    turned_re = back_re * twist_cos - back_im * twist_sin
    turned_im = back_im * twist_cos + back_re * twist_sin
    outer_cos, outer_sin = phase_pair(seq_parts, 2 * seq_parts, 2 * seq_parts, 0, 0)
    piece_re = lax.all_to_all(turned_re, "seq", split_axis=1, concat_axis=0, tiled=True)
    piece_im = lax.all_to_all(turned_im, "seq", split_axis=1, concat_axis=0, tiled=True)
    summed = contract("pc,crk->prk", outer_cos, piece_re) - contract(
        "pc,crk->prk", outer_sin, piece_im
    )
    returned = summed * (1.0 / period)
    return lax.all_to_all(returned, "seq", split_axis=0, concat_axis=1, tiled=True)[0]


def spread_layer(qkv, filt, skip_gain, short_weight, w_out, g_out):
    row_count = qkv.shape[1]
    slab_width = qkv.shape[2]
    tail_rows = passed_along(qkv[:, row_count - 2 :, :], "seq", 1)
    extended = jnp.concatenate([tail_rows, qkv], axis=1)
    short = (
        short_weight[:, 0, None, :] * extended[:, 2:, :]
        + short_weight[:, 1, None, :] * extended[:, 1:-1, :]
        + short_weight[:, 2, None, :] * extended[:, :-2, :]
    )
    query_gate = short[0]
    key_short = short[1]
    value_short = short[2]
    mixed = key_short * value_short
    both_re, both_im = forward_spectrum(jnp.concatenate([mixed, filt], axis=1))
    signal_re = both_re[:, :, :slab_width]
    signal_im = both_im[:, :, :slab_width]
    kernel_re = both_re[:, :, slab_width:]
    kernel_im = both_im[:, :, slab_width:]
    conv_out = time_signal(
        signal_re * kernel_re - signal_im * kernel_im, signal_re * kernel_im + signal_im * kernel_re
    )
    long_out = conv_out + skip_gain * mixed
    gated_out = (query_gate * long_out).astype(jnp.bfloat16)
    projected = jnp.dot(
        lax.all_gather(gated_out, "ch", axis=1, tiled=True),
        w_out,
        preferred_element_type=jnp.float32,
    )
    output = projected.astype(jnp.bfloat16)
    grad_all = lax.all_gather(g_out, "ch", axis=1, tiled=True)
    rows_all = lax.all_to_all(w_out, "ch", split_axis=0, concat_axis=1, tiled=True)
    grad_gated = lax.dot_general(
        grad_all, rows_all, (((1,), (1,)), ((), ())), preferred_element_type=jnp.float32
    )
    grad_long = grad_gated * query_gate
    grad_query = grad_gated * long_out
    grad_re, grad_im = forward_spectrum(grad_long)
    pair_re = jnp.concatenate(
        [kernel_re * grad_re + kernel_im * grad_im, signal_re * grad_re + signal_im * grad_im],
        axis=2,
    )
    pair_im = jnp.concatenate(
        [kernel_re * grad_im - kernel_im * grad_re, signal_re * grad_im - signal_im * grad_re],
        axis=2,
    )
    pair_time = time_signal(pair_re, pair_im)
    grad_mixed = pair_time[:, :slab_width] + skip_gain * grad_long
    token_total = lax.axis_size("seq") * row_count
    grad_filter = pair_time[:, slab_width:] * (1.0 / math.sqrt(token_total))
    grad_short = jnp.stack([grad_query, grad_mixed * value_short, grad_mixed * key_short])
    head_rows = passed_along(grad_short[:, :2, :], "seq", -1)
    extended_grad = jnp.concatenate([grad_short, head_rows], axis=1)
    grad_qkv = (
        short_weight[:, 0, None, :] * extended_grad[:, :-2, :]
        + short_weight[:, 1, None, :] * extended_grad[:, 1:-1, :]
        + short_weight[:, 2, None, :] * extended_grad[:, 2:, :]
    ).astype(jnp.bfloat16)
    return (output, grad_qkv, grad_filter)


def split_bf16(values):
    high = values.astype(np.float32).astype(jnp.bfloat16)
    low = (values - high.astype(np.float64)).astype(np.float32).astype(jnp.bfloat16)
    return high, low


def phase_tables(tokens):
    quarter = tokens // PHASES
    freq = 2 * np.arange(quarter)[:, None] + 1
    turn = math.pi / (2 * tokens)
    angle = (freq * PHASES * np.arange(quarter)[None, :] % (4 * tokens)) * turn
    forward = np.concatenate([np.cos(angle), -np.sin(angle)], axis=1)
    backward = np.concatenate([np.cos(angle).T, -np.sin(angle).T], axis=1) / tokens
    angle = freq * np.arange(PHASES)[None, :] * turn
    twist = np.concatenate([np.cos(angle), np.sin(angle)], axis=1)
    twist = np.pad(twist, ((0, 0), (0, LANES - 2 * PHASES)))
    high, rest = split_bf16(twist)
    last = split_bf16(twist - high.astype(np.float64) - rest.astype(np.float64))[0]
    tables = np.zeros((8, quarter, 2 * quarter), jnp.bfloat16)
    tables[0], tables[1] = split_bf16(forward)
    tables[2], tables[3] = split_bf16(backward)
    for i, term in enumerate((high, rest, last)):
        tables[4, :, i * LANES : (i + 1) * LANES] = term
    return tables


def row_order(rows):
    order = np.zeros((rows, rows), np.float32)
    share = rows // PHASES
    for phase in range(PHASES):
        for j in range(share):
            order[phase * share + j, PHASES * j + phase] = 1.0
    return order.astype(jnp.bfloat16)


def mm(a, b):
    return lax.dot_general(a, b, (((1,), (0,)), ((), ())), preferred_element_type=F32)


def low_lanes(shape):
    return lax.broadcasted_iota(jnp.int32, shape, 1) < HALF


def swap(x):
    return pltpu.roll(x, HALF, 1)


class Near:
    def __init__(self, array):
        self.array = array


class Far:
    def __init__(self, array, cuts=None, turned=0):
        self.array = array
        self.turned = turned
        if turned:
            step = array.shape[0] // turned
            cuts = [(i * step, step) for i in range(turned)]
        self.cuts = cuts or [(0, array.shape[0])]
        self.rows = sum(count for _, count in self.cuts)


class Stage:
    def __init__(self, items, count_in, refs):
        arrays, scratch = list(refs[: len(items)]), list(refs[len(items) :])
        sems = scratch.pop()
        self.count_in = count_in
        self.held, self.copies, self.waiting = [], [], []
        used = 0
        for i, (item, array) in enumerate(zip(items, arrays)):
            group = []
            if isinstance(item, Near):
                self.held.append(array)
            else:
                held = scratch.pop(0)
                self.held.append(held)
                for cut, (start, count) in enumerate(item.cuts):
                    there = held.at[pl.ds(start, count)]
                    if item.turned:
                        start = pl.multiple_of((lax.axis_index("ch") ^ cut) * count, count)
                    here = array.at[pl.ds(start, count)]
                    if i >= count_in:
                        here, there = there, here
                    group.append(pltpu.make_async_copy(here, there, sems.at[used]))
                    used += 1
            self.copies.append(group)
            self.waiting.append(set(range(len(group))))
        self.given = set()

    def bring(self, index):
        for copy in self.copies[index]:
            copy.start()

    def take(self, index, cut=None):
        for i in sorted(self.waiting[index]):
            if cut is None or cut == i:
                self.copies[index][i].wait()
                self.waiting[index].discard(i)
        return self.held[index]

    def out(self, index):
        return self.held[self.count_in + index]

    def give(self, index):
        if index not in self.given:
            self.bring(self.count_in + index)
            self.given.add(index)


def staged(kernel, items, count_in, *refs):
    stage = Stage(items, count_in, refs)
    for i in range(count_in):
        stage.bring(i)
    kernel(stage)
    for i in range(count_in):
        stage.take(i)
    for i in range(len(items) - count_in):
        stage.give(i)
    for i in range(len(items) - count_in):
        stage.take(count_in + i)


def in_hbm(x):
    return pltpu.with_memory_space_constraint(x, pltpu.HBM)


def call(kernel, results, *args, flops=0):
    items = list(args) + list(results)
    specs, scratch, used = [], [], 0
    for item in items:
        near = isinstance(item, Near)
        specs.append(pl.BlockSpec(memory_space=pltpu.VMEM if near else pltpu.HBM))
        if not near:
            scratch.append(pltpu.VMEM((item.rows, *item.array.shape[1:]), item.array.dtype))
            used += len(item.cuts)
    moved = sum(math.prod(x.array.shape) * x.array.dtype.itemsize for x in items)
    return pl.pallas_call(
        functools.partial(staged, kernel, items, len(args)),
        out_shape=[
            (jax.ShapeDtypeStruct if isinstance(x, Near) else pltpu.HBM)(
                x.array.shape, x.array.dtype
            )
            for x in results
        ],
        in_specs=specs[: len(args)],
        out_specs=specs[len(args) :],
        scratch_shapes=scratch + [pltpu.SemaphoreType.DMA((max(used, 1),))],
        compiler_params=pltpu.CompilerParams(vmem_limit_bytes=VMEM_LIMIT),
        cost_estimate=pl.CostEstimate(flops=flops, bytes_accessed=moved, transcendentals=0),
    )(*[x.array if isinstance(x, Near) else in_hbm(x.array) for x in args])


def lane_tile(x, index):
    return x[:, index * LANES : (index + 1) * LANES]


def pair(first, second):
    low = low_lanes(first.shape)
    return jnp.where(low, first, swap(second)), jnp.where(low, swap(first), second)


def both(x):
    turned, low = swap(x), low_lanes(x.shape)
    return jnp.where(low, x, turned), jnp.where(low, turned, x)


def start_kernel(parts, stage):
    g = stage.take(0)[...]
    width = g.shape[1]
    for part in range(parts):
        w = stage.take(1, part)[part * width : (part + 1) * width, :]
        stage.out(part)[...] = lax.dot_general(
            g, w, (((1,), (1,)), ((), ())), preferred_element_type=F32
        ).astype(BF16)
        stage.give(part)
    send_ref = stage.out(parts)
    order = stage.take(2)[...]
    qkv_ref = stage.take(3)
    query, key, value = [mm(order, qkv_ref[i]) for i in range(3)]
    taps = mm(order, stage.take(4)[...].astype(BF16))
    rows = query.shape[0]
    for tile in range(width // LANES):
        for row, (x, y) in enumerate(((key, value), (query, taps))):
            here = slice(row * rows, (row + 1) * rows)
            x, y = pair(lane_tile(x, tile), lane_tile(y, tile))
            send_ref[2 * tile, here] = x.astype(BF16)
            send_ref[2 * tile + 1, here] = y.astype(BF16)


def sum_kernel(parts, stage):
    send_ref, order_ref = stage.out(0), stage.take(0)
    total = stage.take(1)[...].astype(F32)
    for part in range(1, parts):
        total = total + stage.take(1 + part)[...].astype(F32)
    total = mm(order_ref[...], total.astype(BF16))
    half = total.shape[0] // 2
    for tile in range(total.shape[1] // LANES):
        t = lane_tile(total, tile)
        x, y = pair(t[:half], t[half:])
        send_ref[2 * tile] = x.astype(BF16)
        send_ref[2 * tile + 1] = y.astype(BF16)


def spread_phases(parts):
    (a_re, a_im), (b_re, b_im), (c_re, c_im), (d_re, d_im) = parts
    s_re, s_im, t_re, t_im = a_re + c_re, a_im + c_im, a_re - c_re, a_im - c_im
    u_re, u_im, v_re, v_im = b_re + d_re, b_im + d_im, b_re - d_re, b_im - d_im
    return [
        (s_re + u_re, s_im + u_im),
        (t_re + v_im, t_im - v_re),
        (s_re - u_re, s_im - u_im),
        (t_re - v_im, t_im + v_re),
    ]


def gather_phases(parts):
    (a_re, a_im), (b_re, b_im), (c_re, c_im), (d_re, d_im) = parts
    s_re, s_im, t_re, t_im = a_re + c_re, a_im + c_im, a_re - c_re, a_im - c_im
    u_re, u_im, v_re, v_im = b_re + d_re, b_im + d_im, b_re - d_re, b_im - d_im
    return [
        (s_re + u_re, s_im + u_im),
        (t_re - v_im, t_im + v_re),
        (s_re - u_re, s_im - u_im),
        (t_re + v_im, t_im - v_re),
    ]


def rows_of(ref, start, count):
    block = ref[:, start : start + count, :]
    return block.reshape(ref.shape[0] * count, ref.shape[2])


def turned_back(re, im, twist, phase):
    if phase == 0:
        return re, im
    c, s = twist[:, phase : phase + 1], twist[:, PHASES + phase : PHASES + phase + 1]
    return re * c + im * s, im * c - re * s


def turned_on(re, im, twist, phase):
    if phase == 0:
        return re, im
    c, s = twist[:, phase : phase + 1], twist[:, PHASES + phase : PHASES + phase + 1]
    return re * c - im * s, re * s + im * c


def lane_tile(x, index):
    return x[:, index * LANES : (index + 1) * LANES]


def causal(parts, weight):
    rows = lax.broadcasted_iota(jnp.int32, parts[0].shape, 0)
    two, three = [jnp.where(rows == 0, 0.0, pltpu.roll(parts[p], 1, 0)) for p in (2, 3)]
    once, twice = [three, *parts[:3]], [two, three, *parts[:2]]
    return [
        weight[0:1] * x + weight[1:2] * y + weight[2:3] * z for x, y, z in zip(parts, once, twice)
    ]


def anticausal(parts, weight):
    count = parts[0].shape[0]
    rows = lax.broadcasted_iota(jnp.int32, parts[0].shape, 0)
    zero, one = [
        jnp.where(rows == count - 1, 0.0, pltpu.roll(parts[p], count - 1, 0)) for p in (0, 1)
    ]
    once, twice = [*parts[1:], zero], [*parts[2:], zero, one]
    return [
        weight[0:1] * x + weight[1:2] * y + weight[2:3] * z for x, y, z in zip(parts, once, twice)
    ]


def halves(x):
    high = x.astype(BF16)
    return high, (x - high.astype(F32)).astype(BF16)


def twiddles(table_ref):
    terms = [table_ref[4, :, i * LANES : (i + 1) * LANES].astype(F32) for i in range(3)]
    return terms[0] + (terms[1] + terms[2])


def transformed(parts, table_ref, twist):
    quarter = parts[0].shape[0]
    high, rest = halves(jnp.concatenate(parts, axis=1))
    sides = []
    for side in (slice(0, quarter), slice(quarter, 2 * quarter)):
        fh, fl = table_ref[0, :, side], table_ref[1, :, side]
        sides.append(mm(fh, high) + mm(fl, high) + mm(fh, rest))
    turned = []
    for phase in range(PHASES):
        re, im = [lane_tile(side, phase) for side in sides]
        turned.append(turned_back(re, im, twist, phase))
    return spread_phases(turned)


def in_time(spectrum, table_ref, twist):
    bh, bl = table_ref[2], table_ref[3]
    parts = []
    for phase, (re, im) in enumerate(gather_phases(spectrum)):
        parts.append(jnp.concatenate(turned_on(re, im, twist, phase), axis=0))
    high, rest = halves(jnp.concatenate(parts, axis=1))
    t = mm(bh, high) + mm(bl, high) + mm(bh, rest)
    return [lane_tile(t, phase) for phase in range(PHASES)]


def own_weights(weight_ref, gain_ref):
    place = lax.axis_index("seq")
    lanes = pl.ds(pl.multiple_of(place // 2 * LANES, LANES), LANES)
    odd = place % 2 == 1

    def mine(x):
        return jnp.where(odd, swap(x), x)

    weights = [mine(weight_ref[i, :, lanes]) for i in range(3)]
    gain = both(mine(gain_ref[:, lanes]))[0]
    low = low_lanes(weights[0].shape)
    only = (lax.broadcasted_iota(jnp.int32, weights[0].shape, 0) == 0).astype(F32)
    pair_weight = jnp.where(low, weights[1], swap(weights[2]))
    query_weight = jnp.where(low, weights[0], only)
    return pair_weight, query_weight, gain


def forward_kernel(stage):
    recv_ref, weight_ref, gain_ref = [stage.take(i) for i in range(3)]
    gated_ref, saved_ref = stage.out(0), stage.out(1)
    blocks = recv_ref.shape[0]
    rows = recv_ref.shape[1] // 2
    share = rows // PHASES
    quarter = blocks * share
    low = low_lanes((quarter, LANES))
    pair_weight, query_weight, gain = own_weights(weight_ref, gain_ref)

    starts = [phase * share for phase in range(PHASES)]
    pairs = causal([rows_of(recv_ref, at, share).astype(F32) for at in starts], pair_weight)
    gates = causal([rows_of(recv_ref, rows + at, share).astype(F32) for at in starts], query_weight)
    for phase in range(PHASES):
        saved_ref[8 + phase] = pairs[phase]
    mixed = [x * swap(x) for x in pairs]
    query = [both(x)[0] for x in gates]
    stage.take(3, 1)
    table_ref = stage.take(3, 0)
    twist = twiddles(table_ref)
    spectrum = transformed([jnp.where(low, x, y) for x, y in zip(mixed, gates)], table_ref, twist)
    product = []
    for r, (re, im) in enumerate(spectrum):
        saved_ref[2 * r] = re
        saved_ref[2 * r + 1] = im
        other_re, other_im = swap(re), swap(im)
        product.append((re * other_re - im * other_im, re * other_im + im * other_re))
    stage.copies[stage.count_in + 1][0].start()
    conv = in_time(product, stage.take(3), twist)
    long_out = [x + gain * y for x, y in zip(conv, mixed)]
    gated = [x * y for x, y in zip(query, long_out)]
    for phase in range(PHASES // 2):
        t = jnp.where(low, gated[phase], gated[phase + 2]).astype(BF16)
        gated_ref[:, starts[phase] : starts[phase] + share, :] = t.reshape(blocks, share, LANES)
    for phase in range(PHASES):
        saved_ref[12 + phase] = jnp.where(low, query[phase], long_out[phase])
    stage.copies[stage.count_in + 1][1].start()
    stage.given.add(1)


def backward_kernel(stage):
    grad_ref, weight_ref, gain_ref = [stage.take(i) for i in range(3)]
    saved_ref = stage.take(4, 0)
    send_ref = stage.out(0)
    blocks = grad_ref.shape[0]
    share = grad_ref.shape[1] // 2
    rows = PHASES * share
    quarter = blocks * share
    low = low_lanes((quarter, LANES))
    pair_weight, query_weight, gain = own_weights(weight_ref, gain_ref)

    starts = [phase * share for phase in range(PHASES)]
    packed = [rows_of(grad_ref, at, share).astype(F32) for at in starts[:2]]
    grad_gated = [both(x)[i] for i in range(2) for x in packed]
    gates = [both(saved_ref[12 + phase]) for phase in range(PHASES)]
    grad_long = [x * y for x, (y, _) in zip(grad_gated, gates)]
    grad_query = anticausal([x * y for x, (_, y) in zip(grad_gated, gates)], query_weight)
    stage.take(3, 1)
    table_ref = stage.take(3, 0)
    twist = twiddles(table_ref)
    grad_spectrum = transformed(grad_long, table_ref, twist)
    stage.take(4)
    product = []
    for r, (re, im) in enumerate(grad_spectrum):
        k_re, k_im = saved_ref[2 * r], saved_ref[2 * r + 1]
        product.append((k_re * re + k_im * im, k_re * im - k_im * re))
    times = in_time(product, stage.take(3), twist)
    grad_mixed = [both(x + gain * y)[1] for x, y in zip(times, grad_long)]
    grad_pairs = anticausal(
        [x * swap(saved_ref[8 + phase]) for phase, x in enumerate(grad_mixed)], pair_weight
    )
    scale = 1.0 / math.sqrt(PHASES * quarter)
    for phase, at in enumerate(starts):
        x = grad_pairs[phase].astype(BF16)
        y = jnp.where(low, grad_query[phase], swap(times[phase]) * scale).astype(BF16)
        send_ref[:, at : at + share, :] = x.reshape(blocks, share, LANES)
        send_ref[:, rows + at : rows + at + share, :] = y.reshape(blocks, share, LANES)


def unpacked(blocks, order):
    half = blocks[0].shape[0]
    tiles = []
    for tile in range(len(blocks) // 2):
        top, bottom = pair(blocks[2 * tile].astype(F32), blocks[2 * tile + 1].astype(F32))
        tiles.append(jnp.concatenate([top, bottom], axis=0))
    return mm(order, jnp.concatenate(tiles, axis=1).astype(BF16))


def end_kernel(stage):
    recv_ref, order_ref = stage.take(0), stage.take(1)
    output_ref, grad_ref, filter_ref = [stage.out(i) for i in range(3)]
    order = order_ref[...]
    blocks = recv_ref.shape[0]
    rows = recv_ref.shape[1] // 2
    sides = []
    for at in (0, rows):
        firsts, seconds = [], []
        for tile in range(blocks // 2):
            x, y = [recv_ref[2 * tile + i, at : at + rows].astype(F32) for i in range(2)]
            first, second = pair(x, y)
            firsts.append(first)
            seconds.append(second)
        for side in (firsts, seconds):
            sides.append(mm(order, jnp.concatenate(side, axis=1).astype(BF16)))
    key, value, query, taps = sides
    filter_ref[...] = taps
    stage.give(2)
    grad_ref[0] = query.astype(BF16)
    grad_ref[1] = key.astype(BF16)
    grad_ref[2] = value.astype(BF16)
    stage.give(1)
    gated_ref, w_ref = stage.take(2), stage.take(3)
    parts = gated_ref.shape[0]
    width = w_ref.shape[0] // parts
    total = None
    for part in range(parts):
        block = unpacked([gated_ref[part, i] for i in range(blocks)], order).astype(BF16)
        term = mm(block, w_ref[part * width : (part + 1) * width, :])
        total = term if total is None else total + term
    output_ref[...] = total.astype(BF16)


def partner(x, axis, mask):
    return lax.ppermute(x, axis, [(i, i ^ mask) for i in range(lax.axis_size(axis))])


def exchanged(x, axis):
    return lax.all_to_all(x, axis, split_axis=0, concat_axis=0, tiled=True)


def owner_layer(qkv, filt, skip_gain, short_weight, w_out, g_out):
    shape = jax.ShapeDtypeStruct
    seq_parts, ch_parts = lax.axis_size("seq"), lax.axis_size("ch")
    rows, width = qkv.shape[1], qkv.shape[2]
    tokens = seq_parts * rows
    quarter = tokens // PHASES
    order = row_order(rows)
    tables = Far(jnp.asarray(phase_tables(tokens)), [(0, 2), (4, 1), (2, 2)])
    table_flops = 2 * 2 * 2 * 3 * tokens * tokens // PHASES * LANES
    product_flops = 2 * rows * width * width * ch_parts
    packed = shape((seq_parts, rows // 2, LANES), BF16)
    double = shape((seq_parts, 2 * rows, LANES), BF16)
    column = shape((rows, width), BF16)
    saved = shape((4 * PHASES, quarter, LANES), F32)
    weight, gain = Far(short_weight), Far(skip_gain[None, :])

    *partial, send = call(
        functools.partial(start_kernel, ch_parts),
        [Far(column)] * ch_parts + [Far(double)],
        Far(g_out),
        Far(w_out, turned=ch_parts),
        Far(order),
        Far(qkv),
        Far(filt),
        flops=product_flops,
    )
    recv = exchanged(send, "seq")
    partial = [partner(x, "ch", mask) if mask else x for mask, x in enumerate(partial)]
    (send,) = call(
        functools.partial(sum_kernel, ch_parts),
        [Far(packed)],
        Far(order),
        Far(partial[0]),
        *[Near(x) for x in partial[1:]],
    )
    grad_recv = exchanged(send, "seq")
    send, kept = call(
        forward_kernel,
        [Far(packed), Far(saved, [(0, 12), (12, 4)])],
        Near(recv),
        weight,
        gain,
        tables,
        flops=table_flops,
    )
    gated = exchanged(send, "seq")
    (send,) = call(
        backward_kernel,
        [Far(double)],
        Far(grad_recv),
        weight,
        gain,
        tables,
        Far(kept, [(12, 4), (0, 12)]),
        flops=table_flops,
    )
    grad_recv = exchanged(send, "seq")
    gated = lax.all_gather(gated, "ch", axis=0, tiled=False)
    output, grad_qkv, grad_filter = call(
        end_kernel,
        [Far(column), Far(shape((3, rows, width), BF16)), Far(shape((rows, width), F32))],
        Near(grad_recv),
        Far(order.T),
        Far(gated),
        Far(w_out),
        flops=product_flops,
    )
    return (output, grad_qkv, grad_filter)


def local(qkv, filt, skip_gain, short_weight, w_out, g_out):
    seq_parts = lax.axis_size("seq")
    rows, width = qkv.shape[1], qkv.shape[2]
    fits = width == HALF * seq_parts and rows % HALF == 0 and rows * seq_parts <= 2048
    if fits and lax.axis_size("ch") == 4:
        return owner_layer(qkv, filt, skip_gain, short_weight, w_out, g_out)
    return spread_layer(qkv, filt, skip_gain, short_weight, w_out, g_out)


def solution(mesh):
    in_specs = (
        P(None, "seq", "ch"),
        P("seq", "ch"),
        P("ch"),
        P(None, None, "ch"),
        P(None, "ch"),
        P("seq", "ch"),
    )
    out_specs = (P("seq", "ch"), P(None, "seq", "ch"), P("seq", "ch"))
    return jax.shard_map(local, mesh=mesh, in_specs=in_specs, out_specs=out_specs, check_vma=False)
```

```python
import functools
import math

import jax
import jax.numpy as jnp
import numpy as np
from jax import lax
from jax.experimental import pallas as pl
from jax.experimental.pallas import tpu as pltpu
from jax.sharding import PartitionSpec as P

HIGHEST = lax.Precision.HIGHEST
TWO_PI = 2.0 * math.pi
LANES = 128
HALF = 64
PHASES = 4
BF16 = jnp.bfloat16
F32 = jnp.float32
VMEM_LIMIT = 24 * 1024 * 1024


def passed_along(block, axis, distance):
    devices = range(lax.axis_size(axis))
    route = [(i - distance, i) for i in devices if i - distance in devices]
    return lax.ppermute(block, axis, route)


def phase_pair(left_count, right_count, period, left_start, right_start):
    left_idx = lax.broadcasted_iota(jnp.int32, (left_count, right_count), 0) + left_start
    right_idx = lax.broadcasted_iota(jnp.int32, (left_count, right_count), 1) + right_start
    angle_all = (left_idx * right_idx % period).astype(jnp.float32) * (TWO_PI / period)
    return (jnp.cos(angle_all), jnp.sin(angle_all))


def contract(pattern, matrix, values):
    return jnp.einsum(
        pattern, matrix, values, precision=HIGHEST, preferred_element_type=jnp.float32
    )


def forward_spectrum(signal):
    seq_parts = lax.axis_size("seq")
    row_count = signal.shape[0]
    row_share = row_count // seq_parts
    period = 2 * seq_parts * row_count
    spread_in = lax.all_to_all(signal[None], "seq", split_axis=1, concat_axis=0, tiled=True)
    outer_cos, outer_sin = phase_pair(2 * seq_parts, seq_parts, 2 * seq_parts, 0, 0)
    section_re = contract("cp,prw->crw", outer_cos, spread_in)
    section_im = -contract("cp,prw->crw", outer_sin, spread_in)
    twist_cos, twist_sin = phase_pair(
        2 * seq_parts, row_share, period, 0, lax.axis_index("seq") * row_share
    )
    twist_cos = twist_cos[:, :, None]
    twist_sin = twist_sin[:, :, None]
    turned_re = section_re * twist_cos + section_im * twist_sin
    turned_im = section_im * twist_cos - section_re * twist_sin
    inner_cos, inner_sin = phase_pair(row_count, row_count, row_count, 0, 0)
    piece_re = lax.all_to_all(turned_re, "seq", split_axis=0, concat_axis=1, tiled=True)
    piece_im = lax.all_to_all(turned_im, "seq", split_axis=0, concat_axis=1, tiled=True)
    spec_re = contract("dm,cmk->cdk", inner_cos, piece_re) + contract(
        "dm,cmk->cdk", inner_sin, piece_im
    )
    spec_im = contract("dm,cmk->cdk", inner_cos, piece_im) - contract(
        "dm,cmk->cdk", inner_sin, piece_re
    )
    return (spec_re, spec_im)


def time_signal(spec_re, spec_im):
    seq_parts = lax.axis_size("seq")
    row_count = spec_re.shape[1]
    period = 2 * seq_parts * row_count
    inner_cos, inner_sin = phase_pair(row_count, row_count, row_count, 0, 0)
    back_re = contract("md,cdk->cmk", inner_cos, spec_re) - contract(
        "md,cdk->cmk", inner_sin, spec_im
    )
    back_im = contract("md,cdk->cmk", inner_cos, spec_im) + contract(
        "md,cdk->cmk", inner_sin, spec_re
    )
    twist_cos, twist_sin = phase_pair(2, row_count, period, 2 * lax.axis_index("seq"), 0)
    twist_cos = twist_cos[:, :, None]
    twist_sin = twist_sin[:, :, None]
    turned_re = back_re * twist_cos - back_im * twist_sin
    turned_im = back_im * twist_cos + back_re * twist_sin
    outer_cos, outer_sin = phase_pair(seq_parts, 2 * seq_parts, 2 * seq_parts, 0, 0)
    piece_re = lax.all_to_all(turned_re, "seq", split_axis=1, concat_axis=0, tiled=True)
    piece_im = lax.all_to_all(turned_im, "seq", split_axis=1, concat_axis=0, tiled=True)
    summed = contract("pc,crk->prk", outer_cos, piece_re) - contract(
        "pc,crk->prk", outer_sin, piece_im
    )
    returned = summed * (1.0 / period)
    return lax.all_to_all(returned, "seq", split_axis=0, concat_axis=1, tiled=True)[0]


def spread_layer(qkv, filt, skip_gain, short_weight, w_out, g_out):
    row_count = qkv.shape[1]
    slab_width = qkv.shape[2]
    tail_rows = passed_along(qkv[:, row_count - 2 :, :], "seq", 1)
    extended = jnp.concatenate([tail_rows, qkv], axis=1)
    short = (
        short_weight[:, 0, None, :] * extended[:, 2:, :]
        + short_weight[:, 1, None, :] * extended[:, 1:-1, :]
        + short_weight[:, 2, None, :] * extended[:, :-2, :]
    )
    query_gate = short[0]
    key_short = short[1]
    value_short = short[2]
    mixed = key_short * value_short
    both_re, both_im = forward_spectrum(jnp.concatenate([mixed, filt], axis=1))
    signal_re = both_re[:, :, :slab_width]
    signal_im = both_im[:, :, :slab_width]
    kernel_re = both_re[:, :, slab_width:]
    kernel_im = both_im[:, :, slab_width:]
    conv_out = time_signal(
        signal_re * kernel_re - signal_im * kernel_im, signal_re * kernel_im + signal_im * kernel_re
    )
    long_out = conv_out + skip_gain * mixed
    gated_out = (query_gate * long_out).astype(jnp.bfloat16)
    projected = jnp.dot(
        lax.all_gather(gated_out, "ch", axis=1, tiled=True),
        w_out,
        preferred_element_type=jnp.float32,
    )
    output = projected.astype(jnp.bfloat16)
    grad_all = lax.all_gather(g_out, "ch", axis=1, tiled=True)
    rows_all = lax.all_to_all(w_out, "ch", split_axis=0, concat_axis=1, tiled=True)
    grad_gated = lax.dot_general(
        grad_all, rows_all, (((1,), (1,)), ((), ())), preferred_element_type=jnp.float32
    )
    grad_long = grad_gated * query_gate
    grad_query = grad_gated * long_out
    grad_re, grad_im = forward_spectrum(grad_long)
    pair_re = jnp.concatenate(
        [kernel_re * grad_re + kernel_im * grad_im, signal_re * grad_re + signal_im * grad_im],
        axis=2,
    )
    pair_im = jnp.concatenate(
        [kernel_re * grad_im - kernel_im * grad_re, signal_re * grad_im - signal_im * grad_re],
        axis=2,
    )
    pair_time = time_signal(pair_re, pair_im)
    grad_mixed = pair_time[:, :slab_width] + skip_gain * grad_long
    token_total = lax.axis_size("seq") * row_count
    grad_filter = pair_time[:, slab_width:] * (1.0 / math.sqrt(token_total))
    grad_short = jnp.stack([grad_query, grad_mixed * value_short, grad_mixed * key_short])
    head_rows = passed_along(grad_short[:, :2, :], "seq", -1)
    extended_grad = jnp.concatenate([grad_short, head_rows], axis=1)
    grad_qkv = (
        short_weight[:, 0, None, :] * extended_grad[:, :-2, :]
        + short_weight[:, 1, None, :] * extended_grad[:, 1:-1, :]
        + short_weight[:, 2, None, :] * extended_grad[:, 2:, :]
    ).astype(jnp.bfloat16)
    return (output, grad_qkv, grad_filter)


def split_bf16(values):
    high = values.astype(np.float32).astype(jnp.bfloat16)
    low = (values - high.astype(np.float64)).astype(np.float32).astype(jnp.bfloat16)
    return high, low


def phase_tables(tokens):
    quarter = tokens // PHASES
    freq = 2 * np.arange(quarter)[:, None] + 1
    turn = math.pi / (2 * tokens)
    angle = (freq * PHASES * np.arange(quarter)[None, :] % (4 * tokens)) * turn
    forward = np.concatenate([np.cos(angle), -np.sin(angle)], axis=1)
    backward = np.concatenate([np.cos(angle).T, -np.sin(angle).T], axis=1) / tokens
    angle = freq * np.arange(PHASES)[None, :] * turn
    twist = np.concatenate([np.cos(angle), np.sin(angle)], axis=1)
    twist = np.pad(twist, ((0, 0), (0, LANES - 2 * PHASES)))
    high, rest = split_bf16(twist)
    last = split_bf16(twist - high.astype(np.float64) - rest.astype(np.float64))[0]
    tables = np.zeros((8, quarter, 2 * quarter), jnp.bfloat16)
    tables[0], tables[1] = split_bf16(forward)
    tables[2], tables[3] = split_bf16(backward)
    for i, term in enumerate((high, rest, last)):
        tables[4, :, i * LANES : (i + 1) * LANES] = term
    return tables


def row_order(rows):
    order = np.zeros((rows, rows), np.float32)
    share = rows // PHASES
    for phase in range(PHASES):
        for j in range(share):
            order[phase * share + j, PHASES * j + phase] = 1.0
    return order.astype(jnp.bfloat16)


def mm(a, b):
    return lax.dot_general(a, b, (((1,), (0,)), ((), ())), preferred_element_type=F32)


def low_lanes(shape):
    return lax.broadcasted_iota(jnp.int32, shape, 1) < HALF


def swap(x):
    return pltpu.roll(x, HALF, 1)


class Near:
    def __init__(self, array, kept=False):
        self.array = array
        self.kept = kept


class Far:
    def __init__(self, array, cuts=None, turned=0, into=None):
        self.array = array
        self.turned = turned
        self.into = into
        if turned:
            step = array.shape[0] // turned
            cuts = [(i * step, step) for i in range(turned)]
        self.cuts = cuts or [(0, array.shape[0])]
        self.rows = sum(count for _, count in self.cuts)


class Stage:
    def __init__(self, items, count_in, refs):
        arrays, scratch = list(refs[: len(items)]), list(refs[len(items) :])
        sems = scratch.pop()
        self.count_in = count_in
        self.held, self.copies, self.waiting = [], [], []
        used = 0
        for i, (item, array) in enumerate(zip(items, arrays)):
            group = []
            if isinstance(item, Near):
                self.held.append(array)
            else:
                held = scratch.pop(0) if item.into is None else arrays[count_in + item.into]
                self.held.append(held)
                at = 0
                for cut, (start, count) in enumerate(item.cuts):
                    there = held.at[pl.ds(at, count)]
                    at += count
                    if item.turned:
                        start = pl.multiple_of((lax.axis_index("ch") ^ cut) * count, count)
                    here = array.at[pl.ds(start, count)]
                    if i >= count_in:
                        here, there = there, here
                    group.append(pltpu.make_async_copy(here, there, sems.at[used]))
                    used += 1
            self.copies.append(group)
            self.waiting.append(set(range(len(group))))
        self.given = set()

    def bring(self, index):
        for copy in self.copies[index]:
            copy.start()

    def take(self, index, cut=None):
        for i in sorted(self.waiting[index]):
            if cut is None or cut == i:
                self.copies[index][i].wait()
                self.waiting[index].discard(i)
        return self.held[index]

    def out(self, index):
        return self.held[self.count_in + index]

    def give(self, index):
        if index not in self.given:
            self.bring(self.count_in + index)
            self.given.add(index)


def staged(kernel, items, count_in, *refs):
    stage = Stage(items, count_in, refs)
    for i in range(count_in):
        stage.bring(i)
    kernel(stage)
    for i in range(count_in):
        stage.take(i)
    for i in range(len(items) - count_in):
        stage.give(i)
    for i in range(len(items) - count_in):
        stage.take(count_in + i)


def in_hbm(x):
    return pltpu.with_memory_space_constraint(x, pltpu.HBM)


def result_of(x):
    make = pltpu.HBM if isinstance(x, Far) else pltpu.VMEM if x.kept else jax.ShapeDtypeStruct
    return make(x.array.shape, x.array.dtype)


def call(kernel, results, *args, flops=0):
    items = list(args) + list(results)
    specs, scratch, used = [], [], 0
    for item in items:
        near = isinstance(item, Near)
        specs.append(pl.BlockSpec(memory_space=pltpu.VMEM if near else pltpu.HBM))
        if not near:
            used += len(item.cuts)
            if item.into is None:
                scratch.append(pltpu.VMEM((item.rows, *item.array.shape[1:]), item.array.dtype))
    moved = sum(math.prod(x.array.shape) * x.array.dtype.itemsize for x in items)
    return pl.pallas_call(
        functools.partial(staged, kernel, items, len(args)),
        out_shape=[result_of(x) for x in results],
        in_specs=specs[: len(args)],
        out_specs=specs[len(args) :],
        scratch_shapes=scratch + [pltpu.SemaphoreType.DMA((max(used, 1),))],
        compiler_params=pltpu.CompilerParams(vmem_limit_bytes=VMEM_LIMIT),
        cost_estimate=pl.CostEstimate(flops=flops, bytes_accessed=moved, transcendentals=0),
    )(*[x.array if isinstance(x, Near) else in_hbm(x.array) for x in args])


def lane_tile(x, index):
    return x[:, index * LANES : (index + 1) * LANES]


def pair(first, second):
    low = low_lanes(first.shape)
    return jnp.where(low, first, swap(second)), jnp.where(low, swap(first), second)


def both(x):
    turned, low = swap(x), low_lanes(x.shape)
    return jnp.where(low, x, turned), jnp.where(low, turned, x)


def start_kernel(parts, stage):
    g = stage.take(0)[...]
    width = g.shape[1]
    for part in range(parts):
        w = stage.take(1, part)[part * width : (part + 1) * width, :]
        stage.out(part)[...] = lax.dot_general(
            g, w, (((1,), (1,)), ((), ())), preferred_element_type=F32
        ).astype(BF16)
        stage.give(part)
    send_ref = stage.out(parts)
    order = stage.take(2)[...]
    qkv_ref = stage.take(3)
    query, key, value = [mm(order, qkv_ref[i]) for i in range(3)]
    taps = mm(order, stage.take(4)[...].astype(BF16))
    rows = query.shape[0]
    for tile in range(width // LANES):
        for row, (x, y) in enumerate(((key, value), (query, taps))):
            here = slice(row * rows, (row + 1) * rows)
            x, y = pair(lane_tile(x, tile), lane_tile(y, tile))
            send_ref[2 * tile, here] = x.astype(BF16)
            send_ref[2 * tile + 1, here] = y.astype(BF16)


def sum_kernel(parts, stage):
    send_ref, order_ref = stage.out(0), stage.take(0)
    total = stage.take(1)[...].astype(F32)
    for part in range(1, parts):
        total = total + stage.take(1 + part)[...].astype(F32)
    total = mm(order_ref[...], total.astype(BF16))
    half = total.shape[0] // 2
    for tile in range(total.shape[1] // LANES):
        t = lane_tile(total, tile)
        x, y = pair(t[:half], t[half:])
        send_ref[2 * tile] = x.astype(BF16)
        send_ref[2 * tile + 1] = y.astype(BF16)


def spread_phases(parts):
    (a_re, a_im), (b_re, b_im), (c_re, c_im), (d_re, d_im) = parts
    s_re, s_im, t_re, t_im = a_re + c_re, a_im + c_im, a_re - c_re, a_im - c_im
    u_re, u_im, v_re, v_im = b_re + d_re, b_im + d_im, b_re - d_re, b_im - d_im
    return [
        (s_re + u_re, s_im + u_im),
        (t_re + v_im, t_im - v_re),
        (s_re - u_re, s_im - u_im),
        (t_re - v_im, t_im + v_re),
    ]


def gather_phases(parts):
    (a_re, a_im), (b_re, b_im), (c_re, c_im), (d_re, d_im) = parts
    s_re, s_im, t_re, t_im = a_re + c_re, a_im + c_im, a_re - c_re, a_im - c_im
    u_re, u_im, v_re, v_im = b_re + d_re, b_im + d_im, b_re - d_re, b_im - d_im
    return [
        (s_re + u_re, s_im + u_im),
        (t_re - v_im, t_im + v_re),
        (s_re - u_re, s_im - u_im),
        (t_re + v_im, t_im - v_re),
    ]


def rows_of(ref, start, count):
    block = ref[:, start : start + count, :]
    return block.reshape(ref.shape[0] * count, ref.shape[2])


def turned_back(re, im, twist, phase):
    if phase == 0:
        return re, im
    c, s = twist[:, phase : phase + 1], twist[:, PHASES + phase : PHASES + phase + 1]
    return re * c + im * s, im * c - re * s


def turned_on(re, im, twist, phase):
    if phase == 0:
        return re, im
    c, s = twist[:, phase : phase + 1], twist[:, PHASES + phase : PHASES + phase + 1]
    return re * c - im * s, re * s + im * c


def lane_tile(x, index):
    return x[:, index * LANES : (index + 1) * LANES]


def causal(parts, weight):
    rows = lax.broadcasted_iota(jnp.int32, parts[0].shape, 0)
    two, three = [jnp.where(rows == 0, 0.0, pltpu.roll(parts[p], 1, 0)) for p in (2, 3)]
    once, twice = [three, *parts[:3]], [two, three, *parts[:2]]
    return [
        weight[0:1] * x + weight[1:2] * y + weight[2:3] * z for x, y, z in zip(parts, once, twice)
    ]


def anticausal(parts, weight):
    count = parts[0].shape[0]
    rows = lax.broadcasted_iota(jnp.int32, parts[0].shape, 0)
    zero, one = [
        jnp.where(rows == count - 1, 0.0, pltpu.roll(parts[p], count - 1, 0)) for p in (0, 1)
    ]
    once, twice = [*parts[1:], zero], [*parts[2:], zero, one]
    return [
        weight[0:1] * x + weight[1:2] * y + weight[2:3] * z for x, y, z in zip(parts, once, twice)
    ]


def halves(x):
    high = x.astype(BF16)
    return high, (x - high.astype(F32)).astype(BF16)


def twiddles(table_ref):
    terms = [table_ref[2, :, i * LANES : (i + 1) * LANES].astype(F32) for i in range(3)]
    return terms[0] + (terms[1] + terms[2])


def transformed(parts, table_ref, twist):
    quarter = parts[0].shape[0]
    high, rest = halves(jnp.concatenate(parts, axis=1))
    sides = []
    for side in (slice(0, quarter), slice(quarter, 2 * quarter)):
        fh, fl = table_ref[0, :, side], table_ref[1, :, side]
        sides.append(mm(fh, high) + mm(fl, high) + mm(fh, rest))
    turned = []
    for phase in range(PHASES):
        re, im = [lane_tile(side, phase) for side in sides]
        turned.append(turned_back(re, im, twist, phase))
    return spread_phases(turned)


def in_time(spectrum, table_ref, twist):
    bh, bl = table_ref[0], table_ref[1]
    parts = []
    for phase, (re, im) in enumerate(gather_phases(spectrum)):
        parts.append(jnp.concatenate(turned_on(re, im, twist, phase), axis=0))
    high, rest = halves(jnp.concatenate(parts, axis=1))
    t = mm(bh, high) + mm(bl, high) + mm(bh, rest)
    return [lane_tile(t, phase) for phase in range(PHASES)]


def own_weights(weight_ref, gain_ref):
    place = lax.axis_index("seq")
    lanes = pl.ds(pl.multiple_of(place // 2 * LANES, LANES), LANES)
    odd = place % 2 == 1

    def mine(x):
        return jnp.where(odd, swap(x), x)

    weights = [mine(weight_ref[i, :, lanes]) for i in range(3)]
    gain = both(mine(gain_ref[:, lanes]))[0]
    low = low_lanes(weights[0].shape)
    only = (lax.broadcasted_iota(jnp.int32, weights[0].shape, 0) == 0).astype(F32)
    pair_weight = jnp.where(low, weights[1], swap(weights[2]))
    query_weight = jnp.where(low, weights[0], only)
    return pair_weight, query_weight, gain


def forward_kernel(stage):
    recv_ref, weight_ref, gain_ref = [stage.take(i) for i in range(3)]
    gated_ref, saved_ref = stage.out(0), stage.out(1)
    blocks = recv_ref.shape[0]
    rows = recv_ref.shape[1] // 2
    share = rows // PHASES
    quarter = blocks * share
    low = low_lanes((quarter, LANES))
    pair_weight, query_weight, gain = own_weights(weight_ref, gain_ref)

    starts = [phase * share for phase in range(PHASES)]
    pairs = causal([rows_of(recv_ref, at, share).astype(F32) for at in starts], pair_weight)
    gates = causal([rows_of(recv_ref, rows + at, share).astype(F32) for at in starts], query_weight)
    for phase in range(PHASES):
        saved_ref[8 + phase] = pairs[phase]
    mixed = [x * swap(x) for x in pairs]
    query = [both(x)[0] for x in gates]
    table_ref = stage.take(3)
    twist = twiddles(table_ref)
    spectrum = transformed([jnp.where(low, x, y) for x, y in zip(mixed, gates)], table_ref, twist)
    product = []
    for r, (re, im) in enumerate(spectrum):
        saved_ref[2 * r] = re
        saved_ref[2 * r + 1] = im
        other_re, other_im = swap(re), swap(im)
        product.append((re * other_re - im * other_im, re * other_im + im * other_re))
    stage.copies[stage.count_in + 1][0].start()
    conv = in_time(product, stage.take(4), twist)
    long_out = [x + gain * y for x, y in zip(conv, mixed)]
    gated = [x * y for x, y in zip(query, long_out)]
    for phase in range(PHASES // 2):
        t = jnp.where(low, gated[phase], gated[phase + 2]).astype(BF16)
        gated_ref[:, starts[phase] : starts[phase] + share, :] = t.reshape(blocks, share, LANES)
    for phase in range(PHASES):
        saved_ref[12 + phase] = jnp.where(low, query[phase], long_out[phase])
    stage.copies[stage.count_in + 1][1].start()
    stage.given.add(1)


def backward_kernel(stage):
    grad_ref, weight_ref, gain_ref, gates_ref = [stage.take(i) for i in range(4)]
    send_ref = stage.out(0)
    blocks = grad_ref.shape[0]
    share = grad_ref.shape[1] // 2
    rows = PHASES * share
    quarter = blocks * share
    low = low_lanes((quarter, LANES))
    pair_weight, query_weight, gain = own_weights(weight_ref, gain_ref)

    starts = [phase * share for phase in range(PHASES)]
    packed = [rows_of(grad_ref, at, share).astype(F32) for at in starts[:2]]
    grad_gated = [both(x)[i] for i in range(2) for x in packed]
    gates = [both(gates_ref[phase]) for phase in range(PHASES)]
    grad_long = [x * y for x, (y, _) in zip(grad_gated, gates)]
    grad_query = anticausal([x * y for x, (_, y) in zip(grad_gated, gates)], query_weight)
    table_ref = stage.take(4)
    twist = twiddles(table_ref)
    grad_spectrum = transformed(grad_long, table_ref, twist)
    saved_ref = stage.take(5)
    product = []
    for r, (re, im) in enumerate(grad_spectrum):
        k_re, k_im = saved_ref[2 * r], saved_ref[2 * r + 1]
        product.append((k_re * re + k_im * im, k_re * im - k_im * re))
    table_ref = stage.take(6)
    times = in_time(product, table_ref, twist)
    pairs_ref = stage.take(7)
    grad_mixed = [both(x + gain * y)[1] for x, y in zip(times, grad_long)]
    grad_pairs = anticausal(
        [x * swap(pairs_ref[phase]) for phase, x in enumerate(grad_mixed)], pair_weight
    )
    scale = 1.0 / math.sqrt(PHASES * quarter)
    for phase, at in enumerate(starts):
        x = grad_pairs[phase].astype(BF16)
        y = jnp.where(low, grad_query[phase], swap(times[phase]) * scale).astype(BF16)
        send_ref[:, at : at + share, :] = x.reshape(blocks, share, LANES)
        send_ref[:, rows + at : rows + at + share, :] = y.reshape(blocks, share, LANES)


def unpacked(blocks, order):
    half = blocks[0].shape[0]
    tiles = []
    for tile in range(len(blocks) // 2):
        top, bottom = pair(blocks[2 * tile].astype(F32), blocks[2 * tile + 1].astype(F32))
        tiles.append(jnp.concatenate([top, bottom], axis=0))
    return mm(order, jnp.concatenate(tiles, axis=1).astype(BF16))


def end_kernel(stage):
    recv_ref, order_ref = stage.take(0), stage.take(1)
    grad_ref, filter_ref = stage.out(0), stage.out(1)
    order = order_ref[...]
    blocks = recv_ref.shape[0]
    rows = recv_ref.shape[1] // 2
    sides = []
    for at in (0, rows):
        firsts, seconds = [], []
        for tile in range(blocks // 2):
            x, y = [recv_ref[2 * tile + i, at : at + rows].astype(F32) for i in range(2)]
            first, second = pair(x, y)
            firsts.append(first)
            seconds.append(second)
        for side in (firsts, seconds):
            sides.append(mm(order, jnp.concatenate(side, axis=1).astype(BF16)))
    key, value, query, taps = sides
    filter_ref[...] = taps
    stage.give(1)
    grad_ref[0] = query.astype(BF16)
    grad_ref[1] = key.astype(BF16)
    grad_ref[2] = value.astype(BF16)


def output_kernel(parts, stage):
    order, w_ref = stage.take(0)[...], stage.take(1)
    total = None
    for part in range(parts):
        gated_ref = stage.take(2 + part)
        block = unpacked([gated_ref[i] for i in range(gated_ref.shape[0])], order).astype(BF16)
        width = block.shape[1]
        term = mm(block, w_ref[part * width : (part + 1) * width, :])
        total = term if total is None else total + term
    stage.out(0)[...] = total.astype(BF16)


def partner(x, axis, mask):
    return lax.ppermute(x, axis, [(i, i ^ mask) for i in range(lax.axis_size(axis))])


def exchanged(x, axis):
    return lax.all_to_all(x, axis, split_axis=0, concat_axis=0, tiled=True)


def owner_layer(qkv, filt, skip_gain, short_weight, w_out, g_out):
    shape = jax.ShapeDtypeStruct
    seq_parts, ch_parts = lax.axis_size("seq"), lax.axis_size("ch")
    rows, width = qkv.shape[1], qkv.shape[2]
    tokens = seq_parts * rows
    quarter = tokens // PHASES
    order = row_order(rows)
    tables = jnp.asarray(phase_tables(tokens))
    tables_on, tables_back = Far(tables, [(0, 2), (4, 1)]), Far(tables, [(2, 2)])
    table_flops = 2 * 2 * 2 * 3 * tokens * tokens // PHASES * LANES
    product_flops = 2 * rows * width * width * ch_parts
    packed = shape((seq_parts, rows // 2, LANES), BF16)
    double = shape((seq_parts, 2 * rows, LANES), BF16)
    column = shape((rows, width), BF16)
    saved = shape((4 * PHASES, quarter, LANES), F32)
    weight, gain = Far(short_weight), Far(skip_gain[None, :])

    *partial, send, w_kept = call(
        functools.partial(start_kernel, ch_parts),
        [Far(column)] * ch_parts + [Far(double), Near(w_out, kept=True)],
        Far(g_out),
        Far(w_out, turned=ch_parts, into=ch_parts + 1),
        Far(order),
        Far(qkv),
        Far(filt),
        flops=product_flops,
    )
    recv = exchanged(send, "seq")
    partial = [partner(x, "ch", mask) if mask else x for mask, x in enumerate(partial)]
    (send,) = call(
        functools.partial(sum_kernel, ch_parts),
        [Far(packed)],
        Far(order),
        Far(partial[0]),
        *[Near(x) for x in partial[1:]],
    )
    grad_recv = exchanged(send, "seq")
    send, kept = call(
        forward_kernel,
        [Far(packed), Far(saved, [(0, 12), (12, 4)])],
        Near(recv),
        weight,
        gain,
        tables_on,
        tables_back,
        flops=table_flops,
    )
    gated = exchanged(send, "seq")
    (send,) = call(
        backward_kernel,
        [Far(double)],
        Far(grad_recv),
        weight,
        gain,
        Far(kept, [(12, 4)]),
        tables_on,
        Far(kept, [(0, 8)]),
        tables_back,
        Far(kept, [(8, 4)]),
        flops=table_flops,
    )
    grad_recv = exchanged(send, "seq")
    across = partner(gated, "ch", 2)
    near, far = partner(gated, "ch", 1), partner(across, "ch", 1)
    back_order = Far(order.T)
    (output,) = call(
        functools.partial(output_kernel, ch_parts),
        [Far(column)],
        back_order,
        Near(w_kept),
        Far(gated),
        Near(near),
        Near(across),
        Near(far),
        flops=product_flops,
    )
    grad_qkv, grad_filter = call(
        end_kernel,
        [Far(shape((3, rows, width), BF16)), Far(shape((rows, width), F32))],
        Near(grad_recv),
        back_order,
    )
    return (output, grad_qkv, grad_filter)


def local(qkv, filt, skip_gain, short_weight, w_out, g_out):
    seq_parts = lax.axis_size("seq")
    rows, width = qkv.shape[1], qkv.shape[2]
    fits = width == HALF * seq_parts and rows % HALF == 0 and rows * seq_parts <= 2048
    if fits and lax.axis_size("ch") == 4:
        return owner_layer(qkv, filt, skip_gain, short_weight, w_out, g_out)
    return spread_layer(qkv, filt, skip_gain, short_weight, w_out, g_out)


def solution(mesh):
    in_specs = (
        P(None, "seq", "ch"),
        P("seq", "ch"),
        P("ch"),
        P(None, None, "ch"),
        P(None, "ch"),
        P("seq", "ch"),
    )
    out_specs = (P("seq", "ch"), P(None, "seq", "ch"), P("seq", "ch"))
    return jax.shard_map(local, mesh=mesh, in_specs=in_specs, out_specs=out_specs, check_vma=False)
```

```python
import functools
import math

import jax
import jax.numpy as jnp
import numpy as np
from jax import lax
from jax.experimental import pallas as pl
from jax.experimental.pallas import tpu as pltpu
from jax.sharding import PartitionSpec as P

HIGHEST = lax.Precision.HIGHEST
TWO_PI = 2.0 * math.pi
LANES = 128
HALF = 64
PHASES = 4
BF16 = jnp.bfloat16
F32 = jnp.float32
VMEM_LIMIT = 24 * 1024 * 1024


def passed_along(block, axis, distance):
    devices = range(lax.axis_size(axis))
    route = [(i - distance, i) for i in devices if i - distance in devices]
    return lax.ppermute(block, axis, route)


def phase_pair(left_count, right_count, period, left_start, right_start):
    left_idx = lax.broadcasted_iota(jnp.int32, (left_count, right_count), 0) + left_start
    right_idx = lax.broadcasted_iota(jnp.int32, (left_count, right_count), 1) + right_start
    angle_all = (left_idx * right_idx % period).astype(jnp.float32) * (TWO_PI / period)
    return (jnp.cos(angle_all), jnp.sin(angle_all))


def contract(pattern, matrix, values):
    return jnp.einsum(
        pattern, matrix, values, precision=HIGHEST, preferred_element_type=jnp.float32
    )


def forward_spectrum(signal):
    seq_parts = lax.axis_size("seq")
    row_count = signal.shape[0]
    row_share = row_count // seq_parts
    period = 2 * seq_parts * row_count
    spread_in = lax.all_to_all(signal[None], "seq", split_axis=1, concat_axis=0, tiled=True)
    outer_cos, outer_sin = phase_pair(2 * seq_parts, seq_parts, 2 * seq_parts, 0, 0)
    section_re = contract("cp,prw->crw", outer_cos, spread_in)
    section_im = -contract("cp,prw->crw", outer_sin, spread_in)
    twist_cos, twist_sin = phase_pair(
        2 * seq_parts, row_share, period, 0, lax.axis_index("seq") * row_share
    )
    twist_cos = twist_cos[:, :, None]
    twist_sin = twist_sin[:, :, None]
    turned_re = section_re * twist_cos + section_im * twist_sin
    turned_im = section_im * twist_cos - section_re * twist_sin
    inner_cos, inner_sin = phase_pair(row_count, row_count, row_count, 0, 0)
    piece_re = lax.all_to_all(turned_re, "seq", split_axis=0, concat_axis=1, tiled=True)
    piece_im = lax.all_to_all(turned_im, "seq", split_axis=0, concat_axis=1, tiled=True)
    spec_re = contract("dm,cmk->cdk", inner_cos, piece_re) + contract(
        "dm,cmk->cdk", inner_sin, piece_im
    )
    spec_im = contract("dm,cmk->cdk", inner_cos, piece_im) - contract(
        "dm,cmk->cdk", inner_sin, piece_re
    )
    return (spec_re, spec_im)


def time_signal(spec_re, spec_im):
    seq_parts = lax.axis_size("seq")
    row_count = spec_re.shape[1]
    period = 2 * seq_parts * row_count
    inner_cos, inner_sin = phase_pair(row_count, row_count, row_count, 0, 0)
    back_re = contract("md,cdk->cmk", inner_cos, spec_re) - contract(
        "md,cdk->cmk", inner_sin, spec_im
    )
    back_im = contract("md,cdk->cmk", inner_cos, spec_im) + contract(
        "md,cdk->cmk", inner_sin, spec_re
    )
    twist_cos, twist_sin = phase_pair(2, row_count, period, 2 * lax.axis_index("seq"), 0)
    twist_cos = twist_cos[:, :, None]
    twist_sin = twist_sin[:, :, None]
    turned_re = back_re * twist_cos - back_im * twist_sin
    turned_im = back_im * twist_cos + back_re * twist_sin
    outer_cos, outer_sin = phase_pair(seq_parts, 2 * seq_parts, 2 * seq_parts, 0, 0)
    piece_re = lax.all_to_all(turned_re, "seq", split_axis=1, concat_axis=0, tiled=True)
    piece_im = lax.all_to_all(turned_im, "seq", split_axis=1, concat_axis=0, tiled=True)
    summed = contract("pc,crk->prk", outer_cos, piece_re) - contract(
        "pc,crk->prk", outer_sin, piece_im
    )
    returned = summed * (1.0 / period)
    return lax.all_to_all(returned, "seq", split_axis=0, concat_axis=1, tiled=True)[0]


def spread_layer(qkv, filt, skip_gain, short_weight, w_out, g_out):
    row_count = qkv.shape[1]
    slab_width = qkv.shape[2]
    tail_rows = passed_along(qkv[:, row_count - 2 :, :], "seq", 1)
    extended = jnp.concatenate([tail_rows, qkv], axis=1)
    short = (
        short_weight[:, 0, None, :] * extended[:, 2:, :]
        + short_weight[:, 1, None, :] * extended[:, 1:-1, :]
        + short_weight[:, 2, None, :] * extended[:, :-2, :]
    )
    query_gate = short[0]
    key_short = short[1]
    value_short = short[2]
    mixed = key_short * value_short
    both_re, both_im = forward_spectrum(jnp.concatenate([mixed, filt], axis=1))
    signal_re = both_re[:, :, :slab_width]
    signal_im = both_im[:, :, :slab_width]
    kernel_re = both_re[:, :, slab_width:]
    kernel_im = both_im[:, :, slab_width:]
    conv_out = time_signal(
        signal_re * kernel_re - signal_im * kernel_im, signal_re * kernel_im + signal_im * kernel_re
    )
    long_out = conv_out + skip_gain * mixed
    gated_out = (query_gate * long_out).astype(jnp.bfloat16)
    projected = jnp.dot(
        lax.all_gather(gated_out, "ch", axis=1, tiled=True),
        w_out,
        preferred_element_type=jnp.float32,
    )
    output = projected.astype(jnp.bfloat16)
    grad_all = lax.all_gather(g_out, "ch", axis=1, tiled=True)
    rows_all = lax.all_to_all(w_out, "ch", split_axis=0, concat_axis=1, tiled=True)
    grad_gated = lax.dot_general(
        grad_all, rows_all, (((1,), (1,)), ((), ())), preferred_element_type=jnp.float32
    )
    grad_long = grad_gated * query_gate
    grad_query = grad_gated * long_out
    grad_re, grad_im = forward_spectrum(grad_long)
    pair_re = jnp.concatenate(
        [kernel_re * grad_re + kernel_im * grad_im, signal_re * grad_re + signal_im * grad_im],
        axis=2,
    )
    pair_im = jnp.concatenate(
        [kernel_re * grad_im - kernel_im * grad_re, signal_re * grad_im - signal_im * grad_re],
        axis=2,
    )
    pair_time = time_signal(pair_re, pair_im)
    grad_mixed = pair_time[:, :slab_width] + skip_gain * grad_long
    token_total = lax.axis_size("seq") * row_count
    grad_filter = pair_time[:, slab_width:] * (1.0 / math.sqrt(token_total))
    grad_short = jnp.stack([grad_query, grad_mixed * value_short, grad_mixed * key_short])
    head_rows = passed_along(grad_short[:, :2, :], "seq", -1)
    extended_grad = jnp.concatenate([grad_short, head_rows], axis=1)
    grad_qkv = (
        short_weight[:, 0, None, :] * extended_grad[:, :-2, :]
        + short_weight[:, 1, None, :] * extended_grad[:, 1:-1, :]
        + short_weight[:, 2, None, :] * extended_grad[:, 2:, :]
    ).astype(jnp.bfloat16)
    return (output, grad_qkv, grad_filter)


def split_bf16(values):
    high = values.astype(np.float32).astype(jnp.bfloat16)
    low = (values - high.astype(np.float64)).astype(np.float32).astype(jnp.bfloat16)
    return high, low


def phase_tables(tokens):
    quarter = tokens // PHASES
    freq = 2 * np.arange(quarter)[:, None] + 1
    turn = math.pi / (2 * tokens)
    angle = (freq * PHASES * np.arange(quarter)[None, :] % (4 * tokens)) * turn
    forward = np.concatenate([np.cos(angle), -np.sin(angle)], axis=1)
    backward = np.concatenate([np.cos(angle).T, -np.sin(angle).T], axis=1) / tokens
    angle = freq * np.arange(PHASES)[None, :] * turn
    twist = np.concatenate([np.cos(angle), np.sin(angle)], axis=1)
    twist = np.pad(twist, ((0, 0), (0, LANES - 2 * PHASES)))
    high, rest = split_bf16(twist)
    last = split_bf16(twist - high.astype(np.float64) - rest.astype(np.float64))[0]
    tables = np.zeros((8, quarter, 2 * quarter), jnp.bfloat16)
    tables[0], tables[1] = split_bf16(forward)
    tables[2], tables[3] = split_bf16(backward)
    for i, term in enumerate((high, rest, last)):
        tables[4, :, i * LANES : (i + 1) * LANES] = term
    return tables


def row_order(rows):
    order = np.zeros((rows, rows), np.float32)
    share = rows // PHASES
    for phase in range(PHASES):
        for j in range(share):
            order[phase * share + j, PHASES * j + phase] = 1.0
    return order.astype(jnp.bfloat16)


def mm(a, b):
    return lax.dot_general(a, b, (((1,), (0,)), ((), ())), preferred_element_type=F32)


def low_lanes(shape):
    return lax.broadcasted_iota(jnp.int32, shape, 1) < HALF


def swap(x):
    return pltpu.roll(x, HALF, 1)


class Near:
    def __init__(self, array, kept=False):
        self.array = array
        self.kept = kept


class Far:
    def __init__(self, array, cuts=None, turned=0, into=None):
        self.array = array
        self.turned = turned
        self.into = into
        if turned:
            step = array.shape[0] // turned
            cuts = [(i * step, step) for i in range(turned)]
        self.cuts = cuts or [(0, array.shape[0])]
        self.rows = sum(count for _, count in self.cuts)


class Stage:
    def __init__(self, items, count_in, refs):
        arrays, scratch = list(refs[: len(items)]), list(refs[len(items) :])
        sems = scratch.pop()
        self.count_in = count_in
        self.held, self.copies, self.waiting = [], [], []
        used = 0
        for i, (item, array) in enumerate(zip(items, arrays)):
            group = []
            if isinstance(item, Near):
                self.held.append(array)
            else:
                held = scratch.pop(0) if item.into is None else arrays[count_in + item.into]
                self.held.append(held)
                at = 0
                for cut, (start, count) in enumerate(item.cuts):
                    there = held.at[pl.ds(at, count)]
                    at += count
                    if item.turned:
                        start = pl.multiple_of((lax.axis_index("ch") ^ cut) * count, count)
                    here = array.at[pl.ds(start, count)]
                    if i >= count_in:
                        here, there = there, here
                    group.append(pltpu.make_async_copy(here, there, sems.at[used]))
                    used += 1
            self.copies.append(group)
            self.waiting.append(set(range(len(group))))
        self.given = set()

    def bring(self, index):
        for copy in self.copies[index]:
            copy.start()

    def take(self, index, cut=None):
        for i in sorted(self.waiting[index]):
            if cut is None or cut == i:
                self.copies[index][i].wait()
                self.waiting[index].discard(i)
        return self.held[index]

    def out(self, index):
        return self.held[self.count_in + index]

    def give(self, index):
        if index not in self.given:
            self.bring(self.count_in + index)
            self.given.add(index)


def staged(kernel, items, count_in, *refs):
    stage = Stage(items, count_in, refs)
    for i in range(count_in):
        stage.bring(i)
    kernel(stage)
    for i in range(count_in):
        stage.take(i)
    for i in range(len(items) - count_in):
        stage.give(i)
    for i in range(len(items) - count_in):
        stage.take(count_in + i)


def in_hbm(x):
    return pltpu.with_memory_space_constraint(x, pltpu.HBM)


def result_of(x):
    make = pltpu.HBM if isinstance(x, Far) else pltpu.VMEM if x.kept else jax.ShapeDtypeStruct
    return make(x.array.shape, x.array.dtype)


def call(kernel, results, *args, flops=0):
    items = list(args) + list(results)
    specs, scratch, used = [], [], 0
    for item in items:
        near = isinstance(item, Near)
        specs.append(pl.BlockSpec(memory_space=pltpu.VMEM if near else pltpu.HBM))
        if not near:
            used += len(item.cuts)
            if item.into is None:
                scratch.append(pltpu.VMEM((item.rows, *item.array.shape[1:]), item.array.dtype))
    moved = sum(math.prod(x.array.shape) * x.array.dtype.itemsize for x in items)
    return pl.pallas_call(
        functools.partial(staged, kernel, items, len(args)),
        out_shape=[result_of(x) for x in results],
        in_specs=specs[: len(args)],
        out_specs=specs[len(args) :],
        scratch_shapes=scratch + [pltpu.SemaphoreType.DMA((max(used, 1),))],
        compiler_params=pltpu.CompilerParams(vmem_limit_bytes=VMEM_LIMIT),
        cost_estimate=pl.CostEstimate(flops=flops, bytes_accessed=moved, transcendentals=0),
    )(*[x.array if isinstance(x, Near) else in_hbm(x.array) for x in args])


def lane_tile(x, index):
    return x[:, index * LANES : (index + 1) * LANES]


def pair(first, second):
    low = low_lanes(first.shape)
    return jnp.where(low, first, swap(second)), jnp.where(low, swap(first), second)


def both(x):
    turned, low = swap(x), low_lanes(x.shape)
    return jnp.where(low, x, turned), jnp.where(low, turned, x)


def shifted(x, before):
    rows = lax.broadcasted_iota(jnp.int32, x.shape, 0)
    last, first = before[1:2, :], before[0:1, :]
    one = jnp.where(rows == 0, last, pltpu.roll(x, 1, 0))
    two = jnp.where(rows == 0, first, jnp.where(rows == 1, last, pltpu.roll(x, 2, 0)))
    return one, two


def advanced(x, after):
    count = x.shape[0]
    rows = lax.broadcasted_iota(jnp.int32, x.shape, 0)
    first, last = after[0:1, :], after[1:2, :]
    one = jnp.where(rows == count - 1, first, pltpu.roll(x, count - 1, 0))
    two = jnp.where(
        rows == count - 1, last, jnp.where(rows == count - 2, first, pltpu.roll(x, count - 2, 0))
    )
    return one, two


def packed_rows(x, send_ref, at):
    half = x.shape[0] // 2
    for tile in range(x.shape[1] // LANES):
        t = lane_tile(x, tile)
        first, second = pair(t[:half], t[half:])
        send_ref[2 * tile, at : at + half] = first.astype(BF16)
        send_ref[2 * tile + 1, at : at + half] = second.astype(BF16)


def start_kernel(stage):
    send_ref, tail_ref = stage.out(0), stage.out(1)
    qkv_ref, order = stage.take(0), stage.take(1)[...]
    rows = qkv_ref.shape[1]
    tail_ref[...] = qkv_ref[0, rows - tail_ref.shape[0] :, :]
    stage.give(1)
    key, value = mm(order, qkv_ref[1]), mm(order, qkv_ref[2])
    for tile in range(key.shape[1] // LANES):
        x, y = pair(lane_tile(key, tile), lane_tile(value, tile))
        send_ref[2 * tile, :rows] = x.astype(BF16)
        send_ref[2 * tile + 1, :rows] = y.astype(BF16)
    taps = mm(order, stage.take(2)[...].astype(BF16))
    packed_rows(taps, send_ref, rows)


def partial_product(g, w_ref, mask):
    width = g.shape[1]
    block = lax.axis_index("ch") ^ mask
    w = w_ref[pl.ds(pl.multiple_of(block * width, width), width), :]
    return lax.dot_general(g, w, (((1,), (1,)), ((), ())), preferred_element_type=F32)


def first_product_kernel(stage):
    w_ref, g, out_ref = stage.take(1), stage.take(0)[...], stage.out(0)
    for i, mask in enumerate((1, 3)):
        out_ref[i] = partial_product(g, w_ref, mask).astype(BF16)


def second_product_kernel(stage):
    w_ref, g, near_ref = stage.take(1), stage.take(0)[...], stage.take(2)
    across_ref, own_ref = stage.out(0), stage.out(1)
    across = partial_product(g, w_ref, 2) + near_ref[1].astype(F32)
    across_ref[...] = across.astype(BF16)
    stage.give(0)
    own_ref[...] = partial_product(g, w_ref, 0) + near_ref[0].astype(F32)


def sum_kernel(stage):
    q_ref, weight_ref, tail_ref = [stage.take(i) for i in range(3)]
    send_ref, kept_ref = stage.out(0), stage.out(1)
    q = q_ref[0].astype(F32)
    last = tail_ref.shape[0] - 2
    one, two = shifted(q, tail_ref[...].astype(F32)[last:])
    query = weight_ref[0, 0:1, :] * q + weight_ref[0, 1:2, :] * one + weight_ref[0, 2:3, :] * two
    grad_gated = stage.take(3)[...] + stage.take(4)[...].astype(F32)
    kept_ref[0] = query
    kept_ref[1] = grad_gated
    stage.give(1)
    packed_rows(mm(stage.take(5)[...], (grad_gated * query).astype(BF16)), send_ref, 0)


def spread_phases(parts):
    (a_re, a_im), (b_re, b_im), (c_re, c_im), (d_re, d_im) = parts
    s_re, s_im, t_re, t_im = a_re + c_re, a_im + c_im, a_re - c_re, a_im - c_im
    u_re, u_im, v_re, v_im = b_re + d_re, b_im + d_im, b_re - d_re, b_im - d_im
    return [
        (s_re + u_re, s_im + u_im),
        (t_re + v_im, t_im - v_re),
        (s_re - u_re, s_im - u_im),
        (t_re - v_im, t_im + v_re),
    ]


def gather_phases(parts):
    (a_re, a_im), (b_re, b_im), (c_re, c_im), (d_re, d_im) = parts
    s_re, s_im, t_re, t_im = a_re + c_re, a_im + c_im, a_re - c_re, a_im - c_im
    u_re, u_im, v_re, v_im = b_re + d_re, b_im + d_im, b_re - d_re, b_im - d_im
    return [
        (s_re + u_re, s_im + u_im),
        (t_re - v_im, t_im + v_re),
        (s_re - u_re, s_im - u_im),
        (t_re + v_im, t_im - v_re),
    ]


def rows_of(ref, start, count):
    block = ref[:, start : start + count, :]
    return block.reshape(ref.shape[0] * count, ref.shape[2])


def turned_back(re, im, twist, phase):
    if phase == 0:
        return re, im
    c, s = twist[:, phase : phase + 1], twist[:, PHASES + phase : PHASES + phase + 1]
    return re * c + im * s, im * c - re * s


def turned_on(re, im, twist, phase):
    if phase == 0:
        return re, im
    c, s = twist[:, phase : phase + 1], twist[:, PHASES + phase : PHASES + phase + 1]
    return re * c - im * s, re * s + im * c


def lane_tile(x, index):
    return x[:, index * LANES : (index + 1) * LANES]


def causal(parts, weight):
    rows = lax.broadcasted_iota(jnp.int32, parts[0].shape, 0)
    two, three = [jnp.where(rows == 0, 0.0, pltpu.roll(parts[p], 1, 0)) for p in (2, 3)]
    once, twice = [three, *parts[:3]], [two, three, *parts[:2]]
    return [
        weight[0:1] * x + weight[1:2] * y + weight[2:3] * z for x, y, z in zip(parts, once, twice)
    ]


def anticausal(parts, weight):
    count = parts[0].shape[0]
    rows = lax.broadcasted_iota(jnp.int32, parts[0].shape, 0)
    zero, one = [
        jnp.where(rows == count - 1, 0.0, pltpu.roll(parts[p], count - 1, 0)) for p in (0, 1)
    ]
    once, twice = [*parts[1:], zero], [*parts[2:], zero, one]
    return [
        weight[0:1] * x + weight[1:2] * y + weight[2:3] * z for x, y, z in zip(parts, once, twice)
    ]


def halves(x):
    high = x.astype(BF16)
    return high, (x - high.astype(F32)).astype(BF16)


def twiddles(table_ref):
    terms = [table_ref[2, :, i * LANES : (i + 1) * LANES].astype(F32) for i in range(3)]
    return terms[0] + (terms[1] + terms[2])


def transformed(parts, table_ref, twist):
    quarter = parts[0].shape[0]
    high, rest = halves(jnp.concatenate(parts, axis=1))
    sides = []
    for side in (slice(0, quarter), slice(quarter, 2 * quarter)):
        fh, fl = table_ref[0, :, side], table_ref[1, :, side]
        sides.append(mm(fh, high) + mm(fl, high) + mm(fh, rest))
    turned = []
    for phase in range(PHASES):
        re, im = [lane_tile(side, phase) for side in sides]
        turned.append(turned_back(re, im, twist, phase))
    return spread_phases(turned)


def in_time(spectrum, table_ref, twist):
    bh, bl = table_ref[0], table_ref[1]
    parts = []
    for phase, (re, im) in enumerate(gather_phases(spectrum)):
        parts.append(jnp.concatenate(turned_on(re, im, twist, phase), axis=0))
    high, rest = halves(jnp.concatenate(parts, axis=1))
    t = mm(bh, high) + mm(bl, high) + mm(bh, rest)
    return [lane_tile(t, phase) for phase in range(PHASES)]


def own_weights(weight_ref, gain_ref):
    place = lax.axis_index("seq")
    lanes = pl.ds(pl.multiple_of(place // 2 * LANES, LANES), LANES)
    odd = place % 2 == 1

    def mine(x):
        return jnp.where(odd, swap(x), x)

    key, value = [mine(weight_ref[i, :, lanes]) for i in (1, 2)]
    gain = both(mine(gain_ref[:, lanes]))[0]
    return jnp.where(low_lanes(key.shape), key, swap(value)), gain


def whole_phases(ref, at, share):
    packed = [rows_of(ref, at + i * share, share).astype(F32) for i in range(2)]
    return [both(x)[i] for i in range(2) for x in packed]


def put_packed(parts, ref, at):
    blocks = ref.shape[0]
    share = parts[0].shape[0] // blocks
    low = low_lanes(parts[0].shape)
    for i in range(2):
        t = jnp.where(low, parts[i], parts[i + 2]).astype(BF16)
        ref[:, at + i * share : at + (i + 1) * share, :] = t.reshape(blocks, share, LANES)


def forward_kernel(stage):
    recv_ref, weight_ref, gain_ref = [stage.take(i) for i in range(3)]
    long_ref, saved_ref = stage.out(0), stage.out(1)
    rows = recv_ref.shape[1] * 2 // 3
    share = rows // PHASES
    weight, gain = own_weights(weight_ref, gain_ref)
    starts = [phase * share for phase in range(PHASES)]
    pairs = causal([rows_of(recv_ref, at, share).astype(F32) for at in starts], weight)
    for phase in range(PHASES):
        saved_ref[8 + phase] = pairs[phase]
    mixed = [x * swap(x) for x in pairs]
    taps = whole_phases(recv_ref, rows, share)
    low = low_lanes(taps[0].shape)
    table_ref = stage.take(3)
    twist = twiddles(table_ref)
    spectrum = transformed([jnp.where(low, x, y) for x, y in zip(mixed, taps)], table_ref, twist)
    product = []
    for r, (re, im) in enumerate(spectrum):
        saved_ref[2 * r] = re
        saved_ref[2 * r + 1] = im
        other_re, other_im = swap(re), swap(im)
        product.append((re * other_re - im * other_im, re * other_im + im * other_re))
    stage.give(1)
    conv = in_time(product, stage.take(4), twist)
    put_packed([x + gain * y for x, y in zip(conv, mixed)], long_ref, 0)


def backward_kernel(stage):
    grad_ref, weight_ref, gain_ref = [stage.take(i) for i in range(3)]
    send_ref = stage.out(0)
    blocks, half = grad_ref.shape[0], grad_ref.shape[1]
    rows = 2 * half
    share = rows // PHASES
    weight, gain = own_weights(weight_ref, gain_ref)
    grad_long = whole_phases(grad_ref, 0, share)
    table_ref = stage.take(3)
    twist = twiddles(table_ref)
    grad_spectrum = transformed(grad_long, table_ref, twist)
    saved_ref = stage.take(4)
    product = []
    for r, (re, im) in enumerate(grad_spectrum):
        k_re, k_im = saved_ref[2 * r], saved_ref[2 * r + 1]
        product.append((k_re * re + k_im * im, k_re * im - k_im * re))
    times = in_time(product, stage.take(5), twist)
    scale = 1.0 / math.sqrt(blocks * rows)
    put_packed([both(x)[0] * scale for x in times], send_ref, rows)
    pairs_ref = stage.take(6)
    grad_mixed = [both(x + gain * y)[1] for x, y in zip(times, grad_long)]
    grad_pairs = anticausal(
        [x * swap(pairs_ref[phase]) for phase, x in enumerate(grad_mixed)], weight
    )
    for phase, x in enumerate(grad_pairs):
        send_ref[:, phase * share : (phase + 1) * share, :] = x.astype(BF16).reshape(
            blocks, share, LANES
        )


def unpacked(ref, at, half, order):
    tiles = []
    for tile in range(ref.shape[0] // 2):
        x, y = [ref[2 * tile + i, at : at + half].astype(F32) for i in range(2)]
        top, bottom = pair(x, y)
        tiles.append(jnp.concatenate([top, bottom], axis=0))
    return mm(order, jnp.concatenate(tiles, axis=1).astype(BF16))


def gate_kernel(stage):
    long_out = unpacked(stage.take(0), 0, stage.take(0).shape[1], stage.take(1)[...])
    gated_ref, query_ref, head_ref = [stage.out(i) for i in range(3)]
    kept_ref = stage.take(2)
    gated_ref[...] = (kept_ref[0] * long_out).astype(BF16)
    stage.give(0)
    grad_query = kept_ref[1] * long_out
    query_ref[...] = grad_query
    head_ref[...] = grad_query[: head_ref.shape[0]]


def output_kernel(parts, stage):
    w_ref, total = stage.take(0), None
    for mask in range(parts):
        gated = stage.take(1 + mask)[...]
        width = gated.shape[1]
        block = lax.axis_index("ch") ^ mask
        term = mm(gated, w_ref[pl.ds(pl.multiple_of(block * width, width), width), :])
        total = term if total is None else total + term
    stage.out(0)[...] = total.astype(BF16)


def end_kernel(stage):
    recv_ref, order = stage.take(0), stage.take(1)[...]
    grad_ref, filter_ref = stage.out(0), stage.out(1)
    rows = grad_ref.shape[1]
    filter_ref[...] = unpacked(recv_ref, rows, rows // 2, order)
    stage.give(1)
    firsts, seconds = [], []
    for tile in range(recv_ref.shape[0] // 2):
        first, second = pair(*[recv_ref[2 * tile + i, :rows].astype(F32) for i in range(2)])
        firsts.append(first)
        seconds.append(second)
    for i, side in enumerate((firsts, seconds)):
        x = mm(order, jnp.concatenate(side, axis=1).astype(BF16))
        grad_ref[1 + i] = x.astype(BF16)
    query, weight_ref = stage.take(2)[...], stage.take(3)
    one, two = advanced(query, stage.take(4)[...])
    grad_ref[0] = (
        weight_ref[0, 0:1, :] * query + weight_ref[0, 1:2, :] * one + weight_ref[0, 2:3, :] * two
    ).astype(BF16)


def partner(x, axis, mask):
    return lax.ppermute(x, axis, [(i, i ^ mask) for i in range(lax.axis_size(axis))])


def exchanged(x, axis):
    return lax.all_to_all(x, axis, split_axis=0, concat_axis=0, tiled=True)


def owner_layer(qkv, filt, skip_gain, short_weight, w_out, g_out):
    shape = jax.ShapeDtypeStruct
    seq_parts, ch_parts = lax.axis_size("seq"), lax.axis_size("ch")
    rows, width = qkv.shape[1], qkv.shape[2]
    tokens = seq_parts * rows
    quarter = tokens // PHASES
    order = row_order(rows)
    tables = jnp.asarray(phase_tables(tokens))
    tables_on, tables_back = Far(tables, [(0, 2), (4, 1)]), Far(tables, [(2, 2)])
    table_flops = 2 * 2 * 2 * 3 * tokens * tokens // PHASES * LANES
    product_flops = 2 * rows * width * width * ch_parts
    packed = Far(shape((seq_parts, rows // 2, LANES), BF16))
    wide = Far(shape((seq_parts, rows + rows // 2, LANES), BF16))
    column, exact = shape((rows, width), BF16), shape((rows, width), F32)
    weight, gain = Far(short_weight), Far(skip_gain[None, :])
    there, back = Far(order), Far(order.T)

    send, tail = call(
        start_kernel, [wide, Far(shape((16, width), BF16))], Far(qkv), there, Far(filt)
    )
    recv = exchanged(send, "seq")
    (half_sums,) = call(
        first_product_kernel,
        [Far(shape((2, rows, width), BF16))],
        Far(g_out),
        Near(w_out),
        flops=product_flops // 2,
    )
    half_sums = partner(half_sums, "ch", 1)
    tail = passed_along(tail, "seq", 1)
    across, own = call(
        second_product_kernel,
        [Far(column), Far(exact)],
        Far(g_out),
        Near(w_out),
        Near(half_sums),
        flops=product_flops // 2,
    )
    across = partner(across, "ch", 2)
    send, kept = call(
        sum_kernel,
        [packed, Far(shape((2, rows, width), F32))],
        Far(qkv, [(0, 1)]),
        weight,
        Near(tail),
        Far(own),
        Near(across),
        there,
    )
    grad_recv = exchanged(send, "seq")
    send, saved = call(
        forward_kernel,
        [packed, Far(shape((3 * PHASES, quarter, LANES), F32))],
        Near(recv),
        weight,
        gain,
        tables_on,
        tables_back,
        flops=table_flops,
    )
    long_out = exchanged(send, "seq")
    (send,) = call(
        backward_kernel,
        [wide],
        Far(grad_recv),
        weight,
        gain,
        tables_on,
        Far(saved, [(0, 8)]),
        tables_back,
        Far(saved, [(8, 4)]),
        flops=table_flops,
    )
    grad_recv = exchanged(send, "seq")
    gated, grad_query, heads = call(
        gate_kernel,
        [Far(column), Far(exact), Far(shape((8, width), F32))],
        Near(long_out),
        back,
        Far(kept),
    )
    heads = passed_along(heads, "seq", -1)
    across = partner(gated, "ch", 2)
    near, far = partner(gated, "ch", 1), partner(across, "ch", 1)
    (output,) = call(
        functools.partial(output_kernel, ch_parts),
        [Far(column)],
        Near(w_out),
        Far(gated),
        Near(near),
        Near(across),
        Near(far),
        flops=product_flops,
    )
    grad_qkv, grad_filter = call(
        end_kernel,
        [Far(shape((3, rows, width), BF16)), Far(exact)],
        Near(grad_recv),
        back,
        Far(grad_query),
        weight,
        Near(heads),
    )
    return (output, grad_qkv, grad_filter)


def local(qkv, filt, skip_gain, short_weight, w_out, g_out):
    seq_parts = lax.axis_size("seq")
    rows, width = qkv.shape[1], qkv.shape[2]
    fits = width == HALF * seq_parts and rows % HALF == 0 and rows * seq_parts <= 2048
    if fits and lax.axis_size("ch") == 4:
        return owner_layer(qkv, filt, skip_gain, short_weight, w_out, g_out)
    return spread_layer(qkv, filt, skip_gain, short_weight, w_out, g_out)


def solution(mesh):
    in_specs = (
        P(None, "seq", "ch"),
        P("seq", "ch"),
        P("ch"),
        P(None, None, "ch"),
        P(None, "ch"),
        P("seq", "ch"),
    )
    out_specs = (P("seq", "ch"), P(None, "seq", "ch"), P("seq", "ch"))
    return jax.shard_map(local, mesh=mesh, in_specs=in_specs, out_specs=out_specs, check_vma=False)
```

```python
import functools
import math

import jax
import jax.numpy as jnp
import numpy as np
from jax import lax
from jax.experimental import pallas as pl
from jax.experimental.pallas import tpu as pltpu
from jax.sharding import PartitionSpec as P

HIGHEST = lax.Precision.HIGHEST
TWO_PI = 2.0 * math.pi
LANES = 128
HALF = 64
PHASES = 4
BF16 = jnp.bfloat16
F32 = jnp.float32
VMEM_LIMIT = 24 * 1024 * 1024


def passed_along(block, axis, distance):
    devices = range(lax.axis_size(axis))
    route = [(i - distance, i) for i in devices if i - distance in devices]
    return lax.ppermute(block, axis, route)


def phase_pair(left_count, right_count, period, left_start, right_start):
    left_idx = lax.broadcasted_iota(jnp.int32, (left_count, right_count), 0) + left_start
    right_idx = lax.broadcasted_iota(jnp.int32, (left_count, right_count), 1) + right_start
    angle_all = (left_idx * right_idx % period).astype(jnp.float32) * (TWO_PI / period)
    return (jnp.cos(angle_all), jnp.sin(angle_all))


def contract(pattern, matrix, values):
    return jnp.einsum(
        pattern, matrix, values, precision=HIGHEST, preferred_element_type=jnp.float32
    )


def forward_spectrum(signal):
    seq_parts = lax.axis_size("seq")
    row_count = signal.shape[0]
    row_share = row_count // seq_parts
    period = 2 * seq_parts * row_count
    spread_in = lax.all_to_all(signal[None], "seq", split_axis=1, concat_axis=0, tiled=True)
    outer_cos, outer_sin = phase_pair(2 * seq_parts, seq_parts, 2 * seq_parts, 0, 0)
    section_re = contract("cp,prw->crw", outer_cos, spread_in)
    section_im = -contract("cp,prw->crw", outer_sin, spread_in)
    twist_cos, twist_sin = phase_pair(
        2 * seq_parts, row_share, period, 0, lax.axis_index("seq") * row_share
    )
    twist_cos = twist_cos[:, :, None]
    twist_sin = twist_sin[:, :, None]
    turned_re = section_re * twist_cos + section_im * twist_sin
    turned_im = section_im * twist_cos - section_re * twist_sin
    inner_cos, inner_sin = phase_pair(row_count, row_count, row_count, 0, 0)
    piece_re = lax.all_to_all(turned_re, "seq", split_axis=0, concat_axis=1, tiled=True)
    piece_im = lax.all_to_all(turned_im, "seq", split_axis=0, concat_axis=1, tiled=True)
    spec_re = contract("dm,cmk->cdk", inner_cos, piece_re) + contract(
        "dm,cmk->cdk", inner_sin, piece_im
    )
    spec_im = contract("dm,cmk->cdk", inner_cos, piece_im) - contract(
        "dm,cmk->cdk", inner_sin, piece_re
    )
    return (spec_re, spec_im)


def time_signal(spec_re, spec_im):
    seq_parts = lax.axis_size("seq")
    row_count = spec_re.shape[1]
    period = 2 * seq_parts * row_count
    inner_cos, inner_sin = phase_pair(row_count, row_count, row_count, 0, 0)
    back_re = contract("md,cdk->cmk", inner_cos, spec_re) - contract(
        "md,cdk->cmk", inner_sin, spec_im
    )
    back_im = contract("md,cdk->cmk", inner_cos, spec_im) + contract(
        "md,cdk->cmk", inner_sin, spec_re
    )
    twist_cos, twist_sin = phase_pair(2, row_count, period, 2 * lax.axis_index("seq"), 0)
    twist_cos = twist_cos[:, :, None]
    twist_sin = twist_sin[:, :, None]
    turned_re = back_re * twist_cos - back_im * twist_sin
    turned_im = back_im * twist_cos + back_re * twist_sin
    outer_cos, outer_sin = phase_pair(seq_parts, 2 * seq_parts, 2 * seq_parts, 0, 0)
    piece_re = lax.all_to_all(turned_re, "seq", split_axis=1, concat_axis=0, tiled=True)
    piece_im = lax.all_to_all(turned_im, "seq", split_axis=1, concat_axis=0, tiled=True)
    summed = contract("pc,crk->prk", outer_cos, piece_re) - contract(
        "pc,crk->prk", outer_sin, piece_im
    )
    returned = summed * (1.0 / period)
    return lax.all_to_all(returned, "seq", split_axis=0, concat_axis=1, tiled=True)[0]


def spread_layer(qkv, filt, skip_gain, short_weight, w_out, g_out):
    row_count = qkv.shape[1]
    slab_width = qkv.shape[2]
    tail_rows = passed_along(qkv[:, row_count - 2 :, :], "seq", 1)
    extended = jnp.concatenate([tail_rows, qkv], axis=1)
    short = (
        short_weight[:, 0, None, :] * extended[:, 2:, :]
        + short_weight[:, 1, None, :] * extended[:, 1:-1, :]
        + short_weight[:, 2, None, :] * extended[:, :-2, :]
    )
    query_gate = short[0]
    key_short = short[1]
    value_short = short[2]
    mixed = key_short * value_short
    both_re, both_im = forward_spectrum(jnp.concatenate([mixed, filt], axis=1))
    signal_re = both_re[:, :, :slab_width]
    signal_im = both_im[:, :, :slab_width]
    kernel_re = both_re[:, :, slab_width:]
    kernel_im = both_im[:, :, slab_width:]
    conv_out = time_signal(
        signal_re * kernel_re - signal_im * kernel_im, signal_re * kernel_im + signal_im * kernel_re
    )
    long_out = conv_out + skip_gain * mixed
    gated_out = (query_gate * long_out).astype(jnp.bfloat16)
    projected = jnp.dot(
        lax.all_gather(gated_out, "ch", axis=1, tiled=True),
        w_out,
        preferred_element_type=jnp.float32,
    )
    output = projected.astype(jnp.bfloat16)
    grad_all = lax.all_gather(g_out, "ch", axis=1, tiled=True)
    rows_all = lax.all_to_all(w_out, "ch", split_axis=0, concat_axis=1, tiled=True)
    grad_gated = lax.dot_general(
        grad_all, rows_all, (((1,), (1,)), ((), ())), preferred_element_type=jnp.float32
    )
    grad_long = grad_gated * query_gate
    grad_query = grad_gated * long_out
    grad_re, grad_im = forward_spectrum(grad_long)
    pair_re = jnp.concatenate(
        [kernel_re * grad_re + kernel_im * grad_im, signal_re * grad_re + signal_im * grad_im],
        axis=2,
    )
    pair_im = jnp.concatenate(
        [kernel_re * grad_im - kernel_im * grad_re, signal_re * grad_im - signal_im * grad_re],
        axis=2,
    )
    pair_time = time_signal(pair_re, pair_im)
    grad_mixed = pair_time[:, :slab_width] + skip_gain * grad_long
    token_total = lax.axis_size("seq") * row_count
    grad_filter = pair_time[:, slab_width:] * (1.0 / math.sqrt(token_total))
    grad_short = jnp.stack([grad_query, grad_mixed * value_short, grad_mixed * key_short])
    head_rows = passed_along(grad_short[:, :2, :], "seq", -1)
    extended_grad = jnp.concatenate([grad_short, head_rows], axis=1)
    grad_qkv = (
        short_weight[:, 0, None, :] * extended_grad[:, :-2, :]
        + short_weight[:, 1, None, :] * extended_grad[:, 1:-1, :]
        + short_weight[:, 2, None, :] * extended_grad[:, 2:, :]
    ).astype(jnp.bfloat16)
    return (output, grad_qkv, grad_filter)


def split_bf16(values):
    high = values.astype(np.float32).astype(jnp.bfloat16)
    low = (values - high.astype(np.float64)).astype(np.float32).astype(jnp.bfloat16)
    return high, low


def phase_tables(tokens):
    quarter = tokens // PHASES
    freq = 2 * np.arange(quarter)[:, None] + 1
    turn = math.pi / (2 * tokens)
    angle = (freq * PHASES * np.arange(quarter)[None, :] % (4 * tokens)) * turn
    forward = np.concatenate([np.cos(angle), -np.sin(angle)], axis=1)
    backward = np.concatenate([np.cos(angle).T, -np.sin(angle).T], axis=1) / tokens
    angle = freq * np.arange(PHASES)[None, :] * turn
    twist = np.concatenate([np.cos(angle), np.sin(angle)], axis=1)
    twist = np.pad(twist, ((0, 0), (0, LANES - 2 * PHASES)))
    high, rest = split_bf16(twist)
    last = split_bf16(twist - high.astype(np.float64) - rest.astype(np.float64))[0]
    tables = np.zeros((8, quarter, 2 * quarter), jnp.bfloat16)
    tables[0], tables[1] = split_bf16(forward)
    tables[2], tables[3] = split_bf16(backward)
    for i, term in enumerate((high, rest, last)):
        tables[4, :, i * LANES : (i + 1) * LANES] = term
    return tables


def row_order(rows):
    order = np.zeros((rows, rows), np.float32)
    share = rows // PHASES
    for phase in range(PHASES):
        for j in range(share):
            order[phase * share + j, PHASES * j + phase] = 1.0
    return order.astype(jnp.bfloat16)


def mm(a, b):
    return lax.dot_general(a, b, (((1,), (0,)), ((), ())), preferred_element_type=F32)


def low_lanes(shape):
    return lax.broadcasted_iota(jnp.int32, shape, 1) < HALF


def swap(x):
    return pltpu.roll(x, HALF, 1)


class Near:
    def __init__(self, array, kept=False):
        self.array = array
        self.kept = kept


class Far:
    def __init__(self, array, cuts=None, turned=(), into=None):
        self.array = array
        self.turned = turned
        self.into = into
        if turned:
            step = array.shape[0] // len(turned)
            cuts = [(mask * step, step) for mask in turned]
        self.cuts = cuts or [(0, array.shape[0])]
        self.rows = sum(count for _, count in self.cuts)


class Stage:
    def __init__(self, items, count_in, refs):
        arrays, scratch = list(refs[: len(items)]), list(refs[len(items) :])
        sems = scratch.pop()
        self.count_in = count_in
        self.held, self.copies, self.waiting = [], [], []
        used = 0
        for i, (item, array) in enumerate(zip(items, arrays)):
            group = []
            if isinstance(item, Near):
                self.held.append(array)
            else:
                held = scratch.pop(0) if item.into is None else arrays[count_in + item.into]
                self.held.append(held)
                at = 0
                for cut, (start, count) in enumerate(item.cuts):
                    there = held.at[pl.ds(start if item.turned else at, count)]
                    at += count
                    if item.turned:
                        mask = item.turned[cut]
                        start = pl.multiple_of((lax.axis_index("ch") ^ mask) * count, count)
                    here = array.at[pl.ds(start, count)]
                    if i >= count_in:
                        here, there = there, here
                    group.append(pltpu.make_async_copy(here, there, sems.at[used]))
                    used += 1
            self.copies.append(group)
            self.waiting.append(set(range(len(group))))
        self.given = set()

    def bring(self, index):
        for copy in self.copies[index]:
            copy.start()

    def take(self, index, cut=None):
        for i in sorted(self.waiting[index]):
            if cut is None or cut == i:
                self.copies[index][i].wait()
                self.waiting[index].discard(i)
        return self.held[index]

    def out(self, index):
        return self.held[self.count_in + index]

    def give(self, index):
        if index not in self.given:
            self.bring(self.count_in + index)
            self.given.add(index)


def staged(kernel, items, count_in, *refs):
    stage = Stage(items, count_in, refs)
    for i in range(count_in):
        stage.bring(i)
    kernel(stage)
    for i in range(count_in):
        stage.take(i)
    for i in range(len(items) - count_in):
        stage.give(i)
    for i in range(len(items) - count_in):
        stage.take(count_in + i)


def in_hbm(x):
    return pltpu.with_memory_space_constraint(x, pltpu.HBM)


def result_of(x):
    make = pltpu.HBM if isinstance(x, Far) else pltpu.VMEM if x.kept else jax.ShapeDtypeStruct
    return make(x.array.shape, x.array.dtype)


def call(kernel, results, *args, flops=0):
    items = list(args) + list(results)
    specs, scratch, used = [], [], 0
    for item in items:
        near = isinstance(item, Near)
        specs.append(pl.BlockSpec(memory_space=pltpu.VMEM if near else pltpu.HBM))
        if not near:
            used += len(item.cuts)
            if item.into is None:
                scratch.append(pltpu.VMEM((item.rows, *item.array.shape[1:]), item.array.dtype))
    moved = sum(math.prod(x.array.shape) * x.array.dtype.itemsize for x in items)
    return pl.pallas_call(
        functools.partial(staged, kernel, items, len(args)),
        out_shape=[result_of(x) for x in results],
        in_specs=specs[: len(args)],
        out_specs=specs[len(args) :],
        scratch_shapes=scratch + [pltpu.SemaphoreType.DMA((max(used, 1),))],
        compiler_params=pltpu.CompilerParams(vmem_limit_bytes=VMEM_LIMIT),
        cost_estimate=pl.CostEstimate(flops=flops, bytes_accessed=moved, transcendentals=0),
    )(*[x.array if isinstance(x, Near) else in_hbm(x.array) for x in args])


def lane_tile(x, index):
    return x[:, index * LANES : (index + 1) * LANES]


def pair(first, second):
    low = low_lanes(first.shape)
    return jnp.where(low, first, swap(second)), jnp.where(low, swap(first), second)


def both(x):
    turned, low = swap(x), low_lanes(x.shape)
    return jnp.where(low, x, turned), jnp.where(low, turned, x)


def start_kernel(stage):
    send_ref, qkv_ref, order = stage.out(0), stage.take(0), stage.take(1)[...]
    rows = qkv_ref.shape[1]
    query, key, value = [mm(order, qkv_ref[i]) for i in range(3)]
    taps = mm(order, stage.take(2)[...].astype(BF16))
    for tile in range(query.shape[1] // LANES):
        for row, (x, y) in enumerate(((key, value), (query, taps))):
            here = slice(row * rows, (row + 1) * rows)
            x, y = pair(lane_tile(x, tile), lane_tile(y, tile))
            send_ref[2 * tile, here] = x.astype(BF16)
            send_ref[2 * tile + 1, here] = y.astype(BF16)


def partial_product(g, w_ref, mask):
    width = g.shape[1]
    w = w_ref[mask * width : (mask + 1) * width, :]
    return lax.dot_general(g, w, (((1,), (1,)), ((), ())), preferred_element_type=F32)


def first_product_kernel(stage):
    g, out_ref = stage.take(0)[...], stage.out(0)
    for i, mask in enumerate((1, 3)):
        out_ref[i] = partial_product(g, stage.take(1, i), mask).astype(BF16)


def second_product_kernel(stage):
    w_ref, g, near_ref = stage.take(1), stage.take(0)[...], stage.take(2)
    across_ref, own_ref = stage.out(0), stage.out(1)
    across = partial_product(g, w_ref, 2) + near_ref[1].astype(F32)
    across_ref[...] = across.astype(BF16)
    stage.give(0)
    own_ref[...] = partial_product(g, w_ref, 0) + near_ref[0].astype(F32)


def sum_kernel(stage):
    send_ref, order = stage.out(0), stage.take(0)[...]
    total = stage.take(1)[...] + stage.take(2)[...].astype(F32)
    total = mm(order, total.astype(BF16))
    half = total.shape[0] // 2
    for tile in range(total.shape[1] // LANES):
        t = lane_tile(total, tile)
        x, y = pair(t[:half], t[half:])
        send_ref[2 * tile] = x.astype(BF16)
        send_ref[2 * tile + 1] = y.astype(BF16)


def spread_phases(parts):
    (a_re, a_im), (b_re, b_im), (c_re, c_im), (d_re, d_im) = parts
    s_re, s_im, t_re, t_im = a_re + c_re, a_im + c_im, a_re - c_re, a_im - c_im
    u_re, u_im, v_re, v_im = b_re + d_re, b_im + d_im, b_re - d_re, b_im - d_im
    return [
        (s_re + u_re, s_im + u_im),
        (t_re + v_im, t_im - v_re),
        (s_re - u_re, s_im - u_im),
        (t_re - v_im, t_im + v_re),
    ]


def gather_phases(parts):
    (a_re, a_im), (b_re, b_im), (c_re, c_im), (d_re, d_im) = parts
    s_re, s_im, t_re, t_im = a_re + c_re, a_im + c_im, a_re - c_re, a_im - c_im
    u_re, u_im, v_re, v_im = b_re + d_re, b_im + d_im, b_re - d_re, b_im - d_im
    return [
        (s_re + u_re, s_im + u_im),
        (t_re - v_im, t_im + v_re),
        (s_re - u_re, s_im - u_im),
        (t_re + v_im, t_im - v_re),
    ]


def rows_of(ref, start, count):
    block = ref[:, start : start + count, :]
    return block.reshape(ref.shape[0] * count, ref.shape[2])


def turned_back(re, im, twist, phase):
    if phase == 0:
        return re, im
    c, s = twist[:, phase : phase + 1], twist[:, PHASES + phase : PHASES + phase + 1]
    return re * c + im * s, im * c - re * s


def turned_on(re, im, twist, phase):
    if phase == 0:
        return re, im
    c, s = twist[:, phase : phase + 1], twist[:, PHASES + phase : PHASES + phase + 1]
    return re * c - im * s, re * s + im * c


def lane_tile(x, index):
    return x[:, index * LANES : (index + 1) * LANES]


def causal(parts, weight):
    rows = lax.broadcasted_iota(jnp.int32, parts[0].shape, 0)
    two, three = [jnp.where(rows == 0, 0.0, pltpu.roll(parts[p], 1, 0)) for p in (2, 3)]
    once, twice = [three, *parts[:3]], [two, three, *parts[:2]]
    return [
        weight[0:1] * x + weight[1:2] * y + weight[2:3] * z for x, y, z in zip(parts, once, twice)
    ]


def anticausal(parts, weight):
    count = parts[0].shape[0]
    rows = lax.broadcasted_iota(jnp.int32, parts[0].shape, 0)
    zero, one = [
        jnp.where(rows == count - 1, 0.0, pltpu.roll(parts[p], count - 1, 0)) for p in (0, 1)
    ]
    once, twice = [*parts[1:], zero], [*parts[2:], zero, one]
    return [
        weight[0:1] * x + weight[1:2] * y + weight[2:3] * z for x, y, z in zip(parts, once, twice)
    ]


def halves(x):
    high = x.astype(BF16)
    return high, (x - high.astype(F32)).astype(BF16)


def twiddles(table_ref):
    terms = [table_ref[2, :, i * LANES : (i + 1) * LANES].astype(F32) for i in range(3)]
    return terms[0] + (terms[1] + terms[2])


def transformed(parts, table_ref, twist):
    quarter = parts[0].shape[0]
    high, rest = halves(jnp.concatenate(parts, axis=1))
    sides = []
    for side in (slice(0, quarter), slice(quarter, 2 * quarter)):
        fh, fl = table_ref[0, :, side], table_ref[1, :, side]
        sides.append(mm(fh, high) + mm(fl, high) + mm(fh, rest))
    turned = []
    for phase in range(PHASES):
        re, im = [lane_tile(side, phase) for side in sides]
        turned.append(turned_back(re, im, twist, phase))
    return spread_phases(turned)


def in_time(spectrum, table_ref, twist):
    bh, bl = table_ref[0], table_ref[1]
    parts = []
    for phase, (re, im) in enumerate(gather_phases(spectrum)):
        parts.append(jnp.concatenate(turned_on(re, im, twist, phase), axis=0))
    high, rest = halves(jnp.concatenate(parts, axis=1))
    t = mm(bh, high) + mm(bl, high) + mm(bh, rest)
    return [lane_tile(t, phase) for phase in range(PHASES)]


def own_weights(weight_ref, gain_ref):
    place = lax.axis_index("seq")
    lanes = pl.ds(pl.multiple_of(place // 2 * LANES, LANES), LANES)
    odd = place % 2 == 1

    def mine(x):
        return jnp.where(odd, swap(x), x)

    weights = [mine(weight_ref[i, :, lanes]) for i in range(3)]
    gain = both(mine(gain_ref[:, lanes]))[0]
    low = low_lanes(weights[0].shape)
    only = (lax.broadcasted_iota(jnp.int32, weights[0].shape, 0) == 0).astype(F32)
    pair_weight = jnp.where(low, weights[1], swap(weights[2]))
    query_weight = jnp.where(low, weights[0], only)
    return pair_weight, query_weight, gain


def forward_kernel(stage):
    recv_ref, weight_ref, gain_ref = [stage.take(i) for i in range(3)]
    gated_ref, saved_ref = stage.out(0), stage.out(1)
    blocks = recv_ref.shape[0]
    rows = recv_ref.shape[1] // 2
    share = rows // PHASES
    quarter = blocks * share
    low = low_lanes((quarter, LANES))
    pair_weight, query_weight, gain = own_weights(weight_ref, gain_ref)

    starts = [phase * share for phase in range(PHASES)]
    pairs = causal([rows_of(recv_ref, at, share).astype(F32) for at in starts], pair_weight)
    gates = causal([rows_of(recv_ref, rows + at, share).astype(F32) for at in starts], query_weight)
    for phase in range(PHASES):
        saved_ref[8 + phase] = pairs[phase]
    mixed = [x * swap(x) for x in pairs]
    query = [both(x)[0] for x in gates]
    table_ref = stage.take(3)
    twist = twiddles(table_ref)
    spectrum = transformed([jnp.where(low, x, y) for x, y in zip(mixed, gates)], table_ref, twist)
    product = []
    for r, (re, im) in enumerate(spectrum):
        saved_ref[2 * r] = re
        saved_ref[2 * r + 1] = im
        other_re, other_im = swap(re), swap(im)
        product.append((re * other_re - im * other_im, re * other_im + im * other_re))
    stage.copies[stage.count_in + 1][0].start()
    conv = in_time(product, stage.take(4), twist)
    long_out = [x + gain * y for x, y in zip(conv, mixed)]
    gated = [x * y for x, y in zip(query, long_out)]
    for phase in range(PHASES // 2):
        t = jnp.where(low, gated[phase], gated[phase + 2]).astype(BF16)
        gated_ref[:, starts[phase] : starts[phase] + share, :] = t.reshape(blocks, share, LANES)
    for phase in range(PHASES):
        saved_ref[12 + phase] = jnp.where(low, query[phase], long_out[phase])
    stage.copies[stage.count_in + 1][1].start()
    stage.given.add(1)


def backward_kernel(stage):
    grad_ref, weight_ref, gain_ref, gates_ref = [stage.take(i) for i in range(4)]
    send_ref = stage.out(0)
    blocks = grad_ref.shape[0]
    share = grad_ref.shape[1] // 2
    rows = PHASES * share
    quarter = blocks * share
    low = low_lanes((quarter, LANES))
    pair_weight, query_weight, gain = own_weights(weight_ref, gain_ref)

    starts = [phase * share for phase in range(PHASES)]
    packed = [rows_of(grad_ref, at, share).astype(F32) for at in starts[:2]]
    grad_gated = [both(x)[i] for i in range(2) for x in packed]
    gates = [both(gates_ref[phase]) for phase in range(PHASES)]
    grad_long = [x * y for x, (y, _) in zip(grad_gated, gates)]
    grad_query = anticausal([x * y for x, (_, y) in zip(grad_gated, gates)], query_weight)
    table_ref = stage.take(4)
    twist = twiddles(table_ref)
    grad_spectrum = transformed(grad_long, table_ref, twist)
    saved_ref = stage.take(5)
    product = []
    for r, (re, im) in enumerate(grad_spectrum):
        k_re, k_im = saved_ref[2 * r], saved_ref[2 * r + 1]
        product.append((k_re * re + k_im * im, k_re * im - k_im * re))
    table_ref = stage.take(6)
    times = in_time(product, table_ref, twist)
    pairs_ref = stage.take(7)
    grad_mixed = [both(x + gain * y)[1] for x, y in zip(times, grad_long)]
    grad_pairs = anticausal(
        [x * swap(pairs_ref[phase]) for phase, x in enumerate(grad_mixed)], pair_weight
    )
    scale = 1.0 / math.sqrt(PHASES * quarter)
    for phase, at in enumerate(starts):
        x = grad_pairs[phase].astype(BF16)
        y = jnp.where(low, grad_query[phase], swap(times[phase]) * scale).astype(BF16)
        send_ref[:, at : at + share, :] = x.reshape(blocks, share, LANES)
        send_ref[:, rows + at : rows + at + share, :] = y.reshape(blocks, share, LANES)


def unpacked(blocks, order):
    half = blocks[0].shape[0]
    tiles = []
    for tile in range(len(blocks) // 2):
        top, bottom = pair(blocks[2 * tile].astype(F32), blocks[2 * tile + 1].astype(F32))
        tiles.append(jnp.concatenate([top, bottom], axis=0))
    return mm(order, jnp.concatenate(tiles, axis=1).astype(BF16))


def end_kernel(stage):
    recv_ref, order_ref = stage.take(0), stage.take(1)
    grad_ref, filter_ref = stage.out(0), stage.out(1)
    order = order_ref[...]
    blocks = recv_ref.shape[0]
    rows = recv_ref.shape[1] // 2
    sides = []
    for at in (0, rows):
        firsts, seconds = [], []
        for tile in range(blocks // 2):
            x, y = [recv_ref[2 * tile + i, at : at + rows].astype(F32) for i in range(2)]
            first, second = pair(x, y)
            firsts.append(first)
            seconds.append(second)
        for side in (firsts, seconds):
            sides.append(mm(order, jnp.concatenate(side, axis=1).astype(BF16)))
    key, value, query, taps = sides
    filter_ref[...] = taps
    stage.give(1)
    grad_ref[0] = query.astype(BF16)
    grad_ref[1] = key.astype(BF16)
    grad_ref[2] = value.astype(BF16)


def output_kernel(parts, stage):
    order, w_ref = stage.take(0)[...], stage.take(1)
    total = None
    for part in range(parts):
        gated_ref = stage.take(2 + part)
        block = unpacked([gated_ref[i] for i in range(gated_ref.shape[0])], order).astype(BF16)
        width = block.shape[1]
        term = mm(block, w_ref[part * width : (part + 1) * width, :])
        total = term if total is None else total + term
    stage.out(0)[...] = total.astype(BF16)


def partner(x, axis, mask):
    return lax.ppermute(x, axis, [(i, i ^ mask) for i in range(lax.axis_size(axis))])


def exchanged(x, axis):
    return lax.all_to_all(x, axis, split_axis=0, concat_axis=0, tiled=True)


def owner_layer(qkv, filt, skip_gain, short_weight, w_out, g_out):
    shape = jax.ShapeDtypeStruct
    seq_parts, ch_parts = lax.axis_size("seq"), lax.axis_size("ch")
    rows, width = qkv.shape[1], qkv.shape[2]
    tokens = seq_parts * rows
    quarter = tokens // PHASES
    order = row_order(rows)
    tables = jnp.asarray(phase_tables(tokens))
    tables_on, tables_back = Far(tables, [(0, 2), (4, 1)]), Far(tables, [(2, 2)])
    table_flops = 2 * 2 * 2 * 3 * tokens * tokens // PHASES * LANES
    product_flops = 2 * rows * width * width * ch_parts
    packed = shape((seq_parts, rows // 2, LANES), BF16)
    double = shape((seq_parts, 2 * rows, LANES), BF16)
    column = shape((rows, width), BF16)
    saved = shape((4 * PHASES, quarter, LANES), F32)
    weight, gain = Far(short_weight), Far(skip_gain[None, :])

    (send,) = call(start_kernel, [Far(double)], Far(qkv), Far(order), Far(filt))
    recv = exchanged(send, "seq")
    half_sums, w_kept = call(
        first_product_kernel,
        [Far(shape((2, rows, width), BF16)), Near(w_out, kept=True)],
        Far(g_out),
        Far(w_out, turned=(1, 3, 2, 0), into=1),
        flops=product_flops // 2,
    )
    half_sums = partner(half_sums, "ch", 1)
    across, own = call(
        second_product_kernel,
        [Far(column), Far(shape((rows, width), F32))],
        Far(g_out),
        Near(w_kept),
        Near(half_sums),
        flops=product_flops // 2,
    )
    across = partner(across, "ch", 2)
    (send,) = call(sum_kernel, [Far(packed)], Far(order), Far(own), Near(across))
    grad_recv = exchanged(send, "seq")
    send, kept = call(
        forward_kernel,
        [Far(packed), Far(saved, [(0, 12), (12, 4)])],
        Near(recv),
        weight,
        gain,
        tables_on,
        tables_back,
        flops=table_flops,
    )
    gated = exchanged(send, "seq")
    (send,) = call(
        backward_kernel,
        [Far(double)],
        Far(grad_recv),
        weight,
        gain,
        Far(kept, [(12, 4)]),
        tables_on,
        Far(kept, [(0, 8)]),
        tables_back,
        Far(kept, [(8, 4)]),
        flops=table_flops,
    )
    grad_recv = exchanged(send, "seq")
    across = partner(gated, "ch", 2)
    near, far = partner(gated, "ch", 1), partner(across, "ch", 1)
    back_order = Far(order.T)
    (output,) = call(
        functools.partial(output_kernel, ch_parts),
        [Far(column)],
        back_order,
        Near(w_kept),
        Far(gated),
        Near(near),
        Near(across),
        Near(far),
        flops=product_flops,
    )
    grad_qkv, grad_filter = call(
        end_kernel,
        [Far(shape((3, rows, width), BF16)), Far(shape((rows, width), F32))],
        Near(grad_recv),
        back_order,
    )
    return (output, grad_qkv, grad_filter)


def local(qkv, filt, skip_gain, short_weight, w_out, g_out):
    seq_parts = lax.axis_size("seq")
    rows, width = qkv.shape[1], qkv.shape[2]
    fits = width == HALF * seq_parts and rows % HALF == 0 and rows * seq_parts <= 2048
    if fits and lax.axis_size("ch") == 4:
        return owner_layer(qkv, filt, skip_gain, short_weight, w_out, g_out)
    return spread_layer(qkv, filt, skip_gain, short_weight, w_out, g_out)


def solution(mesh):
    in_specs = (
        P(None, "seq", "ch"),
        P("seq", "ch"),
        P("ch"),
        P(None, None, "ch"),
        P(None, "ch"),
        P("seq", "ch"),
    )
    out_specs = (P("seq", "ch"), P(None, "seq", "ch"), P("seq", "ch"))
    return jax.shard_map(local, mesh=mesh, in_specs=in_specs, out_specs=out_specs, check_vma=False)
```

```python
import functools
import math

import jax
import jax.numpy as jnp
import numpy as np
from jax import lax
from jax.experimental import pallas as pl
from jax.experimental.pallas import tpu as pltpu
from jax.sharding import PartitionSpec as P

HIGHEST = lax.Precision.HIGHEST
TWO_PI = 2.0 * math.pi
LANES = 128
HALF = 64
PHASES = 4
BF16 = jnp.bfloat16
F32 = jnp.float32
VMEM_LIMIT = 24 * 1024 * 1024


def passed_along(block, axis, distance):
    devices = range(lax.axis_size(axis))
    route = [(i - distance, i) for i in devices if i - distance in devices]
    return lax.ppermute(block, axis, route)


def phase_pair(left_count, right_count, period, left_start, right_start):
    left_idx = lax.broadcasted_iota(jnp.int32, (left_count, right_count), 0) + left_start
    right_idx = lax.broadcasted_iota(jnp.int32, (left_count, right_count), 1) + right_start
    angle_all = (left_idx * right_idx % period).astype(jnp.float32) * (TWO_PI / period)
    return (jnp.cos(angle_all), jnp.sin(angle_all))


def contract(pattern, matrix, values):
    return jnp.einsum(
        pattern, matrix, values, precision=HIGHEST, preferred_element_type=jnp.float32
    )


def forward_spectrum(signal):
    seq_parts = lax.axis_size("seq")
    row_count = signal.shape[0]
    row_share = row_count // seq_parts
    period = 2 * seq_parts * row_count
    spread_in = lax.all_to_all(signal[None], "seq", split_axis=1, concat_axis=0, tiled=True)
    outer_cos, outer_sin = phase_pair(2 * seq_parts, seq_parts, 2 * seq_parts, 0, 0)
    section_re = contract("cp,prw->crw", outer_cos, spread_in)
    section_im = -contract("cp,prw->crw", outer_sin, spread_in)
    twist_cos, twist_sin = phase_pair(
        2 * seq_parts, row_share, period, 0, lax.axis_index("seq") * row_share
    )
    twist_cos = twist_cos[:, :, None]
    twist_sin = twist_sin[:, :, None]
    turned_re = section_re * twist_cos + section_im * twist_sin
    turned_im = section_im * twist_cos - section_re * twist_sin
    inner_cos, inner_sin = phase_pair(row_count, row_count, row_count, 0, 0)
    piece_re = lax.all_to_all(turned_re, "seq", split_axis=0, concat_axis=1, tiled=True)
    piece_im = lax.all_to_all(turned_im, "seq", split_axis=0, concat_axis=1, tiled=True)
    spec_re = contract("dm,cmk->cdk", inner_cos, piece_re) + contract(
        "dm,cmk->cdk", inner_sin, piece_im
    )
    spec_im = contract("dm,cmk->cdk", inner_cos, piece_im) - contract(
        "dm,cmk->cdk", inner_sin, piece_re
    )
    return (spec_re, spec_im)


def time_signal(spec_re, spec_im):
    seq_parts = lax.axis_size("seq")
    row_count = spec_re.shape[1]
    period = 2 * seq_parts * row_count
    inner_cos, inner_sin = phase_pair(row_count, row_count, row_count, 0, 0)
    back_re = contract("md,cdk->cmk", inner_cos, spec_re) - contract(
        "md,cdk->cmk", inner_sin, spec_im
    )
    back_im = contract("md,cdk->cmk", inner_cos, spec_im) + contract(
        "md,cdk->cmk", inner_sin, spec_re
    )
    twist_cos, twist_sin = phase_pair(2, row_count, period, 2 * lax.axis_index("seq"), 0)
    twist_cos = twist_cos[:, :, None]
    twist_sin = twist_sin[:, :, None]
    turned_re = back_re * twist_cos - back_im * twist_sin
    turned_im = back_im * twist_cos + back_re * twist_sin
    outer_cos, outer_sin = phase_pair(seq_parts, 2 * seq_parts, 2 * seq_parts, 0, 0)
    piece_re = lax.all_to_all(turned_re, "seq", split_axis=1, concat_axis=0, tiled=True)
    piece_im = lax.all_to_all(turned_im, "seq", split_axis=1, concat_axis=0, tiled=True)
    summed = contract("pc,crk->prk", outer_cos, piece_re) - contract(
        "pc,crk->prk", outer_sin, piece_im
    )
    returned = summed * (1.0 / period)
    return lax.all_to_all(returned, "seq", split_axis=0, concat_axis=1, tiled=True)[0]


def spread_layer(qkv, filt, skip_gain, short_weight, w_out, g_out):
    row_count = qkv.shape[1]
    slab_width = qkv.shape[2]
    tail_rows = passed_along(qkv[:, row_count - 2 :, :], "seq", 1)
    extended = jnp.concatenate([tail_rows, qkv], axis=1)
    short = (
        short_weight[:, 0, None, :] * extended[:, 2:, :]
        + short_weight[:, 1, None, :] * extended[:, 1:-1, :]
        + short_weight[:, 2, None, :] * extended[:, :-2, :]
    )
    query_gate = short[0]
    key_short = short[1]
    value_short = short[2]
    mixed = key_short * value_short
    both_re, both_im = forward_spectrum(jnp.concatenate([mixed, filt], axis=1))
    signal_re = both_re[:, :, :slab_width]
    signal_im = both_im[:, :, :slab_width]
    kernel_re = both_re[:, :, slab_width:]
    kernel_im = both_im[:, :, slab_width:]
    conv_out = time_signal(
        signal_re * kernel_re - signal_im * kernel_im, signal_re * kernel_im + signal_im * kernel_re
    )
    long_out = conv_out + skip_gain * mixed
    gated_out = (query_gate * long_out).astype(jnp.bfloat16)
    projected = jnp.dot(
        lax.all_gather(gated_out, "ch", axis=1, tiled=True),
        w_out,
        preferred_element_type=jnp.float32,
    )
    output = projected.astype(jnp.bfloat16)
    grad_all = lax.all_gather(g_out, "ch", axis=1, tiled=True)
    rows_all = lax.all_to_all(w_out, "ch", split_axis=0, concat_axis=1, tiled=True)
    grad_gated = lax.dot_general(
        grad_all, rows_all, (((1,), (1,)), ((), ())), preferred_element_type=jnp.float32
    )
    grad_long = grad_gated * query_gate
    grad_query = grad_gated * long_out
    grad_re, grad_im = forward_spectrum(grad_long)
    pair_re = jnp.concatenate(
        [kernel_re * grad_re + kernel_im * grad_im, signal_re * grad_re + signal_im * grad_im],
        axis=2,
    )
    pair_im = jnp.concatenate(
        [kernel_re * grad_im - kernel_im * grad_re, signal_re * grad_im - signal_im * grad_re],
        axis=2,
    )
    pair_time = time_signal(pair_re, pair_im)
    grad_mixed = pair_time[:, :slab_width] + skip_gain * grad_long
    token_total = lax.axis_size("seq") * row_count
    grad_filter = pair_time[:, slab_width:] * (1.0 / math.sqrt(token_total))
    grad_short = jnp.stack([grad_query, grad_mixed * value_short, grad_mixed * key_short])
    head_rows = passed_along(grad_short[:, :2, :], "seq", -1)
    extended_grad = jnp.concatenate([grad_short, head_rows], axis=1)
    grad_qkv = (
        short_weight[:, 0, None, :] * extended_grad[:, :-2, :]
        + short_weight[:, 1, None, :] * extended_grad[:, 1:-1, :]
        + short_weight[:, 2, None, :] * extended_grad[:, 2:, :]
    ).astype(jnp.bfloat16)
    return (output, grad_qkv, grad_filter)


def split_bf16(values):
    high = values.astype(np.float32).astype(jnp.bfloat16)
    low = (values - high.astype(np.float64)).astype(np.float32).astype(jnp.bfloat16)
    return high, low


def phase_tables(tokens):
    quarter = tokens // PHASES
    freq = 2 * np.arange(quarter)[:, None] + 1
    turn = math.pi / (2 * tokens)
    angle = (freq * PHASES * np.arange(quarter)[None, :] % (4 * tokens)) * turn
    forward = np.concatenate([np.cos(angle), -np.sin(angle)], axis=1)
    backward = np.concatenate([np.cos(angle).T, -np.sin(angle).T], axis=1) / tokens
    angle = freq * np.arange(PHASES)[None, :] * turn
    twist = np.concatenate([np.cos(angle), np.sin(angle)], axis=1)
    twist = np.pad(twist, ((0, 0), (0, LANES - 2 * PHASES)))
    high, rest = split_bf16(twist)
    last = split_bf16(twist - high.astype(np.float64) - rest.astype(np.float64))[0]
    tables = np.zeros((8, quarter, 2 * quarter), jnp.bfloat16)
    tables[0], tables[1] = split_bf16(forward)
    tables[2], tables[3] = split_bf16(backward)
    for i, term in enumerate((high, rest, last)):
        tables[4, :, i * LANES : (i + 1) * LANES] = term
    return tables


def row_order(rows):
    order = np.zeros((rows, rows), np.float32)
    share = rows // PHASES
    for phase in range(PHASES):
        for j in range(share):
            order[phase * share + j, PHASES * j + phase] = 1.0
    return order.astype(jnp.bfloat16)


def mm(a, b):
    return lax.dot_general(a, b, (((1,), (0,)), ((), ())), preferred_element_type=F32)


def low_lanes(shape):
    return lax.broadcasted_iota(jnp.int32, shape, 1) < HALF


def swap(x):
    return pltpu.roll(x, HALF, 1)


class Near:
    def __init__(self, array, kept=False):
        self.array = array
        self.kept = kept


class Far:
    def __init__(self, array, cuts=None, turned=(), into=None):
        self.array = array
        self.turned = turned
        self.into = into
        if turned:
            step = array.shape[0] // len(turned)
            cuts = [(mask * step, step) for mask in turned]
        self.cuts = cuts or [(0, array.shape[0])]
        self.rows = sum(count for _, count in self.cuts)


class Stage:
    def __init__(self, items, count_in, refs):
        arrays, scratch = list(refs[: len(items)]), list(refs[len(items) :])
        sems = scratch.pop()
        self.count_in = count_in
        self.held, self.copies, self.waiting = [], [], []
        used = 0
        for i, (item, array) in enumerate(zip(items, arrays)):
            group = []
            if isinstance(item, Near):
                self.held.append(array)
            else:
                held = scratch.pop(0) if item.into is None else arrays[count_in + item.into]
                self.held.append(held)
                at = 0
                for cut, (start, count) in enumerate(item.cuts):
                    there = held.at[pl.ds(start if item.turned else at, count)]
                    at += count
                    if item.turned:
                        mask = item.turned[cut]
                        start = pl.multiple_of((lax.axis_index("ch") ^ mask) * count, count)
                    here = array.at[pl.ds(start, count)]
                    if i >= count_in:
                        here, there = there, here
                    group.append(pltpu.make_async_copy(here, there, sems.at[used]))
                    used += 1
            self.copies.append(group)
            self.waiting.append(set(range(len(group))))
        self.given = set()

    def bring(self, index):
        for copy in self.copies[index]:
            copy.start()

    def take(self, index, cut=None):
        for i in sorted(self.waiting[index]):
            if cut is None or cut == i:
                self.copies[index][i].wait()
                self.waiting[index].discard(i)
        return self.held[index]

    def out(self, index):
        return self.held[self.count_in + index]

    def give(self, index, cut=None):
        for i, copy in enumerate(self.copies[self.count_in + index]):
            if (index, i) not in self.given and cut in (None, i):
                copy.start()
                self.given.add((index, i))


def staged(kernel, items, count_in, *refs):
    stage = Stage(items, count_in, refs)
    for i in range(count_in):
        stage.bring(i)
    kernel(stage)
    for i in range(count_in):
        stage.take(i)
    for i in range(len(items) - count_in):
        stage.give(i)
    for i in range(len(items) - count_in):
        stage.take(count_in + i)


def in_hbm(x):
    return pltpu.with_memory_space_constraint(x, pltpu.HBM)


def result_of(x):
    make = pltpu.HBM if isinstance(x, Far) else pltpu.VMEM if x.kept else jax.ShapeDtypeStruct
    return make(x.array.shape, x.array.dtype)


def call(kernel, results, *args, flops=0):
    items = list(args) + list(results)
    specs, scratch, used = [], [], 0
    for item in items:
        near = isinstance(item, Near)
        specs.append(pl.BlockSpec(memory_space=pltpu.VMEM if near else pltpu.HBM))
        if not near:
            used += len(item.cuts)
            if item.into is None:
                scratch.append(pltpu.VMEM((item.rows, *item.array.shape[1:]), item.array.dtype))
    moved = sum(math.prod(x.array.shape) * x.array.dtype.itemsize for x in items)
    return pl.pallas_call(
        functools.partial(staged, kernel, items, len(args)),
        out_shape=[result_of(x) for x in results],
        in_specs=specs[: len(args)],
        out_specs=specs[len(args) :],
        scratch_shapes=scratch + [pltpu.SemaphoreType.DMA((max(used, 1),))],
        compiler_params=pltpu.CompilerParams(vmem_limit_bytes=VMEM_LIMIT),
        cost_estimate=pl.CostEstimate(flops=flops, bytes_accessed=moved, transcendentals=0),
    )(*[x.array if isinstance(x, Near) else in_hbm(x.array) for x in args])


def lane_tile(x, index):
    return x[:, index * LANES : (index + 1) * LANES]


def pair(first, second):
    low = low_lanes(first.shape)
    return jnp.where(low, first, swap(second)), jnp.where(low, swap(first), second)


def both(x):
    turned, low = swap(x), low_lanes(x.shape)
    return jnp.where(low, x, turned), jnp.where(low, turned, x)


def start_kernel(stage):
    send_ref, qkv_ref, order = stage.out(0), stage.take(0), stage.take(1)[...]
    rows = qkv_ref.shape[1]
    query, key, value = [mm(order, qkv_ref[i]) for i in range(3)]
    taps = mm(order, stage.take(2)[...].astype(BF16))
    for tile in range(query.shape[1] // LANES):
        for row, (x, y) in enumerate(((key, value), (query, taps))):
            here = slice(row * rows, (row + 1) * rows)
            x, y = pair(lane_tile(x, tile), lane_tile(y, tile))
            send_ref[2 * tile, here] = x.astype(BF16)
            send_ref[2 * tile + 1, here] = y.astype(BF16)
        stage.give(0, tile)


def partial_product(g, w_ref, mask):
    width = g.shape[1]
    w = w_ref[mask * width : (mask + 1) * width, :]
    return lax.dot_general(g, w, (((1,), (1,)), ((), ())), preferred_element_type=F32)


def first_product_kernel(stage):
    g, out_ref = stage.take(0)[...], stage.out(0)
    for i, mask in enumerate((1, 3)):
        out_ref[i] = partial_product(g, stage.take(1, i), mask).astype(BF16)


def second_product_kernel(stage):
    w_ref, g, near_ref = stage.take(1), stage.take(0)[...], stage.take(2)
    across_ref, own_ref = stage.out(0), stage.out(1)
    across = partial_product(g, w_ref, 2) + near_ref[1].astype(F32)
    across_ref[...] = across.astype(BF16)
    stage.give(0)
    own_ref[...] = partial_product(g, w_ref, 0) + near_ref[0].astype(F32)


def sum_kernel(stage):
    send_ref, order = stage.out(0), stage.take(0)[...]
    total = stage.take(1)[...] + stage.take(2)[...].astype(F32)
    total = mm(order, total.astype(BF16))
    half = total.shape[0] // 2
    for tile in range(total.shape[1] // LANES):
        t = lane_tile(total, tile)
        x, y = pair(t[:half], t[half:])
        send_ref[2 * tile] = x.astype(BF16)
        send_ref[2 * tile + 1] = y.astype(BF16)


def spread_phases(parts):
    (a_re, a_im), (b_re, b_im), (c_re, c_im), (d_re, d_im) = parts
    s_re, s_im, t_re, t_im = a_re + c_re, a_im + c_im, a_re - c_re, a_im - c_im
    u_re, u_im, v_re, v_im = b_re + d_re, b_im + d_im, b_re - d_re, b_im - d_im
    return [
        (s_re + u_re, s_im + u_im),
        (t_re + v_im, t_im - v_re),
        (s_re - u_re, s_im - u_im),
        (t_re - v_im, t_im + v_re),
    ]


def gather_phases(parts):
    (a_re, a_im), (b_re, b_im), (c_re, c_im), (d_re, d_im) = parts
    s_re, s_im, t_re, t_im = a_re + c_re, a_im + c_im, a_re - c_re, a_im - c_im
    u_re, u_im, v_re, v_im = b_re + d_re, b_im + d_im, b_re - d_re, b_im - d_im
    return [
        (s_re + u_re, s_im + u_im),
        (t_re - v_im, t_im + v_re),
        (s_re - u_re, s_im - u_im),
        (t_re + v_im, t_im - v_re),
    ]


def rows_of(ref, start, count):
    block = ref[:, start : start + count, :]
    return block.reshape(ref.shape[0] * count, ref.shape[2])


def turned_back(re, im, twist, phase):
    if phase == 0:
        return re, im
    c, s = twist[:, phase : phase + 1], twist[:, PHASES + phase : PHASES + phase + 1]
    return re * c + im * s, im * c - re * s


def turned_on(re, im, twist, phase):
    if phase == 0:
        return re, im
    c, s = twist[:, phase : phase + 1], twist[:, PHASES + phase : PHASES + phase + 1]
    return re * c - im * s, re * s + im * c


def lane_tile(x, index):
    return x[:, index * LANES : (index + 1) * LANES]


def causal(parts, weight):
    rows = lax.broadcasted_iota(jnp.int32, parts[0].shape, 0)
    two, three = [jnp.where(rows == 0, 0.0, pltpu.roll(parts[p], 1, 0)) for p in (2, 3)]
    once, twice = [three, *parts[:3]], [two, three, *parts[:2]]
    return [
        weight[0:1] * x + weight[1:2] * y + weight[2:3] * z for x, y, z in zip(parts, once, twice)
    ]


def anticausal(parts, weight):
    count = parts[0].shape[0]
    rows = lax.broadcasted_iota(jnp.int32, parts[0].shape, 0)
    zero, one = [
        jnp.where(rows == count - 1, 0.0, pltpu.roll(parts[p], count - 1, 0)) for p in (0, 1)
    ]
    once, twice = [*parts[1:], zero], [*parts[2:], zero, one]
    return [
        weight[0:1] * x + weight[1:2] * y + weight[2:3] * z for x, y, z in zip(parts, once, twice)
    ]


def halves(x):
    high = x.astype(BF16)
    return high, (x - high.astype(F32)).astype(BF16)


def twiddles(table_ref):
    terms = [table_ref[2, :, i * LANES : (i + 1) * LANES].astype(F32) for i in range(3)]
    return terms[0] + (terms[1] + terms[2])


def transformed(parts, table_ref, twist):
    quarter = parts[0].shape[0]
    high, rest = halves(jnp.concatenate(parts, axis=1))
    sides = []
    for side in (slice(0, quarter), slice(quarter, 2 * quarter)):
        fh, fl = table_ref[0, :, side], table_ref[1, :, side]
        sides.append(mm(fh, high) + mm(fl, high) + mm(fh, rest))
    turned = []
    for phase in range(PHASES):
        re, im = [lane_tile(side, phase) for side in sides]
        turned.append(turned_back(re, im, twist, phase))
    return spread_phases(turned)


def in_time(spectrum, table_ref, twist):
    bh, bl = table_ref[0], table_ref[1]
    parts = []
    for phase, (re, im) in enumerate(gather_phases(spectrum)):
        parts.append(jnp.concatenate(turned_on(re, im, twist, phase), axis=0))
    high, rest = halves(jnp.concatenate(parts, axis=1))
    t = mm(bh, high) + mm(bl, high) + mm(bh, rest)
    return [lane_tile(t, phase) for phase in range(PHASES)]


def own_weights(weight_ref, gain_ref):
    place = lax.axis_index("seq")
    lanes = pl.ds(pl.multiple_of(place // 2 * LANES, LANES), LANES)
    odd = place % 2 == 1

    def mine(x):
        return jnp.where(odd, swap(x), x)

    weights = [mine(weight_ref[i, :, lanes]) for i in range(3)]
    gain = both(mine(gain_ref[:, lanes]))[0]
    low = low_lanes(weights[0].shape)
    only = (lax.broadcasted_iota(jnp.int32, weights[0].shape, 0) == 0).astype(F32)
    pair_weight = jnp.where(low, weights[1], swap(weights[2]))
    query_weight = jnp.where(low, weights[0], only)
    return pair_weight, query_weight, gain


def forward_kernel(stage):
    recv_ref, weight_ref, gain_ref = [stage.take(i) for i in range(3)]
    gated_ref, saved_ref = stage.out(0), stage.out(1)
    blocks = recv_ref.shape[0]
    rows = recv_ref.shape[1] // 2
    share = rows // PHASES
    quarter = blocks * share
    low = low_lanes((quarter, LANES))
    pair_weight, query_weight, gain = own_weights(weight_ref, gain_ref)

    starts = [phase * share for phase in range(PHASES)]
    pairs = causal([rows_of(recv_ref, at, share).astype(F32) for at in starts], pair_weight)
    gates = causal([rows_of(recv_ref, rows + at, share).astype(F32) for at in starts], query_weight)
    for phase in range(PHASES):
        saved_ref[8 + phase] = pairs[phase]
    mixed = [x * swap(x) for x in pairs]
    query = [both(x)[0] for x in gates]
    table_ref = stage.take(3)
    twist = twiddles(table_ref)
    spectrum = transformed([jnp.where(low, x, y) for x, y in zip(mixed, gates)], table_ref, twist)
    product = []
    for r, (re, im) in enumerate(spectrum):
        saved_ref[2 * r] = re
        saved_ref[2 * r + 1] = im
        other_re, other_im = swap(re), swap(im)
        product.append((re * other_re - im * other_im, re * other_im + im * other_re))
    stage.give(1, 0)
    conv = in_time(product, stage.take(4), twist)
    long_out = [x + gain * y for x, y in zip(conv, mixed)]
    gated = [x * y for x, y in zip(query, long_out)]
    for phase in range(PHASES // 2):
        t = jnp.where(low, gated[phase], gated[phase + 2]).astype(BF16)
        gated_ref[:, starts[phase] : starts[phase] + share, :] = t.reshape(blocks, share, LANES)
    for phase in range(PHASES):
        saved_ref[12 + phase] = jnp.where(low, query[phase], long_out[phase])
    stage.give(1, 1)


def backward_kernel(stage):
    grad_ref, weight_ref, gain_ref, gates_ref = [stage.take(i) for i in range(4)]
    send_ref = stage.out(0)
    blocks = grad_ref.shape[0]
    share = grad_ref.shape[1] // 2
    rows = PHASES * share
    quarter = blocks * share
    low = low_lanes((quarter, LANES))
    pair_weight, query_weight, gain = own_weights(weight_ref, gain_ref)

    starts = [phase * share for phase in range(PHASES)]
    packed = [rows_of(grad_ref, at, share).astype(F32) for at in starts[:2]]
    grad_gated = [both(x)[i] for i in range(2) for x in packed]
    gates = [both(gates_ref[phase]) for phase in range(PHASES)]
    grad_long = [x * y for x, (y, _) in zip(grad_gated, gates)]
    grad_query = anticausal([x * y for x, (_, y) in zip(grad_gated, gates)], query_weight)
    table_ref = stage.take(4)
    twist = twiddles(table_ref)
    grad_spectrum = transformed(grad_long, table_ref, twist)
    saved_ref = stage.take(5)
    product = []
    for r, (re, im) in enumerate(grad_spectrum):
        k_re, k_im = saved_ref[2 * r], saved_ref[2 * r + 1]
        product.append((k_re * re + k_im * im, k_re * im - k_im * re))
    table_ref = stage.take(6)
    times = in_time(product, table_ref, twist)
    pairs_ref = stage.take(7)
    grad_mixed = [both(x + gain * y)[1] for x, y in zip(times, grad_long)]
    grad_pairs = anticausal(
        [x * swap(pairs_ref[phase]) for phase, x in enumerate(grad_mixed)], pair_weight
    )
    scale = 1.0 / math.sqrt(PHASES * quarter)
    for phase, at in enumerate(starts):
        x = grad_pairs[phase].astype(BF16)
        y = jnp.where(low, grad_query[phase], swap(times[phase]) * scale).astype(BF16)
        send_ref[:, at : at + share, :] = x.reshape(blocks, share, LANES)
        send_ref[:, rows + at : rows + at + share, :] = y.reshape(blocks, share, LANES)


def unpacked(blocks, order):
    half = blocks[0].shape[0]
    tiles = []
    for tile in range(len(blocks) // 2):
        top, bottom = pair(blocks[2 * tile].astype(F32), blocks[2 * tile + 1].astype(F32))
        tiles.append(jnp.concatenate([top, bottom], axis=0))
    return mm(order, jnp.concatenate(tiles, axis=1).astype(BF16))


def end_kernel(stage):
    recv_ref, order_ref = stage.take(0), stage.take(1)
    grad_ref, filter_ref = stage.out(0), stage.out(1)
    order = order_ref[...]
    blocks = recv_ref.shape[0]
    rows = recv_ref.shape[1] // 2
    sides = []
    for at in (0, rows):
        firsts, seconds = [], []
        for tile in range(blocks // 2):
            x, y = [recv_ref[2 * tile + i, at : at + rows].astype(F32) for i in range(2)]
            first, second = pair(x, y)
            firsts.append(first)
            seconds.append(second)
        for side in (firsts, seconds):
            sides.append(mm(order, jnp.concatenate(side, axis=1).astype(BF16)))
    key, value, query, taps = sides
    filter_ref[...] = taps
    stage.give(1)
    grad_ref[0] = query.astype(BF16)
    grad_ref[1] = key.astype(BF16)
    grad_ref[2] = value.astype(BF16)


def output_kernel(parts, stage):
    order, w_ref = stage.take(0)[...], stage.take(1)
    total = None
    for part in range(parts):
        gated_ref = stage.take(2 + part)
        block = unpacked([gated_ref[i] for i in range(gated_ref.shape[0])], order).astype(BF16)
        width = block.shape[1]
        term = mm(block, w_ref[part * width : (part + 1) * width, :])
        total = term if total is None else total + term
    stage.out(0)[...] = total.astype(BF16)


def partner(x, axis, mask):
    return lax.ppermute(x, axis, [(i, i ^ mask) for i in range(lax.axis_size(axis))])


def exchanged(x, axis):
    return lax.all_to_all(x, axis, split_axis=0, concat_axis=0, tiled=True)


def owner_layer(qkv, filt, skip_gain, short_weight, w_out, g_out):
    shape = jax.ShapeDtypeStruct
    seq_parts, ch_parts = lax.axis_size("seq"), lax.axis_size("ch")
    rows, width = qkv.shape[1], qkv.shape[2]
    tokens = seq_parts * rows
    quarter = tokens // PHASES
    order = row_order(rows)
    tables = jnp.asarray(phase_tables(tokens))
    tables_on, tables_back = Far(tables, [(0, 2), (4, 1)]), Far(tables, [(2, 2)])
    table_flops = 2 * 2 * 2 * 3 * tokens * tokens // PHASES * LANES
    product_flops = 2 * rows * width * width * ch_parts
    packed = shape((seq_parts, rows // 2, LANES), BF16)
    double = shape((seq_parts, 2 * rows, LANES), BF16)
    column = shape((rows, width), BF16)
    saved = shape((4 * PHASES, quarter, LANES), F32)
    weight, gain = Far(short_weight), Far(skip_gain[None, :])

    tile_cuts = [(at, 2) for at in range(0, seq_parts, 2)]
    (send,) = call(start_kernel, [Far(double, tile_cuts)], Far(qkv), Far(order), Far(filt))
    recv = exchanged(send, "seq")
    half_sums, w_kept, g_kept = call(
        first_product_kernel,
        [
            Near(shape((2, rows, width), BF16), kept=True),
            Near(w_out, kept=True),
            Near(g_out, kept=True),
        ],
        Far(g_out, into=2),
        Far(w_out, turned=(1, 3, 2, 0), into=1),
        flops=product_flops // 2,
    )
    half_sums = partner(half_sums, "ch", 1)
    across, own = call(
        second_product_kernel,
        [Near(column, kept=True), Near(shape((rows, width), F32), kept=True)],
        Near(g_kept),
        Near(w_kept),
        Near(half_sums),
        flops=product_flops // 2,
    )
    across = partner(across, "ch", 2)
    (send,) = call(sum_kernel, [Far(packed)], Far(order), Near(own), Near(across))
    grad_recv = exchanged(send, "seq")
    send, kept = call(
        forward_kernel,
        [Far(packed), Far(saved, [(0, 12), (12, 4)])],
        Near(recv),
        weight,
        gain,
        tables_on,
        tables_back,
        flops=table_flops,
    )
    gated = exchanged(send, "seq")
    (send,) = call(
        backward_kernel,
        [Far(double)],
        Far(grad_recv),
        weight,
        gain,
        Far(kept, [(12, 4)]),
        tables_on,
        Far(kept, [(0, 8)]),
        tables_back,
        Far(kept, [(8, 4)]),
        flops=table_flops,
    )
    grad_recv = exchanged(send, "seq")
    across = partner(gated, "ch", 2)
    near, far = partner(gated, "ch", 1), partner(across, "ch", 1)
    back_order = Far(order.T)
    (output,) = call(
        functools.partial(output_kernel, ch_parts),
        [Far(column)],
        back_order,
        Near(w_kept),
        Near(gated),
        Near(near),
        Near(across),
        Near(far),
        flops=product_flops,
    )
    grad_qkv, grad_filter = call(
        end_kernel,
        [Far(shape((3, rows, width), BF16)), Far(shape((rows, width), F32))],
        Near(grad_recv),
        back_order,
    )
    return (output, grad_qkv, grad_filter)


def local(qkv, filt, skip_gain, short_weight, w_out, g_out):
    seq_parts = lax.axis_size("seq")
    rows, width = qkv.shape[1], qkv.shape[2]
    fits = width == HALF * seq_parts and rows % HALF == 0 and rows * seq_parts <= 2048
    if fits and lax.axis_size("ch") == 4:
        return owner_layer(qkv, filt, skip_gain, short_weight, w_out, g_out)
    return spread_layer(qkv, filt, skip_gain, short_weight, w_out, g_out)


def solution(mesh):
    in_specs = (
        P(None, "seq", "ch"),
        P("seq", "ch"),
        P("ch"),
        P(None, None, "ch"),
        P(None, "ch"),
        P("seq", "ch"),
    )
    out_specs = (P("seq", "ch"), P(None, "seq", "ch"), P("seq", "ch"))
    return jax.shard_map(local, mesh=mesh, in_specs=in_specs, out_specs=out_specs, check_vma=False)
```

```python
import functools
import math

import jax
import jax.numpy as jnp
import numpy as np
from jax import lax
from jax.experimental import pallas as pl
from jax.experimental.pallas import tpu as pltpu
from jax.sharding import PartitionSpec as P

HIGHEST = lax.Precision.HIGHEST
TWO_PI = 2.0 * math.pi
LANES = 128
HALF = 64
PHASES = 4
BF16 = jnp.bfloat16
F32 = jnp.float32
VMEM_LIMIT = 24 * 1024 * 1024


def passed_along(block, axis, distance):
    devices = range(lax.axis_size(axis))
    route = [(i - distance, i) for i in devices if i - distance in devices]
    return lax.ppermute(block, axis, route)


def phase_pair(left_count, right_count, period, left_start, right_start):
    left_idx = lax.broadcasted_iota(jnp.int32, (left_count, right_count), 0) + left_start
    right_idx = lax.broadcasted_iota(jnp.int32, (left_count, right_count), 1) + right_start
    angle_all = (left_idx * right_idx % period).astype(jnp.float32) * (TWO_PI / period)
    return (jnp.cos(angle_all), jnp.sin(angle_all))


def contract(pattern, matrix, values):
    return jnp.einsum(
        pattern, matrix, values, precision=HIGHEST, preferred_element_type=jnp.float32
    )


def forward_spectrum(signal):
    seq_parts = lax.axis_size("seq")
    row_count = signal.shape[0]
    row_share = row_count // seq_parts
    period = 2 * seq_parts * row_count
    spread_in = lax.all_to_all(signal[None], "seq", split_axis=1, concat_axis=0, tiled=True)
    outer_cos, outer_sin = phase_pair(2 * seq_parts, seq_parts, 2 * seq_parts, 0, 0)
    section_re = contract("cp,prw->crw", outer_cos, spread_in)
    section_im = -contract("cp,prw->crw", outer_sin, spread_in)
    twist_cos, twist_sin = phase_pair(
        2 * seq_parts, row_share, period, 0, lax.axis_index("seq") * row_share
    )
    twist_cos = twist_cos[:, :, None]
    twist_sin = twist_sin[:, :, None]
    turned_re = section_re * twist_cos + section_im * twist_sin
    turned_im = section_im * twist_cos - section_re * twist_sin
    inner_cos, inner_sin = phase_pair(row_count, row_count, row_count, 0, 0)
    piece_re = lax.all_to_all(turned_re, "seq", split_axis=0, concat_axis=1, tiled=True)
    piece_im = lax.all_to_all(turned_im, "seq", split_axis=0, concat_axis=1, tiled=True)
    spec_re = contract("dm,cmk->cdk", inner_cos, piece_re) + contract(
        "dm,cmk->cdk", inner_sin, piece_im
    )
    spec_im = contract("dm,cmk->cdk", inner_cos, piece_im) - contract(
        "dm,cmk->cdk", inner_sin, piece_re
    )
    return (spec_re, spec_im)


def time_signal(spec_re, spec_im):
    seq_parts = lax.axis_size("seq")
    row_count = spec_re.shape[1]
    period = 2 * seq_parts * row_count
    inner_cos, inner_sin = phase_pair(row_count, row_count, row_count, 0, 0)
    back_re = contract("md,cdk->cmk", inner_cos, spec_re) - contract(
        "md,cdk->cmk", inner_sin, spec_im
    )
    back_im = contract("md,cdk->cmk", inner_cos, spec_im) + contract(
        "md,cdk->cmk", inner_sin, spec_re
    )
    twist_cos, twist_sin = phase_pair(2, row_count, period, 2 * lax.axis_index("seq"), 0)
    twist_cos = twist_cos[:, :, None]
    twist_sin = twist_sin[:, :, None]
    turned_re = back_re * twist_cos - back_im * twist_sin
    turned_im = back_im * twist_cos + back_re * twist_sin
    outer_cos, outer_sin = phase_pair(seq_parts, 2 * seq_parts, 2 * seq_parts, 0, 0)
    piece_re = lax.all_to_all(turned_re, "seq", split_axis=1, concat_axis=0, tiled=True)
    piece_im = lax.all_to_all(turned_im, "seq", split_axis=1, concat_axis=0, tiled=True)
    summed = contract("pc,crk->prk", outer_cos, piece_re) - contract(
        "pc,crk->prk", outer_sin, piece_im
    )
    returned = summed * (1.0 / period)
    return lax.all_to_all(returned, "seq", split_axis=0, concat_axis=1, tiled=True)[0]


def spread_layer(qkv, filt, skip_gain, short_weight, w_out, g_out):
    row_count = qkv.shape[1]
    slab_width = qkv.shape[2]
    tail_rows = passed_along(qkv[:, row_count - 2 :, :], "seq", 1)
    extended = jnp.concatenate([tail_rows, qkv], axis=1)
    short = (
        short_weight[:, 0, None, :] * extended[:, 2:, :]
        + short_weight[:, 1, None, :] * extended[:, 1:-1, :]
        + short_weight[:, 2, None, :] * extended[:, :-2, :]
    )
    query_gate = short[0]
    key_short = short[1]
    value_short = short[2]
    mixed = key_short * value_short
    both_re, both_im = forward_spectrum(jnp.concatenate([mixed, filt], axis=1))
    signal_re = both_re[:, :, :slab_width]
    signal_im = both_im[:, :, :slab_width]
    kernel_re = both_re[:, :, slab_width:]
    kernel_im = both_im[:, :, slab_width:]
    conv_out = time_signal(
        signal_re * kernel_re - signal_im * kernel_im, signal_re * kernel_im + signal_im * kernel_re
    )
    long_out = conv_out + skip_gain * mixed
    gated_out = (query_gate * long_out).astype(jnp.bfloat16)
    projected = jnp.dot(
        lax.all_gather(gated_out, "ch", axis=1, tiled=True),
        w_out,
        preferred_element_type=jnp.float32,
    )
    output = projected.astype(jnp.bfloat16)
    grad_all = lax.all_gather(g_out, "ch", axis=1, tiled=True)
    rows_all = lax.all_to_all(w_out, "ch", split_axis=0, concat_axis=1, tiled=True)
    grad_gated = lax.dot_general(
        grad_all, rows_all, (((1,), (1,)), ((), ())), preferred_element_type=jnp.float32
    )
    grad_long = grad_gated * query_gate
    grad_query = grad_gated * long_out
    grad_re, grad_im = forward_spectrum(grad_long)
    pair_re = jnp.concatenate(
        [kernel_re * grad_re + kernel_im * grad_im, signal_re * grad_re + signal_im * grad_im],
        axis=2,
    )
    pair_im = jnp.concatenate(
        [kernel_re * grad_im - kernel_im * grad_re, signal_re * grad_im - signal_im * grad_re],
        axis=2,
    )
    pair_time = time_signal(pair_re, pair_im)
    grad_mixed = pair_time[:, :slab_width] + skip_gain * grad_long
    token_total = lax.axis_size("seq") * row_count
    grad_filter = pair_time[:, slab_width:] * (1.0 / math.sqrt(token_total))
    grad_short = jnp.stack([grad_query, grad_mixed * value_short, grad_mixed * key_short])
    head_rows = passed_along(grad_short[:, :2, :], "seq", -1)
    extended_grad = jnp.concatenate([grad_short, head_rows], axis=1)
    grad_qkv = (
        short_weight[:, 0, None, :] * extended_grad[:, :-2, :]
        + short_weight[:, 1, None, :] * extended_grad[:, 1:-1, :]
        + short_weight[:, 2, None, :] * extended_grad[:, 2:, :]
    ).astype(jnp.bfloat16)
    return (output, grad_qkv, grad_filter)


def split_bf16(values):
    high = values.astype(np.float32).astype(jnp.bfloat16)
    low = (values - high.astype(np.float64)).astype(np.float32).astype(jnp.bfloat16)
    return high, low


def phase_tables(tokens):
    quarter = tokens // PHASES
    freq = 2 * np.arange(quarter)[:, None] + 1
    turn = math.pi / (2 * tokens)
    angle = (freq * PHASES * np.arange(quarter)[None, :] % (4 * tokens)) * turn
    forward = np.concatenate([np.cos(angle), -np.sin(angle)], axis=1)
    backward = np.concatenate([np.cos(angle).T, -np.sin(angle).T], axis=1) / tokens
    angle = freq * np.arange(PHASES)[None, :] * turn
    twist = np.concatenate([np.cos(angle), np.sin(angle)], axis=1)
    twist = np.pad(twist, ((0, 0), (0, LANES - 2 * PHASES)))
    high, rest = split_bf16(twist)
    last = split_bf16(twist - high.astype(np.float64) - rest.astype(np.float64))[0]
    tables = np.zeros((8, quarter, 2 * quarter), jnp.bfloat16)
    tables[0], tables[1] = split_bf16(forward)
    tables[2], tables[3] = split_bf16(backward)
    for i, term in enumerate((high, rest, last)):
        tables[4, :, i * LANES : (i + 1) * LANES] = term
    return tables


def row_order(rows):
    order = np.zeros((rows, rows), np.float32)
    share = rows // PHASES
    for phase in range(PHASES):
        for j in range(share):
            order[phase * share + j, PHASES * j + phase] = 1.0
    return order.astype(jnp.bfloat16)


def mm(a, b):
    return lax.dot_general(a, b, (((1,), (0,)), ((), ())), preferred_element_type=F32)


def low_lanes(shape):
    return lax.broadcasted_iota(jnp.int32, shape, 1) < HALF


def swap(x):
    return pltpu.roll(x, HALF, 1)


def order_mask(parts, column=0):
    return ((lax.axis_index("ch") ^ column) % 2) * (parts - 1)


class Near:
    def __init__(self, array, kept=False):
        self.array = array
        self.kept = kept


class Far:
    def __init__(self, array, cuts=None, turned=(), into=None, placed=False):
        self.array = array
        self.turned = turned
        self.into = into
        self.placed = placed
        if placed:
            cuts = [(i, 1) for i in range(array.shape[0])]
        if turned:
            step = array.shape[0] // len(turned)
            cuts = [(mask * step, step) for mask in turned]
        self.cuts = cuts or [(0, array.shape[0])]
        self.rows = sum(count for _, count in self.cuts)


class Stage:
    def __init__(self, items, count_in, refs):
        arrays, scratch = list(refs[: len(items)]), list(refs[len(items) :])
        sems = scratch.pop()
        self.count_in = count_in
        self.held, self.copies, self.waiting = [], [], []
        used = 0
        for i, (item, array) in enumerate(zip(items, arrays)):
            group = []
            if isinstance(item, Near):
                self.held.append(array)
            else:
                held = scratch.pop(0) if item.into is None else arrays[count_in + item.into]
                self.held.append(held)
                at = 0
                for cut, (start, count) in enumerate(item.cuts):
                    there = held.at[pl.ds(start if item.turned else at, count)]
                    at += count
                    if item.turned:
                        mask = item.turned[cut]
                        start = pl.multiple_of((lax.axis_index("ch") ^ mask) * count, count)
                    if item.placed:
                        start = start ^ order_mask(array.shape[0])
                    here = array.at[pl.ds(start, count)]
                    if i >= count_in:
                        here, there = there, here
                    group.append(pltpu.make_async_copy(here, there, sems.at[used]))
                    used += 1
            self.copies.append(group)
            self.waiting.append(set(range(len(group))))
        self.given = set()

    def bring(self, index):
        for copy in self.copies[index]:
            copy.start()

    def take(self, index, cut=None):
        for i in sorted(self.waiting[index]):
            if cut is None or cut == i:
                self.copies[index][i].wait()
                self.waiting[index].discard(i)
        return self.held[index]

    def out(self, index):
        return self.held[self.count_in + index]

    def give(self, index, cut=None):
        for i, copy in enumerate(self.copies[self.count_in + index]):
            if (index, i) not in self.given and cut in (None, i):
                copy.start()
                self.given.add((index, i))


def staged(kernel, items, count_in, *refs):
    stage = Stage(items, count_in, refs)
    for i in range(count_in):
        stage.bring(i)
    kernel(stage)
    for i in range(count_in):
        stage.take(i)
    for i in range(len(items) - count_in):
        stage.give(i)
    for i in range(len(items) - count_in):
        stage.take(count_in + i)


def in_hbm(x):
    return pltpu.with_memory_space_constraint(x, pltpu.HBM)


def result_of(x):
    make = pltpu.HBM if isinstance(x, Far) else pltpu.VMEM if x.kept else jax.ShapeDtypeStruct
    return make(x.array.shape, x.array.dtype)


def call(kernel, results, *args, flops=0):
    items = list(args) + list(results)
    specs, scratch, used = [], [], 0
    for item in items:
        near = isinstance(item, Near)
        specs.append(pl.BlockSpec(memory_space=pltpu.VMEM if near else pltpu.HBM))
        if not near:
            used += len(item.cuts)
            if item.into is None:
                scratch.append(pltpu.VMEM((item.rows, *item.array.shape[1:]), item.array.dtype))
    moved = sum(math.prod(x.array.shape) * x.array.dtype.itemsize for x in items)
    return pl.pallas_call(
        functools.partial(staged, kernel, items, len(args)),
        out_shape=[result_of(x) for x in results],
        in_specs=specs[: len(args)],
        out_specs=specs[len(args) :],
        scratch_shapes=scratch + [pltpu.SemaphoreType.DMA((max(used, 1),))],
        compiler_params=pltpu.CompilerParams(vmem_limit_bytes=VMEM_LIMIT),
        cost_estimate=pl.CostEstimate(flops=flops, bytes_accessed=moved, transcendentals=0),
    )(*[x.array if isinstance(x, Near) else in_hbm(x.array) for x in args])


def lane_tile(x, index):
    return x[:, index * LANES : (index + 1) * LANES]


def pair(first, second):
    low = low_lanes(first.shape)
    return jnp.where(low, first, swap(second)), jnp.where(low, swap(first), second)


def both(x):
    turned, low = swap(x), low_lanes(x.shape)
    return jnp.where(low, x, turned), jnp.where(low, turned, x)


def start_kernel(stage):
    send_ref, qkv_ref, order = stage.out(0), stage.take(0), stage.take(1)[...]
    rows = qkv_ref.shape[1]
    query, key, value = [mm(order, qkv_ref[i]) for i in range(3)]
    taps = mm(order, stage.take(2)[...].astype(BF16))
    for tile in range(query.shape[1] // LANES):
        for row, (x, y) in enumerate(((key, value), (query, taps))):
            here = slice(row * rows, (row + 1) * rows)
            x, y = pair(lane_tile(x, tile), lane_tile(y, tile))
            send_ref[2 * tile, here] = x.astype(BF16)
            send_ref[2 * tile + 1, here] = y.astype(BF16)
        stage.give(0, 2 * tile)
        stage.give(0, 2 * tile + 1)


def partial_product(g, w_ref, mask):
    width = g.shape[1]
    w = w_ref[mask * width : (mask + 1) * width, :]
    return lax.dot_general(g, w, (((1,), (1,)), ((), ())), preferred_element_type=F32)


def first_product_kernel(stage):
    g, out_ref = stage.take(0)[...], stage.out(0)
    for i, mask in enumerate((1, 3)):
        out_ref[i] = partial_product(g, stage.take(1, i), mask).astype(BF16)


def second_product_kernel(stage):
    w_ref, g, near_ref = stage.take(1), stage.take(0)[...], stage.take(2)
    across_ref, own_ref = stage.out(0), stage.out(1)
    across = partial_product(g, w_ref, 2) + near_ref[1].astype(F32)
    across_ref[...] = across.astype(BF16)
    stage.give(0)
    own_ref[...] = partial_product(g, w_ref, 0) + near_ref[0].astype(F32)


def sum_kernel(stage):
    send_ref, order = stage.out(0), stage.take(0)[...]
    total = stage.take(1)[...] + stage.take(2)[...].astype(F32)
    total = mm(order, total.astype(BF16))
    half = total.shape[0] // 2
    for tile in range(total.shape[1] // LANES):
        t = lane_tile(total, tile)
        x, y = pair(t[:half], t[half:])
        send_ref[2 * tile] = x.astype(BF16)
        send_ref[2 * tile + 1] = y.astype(BF16)


def spread_phases(parts):
    (a_re, a_im), (b_re, b_im), (c_re, c_im), (d_re, d_im) = parts
    s_re, s_im, t_re, t_im = a_re + c_re, a_im + c_im, a_re - c_re, a_im - c_im
    u_re, u_im, v_re, v_im = b_re + d_re, b_im + d_im, b_re - d_re, b_im - d_im
    return [
        (s_re + u_re, s_im + u_im),
        (t_re + v_im, t_im - v_re),
        (s_re - u_re, s_im - u_im),
        (t_re - v_im, t_im + v_re),
    ]


def gather_phases(parts):
    (a_re, a_im), (b_re, b_im), (c_re, c_im), (d_re, d_im) = parts
    s_re, s_im, t_re, t_im = a_re + c_re, a_im + c_im, a_re - c_re, a_im - c_im
    u_re, u_im, v_re, v_im = b_re + d_re, b_im + d_im, b_re - d_re, b_im - d_im
    return [
        (s_re + u_re, s_im + u_im),
        (t_re - v_im, t_im + v_re),
        (s_re - u_re, s_im - u_im),
        (t_re + v_im, t_im - v_re),
    ]


def rows_of(ref, start, count, mask=None):
    if mask is None:
        return ref[:, start : start + count, :].reshape(ref.shape[0] * count, ref.shape[2])
    blocks = [ref[i ^ mask, start : start + count, :] for i in range(ref.shape[0])]
    return jnp.concatenate(blocks, axis=0)


def turned_back(re, im, twist, phase):
    if phase == 0:
        return re, im
    c, s = twist[:, phase : phase + 1], twist[:, PHASES + phase : PHASES + phase + 1]
    return re * c + im * s, im * c - re * s


def turned_on(re, im, twist, phase):
    if phase == 0:
        return re, im
    c, s = twist[:, phase : phase + 1], twist[:, PHASES + phase : PHASES + phase + 1]
    return re * c - im * s, re * s + im * c


def lane_tile(x, index):
    return x[:, index * LANES : (index + 1) * LANES]


def causal(parts, weight):
    rows = lax.broadcasted_iota(jnp.int32, parts[0].shape, 0)
    two, three = [jnp.where(rows == 0, 0.0, pltpu.roll(parts[p], 1, 0)) for p in (2, 3)]
    once, twice = [three, *parts[:3]], [two, three, *parts[:2]]
    return [
        weight[0:1] * x + weight[1:2] * y + weight[2:3] * z for x, y, z in zip(parts, once, twice)
    ]


def anticausal(parts, weight):
    count = parts[0].shape[0]
    rows = lax.broadcasted_iota(jnp.int32, parts[0].shape, 0)
    zero, one = [
        jnp.where(rows == count - 1, 0.0, pltpu.roll(parts[p], count - 1, 0)) for p in (0, 1)
    ]
    once, twice = [*parts[1:], zero], [*parts[2:], zero, one]
    return [
        weight[0:1] * x + weight[1:2] * y + weight[2:3] * z for x, y, z in zip(parts, once, twice)
    ]


def halves(x):
    high = x.astype(BF16)
    return high, (x - high.astype(F32)).astype(BF16)


def twiddles(table_ref):
    terms = [table_ref[2, :, i * LANES : (i + 1) * LANES].astype(F32) for i in range(3)]
    return terms[0] + (terms[1] + terms[2])


def transformed(parts, table_ref, twist):
    quarter = parts[0].shape[0]
    high, rest = halves(jnp.concatenate(parts, axis=1))
    sides = []
    for side in (slice(0, quarter), slice(quarter, 2 * quarter)):
        fh, fl = table_ref[0, :, side], table_ref[1, :, side]
        sides.append(mm(fh, high) + mm(fl, high) + mm(fh, rest))
    turned = []
    for phase in range(PHASES):
        re, im = [lane_tile(side, phase) for side in sides]
        turned.append(turned_back(re, im, twist, phase))
    return spread_phases(turned)


def in_time(spectrum, table_ref, twist):
    bh, bl = table_ref[0], table_ref[1]
    parts = []
    for phase, (re, im) in enumerate(gather_phases(spectrum)):
        parts.append(jnp.concatenate(turned_on(re, im, twist, phase), axis=0))
    high, rest = halves(jnp.concatenate(parts, axis=1))
    t = mm(bh, high) + mm(bl, high) + mm(bh, rest)
    return [lane_tile(t, phase) for phase in range(PHASES)]


def own_weights(weight_ref, gain_ref):
    place = lax.axis_index("seq")
    lanes = pl.ds(pl.multiple_of(place // 2 * LANES, LANES), LANES)
    odd = place % 2 == 1

    def mine(x):
        return jnp.where(odd, swap(x), x)

    weights = [mine(weight_ref[i, :, lanes]) for i in range(3)]
    gain = both(mine(gain_ref[:, lanes]))[0]
    low = low_lanes(weights[0].shape)
    only = (lax.broadcasted_iota(jnp.int32, weights[0].shape, 0) == 0).astype(F32)
    pair_weight = jnp.where(low, weights[1], swap(weights[2]))
    query_weight = jnp.where(low, weights[0], only)
    return pair_weight, query_weight, gain


def forward_kernel(stage):
    recv_ref, weight_ref, gain_ref = [stage.take(i) for i in range(3)]
    gated_ref, saved_ref = stage.out(0), stage.out(1)
    blocks = recv_ref.shape[0]
    rows = recv_ref.shape[1] // 2
    share = rows // PHASES
    quarter = blocks * share
    low = low_lanes((quarter, LANES))
    pair_weight, query_weight, gain = own_weights(weight_ref, gain_ref)

    starts = [phase * share for phase in range(PHASES)]
    mask = order_mask(blocks)
    pairs = [rows_of(recv_ref, at, share, mask).astype(F32) for at in starts]
    pairs = causal(pairs, pair_weight)
    gates = [rows_of(recv_ref, rows + at, share, mask).astype(F32) for at in starts]
    gates = causal(gates, query_weight)
    for phase in range(PHASES):
        saved_ref[8 + phase] = pairs[phase]
    mixed = [x * swap(x) for x in pairs]
    query = [both(x)[0] for x in gates]
    table_ref = stage.take(3)
    twist = twiddles(table_ref)
    spectrum = transformed([jnp.where(low, x, y) for x, y in zip(mixed, gates)], table_ref, twist)
    product = []
    for r, (re, im) in enumerate(spectrum):
        saved_ref[2 * r] = re
        saved_ref[2 * r + 1] = im
        other_re, other_im = swap(re), swap(im)
        product.append((re * other_re - im * other_im, re * other_im + im * other_re))
    stage.give(1, 0)
    conv = in_time(product, stage.take(4), twist)
    long_out = [x + gain * y for x, y in zip(conv, mixed)]
    gated = [x * y for x, y in zip(query, long_out)]
    for phase in range(PHASES // 2):
        t = jnp.where(low, gated[phase], gated[phase + 2]).astype(BF16)
        gated_ref[:, starts[phase] : starts[phase] + share, :] = t.reshape(blocks, share, LANES)
    for phase in range(PHASES):
        saved_ref[12 + phase] = jnp.where(low, query[phase], long_out[phase])
    stage.give(1, 1)


def backward_kernel(stage):
    grad_ref, weight_ref, gain_ref, gates_ref = [stage.take(i) for i in range(4)]
    send_ref = stage.out(0)
    blocks = grad_ref.shape[0]
    share = grad_ref.shape[1] // 2
    rows = PHASES * share
    quarter = blocks * share
    low = low_lanes((quarter, LANES))
    pair_weight, query_weight, gain = own_weights(weight_ref, gain_ref)

    starts = [phase * share for phase in range(PHASES)]
    packed = [rows_of(grad_ref, at, share).astype(F32) for at in starts[:2]]
    grad_gated = [both(x)[i] for i in range(2) for x in packed]
    gates = [both(gates_ref[phase]) for phase in range(PHASES)]
    grad_long = [x * y for x, (y, _) in zip(grad_gated, gates)]
    grad_query = anticausal([x * y for x, (_, y) in zip(grad_gated, gates)], query_weight)
    table_ref = stage.take(4)
    twist = twiddles(table_ref)
    grad_spectrum = transformed(grad_long, table_ref, twist)
    saved_ref = stage.take(5)
    product = []
    for r, (re, im) in enumerate(grad_spectrum):
        k_re, k_im = saved_ref[2 * r], saved_ref[2 * r + 1]
        product.append((k_re * re + k_im * im, k_re * im - k_im * re))
    table_ref = stage.take(6)
    times = in_time(product, table_ref, twist)
    pairs_ref = stage.take(7)
    grad_mixed = [both(x + gain * y)[1] for x, y in zip(times, grad_long)]
    grad_pairs = anticausal(
        [x * swap(pairs_ref[phase]) for phase, x in enumerate(grad_mixed)], pair_weight
    )
    scale = 1.0 / math.sqrt(PHASES * quarter)
    for phase, at in enumerate(starts):
        x = grad_pairs[phase].astype(BF16)
        y = jnp.where(low, grad_query[phase], swap(times[phase]) * scale).astype(BF16)
        send_ref[:, at : at + share, :] = x.reshape(blocks, share, LANES)
        send_ref[:, rows + at : rows + at + share, :] = y.reshape(blocks, share, LANES)


def unpacked(blocks, order):
    half = blocks[0].shape[0]
    tiles = []
    for tile in range(len(blocks) // 2):
        top, bottom = pair(blocks[2 * tile].astype(F32), blocks[2 * tile + 1].astype(F32))
        tiles.append(jnp.concatenate([top, bottom], axis=0))
    return mm(order, jnp.concatenate(tiles, axis=1).astype(BF16))


def end_kernel(stage):
    recv_ref, order_ref = stage.take(0), stage.take(1)
    grad_ref, filter_ref = stage.out(0), stage.out(1)
    order = order_ref[...]
    blocks = recv_ref.shape[0]
    rows = recv_ref.shape[1] // 2
    mask = order_mask(blocks)
    sides = []
    for at in (0, rows):
        firsts, seconds = [], []
        for tile in range(blocks // 2):
            x, y = [recv_ref[(2 * tile + i) ^ mask, at : at + rows].astype(F32) for i in range(2)]
            first, second = pair(x, y)
            firsts.append(first)
            seconds.append(second)
        for side in (firsts, seconds):
            sides.append(mm(order, jnp.concatenate(side, axis=1).astype(BF16)))
    key, value, query, taps = sides
    filter_ref[...] = taps
    stage.give(1)
    grad_ref[0] = query.astype(BF16)
    grad_ref[1] = key.astype(BF16)
    grad_ref[2] = value.astype(BF16)


def output_kernel(parts, stage):
    order, w_ref = stage.take(0)[...], stage.take(1)
    total = None
    for part in range(parts):
        gated_ref = stage.take(2 + part)
        blocks = gated_ref.shape[0]
        mask = order_mask(blocks, part)
        block = unpacked([gated_ref[i ^ mask] for i in range(blocks)], order).astype(BF16)
        width = block.shape[1]
        term = mm(block, w_ref[part * width : (part + 1) * width, :])
        total = term if total is None else total + term
    stage.out(0)[...] = total.astype(BF16)


def partner(x, axis, mask):
    return lax.ppermute(x, axis, [(i, i ^ mask) for i in range(lax.axis_size(axis))])


def exchanged(x):
    places, columns = lax.axis_size("seq"), lax.axis_size("ch")
    groups = []
    for column in range(columns):
        group = [place * columns + column for place in range(places)]
        groups.append(group[::-1] if column % 2 else group)
    return lax.all_to_all(
        x, ("seq", "ch"), split_axis=0, concat_axis=0, tiled=True, axis_index_groups=groups
    )


def owner_layer(qkv, filt, skip_gain, short_weight, w_out, g_out):
    shape = jax.ShapeDtypeStruct
    seq_parts, ch_parts = lax.axis_size("seq"), lax.axis_size("ch")
    rows, width = qkv.shape[1], qkv.shape[2]
    tokens = seq_parts * rows
    quarter = tokens // PHASES
    order = row_order(rows)
    tables = jnp.asarray(phase_tables(tokens))
    tables_on, tables_back = Far(tables, [(0, 2), (4, 1)]), Far(tables, [(2, 2)])
    table_flops = 2 * 2 * 2 * 3 * tokens * tokens // PHASES * LANES
    product_flops = 2 * rows * width * width * ch_parts
    packed = shape((seq_parts, rows // 2, LANES), BF16)
    double = shape((seq_parts, 2 * rows, LANES), BF16)
    column = shape((rows, width), BF16)
    saved = shape((4 * PHASES, quarter, LANES), F32)
    weight, gain = Far(short_weight), Far(skip_gain[None, :])

    (send,) = call(start_kernel, [Far(double, placed=True)], Far(qkv), Far(order), Far(filt))
    recv = exchanged(send)
    half_sums, w_kept, g_kept = call(
        first_product_kernel,
        [
            Near(shape((2, rows, width), BF16), kept=True),
            Near(w_out, kept=True),
            Near(g_out, kept=True),
        ],
        Far(g_out, into=2),
        Far(w_out, turned=(1, 3, 2, 0), into=1),
        flops=product_flops // 2,
    )
    half_sums = partner(half_sums, "ch", 1)
    across, own = call(
        second_product_kernel,
        [Near(column, kept=True), Near(shape((rows, width), F32), kept=True)],
        Near(g_kept),
        Near(w_kept),
        Near(half_sums),
        flops=product_flops // 2,
    )
    across = partner(across, "ch", 2)
    (send,) = call(sum_kernel, [Far(packed, placed=True)], Far(order), Near(own), Near(across))
    grad_recv = exchanged(send)
    send, kept = call(
        forward_kernel,
        [Far(packed, placed=True), Far(saved, [(0, 12), (12, 4)])],
        Near(recv),
        weight,
        gain,
        tables_on,
        tables_back,
        flops=table_flops,
    )
    gated = exchanged(send)
    (send,) = call(
        backward_kernel,
        [Far(double, placed=True)],
        Far(grad_recv, placed=True),
        weight,
        gain,
        Far(kept, [(12, 4)]),
        tables_on,
        Far(kept, [(0, 8)]),
        tables_back,
        Far(kept, [(8, 4)]),
        flops=table_flops,
    )
    grad_recv = exchanged(send)
    across = partner(gated, "ch", 2)
    near, far = partner(gated, "ch", 1), partner(across, "ch", 1)
    back_order = Far(order.T)
    (output,) = call(
        functools.partial(output_kernel, ch_parts),
        [Far(column)],
        back_order,
        Near(w_kept),
        Near(gated),
        Near(near),
        Near(across),
        Near(far),
        flops=product_flops,
    )
    grad_qkv, grad_filter = call(
        end_kernel,
        [Far(shape((3, rows, width), BF16)), Far(shape((rows, width), F32))],
        Near(grad_recv),
        back_order,
    )
    return (output, grad_qkv, grad_filter)


def local(qkv, filt, skip_gain, short_weight, w_out, g_out):
    seq_parts = lax.axis_size("seq")
    rows, width = qkv.shape[1], qkv.shape[2]
    fits = width == HALF * seq_parts and rows % HALF == 0 and rows * seq_parts <= 2048
    if fits and lax.axis_size("ch") == 4:
        return owner_layer(qkv, filt, skip_gain, short_weight, w_out, g_out)
    return spread_layer(qkv, filt, skip_gain, short_weight, w_out, g_out)


def solution(mesh):
    in_specs = (
        P(None, "seq", "ch"),
        P("seq", "ch"),
        P("ch"),
        P(None, None, "ch"),
        P(None, "ch"),
        P("seq", "ch"),
    )
    out_specs = (P("seq", "ch"), P(None, "seq", "ch"), P("seq", "ch"))
    return jax.shard_map(local, mesh=mesh, in_specs=in_specs, out_specs=out_specs, check_vma=False)
```

```python
import functools
import math

import jax
import jax.numpy as jnp
import numpy as np
from jax import lax
from jax.experimental import pallas as pl
from jax.experimental.pallas import tpu as pltpu
from jax.sharding import PartitionSpec as P

HIGHEST = lax.Precision.HIGHEST
TWO_PI = 2.0 * math.pi
LANES = 128
HALF = 64
PHASES = 4
BF16 = jnp.bfloat16
F32 = jnp.float32
VMEM_LIMIT = 24 * 1024 * 1024


def passed_along(block, axis, distance):
    devices = range(lax.axis_size(axis))
    route = [(i - distance, i) for i in devices if i - distance in devices]
    return lax.ppermute(block, axis, route)


def phase_pair(left_count, right_count, period, left_start, right_start):
    left_idx = lax.broadcasted_iota(jnp.int32, (left_count, right_count), 0) + left_start
    right_idx = lax.broadcasted_iota(jnp.int32, (left_count, right_count), 1) + right_start
    angle_all = (left_idx * right_idx % period).astype(jnp.float32) * (TWO_PI / period)
    return (jnp.cos(angle_all), jnp.sin(angle_all))


def contract(pattern, matrix, values):
    return jnp.einsum(
        pattern, matrix, values, precision=HIGHEST, preferred_element_type=jnp.float32
    )


def forward_spectrum(signal):
    seq_parts = lax.axis_size("seq")
    row_count = signal.shape[0]
    row_share = row_count // seq_parts
    period = 2 * seq_parts * row_count
    spread_in = lax.all_to_all(signal[None], "seq", split_axis=1, concat_axis=0, tiled=True)
    outer_cos, outer_sin = phase_pair(2 * seq_parts, seq_parts, 2 * seq_parts, 0, 0)
    section_re = contract("cp,prw->crw", outer_cos, spread_in)
    section_im = -contract("cp,prw->crw", outer_sin, spread_in)
    twist_cos, twist_sin = phase_pair(
        2 * seq_parts, row_share, period, 0, lax.axis_index("seq") * row_share
    )
    twist_cos = twist_cos[:, :, None]
    twist_sin = twist_sin[:, :, None]
    turned_re = section_re * twist_cos + section_im * twist_sin
    turned_im = section_im * twist_cos - section_re * twist_sin
    inner_cos, inner_sin = phase_pair(row_count, row_count, row_count, 0, 0)
    piece_re = lax.all_to_all(turned_re, "seq", split_axis=0, concat_axis=1, tiled=True)
    piece_im = lax.all_to_all(turned_im, "seq", split_axis=0, concat_axis=1, tiled=True)
    spec_re = contract("dm,cmk->cdk", inner_cos, piece_re) + contract(
        "dm,cmk->cdk", inner_sin, piece_im
    )
    spec_im = contract("dm,cmk->cdk", inner_cos, piece_im) - contract(
        "dm,cmk->cdk", inner_sin, piece_re
    )
    return (spec_re, spec_im)


def time_signal(spec_re, spec_im):
    seq_parts = lax.axis_size("seq")
    row_count = spec_re.shape[1]
    period = 2 * seq_parts * row_count
    inner_cos, inner_sin = phase_pair(row_count, row_count, row_count, 0, 0)
    back_re = contract("md,cdk->cmk", inner_cos, spec_re) - contract(
        "md,cdk->cmk", inner_sin, spec_im
    )
    back_im = contract("md,cdk->cmk", inner_cos, spec_im) + contract(
        "md,cdk->cmk", inner_sin, spec_re
    )
    twist_cos, twist_sin = phase_pair(2, row_count, period, 2 * lax.axis_index("seq"), 0)
    twist_cos = twist_cos[:, :, None]
    twist_sin = twist_sin[:, :, None]
    turned_re = back_re * twist_cos - back_im * twist_sin
    turned_im = back_im * twist_cos + back_re * twist_sin
    outer_cos, outer_sin = phase_pair(seq_parts, 2 * seq_parts, 2 * seq_parts, 0, 0)
    piece_re = lax.all_to_all(turned_re, "seq", split_axis=1, concat_axis=0, tiled=True)
    piece_im = lax.all_to_all(turned_im, "seq", split_axis=1, concat_axis=0, tiled=True)
    summed = contract("pc,crk->prk", outer_cos, piece_re) - contract(
        "pc,crk->prk", outer_sin, piece_im
    )
    returned = summed * (1.0 / period)
    return lax.all_to_all(returned, "seq", split_axis=0, concat_axis=1, tiled=True)[0]


def spread_layer(qkv, filt, skip_gain, short_weight, w_out, g_out):
    row_count = qkv.shape[1]
    slab_width = qkv.shape[2]
    tail_rows = passed_along(qkv[:, row_count - 2 :, :], "seq", 1)
    extended = jnp.concatenate([tail_rows, qkv], axis=1)
    short = (
        short_weight[:, 0, None, :] * extended[:, 2:, :]
        + short_weight[:, 1, None, :] * extended[:, 1:-1, :]
        + short_weight[:, 2, None, :] * extended[:, :-2, :]
    )
    query_gate = short[0]
    key_short = short[1]
    value_short = short[2]
    mixed = key_short * value_short
    both_re, both_im = forward_spectrum(jnp.concatenate([mixed, filt], axis=1))
    signal_re = both_re[:, :, :slab_width]
    signal_im = both_im[:, :, :slab_width]
    kernel_re = both_re[:, :, slab_width:]
    kernel_im = both_im[:, :, slab_width:]
    conv_out = time_signal(
        signal_re * kernel_re - signal_im * kernel_im, signal_re * kernel_im + signal_im * kernel_re
    )
    long_out = conv_out + skip_gain * mixed
    gated_out = (query_gate * long_out).astype(jnp.bfloat16)
    projected = jnp.dot(
        lax.all_gather(gated_out, "ch", axis=1, tiled=True),
        w_out,
        preferred_element_type=jnp.float32,
    )
    output = projected.astype(jnp.bfloat16)
    grad_all = lax.all_gather(g_out, "ch", axis=1, tiled=True)
    rows_all = lax.all_to_all(w_out, "ch", split_axis=0, concat_axis=1, tiled=True)
    grad_gated = lax.dot_general(
        grad_all, rows_all, (((1,), (1,)), ((), ())), preferred_element_type=jnp.float32
    )
    grad_long = grad_gated * query_gate
    grad_query = grad_gated * long_out
    grad_re, grad_im = forward_spectrum(grad_long)
    pair_re = jnp.concatenate(
        [kernel_re * grad_re + kernel_im * grad_im, signal_re * grad_re + signal_im * grad_im],
        axis=2,
    )
    pair_im = jnp.concatenate(
        [kernel_re * grad_im - kernel_im * grad_re, signal_re * grad_im - signal_im * grad_re],
        axis=2,
    )
    pair_time = time_signal(pair_re, pair_im)
    grad_mixed = pair_time[:, :slab_width] + skip_gain * grad_long
    token_total = lax.axis_size("seq") * row_count
    grad_filter = pair_time[:, slab_width:] * (1.0 / math.sqrt(token_total))
    grad_short = jnp.stack([grad_query, grad_mixed * value_short, grad_mixed * key_short])
    head_rows = passed_along(grad_short[:, :2, :], "seq", -1)
    extended_grad = jnp.concatenate([grad_short, head_rows], axis=1)
    grad_qkv = (
        short_weight[:, 0, None, :] * extended_grad[:, :-2, :]
        + short_weight[:, 1, None, :] * extended_grad[:, 1:-1, :]
        + short_weight[:, 2, None, :] * extended_grad[:, 2:, :]
    ).astype(jnp.bfloat16)
    return (output, grad_qkv, grad_filter)


def split_bf16(values):
    high = values.astype(np.float32).astype(jnp.bfloat16)
    low = (values - high.astype(np.float64)).astype(np.float32).astype(jnp.bfloat16)
    return high, low


def phase_tables(tokens):
    quarter = tokens // PHASES
    freq = 2 * np.arange(quarter)[:, None] + 1
    turn = math.pi / (2 * tokens)
    angle = (freq * PHASES * np.arange(quarter)[None, :] % (4 * tokens)) * turn
    forward = np.concatenate([np.cos(angle), -np.sin(angle)], axis=1)
    backward = np.concatenate([np.cos(angle).T, -np.sin(angle).T], axis=1) / tokens
    angle = freq * np.arange(PHASES)[None, :] * turn
    twist = np.concatenate([np.cos(angle), np.sin(angle)], axis=1)
    twist = np.pad(twist, ((0, 0), (0, LANES - 2 * PHASES)))
    high, rest = split_bf16(twist)
    last = split_bf16(twist - high.astype(np.float64) - rest.astype(np.float64))[0]
    tables = np.zeros((8, quarter, 2 * quarter), jnp.bfloat16)
    tables[0], tables[1] = split_bf16(forward)
    tables[2], tables[3] = split_bf16(backward)
    for i, term in enumerate((high, rest, last)):
        tables[4, :, i * LANES : (i + 1) * LANES] = term
    return tables


def row_order(rows):
    order = np.zeros((rows, rows), np.float32)
    share = rows // PHASES
    for phase in range(PHASES):
        for j in range(share):
            order[phase * share + j, PHASES * j + phase] = 1.0
    return order.astype(jnp.bfloat16)


def mm(a, b):
    return lax.dot_general(a, b, (((1,), (0,)), ((), ())), preferred_element_type=F32)


def low_lanes(shape):
    return lax.broadcasted_iota(jnp.int32, shape, 1) < HALF


def swap(x):
    return pltpu.roll(x, HALF, 1)


class Near:
    def __init__(self, array, kept=False):
        self.array = array
        self.kept = kept


class Far:
    def __init__(self, array, cuts=None, turned=(), into=None):
        self.array = array
        self.turned = turned
        self.into = into
        if turned:
            step = array.shape[0] // len(turned)
            cuts = [(mask * step, step) for mask in turned]
        self.cuts = cuts or [(0, array.shape[0])]
        self.rows = sum(count for _, count in self.cuts)


class Stage:
    def __init__(self, items, count_in, refs):
        arrays, scratch = list(refs[: len(items)]), list(refs[len(items) :])
        sems = scratch.pop()
        self.count_in = count_in
        self.held, self.copies, self.waiting = [], [], []
        used = 0
        for i, (item, array) in enumerate(zip(items, arrays)):
            group = []
            if isinstance(item, Near):
                self.held.append(array)
            else:
                held = scratch.pop(0) if item.into is None else arrays[count_in + item.into]
                self.held.append(held)
                at = 0
                for cut, (start, count) in enumerate(item.cuts):
                    there = held.at[pl.ds(start if item.turned else at, count)]
                    at += count
                    if item.turned:
                        mask = item.turned[cut]
                        start = pl.multiple_of((lax.axis_index("ch") ^ mask) * count, count)
                    here = array.at[pl.ds(start, count)]
                    if i >= count_in:
                        here, there = there, here
                    group.append(pltpu.make_async_copy(here, there, sems.at[used]))
                    used += 1
            self.copies.append(group)
            self.waiting.append(set(range(len(group))))
        self.given = set()

    def bring(self, index):
        for copy in self.copies[index]:
            copy.start()

    def take(self, index, cut=None):
        for i in sorted(self.waiting[index]):
            if cut is None or cut == i:
                self.copies[index][i].wait()
                self.waiting[index].discard(i)
        return self.held[index]

    def out(self, index):
        return self.held[self.count_in + index]

    def give(self, index, cut=None):
        for i, copy in enumerate(self.copies[self.count_in + index]):
            if (index, i) not in self.given and cut in (None, i):
                copy.start()
                self.given.add((index, i))


def staged(kernel, items, count_in, *refs):
    stage = Stage(items, count_in, refs)
    for i in range(count_in):
        stage.bring(i)
    kernel(stage)
    for i in range(count_in):
        stage.take(i)
    for i in range(len(items) - count_in):
        stage.give(i)
    for i in range(len(items) - count_in):
        stage.take(count_in + i)


def in_hbm(x):
    return pltpu.with_memory_space_constraint(x, pltpu.HBM)


def result_of(x):
    make = pltpu.HBM if isinstance(x, Far) else pltpu.VMEM if x.kept else jax.ShapeDtypeStruct
    return make(x.array.shape, x.array.dtype)


def call(kernel, results, *args, flops=0):
    items = list(args) + list(results)
    specs, scratch, used = [], [], 0
    for item in items:
        near = isinstance(item, Near)
        specs.append(pl.BlockSpec(memory_space=pltpu.VMEM if near else pltpu.HBM))
        if not near:
            used += len(item.cuts)
            if item.into is None:
                scratch.append(pltpu.VMEM((item.rows, *item.array.shape[1:]), item.array.dtype))
    moved = sum(math.prod(x.array.shape) * x.array.dtype.itemsize for x in items)
    return pl.pallas_call(
        functools.partial(staged, kernel, items, len(args)),
        out_shape=[result_of(x) for x in results],
        in_specs=specs[: len(args)],
        out_specs=specs[len(args) :],
        scratch_shapes=scratch + [pltpu.SemaphoreType.DMA((max(used, 1),))],
        compiler_params=pltpu.CompilerParams(vmem_limit_bytes=VMEM_LIMIT),
        cost_estimate=pl.CostEstimate(flops=flops, bytes_accessed=moved, transcendentals=0),
    )(*[x.array if isinstance(x, Near) else in_hbm(x.array) for x in args])


def lane_tile(x, index):
    return x[:, index * LANES : (index + 1) * LANES]


def pair(first, second):
    low = low_lanes(first.shape)
    return jnp.where(low, first, swap(second)), jnp.where(low, swap(first), second)


def both(x):
    turned, low = swap(x), low_lanes(x.shape)
    return jnp.where(low, x, turned), jnp.where(low, turned, x)


def start_kernel(stage):
    send_ref, qkv_ref, order = stage.out(0), stage.take(0), stage.take(1)[...]
    rows = qkv_ref.shape[1]
    query, key, value = [mm(order, qkv_ref[i]) for i in range(3)]
    taps = mm(order, stage.take(2)[...].astype(BF16))
    for tile in range(query.shape[1] // LANES):
        for row, (x, y) in enumerate(((key, value), (query, taps))):
            here = slice(row * rows, (row + 1) * rows)
            x, y = pair(lane_tile(x, tile), lane_tile(y, tile))
            send_ref[2 * tile, here] = x.astype(BF16)
            send_ref[2 * tile + 1, here] = y.astype(BF16)
        stage.give(0, tile)


def partial_product(g, w_ref, mask):
    width = g.shape[1]
    w = w_ref[mask * width : (mask + 1) * width, :]
    return lax.dot_general(g, w, (((1,), (1,)), ((), ())), preferred_element_type=F32)


def first_product_kernel(stage):
    g, out_ref = stage.take(0)[...], stage.out(0)
    for i, mask in enumerate((1, 3)):
        out_ref[i] = partial_product(g, stage.take(1, i), mask).astype(BF16)


def second_product_kernel(stage):
    w_ref, g, near_ref = stage.take(1), stage.take(0)[...], stage.take(2)
    across_ref, own_ref = stage.out(0), stage.out(1)
    across = partial_product(g, w_ref, 2) + near_ref[1].astype(F32)
    across_ref[...] = across.astype(BF16)
    stage.give(0)
    own_ref[...] = partial_product(g, w_ref, 0) + near_ref[0].astype(F32)


def sum_kernel(stage):
    send_ref, order = stage.out(0), stage.take(0)[...]
    total = stage.take(1)[...] + stage.take(2)[...].astype(F32)
    total = mm(order, total.astype(BF16))
    half = total.shape[0] // 2
    for tile in range(total.shape[1] // LANES):
        t = lane_tile(total, tile)
        x, y = pair(t[:half], t[half:])
        send_ref[2 * tile] = x.astype(BF16)
        send_ref[2 * tile + 1] = y.astype(BF16)


def spread_phases(parts):
    (a_re, a_im), (b_re, b_im), (c_re, c_im), (d_re, d_im) = parts
    s_re, s_im, t_re, t_im = a_re + c_re, a_im + c_im, a_re - c_re, a_im - c_im
    u_re, u_im, v_re, v_im = b_re + d_re, b_im + d_im, b_re - d_re, b_im - d_im
    return [
        (s_re + u_re, s_im + u_im),
        (t_re + v_im, t_im - v_re),
        (s_re - u_re, s_im - u_im),
        (t_re - v_im, t_im + v_re),
    ]


def gather_phases(parts):
    (a_re, a_im), (b_re, b_im), (c_re, c_im), (d_re, d_im) = parts
    s_re, s_im, t_re, t_im = a_re + c_re, a_im + c_im, a_re - c_re, a_im - c_im
    u_re, u_im, v_re, v_im = b_re + d_re, b_im + d_im, b_re - d_re, b_im - d_im
    return [
        (s_re + u_re, s_im + u_im),
        (t_re - v_im, t_im + v_re),
        (s_re - u_re, s_im - u_im),
        (t_re + v_im, t_im - v_re),
    ]


def rows_of(ref, start, count):
    block = ref[:, start : start + count, :]
    return block.reshape(ref.shape[0] * count, ref.shape[2])


def turned_back(re, im, twist, phase):
    if phase == 0:
        return re, im
    c, s = twist[:, phase : phase + 1], twist[:, PHASES + phase : PHASES + phase + 1]
    return re * c + im * s, im * c - re * s


def turned_on(re, im, twist, phase):
    if phase == 0:
        return re, im
    c, s = twist[:, phase : phase + 1], twist[:, PHASES + phase : PHASES + phase + 1]
    return re * c - im * s, re * s + im * c


def lane_tile(x, index):
    return x[:, index * LANES : (index + 1) * LANES]


def causal(parts, weight):
    rows = lax.broadcasted_iota(jnp.int32, parts[0].shape, 0)
    two, three = [jnp.where(rows == 0, 0.0, pltpu.roll(parts[p], 1, 0)) for p in (2, 3)]
    once, twice = [three, *parts[:3]], [two, three, *parts[:2]]
    return [
        weight[0:1] * x + weight[1:2] * y + weight[2:3] * z for x, y, z in zip(parts, once, twice)
    ]


def anticausal(parts, weight):
    count = parts[0].shape[0]
    rows = lax.broadcasted_iota(jnp.int32, parts[0].shape, 0)
    zero, one = [
        jnp.where(rows == count - 1, 0.0, pltpu.roll(parts[p], count - 1, 0)) for p in (0, 1)
    ]
    once, twice = [*parts[1:], zero], [*parts[2:], zero, one]
    return [
        weight[0:1] * x + weight[1:2] * y + weight[2:3] * z for x, y, z in zip(parts, once, twice)
    ]


def halves(x):
    high = x.astype(BF16)
    return high, (x - high.astype(F32)).astype(BF16)


def twiddles(table_ref):
    terms = [table_ref[2, :, i * LANES : (i + 1) * LANES].astype(F32) for i in range(3)]
    return terms[0] + (terms[1] + terms[2])


def transformed(parts, table_ref, twist):
    quarter = parts[0].shape[0]
    high, rest = halves(jnp.concatenate(parts, axis=1))
    sides = []
    for side in (slice(0, quarter), slice(quarter, 2 * quarter)):
        fh, fl = table_ref[0, :, side], table_ref[1, :, side]
        sides.append(mm(fh, high) + mm(fl, high) + mm(fh, rest))
    turned = []
    for phase in range(PHASES):
        re, im = [lane_tile(side, phase) for side in sides]
        turned.append(turned_back(re, im, twist, phase))
    return spread_phases(turned)


def in_time(spectrum, table_ref, twist):
    bh, bl = table_ref[0], table_ref[1]
    parts = []
    for phase, (re, im) in enumerate(gather_phases(spectrum)):
        parts.append(jnp.concatenate(turned_on(re, im, twist, phase), axis=0))
    high, rest = halves(jnp.concatenate(parts, axis=1))
    t = mm(bh, high) + mm(bl, high) + mm(bh, rest)
    return [lane_tile(t, phase) for phase in range(PHASES)]


def own_weights(weight_ref, gain_ref):
    place = lax.axis_index("seq")
    lanes = pl.ds(pl.multiple_of(place // 2 * LANES, LANES), LANES)
    odd = place % 2 == 1

    def mine(x):
        return jnp.where(odd, swap(x), x)

    weights = [mine(weight_ref[i, :, lanes]) for i in range(3)]
    gain = both(mine(gain_ref[:, lanes]))[0]
    low = low_lanes(weights[0].shape)
    only = (lax.broadcasted_iota(jnp.int32, weights[0].shape, 0) == 0).astype(F32)
    pair_weight = jnp.where(low, weights[1], swap(weights[2]))
    query_weight = jnp.where(low, weights[0], only)
    return pair_weight, query_weight, gain


def forward_kernel(stage):
    recv_ref, weight_ref, gain_ref = [stage.take(i) for i in range(3)]
    send_ref, saved_ref = stage.out(0), stage.out(1)
    half = send_ref.shape[1] // 2
    send_ref[:, half:, :] = stage.take(5)[...]
    blocks = recv_ref.shape[0]
    rows = recv_ref.shape[1] // 2
    share = rows // PHASES
    quarter = blocks * share
    low = low_lanes((quarter, LANES))
    pair_weight, query_weight, gain = own_weights(weight_ref, gain_ref)

    starts = [phase * share for phase in range(PHASES)]
    pairs = causal([rows_of(recv_ref, at, share).astype(F32) for at in starts], pair_weight)
    gates = causal([rows_of(recv_ref, rows + at, share).astype(F32) for at in starts], query_weight)
    for phase in range(PHASES):
        saved_ref[8 + phase] = pairs[phase]
    mixed = [x * swap(x) for x in pairs]
    query = [both(x)[0] for x in gates]
    table_ref = stage.take(3)
    twist = twiddles(table_ref)
    spectrum = transformed([jnp.where(low, x, y) for x, y in zip(mixed, gates)], table_ref, twist)
    product = []
    for r, (re, im) in enumerate(spectrum):
        saved_ref[2 * r] = re
        saved_ref[2 * r + 1] = im
        other_re, other_im = swap(re), swap(im)
        product.append((re * other_re - im * other_im, re * other_im + im * other_re))
    conv = in_time(product, stage.take(4), twist)
    long_out = [x + gain * y for x, y in zip(conv, mixed)]
    gated = [x * y for x, y in zip(query, long_out)]
    for phase in range(PHASES // 2):
        t = jnp.where(low, gated[phase], gated[phase + 2]).astype(BF16)
        send_ref[:, starts[phase] : starts[phase] + share, :] = t.reshape(blocks, share, LANES)
    stage.give(0)
    for phase in range(PHASES):
        saved_ref[12 + phase] = jnp.where(low, query[phase], long_out[phase])


def backward_kernel(stage):
    grad_ref, weight_ref, gain_ref, saved_ref = [stage.take(i) for i in range(4)]
    send_ref = stage.out(0)
    blocks = grad_ref.shape[0]
    rows = grad_ref.shape[1]
    share = rows // PHASES
    stage.out(1)[...] = grad_ref[:, : rows // 2, :]
    quarter = blocks * share
    low = low_lanes((quarter, LANES))
    pair_weight, query_weight, gain = own_weights(weight_ref, gain_ref)

    starts = [phase * share for phase in range(PHASES)]
    packed = [rows_of(grad_ref, at, share).astype(F32) for at in starts[2:]]
    grad_gated = [both(x)[i] for i in range(2) for x in packed]
    gates = [both(saved_ref[12 + phase]) for phase in range(PHASES)]
    grad_long = [x * y for x, (y, _) in zip(grad_gated, gates)]
    grad_query = anticausal([x * y for x, (_, y) in zip(grad_gated, gates)], query_weight)
    table_ref = stage.take(4)
    twist = twiddles(table_ref)
    grad_spectrum = transformed(grad_long, table_ref, twist)
    product = []
    for r, (re, im) in enumerate(grad_spectrum):
        k_re, k_im = saved_ref[2 * r], saved_ref[2 * r + 1]
        product.append((k_re * re + k_im * im, k_re * im - k_im * re))
    times = in_time(product, stage.take(5), twist)
    grad_mixed = [both(x + gain * y)[1] for x, y in zip(times, grad_long)]
    grad_pairs = anticausal(
        [x * swap(saved_ref[8 + phase]) for phase, x in enumerate(grad_mixed)], pair_weight
    )
    scale = 1.0 / math.sqrt(PHASES * quarter)
    for phase, at in enumerate(starts):
        x = grad_pairs[phase].astype(BF16)
        y = jnp.where(low, grad_query[phase], swap(times[phase]) * scale).astype(BF16)
        send_ref[:, at : at + share, :] = x.reshape(blocks, share, LANES)
        send_ref[:, rows + at : rows + at + share, :] = y.reshape(blocks, share, LANES)


def unpacked(blocks, order):
    half = blocks[0].shape[0]
    tiles = []
    for tile in range(len(blocks) // 2):
        top, bottom = pair(blocks[2 * tile].astype(F32), blocks[2 * tile + 1].astype(F32))
        tiles.append(jnp.concatenate([top, bottom], axis=0))
    return mm(order, jnp.concatenate(tiles, axis=1).astype(BF16))


def end_kernel(stage):
    recv_ref, order_ref = stage.take(0), stage.take(1)
    grad_ref, filter_ref = stage.out(0), stage.out(1)
    order = order_ref[...]
    blocks = recv_ref.shape[0]
    rows = recv_ref.shape[1] // 2
    sides = []
    for at in (0, rows):
        firsts, seconds = [], []
        for tile in range(blocks // 2):
            x, y = [recv_ref[2 * tile + i, at : at + rows].astype(F32) for i in range(2)]
            first, second = pair(x, y)
            firsts.append(first)
            seconds.append(second)
        for side in (firsts, seconds):
            sides.append(mm(order, jnp.concatenate(side, axis=1).astype(BF16)))
    key, value, query, taps = sides
    filter_ref[...] = taps
    stage.give(1)
    grad_ref[0] = query.astype(BF16)
    grad_ref[1] = key.astype(BF16)
    grad_ref[2] = value.astype(BF16)


def output_kernel(parts, stage):
    order, w_ref = stage.take(0)[...], stage.take(1)
    total = None
    for part in range(parts):
        gated_ref = stage.take(2 + part)
        block = unpacked([gated_ref[i] for i in range(gated_ref.shape[0])], order).astype(BF16)
        width = block.shape[1]
        term = mm(block, w_ref[part * width : (part + 1) * width, :])
        total = term if total is None else total + term
    stage.out(0)[...] = total.astype(BF16)


def partner(x, axis, mask):
    return lax.ppermute(x, axis, [(i, i ^ mask) for i in range(lax.axis_size(axis))])


def exchanged(x, axis):
    return lax.all_to_all(x, axis, split_axis=0, concat_axis=0, tiled=True)


def owner_layer(qkv, filt, skip_gain, short_weight, w_out, g_out):
    shape = jax.ShapeDtypeStruct
    seq_parts, ch_parts = lax.axis_size("seq"), lax.axis_size("ch")
    rows, width = qkv.shape[1], qkv.shape[2]
    tokens = seq_parts * rows
    quarter = tokens // PHASES
    order = row_order(rows)
    tables = jnp.asarray(phase_tables(tokens))
    table_flops = 2 * 2 * 2 * 3 * tokens * tokens // PHASES * LANES
    product_flops = 2 * rows * width * width * ch_parts
    packed = shape((seq_parts, rows // 2, LANES), BF16)
    double = shape((seq_parts, 2 * rows, LANES), BF16)
    column = shape((rows, width), BF16)
    saved = shape((4 * PHASES, quarter, LANES), F32)
    gain = skip_gain[None, :]

    tile_cuts = [(at, 2) for at in range(0, seq_parts, 2)]
    (send,) = call(start_kernel, [Far(double, tile_cuts)], Far(qkv), Far(order), Far(filt))
    recv = exchanged(send, "seq")
    half_sums, w_kept, g_kept = call(
        first_product_kernel,
        [
            Near(shape((2, rows, width), BF16), kept=True),
            Near(w_out, kept=True),
            Near(g_out, kept=True),
        ],
        Far(g_out, into=2),
        Far(w_out, turned=(1, 3, 2, 0), into=1),
        flops=product_flops // 2,
    )
    half_sums = partner(half_sums, "ch", 1)
    across, own = call(
        second_product_kernel,
        [Near(column, kept=True), Near(shape((rows, width), F32), kept=True)],
        Near(g_kept),
        Near(w_kept),
        Near(half_sums),
        flops=product_flops // 2,
    )
    across = partner(across, "ch", 2)
    def pinned(x):
        return Near(x, kept=True)

    grad_gated, tables_on, tables_back, weight, gain = call(
        sum_kernel,
        [
            pinned(packed),
            pinned(shape((3, *tables.shape[1:]), BF16)),
            pinned(shape((2, *tables.shape[1:]), BF16)),
            pinned(short_weight),
            pinned(gain),
        ],
        Far(order),
        Near(own),
        Near(across),
        Far(tables, [(0, 2), (4, 1)], into=1),
        Far(tables, [(2, 2)], into=2),
        Far(short_weight, into=3),
        Far(gain, into=4),
    )
    send, saved = call(
        forward_kernel,
        [Far(shape((seq_parts, rows, LANES), BF16)), pinned(saved)],
        Near(recv),
        Near(weight),
        Near(gain),
        Near(tables_on),
        Near(tables_back),
        Near(grad_gated),
        flops=table_flops,
    )
    swapped = exchanged(send, "seq")
    send, gated = call(
        backward_kernel,
        [Far(double), pinned(packed)],
        Near(swapped),
        Near(weight),
        Near(gain),
        Near(saved),
        Near(tables_on),
        Near(tables_back),
        flops=table_flops,
    )
    grad_recv = exchanged(send, "seq")
    across = partner(gated, "ch", 2)
    near, far = partner(gated, "ch", 1), partner(across, "ch", 1)
    back_order = Far(order.T)
    (output,) = call(
        functools.partial(output_kernel, ch_parts),
        [Far(column)],
        back_order,
        Near(w_kept),
        Near(gated),
        Near(near),
        Near(across),
        Near(far),
        flops=product_flops,
    )
    grad_qkv, grad_filter = call(
        end_kernel,
        [Far(shape((3, rows, width), BF16)), Far(shape((rows, width), F32))],
        Near(grad_recv),
        back_order,
    )
    return (output, grad_qkv, grad_filter)


def local(qkv, filt, skip_gain, short_weight, w_out, g_out):
    seq_parts = lax.axis_size("seq")
    rows, width = qkv.shape[1], qkv.shape[2]
    fits = width == HALF * seq_parts and rows % HALF == 0 and rows * seq_parts <= 2048
    if fits and lax.axis_size("ch") == 4:
        return owner_layer(qkv, filt, skip_gain, short_weight, w_out, g_out)
    return spread_layer(qkv, filt, skip_gain, short_weight, w_out, g_out)


def solution(mesh):
    in_specs = (
        P(None, "seq", "ch"),
        P("seq", "ch"),
        P("ch"),
        P(None, None, "ch"),
        P(None, "ch"),
        P("seq", "ch"),
    )
    out_specs = (P("seq", "ch"), P(None, "seq", "ch"), P("seq", "ch"))
    return jax.shard_map(local, mesh=mesh, in_specs=in_specs, out_specs=out_specs, check_vma=False)
```

```python
import functools
import math

import jax
import jax.numpy as jnp
import numpy as np
from jax import lax
from jax.experimental import pallas as pl
from jax.experimental.pallas import tpu as pltpu
from jax.sharding import PartitionSpec as P

HIGHEST = lax.Precision.HIGHEST
TWO_PI = 2.0 * math.pi
LANES = 128
HALF = 64
PHASES = 4
BF16 = jnp.bfloat16
F32 = jnp.float32
VMEM_LIMIT = 24 * 1024 * 1024


def passed_along(block, axis, distance):
    devices = range(lax.axis_size(axis))
    route = [(i - distance, i) for i in devices if i - distance in devices]
    return lax.ppermute(block, axis, route)


def phase_pair(left_count, right_count, period, left_start, right_start):
    left_idx = lax.broadcasted_iota(jnp.int32, (left_count, right_count), 0) + left_start
    right_idx = lax.broadcasted_iota(jnp.int32, (left_count, right_count), 1) + right_start
    angle_all = (left_idx * right_idx % period).astype(jnp.float32) * (TWO_PI / period)
    return (jnp.cos(angle_all), jnp.sin(angle_all))


def contract(pattern, matrix, values):
    return jnp.einsum(
        pattern, matrix, values, precision=HIGHEST, preferred_element_type=jnp.float32
    )


def forward_spectrum(signal):
    seq_parts = lax.axis_size("seq")
    row_count = signal.shape[0]
    row_share = row_count // seq_parts
    period = 2 * seq_parts * row_count
    spread_in = lax.all_to_all(signal[None], "seq", split_axis=1, concat_axis=0, tiled=True)
    outer_cos, outer_sin = phase_pair(2 * seq_parts, seq_parts, 2 * seq_parts, 0, 0)
    section_re = contract("cp,prw->crw", outer_cos, spread_in)
    section_im = -contract("cp,prw->crw", outer_sin, spread_in)
    twist_cos, twist_sin = phase_pair(
        2 * seq_parts, row_share, period, 0, lax.axis_index("seq") * row_share
    )
    twist_cos = twist_cos[:, :, None]
    twist_sin = twist_sin[:, :, None]
    turned_re = section_re * twist_cos + section_im * twist_sin
    turned_im = section_im * twist_cos - section_re * twist_sin
    inner_cos, inner_sin = phase_pair(row_count, row_count, row_count, 0, 0)
    piece_re = lax.all_to_all(turned_re, "seq", split_axis=0, concat_axis=1, tiled=True)
    piece_im = lax.all_to_all(turned_im, "seq", split_axis=0, concat_axis=1, tiled=True)
    spec_re = contract("dm,cmk->cdk", inner_cos, piece_re) + contract(
        "dm,cmk->cdk", inner_sin, piece_im
    )
    spec_im = contract("dm,cmk->cdk", inner_cos, piece_im) - contract(
        "dm,cmk->cdk", inner_sin, piece_re
    )
    return (spec_re, spec_im)


def time_signal(spec_re, spec_im):
    seq_parts = lax.axis_size("seq")
    row_count = spec_re.shape[1]
    period = 2 * seq_parts * row_count
    inner_cos, inner_sin = phase_pair(row_count, row_count, row_count, 0, 0)
    back_re = contract("md,cdk->cmk", inner_cos, spec_re) - contract(
        "md,cdk->cmk", inner_sin, spec_im
    )
    back_im = contract("md,cdk->cmk", inner_cos, spec_im) + contract(
        "md,cdk->cmk", inner_sin, spec_re
    )
    twist_cos, twist_sin = phase_pair(2, row_count, period, 2 * lax.axis_index("seq"), 0)
    twist_cos = twist_cos[:, :, None]
    twist_sin = twist_sin[:, :, None]
    turned_re = back_re * twist_cos - back_im * twist_sin
    turned_im = back_im * twist_cos + back_re * twist_sin
    outer_cos, outer_sin = phase_pair(seq_parts, 2 * seq_parts, 2 * seq_parts, 0, 0)
    piece_re = lax.all_to_all(turned_re, "seq", split_axis=1, concat_axis=0, tiled=True)
    piece_im = lax.all_to_all(turned_im, "seq", split_axis=1, concat_axis=0, tiled=True)
    summed = contract("pc,crk->prk", outer_cos, piece_re) - contract(
        "pc,crk->prk", outer_sin, piece_im
    )
    returned = summed * (1.0 / period)
    return lax.all_to_all(returned, "seq", split_axis=0, concat_axis=1, tiled=True)[0]


def spread_layer(qkv, filt, skip_gain, short_weight, w_out, g_out):
    row_count = qkv.shape[1]
    slab_width = qkv.shape[2]
    tail_rows = passed_along(qkv[:, row_count - 2 :, :], "seq", 1)
    extended = jnp.concatenate([tail_rows, qkv], axis=1)
    short = (
        short_weight[:, 0, None, :] * extended[:, 2:, :]
        + short_weight[:, 1, None, :] * extended[:, 1:-1, :]
        + short_weight[:, 2, None, :] * extended[:, :-2, :]
    )
    query_gate = short[0]
    key_short = short[1]
    value_short = short[2]
    mixed = key_short * value_short
    both_re, both_im = forward_spectrum(jnp.concatenate([mixed, filt], axis=1))
    signal_re = both_re[:, :, :slab_width]
    signal_im = both_im[:, :, :slab_width]
    kernel_re = both_re[:, :, slab_width:]
    kernel_im = both_im[:, :, slab_width:]
    conv_out = time_signal(
        signal_re * kernel_re - signal_im * kernel_im, signal_re * kernel_im + signal_im * kernel_re
    )
    long_out = conv_out + skip_gain * mixed
    gated_out = (query_gate * long_out).astype(jnp.bfloat16)
    projected = jnp.dot(
        lax.all_gather(gated_out, "ch", axis=1, tiled=True),
        w_out,
        preferred_element_type=jnp.float32,
    )
    output = projected.astype(jnp.bfloat16)
    grad_all = lax.all_gather(g_out, "ch", axis=1, tiled=True)
    rows_all = lax.all_to_all(w_out, "ch", split_axis=0, concat_axis=1, tiled=True)
    grad_gated = lax.dot_general(
        grad_all, rows_all, (((1,), (1,)), ((), ())), preferred_element_type=jnp.float32
    )
    grad_long = grad_gated * query_gate
    grad_query = grad_gated * long_out
    grad_re, grad_im = forward_spectrum(grad_long)
    pair_re = jnp.concatenate(
        [kernel_re * grad_re + kernel_im * grad_im, signal_re * grad_re + signal_im * grad_im],
        axis=2,
    )
    pair_im = jnp.concatenate(
        [kernel_re * grad_im - kernel_im * grad_re, signal_re * grad_im - signal_im * grad_re],
        axis=2,
    )
    pair_time = time_signal(pair_re, pair_im)
    grad_mixed = pair_time[:, :slab_width] + skip_gain * grad_long
    token_total = lax.axis_size("seq") * row_count
    grad_filter = pair_time[:, slab_width:] * (1.0 / math.sqrt(token_total))
    grad_short = jnp.stack([grad_query, grad_mixed * value_short, grad_mixed * key_short])
    head_rows = passed_along(grad_short[:, :2, :], "seq", -1)
    extended_grad = jnp.concatenate([grad_short, head_rows], axis=1)
    grad_qkv = (
        short_weight[:, 0, None, :] * extended_grad[:, :-2, :]
        + short_weight[:, 1, None, :] * extended_grad[:, 1:-1, :]
        + short_weight[:, 2, None, :] * extended_grad[:, 2:, :]
    ).astype(jnp.bfloat16)
    return (output, grad_qkv, grad_filter)


def split_bf16(values):
    high = values.astype(np.float32).astype(jnp.bfloat16)
    low = (values - high.astype(np.float64)).astype(np.float32).astype(jnp.bfloat16)
    return high, low


def phase_tables(tokens):
    quarter = tokens // PHASES
    freq = 2 * np.arange(quarter)[:, None] + 1
    turn = math.pi / (2 * tokens)
    angle = (freq * PHASES * np.arange(quarter)[None, :] % (4 * tokens)) * turn
    forward = np.concatenate([np.cos(angle), -np.sin(angle)], axis=1)
    backward = np.concatenate([np.cos(angle).T, -np.sin(angle).T], axis=1) / tokens
    angle = freq * np.arange(PHASES)[None, :] * turn
    twist = np.concatenate([np.cos(angle), np.sin(angle)], axis=1)
    twist = np.pad(twist, ((0, 0), (0, LANES - 2 * PHASES)))
    high, rest = split_bf16(twist)
    last = split_bf16(twist - high.astype(np.float64) - rest.astype(np.float64))[0]
    tables = np.zeros((8, quarter, 2 * quarter), jnp.bfloat16)
    tables[0], tables[1] = split_bf16(forward)
    tables[2], tables[3] = split_bf16(backward)
    for i, term in enumerate((high, rest, last)):
        tables[4, :, i * LANES : (i + 1) * LANES] = term
    return tables


def row_order(rows, back=False):
    to, at = [lax.broadcasted_iota(jnp.int32, (rows, rows), int(i != back)) for i in range(2)]
    share = rows // PHASES
    wanted = (to & (share - 1)) * PHASES + lax.shift_right_logical(to, share.bit_length() - 1)
    return jnp.where(wanted == at, 1.0, 0.0).astype(BF16)


def mm(a, b):
    return lax.dot_general(a, b, (((1,), (0,)), ((), ())), preferred_element_type=F32)


def low_lanes(shape):
    return lax.broadcasted_iota(jnp.int32, shape, 1) < HALF


def swap(x):
    return pltpu.roll(x, HALF, 1)


class Near:
    def __init__(self, array, kept=False):
        self.array = array
        self.kept = kept


class Far:
    def __init__(self, array, cuts=None, turned=(), into=None, axis=0):
        self.array = array
        self.turned = turned
        self.into = into
        self.axis = axis
        if turned:
            step = array.shape[0] // len(turned)
            cuts = [(mask * step, step) for mask in turned]
        self.cuts = cuts or [(0, array.shape[axis])]
        self.shape = list(array.shape)
        self.shape[axis] = sum(count for _, count in self.cuts)


class Stage:
    def __init__(self, items, count_in, refs):
        arrays, scratch = list(refs[: len(items)]), list(refs[len(items) :])
        sems = scratch.pop()
        self.count_in = count_in
        self.held, self.copies, self.waiting = [], [], []
        used = 0
        for i, (item, array) in enumerate(zip(items, arrays)):
            group = []
            if isinstance(item, Near):
                self.held.append(array)
            else:
                held = scratch.pop(0) if item.into is None else arrays[count_in + item.into]
                self.held.append(held)
                at = 0
                for cut, (start, count) in enumerate(item.cuts):
                    lead = (slice(None),) * item.axis
                    there = held.at[(*lead, pl.ds(start if item.turned else at, count))]
                    at += count
                    if item.turned:
                        mask = item.turned[cut]
                        start = pl.multiple_of((lax.axis_index("ch") ^ mask) * count, count)
                    here = array.at[(*lead, pl.ds(start, count))]
                    if i >= count_in:
                        here, there = there, here
                    group.append(pltpu.make_async_copy(here, there, sems.at[used]))
                    used += 1
            self.copies.append(group)
            self.waiting.append(set(range(len(group))))
        self.given = set()

    def bring(self, index):
        for copy in self.copies[index]:
            copy.start()

    def take(self, index, cut=None):
        for i in sorted(self.waiting[index]):
            if cut is None or cut == i:
                self.copies[index][i].wait()
                self.waiting[index].discard(i)
        return self.held[index]

    def out(self, index):
        return self.held[self.count_in + index]

    def give(self, index, cut=None):
        for i, copy in enumerate(self.copies[self.count_in + index]):
            if (index, i) not in self.given and cut in (None, i):
                copy.start()
                self.given.add((index, i))


def staged(kernel, items, count_in, *refs):
    stage = Stage(items, count_in, refs)
    for i in range(count_in):
        stage.bring(i)
    kernel(stage)
    for i in range(count_in):
        stage.take(i)
    for i in range(len(items) - count_in):
        stage.give(i)
    for i in range(len(items) - count_in):
        stage.take(count_in + i)


def operand_of(x):
    if isinstance(x, Near) and not x.kept:
        return x.array
    space = pltpu.VMEM if isinstance(x, Near) else pltpu.HBM
    return pltpu.with_memory_space_constraint(x.array, space)


def result_of(x):
    make = pltpu.HBM if isinstance(x, Far) else pltpu.VMEM if x.kept else jax.ShapeDtypeStruct
    return make(x.array.shape, x.array.dtype)


def call(kernel, results, *args, flops=0):
    items = list(args) + list(results)
    specs, scratch, used = [], [], 0
    for item in items:
        near = isinstance(item, Near)
        specs.append(pl.BlockSpec(memory_space=pltpu.VMEM if near else pltpu.HBM))
        if not near:
            used += len(item.cuts)
            if item.into is None:
                scratch.append(pltpu.VMEM(tuple(item.shape), item.array.dtype))
    moved = sum(math.prod(x.array.shape) * x.array.dtype.itemsize for x in items)
    return pl.pallas_call(
        functools.partial(staged, kernel, items, len(args)),
        out_shape=[result_of(x) for x in results],
        in_specs=specs[: len(args)],
        out_specs=specs[len(args) :],
        scratch_shapes=scratch + [pltpu.SemaphoreType.DMA((max(used, 1),))],
        compiler_params=pltpu.CompilerParams(vmem_limit_bytes=VMEM_LIMIT),
        cost_estimate=pl.CostEstimate(flops=flops, bytes_accessed=moved, transcendentals=0),
    )(*[operand_of(x) for x in args])


def lane_tile(x, index):
    return x[:, index * LANES : (index + 1) * LANES]


def pair(first, second):
    low = low_lanes(first.shape)
    return jnp.where(low, first, swap(second)), jnp.where(low, swap(first), second)


def both(x):
    turned, low = swap(x), low_lanes(x.shape)
    return jnp.where(low, x, turned), jnp.where(low, turned, x)


def start_kernel(stage):
    send_ref, qkv_ref = stage.out(0), stage.take(0)
    rows = qkv_ref.shape[1]
    order = row_order(rows)
    query, key, value = [mm(order, qkv_ref[i]) for i in range(3)]
    taps = mm(order, stage.take(1)[...].astype(BF16))
    for tile in range(query.shape[1] // LANES):
        for row, (x, y) in enumerate(((key, value), (query, taps))):
            here = slice(row * rows, (row + 1) * rows)
            x, y = pair(lane_tile(x, tile), lane_tile(y, tile))
            send_ref[2 * tile, here] = x.astype(BF16)
            send_ref[2 * tile + 1, here] = y.astype(BF16)
        stage.give(0, tile)


def partial_product(g, w_ref, mask):
    width = g.shape[1]
    w = w_ref[mask * width : (mask + 1) * width, :]
    return lax.dot_general(g, w, (((1,), (1,)), ((), ())), preferred_element_type=F32)


def first_product_kernel(stage):
    g, out_ref = stage.take(0)[...], stage.out(0)
    for i, mask in enumerate((1, 3)):
        out_ref[i] = partial_product(g, stage.take(1, i), mask).astype(BF16)


def second_product_kernel(stage):
    w_ref, g, near_ref = stage.take(1), stage.take(0)[...], stage.take(2)
    across_ref, own_ref = stage.out(0), stage.out(1)
    across = partial_product(g, w_ref, 2) + near_ref[1].astype(F32)
    across_ref[...] = across.astype(BF16)
    stage.give(0)
    own_ref[...] = partial_product(g, w_ref, 0) + near_ref[0].astype(F32)


def sum_kernel(stage):
    send_ref = stage.out(0)
    total = stage.take(0)[...] + stage.take(1)[...].astype(F32)
    total = mm(row_order(total.shape[0]), total.astype(BF16))
    half = total.shape[0] // 2
    for tile in range(total.shape[1] // LANES):
        t = lane_tile(total, tile)
        x, y = pair(t[:half], t[half:])
        send_ref[2 * tile] = x.astype(BF16)
        send_ref[2 * tile + 1] = y.astype(BF16)
    stage.give(0)


def spread_phases(parts):
    (a_re, a_im), (b_re, b_im), (c_re, c_im), (d_re, d_im) = parts
    s_re, s_im, t_re, t_im = a_re + c_re, a_im + c_im, a_re - c_re, a_im - c_im
    u_re, u_im, v_re, v_im = b_re + d_re, b_im + d_im, b_re - d_re, b_im - d_im
    return [
        (s_re + u_re, s_im + u_im),
        (t_re + v_im, t_im - v_re),
        (s_re - u_re, s_im - u_im),
        (t_re - v_im, t_im + v_re),
    ]


def gather_phases(parts):
    (a_re, a_im), (b_re, b_im), (c_re, c_im), (d_re, d_im) = parts
    s_re, s_im, t_re, t_im = a_re + c_re, a_im + c_im, a_re - c_re, a_im - c_im
    u_re, u_im, v_re, v_im = b_re + d_re, b_im + d_im, b_re - d_re, b_im - d_im
    return [
        (s_re + u_re, s_im + u_im),
        (t_re - v_im, t_im + v_re),
        (s_re - u_re, s_im - u_im),
        (t_re + v_im, t_im - v_re),
    ]


def rows_of(ref, start, count):
    block = ref[:, start : start + count, :]
    return block.reshape(ref.shape[0] * count, ref.shape[2])


def turned_back(re, im, twist, phase):
    if phase == 0:
        return re, im
    c, s = twist[:, phase : phase + 1], twist[:, PHASES + phase : PHASES + phase + 1]
    return re * c + im * s, im * c - re * s


def turned_on(re, im, twist, phase):
    if phase == 0:
        return re, im
    c, s = twist[:, phase : phase + 1], twist[:, PHASES + phase : PHASES + phase + 1]
    return re * c - im * s, re * s + im * c


def lane_tile(x, index):
    return x[:, index * LANES : (index + 1) * LANES]


def causal(parts, weight):
    rows = lax.broadcasted_iota(jnp.int32, parts[0].shape, 0)
    two, three = [jnp.where(rows == 0, 0.0, pltpu.roll(parts[p], 1, 0)) for p in (2, 3)]
    once, twice = [three, *parts[:3]], [two, three, *parts[:2]]
    return [
        weight[0:1] * x + weight[1:2] * y + weight[2:3] * z for x, y, z in zip(parts, once, twice)
    ]


def anticausal(parts, weight):
    count = parts[0].shape[0]
    rows = lax.broadcasted_iota(jnp.int32, parts[0].shape, 0)
    zero, one = [
        jnp.where(rows == count - 1, 0.0, pltpu.roll(parts[p], count - 1, 0)) for p in (0, 1)
    ]
    once, twice = [*parts[1:], zero], [*parts[2:], zero, one]
    return [
        weight[0:1] * x + weight[1:2] * y + weight[2:3] * z for x, y, z in zip(parts, once, twice)
    ]


def halves(x):
    high = x.astype(BF16)
    return high, (x - high.astype(F32)).astype(BF16)


def twiddles(table_ref):
    terms = [table_ref[2, :, i * LANES : (i + 1) * LANES].astype(F32) for i in range(3)]
    return terms[0] + (terms[1] + terms[2])


def transformed(parts, table_ref, twist):
    quarter = parts[0].shape[0]
    high, rest = halves(jnp.concatenate(parts, axis=1))
    sides = []
    for side in (slice(0, quarter), slice(quarter, 2 * quarter)):
        fh, fl = table_ref[0, :, side], table_ref[1, :, side]
        sides.append(mm(fh, high) + mm(fl, high) + mm(fh, rest))
    turned = []
    for phase in range(PHASES):
        re, im = [lane_tile(side, phase) for side in sides]
        turned.append(turned_back(re, im, twist, phase))
    return spread_phases(turned)


def in_time(spectrum, table_ref, twist):
    bh, bl = table_ref[0], table_ref[1]
    parts = []
    for phase, (re, im) in enumerate(gather_phases(spectrum)):
        parts.append(jnp.concatenate(turned_on(re, im, twist, phase), axis=0))
    high, rest = halves(jnp.concatenate(parts, axis=1))
    t = mm(bh, high) + mm(bl, high) + mm(bh, rest)
    return [lane_tile(t, phase) for phase in range(PHASES)]


def own_weights(weight_ref, gain_ref):
    place = lax.axis_index("seq")
    lanes = pl.ds(pl.multiple_of(place // 2 * LANES, LANES), LANES)
    odd = place % 2 == 1

    def mine(x):
        return jnp.where(odd, swap(x), x)

    weights = [mine(weight_ref[i, :, lanes]) for i in range(3)]
    gain = both(mine(gain_ref[:, lanes]))[0]
    low = low_lanes(weights[0].shape)
    only = (lax.broadcasted_iota(jnp.int32, weights[0].shape, 0) == 0).astype(F32)
    pair_weight = jnp.where(low, weights[1], swap(weights[2]))
    query_weight = jnp.where(low, weights[0], only)
    return pair_weight, query_weight, gain


def forward_kernel(stage):
    recv_ref, weight_ref, gain_ref = [stage.take(i) for i in range(3)]
    send_ref, saved_ref = stage.out(0), stage.out(1)
    blocks = recv_ref.shape[0]
    rows = recv_ref.shape[1] // 2
    share = rows // PHASES
    quarter = blocks * share
    low = low_lanes((quarter, LANES))
    pair_weight, query_weight, gain = own_weights(weight_ref, gain_ref)
    for i, x in enumerate((pair_weight, query_weight, gain)):
        saved_ref[16, 8 * i : 8 * i + x.shape[0], :] = x

    starts = [phase * share for phase in range(PHASES)]
    pairs = causal([rows_of(recv_ref, at, share).astype(F32) for at in starts], pair_weight)
    gates = causal([rows_of(recv_ref, rows + at, share).astype(F32) for at in starts], query_weight)
    for phase in range(PHASES):
        saved_ref[8 + phase] = pairs[phase]
    mixed = [x * swap(x) for x in pairs]
    query = [both(x)[0] for x in gates]
    table_ref = stage.take(3)
    twist = twiddles(table_ref)
    send_ref[:, rows // 2 :, :] = stage.take(5)[...]
    stage.give(0, 1)
    spectrum = transformed([jnp.where(low, x, y) for x, y in zip(mixed, gates)], table_ref, twist)
    product = []
    for r, (re, im) in enumerate(spectrum):
        saved_ref[2 * r] = re
        saved_ref[2 * r + 1] = im
        other_re, other_im = swap(re), swap(im)
        product.append((re * other_re - im * other_im, re * other_im + im * other_re))
    conv = in_time(product, stage.take(4), twist)
    long_out = [x + gain * y for x, y in zip(conv, mixed)]
    gated = [x * y for x, y in zip(query, long_out)]
    for phase in range(PHASES // 2):
        t = jnp.where(low, gated[phase], gated[phase + 2]).astype(BF16)
        send_ref[:, starts[phase] : starts[phase] + share, :] = t.reshape(blocks, share, LANES)
    stage.give(0)
    for phase in range(PHASES):
        saved_ref[12 + phase] = jnp.where(low, query[phase], long_out[phase])


def backward_kernel(stage):
    grad_ref, saved_ref = stage.take(0), stage.take(1)
    send_ref = stage.out(0)
    blocks = grad_ref.shape[0]
    rows = grad_ref.shape[1]
    share = rows // PHASES
    stage.out(1)[...] = grad_ref[:, : rows // 2, :]
    quarter = blocks * share
    low = low_lanes((quarter, LANES))
    pair_weight, query_weight = saved_ref[16, 0:3, :], saved_ref[16, 8:11, :]
    gain = saved_ref[16, 16:17, :]

    starts = [phase * share for phase in range(PHASES)]
    packed = [rows_of(grad_ref, at, share).astype(F32) for at in starts[2:]]
    grad_gated = [both(x)[i] for i in range(2) for x in packed]
    gates = [both(saved_ref[12 + phase]) for phase in range(PHASES)]
    grad_long = [x * y for x, (y, _) in zip(grad_gated, gates)]
    grad_query = anticausal([x * y for x, (_, y) in zip(grad_gated, gates)], query_weight)
    table_ref = stage.take(2)
    twist = twiddles(table_ref)
    grad_spectrum = transformed(grad_long, table_ref, twist)
    product = []
    for r, (re, im) in enumerate(grad_spectrum):
        k_re, k_im = saved_ref[2 * r], saved_ref[2 * r + 1]
        product.append((k_re * re + k_im * im, k_re * im - k_im * re))
    times = in_time(product, stage.take(3), twist)
    scale = 1.0 / math.sqrt(PHASES * quarter)
    for phase, at in enumerate(starts):
        y = jnp.where(low, grad_query[phase], swap(times[phase]) * scale).astype(BF16)
        send_ref[:, rows + at : rows + at + share, :] = y.reshape(blocks, share, LANES)
    stage.give(0, 1)
    grad_mixed = [both(x + gain * y)[1] for x, y in zip(times, grad_long)]
    grad_pairs = anticausal(
        [x * swap(saved_ref[8 + phase]) for phase, x in enumerate(grad_mixed)], pair_weight
    )
    for phase, at in enumerate(starts):
        x = grad_pairs[phase].astype(BF16)
        send_ref[:, at : at + share, :] = x.reshape(blocks, share, LANES)


def unpacked(blocks, order):
    half = blocks[0].shape[0]
    tiles = []
    for tile in range(len(blocks) // 2):
        top, bottom = pair(blocks[2 * tile].astype(F32), blocks[2 * tile + 1].astype(F32))
        tiles.append(jnp.concatenate([top, bottom], axis=0))
    return mm(order, jnp.concatenate(tiles, axis=1).astype(BF16))


def end_kernel(stage):
    recv_ref, grad_ref, filter_ref = stage.take(0), stage.out(0), stage.out(1)
    blocks = recv_ref.shape[0]
    rows = recv_ref.shape[1] // 2
    order = row_order(rows, back=True)
    sides = []
    for at in (0, rows):
        firsts, seconds = [], []
        for tile in range(blocks // 2):
            x, y = [recv_ref[2 * tile + i, at : at + rows].astype(F32) for i in range(2)]
            first, second = pair(x, y)
            firsts.append(first)
            seconds.append(second)
        for side in (firsts, seconds):
            sides.append(mm(order, jnp.concatenate(side, axis=1).astype(BF16)))
    key, value, query, taps = sides
    filter_ref[...] = taps
    stage.give(1)
    grad_ref[0] = query.astype(BF16)
    grad_ref[1] = key.astype(BF16)
    grad_ref[2] = value.astype(BF16)


def output_kernel(parts, stage):
    w_ref, total = stage.take(0), None
    order = row_order(2 * stage.take(1).shape[1], back=True)
    for part in range(parts):
        gated_ref = stage.take(1 + part)
        block = unpacked([gated_ref[i] for i in range(gated_ref.shape[0])], order).astype(BF16)
        width = block.shape[1]
        term = mm(block, w_ref[part * width : (part + 1) * width, :])
        total = term if total is None else total + term
    stage.out(0)[...] = total.astype(BF16)


def partner(x, axis, mask):
    return lax.ppermute(x, axis, [(i, i ^ mask) for i in range(lax.axis_size(axis))])


def exchanged(x, axis):
    return lax.all_to_all(x, axis, split_axis=0, concat_axis=0, tiled=True)


def owner_layer(qkv, filt, skip_gain, short_weight, w_out, g_out):
    shape = jax.ShapeDtypeStruct
    seq_parts, ch_parts = lax.axis_size("seq"), lax.axis_size("ch")
    rows, width = qkv.shape[1], qkv.shape[2]
    tokens = seq_parts * rows
    quarter = tokens // PHASES
    tables = jnp.asarray(phase_tables(tokens))
    table_flops = 2 * 2 * 2 * 3 * tokens * tokens // PHASES * LANES
    product_flops = 2 * rows * width * width * ch_parts
    packed = shape((seq_parts, rows // 2, LANES), BF16)
    double = shape((seq_parts, 2 * rows, LANES), BF16)
    column = shape((rows, width), BF16)
    saved = shape((4 * PHASES + 1, quarter, LANES), F32)
    gain = skip_gain[None, :]

    tile_cuts = [(at, 2) for at in range(0, seq_parts, 2)]
    (send,) = call(start_kernel, [Far(double, tile_cuts)], Far(qkv), Far(filt))
    recv = exchanged(send, "seq")
    half_sums, w_kept, g_kept = call(
        first_product_kernel,
        [
            Near(shape((2, rows, width), BF16), kept=True),
            Near(w_out, kept=True),
            Near(g_out, kept=True),
        ],
        Far(g_out, into=2),
        Far(w_out, turned=(1, 3, 2, 0), into=1),
        flops=product_flops // 2,
    )
    half_sums = partner(half_sums, "ch", 1)
    across, own = call(
        second_product_kernel,
        [Near(column, kept=True), Near(shape((rows, width), F32), kept=True)],
        Near(g_kept),
        Near(w_kept),
        Near(half_sums),
        flops=product_flops // 2,
    )
    across = partner(across, "ch", 2)
    def pinned(x):
        return Near(x, kept=True)

    grad_gated, tables_on, tables_back, weight, gain = call(
        sum_kernel,
        [
            Far(packed),
            pinned(shape((3, *tables.shape[1:]), BF16)),
            pinned(shape((2, *tables.shape[1:]), BF16)),
            pinned(short_weight),
            pinned(gain),
        ],
        Near(own),
        Near(across),
        Far(tables, [(0, 2), (4, 1)], into=1),
        Far(tables, [(2, 2)], into=2),
        Far(short_weight, into=3),
        Far(gain, into=4),
    )
    send, saved = call(
        forward_kernel,
        [
            Far(shape((seq_parts, rows, LANES), BF16), [(0, rows // 2), (rows // 2,) * 2], axis=1),
            pinned(saved),
        ],
        pinned(recv),
        Near(weight),
        Near(gain),
        Near(tables_on),
        Near(tables_back),
        Far(grad_gated),
        flops=table_flops,
    )
    swapped = exchanged(send, "seq")
    send, gated = call(
        backward_kernel,
        [Far(double, [(0, rows), (rows, rows)], axis=1), pinned(packed)],
        Near(swapped),
        Near(saved),
        Near(tables_on),
        Near(tables_back),
        flops=table_flops,
    )
    grad_recv = exchanged(send, "seq")
    across = partner(gated, "ch", 2)
    near, far = partner(gated, "ch", 1), partner(across, "ch", 1)
    (output,) = call(
        functools.partial(output_kernel, ch_parts),
        [Far(column)],
        Near(w_kept),
        Near(gated),
        Near(near),
        Near(across),
        Near(far),
        flops=product_flops,
    )
    grad_qkv, grad_filter = call(
        end_kernel,
        [Far(shape((3, rows, width), BF16)), Far(shape((rows, width), F32))],
        Near(grad_recv),
    )
    return (output, grad_qkv, grad_filter)


def local(qkv, filt, skip_gain, short_weight, w_out, g_out):
    seq_parts = lax.axis_size("seq")
    rows, width = qkv.shape[1], qkv.shape[2]
    fits = width == HALF * seq_parts and rows % HALF == 0 and rows & (rows - 1) == 0 and rows * seq_parts <= 2048
    if fits and lax.axis_size("ch") == 4:
        return owner_layer(qkv, filt, skip_gain, short_weight, w_out, g_out)
    return spread_layer(qkv, filt, skip_gain, short_weight, w_out, g_out)


def solution(mesh):
    in_specs = (
        P(None, "seq", "ch"),
        P("seq", "ch"),
        P("ch"),
        P(None, None, "ch"),
        P(None, "ch"),
        P("seq", "ch"),
    )
    out_specs = (P("seq", "ch"), P(None, "seq", "ch"), P("seq", "ch"))
    return jax.shard_map(local, mesh=mesh, in_specs=in_specs, out_specs=out_specs, check_vma=False)
```

```python
import functools
import math

import jax
import jax.numpy as jnp
import numpy as np
from jax import lax
from jax.experimental import pallas as pl
from jax.experimental.pallas import tpu as pltpu
from jax.sharding import PartitionSpec as P

HIGHEST = lax.Precision.HIGHEST
TWO_PI = 2.0 * math.pi
LANES = 128
HALF = 64
PHASES = 4
BF16 = jnp.bfloat16
F32 = jnp.float32
VMEM_LIMIT = 24 * 1024 * 1024


def passed_along(block, axis, distance):
    devices = range(lax.axis_size(axis))
    route = [(i - distance, i) for i in devices if i - distance in devices]
    return lax.ppermute(block, axis, route)


def phase_pair(left_count, right_count, period, left_start, right_start):
    left_idx = lax.broadcasted_iota(jnp.int32, (left_count, right_count), 0) + left_start
    right_idx = lax.broadcasted_iota(jnp.int32, (left_count, right_count), 1) + right_start
    angle_all = (left_idx * right_idx % period).astype(jnp.float32) * (TWO_PI / period)
    return (jnp.cos(angle_all), jnp.sin(angle_all))


def contract(pattern, matrix, values):
    return jnp.einsum(
        pattern, matrix, values, precision=HIGHEST, preferred_element_type=jnp.float32
    )


def forward_spectrum(signal):
    seq_parts = lax.axis_size("seq")
    row_count = signal.shape[0]
    row_share = row_count // seq_parts
    period = 2 * seq_parts * row_count
    spread_in = lax.all_to_all(signal[None], "seq", split_axis=1, concat_axis=0, tiled=True)
    outer_cos, outer_sin = phase_pair(2 * seq_parts, seq_parts, 2 * seq_parts, 0, 0)
    section_re = contract("cp,prw->crw", outer_cos, spread_in)
    section_im = -contract("cp,prw->crw", outer_sin, spread_in)
    twist_cos, twist_sin = phase_pair(
        2 * seq_parts, row_share, period, 0, lax.axis_index("seq") * row_share
    )
    twist_cos = twist_cos[:, :, None]
    twist_sin = twist_sin[:, :, None]
    turned_re = section_re * twist_cos + section_im * twist_sin
    turned_im = section_im * twist_cos - section_re * twist_sin
    inner_cos, inner_sin = phase_pair(row_count, row_count, row_count, 0, 0)
    piece_re = lax.all_to_all(turned_re, "seq", split_axis=0, concat_axis=1, tiled=True)
    piece_im = lax.all_to_all(turned_im, "seq", split_axis=0, concat_axis=1, tiled=True)
    spec_re = contract("dm,cmk->cdk", inner_cos, piece_re) + contract(
        "dm,cmk->cdk", inner_sin, piece_im
    )
    spec_im = contract("dm,cmk->cdk", inner_cos, piece_im) - contract(
        "dm,cmk->cdk", inner_sin, piece_re
    )
    return (spec_re, spec_im)


def time_signal(spec_re, spec_im):
    seq_parts = lax.axis_size("seq")
    row_count = spec_re.shape[1]
    period = 2 * seq_parts * row_count
    inner_cos, inner_sin = phase_pair(row_count, row_count, row_count, 0, 0)
    back_re = contract("md,cdk->cmk", inner_cos, spec_re) - contract(
        "md,cdk->cmk", inner_sin, spec_im
    )
    back_im = contract("md,cdk->cmk", inner_cos, spec_im) + contract(
        "md,cdk->cmk", inner_sin, spec_re
    )
    twist_cos, twist_sin = phase_pair(2, row_count, period, 2 * lax.axis_index("seq"), 0)
    twist_cos = twist_cos[:, :, None]
    twist_sin = twist_sin[:, :, None]
    turned_re = back_re * twist_cos - back_im * twist_sin
    turned_im = back_im * twist_cos + back_re * twist_sin
    outer_cos, outer_sin = phase_pair(seq_parts, 2 * seq_parts, 2 * seq_parts, 0, 0)
    piece_re = lax.all_to_all(turned_re, "seq", split_axis=1, concat_axis=0, tiled=True)
    piece_im = lax.all_to_all(turned_im, "seq", split_axis=1, concat_axis=0, tiled=True)
    summed = contract("pc,crk->prk", outer_cos, piece_re) - contract(
        "pc,crk->prk", outer_sin, piece_im
    )
    returned = summed * (1.0 / period)
    return lax.all_to_all(returned, "seq", split_axis=0, concat_axis=1, tiled=True)[0]


def spread_layer(qkv, filt, skip_gain, short_weight, w_out, g_out):
    row_count = qkv.shape[1]
    slab_width = qkv.shape[2]
    tail_rows = passed_along(qkv[:, row_count - 2 :, :], "seq", 1)
    extended = jnp.concatenate([tail_rows, qkv], axis=1)
    short = (
        short_weight[:, 0, None, :] * extended[:, 2:, :]
        + short_weight[:, 1, None, :] * extended[:, 1:-1, :]
        + short_weight[:, 2, None, :] * extended[:, :-2, :]
    )
    query_gate = short[0]
    key_short = short[1]
    value_short = short[2]
    mixed = key_short * value_short
    both_re, both_im = forward_spectrum(jnp.concatenate([mixed, filt], axis=1))
    signal_re = both_re[:, :, :slab_width]
    signal_im = both_im[:, :, :slab_width]
    kernel_re = both_re[:, :, slab_width:]
    kernel_im = both_im[:, :, slab_width:]
    conv_out = time_signal(
        signal_re * kernel_re - signal_im * kernel_im, signal_re * kernel_im + signal_im * kernel_re
    )
    long_out = conv_out + skip_gain * mixed
    gated_out = (query_gate * long_out).astype(jnp.bfloat16)
    projected = jnp.dot(
        lax.all_gather(gated_out, "ch", axis=1, tiled=True),
        w_out,
        preferred_element_type=jnp.float32,
    )
    output = projected.astype(jnp.bfloat16)
    grad_all = lax.all_gather(g_out, "ch", axis=1, tiled=True)
    rows_all = lax.all_to_all(w_out, "ch", split_axis=0, concat_axis=1, tiled=True)
    grad_gated = lax.dot_general(
        grad_all, rows_all, (((1,), (1,)), ((), ())), preferred_element_type=jnp.float32
    )
    grad_long = grad_gated * query_gate
    grad_query = grad_gated * long_out
    grad_re, grad_im = forward_spectrum(grad_long)
    pair_re = jnp.concatenate(
        [kernel_re * grad_re + kernel_im * grad_im, signal_re * grad_re + signal_im * grad_im],
        axis=2,
    )
    pair_im = jnp.concatenate(
        [kernel_re * grad_im - kernel_im * grad_re, signal_re * grad_im - signal_im * grad_re],
        axis=2,
    )
    pair_time = time_signal(pair_re, pair_im)
    grad_mixed = pair_time[:, :slab_width] + skip_gain * grad_long
    token_total = lax.axis_size("seq") * row_count
    grad_filter = pair_time[:, slab_width:] * (1.0 / math.sqrt(token_total))
    grad_short = jnp.stack([grad_query, grad_mixed * value_short, grad_mixed * key_short])
    head_rows = passed_along(grad_short[:, :2, :], "seq", -1)
    extended_grad = jnp.concatenate([grad_short, head_rows], axis=1)
    grad_qkv = (
        short_weight[:, 0, None, :] * extended_grad[:, :-2, :]
        + short_weight[:, 1, None, :] * extended_grad[:, 1:-1, :]
        + short_weight[:, 2, None, :] * extended_grad[:, 2:, :]
    ).astype(jnp.bfloat16)
    return (output, grad_qkv, grad_filter)


def split_bf16(values):
    high = values.astype(np.float32).astype(jnp.bfloat16)
    low = (values - high.astype(np.float64)).astype(np.float32).astype(jnp.bfloat16)
    return high, low


def phase_tables(tokens):
    quarter = tokens // PHASES
    freq = 2 * np.arange(quarter)[:, None] + 1
    turn = math.pi / (2 * tokens)
    angle = (freq * PHASES * np.arange(quarter)[None, :] % (4 * tokens)) * turn
    forward = np.concatenate([np.cos(angle), -np.sin(angle)], axis=1)
    backward = np.concatenate([np.cos(angle).T, -np.sin(angle).T], axis=1) / tokens
    angle = freq * np.arange(PHASES)[None, :] * turn
    twist = np.concatenate([np.cos(angle), np.sin(angle)], axis=1)
    twist = np.pad(twist, ((0, 0), (0, LANES - 2 * PHASES)))
    high, rest = split_bf16(twist)
    last = split_bf16(twist - high.astype(np.float64) - rest.astype(np.float64))[0]
    tables = np.zeros((8, quarter, 2 * quarter), jnp.bfloat16)
    tables[0], tables[1] = split_bf16(forward)
    tables[2], tables[3] = split_bf16(backward)
    for i, term in enumerate((high, rest, last)):
        tables[4, :, i * LANES : (i + 1) * LANES] = term
    return tables


def row_order(rows, back=False):
    to, at = [lax.broadcasted_iota(jnp.int32, (rows, rows), int(i != back)) for i in range(2)]
    share = rows // PHASES
    wanted = (to & (share - 1)) * PHASES + lax.shift_right_logical(to, share.bit_length() - 1)
    return jnp.where(wanted == at, 1.0, 0.0).astype(BF16)


def mm(a, b):
    return lax.dot_general(a, b, (((1,), (0,)), ((), ())), preferred_element_type=F32)


def low_lanes(shape):
    return lax.broadcasted_iota(jnp.int32, shape, 1) < HALF


def swap(x):
    return pltpu.roll(x, HALF, 1)


class Near:
    def __init__(self, array, kept=False):
        self.array = array
        self.kept = kept


class Far:
    def __init__(self, array, cuts=None, turned=(), into=None, axis=0):
        self.array = array
        self.turned = turned
        self.into = into
        self.axis = axis
        if turned:
            step = array.shape[0] // len(turned)
            cuts = [(mask * step, step) for mask in turned]
        self.cuts = cuts or [(0, array.shape[axis])]
        self.shape = list(array.shape)
        self.shape[axis] = sum(count for _, count in self.cuts)


class Stage:
    def __init__(self, items, count_in, refs):
        arrays, scratch = list(refs[: len(items)]), list(refs[len(items) :])
        sems = scratch.pop()
        self.count_in = count_in
        self.held, self.copies, self.waiting = [], [], []
        used = 0
        for i, (item, array) in enumerate(zip(items, arrays)):
            group = []
            if isinstance(item, Near):
                self.held.append(array)
            else:
                held = scratch.pop(0) if item.into is None else arrays[count_in + item.into]
                self.held.append(held)
                at = 0
                for cut, (start, count) in enumerate(item.cuts):
                    lead = (slice(None),) * item.axis
                    there = held.at[(*lead, pl.ds(start if item.turned else at, count))]
                    at += count
                    if item.turned:
                        mask = item.turned[cut]
                        start = pl.multiple_of((lax.axis_index("ch") ^ mask) * count, count)
                    here = array.at[(*lead, pl.ds(start, count))]
                    if i >= count_in:
                        here, there = there, here
                    group.append(pltpu.make_async_copy(here, there, sems.at[used]))
                    used += 1
            self.copies.append(group)
            self.waiting.append(set(range(len(group))))
        self.given = set()

    def bring(self, index):
        for copy in self.copies[index]:
            copy.start()

    def take(self, index, cut=None):
        for i in sorted(self.waiting[index]):
            if cut is None or cut == i:
                self.copies[index][i].wait()
                self.waiting[index].discard(i)
        return self.held[index]

    def out(self, index):
        return self.held[self.count_in + index]

    def give(self, index, cut=None):
        for i, copy in enumerate(self.copies[self.count_in + index]):
            if (index, i) not in self.given and cut in (None, i):
                copy.start()
                self.given.add((index, i))


def staged(kernel, items, count_in, *refs):
    stage = Stage(items, count_in, refs)
    for i in range(count_in):
        stage.bring(i)
    kernel(stage)
    for i in range(count_in):
        stage.take(i)
    for i in range(len(items) - count_in):
        stage.give(i)
    for i in range(len(items) - count_in):
        stage.take(count_in + i)


def operand_of(x):
    if isinstance(x, Near) and not x.kept:
        return x.array
    space = pltpu.VMEM if isinstance(x, Near) else pltpu.HBM
    return pltpu.with_memory_space_constraint(x.array, space)


def result_of(x):
    make = pltpu.HBM if isinstance(x, Far) else pltpu.VMEM if x.kept else jax.ShapeDtypeStruct
    return make(x.array.shape, x.array.dtype)


def call(kernel, results, *args, flops=0):
    items = list(args) + list(results)
    specs, scratch, used = [], [], 0
    for item in items:
        near = isinstance(item, Near)
        specs.append(pl.BlockSpec(memory_space=pltpu.VMEM if near else pltpu.HBM))
        if not near:
            used += len(item.cuts)
            if item.into is None:
                scratch.append(pltpu.VMEM(tuple(item.shape), item.array.dtype))
    moved = sum(math.prod(x.array.shape) * x.array.dtype.itemsize for x in items)
    return pl.pallas_call(
        functools.partial(staged, kernel, items, len(args)),
        out_shape=[result_of(x) for x in results],
        in_specs=specs[: len(args)],
        out_specs=specs[len(args) :],
        scratch_shapes=scratch + [pltpu.SemaphoreType.DMA((max(used, 1),))],
        compiler_params=pltpu.CompilerParams(vmem_limit_bytes=VMEM_LIMIT),
        cost_estimate=pl.CostEstimate(flops=flops, bytes_accessed=moved, transcendentals=0),
    )(*[operand_of(x) for x in args])


def lane_tile(x, index):
    return x[:, index * LANES : (index + 1) * LANES]


def pair(first, second):
    low = low_lanes(first.shape)
    return jnp.where(low, first, swap(second)), jnp.where(low, swap(first), second)


def both(x):
    turned, low = swap(x), low_lanes(x.shape)
    return jnp.where(low, x, turned), jnp.where(low, turned, x)


def start_kernel(stage):
    send_ref, qkv_ref = stage.out(0), stage.take(0)
    rows = qkv_ref.shape[1]
    order = row_order(rows)
    query, key, value = [mm(order, qkv_ref[i]) for i in range(3)]
    taps = mm(order, stage.take(1)[...].astype(BF16))
    for tile in range(query.shape[1] // LANES):
        for row, (x, y) in enumerate(((key, value), (query, taps))):
            here = slice(row * rows, (row + 1) * rows)
            x, y = pair(lane_tile(x, tile), lane_tile(y, tile))
            send_ref[2 * tile, here] = x.astype(BF16)
            send_ref[2 * tile + 1, here] = y.astype(BF16)
        stage.give(0, tile)


def partial_product(g, w_ref, mask):
    width = g.shape[1]
    w = w_ref[mask * width : (mask + 1) * width, :]
    return lax.dot_general(g, w, (((1,), (1,)), ((), ())), preferred_element_type=F32)


def first_product_kernel(stage):
    g, out_ref = stage.take(0)[...], stage.out(0)
    for i, mask in enumerate((1, 3)):
        out_ref[i] = partial_product(g, stage.take(1, i), mask).astype(BF16)


def second_product_kernel(stage):
    w_ref, g, near_ref = stage.take(1), stage.take(0)[...], stage.take(2)
    across_ref, own_ref = stage.out(0), stage.out(1)
    across = partial_product(g, w_ref, 2) + near_ref[1].astype(F32)
    across_ref[...] = across.astype(BF16)
    stage.give(0)
    own_ref[...] = partial_product(g, w_ref, 0) + near_ref[0].astype(F32)


def sum_kernel(stage):
    send_ref = stage.out(0)
    total = stage.take(0)[...] + stage.take(1)[...].astype(F32)
    total = mm(row_order(total.shape[0]), total.astype(BF16))
    half = total.shape[0] // 2
    for tile in range(total.shape[1] // LANES):
        t = lane_tile(total, tile)
        x, y = pair(t[:half], t[half:])
        send_ref[2 * tile] = x.astype(BF16)
        send_ref[2 * tile + 1] = y.astype(BF16)
    stage.give(0)


def spread_phases(parts):
    (a_re, a_im), (b_re, b_im), (c_re, c_im), (d_re, d_im) = parts
    s_re, s_im, t_re, t_im = a_re + c_re, a_im + c_im, a_re - c_re, a_im - c_im
    u_re, u_im, v_re, v_im = b_re + d_re, b_im + d_im, b_re - d_re, b_im - d_im
    return [
        (s_re + u_re, s_im + u_im),
        (t_re + v_im, t_im - v_re),
        (s_re - u_re, s_im - u_im),
        (t_re - v_im, t_im + v_re),
    ]


def gather_phases(parts):
    (a_re, a_im), (b_re, b_im), (c_re, c_im), (d_re, d_im) = parts
    s_re, s_im, t_re, t_im = a_re + c_re, a_im + c_im, a_re - c_re, a_im - c_im
    u_re, u_im, v_re, v_im = b_re + d_re, b_im + d_im, b_re - d_re, b_im - d_im
    return [
        (s_re + u_re, s_im + u_im),
        (t_re - v_im, t_im + v_re),
        (s_re - u_re, s_im - u_im),
        (t_re + v_im, t_im - v_re),
    ]


def rows_of(ref, start, count):
    block = ref[:, start : start + count, :]
    return block.reshape(ref.shape[0] * count, ref.shape[2])


def turned_back(re, im, twist, phase):
    if phase == 0:
        return re, im
    c, s = twist[:, phase : phase + 1], twist[:, PHASES + phase : PHASES + phase + 1]
    return re * c + im * s, im * c - re * s


def turned_on(re, im, twist, phase):
    if phase == 0:
        return re, im
    c, s = twist[:, phase : phase + 1], twist[:, PHASES + phase : PHASES + phase + 1]
    return re * c - im * s, re * s + im * c


def lane_tile(x, index):
    return x[:, index * LANES : (index + 1) * LANES]


def causal(parts, weight):
    rows = lax.broadcasted_iota(jnp.int32, parts[0].shape, 0)
    two, three = [jnp.where(rows == 0, 0.0, pltpu.roll(parts[p], 1, 0)) for p in (2, 3)]
    once, twice = [three, *parts[:3]], [two, three, *parts[:2]]
    return [
        weight[0:1] * x + weight[1:2] * y + weight[2:3] * z for x, y, z in zip(parts, once, twice)
    ]


def anticausal(parts, weight):
    count = parts[0].shape[0]
    rows = lax.broadcasted_iota(jnp.int32, parts[0].shape, 0)
    zero, one = [
        jnp.where(rows == count - 1, 0.0, pltpu.roll(parts[p], count - 1, 0)) for p in (0, 1)
    ]
    once, twice = [*parts[1:], zero], [*parts[2:], zero, one]
    return [
        weight[0:1] * x + weight[1:2] * y + weight[2:3] * z for x, y, z in zip(parts, once, twice)
    ]


def halves(x):
    high = x.astype(BF16)
    return high, (x - high.astype(F32)).astype(BF16)


def twiddles(table_ref):
    terms = [table_ref[2, :, i * LANES : (i + 1) * LANES].astype(F32) for i in range(3)]
    return terms[0] + (terms[1] + terms[2])


def columns(parts):
    return jnp.concatenate(parts, axis=1)


def two_sides(table, x):
    quarter = table.shape[0]
    return [mm(table[:, :quarter], x), mm(table[:, quarter:], x)]


def spectrum_of(sides, twist):
    turned = []
    for phase, (re, im) in enumerate(sides):
        turned.append(turned_back(re, im, twist, phase))
    return spread_phases(turned)


def back_values(spectrum, twist):
    return [
        jnp.concatenate(turned_on(re, im, twist, phase), axis=0)
        for phase, (re, im) in enumerate(gather_phases(spectrum))
    ]


def own_weights(weight_ref, gain_ref):
    place = lax.axis_index("seq")
    lanes = pl.ds(pl.multiple_of(place // 2 * LANES, LANES), LANES)
    odd = place % 2 == 1

    def mine(x):
        return jnp.where(odd, swap(x), x)

    weights = [mine(weight_ref[i, :, lanes]) for i in range(3)]
    gain = both(mine(gain_ref[:, lanes]))[0]
    low = low_lanes(weights[0].shape)
    only = (lax.broadcasted_iota(jnp.int32, weights[0].shape, 0) == 0).astype(F32)
    pair_weight = jnp.where(low, weights[1], swap(weights[2]))
    query_weight = jnp.where(low, weights[0], only)
    return pair_weight, query_weight, gain


def forward_kernel(stage):
    recv_ref, weight_ref, gain_ref = [stage.take(i) for i in range(3)]
    send_ref, saved_ref = stage.out(0), stage.out(1)
    blocks = recv_ref.shape[0]
    rows = recv_ref.shape[1] // 2
    share = rows // PHASES
    quarter = blocks * share
    low = low_lanes((quarter, LANES))
    pair_weight, query_weight, gain = own_weights(weight_ref, gain_ref)
    for i, x in enumerate((pair_weight, query_weight, gain)):
        saved_ref[16, 8 * i : 8 * i + x.shape[0], :] = x

    starts = [phase * share for phase in range(PHASES)]
    pairs = causal([rows_of(recv_ref, at, share).astype(F32) for at in starts], pair_weight)
    gates = causal([rows_of(recv_ref, rows + at, share).astype(F32) for at in starts], query_weight)
    for phase in range(PHASES):
        saved_ref[8 + phase] = pairs[phase]
    mixed = [x * swap(x) for x in pairs]

    fh, fl = stage.take(3)[0], stage.take(3)[1]
    twist = twiddles(stage.take(3))
    high = [jnp.where(low, x, y).astype(BF16) for x, y in zip(mixed, gates)]
    rest = [x - y.astype(F32) for x, y in zip(mixed, high)]
    rest = [jnp.where(low, rest[i], swap(rest[i + 2])).astype(BF16) for i in range(2)]
    high, rest = columns(high), columns(rest)
    main = [x + y for x, y in zip(two_sides(fh, high), two_sides(fl, high))]
    more = two_sides(fh, rest)
    sides = []
    for phase in range(PHASES):
        extra = [lane_tile(x, phase % 2) for x in more]
        if phase >= 2:
            extra = [swap(x) for x in extra]
        sides.append([lane_tile(x, phase) + jnp.where(low, y, 0.0) for x, y in zip(main, extra)])
    send_ref[:, rows // 2 :, :] = stage.take(5)[...]
    stage.give(0, 1)
    product = []
    for r, (re, im) in enumerate(spectrum_of(sides, twist)):
        saved_ref[2 * r] = re
        saved_ref[2 * r + 1] = im
        other_re, other_im = swap(re), swap(im)
        product.append((re * other_re - im * other_im, re * other_im + im * other_re))

    values = back_values(product, twist)
    bh, bl = stage.take(4)[0], stage.take(4)[1]
    wide = low_lanes((2 * quarter, LANES))
    high = [x.astype(BF16) for x in values]
    wider = [x.astype(F32) for x in high]
    both_parts = [jnp.where(wide, y, x - y).astype(BF16) for x, y in zip(values, wider)]
    high = [jnp.where(wide, wider[i], wider[i + 2]).astype(BF16) for i in range(2)]
    main, more = mm(bh, columns(both_parts)), mm(bl, columns(high))
    summed = [x + swap(x) for x in (lane_tile(main, phase) for phase in range(PHASES))]
    for i in range(2):
        conv = jnp.where(low, summed[i], summed[i + 2]) + lane_tile(more, i)
        long_out = conv + gain * jnp.where(low, mixed[i], mixed[i + 2])
        query = jnp.where(low, gates[i], swap(gates[i + 2]))
        gated = (query * long_out).astype(BF16)
        send_ref[:, starts[i] : starts[i] + share, :] = gated.reshape(blocks, share, LANES)
        saved_ref[12 + i] = query
        saved_ref[14 + i] = long_out


def backward_kernel(stage):
    grad_ref, saved_ref = stage.take(0), stage.take(1)
    send_ref = stage.out(0)
    blocks = grad_ref.shape[0]
    rows = grad_ref.shape[1]
    share = rows // PHASES
    quarter = blocks * share
    stage.out(1)[...] = grad_ref[:, : rows // 2, :]
    low = low_lanes((quarter, LANES))
    pair_weight, query_weight = saved_ref[16, 0:3, :], saved_ref[16, 8:11, :]
    gain = saved_ref[16, 16:17, :]

    starts = [phase * share for phase in range(PHASES)]
    grad_gated = [rows_of(grad_ref, at, share).astype(F32) for at in starts[2:]]
    grad_long = [x * saved_ref[12 + i] for i, x in enumerate(grad_gated)]
    grad_query = [x * saved_ref[14 + i] for i, x in enumerate(grad_gated)]
    grad_query = anticausal(grad_query + [swap(x) for x in grad_query], query_weight)

    fh, fl = stage.take(2)[0], stage.take(2)[1]
    twist = twiddles(stage.take(2))
    high, rest = halves(columns(grad_long))
    three = zip(two_sides(fh, high), two_sides(fl, high), two_sides(fh, rest))
    main = [x + y + z for x, y, z in three]
    sides = []
    for phase in range(PHASES):
        sides.append([both(lane_tile(x, phase % 2))[phase // 2] for x in main])
    product = []
    for r, (re, im) in enumerate(spectrum_of(sides, twist)):
        k_re, k_im = saved_ref[2 * r], saved_ref[2 * r + 1]
        product.append((k_re * re + k_im * im, k_re * im - k_im * re))
    high, rest = halves(columns(back_values(product, twist)))
    bh, bl = stage.take(3)[0], stage.take(3)[1]
    times = mm(bh, high) + mm(bl, high) + mm(bh, rest)
    times = [lane_tile(times, phase) for phase in range(PHASES)]

    scale = 1.0 / math.sqrt(PHASES * quarter)
    for phase, at in enumerate(starts):
        y = jnp.where(low, grad_query[phase], swap(times[phase]) * scale).astype(BF16)
        send_ref[:, rows + at : rows + at + share, :] = y.reshape(blocks, share, LANES)
    stage.give(0, 1)
    grad_long = [both(x)[i] for i in range(2) for x in grad_long]
    grad_mixed = [both(x + gain * y)[1] for x, y in zip(times, grad_long)]
    grad_pairs = anticausal(
        [x * swap(saved_ref[8 + phase]) for phase, x in enumerate(grad_mixed)], pair_weight
    )
    for phase, at in enumerate(starts):
        x = grad_pairs[phase].astype(BF16)
        send_ref[:, at : at + share, :] = x.reshape(blocks, share, LANES)


def unpacked(blocks, order):
    half = blocks[0].shape[0]
    tiles = []
    for tile in range(len(blocks) // 2):
        top, bottom = pair(blocks[2 * tile].astype(F32), blocks[2 * tile + 1].astype(F32))
        tiles.append(jnp.concatenate([top, bottom], axis=0))
    return mm(order, jnp.concatenate(tiles, axis=1).astype(BF16))


def end_kernel(stage):
    recv_ref, grad_ref, filter_ref = stage.take(0), stage.out(0), stage.out(1)
    blocks = recv_ref.shape[0]
    rows = recv_ref.shape[1] // 2
    order = row_order(rows, back=True)
    sides = []
    for at in (0, rows):
        firsts, seconds = [], []
        for tile in range(blocks // 2):
            x, y = [recv_ref[2 * tile + i, at : at + rows].astype(F32) for i in range(2)]
            first, second = pair(x, y)
            firsts.append(first)
            seconds.append(second)
        for side in (firsts, seconds):
            sides.append(mm(order, jnp.concatenate(side, axis=1).astype(BF16)))
    key, value, query, taps = sides
    filter_ref[...] = taps
    stage.give(1)
    grad_ref[0] = query.astype(BF16)
    grad_ref[1] = key.astype(BF16)
    grad_ref[2] = value.astype(BF16)


def output_kernel(parts, stage):
    w_ref, total = stage.take(0), None
    order = row_order(2 * stage.take(1).shape[1], back=True)
    for part in range(parts):
        gated_ref = stage.take(1 + part)
        block = unpacked([gated_ref[i] for i in range(gated_ref.shape[0])], order).astype(BF16)
        width = block.shape[1]
        term = mm(block, w_ref[part * width : (part + 1) * width, :])
        total = term if total is None else total + term
    stage.out(0)[...] = total.astype(BF16)


def partner(x, axis, mask):
    return lax.ppermute(x, axis, [(i, i ^ mask) for i in range(lax.axis_size(axis))])


def exchanged(x, axis):
    return lax.all_to_all(x, axis, split_axis=0, concat_axis=0, tiled=True)


def owner_layer(qkv, filt, skip_gain, short_weight, w_out, g_out):
    shape = jax.ShapeDtypeStruct
    seq_parts, ch_parts = lax.axis_size("seq"), lax.axis_size("ch")
    rows, width = qkv.shape[1], qkv.shape[2]
    tokens = seq_parts * rows
    quarter = tokens // PHASES
    tables = jnp.asarray(phase_tables(tokens))
    table_flops = 2 * 2 * 2 * 3 * tokens * tokens // PHASES * LANES
    product_flops = 2 * rows * width * width * ch_parts
    packed = shape((seq_parts, rows // 2, LANES), BF16)
    double = shape((seq_parts, 2 * rows, LANES), BF16)
    column = shape((rows, width), BF16)
    saved = shape((4 * PHASES + 1, quarter, LANES), F32)
    gain = skip_gain[None, :]

    tile_cuts = [(at, 2) for at in range(0, seq_parts, 2)]
    (send,) = call(start_kernel, [Far(double, tile_cuts)], Far(qkv), Far(filt))
    recv = exchanged(send, "seq")
    half_sums, w_kept, g_kept = call(
        first_product_kernel,
        [
            Near(shape((2, rows, width), BF16), kept=True),
            Near(w_out, kept=True),
            Near(g_out, kept=True),
        ],
        Far(g_out, into=2),
        Far(w_out, turned=(1, 3, 2, 0), into=1),
        flops=product_flops // 2,
    )
    half_sums = partner(half_sums, "ch", 1)
    across, own = call(
        second_product_kernel,
        [Near(column, kept=True), Near(shape((rows, width), F32), kept=True)],
        Near(g_kept),
        Near(w_kept),
        Near(half_sums),
        flops=product_flops // 2,
    )
    across = partner(across, "ch", 2)
    def pinned(x):
        return Near(x, kept=True)

    tables_back = Far(tables, [(2, 2)])
    grad_gated, tables_on, weight, gain = call(
        sum_kernel,
        [
            Far(packed),
            pinned(shape((3, *tables.shape[1:]), BF16)),
            pinned(short_weight),
            pinned(gain),
        ],
        Near(own),
        Near(across),
        Far(tables, [(0, 2), (4, 1)], into=1),
        Far(short_weight, into=2),
        Far(gain, into=3),
    )
    send, saved = call(
        forward_kernel,
        [
            Far(shape((seq_parts, rows, LANES), BF16), [(0, rows // 2), (rows // 2,) * 2], axis=1),
            pinned(saved),
        ],
        pinned(recv),
        Near(weight),
        Near(gain),
        Near(tables_on),
        tables_back,
        Far(grad_gated),
        flops=table_flops,
    )
    swapped = exchanged(send, "seq")
    send, gated = call(
        backward_kernel,
        [Far(double, [(0, rows), (rows, rows)], axis=1), pinned(packed)],
        Near(swapped),
        Near(saved),
        Near(tables_on),
        tables_back,
        flops=table_flops,
    )
    grad_recv = exchanged(send, "seq")
    across = partner(gated, "ch", 2)
    near, far = partner(gated, "ch", 1), partner(across, "ch", 1)
    (output,) = call(
        functools.partial(output_kernel, ch_parts),
        [Far(column)],
        Near(w_kept),
        Near(gated),
        Near(near),
        Near(across),
        Near(far),
        flops=product_flops,
    )
    grad_qkv, grad_filter = call(
        end_kernel,
        [Far(shape((3, rows, width), BF16)), Far(shape((rows, width), F32))],
        Near(grad_recv),
    )
    return (output, grad_qkv, grad_filter)


def local(qkv, filt, skip_gain, short_weight, w_out, g_out):
    seq_parts = lax.axis_size("seq")
    rows, width = qkv.shape[1], qkv.shape[2]
    fits = width == HALF * seq_parts and rows % HALF == 0 and rows & (rows - 1) == 0 and rows * seq_parts <= 2048
    if fits and lax.axis_size("ch") == 4:
        return owner_layer(qkv, filt, skip_gain, short_weight, w_out, g_out)
    return spread_layer(qkv, filt, skip_gain, short_weight, w_out, g_out)


def solution(mesh):
    in_specs = (
        P(None, "seq", "ch"),
        P("seq", "ch"),
        P("ch"),
        P(None, None, "ch"),
        P(None, "ch"),
        P("seq", "ch"),
    )
    out_specs = (P("seq", "ch"), P(None, "seq", "ch"), P("seq", "ch"))
    return jax.shard_map(local, mesh=mesh, in_specs=in_specs, out_specs=out_specs, check_vma=False)
```

```python
import functools
import math

import jax
import jax.numpy as jnp
import numpy as np
from jax import lax
from jax.experimental import pallas as pl
from jax.experimental.pallas import tpu as pltpu
from jax.sharding import PartitionSpec as P

HIGHEST = lax.Precision.HIGHEST
TWO_PI = 2.0 * math.pi
LANES = 128
HALF = 64
PHASES = 4
STRIP = 16
BF16 = jnp.bfloat16
F32 = jnp.float32
VMEM_LIMIT = 24 * 1024 * 1024


def passed_along(block, axis, distance):
    devices = range(lax.axis_size(axis))
    route = [(i - distance, i) for i in devices if i - distance in devices]
    return lax.ppermute(block, axis, route)


def phase_pair(left_count, right_count, period, left_start, right_start):
    left_idx = lax.broadcasted_iota(jnp.int32, (left_count, right_count), 0) + left_start
    right_idx = lax.broadcasted_iota(jnp.int32, (left_count, right_count), 1) + right_start
    angle_all = (left_idx * right_idx % period).astype(jnp.float32) * (TWO_PI / period)
    return (jnp.cos(angle_all), jnp.sin(angle_all))


def contract(pattern, matrix, values):
    return jnp.einsum(
        pattern, matrix, values, precision=HIGHEST, preferred_element_type=jnp.float32
    )


def forward_spectrum(signal):
    seq_parts = lax.axis_size("seq")
    row_count = signal.shape[0]
    row_share = row_count // seq_parts
    period = 2 * seq_parts * row_count
    spread_in = lax.all_to_all(signal[None], "seq", split_axis=1, concat_axis=0, tiled=True)
    outer_cos, outer_sin = phase_pair(2 * seq_parts, seq_parts, 2 * seq_parts, 0, 0)
    section_re = contract("cp,prw->crw", outer_cos, spread_in)
    section_im = -contract("cp,prw->crw", outer_sin, spread_in)
    twist_cos, twist_sin = phase_pair(
        2 * seq_parts, row_share, period, 0, lax.axis_index("seq") * row_share
    )
    twist_cos = twist_cos[:, :, None]
    twist_sin = twist_sin[:, :, None]
    turned_re = section_re * twist_cos + section_im * twist_sin
    turned_im = section_im * twist_cos - section_re * twist_sin
    inner_cos, inner_sin = phase_pair(row_count, row_count, row_count, 0, 0)
    piece_re = lax.all_to_all(turned_re, "seq", split_axis=0, concat_axis=1, tiled=True)
    piece_im = lax.all_to_all(turned_im, "seq", split_axis=0, concat_axis=1, tiled=True)
    spec_re = contract("dm,cmk->cdk", inner_cos, piece_re) + contract(
        "dm,cmk->cdk", inner_sin, piece_im
    )
    spec_im = contract("dm,cmk->cdk", inner_cos, piece_im) - contract(
        "dm,cmk->cdk", inner_sin, piece_re
    )
    return (spec_re, spec_im)


def time_signal(spec_re, spec_im):
    seq_parts = lax.axis_size("seq")
    row_count = spec_re.shape[1]
    period = 2 * seq_parts * row_count
    inner_cos, inner_sin = phase_pair(row_count, row_count, row_count, 0, 0)
    back_re = contract("md,cdk->cmk", inner_cos, spec_re) - contract(
        "md,cdk->cmk", inner_sin, spec_im
    )
    back_im = contract("md,cdk->cmk", inner_cos, spec_im) + contract(
        "md,cdk->cmk", inner_sin, spec_re
    )
    twist_cos, twist_sin = phase_pair(2, row_count, period, 2 * lax.axis_index("seq"), 0)
    twist_cos = twist_cos[:, :, None]
    twist_sin = twist_sin[:, :, None]
    turned_re = back_re * twist_cos - back_im * twist_sin
    turned_im = back_im * twist_cos + back_re * twist_sin
    outer_cos, outer_sin = phase_pair(seq_parts, 2 * seq_parts, 2 * seq_parts, 0, 0)
    piece_re = lax.all_to_all(turned_re, "seq", split_axis=1, concat_axis=0, tiled=True)
    piece_im = lax.all_to_all(turned_im, "seq", split_axis=1, concat_axis=0, tiled=True)
    summed = contract("pc,crk->prk", outer_cos, piece_re) - contract(
        "pc,crk->prk", outer_sin, piece_im
    )
    returned = summed * (1.0 / period)
    return lax.all_to_all(returned, "seq", split_axis=0, concat_axis=1, tiled=True)[0]


def spread_layer(qkv, filt, skip_gain, short_weight, w_out, g_out):
    row_count = qkv.shape[1]
    slab_width = qkv.shape[2]
    tail_rows = passed_along(qkv[:, row_count - 2 :, :], "seq", 1)
    extended = jnp.concatenate([tail_rows, qkv], axis=1)
    short = (
        short_weight[:, 0, None, :] * extended[:, 2:, :]
        + short_weight[:, 1, None, :] * extended[:, 1:-1, :]
        + short_weight[:, 2, None, :] * extended[:, :-2, :]
    )
    query_gate = short[0]
    key_short = short[1]
    value_short = short[2]
    mixed = key_short * value_short
    both_re, both_im = forward_spectrum(jnp.concatenate([mixed, filt], axis=1))
    signal_re = both_re[:, :, :slab_width]
    signal_im = both_im[:, :, :slab_width]
    kernel_re = both_re[:, :, slab_width:]
    kernel_im = both_im[:, :, slab_width:]
    conv_out = time_signal(
        signal_re * kernel_re - signal_im * kernel_im, signal_re * kernel_im + signal_im * kernel_re
    )
    long_out = conv_out + skip_gain * mixed
    gated_out = (query_gate * long_out).astype(jnp.bfloat16)
    projected = jnp.dot(
        lax.all_gather(gated_out, "ch", axis=1, tiled=True),
        w_out,
        preferred_element_type=jnp.float32,
    )
    output = projected.astype(jnp.bfloat16)
    grad_all = lax.all_gather(g_out, "ch", axis=1, tiled=True)
    rows_all = lax.all_to_all(w_out, "ch", split_axis=0, concat_axis=1, tiled=True)
    grad_gated = lax.dot_general(
        grad_all, rows_all, (((1,), (1,)), ((), ())), preferred_element_type=jnp.float32
    )
    grad_long = grad_gated * query_gate
    grad_query = grad_gated * long_out
    grad_re, grad_im = forward_spectrum(grad_long)
    pair_re = jnp.concatenate(
        [kernel_re * grad_re + kernel_im * grad_im, signal_re * grad_re + signal_im * grad_im],
        axis=2,
    )
    pair_im = jnp.concatenate(
        [kernel_re * grad_im - kernel_im * grad_re, signal_re * grad_im - signal_im * grad_re],
        axis=2,
    )
    pair_time = time_signal(pair_re, pair_im)
    grad_mixed = pair_time[:, :slab_width] + skip_gain * grad_long
    token_total = lax.axis_size("seq") * row_count
    grad_filter = pair_time[:, slab_width:] * (1.0 / math.sqrt(token_total))
    grad_short = jnp.stack([grad_query, grad_mixed * value_short, grad_mixed * key_short])
    head_rows = passed_along(grad_short[:, :2, :], "seq", -1)
    extended_grad = jnp.concatenate([grad_short, head_rows], axis=1)
    grad_qkv = (
        short_weight[:, 0, None, :] * extended_grad[:, :-2, :]
        + short_weight[:, 1, None, :] * extended_grad[:, 1:-1, :]
        + short_weight[:, 2, None, :] * extended_grad[:, 2:, :]
    ).astype(jnp.bfloat16)
    return (output, grad_qkv, grad_filter)


def split_bf16(values):
    high = values.astype(np.float32).astype(jnp.bfloat16)
    low = (values - high.astype(np.float64)).astype(np.float32).astype(jnp.bfloat16)
    return high, low


def phase_tables(tokens):
    quarter = tokens // PHASES
    freq = 2 * np.arange(quarter)[:, None] + 1
    turn = math.pi / (2 * tokens)
    angle = (freq * PHASES * np.arange(quarter)[None, :] % (4 * tokens)) * turn
    forward = np.concatenate([np.cos(angle), -np.sin(angle)], axis=1)
    backward = np.concatenate([np.cos(angle).T, -np.sin(angle).T], axis=1) / tokens
    angle = freq * np.arange(PHASES)[None, :] * turn
    twist = np.concatenate([np.cos(angle), np.sin(angle)], axis=1)
    twist = np.pad(twist, ((0, 0), (0, LANES - 2 * PHASES)))
    high, rest = split_bf16(twist)
    last = split_bf16(twist - high.astype(np.float64) - rest.astype(np.float64))[0]
    tables = np.zeros((8, quarter, 2 * quarter), jnp.bfloat16)
    tables[0], tables[1] = split_bf16(forward)
    tables[2], tables[3] = split_bf16(backward)
    for i, term in enumerate((high, rest, last)):
        tables[4, :, i * LANES : (i + 1) * LANES] = term
    return tables


def row_order(rows, back=False):
    to, at = [lax.broadcasted_iota(jnp.int32, (rows, rows), int(i != back)) for i in range(2)]
    share = rows // PHASES
    wanted = (to & (share - 1)) * PHASES + lax.shift_right_logical(to, share.bit_length() - 1)
    return jnp.where(wanted == at, 1.0, 0.0).astype(BF16)


def mm(a, b):
    return lax.dot_general(a, b, (((1,), (0,)), ((), ())), preferred_element_type=F32)


def low_lanes(shape):
    return lax.broadcasted_iota(jnp.int32, shape, 1) < HALF


def swap(x):
    return pltpu.roll(x, HALF, 1)


class Near:
    def __init__(self, array, kept=False):
        self.array = array
        self.kept = kept


class Far:
    def __init__(self, array, cuts=None, turned=(), into=None, axis=0):
        self.array = array
        self.turned = turned
        self.into = into
        self.axis = axis
        if turned:
            step = array.shape[0] // len(turned)
            cuts = [(mask * step, step) for mask in turned]
        self.cuts = cuts or [(0, array.shape[axis])]
        self.shape = list(array.shape)
        self.shape[axis] = sum(count for _, count in self.cuts)


class Stage:
    def __init__(self, items, count_in, refs):
        arrays, scratch = list(refs[: len(items)]), list(refs[len(items) :])
        sems = scratch.pop()
        self.count_in = count_in
        self.held, self.copies, self.waiting = [], [], []
        used = 0
        for i, (item, array) in enumerate(zip(items, arrays)):
            group = []
            if isinstance(item, Near):
                self.held.append(array)
            else:
                held = scratch.pop(0) if item.into is None else arrays[count_in + item.into]
                self.held.append(held)
                at = 0
                for cut, (start, count) in enumerate(item.cuts):
                    lead = (slice(None),) * item.axis
                    there = held.at[(*lead, pl.ds(start if item.turned else at, count))]
                    at += count
                    if item.turned:
                        mask = item.turned[cut]
                        start = pl.multiple_of((lax.axis_index("ch") ^ mask) * count, count)
                    here = array.at[(*lead, pl.ds(start, count))]
                    if i >= count_in:
                        here, there = there, here
                    group.append(pltpu.make_async_copy(here, there, sems.at[used]))
                    used += 1
            self.copies.append(group)
            self.waiting.append(set(range(len(group))))
        self.given = set()

    def bring(self, index):
        for copy in self.copies[index]:
            copy.start()

    def take(self, index, cut=None):
        for i in sorted(self.waiting[index]):
            if cut is None or cut == i:
                self.copies[index][i].wait()
                self.waiting[index].discard(i)
        return self.held[index]

    def out(self, index):
        return self.held[self.count_in + index]

    def give(self, index, cut=None):
        for i, copy in enumerate(self.copies[self.count_in + index]):
            if (index, i) not in self.given and cut in (None, i):
                copy.start()
                self.given.add((index, i))


def staged(kernel, items, count_in, *refs):
    stage = Stage(items, count_in, refs)
    for i in range(count_in):
        stage.bring(i)
    kernel(stage)
    for i in range(count_in):
        stage.take(i)
    for i in range(len(items) - count_in):
        stage.give(i)
    for i in range(len(items) - count_in):
        stage.take(count_in + i)


def operand_of(x):
    if isinstance(x, Near) and not x.kept:
        return x.array
    space = pltpu.VMEM if isinstance(x, Near) else pltpu.HBM
    return pltpu.with_memory_space_constraint(x.array, space)


def result_of(x):
    make = pltpu.HBM if isinstance(x, Far) else pltpu.VMEM if x.kept else jax.ShapeDtypeStruct
    return make(x.array.shape, x.array.dtype)


def call(kernel, results, *args, flops=0):
    items = list(args) + list(results)
    specs, scratch, used = [], [], 0
    for item in items:
        near = isinstance(item, Near)
        specs.append(pl.BlockSpec(memory_space=pltpu.VMEM if near else pltpu.HBM))
        if not near:
            used += len(item.cuts)
            if item.into is None:
                scratch.append(pltpu.VMEM(tuple(item.shape), item.array.dtype))
    moved = sum(math.prod(x.array.shape) * x.array.dtype.itemsize for x in items)
    return pl.pallas_call(
        functools.partial(staged, kernel, items, len(args)),
        out_shape=[result_of(x) for x in results],
        in_specs=specs[: len(args)],
        out_specs=specs[len(args) :],
        scratch_shapes=scratch + [pltpu.SemaphoreType.DMA((max(used, 1),))],
        compiler_params=pltpu.CompilerParams(vmem_limit_bytes=VMEM_LIMIT),
        cost_estimate=pl.CostEstimate(flops=flops, bytes_accessed=moved, transcendentals=0),
    )(*[operand_of(x) for x in args])


def lane_tile(x, index):
    return x[:, index * LANES : (index + 1) * LANES]


def pair(first, second):
    low = low_lanes(first.shape)
    return jnp.where(low, first, swap(second)), jnp.where(low, swap(first), second)


def both(x):
    turned, low = swap(x), low_lanes(x.shape)
    return jnp.where(low, x, turned), jnp.where(low, turned, x)


def shifted(x, before):
    rows = lax.broadcasted_iota(jnp.int32, x.shape, 0)
    last, first = before[1:2, :], before[0:1, :]
    one = jnp.where(rows == 0, last, pltpu.roll(x, 1, 0))
    two = jnp.where(rows == 0, first, jnp.where(rows == 1, last, pltpu.roll(x, 2, 0)))
    return one, two


def advanced(x, after):
    count = x.shape[0]
    rows = lax.broadcasted_iota(jnp.int32, x.shape, 0)
    first, last = after[0:1, :], after[1:2, :]
    one = jnp.where(rows == count - 1, first, pltpu.roll(x, count - 1, 0))
    two = jnp.where(
        rows == count - 1, last, jnp.where(rows == count - 2, first, pltpu.roll(x, count - 2, 0))
    )
    return one, two


def put_rows(x, send_ref, at):
    half = x.shape[0] // 2
    for tile in range(x.shape[1] // LANES):
        t = lane_tile(x, tile)
        first, second = pair(t[:half], t[half:])
        send_ref[2 * tile, at : at + half] = first.astype(BF16)
        send_ref[2 * tile + 1, at : at + half] = second.astype(BF16)


def put_strip(x, send_ref, at):
    x = jnp.concatenate([x, jnp.zeros((STRIP - x.shape[0], x.shape[1]), F32)], axis=0)
    for tile in range(x.shape[1] // LANES):
        t = lane_tile(x, tile)
        send_ref[2 * tile, at : at + STRIP] = t.astype(BF16)
        send_ref[2 * tile + 1, at : at + STRIP] = swap(t).astype(BF16)


def strip_of(ref, at):
    tiles = []
    for tile in range(ref.shape[0] // 2):
        x, y = [ref[2 * tile + i, at : at + STRIP].astype(F32) for i in range(2)]
        tiles.append(jnp.where(low_lanes(x.shape), x, swap(y)))
    return jnp.concatenate(tiles, axis=1)


def exact_rows(x):
    high = x.astype(BF16).astype(F32)
    return jnp.concatenate([high, x - high], axis=0)


def start_kernel(stage):
    send_ref, qkv_ref = stage.out(0), stage.take(0)
    rows = qkv_ref.shape[1]
    order = row_order(rows)
    query = qkv_ref[0].astype(F32)
    key, value = mm(order, qkv_ref[1]), mm(order, qkv_ref[2])
    for tile in range(key.shape[1] // LANES):
        x, y = pair(lane_tile(key, tile), lane_tile(value, tile))
        send_ref[2 * tile, :rows] = x.astype(BF16)
        send_ref[2 * tile + 1, :rows] = y.astype(BF16)
    put_strip(jnp.concatenate([query[:2], query[rows - 2 :]], axis=0), send_ref, rows + rows // 2)
    put_rows(mm(order, stage.take(1)[...].astype(BF16)), send_ref, rows)


def partial_product(g, w_ref, mask):
    width = g.shape[1]
    w = w_ref[mask * width : (mask + 1) * width, :]
    return lax.dot_general(g, w, (((1,), (1,)), ((), ())), preferred_element_type=F32)


def first_product_kernel(stage):
    g, out_ref = stage.take(0)[...], stage.out(0)
    for i, mask in enumerate((1, 3)):
        out_ref[i] = partial_product(g, stage.take(1, i), mask).astype(BF16)


def second_product_kernel(stage):
    w_ref, g, near_ref = stage.take(1), stage.take(0)[...], stage.take(2)
    across_ref, own_ref = stage.out(0), stage.out(1)
    across = partial_product(g, w_ref, 2) + near_ref[1].astype(F32)
    across_ref[...] = across.astype(BF16)
    stage.give(0)
    own_ref[...] = partial_product(g, w_ref, 0) + near_ref[0].astype(F32)


def sum_kernel(stage):
    send_ref, kept_ref = stage.out(0), stage.out(1)
    weight_ref, q = stage.take(3), stage.take(4)[0].astype(F32)
    rows = q.shape[0]
    one, two = shifted(q, jnp.zeros((2, q.shape[1]), F32))
    query = weight_ref[0, 0:1, :] * q + weight_ref[0, 1:2, :] * one + weight_ref[0, 2:3, :] * two
    grad_gated = stage.take(0)[...] + stage.take(1)[...].astype(F32)
    put_rows(mm(row_order(rows), (grad_gated * query).astype(BF16)), send_ref, 0)
    first = exact_rows(grad_gated[:2])
    put_strip(jnp.concatenate([jnp.zeros_like(first), first], axis=0), send_ref, rows // 2)
    stage.give(0)
    kept_ref[0] = query
    kept_ref[1] = grad_gated


def spread_phases(parts):
    (a_re, a_im), (b_re, b_im), (c_re, c_im), (d_re, d_im) = parts
    s_re, s_im, t_re, t_im = a_re + c_re, a_im + c_im, a_re - c_re, a_im - c_im
    u_re, u_im, v_re, v_im = b_re + d_re, b_im + d_im, b_re - d_re, b_im - d_im
    return [
        (s_re + u_re, s_im + u_im),
        (t_re + v_im, t_im - v_re),
        (s_re - u_re, s_im - u_im),
        (t_re - v_im, t_im + v_re),
    ]


def gather_phases(parts):
    (a_re, a_im), (b_re, b_im), (c_re, c_im), (d_re, d_im) = parts
    s_re, s_im, t_re, t_im = a_re + c_re, a_im + c_im, a_re - c_re, a_im - c_im
    u_re, u_im, v_re, v_im = b_re + d_re, b_im + d_im, b_re - d_re, b_im - d_im
    return [
        (s_re + u_re, s_im + u_im),
        (t_re - v_im, t_im + v_re),
        (s_re - u_re, s_im - u_im),
        (t_re + v_im, t_im - v_re),
    ]


def rows_of(ref, start, count):
    block = ref[:, start : start + count, :]
    return block.reshape(ref.shape[0] * count, ref.shape[2])


def turned_back(re, im, twist, phase):
    if phase == 0:
        return re, im
    c, s = twist[:, phase : phase + 1], twist[:, PHASES + phase : PHASES + phase + 1]
    return re * c + im * s, im * c - re * s


def turned_on(re, im, twist, phase):
    if phase == 0:
        return re, im
    c, s = twist[:, phase : phase + 1], twist[:, PHASES + phase : PHASES + phase + 1]
    return re * c - im * s, re * s + im * c


def lane_tile(x, index):
    return x[:, index * LANES : (index + 1) * LANES]


def causal(parts, weight):
    rows = lax.broadcasted_iota(jnp.int32, parts[0].shape, 0)
    two, three = [jnp.where(rows == 0, 0.0, pltpu.roll(parts[p], 1, 0)) for p in (2, 3)]
    once, twice = [three, *parts[:3]], [two, three, *parts[:2]]
    return [
        weight[0:1] * x + weight[1:2] * y + weight[2:3] * z for x, y, z in zip(parts, once, twice)
    ]


def anticausal(parts, weight):
    count = parts[0].shape[0]
    rows = lax.broadcasted_iota(jnp.int32, parts[0].shape, 0)
    zero, one = [
        jnp.where(rows == count - 1, 0.0, pltpu.roll(parts[p], count - 1, 0)) for p in (0, 1)
    ]
    once, twice = [*parts[1:], zero], [*parts[2:], zero, one]
    return [
        weight[0:1] * x + weight[1:2] * y + weight[2:3] * z for x, y, z in zip(parts, once, twice)
    ]


def halves(x):
    high = x.astype(BF16)
    return high, (x - high.astype(F32)).astype(BF16)


def twiddles(table_ref):
    terms = [table_ref[2, :, i * LANES : (i + 1) * LANES].astype(F32) for i in range(3)]
    return terms[0] + (terms[1] + terms[2])


def columns(parts):
    return jnp.concatenate(parts, axis=1)


def two_sides(table, x):
    quarter = table.shape[0]
    return [mm(table[:, :quarter], x), mm(table[:, quarter:], x)]


def spectrum_of(sides, twist):
    turned = []
    for phase, (re, im) in enumerate(sides):
        turned.append(turned_back(re, im, twist, phase))
    return spread_phases(turned)


def back_values(spectrum, twist):
    return [
        jnp.concatenate(turned_on(re, im, twist, phase), axis=0)
        for phase, (re, im) in enumerate(gather_phases(spectrum))
    ]


def own_weights(weight_ref, gain_ref):
    place = lax.axis_index("seq")
    lanes = pl.ds(pl.multiple_of(place // 2 * LANES, LANES), LANES)
    odd = place % 2 == 1

    def mine(x):
        return jnp.where(odd, swap(x), x)

    query, key, value = [mine(weight_ref[i, :, lanes]) for i in range(3)]
    gain = both(mine(gain_ref[:, lanes]))[0]
    return jnp.where(low_lanes(key.shape), key, swap(value)), query, gain


def forward_kernel(stage):
    recv_ref, weight_ref, gain_ref = [stage.take(i) for i in range(3)]
    send_ref, saved_ref = stage.out(0), stage.out(1)
    blocks = recv_ref.shape[0]
    rows = (recv_ref.shape[1] - STRIP) * 2 // 3
    share = rows // PHASES
    quarter = blocks * share
    low = low_lanes((quarter, LANES))
    pair_weight, query_weight, gain = own_weights(weight_ref, gain_ref)
    saved_ref[14, 0:3, :] = pair_weight
    saved_ref[14, 8:9, :] = gain
    firsts = [jnp.zeros((STRIP, LANES), F32)]
    for i in range(blocks):
        firsts.append(recv_ref[i, rows + rows // 2 :, :].astype(F32))
    w = [query_weight[i : i + 1] for i in range(3)]
    for i in range(blocks):
        last, own = firsts[i], firsts[i + 1]
        zero = w[0] * own[0:1] + w[1] * last[3:4] + w[2] * last[2:3]
        one = w[0] * own[1:2] + w[1] * own[0:1] + w[2] * last[3:4]
        query = jnp.concatenate([zero, one], axis=0)
        saved_ref[14, 16 + 8 * i : 18 + 8 * i, :] = query
        query = jnp.concatenate([exact_rows(query), jnp.zeros((STRIP - 4, LANES), F32)], axis=0)
        send_ref[i, rows:, :] = query.astype(BF16)

    starts = [phase * share for phase in range(PHASES)]
    pairs = causal([rows_of(recv_ref, at, share).astype(F32) for at in starts], pair_weight)
    taps = [rows_of(recv_ref, rows + at, share).astype(F32) for at in starts[:2]]
    taps = [swap(x) for x in taps] + taps
    for phase in range(PHASES):
        saved_ref[8 + phase] = pairs[phase]
    mixed = [x * swap(x) for x in pairs]

    fh, fl = stage.take(3)[0], stage.take(3)[1]
    twist = twiddles(stage.take(3))
    high = [jnp.where(low, x, y).astype(BF16) for x, y in zip(mixed, taps)]
    rest = [x - y.astype(F32) for x, y in zip(mixed, high)]
    rest = [jnp.where(low, rest[i], swap(rest[i + 2])).astype(BF16) for i in range(2)]
    high, rest = columns(high), columns(rest)
    main = [x + y for x, y in zip(two_sides(fh, high), two_sides(fl, high))]
    more = two_sides(fh, rest)
    sides = []
    for phase in range(PHASES):
        extra = [lane_tile(x, phase % 2) for x in more]
        if phase >= 2:
            extra = [swap(x) for x in extra]
        sides.append([lane_tile(x, phase) + jnp.where(low, y, 0.0) for x, y in zip(main, extra)])
    grad_ref = stage.take(5)
    send_ref[:, rows // 2 : rows, :] = grad_ref[:, : rows // 2, :]
    send_ref[:, rows:, :] = send_ref[:, rows:, :] + grad_ref[:, rows // 2 :, :]
    stage.give(0, 1)
    product = []
    for r, (re, im) in enumerate(spectrum_of(sides, twist)):
        saved_ref[2 * r] = re
        saved_ref[2 * r + 1] = im
        other_re, other_im = swap(re), swap(im)
        product.append((re * other_re - im * other_im, re * other_im + im * other_re))

    values = back_values(product, twist)
    bh, bl = stage.take(4)[0], stage.take(4)[1]
    wide = low_lanes((2 * quarter, LANES))
    high = [x.astype(BF16) for x in values]
    wider = [x.astype(F32) for x in high]
    both_parts = [jnp.where(wide, y, x - y).astype(BF16) for x, y in zip(values, wider)]
    high = [jnp.where(wide, wider[i], wider[i + 2]).astype(BF16) for i in range(2)]
    main, more = mm(bh, columns(both_parts)), mm(bl, columns(high))
    summed = [x + swap(x) for x in (lane_tile(main, phase) for phase in range(PHASES))]
    for i in range(2):
        conv = jnp.where(low, summed[i], summed[i + 2]) + lane_tile(more, i)
        long_out = conv + gain * jnp.where(low, mixed[i], mixed[i + 2])
        saved_ref[12 + i] = long_out
        packed = long_out.astype(BF16).reshape(blocks, share, LANES)
        send_ref[:, starts[i] : starts[i] + share, :] = packed


def backward_kernel(stage):
    grad_ref, saved_ref = stage.take(0), stage.take(1)
    send_ref = stage.out(0)
    blocks = grad_ref.shape[0]
    rows = grad_ref.shape[1] - STRIP
    share = rows // PHASES
    quarter = blocks * share
    low = low_lanes((quarter, LANES))
    pair_weight, gain = saved_ref[14, 0:3, :], saved_ref[14, 8:9, :]

    starts = [phase * share for phase in range(PHASES)]
    firsts = [[], []]
    heads = []
    for block in range(blocks):
        strip = grad_ref[block, rows:, :].astype(F32)
        first = strip[4:6] + strip[6:8]
        fixed = first * saved_ref[14, 16 + 8 * block : 18 + 8 * block, :]
        long_out = [saved_ref[12 + i, block * share : block * share + 1, :] for i in range(2)]
        heads.append(first * jnp.concatenate(long_out, axis=0))
        for i in range(2):
            firsts[i].append(jnp.broadcast_to(fixed[i : i + 1], (share, LANES)))
    heads.append(jnp.zeros_like(heads[0]))
    for block in range(blocks):
        head = exact_rows(heads[block + 1])
        head = jnp.concatenate([head, jnp.zeros((STRIP - 4, LANES), F32)], axis=0)
        send_ref[block, rows + rows // 2 :, :] = head.astype(BF16)
    stage.give(0, 2)
    starting = lax.broadcasted_iota(jnp.int32, (quarter, LANES), 0) & (share - 1)
    starting = (starting == 0) & low
    grad_long = []
    for at, first in zip(starts[2:], firsts):
        x = rows_of(grad_ref, at, share).astype(F32)
        grad_long.append(jnp.where(starting, jnp.concatenate(first, axis=0), x))

    fh, fl = stage.take(2)[0], stage.take(2)[1]
    twist = twiddles(stage.take(2))
    high, rest = halves(columns(grad_long))
    three = zip(two_sides(fh, high), two_sides(fl, high), two_sides(fh, rest))
    main = [x + y + z for x, y, z in three]
    sides = []
    for phase in range(PHASES):
        sides.append([both(lane_tile(x, phase % 2))[phase // 2] for x in main])
    product = []
    for r, (re, im) in enumerate(spectrum_of(sides, twist)):
        k_re, k_im = saved_ref[2 * r], saved_ref[2 * r + 1]
        product.append((k_re * re + k_im * im, k_re * im - k_im * re))
    high, rest = halves(columns(back_values(product, twist)))
    bh, bl = stage.take(3)[0], stage.take(3)[1]
    times = mm(bh, high) + mm(bl, high) + mm(bh, rest)
    times = [lane_tile(times, phase) for phase in range(PHASES)]

    scale = 1.0 / math.sqrt(PHASES * quarter)
    for i, at in enumerate(starts[:2]):
        y = (jnp.where(low, times[i], swap(times[i + 2])) * scale).astype(BF16)
        send_ref[:, rows + at : rows + at + share, :] = y.reshape(blocks, share, LANES)
    stage.give(0, 1)
    grad_long = [both(x)[i] for i in range(2) for x in grad_long]
    grad_mixed = [both(x + gain * y)[1] for x, y in zip(times, grad_long)]
    grad_pairs = anticausal(
        [x * swap(saved_ref[8 + phase]) for phase, x in enumerate(grad_mixed)], pair_weight
    )
    for phase, at in enumerate(starts):
        x = grad_pairs[phase].astype(BF16)
        send_ref[:, at : at + share, :] = x.reshape(blocks, share, LANES)


def unpacked(ref, at, half, order):
    tiles = []
    for tile in range(ref.shape[0] // 2):
        x, y = [ref[2 * tile + i, at : at + half].astype(F32) for i in range(2)]
        top, bottom = pair(x, y)
        tiles.append(jnp.concatenate([top, bottom], axis=0))
    return mm(order, jnp.concatenate(tiles, axis=1).astype(BF16))


def gate_kernel(stage):
    recv_ref, kept_ref, gated_ref, grad_ref = stage.take(0), stage.take(1), stage.out(0), stage.out(1)
    rows = recv_ref.shape[1] - STRIP
    long_out = unpacked(recv_ref, 0, rows // 2, row_order(rows, back=True))
    strip = strip_of(recv_ref, rows)
    first = strip[0:2] + strip[2:4]
    grad_ref[...] = kept_ref[1] * long_out
    gated_ref[...] = (kept_ref[0] * long_out).astype(BF16)
    tile = (first * long_out[0:2]).astype(F32)
    at = lax.broadcasted_iota(jnp.int32, (STRIP, long_out.shape[1]), 0)
    top = kept_ref[0, 0:STRIP, :] * long_out[0:STRIP]
    top = jnp.where(at == 0, tile[0:1], jnp.where(at == 1, tile[1:2], top))
    gated_ref[0:STRIP, :] = top.astype(BF16)


def output_kernel(parts, stage):
    w_ref, total = stage.take(0), None
    for part in range(parts):
        gated = stage.take(1 + part)[...]
        width = gated.shape[1]
        term = mm(gated, w_ref[part * width : (part + 1) * width, :])
        total = term if total is None else total + term
    stage.out(0)[...] = total.astype(BF16)


def end_kernel(stage):
    recv_ref, grad_ref, filter_ref = stage.take(0), stage.out(0), stage.out(1)
    rows = grad_ref.shape[1]
    order = row_order(rows, back=True)
    filter_ref[...] = unpacked(recv_ref, rows, rows // 2, order)
    stage.give(1)
    firsts, seconds = [], []
    for tile in range(recv_ref.shape[0] // 2):
        first, second = pair(*[recv_ref[2 * tile + i, :rows].astype(F32) for i in range(2)])
        firsts.append(first)
        seconds.append(second)
    for i, side in enumerate((firsts, seconds)):
        x = mm(order, jnp.concatenate(side, axis=1).astype(BF16))
        grad_ref[1 + i] = x.astype(BF16)
    query, weight_ref = stage.take(1)[...], stage.take(2)
    strip = strip_of(recv_ref, rows + rows // 2)
    one, two = advanced(query, strip[0:2] + strip[2:4])
    grad_ref[0] = (
        weight_ref[0, 0:1, :] * query + weight_ref[0, 1:2, :] * one + weight_ref[0, 2:3, :] * two
    ).astype(BF16)


def partner(x, axis, mask):
    return lax.ppermute(x, axis, [(i, i ^ mask) for i in range(lax.axis_size(axis))])


def exchanged(x, axis):
    return lax.all_to_all(x, axis, split_axis=0, concat_axis=0, tiled=True)


def owner_layer(qkv, filt, skip_gain, short_weight, w_out, g_out):
    shape = jax.ShapeDtypeStruct
    seq_parts, ch_parts = lax.axis_size("seq"), lax.axis_size("ch")
    rows, width = qkv.shape[1], qkv.shape[2]
    tokens = seq_parts * rows
    quarter = tokens // PHASES
    tables = jnp.asarray(phase_tables(tokens))
    table_flops = 2 * 2 * 2 * 3 * tokens * tokens // PHASES * LANES
    product_flops = 2 * rows * width * width * ch_parts
    half = rows // 2
    wide = shape((seq_parts, rows + half + STRIP, LANES), BF16)
    column = shape((rows, width), BF16)
    saved = shape((15, quarter, LANES), F32)
    gain = skip_gain[None, :]

    (send,) = call(start_kernel, [Far(wide)], Far(qkv), Far(filt))
    recv = exchanged(send, "seq")
    half_sums, w_kept, g_kept = call(
        first_product_kernel,
        [
            Near(shape((2, rows, width), BF16), kept=True),
            Near(w_out, kept=True),
            Near(g_out, kept=True),
        ],
        Far(g_out, into=2),
        Far(w_out, turned=(1, 3, 2, 0), into=1),
        flops=product_flops // 2,
    )
    half_sums = partner(half_sums, "ch", 1)
    across, own = call(
        second_product_kernel,
        [Near(column, kept=True), Near(shape((rows, width), F32), kept=True)],
        Near(g_kept),
        Near(w_kept),
        Near(half_sums),
        flops=product_flops // 2,
    )
    across = partner(across, "ch", 2)
    def pinned(x):
        return Near(x, kept=True)

    tables_back = Far(tables, [(2, 2)])
    grad_long, kept, tables_on, weight, gain = call(
        sum_kernel,
        [
            Far(shape((seq_parts, half + STRIP, LANES), BF16)),
            pinned(shape((2, rows, width), F32)),
            pinned(shape((3, *tables.shape[1:]), BF16)),
            pinned(short_weight),
            pinned(gain),
        ],
        Near(own),
        Near(across),
        Far(tables, [(0, 2), (4, 1)], into=2),
        Far(short_weight, into=3),
        Far(qkv, [(0, 1)]),
        Far(gain, into=4),
    )
    send, saved = call(
        forward_kernel,
        [
            Far(
                shape((seq_parts, rows + STRIP, LANES), BF16),
                [(0, half), (half, half + STRIP)],
                axis=1,
            ),
            pinned(saved),
        ],
        pinned(recv),
        Near(weight),
        Near(gain),
        Near(tables_on),
        tables_back,
        Far(grad_long),
        flops=table_flops,
    )
    swapped = exchanged(send, "seq")
    (send,) = call(
        backward_kernel,
        [Far(wide, [(0, rows), (rows, half), (rows + half, STRIP)], axis=1)],
        Near(swapped),
        Near(saved),
        Near(tables_on),
        tables_back,
        flops=table_flops,
    )
    grad_recv = exchanged(send, "seq")
    gated, grad_query = call(
        gate_kernel, [pinned(column), pinned(shape((rows, width), F32))], Near(swapped), Near(kept)
    )
    across = partner(gated, "ch", 2)
    near, far = partner(gated, "ch", 1), partner(across, "ch", 1)
    (output,) = call(
        functools.partial(output_kernel, ch_parts),
        [Far(column)],
        Near(w_kept),
        Near(gated),
        Near(near),
        Near(across),
        Near(far),
        flops=product_flops,
    )
    grad_qkv, grad_filter = call(
        end_kernel,
        [Far(shape((3, rows, width), BF16)), Far(shape((rows, width), F32))],
        Near(grad_recv),
        Near(grad_query),
        Far(short_weight),
    )
    return (output, grad_qkv, grad_filter)


def local(qkv, filt, skip_gain, short_weight, w_out, g_out):
    seq_parts = lax.axis_size("seq")
    rows, width = qkv.shape[1], qkv.shape[2]
    fits = width == HALF * seq_parts and rows % HALF == 0 and rows & (rows - 1) == 0 and rows * seq_parts <= 2048
    if fits and lax.axis_size("ch") == 4:
        return owner_layer(qkv, filt, skip_gain, short_weight, w_out, g_out)
    return spread_layer(qkv, filt, skip_gain, short_weight, w_out, g_out)


def solution(mesh):
    in_specs = (
        P(None, "seq", "ch"),
        P("seq", "ch"),
        P("ch"),
        P(None, None, "ch"),
        P(None, "ch"),
        P("seq", "ch"),
    )
    out_specs = (P("seq", "ch"), P(None, "seq", "ch"), P("seq", "ch"))
    return jax.shard_map(local, mesh=mesh, in_specs=in_specs, out_specs=out_specs, check_vma=False)
```

```python
import functools
import math

import jax
import jax.numpy as jnp
import numpy as np
from jax import lax
from jax.experimental import pallas as pl
from jax.experimental.pallas import tpu as pltpu
from jax.sharding import PartitionSpec as P

HIGHEST = lax.Precision.HIGHEST
TWO_PI = 2.0 * math.pi
LANES = 128
HALF = 64
PHASES = 4
STRIP = 16
BF16 = jnp.bfloat16
F32 = jnp.float32
VMEM_LIMIT = 24 * 1024 * 1024


def passed_along(block, axis, distance):
    devices = range(lax.axis_size(axis))
    route = [(i - distance, i) for i in devices if i - distance in devices]
    return lax.ppermute(block, axis, route)


def phase_pair(left_count, right_count, period, left_start, right_start):
    left_idx = lax.broadcasted_iota(jnp.int32, (left_count, right_count), 0) + left_start
    right_idx = lax.broadcasted_iota(jnp.int32, (left_count, right_count), 1) + right_start
    angle_all = (left_idx * right_idx % period).astype(jnp.float32) * (TWO_PI / period)
    return (jnp.cos(angle_all), jnp.sin(angle_all))


def contract(pattern, matrix, values):
    return jnp.einsum(
        pattern, matrix, values, precision=HIGHEST, preferred_element_type=jnp.float32
    )


def forward_spectrum(signal):
    seq_parts = lax.axis_size("seq")
    row_count = signal.shape[0]
    row_share = row_count // seq_parts
    period = 2 * seq_parts * row_count
    spread_in = lax.all_to_all(signal[None], "seq", split_axis=1, concat_axis=0, tiled=True)
    outer_cos, outer_sin = phase_pair(2 * seq_parts, seq_parts, 2 * seq_parts, 0, 0)
    section_re = contract("cp,prw->crw", outer_cos, spread_in)
    section_im = -contract("cp,prw->crw", outer_sin, spread_in)
    twist_cos, twist_sin = phase_pair(
        2 * seq_parts, row_share, period, 0, lax.axis_index("seq") * row_share
    )
    twist_cos = twist_cos[:, :, None]
    twist_sin = twist_sin[:, :, None]
    turned_re = section_re * twist_cos + section_im * twist_sin
    turned_im = section_im * twist_cos - section_re * twist_sin
    inner_cos, inner_sin = phase_pair(row_count, row_count, row_count, 0, 0)
    piece_re = lax.all_to_all(turned_re, "seq", split_axis=0, concat_axis=1, tiled=True)
    piece_im = lax.all_to_all(turned_im, "seq", split_axis=0, concat_axis=1, tiled=True)
    spec_re = contract("dm,cmk->cdk", inner_cos, piece_re) + contract(
        "dm,cmk->cdk", inner_sin, piece_im
    )
    spec_im = contract("dm,cmk->cdk", inner_cos, piece_im) - contract(
        "dm,cmk->cdk", inner_sin, piece_re
    )
    return (spec_re, spec_im)


def time_signal(spec_re, spec_im):
    seq_parts = lax.axis_size("seq")
    row_count = spec_re.shape[1]
    period = 2 * seq_parts * row_count
    inner_cos, inner_sin = phase_pair(row_count, row_count, row_count, 0, 0)
    back_re = contract("md,cdk->cmk", inner_cos, spec_re) - contract(
        "md,cdk->cmk", inner_sin, spec_im
    )
    back_im = contract("md,cdk->cmk", inner_cos, spec_im) + contract(
        "md,cdk->cmk", inner_sin, spec_re
    )
    twist_cos, twist_sin = phase_pair(2, row_count, period, 2 * lax.axis_index("seq"), 0)
    twist_cos = twist_cos[:, :, None]
    twist_sin = twist_sin[:, :, None]
    turned_re = back_re * twist_cos - back_im * twist_sin
    turned_im = back_im * twist_cos + back_re * twist_sin
    outer_cos, outer_sin = phase_pair(seq_parts, 2 * seq_parts, 2 * seq_parts, 0, 0)
    piece_re = lax.all_to_all(turned_re, "seq", split_axis=1, concat_axis=0, tiled=True)
    piece_im = lax.all_to_all(turned_im, "seq", split_axis=1, concat_axis=0, tiled=True)
    summed = contract("pc,crk->prk", outer_cos, piece_re) - contract(
        "pc,crk->prk", outer_sin, piece_im
    )
    returned = summed * (1.0 / period)
    return lax.all_to_all(returned, "seq", split_axis=0, concat_axis=1, tiled=True)[0]


def spread_layer(qkv, filt, skip_gain, short_weight, w_out, g_out):
    row_count = qkv.shape[1]
    slab_width = qkv.shape[2]
    tail_rows = passed_along(qkv[:, row_count - 2 :, :], "seq", 1)
    extended = jnp.concatenate([tail_rows, qkv], axis=1)
    short = (
        short_weight[:, 0, None, :] * extended[:, 2:, :]
        + short_weight[:, 1, None, :] * extended[:, 1:-1, :]
        + short_weight[:, 2, None, :] * extended[:, :-2, :]
    )
    query_gate = short[0]
    key_short = short[1]
    value_short = short[2]
    mixed = key_short * value_short
    both_re, both_im = forward_spectrum(jnp.concatenate([mixed, filt], axis=1))
    signal_re = both_re[:, :, :slab_width]
    signal_im = both_im[:, :, :slab_width]
    kernel_re = both_re[:, :, slab_width:]
    kernel_im = both_im[:, :, slab_width:]
    conv_out = time_signal(
        signal_re * kernel_re - signal_im * kernel_im, signal_re * kernel_im + signal_im * kernel_re
    )
    long_out = conv_out + skip_gain * mixed
    gated_out = (query_gate * long_out).astype(jnp.bfloat16)
    projected = jnp.dot(
        lax.all_gather(gated_out, "ch", axis=1, tiled=True),
        w_out,
        preferred_element_type=jnp.float32,
    )
    output = projected.astype(jnp.bfloat16)
    grad_all = lax.all_gather(g_out, "ch", axis=1, tiled=True)
    rows_all = lax.all_to_all(w_out, "ch", split_axis=0, concat_axis=1, tiled=True)
    grad_gated = lax.dot_general(
        grad_all, rows_all, (((1,), (1,)), ((), ())), preferred_element_type=jnp.float32
    )
    grad_long = grad_gated * query_gate
    grad_query = grad_gated * long_out
    grad_re, grad_im = forward_spectrum(grad_long)
    pair_re = jnp.concatenate(
        [kernel_re * grad_re + kernel_im * grad_im, signal_re * grad_re + signal_im * grad_im],
        axis=2,
    )
    pair_im = jnp.concatenate(
        [kernel_re * grad_im - kernel_im * grad_re, signal_re * grad_im - signal_im * grad_re],
        axis=2,
    )
    pair_time = time_signal(pair_re, pair_im)
    grad_mixed = pair_time[:, :slab_width] + skip_gain * grad_long
    token_total = lax.axis_size("seq") * row_count
    grad_filter = pair_time[:, slab_width:] * (1.0 / math.sqrt(token_total))
    grad_short = jnp.stack([grad_query, grad_mixed * value_short, grad_mixed * key_short])
    head_rows = passed_along(grad_short[:, :2, :], "seq", -1)
    extended_grad = jnp.concatenate([grad_short, head_rows], axis=1)
    grad_qkv = (
        short_weight[:, 0, None, :] * extended_grad[:, :-2, :]
        + short_weight[:, 1, None, :] * extended_grad[:, 1:-1, :]
        + short_weight[:, 2, None, :] * extended_grad[:, 2:, :]
    ).astype(jnp.bfloat16)
    return (output, grad_qkv, grad_filter)


def split_bf16(values):
    high = values.astype(np.float32).astype(jnp.bfloat16)
    low = (values - high.astype(np.float64)).astype(np.float32).astype(jnp.bfloat16)
    return high, low


def phase_tables(tokens):
    quarter = tokens // PHASES
    freq = 2 * np.arange(quarter)[:, None] + 1
    turn = math.pi / (2 * tokens)
    angle = (freq * PHASES * np.arange(quarter)[None, :] % (4 * tokens)) * turn
    forward = np.concatenate([np.cos(angle), -np.sin(angle)], axis=1)
    backward = np.concatenate([np.cos(angle).T, -np.sin(angle).T], axis=1) / tokens
    angle = freq * np.arange(PHASES)[None, :] * turn
    twist = np.concatenate([np.cos(angle), np.sin(angle)], axis=1)
    twist = np.pad(twist, ((0, 0), (0, LANES - 2 * PHASES)))
    high, rest = split_bf16(twist)
    last = split_bf16(twist - high.astype(np.float64) - rest.astype(np.float64))[0]
    tables = np.zeros((8, quarter, 2 * quarter), jnp.bfloat16)
    tables[0], tables[1] = split_bf16(forward)
    tables[2], tables[3] = split_bf16(backward)
    for i, term in enumerate((high, rest, last)):
        tables[4, :, i * LANES : (i + 1) * LANES] = term
    return tables


def row_order(rows, back=False):
    to, at = [lax.broadcasted_iota(jnp.int32, (rows, rows), int(i != back)) for i in range(2)]
    share = rows // PHASES
    wanted = (to & (share - 1)) * PHASES + lax.shift_right_logical(to, share.bit_length() - 1)
    return jnp.where(wanted == at, 1.0, 0.0).astype(BF16)


def mm(a, b):
    return lax.dot_general(a, b, (((1,), (0,)), ((), ())), preferred_element_type=F32)


def low_lanes(shape):
    return lax.broadcasted_iota(jnp.int32, shape, 1) < HALF


def swap(x):
    return pltpu.roll(x, HALF, 1)


class Near:
    def __init__(self, array, kept=False):
        self.array = array
        self.kept = kept


class Far:
    def __init__(self, array, cuts=None, turned=(), into=None, axis=0):
        self.array = array
        self.turned = turned
        self.into = into
        self.axis = axis
        if turned:
            step = array.shape[0] // len(turned)
            cuts = [(mask * step, step) for mask in turned]
        self.cuts = cuts or [(0, array.shape[axis])]
        self.shape = list(array.shape)
        self.shape[axis] = sum(count for _, count in self.cuts)


class Stage:
    def __init__(self, items, count_in, refs):
        arrays, scratch = list(refs[: len(items)]), list(refs[len(items) :])
        sems = scratch.pop()
        self.count_in = count_in
        self.held, self.copies, self.waiting = [], [], []
        used = 0
        for i, (item, array) in enumerate(zip(items, arrays)):
            group = []
            if isinstance(item, Near):
                self.held.append(array)
            else:
                held = scratch.pop(0) if item.into is None else arrays[count_in + item.into]
                self.held.append(held)
                at = 0
                for cut, (start, count) in enumerate(item.cuts):
                    lead = (slice(None),) * item.axis
                    there = held.at[(*lead, pl.ds(start if item.turned else at, count))]
                    at += count
                    if item.turned:
                        mask = item.turned[cut]
                        start = pl.multiple_of((lax.axis_index("ch") ^ mask) * count, count)
                    here = array.at[(*lead, pl.ds(start, count))]
                    if i >= count_in:
                        here, there = there, here
                    group.append(pltpu.make_async_copy(here, there, sems.at[used]))
                    used += 1
            self.copies.append(group)
            self.waiting.append(set(range(len(group))))
        self.given = set()

    def bring(self, index):
        for copy in self.copies[index]:
            copy.start()

    def take(self, index, cut=None):
        for i in sorted(self.waiting[index]):
            if cut is None or cut == i:
                self.copies[index][i].wait()
                self.waiting[index].discard(i)
        return self.held[index]

    def out(self, index):
        return self.held[self.count_in + index]

    def give(self, index, cut=None):
        for i, copy in enumerate(self.copies[self.count_in + index]):
            if (index, i) not in self.given and cut in (None, i):
                copy.start()
                self.given.add((index, i))


def staged(kernel, items, count_in, *refs):
    stage = Stage(items, count_in, refs)
    for i in range(count_in):
        stage.bring(i)
    kernel(stage)
    for i in range(count_in):
        stage.take(i)
    for i in range(len(items) - count_in):
        stage.give(i)
    for i in range(len(items) - count_in):
        stage.take(count_in + i)


def operand_of(x):
    if isinstance(x, Near) and not x.kept:
        return x.array
    space = pltpu.VMEM if isinstance(x, Near) else pltpu.HBM
    return pltpu.with_memory_space_constraint(x.array, space)


def result_of(x):
    make = pltpu.HBM if isinstance(x, Far) else pltpu.VMEM if x.kept else jax.ShapeDtypeStruct
    return make(x.array.shape, x.array.dtype)


def call(kernel, results, *args, flops=0):
    items = list(args) + list(results)
    specs, scratch, used = [], [], 0
    for item in items:
        near = isinstance(item, Near)
        specs.append(pl.BlockSpec(memory_space=pltpu.VMEM if near else pltpu.HBM))
        if not near:
            used += len(item.cuts)
            if item.into is None:
                scratch.append(pltpu.VMEM(tuple(item.shape), item.array.dtype))
    moved = sum(math.prod(x.array.shape) * x.array.dtype.itemsize for x in items)
    return pl.pallas_call(
        functools.partial(staged, kernel, items, len(args)),
        out_shape=[result_of(x) for x in results],
        in_specs=specs[: len(args)],
        out_specs=specs[len(args) :],
        scratch_shapes=scratch + [pltpu.SemaphoreType.DMA((max(used, 1),))],
        compiler_params=pltpu.CompilerParams(vmem_limit_bytes=VMEM_LIMIT),
        cost_estimate=pl.CostEstimate(flops=flops, bytes_accessed=moved, transcendentals=0),
    )(*[operand_of(x) for x in args])


def lane_tile(x, index):
    return x[:, index * LANES : (index + 1) * LANES]


def pair(first, second):
    low = low_lanes(first.shape)
    return jnp.where(low, first, swap(second)), jnp.where(low, swap(first), second)


def both(x):
    turned, low = swap(x), low_lanes(x.shape)
    return jnp.where(low, x, turned), jnp.where(low, turned, x)


def shifted(x, before):
    rows = lax.broadcasted_iota(jnp.int32, x.shape, 0)
    last, first = before[1:2, :], before[0:1, :]
    one = jnp.where(rows == 0, last, pltpu.roll(x, 1, 0))
    two = jnp.where(rows == 0, first, jnp.where(rows == 1, last, pltpu.roll(x, 2, 0)))
    return one, two


def advanced(x, after):
    count = x.shape[0]
    rows = lax.broadcasted_iota(jnp.int32, x.shape, 0)
    first, last = after[0:1, :], after[1:2, :]
    one = jnp.where(rows == count - 1, first, pltpu.roll(x, count - 1, 0))
    two = jnp.where(
        rows == count - 1, last, jnp.where(rows == count - 2, first, pltpu.roll(x, count - 2, 0))
    )
    return one, two


def put_rows(x, send_ref, at):
    half = x.shape[0] // 2
    for tile in range(x.shape[1] // LANES):
        t = lane_tile(x, tile)
        first, second = pair(t[:half], t[half:])
        send_ref[2 * tile, at : at + half] = first.astype(BF16)
        send_ref[2 * tile + 1, at : at + half] = second.astype(BF16)


def put_strip(x, send_ref, at):
    x = jnp.concatenate([x, jnp.zeros((STRIP - x.shape[0], x.shape[1]), F32)], axis=0)
    for tile in range(x.shape[1] // LANES):
        t = lane_tile(x, tile)
        send_ref[2 * tile, at : at + STRIP] = t.astype(BF16)
        send_ref[2 * tile + 1, at : at + STRIP] = swap(t).astype(BF16)


def strip_of(ref, at):
    tiles = []
    for tile in range(ref.shape[0] // 2):
        x, y = [ref[2 * tile + i, at : at + STRIP].astype(F32) for i in range(2)]
        tiles.append(jnp.where(low_lanes(x.shape), x, swap(y)))
    return jnp.concatenate(tiles, axis=1)


def exact_rows(x):
    high = x.astype(BF16).astype(F32)
    return jnp.concatenate([high, x - high], axis=0)


def group_rows(x):
    return lax.broadcasted_iota(jnp.int32, x.shape, 0) & 7


def earlier(x, count):
    return pltpu.roll(x, x.shape[0] - count, 0)


def strip_groups(ref, at):
    x = ref[:, at : at + STRIP, :].astype(F32)[:, :8, :]
    return x.reshape(8 * ref.shape[0], LANES)


def exact_groups(x):
    row = group_rows(x)
    x = jnp.where(row < 2, x, 0.0)
    high = x.astype(BF16).astype(F32)
    x = (high + pltpu.roll(x - high, 2, 0)).reshape(x.shape[0] // 8, 8, LANES)
    return jnp.concatenate([x, jnp.zeros_like(x)], axis=1).astype(BF16)


def start_kernel(stage):
    send_ref, qkv_ref = stage.out(0), stage.take(0)
    rows = qkv_ref.shape[1]
    order = row_order(rows)
    query = qkv_ref[0].astype(F32)
    key, value = mm(order, qkv_ref[1]), mm(order, qkv_ref[2])
    for tile in range(key.shape[1] // LANES):
        x, y = pair(lane_tile(key, tile), lane_tile(value, tile))
        send_ref[2 * tile, :rows] = x.astype(BF16)
        send_ref[2 * tile + 1, :rows] = y.astype(BF16)
    none, last = jnp.zeros_like(query[:1]), query[rows - 1 :]
    strip = [query[:2], none, query[:1], last, none, query[rows - 2 :]]
    put_strip(jnp.concatenate(strip, axis=0), send_ref, rows + rows // 2)
    put_rows(mm(order, stage.take(1)[...].astype(BF16)), send_ref, rows)


def partial_product(g, w_ref, mask):
    width = g.shape[1]
    w = w_ref[mask * width : (mask + 1) * width, :]
    return lax.dot_general(g, w, (((1,), (1,)), ((), ())), preferred_element_type=F32)


def first_product_kernel(stage):
    g, out_ref = stage.take(0)[...], stage.out(0)
    for i, mask in enumerate((1, 3)):
        out_ref[i] = partial_product(g, stage.take(1, i), mask).astype(BF16)


def second_product_kernel(stage):
    w_ref, g, near_ref = stage.take(1), stage.take(0)[...], stage.take(2)
    across_ref, own_ref = stage.out(0), stage.out(1)
    across = partial_product(g, w_ref, 2) + near_ref[1].astype(F32)
    across_ref[...] = across.astype(BF16)
    stage.give(0)
    own_ref[...] = partial_product(g, w_ref, 0) + near_ref[0].astype(F32)


def query_kernel(stage):
    weight_ref, q = stage.take(1), stage.take(0)[0].astype(F32)
    one, two = shifted(q, jnp.zeros((2, q.shape[1]), F32))
    query = weight_ref[0, 0:1, :] * q + weight_ref[0, 1:2, :] * one + weight_ref[0, 2:3, :] * two
    stage.out(4)[...] = query
    stage.give(4)
    stage.out(3)[...] = query


def sum_kernel(stage):
    send_ref, kept_ref = stage.out(0), stage.out(1)
    grad_gated = stage.take(0)[...] + stage.take(1)[...].astype(F32)
    kept_ref[...] = grad_gated
    stage.give(1)
    rows = grad_gated.shape[0]
    first = exact_rows(grad_gated[:2])
    put_strip(jnp.concatenate([jnp.zeros_like(first), first], axis=0), send_ref, rows // 2)
    put_rows(mm(row_order(rows), (grad_gated * stage.take(2)[...]).astype(BF16)), send_ref, 0)


def spread_phases(parts):
    (a_re, a_im), (b_re, b_im), (c_re, c_im), (d_re, d_im) = parts
    s_re, s_im, t_re, t_im = a_re + c_re, a_im + c_im, a_re - c_re, a_im - c_im
    u_re, u_im, v_re, v_im = b_re + d_re, b_im + d_im, b_re - d_re, b_im - d_im
    return [
        (s_re + u_re, s_im + u_im),
        (t_re + v_im, t_im - v_re),
        (s_re - u_re, s_im - u_im),
        (t_re - v_im, t_im + v_re),
    ]


def gather_phases(parts):
    (a_re, a_im), (b_re, b_im), (c_re, c_im), (d_re, d_im) = parts
    s_re, s_im, t_re, t_im = a_re + c_re, a_im + c_im, a_re - c_re, a_im - c_im
    u_re, u_im, v_re, v_im = b_re + d_re, b_im + d_im, b_re - d_re, b_im - d_im
    return [
        (s_re + u_re, s_im + u_im),
        (t_re - v_im, t_im + v_re),
        (s_re - u_re, s_im - u_im),
        (t_re + v_im, t_im - v_re),
    ]


def rows_of(ref, start, count):
    block = ref[:, start : start + count, :]
    return block.reshape(ref.shape[0] * count, ref.shape[2])


def turned_back(re, im, twist, phase):
    if phase == 0:
        return re, im
    c, s = twist[:, phase : phase + 1], twist[:, PHASES + phase : PHASES + phase + 1]
    return re * c + im * s, im * c - re * s


def turned_on(re, im, twist, phase):
    if phase == 0:
        return re, im
    c, s = twist[:, phase : phase + 1], twist[:, PHASES + phase : PHASES + phase + 1]
    return re * c - im * s, re * s + im * c


def lane_tile(x, index):
    return x[:, index * LANES : (index + 1) * LANES]


def causal(parts, weight):
    rows = lax.broadcasted_iota(jnp.int32, parts[0].shape, 0)
    two, three = [jnp.where(rows == 0, 0.0, pltpu.roll(parts[p], 1, 0)) for p in (2, 3)]
    once, twice = [three, *parts[:3]], [two, three, *parts[:2]]
    return [
        weight[0:1] * x + weight[1:2] * y + weight[2:3] * z for x, y, z in zip(parts, once, twice)
    ]


def anticausal(parts, weight):
    count = parts[0].shape[0]
    rows = lax.broadcasted_iota(jnp.int32, parts[0].shape, 0)
    zero, one = [
        jnp.where(rows == count - 1, 0.0, pltpu.roll(parts[p], count - 1, 0)) for p in (0, 1)
    ]
    once, twice = [*parts[1:], zero], [*parts[2:], zero, one]
    return [
        weight[0:1] * x + weight[1:2] * y + weight[2:3] * z for x, y, z in zip(parts, once, twice)
    ]


def halves(x):
    high = x.astype(BF16)
    return high, (x - high.astype(F32)).astype(BF16)


def twiddles(table_ref):
    terms = [table_ref[2, :, i * LANES : (i + 1) * LANES].astype(F32) for i in range(3)]
    return terms[0] + (terms[1] + terms[2])


def columns(parts):
    return jnp.concatenate(parts, axis=1)


def two_sides(table, x):
    quarter = table.shape[0]
    return [mm(table[:, :quarter], x), mm(table[:, quarter:], x)]


def spectrum_of(sides, twist):
    turned = []
    for phase, (re, im) in enumerate(sides):
        turned.append(turned_back(re, im, twist, phase))
    return spread_phases(turned)


def back_values(spectrum, twist):
    return [
        jnp.concatenate(turned_on(re, im, twist, phase), axis=0)
        for phase, (re, im) in enumerate(gather_phases(spectrum))
    ]


def own_weights(weight_ref, gain_ref):
    place = lax.axis_index("seq")
    lanes = pl.ds(pl.multiple_of(place // 2 * LANES, LANES), LANES)
    odd = place % 2 == 1

    def mine(x):
        return jnp.where(odd, swap(x), x)

    query, key, value = [mine(weight_ref[i, :, lanes]) for i in range(3)]
    gain = both(mine(gain_ref[:, lanes]))[0]
    return jnp.where(low_lanes(key.shape), key, swap(value)), query, gain


def forward_kernel(stage):
    recv_ref, weight_ref, gain_ref = [stage.take(i) for i in range(3)]
    send_ref, saved_ref = stage.out(0), stage.out(1)
    blocks = recv_ref.shape[0]
    rows = (recv_ref.shape[1] - STRIP) * 2 // 3
    share = rows // PHASES
    quarter = blocks * share
    low = low_lanes((quarter, LANES))
    pair_weight, query_weight, gain = own_weights(weight_ref, gain_ref)
    saved_ref[14, 0:3, :] = pair_weight
    saved_ref[14, 8:9, :] = gain
    own = strip_groups(recv_ref, rows + rows // 2)
    last = jnp.concatenate([jnp.zeros((8, LANES), F32), own[: own.shape[0] - 8]], axis=0)
    query = (
        query_weight[0:1] * own
        + query_weight[1:2] * (earlier(own, 2) + earlier(last, 4))
        + query_weight[2:3] * earlier(last, 6)
    )
    saved_ref[14, 64 : 64 + 8 * blocks, :] = query
    send_ref[:, rows:, :] = exact_groups(query)

    starts = [phase * share for phase in range(PHASES)]
    pairs = causal([rows_of(recv_ref, at, share).astype(F32) for at in starts], pair_weight)
    taps = [rows_of(recv_ref, rows + at, share).astype(F32) for at in starts[:2]]
    taps = [swap(x) for x in taps] + taps
    for phase in range(PHASES):
        saved_ref[8 + phase] = pairs[phase]
    mixed = [x * swap(x) for x in pairs]

    fh, fl = stage.take(3)[0], stage.take(3)[1]
    twist = twiddles(stage.take(3))
    high = [jnp.where(low, x, y).astype(BF16) for x, y in zip(mixed, taps)]
    rest = [x - y.astype(F32) for x, y in zip(mixed, high)]
    rest = [jnp.where(low, rest[i], swap(rest[i + 2])).astype(BF16) for i in range(2)]
    high, rest = columns(high), columns(rest)
    main = [x + y for x, y in zip(two_sides(fh, high), two_sides(fl, high))]
    more = two_sides(fh, rest)
    sides = []
    for phase in range(PHASES):
        extra = [lane_tile(x, phase % 2) for x in more]
        if phase >= 2:
            extra = [swap(x) for x in extra]
        sides.append([lane_tile(x, phase) + jnp.where(low, y, 0.0) for x, y in zip(main, extra)])
    grad_ref = stage.take(5)
    send_ref[:, rows // 2 : rows, :] = grad_ref[:, : rows // 2, :]
    send_ref[:, rows:, :] = send_ref[:, rows:, :] + grad_ref[:, rows // 2 :, :]
    stage.give(0, 1)
    product = []
    for r, (re, im) in enumerate(spectrum_of(sides, twist)):
        saved_ref[2 * r] = re
        saved_ref[2 * r + 1] = im
        other_re, other_im = swap(re), swap(im)
        product.append((re * other_re - im * other_im, re * other_im + im * other_re))

    values = back_values(product, twist)
    bh, bl = stage.take(4)[0], stage.take(4)[1]
    wide = low_lanes((2 * quarter, LANES))
    high = [x.astype(BF16) for x in values]
    wider = [x.astype(F32) for x in high]
    both_parts = [jnp.where(wide, y, x - y).astype(BF16) for x, y in zip(values, wider)]
    high = [jnp.where(wide, wider[i], wider[i + 2]).astype(BF16) for i in range(2)]
    main, more = mm(bh, columns(both_parts)), mm(bl, columns(high))
    summed = [x + swap(x) for x in (lane_tile(main, phase) for phase in range(PHASES))]
    for i in range(2):
        conv = jnp.where(low, summed[i], summed[i + 2]) + lane_tile(more, i)
        long_out = conv + gain * jnp.where(low, mixed[i], mixed[i + 2])
        saved_ref[12 + i] = long_out
        packed = long_out.astype(BF16).reshape(blocks, share, LANES)
        send_ref[:, starts[i] : starts[i] + share, :] = packed


def backward_kernel(stage):
    grad_ref, saved_ref = stage.take(0), stage.take(1)
    send_ref = stage.out(0)
    blocks = grad_ref.shape[0]
    rows = grad_ref.shape[1] - STRIP
    share = rows // PHASES
    quarter = blocks * share
    low = low_lanes((quarter, LANES))
    pair_weight, gain = saved_ref[14, 0:3, :], saved_ref[14, 8:9, :]

    starts = [phase * share for phase in range(PHASES)]
    strip = strip_groups(grad_ref, rows)
    first = earlier(strip, 4) + earlier(strip, 6)
    fixed = (first * saved_ref[14, 64 : 64 + 8 * blocks, :]).reshape(blocks, 8, LANES)
    fixed = [jnp.broadcast_to(fixed[:, i : i + 1, :], (blocks, share, LANES)) for i in range(2)]
    long_out = []
    for i in range(2):
        tops = [saved_ref[12 + i, at : at + 8, :] for at in range(0, quarter, share)]
        long_out.append(jnp.concatenate(tops, axis=0))
    row = group_rows(first)
    head = first * jnp.where(row == 0, long_out[0], pltpu.roll(long_out[1], 1, 0))
    head = jnp.concatenate([head[8:], jnp.zeros((8, LANES), F32)], axis=0)
    send_ref[:, rows + rows // 2 :, :] = exact_groups(head)
    stage.give(0, 2)
    starting = lax.broadcasted_iota(jnp.int32, (quarter, LANES), 0) & (share - 1)
    starting = (starting == 0) & low
    grad_long = []
    for at, x in zip(starts[2:], fixed):
        packed = rows_of(grad_ref, at, share).astype(F32)
        grad_long.append(jnp.where(starting, x.reshape(quarter, LANES), packed))

    fh, fl = stage.take(2)[0], stage.take(2)[1]
    twist = twiddles(stage.take(2))
    high, rest = halves(columns(grad_long))
    three = zip(two_sides(fh, high), two_sides(fl, high), two_sides(fh, rest))
    main = [x + y + z for x, y, z in three]
    sides = []
    for phase in range(PHASES):
        sides.append([both(lane_tile(x, phase % 2))[phase // 2] for x in main])
    product = []
    for r, (re, im) in enumerate(spectrum_of(sides, twist)):
        k_re, k_im = saved_ref[2 * r], saved_ref[2 * r + 1]
        product.append((k_re * re + k_im * im, k_re * im - k_im * re))
    high, rest = halves(columns(back_values(product, twist)))
    bh, bl = stage.take(3)[0], stage.take(3)[1]
    times = mm(bh, high) + mm(bl, high) + mm(bh, rest)
    times = [lane_tile(times, phase) for phase in range(PHASES)]

    scale = 1.0 / math.sqrt(PHASES * quarter)
    for i, at in enumerate(starts[:2]):
        y = (jnp.where(low, times[i], swap(times[i + 2])) * scale).astype(BF16)
        send_ref[:, rows + at : rows + at + share, :] = y.reshape(blocks, share, LANES)
    stage.give(0, 1)
    grad_long = [both(x)[i] for i in range(2) for x in grad_long]
    grad_mixed = [both(x + gain * y)[1] for x, y in zip(times, grad_long)]
    grad_pairs = anticausal(
        [x * swap(saved_ref[8 + phase]) for phase, x in enumerate(grad_mixed)], pair_weight
    )
    for phase, at in enumerate(starts):
        x = grad_pairs[phase].astype(BF16)
        send_ref[:, at : at + share, :] = x.reshape(blocks, share, LANES)


def unpacked(ref, at, half, order):
    tiles = []
    for tile in range(ref.shape[0] // 2):
        x, y = [ref[2 * tile + i, at : at + half].astype(F32) for i in range(2)]
        top, bottom = pair(x, y)
        tiles.append(jnp.concatenate([top, bottom], axis=0))
    return mm(order, jnp.concatenate(tiles, axis=1).astype(BF16))


def gate_kernel(stage):
    recv_ref, query_ref = stage.take(0), stage.take(1)
    gated_ref, grad_ref = stage.out(0), stage.out(1)
    rows = recv_ref.shape[1] - STRIP
    long_out = unpacked(recv_ref, 0, rows // 2, row_order(rows, back=True))
    grad_ref[...] = stage.take(2)[...] * long_out
    gated_ref[...] = (query_ref[...] * long_out).astype(BF16)
    strip = strip_of(recv_ref, rows)
    first = strip + earlier(strip, 2)
    row = lax.broadcasted_iota(jnp.int32, first.shape, 0)
    first = jnp.where(row < 2, first, query_ref[:STRIP, :])
    gated_ref[:STRIP, :] = (first * long_out[:STRIP]).astype(BF16)


def output_kernel(parts, stage):
    w_ref, total = stage.take(0), None
    for part in range(parts):
        gated = stage.take(1 + part)[...]
        width = gated.shape[1]
        term = mm(gated, w_ref[part * width : (part + 1) * width, :])
        total = term if total is None else total + term
    stage.out(0)[...] = total.astype(BF16)


def end_kernel(stage):
    recv_ref, grad_ref, filter_ref = stage.take(0), stage.out(0), stage.out(1)
    rows = grad_ref.shape[1]
    order = row_order(rows, back=True)
    filter_ref[...] = unpacked(recv_ref, rows, rows // 2, order)
    stage.give(1)
    firsts, seconds = [], []
    for tile in range(recv_ref.shape[0] // 2):
        first, second = pair(*[recv_ref[2 * tile + i, :rows].astype(F32) for i in range(2)])
        firsts.append(first)
        seconds.append(second)
    for i, side in enumerate((firsts, seconds)):
        x = mm(order, jnp.concatenate(side, axis=1).astype(BF16))
        grad_ref[1 + i] = x.astype(BF16)
    query, weight_ref = stage.take(1)[...], stage.take(2)
    strip = strip_of(recv_ref, rows + rows // 2)
    one, two = advanced(query, strip[0:2] + strip[2:4])
    grad_ref[0] = (
        weight_ref[0, 0:1, :] * query + weight_ref[0, 1:2, :] * one + weight_ref[0, 2:3, :] * two
    ).astype(BF16)


def partner(x, axis, mask):
    return lax.ppermute(x, axis, [(i, i ^ mask) for i in range(lax.axis_size(axis))])


def exchanged(x, axis):
    return lax.all_to_all(x, axis, split_axis=0, concat_axis=0, tiled=True)


def owner_layer(qkv, filt, skip_gain, short_weight, w_out, g_out):
    shape = jax.ShapeDtypeStruct
    seq_parts, ch_parts = lax.axis_size("seq"), lax.axis_size("ch")
    rows, width = qkv.shape[1], qkv.shape[2]
    tokens = seq_parts * rows
    quarter = tokens // PHASES
    tables = jnp.asarray(phase_tables(tokens))
    table_flops = 2 * 2 * 2 * 3 * tokens * tokens // PHASES * LANES
    product_flops = 2 * rows * width * width * ch_parts
    half = rows // 2
    wide = shape((seq_parts, rows + half + STRIP, LANES), BF16)
    column = shape((rows, width), BF16)
    saved = shape((15, quarter, LANES), F32)
    gain = skip_gain[None, :]

    (send,) = call(start_kernel, [Far(wide)], Far(qkv), Far(filt))
    recv = exchanged(send, "seq")
    half_sums, w_kept, g_kept = call(
        first_product_kernel,
        [
            Near(shape((2, rows, width), BF16), kept=True),
            Near(w_out, kept=True),
            Near(g_out, kept=True),
        ],
        Far(g_out, into=2),
        Far(w_out, turned=(1, 3, 2, 0), into=1),
        flops=product_flops // 2,
    )
    half_sums = partner(half_sums, "ch", 1)
    across, own = call(
        second_product_kernel,
        [Near(column, kept=True), Near(shape((rows, width), F32), kept=True)],
        Near(g_kept),
        Near(w_kept),
        Near(half_sums),
        flops=product_flops // 2,
    )
    across = partner(across, "ch", 2)
    def pinned(x):
        return Near(x, kept=True)

    tables_back = Far(tables, [(2, 2)])
    exact = shape((rows, width), F32)
    tables_on, weight, gain, query, query_far = call(
        query_kernel,
        [
            pinned(shape((3, *tables.shape[1:]), BF16)),
            pinned(short_weight),
            pinned(gain),
            pinned(exact),
            Far(exact),
        ],
        Far(qkv, [(0, 1)]),
        Far(short_weight, into=1),
        Far(tables, [(0, 2), (4, 1)], into=0),
        Far(gain, into=2),
    )
    grad_long, grad_far = call(
        sum_kernel,
        [Far(shape((seq_parts, half + STRIP, LANES), BF16)), Far(exact)],
        Near(own),
        Near(across),
        Near(query),
    )
    send, saved = call(
        forward_kernel,
        [
            Far(
                shape((seq_parts, rows + STRIP, LANES), BF16),
                [(0, half), (half, half + STRIP)],
                axis=1,
            ),
            pinned(saved),
        ],
        pinned(recv),
        Near(weight),
        Near(gain),
        Near(tables_on),
        tables_back,
        Far(grad_long),
        flops=table_flops,
    )
    swapped = exchanged(send, "seq")
    send, query, grad_gated = call(
        backward_kernel,
        [
            Far(wide, [(0, rows), (rows, half), (rows + half, STRIP)], axis=1),
            pinned(exact),
            pinned(exact),
        ],
        Near(swapped),
        Near(saved),
        Near(tables_on),
        tables_back,
        Far(query_far, into=1),
        Far(grad_far, into=2),
        flops=table_flops,
    )
    grad_recv = exchanged(send, "seq")
    gated, grad_query = call(
        gate_kernel,
        [pinned(column), pinned(exact)],
        Near(swapped),
        Near(query),
        Near(grad_gated),
    )
    across = partner(gated, "ch", 2)
    near, far = partner(gated, "ch", 1), partner(across, "ch", 1)
    (output,) = call(
        functools.partial(output_kernel, ch_parts),
        [Far(column)],
        Near(w_kept),
        Near(gated),
        Near(near),
        Near(across),
        Near(far),
        flops=product_flops,
    )
    grad_qkv, grad_filter = call(
        end_kernel,
        [Far(shape((3, rows, width), BF16)), Far(shape((rows, width), F32))],
        Near(grad_recv),
        Near(grad_query),
        Far(short_weight),
    )
    return (output, grad_qkv, grad_filter)


def local(qkv, filt, skip_gain, short_weight, w_out, g_out):
    seq_parts = lax.axis_size("seq")
    rows, width = qkv.shape[1], qkv.shape[2]
    fits = width == HALF * seq_parts and rows % HALF == 0 and rows & (rows - 1) == 0 and rows * seq_parts <= 2048
    if fits and lax.axis_size("ch") == 4:
        return owner_layer(qkv, filt, skip_gain, short_weight, w_out, g_out)
    return spread_layer(qkv, filt, skip_gain, short_weight, w_out, g_out)


def solution(mesh):
    in_specs = (
        P(None, "seq", "ch"),
        P("seq", "ch"),
        P("ch"),
        P(None, None, "ch"),
        P(None, "ch"),
        P("seq", "ch"),
    )
    out_specs = (P("seq", "ch"), P(None, "seq", "ch"), P("seq", "ch"))
    return jax.shard_map(local, mesh=mesh, in_specs=in_specs, out_specs=out_specs, check_vma=False)
```

```python
import functools
import math

import jax
import jax.numpy as jnp
import numpy as np
from jax import lax
from jax.experimental import pallas as pl
from jax.experimental.pallas import tpu as pltpu
from jax.sharding import PartitionSpec as P

HIGHEST = lax.Precision.HIGHEST
TWO_PI = 2.0 * math.pi
LANES = 128
HALF = 64
PHASES = 4
STRIP = 16
BF16 = jnp.bfloat16
F32 = jnp.float32
VMEM_LIMIT = 24 * 1024 * 1024


def passed_along(block, axis, distance):
    devices = range(lax.axis_size(axis))
    route = [(i - distance, i) for i in devices if i - distance in devices]
    return lax.ppermute(block, axis, route)


def phase_pair(left_count, right_count, period, left_start, right_start):
    left_idx = lax.broadcasted_iota(jnp.int32, (left_count, right_count), 0) + left_start
    right_idx = lax.broadcasted_iota(jnp.int32, (left_count, right_count), 1) + right_start
    angle_all = (left_idx * right_idx % period).astype(jnp.float32) * (TWO_PI / period)
    return (jnp.cos(angle_all), jnp.sin(angle_all))


def contract(pattern, matrix, values):
    return jnp.einsum(
        pattern, matrix, values, precision=HIGHEST, preferred_element_type=jnp.float32
    )


def forward_spectrum(signal):
    seq_parts = lax.axis_size("seq")
    row_count = signal.shape[0]
    row_share = row_count // seq_parts
    period = 2 * seq_parts * row_count
    spread_in = lax.all_to_all(signal[None], "seq", split_axis=1, concat_axis=0, tiled=True)
    outer_cos, outer_sin = phase_pair(2 * seq_parts, seq_parts, 2 * seq_parts, 0, 0)
    section_re = contract("cp,prw->crw", outer_cos, spread_in)
    section_im = -contract("cp,prw->crw", outer_sin, spread_in)
    twist_cos, twist_sin = phase_pair(
        2 * seq_parts, row_share, period, 0, lax.axis_index("seq") * row_share
    )
    twist_cos = twist_cos[:, :, None]
    twist_sin = twist_sin[:, :, None]
    turned_re = section_re * twist_cos + section_im * twist_sin
    turned_im = section_im * twist_cos - section_re * twist_sin
    inner_cos, inner_sin = phase_pair(row_count, row_count, row_count, 0, 0)
    piece_re = lax.all_to_all(turned_re, "seq", split_axis=0, concat_axis=1, tiled=True)
    piece_im = lax.all_to_all(turned_im, "seq", split_axis=0, concat_axis=1, tiled=True)
    spec_re = contract("dm,cmk->cdk", inner_cos, piece_re) + contract(
        "dm,cmk->cdk", inner_sin, piece_im
    )
    spec_im = contract("dm,cmk->cdk", inner_cos, piece_im) - contract(
        "dm,cmk->cdk", inner_sin, piece_re
    )
    return (spec_re, spec_im)


def time_signal(spec_re, spec_im):
    seq_parts = lax.axis_size("seq")
    row_count = spec_re.shape[1]
    period = 2 * seq_parts * row_count
    inner_cos, inner_sin = phase_pair(row_count, row_count, row_count, 0, 0)
    back_re = contract("md,cdk->cmk", inner_cos, spec_re) - contract(
        "md,cdk->cmk", inner_sin, spec_im
    )
    back_im = contract("md,cdk->cmk", inner_cos, spec_im) + contract(
        "md,cdk->cmk", inner_sin, spec_re
    )
    twist_cos, twist_sin = phase_pair(2, row_count, period, 2 * lax.axis_index("seq"), 0)
    twist_cos = twist_cos[:, :, None]
    twist_sin = twist_sin[:, :, None]
    turned_re = back_re * twist_cos - back_im * twist_sin
    turned_im = back_im * twist_cos + back_re * twist_sin
    outer_cos, outer_sin = phase_pair(seq_parts, 2 * seq_parts, 2 * seq_parts, 0, 0)
    piece_re = lax.all_to_all(turned_re, "seq", split_axis=1, concat_axis=0, tiled=True)
    piece_im = lax.all_to_all(turned_im, "seq", split_axis=1, concat_axis=0, tiled=True)
    summed = contract("pc,crk->prk", outer_cos, piece_re) - contract(
        "pc,crk->prk", outer_sin, piece_im
    )
    returned = summed * (1.0 / period)
    return lax.all_to_all(returned, "seq", split_axis=0, concat_axis=1, tiled=True)[0]


def spread_layer(qkv, filt, skip_gain, short_weight, w_out, g_out):
    row_count = qkv.shape[1]
    slab_width = qkv.shape[2]
    tail_rows = passed_along(qkv[:, row_count - 2 :, :], "seq", 1)
    extended = jnp.concatenate([tail_rows, qkv], axis=1)
    short = (
        short_weight[:, 0, None, :] * extended[:, 2:, :]
        + short_weight[:, 1, None, :] * extended[:, 1:-1, :]
        + short_weight[:, 2, None, :] * extended[:, :-2, :]
    )
    query_gate = short[0]
    key_short = short[1]
    value_short = short[2]
    mixed = key_short * value_short
    both_re, both_im = forward_spectrum(jnp.concatenate([mixed, filt], axis=1))
    signal_re = both_re[:, :, :slab_width]
    signal_im = both_im[:, :, :slab_width]
    kernel_re = both_re[:, :, slab_width:]
    kernel_im = both_im[:, :, slab_width:]
    conv_out = time_signal(
        signal_re * kernel_re - signal_im * kernel_im, signal_re * kernel_im + signal_im * kernel_re
    )
    long_out = conv_out + skip_gain * mixed
    gated_out = (query_gate * long_out).astype(jnp.bfloat16)
    projected = jnp.dot(
        lax.all_gather(gated_out, "ch", axis=1, tiled=True),
        w_out,
        preferred_element_type=jnp.float32,
    )
    output = projected.astype(jnp.bfloat16)
    grad_all = lax.all_gather(g_out, "ch", axis=1, tiled=True)
    rows_all = lax.all_to_all(w_out, "ch", split_axis=0, concat_axis=1, tiled=True)
    grad_gated = lax.dot_general(
        grad_all, rows_all, (((1,), (1,)), ((), ())), preferred_element_type=jnp.float32
    )
    grad_long = grad_gated * query_gate
    grad_query = grad_gated * long_out
    grad_re, grad_im = forward_spectrum(grad_long)
    pair_re = jnp.concatenate(
        [kernel_re * grad_re + kernel_im * grad_im, signal_re * grad_re + signal_im * grad_im],
        axis=2,
    )
    pair_im = jnp.concatenate(
        [kernel_re * grad_im - kernel_im * grad_re, signal_re * grad_im - signal_im * grad_re],
        axis=2,
    )
    pair_time = time_signal(pair_re, pair_im)
    grad_mixed = pair_time[:, :slab_width] + skip_gain * grad_long
    token_total = lax.axis_size("seq") * row_count
    grad_filter = pair_time[:, slab_width:] * (1.0 / math.sqrt(token_total))
    grad_short = jnp.stack([grad_query, grad_mixed * value_short, grad_mixed * key_short])
    head_rows = passed_along(grad_short[:, :2, :], "seq", -1)
    extended_grad = jnp.concatenate([grad_short, head_rows], axis=1)
    grad_qkv = (
        short_weight[:, 0, None, :] * extended_grad[:, :-2, :]
        + short_weight[:, 1, None, :] * extended_grad[:, 1:-1, :]
        + short_weight[:, 2, None, :] * extended_grad[:, 2:, :]
    ).astype(jnp.bfloat16)
    return (output, grad_qkv, grad_filter)


def split_bf16(values):
    high = values.astype(np.float32).astype(jnp.bfloat16)
    low = (values - high.astype(np.float64)).astype(np.float32).astype(jnp.bfloat16)
    return high, low


def phase_tables(tokens):
    quarter = tokens // PHASES
    freq = 2 * np.arange(quarter)[:, None] + 1
    turn = math.pi / (2 * tokens)
    angle = (freq * PHASES * np.arange(quarter)[None, :] % (4 * tokens)) * turn
    forward = np.concatenate([np.cos(angle), -np.sin(angle)], axis=1)
    backward = np.concatenate([np.cos(angle).T, -np.sin(angle).T], axis=1) / tokens
    angle = freq * np.arange(PHASES)[None, :] * turn
    twist = np.concatenate([np.cos(angle), np.sin(angle)], axis=1)
    twist = np.pad(twist, ((0, 0), (0, LANES - 2 * PHASES)))
    high, rest = split_bf16(twist)
    last = split_bf16(twist - high.astype(np.float64) - rest.astype(np.float64))[0]
    tables = np.zeros((8, quarter, 2 * quarter), jnp.bfloat16)
    tables[0], tables[1] = split_bf16(forward)
    tables[2], tables[3] = split_bf16(backward)
    for i, term in enumerate((high, rest, last)):
        tables[4, :, i * LANES : (i + 1) * LANES] = term
    return tables


def row_order(rows, back=False):
    to, at = [lax.broadcasted_iota(jnp.int32, (rows, rows), int(i != back)) for i in range(2)]
    share = rows // PHASES
    wanted = (to & (share - 1)) * PHASES + lax.shift_right_logical(to, share.bit_length() - 1)
    return jnp.where(wanted == at, 1.0, 0.0).astype(BF16)


def mm(a, b):
    return lax.dot_general(a, b, (((1,), (0,)), ((), ())), preferred_element_type=F32)


def low_lanes(shape):
    return lax.broadcasted_iota(jnp.int32, shape, 1) < HALF


def swap(x):
    return pltpu.roll(x, HALF, 1)


class Near:
    def __init__(self, array, kept=False):
        self.array = array
        self.kept = kept


class Far:
    def __init__(self, array, cuts=None, turned=(), into=None, axis=0):
        self.array = array
        self.turned = turned
        self.into = into
        self.axis = axis
        if turned:
            step = array.shape[0] // len(turned)
            cuts = [(mask * step, step) for mask in turned]
        self.cuts = cuts or [(0, array.shape[axis])]
        self.shape = list(array.shape)
        self.shape[axis] = sum(count for _, count in self.cuts)


class Stage:
    def __init__(self, items, count_in, refs):
        arrays, scratch = list(refs[: len(items)]), list(refs[len(items) :])
        sems = scratch.pop()
        self.count_in = count_in
        self.held, self.copies, self.waiting = [], [], []
        used = 0
        for i, (item, array) in enumerate(zip(items, arrays)):
            group = []
            if isinstance(item, Near):
                self.held.append(array)
            else:
                held = scratch.pop(0) if item.into is None else arrays[count_in + item.into]
                self.held.append(held)
                at = 0
                for cut, (start, count) in enumerate(item.cuts):
                    lead = (slice(None),) * item.axis
                    there = held.at[(*lead, pl.ds(start if item.turned else at, count))]
                    at += count
                    if item.turned:
                        mask = item.turned[cut]
                        start = pl.multiple_of((lax.axis_index("ch") ^ mask) * count, count)
                    here = array.at[(*lead, pl.ds(start, count))]
                    if i >= count_in:
                        here, there = there, here
                    group.append(pltpu.make_async_copy(here, there, sems.at[used]))
                    used += 1
            self.copies.append(group)
            self.waiting.append(set(range(len(group))))
        self.given = set()

    def bring(self, index):
        for copy in self.copies[index]:
            copy.start()

    def take(self, index, cut=None):
        for i in sorted(self.waiting[index]):
            if cut is None or cut == i:
                self.copies[index][i].wait()
                self.waiting[index].discard(i)
        return self.held[index]

    def out(self, index):
        return self.held[self.count_in + index]

    def give(self, index, cut=None):
        for i, copy in enumerate(self.copies[self.count_in + index]):
            if (index, i) not in self.given and cut in (None, i):
                copy.start()
                self.given.add((index, i))


def staged(kernel, items, count_in, *refs):
    stage = Stage(items, count_in, refs)
    for i in range(count_in):
        stage.bring(i)
    kernel(stage)
    for i in range(count_in):
        stage.take(i)
    for i in range(len(items) - count_in):
        stage.give(i)
    for i in range(len(items) - count_in):
        stage.take(count_in + i)


def operand_of(x):
    if isinstance(x, Near) and not x.kept:
        return x.array
    space = pltpu.VMEM if isinstance(x, Near) else pltpu.HBM
    return pltpu.with_memory_space_constraint(x.array, space)


def result_of(x):
    make = pltpu.HBM if isinstance(x, Far) else pltpu.VMEM if x.kept else jax.ShapeDtypeStruct
    return make(x.array.shape, x.array.dtype)


def call(kernel, results, *args, flops=0):
    items = list(args) + list(results)
    specs, scratch, used = [], [], 0
    for item in items:
        near = isinstance(item, Near)
        specs.append(pl.BlockSpec(memory_space=pltpu.VMEM if near else pltpu.HBM))
        if not near:
            used += len(item.cuts)
            if item.into is None:
                scratch.append(pltpu.VMEM(tuple(item.shape), item.array.dtype))
    moved = sum(math.prod(x.array.shape) * x.array.dtype.itemsize for x in items)
    return pl.pallas_call(
        functools.partial(staged, kernel, items, len(args)),
        out_shape=[result_of(x) for x in results],
        in_specs=specs[: len(args)],
        out_specs=specs[len(args) :],
        scratch_shapes=scratch + [pltpu.SemaphoreType.DMA((max(used, 1),))],
        compiler_params=pltpu.CompilerParams(vmem_limit_bytes=VMEM_LIMIT),
        cost_estimate=pl.CostEstimate(flops=flops, bytes_accessed=moved, transcendentals=0),
    )(*[operand_of(x) for x in args])


def lane_tile(x, index):
    return x[:, index * LANES : (index + 1) * LANES]


def pair(first, second):
    low = low_lanes(first.shape)
    return jnp.where(low, first, swap(second)), jnp.where(low, swap(first), second)


def both(x):
    turned, low = swap(x), low_lanes(x.shape)
    return jnp.where(low, x, turned), jnp.where(low, turned, x)


def shifted(x, before):
    rows = lax.broadcasted_iota(jnp.int32, x.shape, 0)
    last, first = before[1:2, :], before[0:1, :]
    one = jnp.where(rows == 0, last, pltpu.roll(x, 1, 0))
    two = jnp.where(rows == 0, first, jnp.where(rows == 1, last, pltpu.roll(x, 2, 0)))
    return one, two


def advanced(x, after):
    count = x.shape[0]
    rows = lax.broadcasted_iota(jnp.int32, x.shape, 0)
    first, last = after[0:1, :], after[1:2, :]
    one = jnp.where(rows == count - 1, first, pltpu.roll(x, count - 1, 0))
    two = jnp.where(
        rows == count - 1, last, jnp.where(rows == count - 2, first, pltpu.roll(x, count - 2, 0))
    )
    return one, two


def put_rows(x, send_ref, at):
    half = x.shape[0] // 2
    for tile in range(x.shape[1] // LANES):
        t = lane_tile(x, tile)
        first, second = pair(t[:half], t[half:])
        send_ref[2 * tile, at : at + half] = first.astype(BF16)
        send_ref[2 * tile + 1, at : at + half] = second.astype(BF16)


def put_strip(x, send_ref, at):
    x = jnp.concatenate([x, jnp.zeros((STRIP - x.shape[0], x.shape[1]), F32)], axis=0)
    for tile in range(x.shape[1] // LANES):
        t = lane_tile(x, tile)
        send_ref[2 * tile, at : at + STRIP] = t.astype(BF16)
        send_ref[2 * tile + 1, at : at + STRIP] = swap(t).astype(BF16)


def strip_of(ref, at):
    tiles = []
    for tile in range(ref.shape[0] // 2):
        x, y = [ref[2 * tile + i, at : at + STRIP].astype(F32) for i in range(2)]
        tiles.append(jnp.where(low_lanes(x.shape), x, swap(y)))
    return jnp.concatenate(tiles, axis=1)


def exact_rows(x):
    high = x.astype(BF16).astype(F32)
    return jnp.concatenate([high, x - high], axis=0)


def group_rows(x):
    return lax.broadcasted_iota(jnp.int32, x.shape, 0) & 7


def earlier(x, count):
    return pltpu.roll(x, x.shape[0] - count, 0)


def strip_groups(ref, at):
    x = ref[:, at : at + STRIP, :].astype(F32)[:, :8, :]
    return x.reshape(8 * ref.shape[0], LANES)


def exact_groups(x):
    row = group_rows(x)
    x = jnp.where(row < 2, x, 0.0)
    high = x.astype(BF16).astype(F32)
    x = (high + pltpu.roll(x - high, 2, 0)).reshape(x.shape[0] // 8, 8, LANES)
    return jnp.concatenate([x, jnp.zeros_like(x)], axis=1).astype(BF16)


def start_kernel(stage):
    send_ref, qkv_ref = stage.out(0), stage.take(0)
    rows = qkv_ref.shape[1]
    order = row_order(rows)
    query = qkv_ref[0].astype(F32)
    key, value = mm(order, qkv_ref[1]), mm(order, qkv_ref[2])
    for tile in range(key.shape[1] // LANES):
        x, y = pair(lane_tile(key, tile), lane_tile(value, tile))
        send_ref[2 * tile, :rows] = x.astype(BF16)
        send_ref[2 * tile + 1, :rows] = y.astype(BF16)
    none, last = jnp.zeros_like(query[:1]), query[rows - 1 :]
    strip = [query[:2], none, query[:1], last, none, query[rows - 2 :]]
    put_strip(jnp.concatenate(strip, axis=0), send_ref, rows + rows // 2)
    put_rows(mm(order, stage.take(1)[...].astype(BF16)), send_ref, rows)


def partial_product(g, w_ref, mask):
    width = g.shape[1]
    w = w_ref[mask * width : (mask + 1) * width, :]
    return lax.dot_general(g, w, (((1,), (1,)), ((), ())), preferred_element_type=F32)


def first_product_kernel(stage):
    g, out_ref = stage.take(0)[...], stage.out(0)
    for i, mask in enumerate((1, 3)):
        out_ref[i] = partial_product(g, stage.take(1, i), mask).astype(BF16)


def second_product_kernel(stage):
    w_ref, g, near_ref = stage.take(1), stage.take(0)[...], stage.take(2)
    across_ref, own_ref = stage.out(0), stage.out(1)
    across = partial_product(g, w_ref, 2) + near_ref[1].astype(F32)
    across_ref[...] = across.astype(BF16)
    stage.give(0)
    own_ref[...] = partial_product(g, w_ref, 0) + near_ref[0].astype(F32)


def query_kernel(stage):
    weight_ref, q = stage.take(1), stage.take(0)[0].astype(F32)
    one, two = shifted(q, jnp.zeros((2, q.shape[1]), F32))
    query = weight_ref[0, 0:1, :] * q + weight_ref[0, 1:2, :] * one + weight_ref[0, 2:3, :] * two
    stage.out(4)[...] = query
    stage.give(4)
    stage.out(3)[...] = query


def sum_kernel(stage):
    send_ref, kept_ref = stage.out(0), stage.out(1)
    grad_gated = stage.take(0)[...] + stage.take(1)[...].astype(F32)
    kept_ref[...] = grad_gated
    stage.give(1)
    rows = grad_gated.shape[0]
    first = exact_rows(grad_gated[:2])
    put_strip(jnp.concatenate([jnp.zeros_like(first), first], axis=0), send_ref, rows // 2)
    put_rows(mm(row_order(rows), (grad_gated * stage.take(2)[...]).astype(BF16)), send_ref, 0)


def spread_phases(parts):
    (a_re, a_im), (b_re, b_im), (c_re, c_im), (d_re, d_im) = parts
    s_re, s_im, t_re, t_im = a_re + c_re, a_im + c_im, a_re - c_re, a_im - c_im
    u_re, u_im, v_re, v_im = b_re + d_re, b_im + d_im, b_re - d_re, b_im - d_im
    return [
        (s_re + u_re, s_im + u_im),
        (t_re + v_im, t_im - v_re),
        (s_re - u_re, s_im - u_im),
        (t_re - v_im, t_im + v_re),
    ]


def gather_phases(parts):
    (a_re, a_im), (b_re, b_im), (c_re, c_im), (d_re, d_im) = parts
    s_re, s_im, t_re, t_im = a_re + c_re, a_im + c_im, a_re - c_re, a_im - c_im
    u_re, u_im, v_re, v_im = b_re + d_re, b_im + d_im, b_re - d_re, b_im - d_im
    return [
        (s_re + u_re, s_im + u_im),
        (t_re - v_im, t_im + v_re),
        (s_re - u_re, s_im - u_im),
        (t_re + v_im, t_im - v_re),
    ]


def rows_of(ref, start, count):
    block = ref[:, start : start + count, :]
    return block.reshape(ref.shape[0] * count, ref.shape[2])


def turned_back(re, im, twist, phase):
    if phase == 0:
        return re, im
    c, s = twist[:, phase : phase + 1], twist[:, PHASES + phase : PHASES + phase + 1]
    return re * c + im * s, im * c - re * s


def turned_on(re, im, twist, phase):
    if phase == 0:
        return re, im
    c, s = twist[:, phase : phase + 1], twist[:, PHASES + phase : PHASES + phase + 1]
    return re * c - im * s, re * s + im * c


def lane_tile(x, index):
    return x[:, index * LANES : (index + 1) * LANES]


def causal(parts, weight):
    rows = lax.broadcasted_iota(jnp.int32, parts[0].shape, 0)
    two, three = [jnp.where(rows == 0, 0.0, pltpu.roll(parts[p], 1, 0)) for p in (2, 3)]
    once, twice = [three, *parts[:3]], [two, three, *parts[:2]]
    return [
        weight[0:1] * x + weight[1:2] * y + weight[2:3] * z for x, y, z in zip(parts, once, twice)
    ]


def anticausal(parts, weight):
    count = parts[0].shape[0]
    rows = lax.broadcasted_iota(jnp.int32, parts[0].shape, 0)
    zero, one = [
        jnp.where(rows == count - 1, 0.0, pltpu.roll(parts[p], count - 1, 0)) for p in (0, 1)
    ]
    once, twice = [*parts[1:], zero], [*parts[2:], zero, one]
    return [
        weight[0:1] * x + weight[1:2] * y + weight[2:3] * z for x, y, z in zip(parts, once, twice)
    ]


def halves(x):
    high = x.astype(BF16)
    return high, (x - high.astype(F32)).astype(BF16)


def twiddles(table_ref):
    terms = [table_ref[2, :, i * LANES : (i + 1) * LANES].astype(F32) for i in range(3)]
    return terms[0] + (terms[1] + terms[2])


def columns(parts):
    return jnp.concatenate(parts, axis=1)


def two_sides(table, x):
    quarter = table.shape[0]
    return [mm(table[:, :quarter], x), mm(table[:, quarter:], x)]


def spectrum_of(sides, twist):
    turned = []
    for phase, (re, im) in enumerate(sides):
        turned.append(turned_back(re, im, twist, phase))
    return spread_phases(turned)


def back_values(spectrum, twist):
    return [
        jnp.concatenate(turned_on(re, im, twist, phase), axis=0)
        for phase, (re, im) in enumerate(gather_phases(spectrum))
    ]


def own_weights(weight_ref, gain_ref):
    place = lax.axis_index("seq")
    lanes = pl.ds(pl.multiple_of(place // 2 * LANES, LANES), LANES)
    odd = place % 2 == 1

    def mine(x):
        return jnp.where(odd, swap(x), x)

    query, key, value = [mine(weight_ref[i, :, lanes]) for i in range(3)]
    gain = both(mine(gain_ref[:, lanes]))[0]
    return jnp.where(low_lanes(key.shape), key, swap(value)), query, gain


def forward_kernel(stage):
    recv_ref, weight_ref, gain_ref = [stage.take(i) for i in range(3)]
    send_ref, saved_ref = stage.out(0), stage.out(1)
    blocks = recv_ref.shape[0]
    rows = (recv_ref.shape[1] - STRIP) * 2 // 3
    share = rows // PHASES
    quarter = blocks * share
    low = low_lanes((quarter, LANES))
    pair_weight, query_weight, gain = own_weights(weight_ref, gain_ref)
    saved_ref[14, 0:3, :] = pair_weight
    saved_ref[14, 8:9, :] = gain
    own = strip_groups(recv_ref, rows + rows // 2)
    last = jnp.concatenate([jnp.zeros((8, LANES), F32), own[: own.shape[0] - 8]], axis=0)
    query = (
        query_weight[0:1] * own
        + query_weight[1:2] * (earlier(own, 2) + earlier(last, 4))
        + query_weight[2:3] * earlier(last, 6)
    )
    saved_ref[14, 64 : 64 + 8 * blocks, :] = query
    send_ref[:, rows:, :] = exact_groups(query)

    starts = [phase * share for phase in range(PHASES)]
    pairs = causal([rows_of(recv_ref, at, share).astype(F32) for at in starts], pair_weight)
    taps = [rows_of(recv_ref, rows + at, share).astype(F32) for at in starts[:2]]
    taps = [swap(x) for x in taps] + taps
    for phase in range(PHASES):
        saved_ref[8 + phase] = pairs[phase]
    mixed = [x * swap(x) for x in pairs]

    fh, fl = stage.take(3)[0], stage.take(3)[1]
    twist = twiddles(stage.take(3))
    high = [jnp.where(low, x, y).astype(BF16) for x, y in zip(mixed, taps)]
    rest = [x - y.astype(F32) for x, y in zip(mixed, high)]
    rest = [jnp.where(low, rest[i], swap(rest[i + 2])).astype(BF16) for i in range(2)]
    high, rest = columns(high), columns(rest)
    main = [x + y for x, y in zip(two_sides(fh, high), two_sides(fl, high))]
    more = two_sides(fh, rest)
    sides = []
    for phase in range(PHASES):
        extra = [lane_tile(x, phase % 2) for x in more]
        if phase >= 2:
            extra = [swap(x) for x in extra]
        sides.append([lane_tile(x, phase) + jnp.where(low, y, 0.0) for x, y in zip(main, extra)])
    product = []
    for r, (re, im) in enumerate(spectrum_of(sides, twist)):
        saved_ref[2 * r] = re
        saved_ref[2 * r + 1] = im
        other_re, other_im = swap(re), swap(im)
        product.append((re * other_re - im * other_im, re * other_im + im * other_re))

    values = back_values(product, twist)
    bh, bl = stage.take(4)[0], stage.take(4)[1]
    wide = low_lanes((2 * quarter, LANES))
    high = [x.astype(BF16) for x in values]
    wider = [x.astype(F32) for x in high]
    both_parts = [jnp.where(wide, y, x - y).astype(BF16) for x, y in zip(values, wider)]
    high = [jnp.where(wide, wider[i], wider[i + 2]).astype(BF16) for i in range(2)]
    main, more = mm(bh, columns(both_parts)), mm(bl, columns(high))
    grad_ref = stage.take(5)
    send_ref[:, rows // 2 : rows, :] = grad_ref[:, : rows // 2, :]
    send_ref[:, rows:, :] = send_ref[:, rows:, :] + grad_ref[:, rows // 2 :, :]
    stage.give(0, 1)
    summed = [x + swap(x) for x in (lane_tile(main, phase) for phase in range(PHASES))]
    for i in range(2):
        conv = jnp.where(low, summed[i], summed[i + 2]) + lane_tile(more, i)
        long_out = conv + gain * jnp.where(low, mixed[i], mixed[i + 2])
        saved_ref[12 + i] = long_out
        packed = long_out.astype(BF16).reshape(blocks, share, LANES)
        send_ref[:, starts[i] : starts[i] + share, :] = packed


def backward_kernel(stage):
    grad_ref, saved_ref = stage.take(0), stage.take(1)
    send_ref = stage.out(0)
    blocks = grad_ref.shape[0]
    rows = grad_ref.shape[1] - STRIP
    share = rows // PHASES
    quarter = blocks * share
    low = low_lanes((quarter, LANES))
    pair_weight, gain = saved_ref[14, 0:3, :], saved_ref[14, 8:9, :]

    starts = [phase * share for phase in range(PHASES)]
    strip = strip_groups(grad_ref, rows)
    first = earlier(strip, 4) + earlier(strip, 6)
    fixed = (first * saved_ref[14, 64 : 64 + 8 * blocks, :]).reshape(blocks, 8, LANES)
    fixed = [jnp.broadcast_to(fixed[:, i : i + 1, :], (blocks, share, LANES)) for i in range(2)]
    long_out = []
    for i in range(2):
        tops = [saved_ref[12 + i, at : at + 8, :] for at in range(0, quarter, share)]
        long_out.append(jnp.concatenate(tops, axis=0))
    row = group_rows(first)
    head = first * jnp.where(row == 0, long_out[0], pltpu.roll(long_out[1], 1, 0))
    head = jnp.concatenate([head[8:], jnp.zeros((8, LANES), F32)], axis=0)
    send_ref[:, rows + rows // 2 :, :] = exact_groups(head)
    stage.give(0, 2)
    starting = lax.broadcasted_iota(jnp.int32, (quarter, LANES), 0) & (share - 1)
    starting = (starting == 0) & low
    grad_long = []
    for at, x in zip(starts[2:], fixed):
        packed = rows_of(grad_ref, at, share).astype(F32)
        grad_long.append(jnp.where(starting, x.reshape(quarter, LANES), packed))

    fh, fl = stage.take(2)[0], stage.take(2)[1]
    twist = twiddles(stage.take(2))
    high, rest = halves(columns(grad_long))
    three = zip(two_sides(fh, high), two_sides(fl, high), two_sides(fh, rest))
    main = [x + y + z for x, y, z in three]
    sides = []
    for phase in range(PHASES):
        sides.append([both(lane_tile(x, phase % 2))[phase // 2] for x in main])
    product = []
    for r, (re, im) in enumerate(spectrum_of(sides, twist)):
        k_re, k_im = saved_ref[2 * r], saved_ref[2 * r + 1]
        product.append((k_re * re + k_im * im, k_re * im - k_im * re))
    high, rest = halves(columns(back_values(product, twist)))
    bh, bl = stage.take(3)[0], stage.take(3)[1]
    times = mm(bh, high) + mm(bl, high) + mm(bh, rest)
    times = [lane_tile(times, phase) for phase in range(PHASES)]

    scale = 1.0 / math.sqrt(PHASES * quarter)
    for i, at in enumerate(starts[:2]):
        y = (jnp.where(low, times[i], swap(times[i + 2])) * scale).astype(BF16)
        send_ref[:, rows + at : rows + at + share, :] = y.reshape(blocks, share, LANES)
    stage.give(0, 1)
    grad_long = [both(x)[i] for i in range(2) for x in grad_long]
    grad_mixed = [both(x + gain * y)[1] for x, y in zip(times, grad_long)]
    grad_pairs = anticausal(
        [x * swap(saved_ref[8 + phase]) for phase, x in enumerate(grad_mixed)], pair_weight
    )
    for phase, at in enumerate(starts):
        x = grad_pairs[phase].astype(BF16)
        send_ref[:, at : at + share, :] = x.reshape(blocks, share, LANES)


def unpacked(ref, at, half, order):
    tiles = []
    for tile in range(ref.shape[0] // 2):
        x, y = [ref[2 * tile + i, at : at + half].astype(F32) for i in range(2)]
        top, bottom = pair(x, y)
        tiles.append(jnp.concatenate([top, bottom], axis=0))
    return mm(order, jnp.concatenate(tiles, axis=1).astype(BF16))


def gate_kernel(stage):
    recv_ref, gated_ref, grad_ref = stage.take(0), stage.out(0), stage.out(1)
    rows = recv_ref.shape[1] - STRIP
    long_out = unpacked(recv_ref, 0, rows // 2, row_order(rows, back=True))
    query_ref = stage.take(1)
    grad_ref[...] = stage.take(2)[...] * long_out
    stage.give(1)
    gated_ref[...] = (query_ref[...] * long_out).astype(BF16)
    strip = strip_of(recv_ref, rows)
    first = strip + earlier(strip, 2)
    row = lax.broadcasted_iota(jnp.int32, first.shape, 0)
    first = jnp.where(row < 2, first, query_ref[:STRIP, :])
    gated_ref[:STRIP, :] = (first * long_out[:STRIP]).astype(BF16)


def output_kernel(parts, stage):
    w_ref, total = stage.take(0), None
    for part in range(parts):
        gated = stage.take(1 + part)[...]
        width = gated.shape[1]
        term = mm(gated, w_ref[part * width : (part + 1) * width, :])
        total = term if total is None else total + term
    stage.out(0)[...] = total.astype(BF16)


def end_kernel(stage):
    recv_ref, grad_ref, filter_ref = stage.take(0), stage.out(0), stage.out(1)
    rows = grad_ref.shape[1]
    order = row_order(rows, back=True)
    filter_ref[...] = unpacked(recv_ref, rows, rows // 2, order)
    stage.give(1)
    firsts, seconds = [], []
    for tile in range(recv_ref.shape[0] // 2):
        first, second = pair(*[recv_ref[2 * tile + i, :rows].astype(F32) for i in range(2)])
        firsts.append(first)
        seconds.append(second)
    for i, side in enumerate((firsts, seconds)):
        x = mm(order, jnp.concatenate(side, axis=1).astype(BF16))
        grad_ref[1 + i] = x.astype(BF16)
    query, weight_ref = stage.take(1)[...], stage.take(2)
    strip = strip_of(recv_ref, rows + rows // 2)
    one, two = advanced(query, strip[0:2] + strip[2:4])
    grad_ref[0] = (
        weight_ref[0, 0:1, :] * query + weight_ref[0, 1:2, :] * one + weight_ref[0, 2:3, :] * two
    ).astype(BF16)


def partner(x, axis, mask):
    return lax.ppermute(x, axis, [(i, i ^ mask) for i in range(lax.axis_size(axis))])


def exchanged(x, axis):
    return lax.all_to_all(x, axis, split_axis=0, concat_axis=0, tiled=True)


def owner_layer(qkv, filt, skip_gain, short_weight, w_out, g_out):
    shape = jax.ShapeDtypeStruct
    seq_parts, ch_parts = lax.axis_size("seq"), lax.axis_size("ch")
    rows, width = qkv.shape[1], qkv.shape[2]
    tokens = seq_parts * rows
    quarter = tokens // PHASES
    tables = jnp.asarray(phase_tables(tokens))
    table_flops = 2 * 2 * 2 * 3 * tokens * tokens // PHASES * LANES
    product_flops = 2 * rows * width * width * ch_parts
    half = rows // 2
    wide = shape((seq_parts, rows + half + STRIP, LANES), BF16)
    column = shape((rows, width), BF16)
    saved = shape((15, quarter, LANES), F32)
    gain = skip_gain[None, :]

    (send,) = call(start_kernel, [Far(wide)], Far(qkv), Far(filt))
    recv = exchanged(send, "seq")
    half_sums, w_kept, g_kept = call(
        first_product_kernel,
        [
            Near(shape((2, rows, width), BF16), kept=True),
            Near(w_out, kept=True),
            Near(g_out, kept=True),
        ],
        Far(g_out, into=2),
        Far(w_out, turned=(1, 3, 2, 0), into=1),
        flops=product_flops // 2,
    )
    half_sums = partner(half_sums, "ch", 1)
    across, own = call(
        second_product_kernel,
        [Near(column, kept=True), Near(shape((rows, width), F32), kept=True)],
        Near(g_kept),
        Near(w_kept),
        Near(half_sums),
        flops=product_flops // 2,
    )
    across = partner(across, "ch", 2)
    def pinned(x):
        return Near(x, kept=True)

    tables_back = Far(tables, [(2, 2)])
    exact = shape((rows, width), F32)
    tables_on, weight, gain, query, query_far = call(
        query_kernel,
        [
            pinned(shape((3, *tables.shape[1:]), BF16)),
            pinned(short_weight),
            pinned(gain),
            pinned(exact),
            Far(exact),
        ],
        Far(qkv, [(0, 1)]),
        Far(short_weight, into=1),
        Far(tables, [(0, 2), (4, 1)], into=0),
        Far(gain, into=2),
    )
    grad_long, grad_far = call(
        sum_kernel,
        [Far(shape((seq_parts, half + STRIP, LANES), BF16)), Far(exact)],
        Near(own),
        Near(across),
        Near(query),
    )
    send, saved = call(
        forward_kernel,
        [
            Far(
                shape((seq_parts, rows + STRIP, LANES), BF16),
                [(0, half), (half, half + STRIP)],
                axis=1,
            ),
            pinned(saved),
        ],
        pinned(recv),
        Near(weight),
        Near(gain),
        Near(tables_on),
        tables_back,
        Far(grad_long),
        flops=table_flops,
    )
    swapped = exchanged(send, "seq")
    (send,) = call(
        backward_kernel,
        [Far(wide, [(0, rows), (rows, half), (rows + half, STRIP)], axis=1)],
        Near(swapped),
        Near(saved),
        Near(tables_on),
        tables_back,
        flops=table_flops,
    )
    grad_recv = exchanged(send, "seq")
    gated, grad_query = call(
        gate_kernel,
        [pinned(column), Far(exact)],
        Near(swapped),
        Far(query_far),
        Far(grad_far),
    )
    across = partner(gated, "ch", 2)
    near, far = partner(gated, "ch", 1), partner(across, "ch", 1)
    (output,) = call(
        functools.partial(output_kernel, ch_parts),
        [Far(column)],
        Near(w_kept),
        Near(gated),
        Near(near),
        Near(across),
        Near(far),
        flops=product_flops,
    )
    grad_qkv, grad_filter = call(
        end_kernel,
        [Far(shape((3, rows, width), BF16)), Far(shape((rows, width), F32))],
        Near(grad_recv),
        Far(grad_query),
        Far(short_weight),
    )
    return (output, grad_qkv, grad_filter)


def local(qkv, filt, skip_gain, short_weight, w_out, g_out):
    seq_parts = lax.axis_size("seq")
    rows, width = qkv.shape[1], qkv.shape[2]
    fits = width == HALF * seq_parts and rows % HALF == 0 and rows & (rows - 1) == 0 and rows * seq_parts <= 2048
    if fits and lax.axis_size("ch") == 4:
        return owner_layer(qkv, filt, skip_gain, short_weight, w_out, g_out)
    return spread_layer(qkv, filt, skip_gain, short_weight, w_out, g_out)


def solution(mesh):
    in_specs = (
        P(None, "seq", "ch"),
        P("seq", "ch"),
        P("ch"),
        P(None, None, "ch"),
        P(None, "ch"),
        P("seq", "ch"),
    )
    out_specs = (P("seq", "ch"), P(None, "seq", "ch"), P("seq", "ch"))
    return jax.shard_map(local, mesh=mesh, in_specs=in_specs, out_specs=out_specs, check_vma=False)
```

```python
import functools
import math

import jax
import jax.numpy as jnp
import numpy as np
from jax import lax
from jax.experimental import pallas as pl
from jax.experimental.pallas import tpu as pltpu
from jax.sharding import PartitionSpec as P

HIGHEST = lax.Precision.HIGHEST
TWO_PI = 2.0 * math.pi
LANES = 128
HALF = 64
PHASES = 4
STRIP = 16
BF16 = jnp.bfloat16
F32 = jnp.float32
VMEM_LIMIT = 24 * 1024 * 1024


def passed_along(block, axis, distance):
    devices = range(lax.axis_size(axis))
    route = [(i - distance, i) for i in devices if i - distance in devices]
    return lax.ppermute(block, axis, route)


def phase_pair(left_count, right_count, period, left_start, right_start):
    left_idx = lax.broadcasted_iota(jnp.int32, (left_count, right_count), 0) + left_start
    right_idx = lax.broadcasted_iota(jnp.int32, (left_count, right_count), 1) + right_start
    angle_all = (left_idx * right_idx % period).astype(jnp.float32) * (TWO_PI / period)
    return (jnp.cos(angle_all), jnp.sin(angle_all))


def contract(pattern, matrix, values):
    return jnp.einsum(
        pattern, matrix, values, precision=HIGHEST, preferred_element_type=jnp.float32
    )


def forward_spectrum(signal):
    seq_parts = lax.axis_size("seq")
    row_count = signal.shape[0]
    row_share = row_count // seq_parts
    period = 2 * seq_parts * row_count
    spread_in = lax.all_to_all(signal[None], "seq", split_axis=1, concat_axis=0, tiled=True)
    outer_cos, outer_sin = phase_pair(2 * seq_parts, seq_parts, 2 * seq_parts, 0, 0)
    section_re = contract("cp,prw->crw", outer_cos, spread_in)
    section_im = -contract("cp,prw->crw", outer_sin, spread_in)
    twist_cos, twist_sin = phase_pair(
        2 * seq_parts, row_share, period, 0, lax.axis_index("seq") * row_share
    )
    twist_cos = twist_cos[:, :, None]
    twist_sin = twist_sin[:, :, None]
    turned_re = section_re * twist_cos + section_im * twist_sin
    turned_im = section_im * twist_cos - section_re * twist_sin
    inner_cos, inner_sin = phase_pair(row_count, row_count, row_count, 0, 0)
    piece_re = lax.all_to_all(turned_re, "seq", split_axis=0, concat_axis=1, tiled=True)
    piece_im = lax.all_to_all(turned_im, "seq", split_axis=0, concat_axis=1, tiled=True)
    spec_re = contract("dm,cmk->cdk", inner_cos, piece_re) + contract(
        "dm,cmk->cdk", inner_sin, piece_im
    )
    spec_im = contract("dm,cmk->cdk", inner_cos, piece_im) - contract(
        "dm,cmk->cdk", inner_sin, piece_re
    )
    return (spec_re, spec_im)


def time_signal(spec_re, spec_im):
    seq_parts = lax.axis_size("seq")
    row_count = spec_re.shape[1]
    period = 2 * seq_parts * row_count
    inner_cos, inner_sin = phase_pair(row_count, row_count, row_count, 0, 0)
    back_re = contract("md,cdk->cmk", inner_cos, spec_re) - contract(
        "md,cdk->cmk", inner_sin, spec_im
    )
    back_im = contract("md,cdk->cmk", inner_cos, spec_im) + contract(
        "md,cdk->cmk", inner_sin, spec_re
    )
    twist_cos, twist_sin = phase_pair(2, row_count, period, 2 * lax.axis_index("seq"), 0)
    twist_cos = twist_cos[:, :, None]
    twist_sin = twist_sin[:, :, None]
    turned_re = back_re * twist_cos - back_im * twist_sin
    turned_im = back_im * twist_cos + back_re * twist_sin
    outer_cos, outer_sin = phase_pair(seq_parts, 2 * seq_parts, 2 * seq_parts, 0, 0)
    piece_re = lax.all_to_all(turned_re, "seq", split_axis=1, concat_axis=0, tiled=True)
    piece_im = lax.all_to_all(turned_im, "seq", split_axis=1, concat_axis=0, tiled=True)
    summed = contract("pc,crk->prk", outer_cos, piece_re) - contract(
        "pc,crk->prk", outer_sin, piece_im
    )
    returned = summed * (1.0 / period)
    return lax.all_to_all(returned, "seq", split_axis=0, concat_axis=1, tiled=True)[0]


def spread_layer(qkv, filt, skip_gain, short_weight, w_out, g_out):
    row_count = qkv.shape[1]
    slab_width = qkv.shape[2]
    tail_rows = passed_along(qkv[:, row_count - 2 :, :], "seq", 1)
    extended = jnp.concatenate([tail_rows, qkv], axis=1)
    short = (
        short_weight[:, 0, None, :] * extended[:, 2:, :]
        + short_weight[:, 1, None, :] * extended[:, 1:-1, :]
        + short_weight[:, 2, None, :] * extended[:, :-2, :]
    )
    query_gate = short[0]
    key_short = short[1]
    value_short = short[2]
    mixed = key_short * value_short
    both_re, both_im = forward_spectrum(jnp.concatenate([mixed, filt], axis=1))
    signal_re = both_re[:, :, :slab_width]
    signal_im = both_im[:, :, :slab_width]
    kernel_re = both_re[:, :, slab_width:]
    kernel_im = both_im[:, :, slab_width:]
    conv_out = time_signal(
        signal_re * kernel_re - signal_im * kernel_im, signal_re * kernel_im + signal_im * kernel_re
    )
    long_out = conv_out + skip_gain * mixed
    gated_out = (query_gate * long_out).astype(jnp.bfloat16)
    projected = jnp.dot(
        lax.all_gather(gated_out, "ch", axis=1, tiled=True),
        w_out,
        preferred_element_type=jnp.float32,
    )
    output = projected.astype(jnp.bfloat16)
    grad_all = lax.all_gather(g_out, "ch", axis=1, tiled=True)
    rows_all = lax.all_to_all(w_out, "ch", split_axis=0, concat_axis=1, tiled=True)
    grad_gated = lax.dot_general(
        grad_all, rows_all, (((1,), (1,)), ((), ())), preferred_element_type=jnp.float32
    )
    grad_long = grad_gated * query_gate
    grad_query = grad_gated * long_out
    grad_re, grad_im = forward_spectrum(grad_long)
    pair_re = jnp.concatenate(
        [kernel_re * grad_re + kernel_im * grad_im, signal_re * grad_re + signal_im * grad_im],
        axis=2,
    )
    pair_im = jnp.concatenate(
        [kernel_re * grad_im - kernel_im * grad_re, signal_re * grad_im - signal_im * grad_re],
        axis=2,
    )
    pair_time = time_signal(pair_re, pair_im)
    grad_mixed = pair_time[:, :slab_width] + skip_gain * grad_long
    token_total = lax.axis_size("seq") * row_count
    grad_filter = pair_time[:, slab_width:] * (1.0 / math.sqrt(token_total))
    grad_short = jnp.stack([grad_query, grad_mixed * value_short, grad_mixed * key_short])
    head_rows = passed_along(grad_short[:, :2, :], "seq", -1)
    extended_grad = jnp.concatenate([grad_short, head_rows], axis=1)
    grad_qkv = (
        short_weight[:, 0, None, :] * extended_grad[:, :-2, :]
        + short_weight[:, 1, None, :] * extended_grad[:, 1:-1, :]
        + short_weight[:, 2, None, :] * extended_grad[:, 2:, :]
    ).astype(jnp.bfloat16)
    return (output, grad_qkv, grad_filter)


def split_bf16(values):
    high = values.astype(np.float32).astype(jnp.bfloat16)
    low = (values - high.astype(np.float64)).astype(np.float32).astype(jnp.bfloat16)
    return high, low


def phase_tables(tokens):
    quarter = tokens // PHASES
    freq = 2 * np.arange(quarter)[:, None] + 1
    turn = math.pi / (2 * tokens)
    angle = (freq * PHASES * np.arange(quarter)[None, :] % (4 * tokens)) * turn
    forward = np.concatenate([np.cos(angle), -np.sin(angle)], axis=1)
    backward = np.concatenate([np.cos(angle).T, -np.sin(angle).T], axis=1) / tokens
    angle = freq * np.arange(PHASES)[None, :] * turn
    twist = np.concatenate([np.cos(angle), np.sin(angle)], axis=1)
    twist = np.pad(twist, ((0, 0), (0, LANES - 2 * PHASES)))
    high, rest = split_bf16(twist)
    last = split_bf16(twist - high.astype(np.float64) - rest.astype(np.float64))[0]
    tables = np.zeros((8, quarter, 2 * quarter), jnp.bfloat16)
    tables[0], tables[1] = split_bf16(forward)
    tables[2], tables[3] = split_bf16(backward)
    for i, term in enumerate((high, rest, last)):
        tables[4, :, i * LANES : (i + 1) * LANES] = term
    return tables


def row_order(rows, back=False):
    to, at = [lax.broadcasted_iota(jnp.int32, (rows, rows), int(i != back)) for i in range(2)]
    share = rows // PHASES
    wanted = (to & (share - 1)) * PHASES + lax.shift_right_logical(to, share.bit_length() - 1)
    return jnp.where(wanted == at, 1.0, 0.0).astype(BF16)


def mm(a, b):
    return lax.dot_general(a, b, (((1,), (0,)), ((), ())), preferred_element_type=F32)


def low_lanes(shape):
    return lax.broadcasted_iota(jnp.int32, shape, 1) < HALF


def swap(x):
    return pltpu.roll(x, HALF, 1)


class Near:
    def __init__(self, array, kept=False):
        self.array = array
        self.kept = kept


class Far:
    def __init__(self, array, cuts=None, turned=(), into=None, axis=0):
        self.array = array
        self.turned = turned
        self.into = into
        self.axis = axis
        if turned:
            step = array.shape[0] // len(turned)
            cuts = [(mask * step, step) for mask in turned]
        self.cuts = cuts or [(0, array.shape[axis])]
        self.shape = list(array.shape)
        self.shape[axis] = sum(count for _, count in self.cuts)


class Stage:
    def __init__(self, items, count_in, refs):
        arrays, scratch = list(refs[: len(items)]), list(refs[len(items) :])
        sems = scratch.pop()
        self.count_in = count_in
        self.held, self.copies, self.waiting = [], [], []
        used = 0
        for i, (item, array) in enumerate(zip(items, arrays)):
            group = []
            if isinstance(item, Near):
                self.held.append(array)
            else:
                held = scratch.pop(0) if item.into is None else arrays[count_in + item.into]
                self.held.append(held)
                at = 0
                for cut, (start, count) in enumerate(item.cuts):
                    lead = (slice(None),) * item.axis
                    there = held.at[(*lead, pl.ds(start if item.turned else at, count))]
                    at += count
                    if item.turned:
                        mask = item.turned[cut]
                        start = pl.multiple_of((lax.axis_index("ch") ^ mask) * count, count)
                    here = array.at[(*lead, pl.ds(start, count))]
                    if i >= count_in:
                        here, there = there, here
                    group.append(pltpu.make_async_copy(here, there, sems.at[used]))
                    used += 1
            self.copies.append(group)
            self.waiting.append(set(range(len(group))))
        self.given = set()

    def bring(self, index):
        for copy in self.copies[index]:
            copy.start()

    def take(self, index, cut=None):
        for i in sorted(self.waiting[index]):
            if cut is None or cut == i:
                self.copies[index][i].wait()
                self.waiting[index].discard(i)
        return self.held[index]

    def out(self, index):
        return self.held[self.count_in + index]

    def give(self, index, cut=None):
        for i, copy in enumerate(self.copies[self.count_in + index]):
            if (index, i) not in self.given and cut in (None, i):
                copy.start()
                self.given.add((index, i))


def staged(kernel, items, count_in, *refs):
    stage = Stage(items, count_in, refs)
    for i in range(count_in):
        stage.bring(i)
    kernel(stage)
    for i in range(count_in):
        stage.take(i)
    for i in range(len(items) - count_in):
        stage.give(i)
    for i in range(len(items) - count_in):
        stage.take(count_in + i)


def operand_of(x):
    if isinstance(x, Near) and not x.kept:
        return x.array
    space = pltpu.VMEM if isinstance(x, Near) else pltpu.HBM
    return pltpu.with_memory_space_constraint(x.array, space)


def result_of(x):
    make = pltpu.HBM if isinstance(x, Far) else pltpu.VMEM if x.kept else jax.ShapeDtypeStruct
    return make(x.array.shape, x.array.dtype)


def call(kernel, results, *args, flops=0):
    items = list(args) + list(results)
    specs, scratch, used = [], [], 0
    for item in items:
        near = isinstance(item, Near)
        specs.append(pl.BlockSpec(memory_space=pltpu.VMEM if near else pltpu.HBM))
        if not near:
            used += len(item.cuts)
            if item.into is None:
                scratch.append(pltpu.VMEM(tuple(item.shape), item.array.dtype))
    moved = sum(math.prod(x.array.shape) * x.array.dtype.itemsize for x in items)
    return pl.pallas_call(
        functools.partial(staged, kernel, items, len(args)),
        out_shape=[result_of(x) for x in results],
        in_specs=specs[: len(args)],
        out_specs=specs[len(args) :],
        scratch_shapes=scratch + [pltpu.SemaphoreType.DMA((max(used, 1),))],
        compiler_params=pltpu.CompilerParams(vmem_limit_bytes=VMEM_LIMIT),
        cost_estimate=pl.CostEstimate(flops=flops, bytes_accessed=moved, transcendentals=0),
    )(*[operand_of(x) for x in args])


def lane_tile(x, index):
    return x[:, index * LANES : (index + 1) * LANES]


def pair(first, second):
    low = low_lanes(first.shape)
    return jnp.where(low, first, swap(second)), jnp.where(low, swap(first), second)


def both(x):
    turned, low = swap(x), low_lanes(x.shape)
    return jnp.where(low, x, turned), jnp.where(low, turned, x)


def shifted(x, before):
    rows = lax.broadcasted_iota(jnp.int32, x.shape, 0)
    last, first = before[1:2, :], before[0:1, :]
    one = jnp.where(rows == 0, last, pltpu.roll(x, 1, 0))
    two = jnp.where(rows == 0, first, jnp.where(rows == 1, last, pltpu.roll(x, 2, 0)))
    return one, two


def advanced(x, after):
    count = x.shape[0]
    rows = lax.broadcasted_iota(jnp.int32, x.shape, 0)
    first, last = after[0:1, :], after[1:2, :]
    one = jnp.where(rows == count - 1, first, pltpu.roll(x, count - 1, 0))
    two = jnp.where(
        rows == count - 1, last, jnp.where(rows == count - 2, first, pltpu.roll(x, count - 2, 0))
    )
    return one, two


def put_rows(x, send_ref, at):
    half = x.shape[0] // 2
    for tile in range(x.shape[1] // LANES):
        t = lane_tile(x, tile)
        first, second = pair(t[:half], t[half:])
        send_ref[2 * tile, at : at + half] = first.astype(BF16)
        send_ref[2 * tile + 1, at : at + half] = second.astype(BF16)


def put_strip(x, send_ref, at):
    x = jnp.concatenate([x, jnp.zeros((STRIP - x.shape[0], x.shape[1]), F32)], axis=0)
    for tile in range(x.shape[1] // LANES):
        t = lane_tile(x, tile)
        send_ref[2 * tile, at : at + STRIP] = t.astype(BF16)
        send_ref[2 * tile + 1, at : at + STRIP] = swap(t).astype(BF16)


def strip_of(ref, at):
    tiles = []
    for tile in range(ref.shape[0] // 2):
        x, y = [ref[2 * tile + i, at : at + STRIP].astype(F32) for i in range(2)]
        tiles.append(jnp.where(low_lanes(x.shape), x, swap(y)))
    return jnp.concatenate(tiles, axis=1)


def exact_rows(x):
    high = x.astype(BF16).astype(F32)
    return jnp.concatenate([high, x - high], axis=0)


def group_rows(x):
    return lax.broadcasted_iota(jnp.int32, x.shape, 0) & 7


def earlier(x, count):
    return pltpu.roll(x, x.shape[0] - count, 0)


def strip_groups(ref, at, half):
    x = ref[:, at : at + STRIP, :].astype(F32)[:, 8 * half : 8 * half + 8, :]
    return x.reshape(8 * ref.shape[0], LANES)


def exact_groups(*halves):
    strips = []
    for x in halves:
        x = jnp.where(group_rows(x) < 2, x, 0.0)
        high = x.astype(BF16).astype(F32)
        strips.append((high + pltpu.roll(x - high, 2, 0)).reshape(x.shape[0] // 8, 8, LANES))
    return jnp.concatenate(strips, axis=1).astype(BF16)


def own_rows(x):
    none, last = jnp.zeros_like(x[:1]), x[x.shape[0] - 1 :]
    return jnp.concatenate([x[:2], none, x[:1], last, none, x[x.shape[0] - 2 :]], axis=0)


def first_rows(groups, weight):
    last = jnp.concatenate([jnp.zeros((8, LANES), F32), groups[: groups.shape[0] - 8]], axis=0)
    return (
        weight[0:1] * groups
        + weight[1:2] * (earlier(groups, 2) + earlier(last, 4))
        + weight[2:3] * earlier(last, 6)
    )


def short_of(x, weight):
    one, two = shifted(x, jnp.zeros((2, x.shape[1]), F32))
    return weight[0:1, :] * x + weight[1:2, :] * one + weight[2:3, :] * two


def adjoint_of(x, after, weight):
    one, two = advanced(x, after)
    return weight[0:1, :] * x + weight[1:2, :] * one + weight[2:3, :] * two


def start_kernel(stage):
    send_ref, weight_ref = stage.out(0), stage.take(0)
    qkv_ref = stage.take(1)
    rows = qkv_ref.shape[1]
    order = row_order(rows)
    query, key, value = [qkv_ref[i].astype(F32) for i in range(3)]
    put_strip(own_rows(query), send_ref, rows)
    key_rows, value_rows = own_rows(key), own_rows(value)
    mixed = short_of(key, weight_ref[1]) * short_of(value, weight_ref[2])
    mixed, taps = mm(order, mixed.astype(BF16)), mm(order, stage.take(2)[...].astype(BF16))
    for tile in range(mixed.shape[1] // LANES):
        strips = pair(lane_tile(key_rows, tile), lane_tile(value_rows, tile))
        parts = pair(lane_tile(mixed, tile), lane_tile(taps, tile))
        for i in range(2):
            send_ref[2 * tile + i, :rows] = parts[i].astype(BF16)
            raw = send_ref[2 * tile + i, rows:].astype(F32)
            raw = jnp.concatenate([raw[:8], strips[i]], axis=0)
            send_ref[2 * tile + i, rows:] = raw.astype(BF16)


def partial_product(g, w_ref, mask):
    width = g.shape[1]
    w = w_ref[mask * width : (mask + 1) * width, :]
    return lax.dot_general(g, w, (((1,), (1,)), ((), ())), preferred_element_type=F32)


def first_product_kernel(stage):
    g, out_ref = stage.take(0)[...], stage.out(0)
    for i, mask in enumerate((1, 3)):
        out_ref[i] = partial_product(g, stage.take(1, i), mask).astype(BF16)


def second_product_kernel(stage):
    w_ref, g, near_ref = stage.take(1), stage.take(0)[...], stage.take(2)
    across_ref, own_ref = stage.out(0), stage.out(1)
    across = partial_product(g, w_ref, 2) + near_ref[1].astype(F32)
    across_ref[...] = across.astype(BF16)
    stage.give(0)
    own_ref[...] = partial_product(g, w_ref, 0) + near_ref[0].astype(F32)


def query_kernel(stage):
    weight_ref, qkv_ref, short_ref = stage.take(1), stage.take(0), stage.out(4)
    for i in range(3):
        short_ref[i] = short_of(qkv_ref[i].astype(F32), weight_ref[i])
    stage.give(4)
    stage.out(3)[...] = short_ref[0]


def sum_kernel(stage):
    send_ref, kept_ref = stage.out(0), stage.out(1)
    grad_gated = stage.take(0)[...] + stage.take(1)[...].astype(F32)
    kept_ref[...] = grad_gated
    stage.give(1)
    rows = grad_gated.shape[0]
    first = exact_rows(grad_gated[:2])
    put_strip(jnp.concatenate([jnp.zeros_like(first), first], axis=0), send_ref, rows // 2)
    put_rows(mm(row_order(rows), (grad_gated * stage.take(2)[...]).astype(BF16)), send_ref, 0)


def spread_phases(parts):
    (a_re, a_im), (b_re, b_im), (c_re, c_im), (d_re, d_im) = parts
    s_re, s_im, t_re, t_im = a_re + c_re, a_im + c_im, a_re - c_re, a_im - c_im
    u_re, u_im, v_re, v_im = b_re + d_re, b_im + d_im, b_re - d_re, b_im - d_im
    return [
        (s_re + u_re, s_im + u_im),
        (t_re + v_im, t_im - v_re),
        (s_re - u_re, s_im - u_im),
        (t_re - v_im, t_im + v_re),
    ]


def gather_phases(parts):
    (a_re, a_im), (b_re, b_im), (c_re, c_im), (d_re, d_im) = parts
    s_re, s_im, t_re, t_im = a_re + c_re, a_im + c_im, a_re - c_re, a_im - c_im
    u_re, u_im, v_re, v_im = b_re + d_re, b_im + d_im, b_re - d_re, b_im - d_im
    return [
        (s_re + u_re, s_im + u_im),
        (t_re - v_im, t_im + v_re),
        (s_re - u_re, s_im - u_im),
        (t_re + v_im, t_im - v_re),
    ]


def rows_of(ref, start, count):
    block = ref[:, start : start + count, :]
    return block.reshape(ref.shape[0] * count, ref.shape[2])


def turned_back(re, im, twist, phase):
    if phase == 0:
        return re, im
    c, s = twist[:, phase : phase + 1], twist[:, PHASES + phase : PHASES + phase + 1]
    return re * c + im * s, im * c - re * s


def turned_on(re, im, twist, phase):
    if phase == 0:
        return re, im
    c, s = twist[:, phase : phase + 1], twist[:, PHASES + phase : PHASES + phase + 1]
    return re * c - im * s, re * s + im * c


def lane_tile(x, index):
    return x[:, index * LANES : (index + 1) * LANES]


def causal(parts, weight):
    rows = lax.broadcasted_iota(jnp.int32, parts[0].shape, 0)
    two, three = [jnp.where(rows == 0, 0.0, pltpu.roll(parts[p], 1, 0)) for p in (2, 3)]
    once, twice = [three, *parts[:3]], [two, three, *parts[:2]]
    return [
        weight[0:1] * x + weight[1:2] * y + weight[2:3] * z for x, y, z in zip(parts, once, twice)
    ]


def anticausal(parts, weight):
    count = parts[0].shape[0]
    rows = lax.broadcasted_iota(jnp.int32, parts[0].shape, 0)
    zero, one = [
        jnp.where(rows == count - 1, 0.0, pltpu.roll(parts[p], count - 1, 0)) for p in (0, 1)
    ]
    once, twice = [*parts[1:], zero], [*parts[2:], zero, one]
    return [
        weight[0:1] * x + weight[1:2] * y + weight[2:3] * z for x, y, z in zip(parts, once, twice)
    ]


def halves(x):
    high = x.astype(BF16)
    return high, (x - high.astype(F32)).astype(BF16)


def twiddles(table_ref):
    terms = [table_ref[2, :, i * LANES : (i + 1) * LANES].astype(F32) for i in range(3)]
    return terms[0] + (terms[1] + terms[2])


def columns(parts):
    return jnp.concatenate(parts, axis=1)


def two_sides(table, x):
    quarter = table.shape[0]
    return [mm(table[:, :quarter], x), mm(table[:, quarter:], x)]


def spectrum_of(sides, twist):
    turned = []
    for phase, (re, im) in enumerate(sides):
        turned.append(turned_back(re, im, twist, phase))
    return spread_phases(turned)


def back_values(spectrum, twist):
    return [
        jnp.concatenate(turned_on(re, im, twist, phase), axis=0)
        for phase, (re, im) in enumerate(gather_phases(spectrum))
    ]


def own_weights(weight_ref, gain_ref):
    place = lax.axis_index("seq")
    lanes = pl.ds(pl.multiple_of(place // 2 * LANES, LANES), LANES)
    odd = place % 2 == 1

    def mine(x):
        return jnp.where(odd, swap(x), x)

    query, key, value = [mine(weight_ref[i, :, lanes]) for i in range(3)]
    gain = both(mine(gain_ref[:, lanes]))[0]
    return jnp.where(low_lanes(key.shape), key, swap(value)), query, gain


def first_mask(quarter, share):
    rows = lax.broadcasted_iota(jnp.int32, (quarter, LANES), 0) & (share - 1)
    return (rows == 0) & low_lanes((quarter, LANES))


def spread_first(groups, index, share):
    x = groups.reshape(groups.shape[0] // 8, 8, LANES)[:, index : index + 1, :]
    return jnp.broadcast_to(x, (x.shape[0], share, LANES)).reshape(x.shape[0] * share, LANES)


def gather_first(parts, share):
    tops = []
    for x in parts:
        tops.append(
            jnp.concatenate([x[at : at + 8] for at in range(0, x.shape[0], share)], axis=0)
        )
    return jnp.where(group_rows(tops[0]) == 0, tops[0], pltpu.roll(tops[1], 1, 0))


def forward_kernel(stage):
    recv_ref, weight_ref, gain_ref = [stage.take(i) for i in range(3)]
    send_ref, saved_ref = stage.out(0), stage.out(1)
    blocks = recv_ref.shape[0]
    rows = recv_ref.shape[1] - STRIP
    share = rows // PHASES
    quarter = blocks * share
    low, starting = low_lanes((quarter, LANES)), first_mask(quarter, share)
    pair_weight, query_weight, gain = own_weights(weight_ref, gain_ref)
    query = first_rows(strip_groups(recv_ref, rows, 0), query_weight)
    pairs = first_rows(strip_groups(recv_ref, rows, 1), pair_weight)
    saved_ref[10, 8:9, :] = gain
    saved_ref[10, 64 : 64 + 8 * blocks, :] = query
    saved_ref[10, 128 : 128 + 8 * blocks, :] = pairs
    strip = exact_groups(query, pairs)
    fixed = pairs * swap(pairs)

    starts = [phase * share for phase in range(PHASES)]
    x = [rows_of(recv_ref, at, share).astype(F32) for at in starts]
    for i in range(2):
        x[i] = jnp.where(starting, spread_first(fixed, i, share), x[i])
    high = columns([y.astype(BF16) for y in x])
    fh, fl = stage.take(3)[0], stage.take(3)[1]
    twist = twiddles(stage.take(3))
    main = [y + z for y, z in zip(two_sides(fh, high), two_sides(fl, high))]
    sides = [[lane_tile(y, phase) for y in main] for phase in range(PHASES)]
    product = []
    for r, (re, im) in enumerate(spectrum_of(sides, twist)):
        saved_ref[2 * r] = re
        saved_ref[2 * r + 1] = im
        other_re, other_im = swap(re), swap(im)
        product.append((re * other_re - im * other_im, re * other_im + im * other_re))

    values = back_values(product, twist)
    bh, bl = stage.take(4)[0], stage.take(4)[1]
    wide = low_lanes((2 * quarter, LANES))
    high = [y.astype(BF16) for y in values]
    wider = [y.astype(F32) for y in high]
    both_parts = [jnp.where(wide, z, y - z).astype(BF16) for y, z in zip(values, wider)]
    high = [jnp.where(wide, wider[i], wider[i + 2]).astype(BF16) for i in range(2)]
    main, more = mm(bh, columns(both_parts)), mm(bl, columns(high))
    grad_ref = stage.take(5)
    send_ref[:, rows // 2 : rows, :] = grad_ref[:, : rows // 2, :]
    send_ref[:, rows:, :] = strip + grad_ref[:, rows // 2 :, :]
    stage.give(0, 1)
    summed = [y + swap(y) for y in (lane_tile(main, phase) for phase in range(PHASES))]
    for i in range(2):
        conv = jnp.where(low, summed[i], summed[i + 2]) + lane_tile(more, i)
        long_out = conv + gain * jnp.where(low, x[i], swap(x[i + 2]))
        saved_ref[8 + i] = long_out
        long_out = long_out.astype(BF16).reshape(blocks, share, LANES)
        send_ref[:, starts[i] : starts[i] + share, :] = long_out


def backward_kernel(stage):
    grad_ref, saved_ref, send_ref = stage.take(0), stage.take(1), stage.out(0)
    blocks = grad_ref.shape[0]
    rows = grad_ref.shape[1] - STRIP
    share = rows // PHASES
    quarter = blocks * share
    low, starting = low_lanes((quarter, LANES)), first_mask(quarter, share)
    gain, groups = saved_ref[10, 8:9, :], 8 * blocks
    query, pairs = [saved_ref[10, at : at + groups, :] for at in (64, 128)]
    strip = strip_groups(grad_ref, rows, 0)
    first = earlier(strip, 4) + earlier(strip, 6)
    fixed = first * query
    starts = [phase * share for phase in range(PHASES)]
    grad_long = []
    for i, at in enumerate(starts[2:]):
        packed = rows_of(grad_ref, at, share).astype(F32)
        grad_long.append(jnp.where(starting, spread_first(fixed, i, share), packed))

    fh, fl = stage.take(2)[0], stage.take(2)[1]
    twist = twiddles(stage.take(2))
    high, rest = halves(columns(grad_long))
    three = zip(two_sides(fh, high), two_sides(fl, high), two_sides(fh, rest))
    main = [x + y + z for x, y, z in three]
    sides = []
    for phase in range(PHASES):
        sides.append([both(lane_tile(x, phase % 2))[phase // 2] for x in main])
    product = []
    for r, (re, im) in enumerate(spectrum_of(sides, twist)):
        k_re, k_im = saved_ref[2 * r], saved_ref[2 * r + 1]
        product.append((k_re * re + k_im * im, k_re * im - k_im * re))
    high, rest = halves(columns(back_values(product, twist)))
    bh, bl = stage.take(3)[0], stage.take(3)[1]
    times = mm(bh, high) + mm(bl, high) + mm(bh, rest)

    scale = 1.0 / math.sqrt(PHASES * quarter)
    grad_long = [swap(x) for x in grad_long] + grad_long
    grads = []
    for phase, at in enumerate(starts):
        x = lane_tile(times, phase)
        grads.append(jnp.where(low, x * scale, x + gain * grad_long[phase]))
        send_ref[:, at : at + share, :] = grads[-1].astype(BF16).reshape(blocks, share, LANES)
    stage.give(0, 0)
    query_head = first * gather_first([saved_ref[8], saved_ref[9]], share)
    pair_head = both(gather_first(grads[:2], share))[1] * swap(pairs)
    heads = []
    for x in (query_head, pair_head):
        heads.append(jnp.concatenate([x[8:], jnp.zeros((8, LANES), F32)], axis=0))
    send_ref[:, rows:, :] = exact_groups(*heads)


def unpacked(ref, at, half, order):
    tiles = []
    for tile in range(ref.shape[0] // 2):
        x, y = [ref[2 * tile + i, at : at + half].astype(F32) for i in range(2)]
        top, bottom = pair(x, y)
        tiles.append(jnp.concatenate([top, bottom], axis=0))
    return mm(order, jnp.concatenate(tiles, axis=1).astype(BF16))


def pair_strip_of(ref, at):
    sides = [[], []]
    for tile in range(ref.shape[0] // 2):
        x, y = [ref[2 * tile + i, at : at + STRIP].astype(F32)[8:] for i in range(2)]
        for side, z in zip(sides, pair(x, y)):
            side.append(z)
    return [columns(side) for side in sides]


def gate_kernel(stage):
    recv_ref, gated_ref, grad_ref, tops_ref = stage.take(0), *[stage.out(i) for i in range(3)]
    rows = recv_ref.shape[1] - STRIP
    key, value = [x[0:2] + x[2:4] for x in pair_strip_of(recv_ref, rows)]
    tops_ref[...] = jnp.concatenate([key, value, key, value], axis=0)
    long_out = unpacked(recv_ref, 0, rows // 2, row_order(rows, back=True))
    query = stage.take(1)[0]
    grad_ref[...] = stage.take(2)[...] * long_out
    stage.give(1)
    gated_ref[...] = (query * long_out).astype(BF16)
    strip = strip_of(recv_ref, rows)
    first = strip + earlier(strip, 2)
    row = lax.broadcasted_iota(jnp.int32, first.shape, 0)
    first = jnp.where(row < 2, first, query[:STRIP])
    gated_ref[:STRIP, :] = (first * long_out[:STRIP]).astype(BF16)


def output_kernel(parts, stage):
    w_ref, total = stage.take(0), None
    for part in range(parts):
        gated = stage.take(1 + part)[...]
        width = gated.shape[1]
        term = mm(gated, w_ref[part * width : (part + 1) * width, :])
        total = term if total is None else total + term
    stage.out(0)[...] = total.astype(BF16)


def end_kernel(stage):
    recv_ref, grad_ref, filter_ref = stage.take(0), stage.out(0), stage.out(1)
    rows = filter_ref.shape[0]
    order = row_order(rows, back=True)
    sides = [[], []]
    for tile in range(recv_ref.shape[0] // 2):
        x, y = [recv_ref[2 * tile + i, :rows].astype(F32) for i in range(2)]
        for side, z in zip(sides, pair(x, y)):
            side.append(z.astype(BF16))
    taps, mixed = [mm(order, columns(side)) for side in sides]
    filter_ref[...] = taps
    stage.give(1)
    weight_ref, tops, short_ref = stage.take(1), stage.take(2)[...], stage.take(3)
    row = lax.broadcasted_iota(jnp.int32, mixed.shape, 0)
    heads = [x[0:2] + x[2:4] for x in pair_strip_of(recv_ref, rows)]
    for i in range(2):
        top = tops[2 - 2 * i : 4 - 2 * i]
        other = jnp.where(row == 0, top[0:1], jnp.where(row == 1, top[1:2], short_ref[1 - i]))
        grad_ref[i] = adjoint_of(mixed * other, heads[i], weight_ref[1 + i]).astype(BF16)
    stage.give(0, 0)
    strip = strip_of(recv_ref, rows)
    head = strip[0:2] + strip[2:4]
    grad_ref[2] = adjoint_of(stage.take(4)[...], head, weight_ref[0]).astype(BF16)


def partner(x, axis, mask):
    return lax.ppermute(x, axis, [(i, i ^ mask) for i in range(lax.axis_size(axis))])


def exchanged(x, axis):
    return lax.all_to_all(x, axis, split_axis=0, concat_axis=0, tiled=True)


def owner_layer(qkv, filt, skip_gain, short_weight, w_out, g_out):
    shape = jax.ShapeDtypeStruct
    seq_parts, ch_parts = lax.axis_size("seq"), lax.axis_size("ch")
    rows, width = qkv.shape[1], qkv.shape[2]
    tokens = seq_parts * rows
    quarter = tokens // PHASES
    tables = jnp.asarray(phase_tables(tokens))
    table_flops = 2 * 2 * 2 * 3 * tokens * tokens // PHASES * LANES
    product_flops = 2 * rows * width * width * ch_parts
    half = rows // 2
    wide = shape((seq_parts, rows + STRIP, LANES), BF16)
    column = shape((rows, width), BF16)
    saved = shape((11, quarter, LANES), F32)
    gain = skip_gain[None, :]

    (send,) = call(start_kernel, [Far(wide)], Far(short_weight), Far(qkv), Far(filt))
    recv = exchanged(send, "seq")
    half_sums, w_kept, g_kept = call(
        first_product_kernel,
        [
            Near(shape((2, rows, width), BF16), kept=True),
            Near(w_out, kept=True),
            Near(g_out, kept=True),
        ],
        Far(g_out, into=2),
        Far(w_out, turned=(1, 3, 2, 0), into=1),
        flops=product_flops // 2,
    )
    half_sums = partner(half_sums, "ch", 1)
    across, own = call(
        second_product_kernel,
        [Near(column, kept=True), Near(shape((rows, width), F32), kept=True)],
        Near(g_kept),
        Near(w_kept),
        Near(half_sums),
        flops=product_flops // 2,
    )
    across = partner(across, "ch", 2)
    def pinned(x):
        return Near(x, kept=True)

    tables_back = Far(tables, [(2, 2)])
    exact = shape((rows, width), F32)
    tables_on, weight, gain, query, short = call(
        query_kernel,
        [
            pinned(shape((3, *tables.shape[1:]), BF16)),
            pinned(short_weight),
            pinned(gain),
            pinned(exact),
            Far(shape((3, rows, width), F32)),
        ],
        Far(qkv),
        Far(short_weight, into=1),
        Far(tables, [(0, 2), (4, 1)], into=0),
        Far(gain, into=2),
    )
    grad_long, grad_far = call(
        sum_kernel,
        [Far(shape((seq_parts, half + STRIP, LANES), BF16)), Far(exact)],
        Near(own),
        Near(across),
        Near(query),
    )
    send, saved = call(
        forward_kernel,
        [
            Far(wide, [(0, half), (half, half + STRIP)], axis=1),
            pinned(saved),
        ],
        pinned(recv),
        Near(weight),
        Near(gain),
        Near(tables_on),
        tables_back,
        Far(grad_long),
        flops=table_flops,
    )
    swapped = exchanged(send, "seq")
    (send,) = call(
        backward_kernel,
        [Far(wide, [(0, rows), (rows, STRIP)], axis=1)],
        Near(swapped),
        Near(saved),
        Near(tables_on),
        tables_back,
        flops=table_flops,
    )
    grad_recv = exchanged(send, "seq")
    gated, grad_query, tops = call(
        gate_kernel,
        [pinned(column), Far(exact), Far(shape((8, width), F32))],
        Near(swapped),
        Far(short, [(0, 1)]),
        Far(grad_far),
    )
    across = partner(gated, "ch", 2)
    near, far = partner(gated, "ch", 1), partner(across, "ch", 1)
    (output,) = call(
        functools.partial(output_kernel, ch_parts),
        [Far(column)],
        Near(w_kept),
        Near(gated),
        Near(near),
        Near(across),
        Near(far),
        flops=product_flops,
    )
    grad_qkv, grad_filter = call(
        end_kernel,
        [Far(shape((3, rows, width), BF16), [(1, 2), (0, 1)]), Far(exact)],
        Near(grad_recv),
        Far(short_weight),
        Far(tops),
        Far(short, [(1, 2)]),
        Far(grad_query),
    )
    return (output, grad_qkv, grad_filter)


def local(qkv, filt, skip_gain, short_weight, w_out, g_out):
    seq_parts = lax.axis_size("seq")
    rows, width = qkv.shape[1], qkv.shape[2]
    fits = width == HALF * seq_parts and rows % HALF == 0 and rows & (rows - 1) == 0 and rows * seq_parts <= 2048
    if fits and lax.axis_size("ch") == 4:
        return owner_layer(qkv, filt, skip_gain, short_weight, w_out, g_out)
    return spread_layer(qkv, filt, skip_gain, short_weight, w_out, g_out)


def solution(mesh):
    in_specs = (
        P(None, "seq", "ch"),
        P("seq", "ch"),
        P("ch"),
        P(None, None, "ch"),
        P(None, "ch"),
        P("seq", "ch"),
    )
    out_specs = (P("seq", "ch"), P(None, "seq", "ch"), P("seq", "ch"))
    return jax.shard_map(local, mesh=mesh, in_specs=in_specs, out_specs=out_specs, check_vma=False)
```

```python
import functools
import math

import jax
import jax.numpy as jnp
import numpy as np
from jax import lax
from jax.experimental import pallas as pl
from jax.experimental.pallas import tpu as pltpu
from jax.sharding import PartitionSpec as P

HIGHEST = lax.Precision.HIGHEST
TWO_PI = 2.0 * math.pi
LANES = 128
HALF = 64
PHASES = 4
STRIP = 16
BF16 = jnp.bfloat16
F32 = jnp.float32
VMEM_LIMIT = 24 * 1024 * 1024


def passed_along(block, axis, distance):
    devices = range(lax.axis_size(axis))
    route = [(i - distance, i) for i in devices if i - distance in devices]
    return lax.ppermute(block, axis, route)


def phase_pair(left_count, right_count, period, left_start, right_start):
    left_idx = lax.broadcasted_iota(jnp.int32, (left_count, right_count), 0) + left_start
    right_idx = lax.broadcasted_iota(jnp.int32, (left_count, right_count), 1) + right_start
    angle_all = (left_idx * right_idx % period).astype(jnp.float32) * (TWO_PI / period)
    return (jnp.cos(angle_all), jnp.sin(angle_all))


def contract(pattern, matrix, values):
    return jnp.einsum(
        pattern, matrix, values, precision=HIGHEST, preferred_element_type=jnp.float32
    )


def forward_spectrum(signal):
    seq_parts = lax.axis_size("seq")
    row_count = signal.shape[0]
    row_share = row_count // seq_parts
    period = 2 * seq_parts * row_count
    spread_in = lax.all_to_all(signal[None], "seq", split_axis=1, concat_axis=0, tiled=True)
    outer_cos, outer_sin = phase_pair(2 * seq_parts, seq_parts, 2 * seq_parts, 0, 0)
    section_re = contract("cp,prw->crw", outer_cos, spread_in)
    section_im = -contract("cp,prw->crw", outer_sin, spread_in)
    twist_cos, twist_sin = phase_pair(
        2 * seq_parts, row_share, period, 0, lax.axis_index("seq") * row_share
    )
    twist_cos = twist_cos[:, :, None]
    twist_sin = twist_sin[:, :, None]
    turned_re = section_re * twist_cos + section_im * twist_sin
    turned_im = section_im * twist_cos - section_re * twist_sin
    inner_cos, inner_sin = phase_pair(row_count, row_count, row_count, 0, 0)
    piece_re = lax.all_to_all(turned_re, "seq", split_axis=0, concat_axis=1, tiled=True)
    piece_im = lax.all_to_all(turned_im, "seq", split_axis=0, concat_axis=1, tiled=True)
    spec_re = contract("dm,cmk->cdk", inner_cos, piece_re) + contract(
        "dm,cmk->cdk", inner_sin, piece_im
    )
    spec_im = contract("dm,cmk->cdk", inner_cos, piece_im) - contract(
        "dm,cmk->cdk", inner_sin, piece_re
    )
    return (spec_re, spec_im)


def time_signal(spec_re, spec_im):
    seq_parts = lax.axis_size("seq")
    row_count = spec_re.shape[1]
    period = 2 * seq_parts * row_count
    inner_cos, inner_sin = phase_pair(row_count, row_count, row_count, 0, 0)
    back_re = contract("md,cdk->cmk", inner_cos, spec_re) - contract(
        "md,cdk->cmk", inner_sin, spec_im
    )
    back_im = contract("md,cdk->cmk", inner_cos, spec_im) + contract(
        "md,cdk->cmk", inner_sin, spec_re
    )
    twist_cos, twist_sin = phase_pair(2, row_count, period, 2 * lax.axis_index("seq"), 0)
    twist_cos = twist_cos[:, :, None]
    twist_sin = twist_sin[:, :, None]
    turned_re = back_re * twist_cos - back_im * twist_sin
    turned_im = back_im * twist_cos + back_re * twist_sin
    outer_cos, outer_sin = phase_pair(seq_parts, 2 * seq_parts, 2 * seq_parts, 0, 0)
    piece_re = lax.all_to_all(turned_re, "seq", split_axis=1, concat_axis=0, tiled=True)
    piece_im = lax.all_to_all(turned_im, "seq", split_axis=1, concat_axis=0, tiled=True)
    summed = contract("pc,crk->prk", outer_cos, piece_re) - contract(
        "pc,crk->prk", outer_sin, piece_im
    )
    returned = summed * (1.0 / period)
    return lax.all_to_all(returned, "seq", split_axis=0, concat_axis=1, tiled=True)[0]


def spread_layer(qkv, filt, skip_gain, short_weight, w_out, g_out):
    row_count = qkv.shape[1]
    slab_width = qkv.shape[2]
    tail_rows = passed_along(qkv[:, row_count - 2 :, :], "seq", 1)
    extended = jnp.concatenate([tail_rows, qkv], axis=1)
    short = (
        short_weight[:, 0, None, :] * extended[:, 2:, :]
        + short_weight[:, 1, None, :] * extended[:, 1:-1, :]
        + short_weight[:, 2, None, :] * extended[:, :-2, :]
    )
    query_gate = short[0]
    key_short = short[1]
    value_short = short[2]
    mixed = key_short * value_short
    both_re, both_im = forward_spectrum(jnp.concatenate([mixed, filt], axis=1))
    signal_re = both_re[:, :, :slab_width]
    signal_im = both_im[:, :, :slab_width]
    kernel_re = both_re[:, :, slab_width:]
    kernel_im = both_im[:, :, slab_width:]
    conv_out = time_signal(
        signal_re * kernel_re - signal_im * kernel_im, signal_re * kernel_im + signal_im * kernel_re
    )
    long_out = conv_out + skip_gain * mixed
    gated_out = (query_gate * long_out).astype(jnp.bfloat16)
    projected = jnp.dot(
        lax.all_gather(gated_out, "ch", axis=1, tiled=True),
        w_out,
        preferred_element_type=jnp.float32,
    )
    output = projected.astype(jnp.bfloat16)
    grad_all = lax.all_gather(g_out, "ch", axis=1, tiled=True)
    rows_all = lax.all_to_all(w_out, "ch", split_axis=0, concat_axis=1, tiled=True)
    grad_gated = lax.dot_general(
        grad_all, rows_all, (((1,), (1,)), ((), ())), preferred_element_type=jnp.float32
    )
    grad_long = grad_gated * query_gate
    grad_query = grad_gated * long_out
    grad_re, grad_im = forward_spectrum(grad_long)
    pair_re = jnp.concatenate(
        [kernel_re * grad_re + kernel_im * grad_im, signal_re * grad_re + signal_im * grad_im],
        axis=2,
    )
    pair_im = jnp.concatenate(
        [kernel_re * grad_im - kernel_im * grad_re, signal_re * grad_im - signal_im * grad_re],
        axis=2,
    )
    pair_time = time_signal(pair_re, pair_im)
    grad_mixed = pair_time[:, :slab_width] + skip_gain * grad_long
    token_total = lax.axis_size("seq") * row_count
    grad_filter = pair_time[:, slab_width:] * (1.0 / math.sqrt(token_total))
    grad_short = jnp.stack([grad_query, grad_mixed * value_short, grad_mixed * key_short])
    head_rows = passed_along(grad_short[:, :2, :], "seq", -1)
    extended_grad = jnp.concatenate([grad_short, head_rows], axis=1)
    grad_qkv = (
        short_weight[:, 0, None, :] * extended_grad[:, :-2, :]
        + short_weight[:, 1, None, :] * extended_grad[:, 1:-1, :]
        + short_weight[:, 2, None, :] * extended_grad[:, 2:, :]
    ).astype(jnp.bfloat16)
    return (output, grad_qkv, grad_filter)


def split_bf16(values):
    high = values.astype(np.float32).astype(jnp.bfloat16)
    low = (values - high.astype(np.float64)).astype(np.float32).astype(jnp.bfloat16)
    return high, low


def phase_tables(tokens):
    quarter = tokens // PHASES
    freq = 2 * np.arange(quarter)[:, None] + 1
    turn = math.pi / (2 * tokens)
    angle = (freq * PHASES * np.arange(quarter)[None, :] % (4 * tokens)) * turn
    forward = np.concatenate([np.cos(angle), -np.sin(angle)], axis=1)
    backward = np.concatenate([np.cos(angle).T, -np.sin(angle).T], axis=1) / tokens
    angle = freq * np.arange(PHASES)[None, :] * turn
    twist = np.concatenate([np.cos(angle), np.sin(angle)], axis=1)
    twist = np.pad(twist, ((0, 0), (0, LANES - 2 * PHASES)))
    high, rest = split_bf16(twist)
    last = split_bf16(twist - high.astype(np.float64) - rest.astype(np.float64))[0]
    tables = np.zeros((8, quarter, 2 * quarter), jnp.bfloat16)
    tables[0], tables[1] = split_bf16(forward)
    tables[2], tables[3] = split_bf16(backward)
    for i, term in enumerate((high, rest, last)):
        tables[4, :, i * LANES : (i + 1) * LANES] = term
    return tables


def row_order(rows, back=False):
    to, at = [lax.broadcasted_iota(jnp.int32, (rows, rows), int(i != back)) for i in range(2)]
    share = rows // PHASES
    wanted = (to & (share - 1)) * PHASES + lax.shift_right_logical(to, share.bit_length() - 1)
    return jnp.where(wanted == at, 1.0, 0.0).astype(BF16)


def mm(a, b):
    return lax.dot_general(a, b, (((1,), (0,)), ((), ())), preferred_element_type=F32)


def low_lanes(shape):
    return lax.broadcasted_iota(jnp.int32, shape, 1) < HALF


def swap(x):
    return pltpu.roll(x, HALF, 1)


class Near:
    def __init__(self, array, kept=False):
        self.array = array
        self.kept = kept


class Far:
    def __init__(self, array, cuts=None, turned=(), into=None, axis=0):
        self.array = array
        self.turned = turned
        self.into = into
        self.axis = axis
        if turned:
            step = array.shape[0] // len(turned)
            cuts = [(mask * step, step) for mask in turned]
        self.cuts = cuts or [(0, array.shape[axis])]
        self.shape = list(array.shape)
        self.shape[axis] = sum(count for _, count in self.cuts)


class Stage:
    def __init__(self, items, count_in, refs):
        arrays, scratch = list(refs[: len(items)]), list(refs[len(items) :])
        sems = scratch.pop()
        self.count_in = count_in
        self.held, self.copies, self.waiting = [], [], []
        used = 0
        for i, (item, array) in enumerate(zip(items, arrays)):
            group = []
            if isinstance(item, Near):
                self.held.append(array)
            else:
                held = scratch.pop(0) if item.into is None else arrays[count_in + item.into]
                self.held.append(held)
                at = 0
                for cut, (start, count) in enumerate(item.cuts):
                    lead = (slice(None),) * item.axis
                    there = held.at[(*lead, pl.ds(start if item.turned else at, count))]
                    at += count
                    if item.turned:
                        mask = item.turned[cut]
                        start = pl.multiple_of((lax.axis_index("ch") ^ mask) * count, count)
                    here = array.at[(*lead, pl.ds(start, count))]
                    if i >= count_in:
                        here, there = there, here
                    group.append(pltpu.make_async_copy(here, there, sems.at[used]))
                    used += 1
            self.copies.append(group)
            self.waiting.append(set(range(len(group))))
        self.given = set()

    def bring(self, index):
        for copy in self.copies[index]:
            copy.start()

    def take(self, index, cut=None):
        for i in sorted(self.waiting[index]):
            if cut is None or cut == i:
                self.copies[index][i].wait()
                self.waiting[index].discard(i)
        return self.held[index]

    def out(self, index):
        return self.held[self.count_in + index]

    def give(self, index, cut=None):
        for i, copy in enumerate(self.copies[self.count_in + index]):
            if (index, i) not in self.given and cut in (None, i):
                copy.start()
                self.given.add((index, i))


def staged(kernel, items, count_in, *refs):
    stage = Stage(items, count_in, refs)
    for i in range(count_in):
        stage.bring(i)
    kernel(stage)
    for i in range(count_in):
        stage.take(i)
    for i in range(len(items) - count_in):
        stage.give(i)
    for i in range(len(items) - count_in):
        stage.take(count_in + i)


def operand_of(x):
    if isinstance(x, Near) and not x.kept:
        return x.array
    space = pltpu.VMEM if isinstance(x, Near) else pltpu.HBM
    return pltpu.with_memory_space_constraint(x.array, space)


def result_of(x):
    make = pltpu.HBM if isinstance(x, Far) else pltpu.VMEM if x.kept else jax.ShapeDtypeStruct
    return make(x.array.shape, x.array.dtype)


def call(kernel, results, *args, flops=0):
    items = list(args) + list(results)
    specs, scratch, used = [], [], 0
    for item in items:
        near = isinstance(item, Near)
        specs.append(pl.BlockSpec(memory_space=pltpu.VMEM if near else pltpu.HBM))
        if not near:
            used += len(item.cuts)
            if item.into is None:
                scratch.append(pltpu.VMEM(tuple(item.shape), item.array.dtype))
    moved = sum(math.prod(x.array.shape) * x.array.dtype.itemsize for x in items)
    return pl.pallas_call(
        functools.partial(staged, kernel, items, len(args)),
        out_shape=[result_of(x) for x in results],
        in_specs=specs[: len(args)],
        out_specs=specs[len(args) :],
        scratch_shapes=scratch + [pltpu.SemaphoreType.DMA((max(used, 1),))],
        compiler_params=pltpu.CompilerParams(vmem_limit_bytes=VMEM_LIMIT),
        cost_estimate=pl.CostEstimate(flops=flops, bytes_accessed=moved, transcendentals=0),
    )(*[operand_of(x) for x in args])


def lane_tile(x, index):
    return x[:, index * LANES : (index + 1) * LANES]


def pair(first, second):
    low = low_lanes(first.shape)
    return jnp.where(low, first, swap(second)), jnp.where(low, swap(first), second)


def both(x):
    turned, low = swap(x), low_lanes(x.shape)
    return jnp.where(low, x, turned), jnp.where(low, turned, x)


def shifted(x, before):
    rows = lax.broadcasted_iota(jnp.int32, x.shape, 0)
    last, first = before[1:2, :], before[0:1, :]
    one = jnp.where(rows == 0, last, pltpu.roll(x, 1, 0))
    two = jnp.where(rows == 0, first, jnp.where(rows == 1, last, pltpu.roll(x, 2, 0)))
    return one, two


def advanced(x, after):
    count = x.shape[0]
    rows = lax.broadcasted_iota(jnp.int32, x.shape, 0)
    first, last = after[0:1, :], after[1:2, :]
    one = jnp.where(rows == count - 1, first, pltpu.roll(x, count - 1, 0))
    two = jnp.where(
        rows == count - 1, last, jnp.where(rows == count - 2, first, pltpu.roll(x, count - 2, 0))
    )
    return one, two


def put_rows(x, send_ref, at):
    half = x.shape[0] // 2
    for tile in range(x.shape[1] // LANES):
        t = lane_tile(x, tile)
        first, second = pair(t[:half], t[half:])
        send_ref[2 * tile, at : at + half] = first.astype(BF16)
        send_ref[2 * tile + 1, at : at + half] = second.astype(BF16)


def put_strip(x, send_ref, at):
    x = jnp.concatenate([x, jnp.zeros((STRIP - x.shape[0], x.shape[1]), F32)], axis=0)
    for tile in range(x.shape[1] // LANES):
        t = lane_tile(x, tile)
        send_ref[2 * tile, at : at + STRIP] = t.astype(BF16)
        send_ref[2 * tile + 1, at : at + STRIP] = swap(t).astype(BF16)


def strip_of(ref, at):
    tiles = []
    for tile in range(ref.shape[0] // 2):
        x, y = [ref[2 * tile + i, at : at + STRIP].astype(F32) for i in range(2)]
        tiles.append(jnp.where(low_lanes(x.shape), x, swap(y)))
    return jnp.concatenate(tiles, axis=1)


def exact_rows(x):
    high = x.astype(BF16).astype(F32)
    return jnp.concatenate([high, x - high], axis=0)


def group_rows(x):
    return lax.broadcasted_iota(jnp.int32, x.shape, 0) & 7


def earlier(x, count):
    return pltpu.roll(x, x.shape[0] - count, 0)


def strip_groups(ref, at, half):
    x = ref[:, at : at + STRIP, :].astype(F32)[:, 8 * half : 8 * half + 8, :]
    return x.reshape(8 * ref.shape[0], LANES)


def exact_groups(*halves):
    strips = []
    for x in halves:
        x = jnp.where(group_rows(x) < 2, x, 0.0)
        high = x.astype(BF16).astype(F32)
        strips.append((high + pltpu.roll(x - high, 2, 0)).reshape(x.shape[0] // 8, 8, LANES))
    return jnp.concatenate(strips, axis=1).astype(BF16)


def own_rows(x):
    none, last = jnp.zeros_like(x[:1]), x[x.shape[0] - 1 :]
    return jnp.concatenate([x[:2], none, x[:1], last, none, x[x.shape[0] - 2 :]], axis=0)


def first_rows(groups, weight):
    last = jnp.concatenate([jnp.zeros((8, LANES), F32), groups[: groups.shape[0] - 8]], axis=0)
    return (
        weight[0:1] * groups
        + weight[1:2] * (earlier(groups, 2) + earlier(last, 4))
        + weight[2:3] * earlier(last, 6)
    )


def short_of(x, weight):
    one, two = shifted(x, jnp.zeros((2, x.shape[1]), F32))
    return weight[0:1, :] * x + weight[1:2, :] * one + weight[2:3, :] * two


def adjoint_of(x, after, weight):
    one, two = advanced(x, after)
    return weight[0:1, :] * x + weight[1:2, :] * one + weight[2:3, :] * two


def start_kernel(stage):
    send_ref, weight_ref = stage.out(0), stage.take(0)
    qkv_ref = stage.take(1)
    rows = qkv_ref.shape[1]
    order = row_order(rows)
    query, key, value = [qkv_ref[i].astype(F32) for i in range(3)]
    put_strip(own_rows(query), send_ref, rows)
    key_rows, value_rows = own_rows(key), own_rows(value)
    mixed = short_of(key, weight_ref[1]) * short_of(value, weight_ref[2])
    mixed, taps = mm(order, mixed.astype(BF16)), mm(order, stage.take(2)[...].astype(BF16))
    for tile in range(mixed.shape[1] // LANES):
        strips = pair(lane_tile(key_rows, tile), lane_tile(value_rows, tile))
        parts = pair(lane_tile(mixed, tile), lane_tile(taps, tile))
        for i in range(2):
            send_ref[2 * tile + i, :rows] = parts[i].astype(BF16)
            raw = send_ref[2 * tile + i, rows:].astype(F32)
            raw = jnp.concatenate([raw[:8], strips[i]], axis=0)
            send_ref[2 * tile + i, rows:] = raw.astype(BF16)


def partial_product(g, w_ref, mask):
    width = g.shape[1]
    w = w_ref[mask * width : (mask + 1) * width, :]
    return lax.dot_general(g, w, (((1,), (1,)), ((), ())), preferred_element_type=F32)


def first_product_kernel(stage):
    g, out_ref = stage.take(0)[...], stage.out(0)
    for i, mask in enumerate((1, 3)):
        out_ref[i] = partial_product(g, stage.take(1, i), mask).astype(BF16)


def second_product_kernel(stage):
    w_ref, g, near_ref = stage.take(1), stage.take(0)[...], stage.take(2)
    across_ref, own_ref = stage.out(0), stage.out(1)
    across = partial_product(g, w_ref, 2) + near_ref[1].astype(F32)
    across_ref[...] = across.astype(BF16)
    stage.give(0)
    own_ref[...] = partial_product(g, w_ref, 0) + near_ref[0].astype(F32)


def query_kernel(stage):
    weight_ref, qkv_ref, short_ref = stage.take(1), stage.take(0), stage.out(4)
    for i in range(3):
        short_ref[i] = short_of(qkv_ref[i].astype(F32), weight_ref[i])
    stage.give(4)
    stage.out(3)[...] = short_ref[0]


def put_grads(stage, at, send_ref):
    grad_gated = stage.take(at)[...] + stage.take(at + 1)[...].astype(F32)
    stage.out(2)[...] = grad_gated
    stage.give(2)
    rows = grad_gated.shape[0]
    first = exact_rows(grad_gated[:2])
    put_strip(jnp.concatenate([jnp.zeros_like(first), first], axis=0), send_ref, rows)
    grad_long = (grad_gated * stage.take(at + 2)[...]).astype(BF16)
    put_rows(mm(row_order(rows), grad_long), send_ref, rows // 2)


def spread_phases(parts):
    (a_re, a_im), (b_re, b_im), (c_re, c_im), (d_re, d_im) = parts
    s_re, s_im, t_re, t_im = a_re + c_re, a_im + c_im, a_re - c_re, a_im - c_im
    u_re, u_im, v_re, v_im = b_re + d_re, b_im + d_im, b_re - d_re, b_im - d_im
    return [
        (s_re + u_re, s_im + u_im),
        (t_re + v_im, t_im - v_re),
        (s_re - u_re, s_im - u_im),
        (t_re - v_im, t_im + v_re),
    ]


def gather_phases(parts):
    (a_re, a_im), (b_re, b_im), (c_re, c_im), (d_re, d_im) = parts
    s_re, s_im, t_re, t_im = a_re + c_re, a_im + c_im, a_re - c_re, a_im - c_im
    u_re, u_im, v_re, v_im = b_re + d_re, b_im + d_im, b_re - d_re, b_im - d_im
    return [
        (s_re + u_re, s_im + u_im),
        (t_re - v_im, t_im + v_re),
        (s_re - u_re, s_im - u_im),
        (t_re + v_im, t_im - v_re),
    ]


def rows_of(ref, start, count):
    block = ref[:, start : start + count, :]
    return block.reshape(ref.shape[0] * count, ref.shape[2])


def turned_back(re, im, twist, phase):
    if phase == 0:
        return re, im
    c, s = twist[:, phase : phase + 1], twist[:, PHASES + phase : PHASES + phase + 1]
    return re * c + im * s, im * c - re * s


def turned_on(re, im, twist, phase):
    if phase == 0:
        return re, im
    c, s = twist[:, phase : phase + 1], twist[:, PHASES + phase : PHASES + phase + 1]
    return re * c - im * s, re * s + im * c


def lane_tile(x, index):
    return x[:, index * LANES : (index + 1) * LANES]


def causal(parts, weight):
    rows = lax.broadcasted_iota(jnp.int32, parts[0].shape, 0)
    two, three = [jnp.where(rows == 0, 0.0, pltpu.roll(parts[p], 1, 0)) for p in (2, 3)]
    once, twice = [three, *parts[:3]], [two, three, *parts[:2]]
    return [
        weight[0:1] * x + weight[1:2] * y + weight[2:3] * z for x, y, z in zip(parts, once, twice)
    ]


def anticausal(parts, weight):
    count = parts[0].shape[0]
    rows = lax.broadcasted_iota(jnp.int32, parts[0].shape, 0)
    zero, one = [
        jnp.where(rows == count - 1, 0.0, pltpu.roll(parts[p], count - 1, 0)) for p in (0, 1)
    ]
    once, twice = [*parts[1:], zero], [*parts[2:], zero, one]
    return [
        weight[0:1] * x + weight[1:2] * y + weight[2:3] * z for x, y, z in zip(parts, once, twice)
    ]


def halves(x):
    high = x.astype(BF16)
    return high, (x - high.astype(F32)).astype(BF16)


def twiddles(table_ref):
    terms = [table_ref[2, :, i * LANES : (i + 1) * LANES].astype(F32) for i in range(3)]
    return terms[0] + (terms[1] + terms[2])


def columns(parts):
    return jnp.concatenate(parts, axis=1)


def two_sides(table, x):
    quarter = table.shape[0]
    return [mm(table[:, :quarter], x), mm(table[:, quarter:], x)]


def spectrum_of(sides, twist):
    turned = []
    for phase, (re, im) in enumerate(sides):
        turned.append(turned_back(re, im, twist, phase))
    return spread_phases(turned)


def back_values(spectrum, twist):
    return [
        jnp.concatenate(turned_on(re, im, twist, phase), axis=0)
        for phase, (re, im) in enumerate(gather_phases(spectrum))
    ]


def own_weights(weight_ref, gain_ref):
    place = lax.axis_index("seq")
    lanes = pl.ds(pl.multiple_of(place // 2 * LANES, LANES), LANES)
    odd = place % 2 == 1

    def mine(x):
        return jnp.where(odd, swap(x), x)

    query, key, value = [mine(weight_ref[i, :, lanes]) for i in range(3)]
    gain = both(mine(gain_ref[:, lanes]))[0]
    return jnp.where(low_lanes(key.shape), key, swap(value)), query, gain


def first_mask(quarter, share):
    rows = lax.broadcasted_iota(jnp.int32, (quarter, LANES), 0) & (share - 1)
    return (rows == 0) & low_lanes((quarter, LANES))


def spread_first(groups, index, share):
    x = groups.reshape(groups.shape[0] // 8, 8, LANES)[:, index : index + 1, :]
    return jnp.broadcast_to(x, (x.shape[0], share, LANES)).reshape(x.shape[0] * share, LANES)


def gather_first(parts, share):
    tops = []
    for x in parts:
        tops.append(
            jnp.concatenate([x[at : at + 8] for at in range(0, x.shape[0], share)], axis=0)
        )
    return jnp.where(group_rows(tops[0]) == 0, tops[0], pltpu.roll(tops[1], 1, 0))


def forward_kernel(stage):
    recv_ref, weight_ref, gain_ref = [stage.take(i) for i in range(3)]
    send_ref, saved_ref = stage.out(0), stage.out(1)
    blocks = recv_ref.shape[0]
    rows = recv_ref.shape[1] - STRIP
    share = rows // PHASES
    quarter = blocks * share
    low, starting = low_lanes((quarter, LANES)), first_mask(quarter, share)
    pair_weight, query_weight, gain = own_weights(weight_ref, gain_ref)
    query = first_rows(strip_groups(recv_ref, rows, 0), query_weight)
    pairs = first_rows(strip_groups(recv_ref, rows, 1), pair_weight)
    saved_ref[10, 8:9, :] = gain
    saved_ref[10, 64 : 64 + 8 * blocks, :] = query
    saved_ref[10, 128 : 128 + 8 * blocks, :] = pairs
    strip = exact_groups(query, pairs)
    fixed = pairs * swap(pairs)

    starts = [phase * share for phase in range(PHASES)]
    x = [rows_of(recv_ref, at, share).astype(F32) for at in starts]
    for i in range(2):
        x[i] = jnp.where(starting, spread_first(fixed, i, share), x[i])
    high = columns([y.astype(BF16) for y in x])
    fh, fl = stage.take(3)[0], stage.take(3)[1]
    twist = twiddles(stage.take(3))
    main = [y + z for y, z in zip(two_sides(fh, high), two_sides(fl, high))]
    sides = [[lane_tile(y, phase) for y in main] for phase in range(PHASES)]
    product = []
    for r, (re, im) in enumerate(spectrum_of(sides, twist)):
        saved_ref[2 * r] = re
        saved_ref[2 * r + 1] = im
        other_re, other_im = swap(re), swap(im)
        product.append((re * other_re - im * other_im, re * other_im + im * other_re))

    values = back_values(product, twist)
    bh, bl = stage.take(4)[0], stage.take(4)[1]
    wide = low_lanes((2 * quarter, LANES))
    high = [y.astype(BF16) for y in values]
    wider = [y.astype(F32) for y in high]
    both_parts = [jnp.where(wide, z, y - z).astype(BF16) for y, z in zip(values, wider)]
    high = [jnp.where(wide, wider[i], wider[i + 2]).astype(BF16) for i in range(2)]
    main, more = mm(bh, columns(both_parts)), mm(bl, columns(high))
    put_grads(stage, 5, send_ref)
    send_ref[:, rows:, :] = strip + send_ref[:, rows:, :]
    stage.give(0, 1)
    summed = [y + swap(y) for y in (lane_tile(main, phase) for phase in range(PHASES))]
    for i in range(2):
        conv = jnp.where(low, summed[i], summed[i + 2]) + lane_tile(more, i)
        long_out = conv + gain * jnp.where(low, x[i], swap(x[i + 2]))
        saved_ref[8 + i] = long_out
        long_out = long_out.astype(BF16).reshape(blocks, share, LANES)
        send_ref[:, starts[i] : starts[i] + share, :] = long_out


def backward_kernel(stage):
    grad_ref, saved_ref, send_ref = stage.take(0), stage.take(1), stage.out(0)
    blocks = grad_ref.shape[0]
    rows = grad_ref.shape[1] - STRIP
    share = rows // PHASES
    quarter = blocks * share
    low, starting = low_lanes((quarter, LANES)), first_mask(quarter, share)
    gain, groups = saved_ref[10, 8:9, :], 8 * blocks
    query, pairs = [saved_ref[10, at : at + groups, :] for at in (64, 128)]
    strip = strip_groups(grad_ref, rows, 0)
    first = earlier(strip, 4) + earlier(strip, 6)
    fixed = first * query
    starts = [phase * share for phase in range(PHASES)]
    grad_long = []
    for i, at in enumerate(starts[2:]):
        packed = rows_of(grad_ref, at, share).astype(F32)
        grad_long.append(jnp.where(starting, spread_first(fixed, i, share), packed))

    fh, fl = stage.take(2)[0], stage.take(2)[1]
    twist = twiddles(stage.take(2))
    high, rest = halves(columns(grad_long))
    three = zip(two_sides(fh, high), two_sides(fl, high), two_sides(fh, rest))
    main = [x + y + z for x, y, z in three]
    sides = []
    for phase in range(PHASES):
        sides.append([both(lane_tile(x, phase % 2))[phase // 2] for x in main])
    product = []
    for r, (re, im) in enumerate(spectrum_of(sides, twist)):
        k_re, k_im = saved_ref[2 * r], saved_ref[2 * r + 1]
        product.append((k_re * re + k_im * im, k_re * im - k_im * re))
    high, rest = halves(columns(back_values(product, twist)))
    bh, bl = stage.take(3)[0], stage.take(3)[1]
    times = mm(bh, high) + mm(bl, high) + mm(bh, rest)

    scale = 1.0 / math.sqrt(PHASES * quarter)
    grad_long = [swap(x) for x in grad_long] + grad_long
    grads = []
    for phase, at in enumerate(starts):
        x = lane_tile(times, phase)
        grads.append(jnp.where(low, x * scale, x + gain * grad_long[phase]))
        send_ref[:, at : at + share, :] = grads[-1].astype(BF16).reshape(blocks, share, LANES)
    stage.give(0, 0)
    query_head = first * gather_first([saved_ref[8], saved_ref[9]], share)
    pair_head = both(gather_first(grads[:2], share))[1] * swap(pairs)
    heads = []
    for x in (query_head, pair_head):
        heads.append(jnp.concatenate([x[8:], jnp.zeros((8, LANES), F32)], axis=0))
    send_ref[:, rows:, :] = exact_groups(*heads)


def unpacked(ref, at, half, order):
    tiles = []
    for tile in range(ref.shape[0] // 2):
        x, y = [ref[2 * tile + i, at : at + half].astype(F32) for i in range(2)]
        top, bottom = pair(x, y)
        tiles.append(jnp.concatenate([top, bottom], axis=0))
    return mm(order, jnp.concatenate(tiles, axis=1).astype(BF16))


def pair_strip_of(ref, at):
    sides = [[], []]
    for tile in range(ref.shape[0] // 2):
        x, y = [ref[2 * tile + i, at : at + STRIP].astype(F32)[8:] for i in range(2)]
        for side, z in zip(sides, pair(x, y)):
            side.append(z)
    return [columns(side) for side in sides]


def gate_kernel(stage):
    recv_ref, gated_ref, long_ref, tops_ref = stage.take(0), *[stage.out(i) for i in range(3)]
    rows = recv_ref.shape[1] - STRIP
    key, value = [x[0:2] + x[2:4] for x in pair_strip_of(recv_ref, rows)]
    tops_ref[...] = jnp.concatenate([key, value, key, value], axis=0)
    long_out = unpacked(recv_ref, 0, rows // 2, row_order(rows, back=True))
    long_ref[...] = long_out
    stage.give(1)
    query = stage.take(1)[0]
    gated_ref[...] = (query * long_out).astype(BF16)
    strip = strip_of(recv_ref, rows)
    first = strip + earlier(strip, 2)
    row = lax.broadcasted_iota(jnp.int32, first.shape, 0)
    first = jnp.where(row < 2, first, query[:STRIP])
    gated_ref[:STRIP, :] = (first * long_out[:STRIP]).astype(BF16)


def output_kernel(parts, stage):
    w_ref, total = stage.take(0), None
    for part in range(parts):
        gated = stage.take(1 + part)[...]
        width = gated.shape[1]
        term = mm(gated, w_ref[part * width : (part + 1) * width, :])
        total = term if total is None else total + term
    stage.out(0)[...] = total.astype(BF16)


def end_kernel(stage):
    recv_ref, grad_ref, filter_ref = stage.take(0), stage.out(0), stage.out(1)
    rows = filter_ref.shape[0]
    order = row_order(rows, back=True)
    sides = [[], []]
    for tile in range(recv_ref.shape[0] // 2):
        x, y = [recv_ref[2 * tile + i, :rows].astype(F32) for i in range(2)]
        for side, z in zip(sides, pair(x, y)):
            side.append(z.astype(BF16))
    taps, mixed = [mm(order, columns(side)) for side in sides]
    filter_ref[...] = taps
    stage.give(1)
    weight_ref, tops, short_ref = stage.take(1), stage.take(2)[...], stage.take(3)
    row = lax.broadcasted_iota(jnp.int32, mixed.shape, 0)
    heads = [x[0:2] + x[2:4] for x in pair_strip_of(recv_ref, rows)]
    for i in range(2):
        top = tops[2 - 2 * i : 4 - 2 * i]
        other = jnp.where(row == 0, top[0:1], jnp.where(row == 1, top[1:2], short_ref[1 - i]))
        grad_ref[i] = adjoint_of(mixed * other, heads[i], weight_ref[1 + i]).astype(BF16)
    stage.give(0, 0)
    strip = strip_of(recv_ref, rows)
    head = strip[0:2] + strip[2:4]
    grad_query = stage.take(4)[...] * stage.take(5)[...]
    grad_ref[2] = adjoint_of(grad_query, head, weight_ref[0]).astype(BF16)


def partner(x, axis, mask):
    return lax.ppermute(x, axis, [(i, i ^ mask) for i in range(lax.axis_size(axis))])


def exchanged(x, axis):
    return lax.all_to_all(x, axis, split_axis=0, concat_axis=0, tiled=True)


def owner_layer(qkv, filt, skip_gain, short_weight, w_out, g_out):
    shape = jax.ShapeDtypeStruct
    seq_parts, ch_parts = lax.axis_size("seq"), lax.axis_size("ch")
    rows, width = qkv.shape[1], qkv.shape[2]
    tokens = seq_parts * rows
    quarter = tokens // PHASES
    tables = jnp.asarray(phase_tables(tokens))
    table_flops = 2 * 2 * 2 * 3 * tokens * tokens // PHASES * LANES
    product_flops = 2 * rows * width * width * ch_parts
    half = rows // 2
    wide = shape((seq_parts, rows + STRIP, LANES), BF16)
    column = shape((rows, width), BF16)
    saved = shape((11, quarter, LANES), F32)
    gain = skip_gain[None, :]

    (send,) = call(start_kernel, [Far(wide)], Far(short_weight), Far(qkv), Far(filt))
    recv = exchanged(send, "seq")
    half_sums, w_kept, g_kept = call(
        first_product_kernel,
        [
            Near(shape((2, rows, width), BF16), kept=True),
            Near(w_out, kept=True),
            Near(g_out, kept=True),
        ],
        Far(g_out, into=2),
        Far(w_out, turned=(1, 3, 2, 0), into=1),
        flops=product_flops // 2,
    )
    half_sums = partner(half_sums, "ch", 1)
    across, own = call(
        second_product_kernel,
        [Near(column, kept=True), Near(shape((rows, width), F32), kept=True)],
        Near(g_kept),
        Near(w_kept),
        Near(half_sums),
        flops=product_flops // 2,
    )
    across = partner(across, "ch", 2)
    def pinned(x):
        return Near(x, kept=True)

    tables_back = Far(tables, [(2, 2)])
    exact = shape((rows, width), F32)
    tables_on, weight, gain, query, short = call(
        query_kernel,
        [
            pinned(shape((3, *tables.shape[1:]), BF16)),
            pinned(short_weight),
            pinned(gain),
            pinned(exact),
            Far(shape((3, rows, width), F32)),
        ],
        Far(qkv),
        Far(short_weight, into=1),
        Far(tables, [(0, 2), (4, 1)], into=0),
        Far(gain, into=2),
    )
    send, saved, grad_far = call(
        forward_kernel,
        [
            Far(wide, [(0, half), (half, half + STRIP)], axis=1),
            pinned(saved),
            Far(exact),
        ],
        pinned(recv),
        Near(weight),
        Near(gain),
        Near(tables_on),
        tables_back,
        Near(own),
        Near(across),
        Near(query),
        flops=table_flops,
    )
    swapped = exchanged(send, "seq")
    (send,) = call(
        backward_kernel,
        [Far(wide, [(0, rows), (rows, STRIP)], axis=1)],
        Near(swapped),
        Near(saved),
        Near(tables_on),
        tables_back,
        flops=table_flops,
    )
    grad_recv = exchanged(send, "seq")
    gated, long_out, tops = call(
        gate_kernel,
        [pinned(column), Far(exact), Far(shape((8, width), F32))],
        Near(swapped),
        Far(short, [(0, 1)]),
    )
    across = partner(gated, "ch", 2)
    near, far = partner(gated, "ch", 1), partner(across, "ch", 1)
    (output,) = call(
        functools.partial(output_kernel, ch_parts),
        [Far(column)],
        Near(w_kept),
        Near(gated),
        Near(near),
        Near(across),
        Near(far),
        flops=product_flops,
    )
    grad_qkv, grad_filter = call(
        end_kernel,
        [Far(shape((3, rows, width), BF16), [(1, 2), (0, 1)]), Far(exact)],
        Near(grad_recv),
        Far(short_weight),
        Far(tops),
        Far(short, [(1, 2)]),
        Far(long_out),
        Far(grad_far),
    )
    return (output, grad_qkv, grad_filter)


def local(qkv, filt, skip_gain, short_weight, w_out, g_out):
    seq_parts = lax.axis_size("seq")
    rows, width = qkv.shape[1], qkv.shape[2]
    fits = width == HALF * seq_parts and rows % HALF == 0 and rows & (rows - 1) == 0 and rows * seq_parts <= 2048
    if fits and lax.axis_size("ch") == 4:
        return owner_layer(qkv, filt, skip_gain, short_weight, w_out, g_out)
    return spread_layer(qkv, filt, skip_gain, short_weight, w_out, g_out)


def solution(mesh):
    in_specs = (
        P(None, "seq", "ch"),
        P("seq", "ch"),
        P("ch"),
        P(None, None, "ch"),
        P(None, "ch"),
        P("seq", "ch"),
    )
    out_specs = (P("seq", "ch"), P(None, "seq", "ch"), P("seq", "ch"))
    return jax.shard_map(local, mesh=mesh, in_specs=in_specs, out_specs=out_specs, check_vma=False)
```

```python
import functools
import math

import jax
import jax.numpy as jnp
import numpy as np
from jax import lax
from jax.experimental import pallas as pl
from jax.experimental.pallas import tpu as pltpu
from jax.sharding import PartitionSpec as P

HIGHEST = lax.Precision.HIGHEST
TWO_PI = 2.0 * math.pi
LANES = 128
HALF = 64
PHASES = 4
STRIP = 16
BF16 = jnp.bfloat16
F32 = jnp.float32
VMEM_LIMIT = 24 * 1024 * 1024


def passed_along(block, axis, distance):
    devices = range(lax.axis_size(axis))
    route = [(i - distance, i) for i in devices if i - distance in devices]
    return lax.ppermute(block, axis, route)


def phase_pair(left_count, right_count, period, left_start, right_start):
    left_idx = lax.broadcasted_iota(jnp.int32, (left_count, right_count), 0) + left_start
    right_idx = lax.broadcasted_iota(jnp.int32, (left_count, right_count), 1) + right_start
    angle_all = (left_idx * right_idx % period).astype(jnp.float32) * (TWO_PI / period)
    return (jnp.cos(angle_all), jnp.sin(angle_all))


def contract(pattern, matrix, values):
    return jnp.einsum(
        pattern, matrix, values, precision=HIGHEST, preferred_element_type=jnp.float32
    )


def forward_spectrum(signal):
    seq_parts = lax.axis_size("seq")
    row_count = signal.shape[0]
    row_share = row_count // seq_parts
    period = 2 * seq_parts * row_count
    spread_in = lax.all_to_all(signal[None], "seq", split_axis=1, concat_axis=0, tiled=True)
    outer_cos, outer_sin = phase_pair(2 * seq_parts, seq_parts, 2 * seq_parts, 0, 0)
    section_re = contract("cp,prw->crw", outer_cos, spread_in)
    section_im = -contract("cp,prw->crw", outer_sin, spread_in)
    twist_cos, twist_sin = phase_pair(
        2 * seq_parts, row_share, period, 0, lax.axis_index("seq") * row_share
    )
    twist_cos = twist_cos[:, :, None]
    twist_sin = twist_sin[:, :, None]
    turned_re = section_re * twist_cos + section_im * twist_sin
    turned_im = section_im * twist_cos - section_re * twist_sin
    inner_cos, inner_sin = phase_pair(row_count, row_count, row_count, 0, 0)
    piece_re = lax.all_to_all(turned_re, "seq", split_axis=0, concat_axis=1, tiled=True)
    piece_im = lax.all_to_all(turned_im, "seq", split_axis=0, concat_axis=1, tiled=True)
    spec_re = contract("dm,cmk->cdk", inner_cos, piece_re) + contract(
        "dm,cmk->cdk", inner_sin, piece_im
    )
    spec_im = contract("dm,cmk->cdk", inner_cos, piece_im) - contract(
        "dm,cmk->cdk", inner_sin, piece_re
    )
    return (spec_re, spec_im)


def time_signal(spec_re, spec_im):
    seq_parts = lax.axis_size("seq")
    row_count = spec_re.shape[1]
    period = 2 * seq_parts * row_count
    inner_cos, inner_sin = phase_pair(row_count, row_count, row_count, 0, 0)
    back_re = contract("md,cdk->cmk", inner_cos, spec_re) - contract(
        "md,cdk->cmk", inner_sin, spec_im
    )
    back_im = contract("md,cdk->cmk", inner_cos, spec_im) + contract(
        "md,cdk->cmk", inner_sin, spec_re
    )
    twist_cos, twist_sin = phase_pair(2, row_count, period, 2 * lax.axis_index("seq"), 0)
    twist_cos = twist_cos[:, :, None]
    twist_sin = twist_sin[:, :, None]
    turned_re = back_re * twist_cos - back_im * twist_sin
    turned_im = back_im * twist_cos + back_re * twist_sin
    outer_cos, outer_sin = phase_pair(seq_parts, 2 * seq_parts, 2 * seq_parts, 0, 0)
    piece_re = lax.all_to_all(turned_re, "seq", split_axis=1, concat_axis=0, tiled=True)
    piece_im = lax.all_to_all(turned_im, "seq", split_axis=1, concat_axis=0, tiled=True)
    summed = contract("pc,crk->prk", outer_cos, piece_re) - contract(
        "pc,crk->prk", outer_sin, piece_im
    )
    returned = summed * (1.0 / period)
    return lax.all_to_all(returned, "seq", split_axis=0, concat_axis=1, tiled=True)[0]


def spread_layer(qkv, filt, skip_gain, short_weight, w_out, g_out):
    row_count = qkv.shape[1]
    slab_width = qkv.shape[2]
    tail_rows = passed_along(qkv[:, row_count - 2 :, :], "seq", 1)
    extended = jnp.concatenate([tail_rows, qkv], axis=1)
    short = (
        short_weight[:, 0, None, :] * extended[:, 2:, :]
        + short_weight[:, 1, None, :] * extended[:, 1:-1, :]
        + short_weight[:, 2, None, :] * extended[:, :-2, :]
    )
    query_gate = short[0]
    key_short = short[1]
    value_short = short[2]
    mixed = key_short * value_short
    both_re, both_im = forward_spectrum(jnp.concatenate([mixed, filt], axis=1))
    signal_re = both_re[:, :, :slab_width]
    signal_im = both_im[:, :, :slab_width]
    kernel_re = both_re[:, :, slab_width:]
    kernel_im = both_im[:, :, slab_width:]
    conv_out = time_signal(
        signal_re * kernel_re - signal_im * kernel_im, signal_re * kernel_im + signal_im * kernel_re
    )
    long_out = conv_out + skip_gain * mixed
    gated_out = (query_gate * long_out).astype(jnp.bfloat16)
    projected = jnp.dot(
        lax.all_gather(gated_out, "ch", axis=1, tiled=True),
        w_out,
        preferred_element_type=jnp.float32,
    )
    output = projected.astype(jnp.bfloat16)
    grad_all = lax.all_gather(g_out, "ch", axis=1, tiled=True)
    rows_all = lax.all_to_all(w_out, "ch", split_axis=0, concat_axis=1, tiled=True)
    grad_gated = lax.dot_general(
        grad_all, rows_all, (((1,), (1,)), ((), ())), preferred_element_type=jnp.float32
    )
    grad_long = grad_gated * query_gate
    grad_query = grad_gated * long_out
    grad_re, grad_im = forward_spectrum(grad_long)
    pair_re = jnp.concatenate(
        [kernel_re * grad_re + kernel_im * grad_im, signal_re * grad_re + signal_im * grad_im],
        axis=2,
    )
    pair_im = jnp.concatenate(
        [kernel_re * grad_im - kernel_im * grad_re, signal_re * grad_im - signal_im * grad_re],
        axis=2,
    )
    pair_time = time_signal(pair_re, pair_im)
    grad_mixed = pair_time[:, :slab_width] + skip_gain * grad_long
    token_total = lax.axis_size("seq") * row_count
    grad_filter = pair_time[:, slab_width:] * (1.0 / math.sqrt(token_total))
    grad_short = jnp.stack([grad_query, grad_mixed * value_short, grad_mixed * key_short])
    head_rows = passed_along(grad_short[:, :2, :], "seq", -1)
    extended_grad = jnp.concatenate([grad_short, head_rows], axis=1)
    grad_qkv = (
        short_weight[:, 0, None, :] * extended_grad[:, :-2, :]
        + short_weight[:, 1, None, :] * extended_grad[:, 1:-1, :]
        + short_weight[:, 2, None, :] * extended_grad[:, 2:, :]
    ).astype(jnp.bfloat16)
    return (output, grad_qkv, grad_filter)


def split_bf16(values):
    high = values.astype(np.float32).astype(jnp.bfloat16)
    low = (values - high.astype(np.float64)).astype(np.float32).astype(jnp.bfloat16)
    return high, low


def phase_tables(tokens):
    quarter = tokens // PHASES
    freq = 2 * np.arange(quarter)[:, None] + 1
    turn = math.pi / (2 * tokens)
    angle = (freq * PHASES * np.arange(quarter)[None, :] % (4 * tokens)) * turn
    forward = np.concatenate([np.cos(angle), -np.sin(angle)], axis=1)
    backward = np.concatenate([np.cos(angle).T, -np.sin(angle).T], axis=1) / tokens
    angle = freq * np.arange(PHASES)[None, :] * turn
    twist = np.concatenate([np.cos(angle), np.sin(angle)], axis=1)
    twist = np.pad(twist, ((0, 0), (0, LANES - 2 * PHASES)))
    high, rest = split_bf16(twist)
    last = split_bf16(twist - high.astype(np.float64) - rest.astype(np.float64))[0]
    tables = np.zeros((8, quarter, 2 * quarter), jnp.bfloat16)
    tables[0], tables[1] = split_bf16(forward)
    tables[2], tables[3] = split_bf16(backward)
    for i, term in enumerate((high, rest, last)):
        tables[4, :, i * LANES : (i + 1) * LANES] = term
    return tables


def row_order(rows, back=False):
    to, at = [lax.broadcasted_iota(jnp.int32, (rows, rows), int(i != back)) for i in range(2)]
    share = rows // PHASES
    wanted = (to & (share - 1)) * PHASES + lax.shift_right_logical(to, share.bit_length() - 1)
    return jnp.where(wanted == at, 1.0, 0.0).astype(BF16)


def mm(a, b):
    return lax.dot_general(a, b, (((1,), (0,)), ((), ())), preferred_element_type=F32)


def low_lanes(shape):
    return lax.broadcasted_iota(jnp.int32, shape, 1) < HALF


def swap(x):
    return pltpu.roll(x, HALF, 1)


class Near:
    def __init__(self, array, kept=False):
        self.array = array
        self.kept = kept


class Far:
    def __init__(self, array, cuts=None, turned=(), into=None, axis=0):
        self.array = array
        self.turned = turned
        self.into = into
        self.axis = axis
        if turned:
            step = array.shape[0] // len(turned)
            cuts = [(mask * step, step) for mask in turned]
        self.cuts = cuts or [(0, array.shape[axis])]
        self.shape = list(array.shape)
        self.shape[axis] = sum(count for _, count in self.cuts)


class Stage:
    def __init__(self, items, count_in, refs):
        arrays, scratch = list(refs[: len(items)]), list(refs[len(items) :])
        sems = scratch.pop()
        self.count_in = count_in
        self.held, self.copies, self.waiting = [], [], []
        used = 0
        for i, (item, array) in enumerate(zip(items, arrays)):
            group = []
            if isinstance(item, Near):
                self.held.append(array)
            else:
                held = scratch.pop(0) if item.into is None else arrays[count_in + item.into]
                self.held.append(held)
                at = 0
                for cut, (start, count) in enumerate(item.cuts):
                    lead = (slice(None),) * item.axis
                    there = held.at[(*lead, pl.ds(start if item.turned else at, count))]
                    at += count
                    if item.turned:
                        mask = item.turned[cut]
                        start = pl.multiple_of((lax.axis_index("ch") ^ mask) * count, count)
                    here = array.at[(*lead, pl.ds(start, count))]
                    if i >= count_in:
                        here, there = there, here
                    group.append(pltpu.make_async_copy(here, there, sems.at[used]))
                    used += 1
            self.copies.append(group)
            self.waiting.append(set(range(len(group))))
        self.given = set()

    def bring(self, index):
        for copy in self.copies[index]:
            copy.start()

    def take(self, index, cut=None):
        for i in sorted(self.waiting[index]):
            if cut is None or cut == i:
                self.copies[index][i].wait()
                self.waiting[index].discard(i)
        return self.held[index]

    def out(self, index):
        return self.held[self.count_in + index]

    def give(self, index, cut=None):
        for i, copy in enumerate(self.copies[self.count_in + index]):
            if (index, i) not in self.given and cut in (None, i):
                copy.start()
                self.given.add((index, i))


def staged(kernel, items, count_in, *refs):
    stage = Stage(items, count_in, refs)
    for i in range(count_in):
        stage.bring(i)
    kernel(stage)
    for i in range(count_in):
        stage.take(i)
    for i in range(len(items) - count_in):
        stage.give(i)
    for i in range(len(items) - count_in):
        stage.take(count_in + i)


def operand_of(x):
    if isinstance(x, Near) and not x.kept:
        return x.array
    space = pltpu.VMEM if isinstance(x, Near) else pltpu.HBM
    return pltpu.with_memory_space_constraint(x.array, space)


def result_of(x):
    make = pltpu.HBM if isinstance(x, Far) else pltpu.VMEM if x.kept else jax.ShapeDtypeStruct
    return make(x.array.shape, x.array.dtype)


def call(kernel, results, *args, flops=0):
    items = list(args) + list(results)
    specs, scratch, used = [], [], 0
    for item in items:
        near = isinstance(item, Near)
        specs.append(pl.BlockSpec(memory_space=pltpu.VMEM if near else pltpu.HBM))
        if not near:
            used += len(item.cuts)
            if item.into is None:
                scratch.append(pltpu.VMEM(tuple(item.shape), item.array.dtype))
    moved = sum(math.prod(x.array.shape) * x.array.dtype.itemsize for x in items)
    return pl.pallas_call(
        functools.partial(staged, kernel, items, len(args)),
        out_shape=[result_of(x) for x in results],
        in_specs=specs[: len(args)],
        out_specs=specs[len(args) :],
        scratch_shapes=scratch + [pltpu.SemaphoreType.DMA((max(used, 1),))],
        compiler_params=pltpu.CompilerParams(vmem_limit_bytes=VMEM_LIMIT),
        cost_estimate=pl.CostEstimate(flops=flops, bytes_accessed=moved, transcendentals=0),
    )(*[operand_of(x) for x in args])


def lane_tile(x, index):
    return x[:, index * LANES : (index + 1) * LANES]


def pair(first, second):
    low = low_lanes(first.shape)
    return jnp.where(low, first, swap(second)), jnp.where(low, swap(first), second)


def both(x):
    turned, low = swap(x), low_lanes(x.shape)
    return jnp.where(low, x, turned), jnp.where(low, turned, x)


def shifted(x, before):
    rows = lax.broadcasted_iota(jnp.int32, x.shape, 0)
    last, first = before[1:2, :], before[0:1, :]
    one = jnp.where(rows == 0, last, pltpu.roll(x, 1, 0))
    two = jnp.where(rows == 0, first, jnp.where(rows == 1, last, pltpu.roll(x, 2, 0)))
    return one, two


def advanced(x, after):
    count = x.shape[0]
    rows = lax.broadcasted_iota(jnp.int32, x.shape, 0)
    first, last = after[0:1, :], after[1:2, :]
    one = jnp.where(rows == count - 1, first, pltpu.roll(x, count - 1, 0))
    two = jnp.where(
        rows == count - 1, last, jnp.where(rows == count - 2, first, pltpu.roll(x, count - 2, 0))
    )
    return one, two


def put_rows(x, send_ref, at):
    half = x.shape[0] // 2
    for tile in range(x.shape[1] // LANES):
        t = lane_tile(x, tile)
        first, second = pair(t[:half], t[half:])
        send_ref[2 * tile, at : at + half] = first.astype(BF16)
        send_ref[2 * tile + 1, at : at + half] = second.astype(BF16)


def put_strip(x, send_ref, at):
    x = jnp.concatenate([x, jnp.zeros((STRIP - x.shape[0], x.shape[1]), F32)], axis=0)
    for tile in range(x.shape[1] // LANES):
        t = lane_tile(x, tile)
        send_ref[2 * tile, at : at + STRIP] = t.astype(BF16)
        send_ref[2 * tile + 1, at : at + STRIP] = swap(t).astype(BF16)


def strip_of(ref, at):
    tiles = []
    for tile in range(ref.shape[0] // 2):
        x, y = [ref[2 * tile + i, at : at + STRIP].astype(F32) for i in range(2)]
        tiles.append(jnp.where(low_lanes(x.shape), x, swap(y)))
    return jnp.concatenate(tiles, axis=1)


def exact_rows(x):
    high = x.astype(BF16).astype(F32)
    return jnp.concatenate([high, x - high], axis=0)


def group_rows(x):
    return lax.broadcasted_iota(jnp.int32, x.shape, 0) & 7


def earlier(x, count):
    return pltpu.roll(x, x.shape[0] - count, 0)


def strip_groups(ref, at, half):
    x = ref[:, at : at + STRIP, :].astype(F32)[:, 8 * half : 8 * half + 8, :]
    return x.reshape(8 * ref.shape[0], LANES)


def exact_groups(*halves):
    strips = []
    for x in halves:
        x = jnp.where(group_rows(x) < 2, x, 0.0)
        high = x.astype(BF16).astype(F32)
        strips.append((high + pltpu.roll(x - high, 2, 0)).reshape(x.shape[0] // 8, 8, LANES))
    return jnp.concatenate(strips, axis=1).astype(BF16)


def own_rows(x):
    none, last = jnp.zeros_like(x[:1]), x[x.shape[0] - 1 :]
    return jnp.concatenate([x[:2], none, x[:1], last, none, x[x.shape[0] - 2 :]], axis=0)


def first_rows(groups, weight):
    last = jnp.concatenate([jnp.zeros((8, LANES), F32), groups[: groups.shape[0] - 8]], axis=0)
    return (
        weight[0:1] * groups
        + weight[1:2] * (earlier(groups, 2) + earlier(last, 4))
        + weight[2:3] * earlier(last, 6)
    )


def short_of(x, weight):
    one, two = shifted(x, jnp.zeros((2, x.shape[1]), F32))
    return weight[0:1, :] * x + weight[1:2, :] * one + weight[2:3, :] * two


def adjoint_of(x, after, weight):
    one, two = advanced(x, after)
    return weight[0:1, :] * x + weight[1:2, :] * one + weight[2:3, :] * two


def start_kernel(stage):
    send_ref, weight_ref = stage.out(0), stage.take(0)
    qkv_ref = stage.take(1)
    rows = qkv_ref.shape[1]
    order = row_order(rows)
    query, key, value = [qkv_ref[i].astype(F32) for i in range(3)]
    put_strip(own_rows(query), send_ref, rows)
    key_rows, value_rows = own_rows(key), own_rows(value)
    mixed = short_of(key, weight_ref[1]) * short_of(value, weight_ref[2])
    mixed, taps = mm(order, mixed.astype(BF16)), mm(order, stage.take(2)[...].astype(BF16))
    for tile in range(mixed.shape[1] // LANES):
        strips = pair(lane_tile(key_rows, tile), lane_tile(value_rows, tile))
        parts = pair(lane_tile(mixed, tile), lane_tile(taps, tile))
        for i in range(2):
            send_ref[2 * tile + i, :rows] = parts[i].astype(BF16)
            raw = send_ref[2 * tile + i, rows:].astype(F32)
            raw = jnp.concatenate([raw[:8], strips[i]], axis=0)
            send_ref[2 * tile + i, rows:] = raw.astype(BF16)


def partial_product(g, w_ref, mask):
    width = g.shape[1]
    w = w_ref[mask * width : (mask + 1) * width, :]
    return lax.dot_general(g, w, (((1,), (1,)), ((), ())), preferred_element_type=F32)


def first_product_kernel(stage):
    g, out_ref = stage.take(0)[...], stage.out(0)
    for i, mask in enumerate((1, 3)):
        out_ref[i] = partial_product(g, stage.take(1, i), mask).astype(BF16)


def second_product_kernel(stage):
    w_ref, g, near_ref = stage.take(1), stage.take(0)[...], stage.take(2)
    across_ref, own_ref = stage.out(0), stage.out(1)
    across = partial_product(g, w_ref, 2) + near_ref[1].astype(F32)
    across_ref[...] = across.astype(BF16)
    stage.give(0)
    own_ref[...] = partial_product(g, w_ref, 0) + near_ref[0].astype(F32)


def query_kernel(stage):
    weight_ref, qkv_ref, short_ref = stage.take(1), stage.take(0), stage.out(4)
    for i in range(3):
        short_ref[i] = short_of(qkv_ref[i].astype(F32), weight_ref[i])
    stage.give(4)
    stage.out(3)[...] = short_ref[0]


def sum_kernel(stage):
    send_ref, kept_ref = stage.out(0), stage.out(1)
    grad_gated = stage.take(0)[...] + stage.take(1)[...].astype(F32)
    kept_ref[...] = grad_gated
    stage.give(1)
    rows = grad_gated.shape[0]
    first = exact_rows(grad_gated[:2])
    put_strip(jnp.concatenate([jnp.zeros_like(first), first], axis=0), send_ref, rows // 2)
    put_rows(mm(row_order(rows), (grad_gated * stage.take(2)[...]).astype(BF16)), send_ref, 0)


def spread_phases(parts):
    (a_re, a_im), (b_re, b_im), (c_re, c_im), (d_re, d_im) = parts
    s_re, s_im, t_re, t_im = a_re + c_re, a_im + c_im, a_re - c_re, a_im - c_im
    u_re, u_im, v_re, v_im = b_re + d_re, b_im + d_im, b_re - d_re, b_im - d_im
    return [
        (s_re + u_re, s_im + u_im),
        (t_re + v_im, t_im - v_re),
        (s_re - u_re, s_im - u_im),
        (t_re - v_im, t_im + v_re),
    ]


def gather_phases(parts):
    (a_re, a_im), (b_re, b_im), (c_re, c_im), (d_re, d_im) = parts
    s_re, s_im, t_re, t_im = a_re + c_re, a_im + c_im, a_re - c_re, a_im - c_im
    u_re, u_im, v_re, v_im = b_re + d_re, b_im + d_im, b_re - d_re, b_im - d_im
    return [
        (s_re + u_re, s_im + u_im),
        (t_re - v_im, t_im + v_re),
        (s_re - u_re, s_im - u_im),
        (t_re + v_im, t_im - v_re),
    ]


def rows_of(ref, start, count):
    block = ref[:, start : start + count, :]
    return block.reshape(ref.shape[0] * count, ref.shape[2])


def turned_back(re, im, twist, phase):
    if phase == 0:
        return re, im
    c, s = twist[:, phase : phase + 1], twist[:, PHASES + phase : PHASES + phase + 1]
    return re * c + im * s, im * c - re * s


def turned_on(re, im, twist, phase):
    if phase == 0:
        return re, im
    c, s = twist[:, phase : phase + 1], twist[:, PHASES + phase : PHASES + phase + 1]
    return re * c - im * s, re * s + im * c


def lane_tile(x, index):
    return x[:, index * LANES : (index + 1) * LANES]


def causal(parts, weight):
    rows = lax.broadcasted_iota(jnp.int32, parts[0].shape, 0)
    two, three = [jnp.where(rows == 0, 0.0, pltpu.roll(parts[p], 1, 0)) for p in (2, 3)]
    once, twice = [three, *parts[:3]], [two, three, *parts[:2]]
    return [
        weight[0:1] * x + weight[1:2] * y + weight[2:3] * z for x, y, z in zip(parts, once, twice)
    ]


def anticausal(parts, weight):
    count = parts[0].shape[0]
    rows = lax.broadcasted_iota(jnp.int32, parts[0].shape, 0)
    zero, one = [
        jnp.where(rows == count - 1, 0.0, pltpu.roll(parts[p], count - 1, 0)) for p in (0, 1)
    ]
    once, twice = [*parts[1:], zero], [*parts[2:], zero, one]
    return [
        weight[0:1] * x + weight[1:2] * y + weight[2:3] * z for x, y, z in zip(parts, once, twice)
    ]


def halves(x):
    high = x.astype(BF16)
    return high, (x - high.astype(F32)).astype(BF16)


def twiddles(table_ref):
    terms = [table_ref[2, :, i * LANES : (i + 1) * LANES].astype(F32) for i in range(3)]
    return terms[0] + (terms[1] + terms[2])


def columns(parts):
    return jnp.concatenate(parts, axis=1)


def two_sides(table, x):
    quarter = table.shape[0]
    return [mm(table[:, :quarter], x), mm(table[:, quarter:], x)]


def spectrum_of(sides, twist):
    turned = []
    for phase, (re, im) in enumerate(sides):
        turned.append(turned_back(re, im, twist, phase))
    return spread_phases(turned)


def back_values(spectrum, twist):
    return [
        jnp.concatenate(turned_on(re, im, twist, phase), axis=0)
        for phase, (re, im) in enumerate(gather_phases(spectrum))
    ]


def own_weights(weight_ref, gain_ref):
    place = lax.axis_index("seq")
    lanes = pl.ds(pl.multiple_of(place // 2 * LANES, LANES), LANES)
    odd = place % 2 == 1

    def mine(x):
        return jnp.where(odd, swap(x), x)

    query, key, value = [mine(weight_ref[i, :, lanes]) for i in range(3)]
    gain = both(mine(gain_ref[:, lanes]))[0]
    return jnp.where(low_lanes(key.shape), key, swap(value)), query, gain


def first_mask(quarter, share):
    rows = lax.broadcasted_iota(jnp.int32, (quarter, LANES), 0) & (share - 1)
    return (rows == 0) & low_lanes((quarter, LANES))


def spread_first(groups, index, share):
    x = groups.reshape(groups.shape[0] // 8, 8, LANES)[:, index : index + 1, :]
    return jnp.broadcast_to(x, (x.shape[0], share, LANES)).reshape(x.shape[0] * share, LANES)


def gather_first(parts, share):
    tops = []
    for x in parts:
        tops.append(
            jnp.concatenate([x[at : at + 8] for at in range(0, x.shape[0], share)], axis=0)
        )
    return jnp.where(group_rows(tops[0]) == 0, tops[0], pltpu.roll(tops[1], 1, 0))


def forward_kernel(stage):
    recv_ref, weight_ref, gain_ref = [stage.take(i) for i in range(3)]
    send_ref, saved_ref = stage.out(0), stage.out(1)
    blocks = recv_ref.shape[0]
    rows = recv_ref.shape[1] - STRIP
    share = rows // PHASES
    quarter = blocks * share
    low, starting = low_lanes((quarter, LANES)), first_mask(quarter, share)
    pair_weight, query_weight, gain = own_weights(weight_ref, gain_ref)
    query = first_rows(strip_groups(recv_ref, rows, 0), query_weight)
    pairs = first_rows(strip_groups(recv_ref, rows, 1), pair_weight)
    saved_ref[10, 8:9, :] = gain
    saved_ref[10, 64 : 64 + 8 * blocks, :] = query
    saved_ref[10, 128 : 128 + 8 * blocks, :] = pairs
    strip = exact_groups(query, pairs)
    fixed = pairs * swap(pairs)

    starts = [phase * share for phase in range(PHASES)]
    x = [rows_of(recv_ref, at, share).astype(F32) for at in starts]
    for i in range(2):
        x[i] = jnp.where(starting, spread_first(fixed, i, share), x[i])
    high = columns([y.astype(BF16) for y in x])
    fh, fl = stage.take(3)[0], stage.take(3)[1]
    twist = twiddles(stage.take(3))
    main = [y + z for y, z in zip(two_sides(fh, high), two_sides(fl, high))]
    sides = [[lane_tile(y, phase) for y in main] for phase in range(PHASES)]
    product = []
    for r, (re, im) in enumerate(spectrum_of(sides, twist)):
        saved_ref[2 * r] = re
        saved_ref[2 * r + 1] = im
        other_re, other_im = swap(re), swap(im)
        product.append((re * other_re - im * other_im, re * other_im + im * other_re))

    values = back_values(product, twist)
    bh, bl = stage.take(4)[0], stage.take(4)[1]
    wide = low_lanes((2 * quarter, LANES))
    high = [y.astype(BF16) for y in values]
    wider = [y.astype(F32) for y in high]
    both_parts = [jnp.where(wide, z, y - z).astype(BF16) for y, z in zip(values, wider)]
    high = [jnp.where(wide, wider[i], wider[i + 2]).astype(BF16) for i in range(2)]
    main, more = mm(bh, columns(both_parts)), mm(bl, columns(high))
    grad_ref = stage.take(5)
    send_ref[:, rows // 2 : rows, :] = grad_ref[:, : rows // 2, :]
    send_ref[:, rows:, :] = strip + grad_ref[:, rows // 2 :, :]
    stage.give(0, 1)
    summed = [y + swap(y) for y in (lane_tile(main, phase) for phase in range(PHASES))]
    for i in range(2):
        conv = jnp.where(low, summed[i], summed[i + 2]) + lane_tile(more, i)
        long_out = conv + gain * jnp.where(low, x[i], swap(x[i + 2]))
        saved_ref[8 + i] = long_out
        long_out = long_out.astype(BF16).reshape(blocks, share, LANES)
        send_ref[:, starts[i] : starts[i] + share, :] = long_out


def backward_kernel(stage):
    grad_ref, saved_ref, send_ref = stage.take(0), stage.take(1), stage.out(0)
    blocks = grad_ref.shape[0]
    rows = grad_ref.shape[1] - STRIP
    share = rows // PHASES
    quarter = blocks * share
    low, starting = low_lanes((quarter, LANES)), first_mask(quarter, share)
    gain, groups = saved_ref[10, 8:9, :], 8 * blocks
    query, pairs = [saved_ref[10, at : at + groups, :] for at in (64, 128)]
    strip = strip_groups(grad_ref, rows, 0)
    first = earlier(strip, 4) + earlier(strip, 6)
    fixed = first * query
    starts = [phase * share for phase in range(PHASES)]
    grad_long = []
    for i, at in enumerate(starts[2:]):
        packed = rows_of(grad_ref, at, share).astype(F32)
        grad_long.append(jnp.where(starting, spread_first(fixed, i, share), packed))

    fh, fl = stage.take(2)[0], stage.take(2)[1]
    twist = twiddles(stage.take(2))
    high, rest = halves(columns(grad_long))
    three = zip(two_sides(fh, high), two_sides(fl, high), two_sides(fh, rest))
    main = [x + y + z for x, y, z in three]
    gate(grad_ref, stage.take(4)[0], *[stage.out(i) for i in (1, 2, 3)])
    stage.give(2)
    stage.give(3)
    sides = []
    for phase in range(PHASES):
        sides.append([both(lane_tile(x, phase % 2))[phase // 2] for x in main])
    product = []
    for r, (re, im) in enumerate(spectrum_of(sides, twist)):
        k_re, k_im = saved_ref[2 * r], saved_ref[2 * r + 1]
        product.append((k_re * re + k_im * im, k_re * im - k_im * re))
    high, rest = halves(columns(back_values(product, twist)))
    bh, bl = stage.take(3)[0], stage.take(3)[1]
    times = mm(bh, high) + mm(bl, high) + mm(bh, rest)

    scale = 1.0 / math.sqrt(PHASES * quarter)
    grad_long = [swap(x) for x in grad_long] + grad_long
    grads = []
    for phase, at in enumerate(starts):
        x = lane_tile(times, phase)
        grads.append(jnp.where(low, x * scale, x + gain * grad_long[phase]))
        send_ref[:, at : at + share, :] = grads[-1].astype(BF16).reshape(blocks, share, LANES)
    stage.give(0, 0)
    query_head = first * gather_first([saved_ref[8], saved_ref[9]], share)
    pair_head = both(gather_first(grads[:2], share))[1] * swap(pairs)
    heads = []
    for x in (query_head, pair_head):
        heads.append(jnp.concatenate([x[8:], jnp.zeros((8, LANES), F32)], axis=0))
    send_ref[:, rows:, :] = exact_groups(*heads)


def unpacked(ref, at, half, order):
    tiles = []
    for tile in range(ref.shape[0] // 2):
        x, y = [ref[2 * tile + i, at : at + half].astype(F32) for i in range(2)]
        top, bottom = pair(x, y)
        tiles.append(jnp.concatenate([top, bottom], axis=0))
    return mm(order, jnp.concatenate(tiles, axis=1).astype(BF16))


def pair_strip_of(ref, at):
    sides = [[], []]
    for tile in range(ref.shape[0] // 2):
        x, y = [ref[2 * tile + i, at : at + STRIP].astype(F32)[8:] for i in range(2)]
        for side, z in zip(sides, pair(x, y)):
            side.append(z)
    return [columns(side) for side in sides]


def gate(recv_ref, query, gated_ref, long_ref, tops_ref):
    rows = recv_ref.shape[1] - STRIP
    key, value = [x[0:2] + x[2:4] for x in pair_strip_of(recv_ref, rows)]
    tops_ref[...] = jnp.concatenate([key, value, key, value], axis=0)
    long_out = unpacked(recv_ref, 0, rows // 2, row_order(rows, back=True))
    long_ref[...] = long_out
    gated_ref[...] = (query * long_out).astype(BF16)
    strip = strip_of(recv_ref, rows)
    first = strip + earlier(strip, 2)
    row = lax.broadcasted_iota(jnp.int32, first.shape, 0)
    first = jnp.where(row < 2, first, query[:STRIP])
    gated_ref[:STRIP, :] = (first * long_out[:STRIP]).astype(BF16)


def output_kernel(parts, stage):
    w_ref, total = stage.take(0), None
    for part in range(parts):
        gated = stage.take(1 + part)[...]
        width = gated.shape[1]
        term = mm(gated, w_ref[part * width : (part + 1) * width, :])
        total = term if total is None else total + term
    stage.out(0)[...] = total.astype(BF16)


def end_kernel(stage):
    recv_ref, grad_ref, filter_ref = stage.take(0), stage.out(0), stage.out(1)
    rows = filter_ref.shape[0]
    order = row_order(rows, back=True)
    sides = [[], []]
    for tile in range(recv_ref.shape[0] // 2):
        x, y = [recv_ref[2 * tile + i, :rows].astype(F32) for i in range(2)]
        for side, z in zip(sides, pair(x, y)):
            side.append(z.astype(BF16))
    taps, mixed = [mm(order, columns(side)) for side in sides]
    filter_ref[...] = taps
    stage.give(1)
    weight_ref, tops, short_ref = stage.take(1), stage.take(2)[...], stage.take(3)
    row = lax.broadcasted_iota(jnp.int32, mixed.shape, 0)
    heads = [x[0:2] + x[2:4] for x in pair_strip_of(recv_ref, rows)]
    for i in range(2):
        top = tops[2 - 2 * i : 4 - 2 * i]
        other = jnp.where(row == 0, top[0:1], jnp.where(row == 1, top[1:2], short_ref[1 - i]))
        grad_ref[i] = adjoint_of(mixed * other, heads[i], weight_ref[1 + i]).astype(BF16)
    stage.give(0, 0)
    strip = strip_of(recv_ref, rows)
    head = strip[0:2] + strip[2:4]
    grad_query = stage.take(4)[...] * stage.take(5)[...]
    grad_ref[2] = adjoint_of(grad_query, head, weight_ref[0]).astype(BF16)


def partner(x, axis, mask):
    return lax.ppermute(x, axis, [(i, i ^ mask) for i in range(lax.axis_size(axis))])


def exchanged(x, axis):
    return lax.all_to_all(x, axis, split_axis=0, concat_axis=0, tiled=True)


def owner_layer(qkv, filt, skip_gain, short_weight, w_out, g_out):
    shape = jax.ShapeDtypeStruct
    seq_parts, ch_parts = lax.axis_size("seq"), lax.axis_size("ch")
    rows, width = qkv.shape[1], qkv.shape[2]
    tokens = seq_parts * rows
    quarter = tokens // PHASES
    tables = jnp.asarray(phase_tables(tokens))
    table_flops = 2 * 2 * 2 * 3 * tokens * tokens // PHASES * LANES
    product_flops = 2 * rows * width * width * ch_parts
    half = rows // 2
    wide = shape((seq_parts, rows + STRIP, LANES), BF16)
    column = shape((rows, width), BF16)
    saved = shape((11, quarter, LANES), F32)
    gain = skip_gain[None, :]

    (send,) = call(start_kernel, [Far(wide)], Far(short_weight), Far(qkv), Far(filt))
    recv = exchanged(send, "seq")
    half_sums, w_kept, g_kept = call(
        first_product_kernel,
        [
            Near(shape((2, rows, width), BF16), kept=True),
            Near(w_out, kept=True),
            Near(g_out, kept=True),
        ],
        Far(g_out, into=2),
        Far(w_out, turned=(1, 3, 2, 0), into=1),
        flops=product_flops // 2,
    )
    half_sums = partner(half_sums, "ch", 1)
    across, own = call(
        second_product_kernel,
        [Near(column, kept=True), Near(shape((rows, width), F32), kept=True)],
        Near(g_kept),
        Near(w_kept),
        Near(half_sums),
        flops=product_flops // 2,
    )
    across = partner(across, "ch", 2)
    def pinned(x):
        return Near(x, kept=True)

    tables_back = Far(tables, [(2, 2)])
    exact = shape((rows, width), F32)
    tables_on, weight, gain, query, short = call(
        query_kernel,
        [
            pinned(shape((3, *tables.shape[1:]), BF16)),
            pinned(short_weight),
            pinned(gain),
            pinned(exact),
            Far(shape((3, rows, width), F32)),
        ],
        Far(qkv),
        Far(short_weight, into=1),
        Far(tables, [(0, 2), (4, 1)], into=0),
        Far(gain, into=2),
    )
    grad_long, grad_far = call(
        sum_kernel,
        [Far(shape((seq_parts, half + STRIP, LANES), BF16)), Far(exact)],
        Near(own),
        Near(across),
        Near(query),
    )
    send, saved = call(
        forward_kernel,
        [
            Far(wide, [(0, half), (half, half + STRIP)], axis=1),
            pinned(saved),
        ],
        pinned(recv),
        Near(weight),
        Near(gain),
        Near(tables_on),
        tables_back,
        Far(grad_long),
        flops=table_flops,
    )
    swapped = exchanged(send, "seq")
    send, gated, long_out, tops = call(
        backward_kernel,
        [
            Far(wide, [(0, rows), (rows, STRIP)], axis=1),
            pinned(column),
            Far(exact),
            Far(shape((8, width), F32)),
        ],
        Near(swapped),
        Near(saved),
        Near(tables_on),
        tables_back,
        Far(short, [(0, 1)]),
        flops=table_flops,
    )
    grad_recv = exchanged(send, "seq")
    across = partner(gated, "ch", 2)
    near, far = partner(gated, "ch", 1), partner(across, "ch", 1)
    (output,) = call(
        functools.partial(output_kernel, ch_parts),
        [Far(column)],
        Near(w_kept),
        Near(gated),
        Near(near),
        Near(across),
        Near(far),
        flops=product_flops,
    )
    grad_qkv, grad_filter = call(
        end_kernel,
        [Far(shape((3, rows, width), BF16), [(1, 2), (0, 1)]), Far(exact)],
        Near(grad_recv),
        Far(short_weight),
        Far(tops),
        Far(short, [(1, 2)]),
        Far(long_out),
        Far(grad_far),
    )
    return (output, grad_qkv, grad_filter)


def local(qkv, filt, skip_gain, short_weight, w_out, g_out):
    seq_parts = lax.axis_size("seq")
    rows, width = qkv.shape[1], qkv.shape[2]
    fits = width == HALF * seq_parts and rows % HALF == 0 and rows & (rows - 1) == 0 and rows * seq_parts <= 2048
    if fits and lax.axis_size("ch") == 4:
        return owner_layer(qkv, filt, skip_gain, short_weight, w_out, g_out)
    return spread_layer(qkv, filt, skip_gain, short_weight, w_out, g_out)


def solution(mesh):
    in_specs = (
        P(None, "seq", "ch"),
        P("seq", "ch"),
        P("ch"),
        P(None, None, "ch"),
        P(None, "ch"),
        P("seq", "ch"),
    )
    out_specs = (P("seq", "ch"), P(None, "seq", "ch"), P("seq", "ch"))
    return jax.shard_map(local, mesh=mesh, in_specs=in_specs, out_specs=out_specs, check_vma=False)
```

```python
import functools
import math

import jax
import jax.numpy as jnp
import numpy as np
from jax import lax
from jax.experimental import pallas as pl
from jax.experimental.pallas import tpu as pltpu
from jax.sharding import PartitionSpec as P

HIGHEST = lax.Precision.HIGHEST
TWO_PI = 2.0 * math.pi
LANES = 128
HALF = 64
PHASES = 4
STRIP = 16
BF16 = jnp.bfloat16
F32 = jnp.float32
VMEM_LIMIT = 24 * 1024 * 1024


def passed_along(block, axis, distance):
    devices = range(lax.axis_size(axis))
    route = [(i - distance, i) for i in devices if i - distance in devices]
    return lax.ppermute(block, axis, route)


def phase_pair(left_count, right_count, period, left_start, right_start):
    left_idx = lax.broadcasted_iota(jnp.int32, (left_count, right_count), 0) + left_start
    right_idx = lax.broadcasted_iota(jnp.int32, (left_count, right_count), 1) + right_start
    angle_all = (left_idx * right_idx % period).astype(jnp.float32) * (TWO_PI / period)
    return (jnp.cos(angle_all), jnp.sin(angle_all))


def contract(pattern, matrix, values):
    return jnp.einsum(
        pattern, matrix, values, precision=HIGHEST, preferred_element_type=jnp.float32
    )


def forward_spectrum(signal):
    seq_parts = lax.axis_size("seq")
    row_count = signal.shape[0]
    row_share = row_count // seq_parts
    period = 2 * seq_parts * row_count
    spread_in = lax.all_to_all(signal[None], "seq", split_axis=1, concat_axis=0, tiled=True)
    outer_cos, outer_sin = phase_pair(2 * seq_parts, seq_parts, 2 * seq_parts, 0, 0)
    section_re = contract("cp,prw->crw", outer_cos, spread_in)
    section_im = -contract("cp,prw->crw", outer_sin, spread_in)
    twist_cos, twist_sin = phase_pair(
        2 * seq_parts, row_share, period, 0, lax.axis_index("seq") * row_share
    )
    twist_cos = twist_cos[:, :, None]
    twist_sin = twist_sin[:, :, None]
    turned_re = section_re * twist_cos + section_im * twist_sin
    turned_im = section_im * twist_cos - section_re * twist_sin
    inner_cos, inner_sin = phase_pair(row_count, row_count, row_count, 0, 0)
    piece_re = lax.all_to_all(turned_re, "seq", split_axis=0, concat_axis=1, tiled=True)
    piece_im = lax.all_to_all(turned_im, "seq", split_axis=0, concat_axis=1, tiled=True)
    spec_re = contract("dm,cmk->cdk", inner_cos, piece_re) + contract(
        "dm,cmk->cdk", inner_sin, piece_im
    )
    spec_im = contract("dm,cmk->cdk", inner_cos, piece_im) - contract(
        "dm,cmk->cdk", inner_sin, piece_re
    )
    return (spec_re, spec_im)


def time_signal(spec_re, spec_im):
    seq_parts = lax.axis_size("seq")
    row_count = spec_re.shape[1]
    period = 2 * seq_parts * row_count
    inner_cos, inner_sin = phase_pair(row_count, row_count, row_count, 0, 0)
    back_re = contract("md,cdk->cmk", inner_cos, spec_re) - contract(
        "md,cdk->cmk", inner_sin, spec_im
    )
    back_im = contract("md,cdk->cmk", inner_cos, spec_im) + contract(
        "md,cdk->cmk", inner_sin, spec_re
    )
    twist_cos, twist_sin = phase_pair(2, row_count, period, 2 * lax.axis_index("seq"), 0)
    twist_cos = twist_cos[:, :, None]
    twist_sin = twist_sin[:, :, None]
    turned_re = back_re * twist_cos - back_im * twist_sin
    turned_im = back_im * twist_cos + back_re * twist_sin
    outer_cos, outer_sin = phase_pair(seq_parts, 2 * seq_parts, 2 * seq_parts, 0, 0)
    piece_re = lax.all_to_all(turned_re, "seq", split_axis=1, concat_axis=0, tiled=True)
    piece_im = lax.all_to_all(turned_im, "seq", split_axis=1, concat_axis=0, tiled=True)
    summed = contract("pc,crk->prk", outer_cos, piece_re) - contract(
        "pc,crk->prk", outer_sin, piece_im
    )
    returned = summed * (1.0 / period)
    return lax.all_to_all(returned, "seq", split_axis=0, concat_axis=1, tiled=True)[0]


def spread_layer(qkv, filt, skip_gain, short_weight, w_out, g_out):
    row_count = qkv.shape[1]
    slab_width = qkv.shape[2]
    tail_rows = passed_along(qkv[:, row_count - 2 :, :], "seq", 1)
    extended = jnp.concatenate([tail_rows, qkv], axis=1)
    short = (
        short_weight[:, 0, None, :] * extended[:, 2:, :]
        + short_weight[:, 1, None, :] * extended[:, 1:-1, :]
        + short_weight[:, 2, None, :] * extended[:, :-2, :]
    )
    query_gate = short[0]
    key_short = short[1]
    value_short = short[2]
    mixed = key_short * value_short
    both_re, both_im = forward_spectrum(jnp.concatenate([mixed, filt], axis=1))
    signal_re = both_re[:, :, :slab_width]
    signal_im = both_im[:, :, :slab_width]
    kernel_re = both_re[:, :, slab_width:]
    kernel_im = both_im[:, :, slab_width:]
    conv_out = time_signal(
        signal_re * kernel_re - signal_im * kernel_im, signal_re * kernel_im + signal_im * kernel_re
    )
    long_out = conv_out + skip_gain * mixed
    gated_out = (query_gate * long_out).astype(jnp.bfloat16)
    projected = jnp.dot(
        lax.all_gather(gated_out, "ch", axis=1, tiled=True),
        w_out,
        preferred_element_type=jnp.float32,
    )
    output = projected.astype(jnp.bfloat16)
    grad_all = lax.all_gather(g_out, "ch", axis=1, tiled=True)
    rows_all = lax.all_to_all(w_out, "ch", split_axis=0, concat_axis=1, tiled=True)
    grad_gated = lax.dot_general(
        grad_all, rows_all, (((1,), (1,)), ((), ())), preferred_element_type=jnp.float32
    )
    grad_long = grad_gated * query_gate
    grad_query = grad_gated * long_out
    grad_re, grad_im = forward_spectrum(grad_long)
    pair_re = jnp.concatenate(
        [kernel_re * grad_re + kernel_im * grad_im, signal_re * grad_re + signal_im * grad_im],
        axis=2,
    )
    pair_im = jnp.concatenate(
        [kernel_re * grad_im - kernel_im * grad_re, signal_re * grad_im - signal_im * grad_re],
        axis=2,
    )
    pair_time = time_signal(pair_re, pair_im)
    grad_mixed = pair_time[:, :slab_width] + skip_gain * grad_long
    token_total = lax.axis_size("seq") * row_count
    grad_filter = pair_time[:, slab_width:] * (1.0 / math.sqrt(token_total))
    grad_short = jnp.stack([grad_query, grad_mixed * value_short, grad_mixed * key_short])
    head_rows = passed_along(grad_short[:, :2, :], "seq", -1)
    extended_grad = jnp.concatenate([grad_short, head_rows], axis=1)
    grad_qkv = (
        short_weight[:, 0, None, :] * extended_grad[:, :-2, :]
        + short_weight[:, 1, None, :] * extended_grad[:, 1:-1, :]
        + short_weight[:, 2, None, :] * extended_grad[:, 2:, :]
    ).astype(jnp.bfloat16)
    return (output, grad_qkv, grad_filter)


def split_bf16(values):
    high = values.astype(np.float32).astype(jnp.bfloat16)
    low = (values - high.astype(np.float64)).astype(np.float32).astype(jnp.bfloat16)
    return high, low


def phase_tables(tokens):
    quarter = tokens // PHASES
    freq = 2 * np.arange(quarter)[:, None] + 1
    turn = math.pi / (2 * tokens)
    angle = (freq * PHASES * np.arange(quarter)[None, :] % (4 * tokens)) * turn
    forward = np.concatenate([np.cos(angle), -np.sin(angle)], axis=1)
    backward = np.concatenate([np.cos(angle).T, -np.sin(angle).T], axis=1) / tokens
    angle = freq * np.arange(PHASES)[None, :] * turn
    twist = np.concatenate([np.cos(angle), np.sin(angle)], axis=1)
    twist = np.pad(twist, ((0, 0), (0, LANES - 2 * PHASES)))
    high, rest = split_bf16(twist)
    last = split_bf16(twist - high.astype(np.float64) - rest.astype(np.float64))[0]
    tables = np.zeros((8, quarter, 2 * quarter), jnp.bfloat16)
    tables[0], tables[1] = split_bf16(forward)
    tables[2], tables[3] = split_bf16(backward)
    for i, term in enumerate((high, rest, last)):
        tables[4, :, i * LANES : (i + 1) * LANES] = term
    return tables


def row_order(rows, back=False):
    to, at = [lax.broadcasted_iota(jnp.int32, (rows, rows), int(i != back)) for i in range(2)]
    share = rows // PHASES
    wanted = (to & (share - 1)) * PHASES + lax.shift_right_logical(to, share.bit_length() - 1)
    return jnp.where(wanted == at, 1.0, 0.0).astype(BF16)


def mm(a, b):
    return lax.dot_general(a, b, (((1,), (0,)), ((), ())), preferred_element_type=F32)


def low_lanes(shape):
    return lax.broadcasted_iota(jnp.int32, shape, 1) < HALF


def swap(x):
    return pltpu.roll(x, HALF, 1)


class Near:
    def __init__(self, array, kept=False):
        self.array = array
        self.kept = kept


class Far:
    def __init__(self, array, cuts=None, turned=(), into=None, axis=0):
        self.array = array
        self.turned = turned
        self.into = into
        self.axis = axis
        if turned:
            step = array.shape[0] // len(turned)
            cuts = [(mask * step, step) for mask in turned]
        self.cuts = cuts or [(0, array.shape[axis])]
        self.shape = list(array.shape)
        self.shape[axis] = sum(count for _, count in self.cuts)


class Stage:
    def __init__(self, items, count_in, refs):
        arrays, scratch = list(refs[: len(items)]), list(refs[len(items) :])
        sems = scratch.pop()
        self.count_in = count_in
        self.held, self.copies, self.waiting = [], [], []
        used = 0
        for i, (item, array) in enumerate(zip(items, arrays)):
            group = []
            if isinstance(item, Near):
                self.held.append(array)
            else:
                held = scratch.pop(0) if item.into is None else arrays[count_in + item.into]
                self.held.append(held)
                at = 0
                for cut, (start, count) in enumerate(item.cuts):
                    lead = (slice(None),) * item.axis
                    there = held.at[(*lead, pl.ds(start if item.turned else at, count))]
                    at += count
                    if item.turned:
                        mask = item.turned[cut]
                        start = pl.multiple_of((lax.axis_index("ch") ^ mask) * count, count)
                    here = array.at[(*lead, pl.ds(start, count))]
                    if i >= count_in:
                        here, there = there, here
                    group.append(pltpu.make_async_copy(here, there, sems.at[used]))
                    used += 1
            self.copies.append(group)
            self.waiting.append(set(range(len(group))))
        self.given = set()

    def bring(self, index):
        for copy in self.copies[index]:
            copy.start()

    def take(self, index, cut=None):
        for i in sorted(self.waiting[index]):
            if cut is None or cut == i:
                self.copies[index][i].wait()
                self.waiting[index].discard(i)
        return self.held[index]

    def out(self, index):
        return self.held[self.count_in + index]

    def give(self, index, cut=None):
        for i, copy in enumerate(self.copies[self.count_in + index]):
            if (index, i) not in self.given and cut in (None, i):
                copy.start()
                self.given.add((index, i))


def staged(kernel, items, count_in, *refs):
    stage = Stage(items, count_in, refs)
    for i in range(count_in):
        stage.bring(i)
    kernel(stage)
    for i in range(count_in):
        stage.take(i)
    for i in range(len(items) - count_in):
        stage.give(i)
    for i in range(len(items) - count_in):
        stage.take(count_in + i)


def operand_of(x):
    if isinstance(x, Near) and not x.kept:
        return x.array
    space = pltpu.VMEM if isinstance(x, Near) else pltpu.HBM
    return pltpu.with_memory_space_constraint(x.array, space)


def result_of(x):
    make = pltpu.HBM if isinstance(x, Far) else pltpu.VMEM if x.kept else jax.ShapeDtypeStruct
    return make(x.array.shape, x.array.dtype)


def call(kernel, results, *args, flops=0):
    items = list(args) + list(results)
    specs, scratch, used = [], [], 0
    for item in items:
        near = isinstance(item, Near)
        specs.append(pl.BlockSpec(memory_space=pltpu.VMEM if near else pltpu.HBM))
        if not near:
            used += len(item.cuts)
            if item.into is None:
                scratch.append(pltpu.VMEM(tuple(item.shape), item.array.dtype))
    moved = sum(math.prod(x.array.shape) * x.array.dtype.itemsize for x in items)
    return pl.pallas_call(
        functools.partial(staged, kernel, items, len(args)),
        out_shape=[result_of(x) for x in results],
        in_specs=specs[: len(args)],
        out_specs=specs[len(args) :],
        scratch_shapes=scratch + [pltpu.SemaphoreType.DMA((max(used, 1),))],
        compiler_params=pltpu.CompilerParams(vmem_limit_bytes=VMEM_LIMIT),
        cost_estimate=pl.CostEstimate(flops=flops, bytes_accessed=moved, transcendentals=0),
    )(*[operand_of(x) for x in args])


def lane_tile(x, index):
    return x[:, index * LANES : (index + 1) * LANES]


def pair(first, second):
    low = low_lanes(first.shape)
    return jnp.where(low, first, swap(second)), jnp.where(low, swap(first), second)


def both(x):
    turned, low = swap(x), low_lanes(x.shape)
    return jnp.where(low, x, turned), jnp.where(low, turned, x)


def shifted(x, before):
    rows = lax.broadcasted_iota(jnp.int32, x.shape, 0)
    last, first = before[1:2, :], before[0:1, :]
    one = jnp.where(rows == 0, last, pltpu.roll(x, 1, 0))
    two = jnp.where(rows == 0, first, jnp.where(rows == 1, last, pltpu.roll(x, 2, 0)))
    return one, two


def advanced(x, after):
    count = x.shape[0]
    rows = lax.broadcasted_iota(jnp.int32, x.shape, 0)
    first, last = after[0:1, :], after[1:2, :]
    one = jnp.where(rows == count - 1, first, pltpu.roll(x, count - 1, 0))
    two = jnp.where(
        rows == count - 1, last, jnp.where(rows == count - 2, first, pltpu.roll(x, count - 2, 0))
    )
    return one, two


def put_rows(x, send_ref, at):
    half = x.shape[0] // 2
    for tile in range(x.shape[1] // LANES):
        t = lane_tile(x, tile)
        first, second = pair(t[:half], t[half:])
        send_ref[2 * tile, at : at + half] = first.astype(BF16)
        send_ref[2 * tile + 1, at : at + half] = second.astype(BF16)


def put_strip(x, send_ref, at):
    x = jnp.concatenate([x, jnp.zeros((STRIP - x.shape[0], x.shape[1]), F32)], axis=0)
    for tile in range(x.shape[1] // LANES):
        t = lane_tile(x, tile)
        send_ref[2 * tile, at : at + STRIP] = t.astype(BF16)
        send_ref[2 * tile + 1, at : at + STRIP] = swap(t).astype(BF16)


def strip_of(ref, at):
    tiles = []
    for tile in range(ref.shape[0] // 2):
        x, y = [ref[2 * tile + i, at : at + STRIP].astype(F32) for i in range(2)]
        tiles.append(jnp.where(low_lanes(x.shape), x, swap(y)))
    return jnp.concatenate(tiles, axis=1)


def exact_rows(x):
    high = x.astype(BF16).astype(F32)
    return jnp.concatenate([high, x - high], axis=0)


def group_rows(x):
    return lax.broadcasted_iota(jnp.int32, x.shape, 0) & 7


def earlier(x, count):
    return pltpu.roll(x, x.shape[0] - count, 0)


def strip_groups(ref, at, half):
    x = ref[:, at : at + STRIP, :].astype(F32)[:, 8 * half : 8 * half + 8, :]
    return x.reshape(8 * ref.shape[0], LANES)


def exact_groups(*halves):
    strips = []
    for x in halves:
        x = jnp.where(group_rows(x) < 2, x, 0.0)
        high = x.astype(BF16).astype(F32)
        strips.append((high + pltpu.roll(x - high, 2, 0)).reshape(x.shape[0] // 8, 8, LANES))
    return jnp.concatenate(strips, axis=1).astype(BF16)


def own_rows(x):
    none, last = jnp.zeros_like(x[:1]), x[x.shape[0] - 1 :]
    return jnp.concatenate([x[:2], none, x[:1], last, none, x[x.shape[0] - 2 :]], axis=0)


def first_rows(groups, weight):
    last = jnp.concatenate([jnp.zeros((8, LANES), F32), groups[: groups.shape[0] - 8]], axis=0)
    return (
        weight[0:1] * groups
        + weight[1:2] * (earlier(groups, 2) + earlier(last, 4))
        + weight[2:3] * earlier(last, 6)
    )


def short_of(x, weight):
    one, two = shifted(x, jnp.zeros((2, x.shape[1]), F32))
    return weight[0:1, :] * x + weight[1:2, :] * one + weight[2:3, :] * two


def adjoint_of(x, after, weight):
    one, two = advanced(x, after)
    return weight[0:1, :] * x + weight[1:2, :] * one + weight[2:3, :] * two


def start_kernel(stage):
    send_ref, weight_ref = stage.out(0), stage.take(0)
    qkv_ref = stage.take(1)
    rows = qkv_ref.shape[1]
    order = row_order(rows)
    query, key, value = [qkv_ref[i].astype(F32) for i in range(3)]
    put_strip(own_rows(query), send_ref, rows)
    key_rows, value_rows = own_rows(key), own_rows(value)
    mixed = short_of(key, weight_ref[1]) * short_of(value, weight_ref[2])
    mixed, taps = mm(order, mixed.astype(BF16)), mm(order, stage.take(2)[...].astype(BF16))
    for tile in range(mixed.shape[1] // LANES):
        strips = pair(lane_tile(key_rows, tile), lane_tile(value_rows, tile))
        parts = pair(lane_tile(mixed, tile), lane_tile(taps, tile))
        for i in range(2):
            send_ref[2 * tile + i, :rows] = parts[i].astype(BF16)
            raw = send_ref[2 * tile + i, rows:].astype(F32)
            raw = jnp.concatenate([raw[:8], strips[i]], axis=0)
            send_ref[2 * tile + i, rows:] = raw.astype(BF16)


def partial_product(g, w_ref, mask):
    width = g.shape[1]
    w = w_ref[mask * width : (mask + 1) * width, :]
    return lax.dot_general(g, w, (((1,), (1,)), ((), ())), preferred_element_type=F32)


def first_product_kernel(stage):
    g, out_ref = stage.take(0)[...], stage.out(0)
    for i, mask in enumerate((1, 3)):
        out_ref[i] = partial_product(g, stage.take(1, i), mask).astype(BF16)


def second_product_kernel(stage):
    w_ref, g, near_ref = stage.take(1), stage.take(0)[...], stage.take(2)
    across_ref, own_ref = stage.out(0), stage.out(1)
    across = partial_product(g, w_ref, 2) + near_ref[1].astype(F32)
    across_ref[...] = across.astype(BF16)
    stage.give(0)
    own_ref[...] = partial_product(g, w_ref, 0) + near_ref[0].astype(F32)


def query_kernel(stage):
    weight_ref, qkv_ref, short_ref = stage.take(1), stage.take(0), stage.out(4)
    for i in range(3):
        short_ref[i] = short_of(qkv_ref[i].astype(F32), weight_ref[i])
    stage.give(4)
    stage.out(3)[...] = short_ref[0]


def sum_kernel(stage):
    send_ref, kept_ref = stage.out(0), stage.out(1)
    grad_gated = stage.take(0)[...] + stage.take(1)[...].astype(F32)
    kept_ref[...] = grad_gated
    stage.give(1)
    rows = grad_gated.shape[0]
    first = exact_rows(grad_gated[:2])
    put_strip(jnp.concatenate([jnp.zeros_like(first), first], axis=0), send_ref, rows // 2)
    put_rows(mm(row_order(rows), (grad_gated * stage.take(2)[...]).astype(BF16)), send_ref, 0)


def spread_phases(parts):
    (a_re, a_im), (b_re, b_im), (c_re, c_im), (d_re, d_im) = parts
    s_re, s_im, t_re, t_im = a_re + c_re, a_im + c_im, a_re - c_re, a_im - c_im
    u_re, u_im, v_re, v_im = b_re + d_re, b_im + d_im, b_re - d_re, b_im - d_im
    return [
        (s_re + u_re, s_im + u_im),
        (t_re + v_im, t_im - v_re),
        (s_re - u_re, s_im - u_im),
        (t_re - v_im, t_im + v_re),
    ]


def gather_phases(parts):
    (a_re, a_im), (b_re, b_im), (c_re, c_im), (d_re, d_im) = parts
    s_re, s_im, t_re, t_im = a_re + c_re, a_im + c_im, a_re - c_re, a_im - c_im
    u_re, u_im, v_re, v_im = b_re + d_re, b_im + d_im, b_re - d_re, b_im - d_im
    return [
        (s_re + u_re, s_im + u_im),
        (t_re - v_im, t_im + v_re),
        (s_re - u_re, s_im - u_im),
        (t_re + v_im, t_im - v_re),
    ]


def rows_of(ref, start, count):
    block = ref[:, start : start + count, :]
    return block.reshape(ref.shape[0] * count, ref.shape[2])


def turned_back(re, im, twist, phase):
    if phase == 0:
        return re, im
    c, s = twist[:, phase : phase + 1], twist[:, PHASES + phase : PHASES + phase + 1]
    return re * c + im * s, im * c - re * s


def turned_on(re, im, twist, phase):
    if phase == 0:
        return re, im
    c, s = twist[:, phase : phase + 1], twist[:, PHASES + phase : PHASES + phase + 1]
    return re * c - im * s, re * s + im * c


def lane_tile(x, index):
    return x[:, index * LANES : (index + 1) * LANES]


def causal(parts, weight):
    rows = lax.broadcasted_iota(jnp.int32, parts[0].shape, 0)
    two, three = [jnp.where(rows == 0, 0.0, pltpu.roll(parts[p], 1, 0)) for p in (2, 3)]
    once, twice = [three, *parts[:3]], [two, three, *parts[:2]]
    return [
        weight[0:1] * x + weight[1:2] * y + weight[2:3] * z for x, y, z in zip(parts, once, twice)
    ]


def anticausal(parts, weight):
    count = parts[0].shape[0]
    rows = lax.broadcasted_iota(jnp.int32, parts[0].shape, 0)
    zero, one = [
        jnp.where(rows == count - 1, 0.0, pltpu.roll(parts[p], count - 1, 0)) for p in (0, 1)
    ]
    once, twice = [*parts[1:], zero], [*parts[2:], zero, one]
    return [
        weight[0:1] * x + weight[1:2] * y + weight[2:3] * z for x, y, z in zip(parts, once, twice)
    ]


def halves(x):
    high = x.astype(BF16)
    return high, (x - high.astype(F32)).astype(BF16)


def twiddles(table_ref):
    terms = [table_ref[2, :, i * LANES : (i + 1) * LANES].astype(F32) for i in range(3)]
    return terms[0] + (terms[1] + terms[2])


def columns(parts):
    return jnp.concatenate(parts, axis=1)


def two_sides(table, x):
    quarter = table.shape[0]
    return [mm(table[:, :quarter], x), mm(table[:, quarter:], x)]


def spectrum_of(sides, twist):
    turned = []
    for phase, (re, im) in enumerate(sides):
        turned.append(turned_back(re, im, twist, phase))
    return spread_phases(turned)


def back_values(spectrum, twist):
    return [
        jnp.concatenate(turned_on(re, im, twist, phase), axis=0)
        for phase, (re, im) in enumerate(gather_phases(spectrum))
    ]


def own_weights(weight_ref, gain_ref):
    place = lax.axis_index("seq")
    lanes = pl.ds(pl.multiple_of(place // 2 * LANES, LANES), LANES)
    odd = place % 2 == 1

    def mine(x):
        return jnp.where(odd, swap(x), x)

    query, key, value = [mine(weight_ref[i, :, lanes]) for i in range(3)]
    gain = both(mine(gain_ref[:, lanes]))[0]
    return jnp.where(low_lanes(key.shape), key, swap(value)), query, gain


def first_mask(quarter, share):
    rows = lax.broadcasted_iota(jnp.int32, (quarter, LANES), 0) & (share - 1)
    return (rows == 0) & low_lanes((quarter, LANES))


def spread_first(groups, index, share):
    x = groups.reshape(groups.shape[0] // 8, 8, LANES)[:, index : index + 1, :]
    return jnp.broadcast_to(x, (x.shape[0], share, LANES)).reshape(x.shape[0] * share, LANES)


def gather_first(parts, share):
    tops = []
    for x in parts:
        tops.append(
            jnp.concatenate([x[at : at + 8] for at in range(0, x.shape[0], share)], axis=0)
        )
    return jnp.where(group_rows(tops[0]) == 0, tops[0], pltpu.roll(tops[1], 1, 0))


def forward_kernel(stage):
    recv_ref, weight_ref, gain_ref = [stage.take(i) for i in range(3)]
    send_ref, saved_ref = stage.out(0), stage.out(1)
    blocks = recv_ref.shape[0]
    rows = recv_ref.shape[1] - STRIP
    share = rows // PHASES
    quarter = blocks * share
    low, starting = low_lanes((quarter, LANES)), first_mask(quarter, share)
    pair_weight, query_weight, gain = own_weights(weight_ref, gain_ref)
    query = first_rows(strip_groups(recv_ref, rows, 0), query_weight)
    pairs = first_rows(strip_groups(recv_ref, rows, 1), pair_weight)
    saved_ref[10, 8:9, :] = gain
    saved_ref[10, 64 : 64 + 8 * blocks, :] = query
    saved_ref[10, 128 : 128 + 8 * blocks, :] = pairs
    strip = exact_groups(query, pairs)
    fixed = pairs * swap(pairs)

    starts = [phase * share for phase in range(PHASES)]
    x = [rows_of(recv_ref, at, share).astype(F32) for at in starts]
    for i in range(2):
        x[i] = jnp.where(starting, spread_first(fixed, i, share), x[i])
    high = columns([y.astype(BF16) for y in x])
    fh, fl = stage.take(3)[0], stage.take(3)[1]
    twist = twiddles(stage.take(3))
    main = [y + z for y, z in zip(two_sides(fh, high), two_sides(fl, high))]
    sides = [[lane_tile(y, phase) for y in main] for phase in range(PHASES)]
    product = []
    for r, (re, im) in enumerate(spectrum_of(sides, twist)):
        saved_ref[2 * r] = re
        saved_ref[2 * r + 1] = im
        other_re, other_im = swap(re), swap(im)
        product.append((re * other_re - im * other_im, re * other_im + im * other_re))

    values = back_values(product, twist)
    bh, bl = stage.take(4)[0], stage.take(4)[1]
    wide = low_lanes((2 * quarter, LANES))
    high = [y.astype(BF16) for y in values]
    wider = [y.astype(F32) for y in high]
    both_parts = [jnp.where(wide, z, y - z).astype(BF16) for y, z in zip(values, wider)]
    high = [jnp.where(wide, wider[i], wider[i + 2]).astype(BF16) for i in range(2)]
    main, more = mm(bh, columns(both_parts)), mm(bl, columns(high))
    grad_ref = stage.take(5)
    send_ref[:, rows // 2 : rows, :] = grad_ref[:, : rows // 2, :]
    send_ref[:, rows:, :] = strip + grad_ref[:, rows // 2 :, :]
    stage.give(0, 1)
    summed = [y + swap(y) for y in (lane_tile(main, phase) for phase in range(PHASES))]
    for i in range(2):
        conv = jnp.where(low, summed[i], summed[i + 2]) + lane_tile(more, i)
        long_out = conv + gain * jnp.where(low, x[i], swap(x[i + 2]))
        saved_ref[8 + i] = long_out
        long_out = long_out.astype(BF16).reshape(blocks, share, LANES)
        send_ref[:, starts[i] : starts[i] + share, :] = long_out


def backward_kernel(stage):
    grad_ref, saved_ref, send_ref = stage.take(0), stage.take(1), stage.out(0)
    blocks = grad_ref.shape[0]
    rows = grad_ref.shape[1] - STRIP
    share = rows // PHASES
    quarter = blocks * share
    low, starting = low_lanes((quarter, LANES)), first_mask(quarter, share)
    gain, groups = saved_ref[10, 8:9, :], 8 * blocks
    query, pairs = [saved_ref[10, at : at + groups, :] for at in (64, 128)]
    strip = strip_groups(grad_ref, rows, 0)
    first = earlier(strip, 4) + earlier(strip, 6)
    fixed = first * query
    starts = [phase * share for phase in range(PHASES)]
    grad_long = []
    for i, at in enumerate(starts[2:]):
        packed = rows_of(grad_ref, at, share).astype(F32)
        grad_long.append(jnp.where(starting, spread_first(fixed, i, share), packed))

    fh, fl = stage.take(2)[0], stage.take(2)[1]
    twist = twiddles(stage.take(2))
    high, rest = halves(columns(grad_long))
    three = zip(two_sides(fh, high), two_sides(fl, high), two_sides(fh, rest))
    main = [x + y + z for x, y, z in three]
    sides = []
    for phase in range(PHASES):
        sides.append([both(lane_tile(x, phase % 2))[phase // 2] for x in main])
    product = []
    for r, (re, im) in enumerate(spectrum_of(sides, twist)):
        k_re, k_im = saved_ref[2 * r], saved_ref[2 * r + 1]
        product.append((k_re * re + k_im * im, k_re * im - k_im * re))
    high, rest = halves(columns(back_values(product, twist)))
    gate(grad_ref, stage.take(3)[0], *[stage.out(i) for i in (1, 2, 3)])
    stage.give(2)
    stage.give(3)
    bh, bl = stage.take(4)[0], stage.take(4)[1]
    times = mm(bh, high) + mm(bl, high) + mm(bh, rest)

    scale = 1.0 / math.sqrt(PHASES * quarter)
    grad_long = [swap(x) for x in grad_long] + grad_long
    grads = []
    for phase, at in enumerate(starts):
        x = lane_tile(times, phase)
        grads.append(jnp.where(low, x * scale, x + gain * grad_long[phase]))
        send_ref[:, at : at + share, :] = grads[-1].astype(BF16).reshape(blocks, share, LANES)
    stage.give(0, 0)
    query_head = first * gather_first([saved_ref[8], saved_ref[9]], share)
    pair_head = both(gather_first(grads[:2], share))[1] * swap(pairs)
    heads = []
    for x in (query_head, pair_head):
        heads.append(jnp.concatenate([x[8:], jnp.zeros((8, LANES), F32)], axis=0))
    send_ref[:, rows:, :] = exact_groups(*heads)


def unpacked(ref, at, half, order):
    tiles = []
    for tile in range(ref.shape[0] // 2):
        x, y = [ref[2 * tile + i, at : at + half].astype(F32) for i in range(2)]
        top, bottom = pair(x, y)
        tiles.append(jnp.concatenate([top, bottom], axis=0))
    return mm(order, jnp.concatenate(tiles, axis=1).astype(BF16))


def pair_strip_of(ref, at):
    sides = [[], []]
    for tile in range(ref.shape[0] // 2):
        x, y = [ref[2 * tile + i, at : at + STRIP].astype(F32)[8:] for i in range(2)]
        for side, z in zip(sides, pair(x, y)):
            side.append(z)
    return [columns(side) for side in sides]


def gate(recv_ref, query, gated_ref, long_ref, tops_ref):
    rows = recv_ref.shape[1] - STRIP
    key, value = [x[0:2] + x[2:4] for x in pair_strip_of(recv_ref, rows)]
    tops_ref[...] = jnp.concatenate([key, value, key, value], axis=0)
    long_out = unpacked(recv_ref, 0, rows // 2, row_order(rows, back=True))
    long_ref[...] = long_out
    gated_ref[...] = (query * long_out).astype(BF16)
    strip = strip_of(recv_ref, rows)
    first = strip + earlier(strip, 2)
    row = lax.broadcasted_iota(jnp.int32, first.shape, 0)
    first = jnp.where(row < 2, first, query[:STRIP])
    gated_ref[:STRIP, :] = (first * long_out[:STRIP]).astype(BF16)


def output_kernel(parts, stage):
    w_ref, total = stage.take(0), None
    for part in range(parts):
        gated = stage.take(1 + part)[...]
        width = gated.shape[1]
        term = mm(gated, w_ref[part * width : (part + 1) * width, :])
        total = term if total is None else total + term
    stage.out(0)[...] = total.astype(BF16)


def end_kernel(stage):
    recv_ref, grad_ref, filter_ref = stage.take(0), stage.out(0), stage.out(1)
    rows = filter_ref.shape[0]
    order = row_order(rows, back=True)
    sides = [[], []]
    for tile in range(recv_ref.shape[0] // 2):
        x, y = [recv_ref[2 * tile + i, :rows].astype(F32) for i in range(2)]
        for side, z in zip(sides, pair(x, y)):
            side.append(z.astype(BF16))
    taps, mixed = [mm(order, columns(side)) for side in sides]
    filter_ref[...] = taps
    stage.give(1)
    weight_ref, tops, short_ref = stage.take(1), stage.take(2)[...], stage.take(3)
    row = lax.broadcasted_iota(jnp.int32, mixed.shape, 0)
    heads = [x[0:2] + x[2:4] for x in pair_strip_of(recv_ref, rows)]
    for i in range(2):
        top = tops[2 - 2 * i : 4 - 2 * i]
        other = jnp.where(row == 0, top[0:1], jnp.where(row == 1, top[1:2], short_ref[1 - i]))
        grad_ref[i] = adjoint_of(mixed * other, heads[i], weight_ref[1 + i]).astype(BF16)
    stage.give(0, 0)
    strip = strip_of(recv_ref, rows)
    head = strip[0:2] + strip[2:4]
    grad_query = stage.take(4)[...] * stage.take(5)[...]
    grad_ref[2] = adjoint_of(grad_query, head, weight_ref[0]).astype(BF16)


def partner(x, axis, mask):
    return lax.ppermute(x, axis, [(i, i ^ mask) for i in range(lax.axis_size(axis))])


def exchanged(x, axis):
    return lax.all_to_all(x, axis, split_axis=0, concat_axis=0, tiled=True)


def owner_layer(qkv, filt, skip_gain, short_weight, w_out, g_out):
    shape = jax.ShapeDtypeStruct
    seq_parts, ch_parts = lax.axis_size("seq"), lax.axis_size("ch")
    rows, width = qkv.shape[1], qkv.shape[2]
    tokens = seq_parts * rows
    quarter = tokens // PHASES
    tables = jnp.asarray(phase_tables(tokens))
    table_flops = 2 * 2 * 2 * 3 * tokens * tokens // PHASES * LANES
    product_flops = 2 * rows * width * width * ch_parts
    half = rows // 2
    wide = shape((seq_parts, rows + STRIP, LANES), BF16)
    column = shape((rows, width), BF16)
    saved = shape((11, quarter, LANES), F32)
    gain = skip_gain[None, :]

    (send,) = call(start_kernel, [Far(wide)], Far(short_weight), Far(qkv), Far(filt))
    recv = exchanged(send, "seq")
    half_sums, w_kept, g_kept = call(
        first_product_kernel,
        [
            Near(shape((2, rows, width), BF16), kept=True),
            Near(w_out, kept=True),
            Near(g_out, kept=True),
        ],
        Far(g_out, into=2),
        Far(w_out, turned=(1, 3, 2, 0), into=1),
        flops=product_flops // 2,
    )
    half_sums = partner(half_sums, "ch", 1)
    across, own = call(
        second_product_kernel,
        [Near(column, kept=True), Near(shape((rows, width), F32), kept=True)],
        Near(g_kept),
        Near(w_kept),
        Near(half_sums),
        flops=product_flops // 2,
    )
    across = partner(across, "ch", 2)
    def pinned(x):
        return Near(x, kept=True)

    tables_back = Far(tables, [(2, 2)])
    exact = shape((rows, width), F32)
    tables_on, weight, gain, query, short = call(
        query_kernel,
        [
            pinned(shape((3, *tables.shape[1:]), BF16)),
            pinned(short_weight),
            pinned(gain),
            pinned(exact),
            Far(shape((3, rows, width), F32)),
        ],
        Far(qkv),
        Far(short_weight, into=1),
        Far(tables, [(0, 2), (4, 1)], into=0),
        Far(gain, into=2),
    )
    grad_long, grad_far = call(
        sum_kernel,
        [Far(shape((seq_parts, half + STRIP, LANES), BF16)), Far(exact)],
        Near(own),
        Near(across),
        Near(query),
    )
    send, saved = call(
        forward_kernel,
        [
            Far(wide, [(0, half), (half, half + STRIP)], axis=1),
            pinned(saved),
        ],
        pinned(recv),
        Near(weight),
        Near(gain),
        Near(tables_on),
        tables_back,
        Far(grad_long),
        flops=table_flops,
    )
    swapped = exchanged(send, "seq")
    send, gated, long_out, tops = call(
        backward_kernel,
        [
            Far(wide, [(0, rows), (rows, STRIP)], axis=1),
            pinned(column),
            Far(exact),
            Far(shape((8, width), F32)),
        ],
        Near(swapped),
        Near(saved),
        Near(tables_on),
        Far(short, [(0, 1)]),
        tables_back,
        flops=table_flops,
    )
    grad_recv = exchanged(send, "seq")
    across = partner(gated, "ch", 2)
    near, far = partner(gated, "ch", 1), partner(across, "ch", 1)
    (output,) = call(
        functools.partial(output_kernel, ch_parts),
        [Far(column)],
        Near(w_kept),
        Near(gated),
        Near(near),
        Near(across),
        Near(far),
        flops=product_flops,
    )
    grad_qkv, grad_filter = call(
        end_kernel,
        [Far(shape((3, rows, width), BF16), [(1, 2), (0, 1)]), Far(exact)],
        Near(grad_recv),
        Far(short_weight),
        Far(tops),
        Far(short, [(1, 2)]),
        Far(long_out),
        Far(grad_far),
    )
    return (output, grad_qkv, grad_filter)


def local(qkv, filt, skip_gain, short_weight, w_out, g_out):
    seq_parts = lax.axis_size("seq")
    rows, width = qkv.shape[1], qkv.shape[2]
    fits = width == HALF * seq_parts and rows % HALF == 0 and rows & (rows - 1) == 0 and rows * seq_parts <= 2048
    if fits and lax.axis_size("ch") == 4:
        return owner_layer(qkv, filt, skip_gain, short_weight, w_out, g_out)
    return spread_layer(qkv, filt, skip_gain, short_weight, w_out, g_out)


def solution(mesh):
    in_specs = (
        P(None, "seq", "ch"),
        P("seq", "ch"),
        P("ch"),
        P(None, None, "ch"),
        P(None, "ch"),
        P("seq", "ch"),
    )
    out_specs = (P("seq", "ch"), P(None, "seq", "ch"), P("seq", "ch"))
    return jax.shard_map(local, mesh=mesh, in_specs=in_specs, out_specs=out_specs, check_vma=False)
```

```python
import functools
import math

import jax
import jax.numpy as jnp
import numpy as np
from jax import lax
from jax.experimental import pallas as pl
from jax.experimental.pallas import tpu as pltpu
from jax.sharding import PartitionSpec as P

HIGHEST = lax.Precision.HIGHEST
TWO_PI = 2.0 * math.pi
LANES = 128
HALF = 64
PHASES = 4
STRIP = 16
BF16 = jnp.bfloat16
F32 = jnp.float32
VMEM_LIMIT = 24 * 1024 * 1024


def passed_along(block, axis, distance):
    devices = range(lax.axis_size(axis))
    route = [(i - distance, i) for i in devices if i - distance in devices]
    return lax.ppermute(block, axis, route)


def phase_pair(left_count, right_count, period, left_start, right_start):
    left_idx = lax.broadcasted_iota(jnp.int32, (left_count, right_count), 0) + left_start
    right_idx = lax.broadcasted_iota(jnp.int32, (left_count, right_count), 1) + right_start
    angle_all = (left_idx * right_idx % period).astype(jnp.float32) * (TWO_PI / period)
    return (jnp.cos(angle_all), jnp.sin(angle_all))


def contract(pattern, matrix, values):
    return jnp.einsum(
        pattern, matrix, values, precision=HIGHEST, preferred_element_type=jnp.float32
    )


def forward_spectrum(signal):
    seq_parts = lax.axis_size("seq")
    row_count = signal.shape[0]
    row_share = row_count // seq_parts
    period = 2 * seq_parts * row_count
    spread_in = lax.all_to_all(signal[None], "seq", split_axis=1, concat_axis=0, tiled=True)
    outer_cos, outer_sin = phase_pair(2 * seq_parts, seq_parts, 2 * seq_parts, 0, 0)
    section_re = contract("cp,prw->crw", outer_cos, spread_in)
    section_im = -contract("cp,prw->crw", outer_sin, spread_in)
    twist_cos, twist_sin = phase_pair(
        2 * seq_parts, row_share, period, 0, lax.axis_index("seq") * row_share
    )
    twist_cos = twist_cos[:, :, None]
    twist_sin = twist_sin[:, :, None]
    turned_re = section_re * twist_cos + section_im * twist_sin
    turned_im = section_im * twist_cos - section_re * twist_sin
    inner_cos, inner_sin = phase_pair(row_count, row_count, row_count, 0, 0)
    piece_re = lax.all_to_all(turned_re, "seq", split_axis=0, concat_axis=1, tiled=True)
    piece_im = lax.all_to_all(turned_im, "seq", split_axis=0, concat_axis=1, tiled=True)
    spec_re = contract("dm,cmk->cdk", inner_cos, piece_re) + contract(
        "dm,cmk->cdk", inner_sin, piece_im
    )
    spec_im = contract("dm,cmk->cdk", inner_cos, piece_im) - contract(
        "dm,cmk->cdk", inner_sin, piece_re
    )
    return (spec_re, spec_im)


def time_signal(spec_re, spec_im):
    seq_parts = lax.axis_size("seq")
    row_count = spec_re.shape[1]
    period = 2 * seq_parts * row_count
    inner_cos, inner_sin = phase_pair(row_count, row_count, row_count, 0, 0)
    back_re = contract("md,cdk->cmk", inner_cos, spec_re) - contract(
        "md,cdk->cmk", inner_sin, spec_im
    )
    back_im = contract("md,cdk->cmk", inner_cos, spec_im) + contract(
        "md,cdk->cmk", inner_sin, spec_re
    )
    twist_cos, twist_sin = phase_pair(2, row_count, period, 2 * lax.axis_index("seq"), 0)
    twist_cos = twist_cos[:, :, None]
    twist_sin = twist_sin[:, :, None]
    turned_re = back_re * twist_cos - back_im * twist_sin
    turned_im = back_im * twist_cos + back_re * twist_sin
    outer_cos, outer_sin = phase_pair(seq_parts, 2 * seq_parts, 2 * seq_parts, 0, 0)
    piece_re = lax.all_to_all(turned_re, "seq", split_axis=1, concat_axis=0, tiled=True)
    piece_im = lax.all_to_all(turned_im, "seq", split_axis=1, concat_axis=0, tiled=True)
    summed = contract("pc,crk->prk", outer_cos, piece_re) - contract(
        "pc,crk->prk", outer_sin, piece_im
    )
    returned = summed * (1.0 / period)
    return lax.all_to_all(returned, "seq", split_axis=0, concat_axis=1, tiled=True)[0]


def spread_layer(qkv, filt, skip_gain, short_weight, w_out, g_out):
    row_count = qkv.shape[1]
    slab_width = qkv.shape[2]
    tail_rows = passed_along(qkv[:, row_count - 2 :, :], "seq", 1)
    extended = jnp.concatenate([tail_rows, qkv], axis=1)
    short = (
        short_weight[:, 0, None, :] * extended[:, 2:, :]
        + short_weight[:, 1, None, :] * extended[:, 1:-1, :]
        + short_weight[:, 2, None, :] * extended[:, :-2, :]
    )
    query_gate = short[0]
    key_short = short[1]
    value_short = short[2]
    mixed = key_short * value_short
    both_re, both_im = forward_spectrum(jnp.concatenate([mixed, filt], axis=1))
    signal_re = both_re[:, :, :slab_width]
    signal_im = both_im[:, :, :slab_width]
    kernel_re = both_re[:, :, slab_width:]
    kernel_im = both_im[:, :, slab_width:]
    conv_out = time_signal(
        signal_re * kernel_re - signal_im * kernel_im, signal_re * kernel_im + signal_im * kernel_re
    )
    long_out = conv_out + skip_gain * mixed
    gated_out = (query_gate * long_out).astype(jnp.bfloat16)
    projected = jnp.dot(
        lax.all_gather(gated_out, "ch", axis=1, tiled=True),
        w_out,
        preferred_element_type=jnp.float32,
    )
    output = projected.astype(jnp.bfloat16)
    grad_all = lax.all_gather(g_out, "ch", axis=1, tiled=True)
    rows_all = lax.all_to_all(w_out, "ch", split_axis=0, concat_axis=1, tiled=True)
    grad_gated = lax.dot_general(
        grad_all, rows_all, (((1,), (1,)), ((), ())), preferred_element_type=jnp.float32
    )
    grad_long = grad_gated * query_gate
    grad_query = grad_gated * long_out
    grad_re, grad_im = forward_spectrum(grad_long)
    pair_re = jnp.concatenate(
        [kernel_re * grad_re + kernel_im * grad_im, signal_re * grad_re + signal_im * grad_im],
        axis=2,
    )
    pair_im = jnp.concatenate(
        [kernel_re * grad_im - kernel_im * grad_re, signal_re * grad_im - signal_im * grad_re],
        axis=2,
    )
    pair_time = time_signal(pair_re, pair_im)
    grad_mixed = pair_time[:, :slab_width] + skip_gain * grad_long
    token_total = lax.axis_size("seq") * row_count
    grad_filter = pair_time[:, slab_width:] * (1.0 / math.sqrt(token_total))
    grad_short = jnp.stack([grad_query, grad_mixed * value_short, grad_mixed * key_short])
    head_rows = passed_along(grad_short[:, :2, :], "seq", -1)
    extended_grad = jnp.concatenate([grad_short, head_rows], axis=1)
    grad_qkv = (
        short_weight[:, 0, None, :] * extended_grad[:, :-2, :]
        + short_weight[:, 1, None, :] * extended_grad[:, 1:-1, :]
        + short_weight[:, 2, None, :] * extended_grad[:, 2:, :]
    ).astype(jnp.bfloat16)
    return (output, grad_qkv, grad_filter)


def split_bf16(values):
    high = values.astype(np.float32).astype(jnp.bfloat16)
    low = (values - high.astype(np.float64)).astype(np.float32).astype(jnp.bfloat16)
    return high, low


def phase_tables(tokens):
    quarter = tokens // PHASES
    freq = 2 * np.arange(quarter)[:, None] + 1
    turn = math.pi / (2 * tokens)
    angle = (freq * PHASES * np.arange(quarter)[None, :] % (4 * tokens)) * turn
    forward = np.concatenate([np.cos(angle), -np.sin(angle)], axis=1)
    backward = np.concatenate([np.cos(angle).T, -np.sin(angle).T], axis=1) / tokens
    angle = freq * np.arange(PHASES)[None, :] * turn
    twist = np.concatenate([np.cos(angle), np.sin(angle)], axis=1)
    twist = np.pad(twist, ((0, 0), (0, LANES - 2 * PHASES)))
    high, rest = split_bf16(twist)
    last = split_bf16(twist - high.astype(np.float64) - rest.astype(np.float64))[0]
    tables = np.zeros((8, quarter, 2 * quarter), jnp.bfloat16)
    tables[0], tables[1] = split_bf16(forward)
    tables[2], tables[3] = split_bf16(backward)
    for i, term in enumerate((high, rest, last)):
        tables[4, :, i * LANES : (i + 1) * LANES] = term
    return tables


def row_order(rows, back=False):
    to, at = [lax.broadcasted_iota(jnp.int32, (rows, rows), int(i != back)) for i in range(2)]
    share = rows // PHASES
    wanted = (to & (share - 1)) * PHASES + lax.shift_right_logical(to, share.bit_length() - 1)
    return jnp.where(wanted == at, 1.0, 0.0).astype(BF16)


def mm(a, b):
    return lax.dot_general(a, b, (((1,), (0,)), ((), ())), preferred_element_type=F32)


def low_lanes(shape):
    return lax.broadcasted_iota(jnp.int32, shape, 1) < HALF


def swap(x):
    return pltpu.roll(x, HALF, 1)


class Near:
    def __init__(self, array, kept=False):
        self.array = array
        self.kept = kept


class Far:
    def __init__(self, array, cuts=None, turned=(), into=None, axis=0):
        self.array = array
        self.turned = turned
        self.into = into
        self.axis = axis
        if turned:
            step = array.shape[0] // len(turned)
            cuts = [(mask * step, step) for mask in turned]
        self.cuts = cuts or [(0, array.shape[axis])]
        self.shape = list(array.shape)
        self.shape[axis] = sum(count for _, count in self.cuts)


class Stage:
    def __init__(self, items, count_in, refs):
        arrays, scratch = list(refs[: len(items)]), list(refs[len(items) :])
        sems = scratch.pop()
        self.count_in = count_in
        self.held, self.copies, self.waiting = [], [], []
        used = 0
        for i, (item, array) in enumerate(zip(items, arrays)):
            group = []
            if isinstance(item, Near):
                self.held.append(array)
            else:
                held = scratch.pop(0) if item.into is None else arrays[count_in + item.into]
                self.held.append(held)
                at = 0
                for cut, (start, count) in enumerate(item.cuts):
                    lead = (slice(None),) * item.axis
                    there = held.at[(*lead, pl.ds(start if item.turned else at, count))]
                    at += count
                    if item.turned:
                        mask = item.turned[cut]
                        start = pl.multiple_of((lax.axis_index("ch") ^ mask) * count, count)
                    here = array.at[(*lead, pl.ds(start, count))]
                    if i >= count_in:
                        here, there = there, here
                    group.append(pltpu.make_async_copy(here, there, sems.at[used]))
                    used += 1
            self.copies.append(group)
            self.waiting.append(set(range(len(group))))
        self.given = set()

    def bring(self, index):
        for copy in self.copies[index]:
            copy.start()

    def take(self, index, cut=None):
        for i in sorted(self.waiting[index]):
            if cut is None or cut == i:
                self.copies[index][i].wait()
                self.waiting[index].discard(i)
        return self.held[index]

    def out(self, index):
        return self.held[self.count_in + index]

    def give(self, index, cut=None):
        for i, copy in enumerate(self.copies[self.count_in + index]):
            if (index, i) not in self.given and cut in (None, i):
                copy.start()
                self.given.add((index, i))


def staged(kernel, items, count_in, *refs):
    stage = Stage(items, count_in, refs)
    for i in range(count_in):
        stage.bring(i)
    kernel(stage)
    for i in range(count_in):
        stage.take(i)
    for i in range(len(items) - count_in):
        stage.give(i)
    for i in range(len(items) - count_in):
        stage.take(count_in + i)


def operand_of(x):
    if isinstance(x, Near) and not x.kept:
        return x.array
    space = pltpu.VMEM if isinstance(x, Near) else pltpu.HBM
    return pltpu.with_memory_space_constraint(x.array, space)


def result_of(x):
    make = pltpu.HBM if isinstance(x, Far) else pltpu.VMEM if x.kept else jax.ShapeDtypeStruct
    return make(x.array.shape, x.array.dtype)


def call(kernel, results, *args, flops=0):
    items = list(args) + list(results)
    specs, scratch, used = [], [], 0
    for item in items:
        near = isinstance(item, Near)
        specs.append(pl.BlockSpec(memory_space=pltpu.VMEM if near else pltpu.HBM))
        if not near:
            used += len(item.cuts)
            if item.into is None:
                scratch.append(pltpu.VMEM(tuple(item.shape), item.array.dtype))
    moved = sum(math.prod(x.array.shape) * x.array.dtype.itemsize for x in items)
    return pl.pallas_call(
        functools.partial(staged, kernel, items, len(args)),
        out_shape=[result_of(x) for x in results],
        in_specs=specs[: len(args)],
        out_specs=specs[len(args) :],
        scratch_shapes=scratch + [pltpu.SemaphoreType.DMA((max(used, 1),))],
        compiler_params=pltpu.CompilerParams(vmem_limit_bytes=VMEM_LIMIT),
        cost_estimate=pl.CostEstimate(flops=flops, bytes_accessed=moved, transcendentals=0),
    )(*[operand_of(x) for x in args])


def lane_tile(x, index):
    return x[:, index * LANES : (index + 1) * LANES]


def pair(first, second):
    low = low_lanes(first.shape)
    return jnp.where(low, first, swap(second)), jnp.where(low, swap(first), second)


def both(x):
    turned, low = swap(x), low_lanes(x.shape)
    return jnp.where(low, x, turned), jnp.where(low, turned, x)


def shifted(x, before):
    rows = lax.broadcasted_iota(jnp.int32, x.shape, 0)
    last, first = before[1:2, :], before[0:1, :]
    one = jnp.where(rows == 0, last, pltpu.roll(x, 1, 0))
    two = jnp.where(rows == 0, first, jnp.where(rows == 1, last, pltpu.roll(x, 2, 0)))
    return one, two


def advanced(x, after):
    count = x.shape[0]
    rows = lax.broadcasted_iota(jnp.int32, x.shape, 0)
    first, last = after[0:1, :], after[1:2, :]
    one = jnp.where(rows == count - 1, first, pltpu.roll(x, count - 1, 0))
    two = jnp.where(
        rows == count - 1, last, jnp.where(rows == count - 2, first, pltpu.roll(x, count - 2, 0))
    )
    return one, two


def put_rows(x, send_ref, at):
    half = x.shape[0] // 2
    for tile in range(x.shape[1] // LANES):
        t = lane_tile(x, tile)
        first, second = pair(t[:half], t[half:])
        send_ref[2 * tile, at : at + half] = first.astype(BF16)
        send_ref[2 * tile + 1, at : at + half] = second.astype(BF16)


def put_strip(x, send_ref, at):
    x = jnp.concatenate([x, jnp.zeros((STRIP - x.shape[0], x.shape[1]), F32)], axis=0)
    for tile in range(x.shape[1] // LANES):
        t = lane_tile(x, tile)
        send_ref[2 * tile, at : at + STRIP] = t.astype(BF16)
        send_ref[2 * tile + 1, at : at + STRIP] = swap(t).astype(BF16)


def strip_of(ref, at):
    tiles = []
    for tile in range(ref.shape[0] // 2):
        x, y = [ref[2 * tile + i, at : at + STRIP].astype(F32) for i in range(2)]
        tiles.append(jnp.where(low_lanes(x.shape), x, swap(y)))
    return jnp.concatenate(tiles, axis=1)


def exact_rows(x):
    high = x.astype(BF16).astype(F32)
    return jnp.concatenate([high, x - high], axis=0)


def group_rows(x):
    return lax.broadcasted_iota(jnp.int32, x.shape, 0) & 7


def earlier(x, count):
    return pltpu.roll(x, x.shape[0] - count, 0)


def strip_groups(ref, at, half):
    x = ref[:, at : at + STRIP, :].astype(F32)[:, 8 * half : 8 * half + 8, :]
    return x.reshape(8 * ref.shape[0], LANES)


def exact_groups(*halves):
    strips = []
    for x in halves:
        x = jnp.where(group_rows(x) < 2, x, 0.0)
        high = x.astype(BF16).astype(F32)
        strips.append((high + pltpu.roll(x - high, 2, 0)).reshape(x.shape[0] // 8, 8, LANES))
    return jnp.concatenate(strips, axis=1).astype(BF16)


def own_rows(x):
    none, last = jnp.zeros_like(x[:1]), x[x.shape[0] - 1 :]
    return jnp.concatenate([x[:2], none, x[:1], last, none, x[x.shape[0] - 2 :]], axis=0)


def first_rows(groups, weight):
    last = jnp.concatenate([jnp.zeros((8, LANES), F32), groups[: groups.shape[0] - 8]], axis=0)
    return (
        weight[0:1] * groups
        + weight[1:2] * (earlier(groups, 2) + earlier(last, 4))
        + weight[2:3] * earlier(last, 6)
    )


def short_of(x, weight):
    one, two = shifted(x, jnp.zeros((2, x.shape[1]), F32))
    return weight[0:1, :] * x + weight[1:2, :] * one + weight[2:3, :] * two


def adjoint_of(x, after, weight):
    one, two = advanced(x, after)
    return weight[0:1, :] * x + weight[1:2, :] * one + weight[2:3, :] * two


def start_kernel(stage):
    send_ref, weight_ref = stage.out(0), stage.take(0)
    qkv_ref = stage.take(1)
    rows = qkv_ref.shape[1]
    order = row_order(rows)
    query, key, value = [qkv_ref[i].astype(F32) for i in range(3)]
    put_strip(own_rows(query), send_ref, rows)
    key_rows, value_rows = own_rows(key), own_rows(value)
    mixed = short_of(key, weight_ref[1]) * short_of(value, weight_ref[2])
    mixed, taps = mm(order, mixed.astype(BF16)), mm(order, stage.take(2)[...].astype(BF16))
    for tile in range(mixed.shape[1] // LANES):
        strips = pair(lane_tile(key_rows, tile), lane_tile(value_rows, tile))
        parts = pair(lane_tile(mixed, tile), lane_tile(taps, tile))
        for i in range(2):
            send_ref[2 * tile + i, :rows] = parts[i].astype(BF16)
            raw = send_ref[2 * tile + i, rows:].astype(F32)
            raw = jnp.concatenate([raw[:8], strips[i]], axis=0)
            send_ref[2 * tile + i, rows:] = raw.astype(BF16)


def partial_product(g, w_ref, mask):
    width = g.shape[1]
    w = w_ref[mask * width : (mask + 1) * width, :]
    return lax.dot_general(g, w, (((1,), (1,)), ((), ())), preferred_element_type=F32)


def first_product_kernel(stage):
    g, out_ref = stage.take(0)[...], stage.out(0)
    for i, mask in enumerate((1, 3)):
        out_ref[i] = partial_product(g, stage.take(1, i), mask).astype(BF16)


def second_product_kernel(stage):
    w_ref, g, near_ref = stage.take(1), stage.take(0)[...], stage.take(2)
    across_ref, own_ref = stage.out(0), stage.out(1)
    across = partial_product(g, w_ref, 2) + near_ref[1].astype(F32)
    across_ref[...] = across.astype(BF16)
    stage.give(0)
    own_ref[...] = partial_product(g, w_ref, 0) + near_ref[0].astype(F32)


def query_kernel(stage):
    weight_ref, qkv_ref, short_ref = stage.take(1), stage.take(0), stage.out(4)
    for i in range(3):
        short_ref[i] = short_of(qkv_ref[i].astype(F32), weight_ref[i])
    stage.give(4)
    stage.out(3)[...] = short_ref[0]


def sum_kernel(stage):
    send_ref, kept_ref = stage.out(0), stage.out(1)
    grad_gated = stage.take(0)[...] + stage.take(1)[...].astype(F32)
    kept_ref[...] = grad_gated
    stage.give(1)
    rows = grad_gated.shape[0]
    first = exact_rows(grad_gated[:2])
    put_strip(jnp.concatenate([jnp.zeros_like(first), first], axis=0), send_ref, rows // 2)
    put_rows(mm(row_order(rows), (grad_gated * stage.take(2)[...]).astype(BF16)), send_ref, 0)


def spread_phases(parts):
    (a_re, a_im), (b_re, b_im), (c_re, c_im), (d_re, d_im) = parts
    s_re, s_im, t_re, t_im = a_re + c_re, a_im + c_im, a_re - c_re, a_im - c_im
    u_re, u_im, v_re, v_im = b_re + d_re, b_im + d_im, b_re - d_re, b_im - d_im
    return [
        (s_re + u_re, s_im + u_im),
        (t_re + v_im, t_im - v_re),
        (s_re - u_re, s_im - u_im),
        (t_re - v_im, t_im + v_re),
    ]


def gather_phases(parts):
    (a_re, a_im), (b_re, b_im), (c_re, c_im), (d_re, d_im) = parts
    s_re, s_im, t_re, t_im = a_re + c_re, a_im + c_im, a_re - c_re, a_im - c_im
    u_re, u_im, v_re, v_im = b_re + d_re, b_im + d_im, b_re - d_re, b_im - d_im
    return [
        (s_re + u_re, s_im + u_im),
        (t_re - v_im, t_im + v_re),
        (s_re - u_re, s_im - u_im),
        (t_re + v_im, t_im - v_re),
    ]


def rows_of(ref, start, count):
    block = ref[:, start : start + count, :]
    return block.reshape(ref.shape[0] * count, ref.shape[2])


def turned_back(re, im, twist, phase):
    if phase == 0:
        return re, im
    c, s = twist[:, phase : phase + 1], twist[:, PHASES + phase : PHASES + phase + 1]
    return re * c + im * s, im * c - re * s


def turned_on(re, im, twist, phase):
    if phase == 0:
        return re, im
    c, s = twist[:, phase : phase + 1], twist[:, PHASES + phase : PHASES + phase + 1]
    return re * c - im * s, re * s + im * c


def lane_tile(x, index):
    return x[:, index * LANES : (index + 1) * LANES]


def causal(parts, weight):
    rows = lax.broadcasted_iota(jnp.int32, parts[0].shape, 0)
    two, three = [jnp.where(rows == 0, 0.0, pltpu.roll(parts[p], 1, 0)) for p in (2, 3)]
    once, twice = [three, *parts[:3]], [two, three, *parts[:2]]
    return [
        weight[0:1] * x + weight[1:2] * y + weight[2:3] * z for x, y, z in zip(parts, once, twice)
    ]


def anticausal(parts, weight):
    count = parts[0].shape[0]
    rows = lax.broadcasted_iota(jnp.int32, parts[0].shape, 0)
    zero, one = [
        jnp.where(rows == count - 1, 0.0, pltpu.roll(parts[p], count - 1, 0)) for p in (0, 1)
    ]
    once, twice = [*parts[1:], zero], [*parts[2:], zero, one]
    return [
        weight[0:1] * x + weight[1:2] * y + weight[2:3] * z for x, y, z in zip(parts, once, twice)
    ]


def halves(x):
    high = x.astype(BF16)
    return high, (x - high.astype(F32)).astype(BF16)


def twiddles(table_ref):
    terms = [table_ref[2, :, i * LANES : (i + 1) * LANES].astype(F32) for i in range(3)]
    return terms[0] + (terms[1] + terms[2])


def columns(parts):
    return jnp.concatenate(parts, axis=1)


def two_sides(table, x):
    quarter = table.shape[0]
    return [mm(table[:, :quarter], x), mm(table[:, quarter:], x)]


def spectrum_of(sides, twist):
    turned = []
    for phase, (re, im) in enumerate(sides):
        turned.append(turned_back(re, im, twist, phase))
    return spread_phases(turned)


def back_values(spectrum, twist):
    return [
        jnp.concatenate(turned_on(re, im, twist, phase), axis=0)
        for phase, (re, im) in enumerate(gather_phases(spectrum))
    ]


def own_weights(weight_ref, gain_ref):
    place = lax.axis_index("seq")
    lanes = pl.ds(pl.multiple_of(place // 2 * LANES, LANES), LANES)
    odd = place % 2 == 1

    def mine(x):
        return jnp.where(odd, swap(x), x)

    query, key, value = [mine(weight_ref[i, :, lanes]) for i in range(3)]
    gain = both(mine(gain_ref[:, lanes]))[0]
    return jnp.where(low_lanes(key.shape), key, swap(value)), query, gain


def first_mask(quarter, share):
    rows = lax.broadcasted_iota(jnp.int32, (quarter, LANES), 0) & (share - 1)
    return (rows == 0) & low_lanes((quarter, LANES))


def spread_first(groups, index, share):
    x = groups.reshape(groups.shape[0] // 8, 8, LANES)[:, index : index + 1, :]
    return jnp.broadcast_to(x, (x.shape[0], share, LANES)).reshape(x.shape[0] * share, LANES)


def gather_first(parts, share):
    tops = []
    for x in parts:
        tops.append(
            jnp.concatenate([x[at : at + 8] for at in range(0, x.shape[0], share)], axis=0)
        )
    return jnp.where(group_rows(tops[0]) == 0, tops[0], pltpu.roll(tops[1], 1, 0))


def forward_kernel(stage):
    recv_ref, weight_ref, gain_ref = [stage.take(i) for i in range(3)]
    send_ref, saved_ref = stage.out(0), stage.out(1)
    blocks = recv_ref.shape[0]
    rows = recv_ref.shape[1] - STRIP
    share = rows // PHASES
    quarter = blocks * share
    low, starting = low_lanes((quarter, LANES)), first_mask(quarter, share)
    pair_weight, query_weight, gain = own_weights(weight_ref, gain_ref)
    query = first_rows(strip_groups(recv_ref, rows, 0), query_weight)
    pairs = first_rows(strip_groups(recv_ref, rows, 1), pair_weight)
    saved_ref[10, 8:9, :] = gain
    saved_ref[10, 64 : 64 + 8 * blocks, :] = query
    saved_ref[10, 128 : 128 + 8 * blocks, :] = pairs
    strip = exact_groups(query, pairs)
    fixed = pairs * swap(pairs)

    starts = [phase * share for phase in range(PHASES)]
    x = [rows_of(recv_ref, at, share).astype(F32) for at in starts]
    for i in range(2):
        x[i] = jnp.where(starting, spread_first(fixed, i, share), x[i])
    high = columns([y.astype(BF16) for y in x])
    fh, fl = stage.take(3)[0], stage.take(3)[1]
    twist = twiddles(stage.take(3))
    main = [y + z for y, z in zip(two_sides(fh, high), two_sides(fl, high))]
    sides = [[lane_tile(y, phase) for y in main] for phase in range(PHASES)]
    product = []
    for r, (re, im) in enumerate(spectrum_of(sides, twist)):
        saved_ref[2 * r] = re
        saved_ref[2 * r + 1] = im
        other_re, other_im = swap(re), swap(im)
        product.append((re * other_re - im * other_im, re * other_im + im * other_re))

    values = back_values(product, twist)
    bh, bl = stage.take(4)[0], stage.take(4)[1]
    wide = low_lanes((2 * quarter, LANES))
    high = [y.astype(BF16) for y in values]
    wider = [y.astype(F32) for y in high]
    both_parts = [jnp.where(wide, z, y - z).astype(BF16) for y, z in zip(values, wider)]
    high = [jnp.where(wide, wider[i], wider[i + 2]).astype(BF16) for i in range(2)]
    main, more = mm(bh, columns(both_parts)), mm(bl, columns(high))
    grad_ref = stage.take(5)
    send_ref[:, rows // 2 : rows, :] = grad_ref[:, : rows // 2, :]
    send_ref[:, rows:, :] = strip + grad_ref[:, rows // 2 :, :]
    stage.give(0, 1)
    summed = [y + swap(y) for y in (lane_tile(main, phase) for phase in range(PHASES))]
    for i in range(2):
        conv = jnp.where(low, summed[i], summed[i + 2]) + lane_tile(more, i)
        long_out = conv + gain * jnp.where(low, x[i], swap(x[i + 2]))
        saved_ref[8 + i] = long_out
        long_out = long_out.astype(BF16).reshape(blocks, share, LANES)
        send_ref[:, starts[i] : starts[i] + share, :] = long_out


def backward_kernel(stage):
    grad_ref, saved_ref, send_ref = stage.take(0), stage.take(1), stage.out(0)
    blocks = grad_ref.shape[0]
    rows = grad_ref.shape[1] - STRIP
    share = rows // PHASES
    quarter = blocks * share
    low, starting = low_lanes((quarter, LANES)), first_mask(quarter, share)
    gain, groups = saved_ref[10, 8:9, :], 8 * blocks
    query, pairs = [saved_ref[10, at : at + groups, :] for at in (64, 128)]
    strip = strip_groups(grad_ref, rows, 0)
    first = earlier(strip, 4) + earlier(strip, 6)
    fixed = first * query
    starts = [phase * share for phase in range(PHASES)]
    grad_long = []
    for i, at in enumerate(starts[2:]):
        packed = rows_of(grad_ref, at, share).astype(F32)
        grad_long.append(jnp.where(starting, spread_first(fixed, i, share), packed))

    fh, fl = stage.take(2)[0], stage.take(2)[1]
    twist = twiddles(stage.take(2))
    high, rest = halves(columns(grad_long))
    three = zip(two_sides(fh, high), two_sides(fl, high), two_sides(fh, rest))
    main = [x + y + z for x, y, z in three]
    sides = []
    for phase in range(PHASES):
        sides.append([both(lane_tile(x, phase % 2))[phase // 2] for x in main])
    product = []
    for r, (re, im) in enumerate(spectrum_of(sides, twist)):
        k_re, k_im = saved_ref[2 * r], saved_ref[2 * r + 1]
        product.append((k_re * re + k_im * im, k_re * im - k_im * re))
    high, rest = halves(columns(back_values(product, twist)))
    gate(grad_ref, stage.take(3)[0], *[stage.out(i) for i in (1, 2, 3)])
    stage.give(2)
    stage.give(3)
    bh, bl = stage.take(4)[0], stage.take(4)[1]
    times = mm(bh, high) + mm(bl, high) + mm(bh, rest)

    scale = 1.0 / math.sqrt(PHASES * quarter)
    grad_long = [swap(x) for x in grad_long] + grad_long
    grads = []
    for phase, at in enumerate(starts):
        x = lane_tile(times, phase)
        grads.append(jnp.where(low, x * scale, x + gain * grad_long[phase]))
        send_ref[:, at : at + share, :] = grads[-1].astype(BF16).reshape(blocks, share, LANES)
    stage.give(0, 0)
    query_head = first * gather_first([saved_ref[8], saved_ref[9]], share)
    pair_head = both(gather_first(grads[:2], share))[1] * swap(pairs)
    heads = []
    for x in (query_head, pair_head):
        heads.append(jnp.concatenate([x[8:], jnp.zeros((8, LANES), F32)], axis=0))
    send_ref[:, rows:, :] = exact_groups(*heads)


def unpacked(ref, at, half, order):
    tiles = []
    for tile in range(ref.shape[0] // 2):
        x, y = [ref[2 * tile + i, at : at + half].astype(F32) for i in range(2)]
        top, bottom = pair(x, y)
        tiles.append(jnp.concatenate([top, bottom], axis=0))
    return mm(order, jnp.concatenate(tiles, axis=1).astype(BF16))


def pair_strip_of(ref, at):
    sides = [[], []]
    for tile in range(ref.shape[0] // 2):
        x, y = [ref[2 * tile + i, at : at + STRIP].astype(F32)[8:] for i in range(2)]
        for side, z in zip(sides, pair(x, y)):
            side.append(z)
    return [columns(side) for side in sides]


def gate(recv_ref, query, gated_ref, long_ref, tops_ref):
    rows = recv_ref.shape[1] - STRIP
    key, value = [x[0:2] + x[2:4] for x in pair_strip_of(recv_ref, rows)]
    tops_ref[...] = jnp.concatenate([key, value, key, value], axis=0)
    long_out = unpacked(recv_ref, 0, rows // 2, row_order(rows, back=True))
    long_ref[...] = long_out
    gated_ref[...] = (query * long_out).astype(BF16)
    strip = strip_of(recv_ref, rows)
    first = strip + earlier(strip, 2)
    row = lax.broadcasted_iota(jnp.int32, first.shape, 0)
    first = jnp.where(row < 2, first, query[:STRIP])
    gated_ref[:STRIP, :] = (first * long_out[:STRIP]).astype(BF16)


def early_output_kernel(parts, stage):
    w_ref, total = stage.take(0), None
    for part in range(parts):
        gated = stage.take(1 + part)[...]
        width = gated.shape[1]
        term = mm(gated, w_ref[part * width : (part + 1) * width, :])
        total = term if total is None else total + term
    stage.out(0)[...] = total


def output_kernel(part, stage):
    gated = stage.take(1)[...]
    width = gated.shape[1]
    term = mm(gated, stage.take(0)[part * width : (part + 1) * width, :])
    stage.out(0)[...] = (stage.take(2)[...] + term).astype(BF16)


def end_kernel(stage):
    recv_ref, grad_ref, filter_ref = stage.take(0), stage.out(0), stage.out(1)
    rows = filter_ref.shape[0]
    order = row_order(rows, back=True)
    sides = [[], []]
    for tile in range(recv_ref.shape[0] // 2):
        x, y = [recv_ref[2 * tile + i, :rows].astype(F32) for i in range(2)]
        for side, z in zip(sides, pair(x, y)):
            side.append(z.astype(BF16))
    taps, mixed = [mm(order, columns(side)) for side in sides]
    filter_ref[...] = taps
    stage.give(1)
    weight_ref, tops, short_ref = stage.take(1), stage.take(2)[...], stage.take(3)
    row = lax.broadcasted_iota(jnp.int32, mixed.shape, 0)
    heads = [x[0:2] + x[2:4] for x in pair_strip_of(recv_ref, rows)]
    for i in range(2):
        top = tops[2 - 2 * i : 4 - 2 * i]
        other = jnp.where(row == 0, top[0:1], jnp.where(row == 1, top[1:2], short_ref[1 - i]))
        grad_ref[i] = adjoint_of(mixed * other, heads[i], weight_ref[1 + i]).astype(BF16)
    stage.give(0, 0)
    strip = strip_of(recv_ref, rows)
    head = strip[0:2] + strip[2:4]
    grad_query = stage.take(4)[...] * stage.take(5)[...]
    grad_ref[2] = adjoint_of(grad_query, head, weight_ref[0]).astype(BF16)


def partner(x, axis, mask):
    return lax.ppermute(x, axis, [(i, i ^ mask) for i in range(lax.axis_size(axis))])


def exchanged(x, axis):
    return lax.all_to_all(x, axis, split_axis=0, concat_axis=0, tiled=True)


def owner_layer(qkv, filt, skip_gain, short_weight, w_out, g_out):
    shape = jax.ShapeDtypeStruct
    seq_parts, ch_parts = lax.axis_size("seq"), lax.axis_size("ch")
    rows, width = qkv.shape[1], qkv.shape[2]
    tokens = seq_parts * rows
    quarter = tokens // PHASES
    tables = jnp.asarray(phase_tables(tokens))
    table_flops = 2 * 2 * 2 * 3 * tokens * tokens // PHASES * LANES
    product_flops = 2 * rows * width * width * ch_parts
    half = rows // 2
    wide = shape((seq_parts, rows + STRIP, LANES), BF16)
    column = shape((rows, width), BF16)
    saved = shape((11, quarter, LANES), F32)
    gain = skip_gain[None, :]

    (send,) = call(start_kernel, [Far(wide)], Far(short_weight), Far(qkv), Far(filt))
    recv = exchanged(send, "seq")
    half_sums, w_kept, g_kept = call(
        first_product_kernel,
        [
            Near(shape((2, rows, width), BF16), kept=True),
            Near(w_out, kept=True),
            Near(g_out, kept=True),
        ],
        Far(g_out, into=2),
        Far(w_out, turned=(1, 3, 2, 0), into=1),
        flops=product_flops // 2,
    )
    half_sums = partner(half_sums, "ch", 1)
    across, own = call(
        second_product_kernel,
        [Near(column, kept=True), Near(shape((rows, width), F32), kept=True)],
        Near(g_kept),
        Near(w_kept),
        Near(half_sums),
        flops=product_flops // 2,
    )
    across = partner(across, "ch", 2)
    def pinned(x):
        return Near(x, kept=True)

    tables_back = Far(tables, [(2, 2)])
    exact = shape((rows, width), F32)
    tables_on, weight, gain, query, short = call(
        query_kernel,
        [
            pinned(shape((3, *tables.shape[1:]), BF16)),
            pinned(short_weight),
            pinned(gain),
            pinned(exact),
            Far(shape((3, rows, width), F32)),
        ],
        Far(qkv),
        Far(short_weight, into=1),
        Far(tables, [(0, 2), (4, 1)], into=0),
        Far(gain, into=2),
    )
    grad_long, grad_far = call(
        sum_kernel,
        [Far(shape((seq_parts, half + STRIP, LANES), BF16)), Far(exact)],
        Near(own),
        Near(across),
        Near(query),
    )
    send, saved = call(
        forward_kernel,
        [
            Far(wide, [(0, half), (half, half + STRIP)], axis=1),
            pinned(saved),
        ],
        pinned(recv),
        Near(weight),
        Near(gain),
        Near(tables_on),
        tables_back,
        Far(grad_long),
        flops=table_flops,
    )
    swapped = exchanged(send, "seq")
    send, gated, long_out, tops = call(
        backward_kernel,
        [
            Far(wide, [(0, rows), (rows, STRIP)], axis=1),
            pinned(column),
            Far(exact),
            Far(shape((8, width), F32)),
        ],
        Near(swapped),
        Near(saved),
        Near(tables_on),
        Far(short, [(0, 1)]),
        tables_back,
        flops=table_flops,
    )
    grad_recv = exchanged(send, "seq")
    across = partner(gated, "ch", 2)
    near, far = partner(gated, "ch", 1), partner(across, "ch", 1)
    (early,) = call(
        functools.partial(early_output_kernel, ch_parts - 1),
        [pinned(exact)],
        Near(w_kept),
        Near(gated),
        Near(near),
        Near(across),
        flops=product_flops * (ch_parts - 1) // ch_parts,
    )
    (output,) = call(
        functools.partial(output_kernel, ch_parts - 1),
        [Far(column)],
        Near(w_kept),
        Near(far),
        Near(early),
        flops=product_flops // ch_parts,
    )
    grad_qkv, grad_filter = call(
        end_kernel,
        [Far(shape((3, rows, width), BF16), [(1, 2), (0, 1)]), Far(exact)],
        Near(grad_recv),
        Far(short_weight),
        Far(tops),
        Far(short, [(1, 2)]),
        Far(long_out),
        Far(grad_far),
    )
    return (output, grad_qkv, grad_filter)


def local(qkv, filt, skip_gain, short_weight, w_out, g_out):
    seq_parts = lax.axis_size("seq")
    rows, width = qkv.shape[1], qkv.shape[2]
    fits = width == HALF * seq_parts and rows % HALF == 0 and rows & (rows - 1) == 0 and rows * seq_parts <= 2048
    if fits and lax.axis_size("ch") == 4:
        return owner_layer(qkv, filt, skip_gain, short_weight, w_out, g_out)
    return spread_layer(qkv, filt, skip_gain, short_weight, w_out, g_out)


def solution(mesh):
    in_specs = (
        P(None, "seq", "ch"),
        P("seq", "ch"),
        P("ch"),
        P(None, None, "ch"),
        P(None, "ch"),
        P("seq", "ch"),
    )
    out_specs = (P("seq", "ch"), P(None, "seq", "ch"), P("seq", "ch"))
    return jax.shard_map(local, mesh=mesh, in_specs=in_specs, out_specs=out_specs, check_vma=False)
```
